32 devices in a mesh: img: 16 (over z, x, core), row: 2 (over y).
Axes of the slice: x: 2, y: 2, z: 4, core: 2. Of those that a mesh axis runs over, the one named last changes fastest.
Arguments:
- hidden: bfloat16 [16, 256, 2048], P('img', 'row'), may hold values from -6 to 6
- mask_index: int32 [16, 256], P('img'), may hold values from 0 to 255, as said below
- mask_count: int32 [16], P('img'), may hold values from 1 to 256, as said below
- mask_embed: float32 [2048], replicated, may hold values from -6 to 6
- norm_gains: float32 [3, 2048], replicated, may hold values from 0.1 to 1.9
- caption: bfloat16 [128, 4096], replicated, may hold values from -6 to 6
- w_qkv: bfloat16 [2048, 3, 2048], P(('img', 'row')), may hold values from -0.125 to 0.125
- w_out: bfloat16 [2048, 2048], P(('img', 'row')), may hold values from -0.5 to 0.5
- w_cross: bfloat16 [2048, 3, 2048], P(('img', 'row')), may hold values from -0.125 to 0.125
- w_cross_out: bfloat16 [2048, 2048], P(('img', 'row')), may hold values from -0.5 to 0.5
- w_text: bfloat16 [2048, 4096], P(('img', 'row')), may hold values from -0.09375 to 0.09375
- w_up: bfloat16 [2048, 8192], P(('img', 'row')), may hold values from -0.125 to 0.125
- w_down: bfloat16 [2048, 8192], P(('img', 'row')), may hold values from -0.09375 to 0.09375
- cotangent: bfloat16 [16, 256, 2048], P('img', 'row'), may hold values from -6 to 6
Outputs:
- output: bfloat16 [16, 256, 2048], P('img', 'row')
- grad_hidden: bfloat16 [16, 256, 2048], P('img', 'row')
- grad_caption: float32 [128, 4096], replicated
- grad_gains: float32 [3, 2048], replicated
- grad_mask: float32 [2048], replicated
- grad_qkv: float32 [2048, 3, 2048], P(('img', 'row'))
- grad_out: float32 [2048, 2048], P(('img', 'row'))
- grad_cross: float32 [2048, 3, 2048], P(('img', 'row'))
- grad_cross_out: float32 [2048, 2048], P(('img', 'row'))
- grad_text_w: float32 [2048, 4096], P(('img', 'row'))
- grad_up: float32 [2048, 8192], P(('img', 'row'))
- grad_down: float32 [2048, 8192], P(('img', 'row'))
The draws below stay inside these ranges and needn't reach their ends.
Inputs may be any that keep to these rules, and one draw needn't show every extreme that they name: `mask_index`: each row lists every position 0 to 255 of its image once; the first mask_count entries are the masked positions. `mask_count`: masked tokens of each image, after a cosine plan; some image has all 256 masked and some image has one.
All inputs are finite; a program needn't handle non-finite values.
Results may differ from the reference program's by a relative error of at most 0.02.
Values may be sent and summed in bfloat16 or wider, within the bound.
No kernel may reach another device: no remote copies, remote signals or barrier semaphores. Data moves between devices by JAX's collectives and lax.ppermute only.
A program may use at most 832 MiB of HBM per device.

```python
import math
import jax
import jax.numpy as jnp
import numpy as np
from jax import lax

SEQ = 256
CTX = 128
D = 2048
H = 16
HD = 128
FF = 8192
DT = 4096
IMAGES = 16


def draw_mask_index(key, part):
    key = jax.random.fold_in(key, 11)
    image_keys = jax.random.split(key, IMAGES)
    return jax.vmap(lambda one_key: jax.random.permutation(one_key, SEQ))(image_keys).astype(jnp.int32)


def draw_mask_count(key, part):
    key = jax.random.fold_in(key, 23)
    pick_key, full_key, other_key = jax.random.split(key, 3)
    table = np.maximum(np.ceil(np.cos(np.pi / 2 * np.arange(1024) / 1024) * SEQ), 1).astype(np.int32)
    picks = jax.random.randint(pick_key, (IMAGES,), 0, 1024)
    counts = jnp.asarray(table)[picks]
    full_image = jax.random.randint(full_key, (), 0, IMAGES)
    other_image = (full_image + 1 + jax.random.randint(other_key, (), 0, IMAGES - 1)) % IMAGES
    counts = counts.at[full_image].set(SEQ)
    counts = counts.at[other_image].set(1)
    return counts.astype(jnp.int32)


def block_levels(own_key, extent, shards, smallest, top_value):
    level, own = 1.0, jax.random.fold_in(own_key, 6)
    for dim, shards_of in shards:
        heights = jnp.exp(jax.random.uniform(jax.random.fold_in(own, dim), (shards_of,), jnp.float32, smallest / len(shards), top_value / len(shards)))
        level = level * jnp.repeat(heights, extent[dim] // shards_of).reshape([-1 if axis == dim else 1 for axis in range(len(extent))])
    return level


def noise(stream_key, extent, spread, most, cuts=(), kind=jnp.bfloat16):
    values = jax.random.normal(stream_key, extent, jnp.float32) * spread
    if len(cuts) > 0:
        values = block_levels(stream_key, extent, cuts, -0.22, 0.18) * values
    return jnp.clip(values, min=-most, max=most).astype(kind)


def setup_inputs(seed: int = 0) -> dict:
    key_list = jax.random.split(jax.random.key(seed), 15)
    return {
        "hidden": noise(key_list[0], (IMAGES, SEQ, D), 1.0, 6.0, ((0, 16), (1, 2))),
        "mask_index": draw_mask_index(jax.random.fold_in(key_list[14], 71), 0),
        "mask_count": draw_mask_count(jax.random.fold_in(key_list[14], 71), 0),
        "mask_embed": noise(key_list[3], (D,), 1.0, 6.0, (), jnp.float32),
        "norm_gains": jnp.clip(1.0 + 0.18 * jax.random.normal(key_list[4], (3, D), jnp.float32), 0.1, 1.9),
        "caption": noise(key_list[5], (CTX, DT), 1.0, 6.0),
        "w_qkv": noise(key_list[6], (D, 3, D), D ** -0.5, 0.125, ((0, 32),)),
        "w_out": noise(key_list[7], (D, D), (D // 16) ** -0.5, 0.5, ((0, 32),)),
        "w_cross": noise(key_list[8], (D, 3, D), D ** -0.5, 0.125, ((0, 32),)),
        "w_cross_out": noise(key_list[9], (D, D), (D // 16) ** -0.5, 0.5, ((0, 32),)),
        "w_text": noise(key_list[10], (D, DT), DT ** -0.5, 0.09375, ((0, 32),)),
        "w_up": noise(key_list[11], (D, FF), D ** -0.5, 0.125, ((0, 32),)),
        "w_down": noise(key_list[12], (D, FF), (FF // 2) ** -0.5, 0.09375, ((0, 32),)),
        "cotangent": noise(key_list[13], (IMAGES, SEQ, D), 1.0, 6.0, ((0, 16), (1, 2))),
    }


@jax.custom_vjp
def low(v):
    return lax.optimization_barrier(v.astype(jnp.bfloat16)).astype(jnp.float32)

@jax.custom_vjp
def low_back(v):
    return v

def low_keep(v):
    return (low(v), None)

def low_pass(kept, grad):
    return (grad,)

def back_keep(v):
    return (v, None)

def back_low(kept, grad):
    return (low(grad),)
low.defvjp(low_keep, low_pass)
low_back.defvjp(back_keep, back_low)
EPS = 1e-05
HIGH = lax.Precision.HIGHEST

def layer_norm(values, gain):
    centred = values - lax.optimization_barrier(jnp.mean(values, axis=-1, keepdims=True))
    return centred * lax.rsqrt(lax.optimization_barrier(jnp.mean(centred * centred, axis=-1, keepdims=True)) + EPS) * gain

def split_heads(values):
    return values.reshape(values.shape[:-1] + (H, HD))

def merge_heads(values):
    return values.reshape(values.shape[:-2] + (H * HD,))

def attention(queries, key_rows, value_rows, score_form, mix_form):
    scores = low_back(jnp.einsum(score_form, split_heads(queries), split_heads(key_rows), precision=HIGH) * (1.0 / math.sqrt(HD)))
    row_peak = lax.optimization_barrier(jnp.max(scores, axis=-1, keepdims=True))
    exp_terms = jnp.exp(scores - row_peak)
    weights = exp_terms / lax.optimization_barrier(jnp.sum(exp_terms, axis=-1, keepdims=True))
    return merge_heads(jnp.einsum(mix_form, low(weights), split_heads(value_rows), precision=HIGH))

def group_forward(params, text_keys, text_values, start_x):
    norm_gains, w_qkv, w_out, w_cross, w_cross_out, w_up, w_down = params
    attn_in = low(layer_norm(start_x, norm_gains[0]))
    projected = low(low_back(jnp.einsum('bsd,dje->bsje', attn_in, w_qkv, precision=HIGH)))
    self_mixed = low(low_back(attention(projected[:, :, 0], projected[:, :, 1], projected[:, :, 2], 'bqhe,bkhe->bhqk', 'bhqk,bkhe->bqhe')))
    after_attn = start_x + low_back(jnp.einsum('bsd,ed->bse', self_mixed, w_out, precision=HIGH))
    cross_in = low(layer_norm(after_attn, norm_gains[1]))
    cross_queries = low(low_back(jnp.einsum('bsd,de->bse', cross_in, w_cross[:, 0], precision=HIGH)))
    cross_mixed = low(low_back(attention(cross_queries, text_keys, text_values, 'bqhe,khe->bhqk', 'bhqk,khe->bqhe')))
    after_cross = after_attn + low_back(jnp.einsum('bsd,ed->bse', cross_mixed, w_cross_out, precision=HIGH))
    mlp_in = low(layer_norm(after_cross, norm_gains[2]))
    pre_act = low_back(jnp.einsum('bsd,df->bsf', mlp_in, w_up, precision=HIGH))
    activated = low(jax.nn.gelu(pre_act))
    return after_cross + low_back(jnp.einsum('bsf,df->bsd', activated, w_down, precision=HIGH))

def forward(hidden, mask_embed, norm_gains, caption, w_qkv, w_out, w_cross, w_cross_out, w_text, w_up, w_down, masked):
    text_hidden = low(low_back(jnp.einsum('cf,df->cd', caption, w_text, precision=HIGH)))
    text_kv = low(low_back(jnp.einsum('cd,dje->cje', text_hidden, w_cross[:, 1:], precision=HIGH)))
    start_x = jnp.where(masked[:, :, None], mask_embed, hidden)
    group_size = math.gcd(hidden.shape[0], 16)
    blocks = start_x.reshape((-1, group_size) + start_x.shape[1:])
    params = (norm_gains, w_qkv, w_out, w_cross, w_cross_out, w_up, w_down)
    step_fn = jax.checkpoint(lambda block: group_forward(params, text_kv[:, 0], text_kv[:, 1], block))
    return lax.map(step_fn, blocks).reshape(hidden.shape)

def mask_of(mask_index, mask_count):
    ranks = jnp.arange(mask_index.shape[1], dtype=jnp.int32)
    live = ranks[None, :] < mask_count[:, None]
    matches = (mask_index[:, :, None] == ranks[None, None, :]) & live[:, :, None]
    return jnp.any(matches, axis=1)

def reference(hidden, mask_index, mask_count, mask_embed, norm_gains, caption, w_qkv, w_out, w_cross, w_cross_out, w_text, w_up, w_down, cotangent):
    masked = mask_of(mask_index, mask_count)
    floats = [array_in.astype(jnp.float32) for array_in in (hidden, mask_embed, norm_gains, caption, w_qkv, w_out, w_cross, w_cross_out, w_text, w_up, w_down)]

    def wrapped(p_hidden, p_mask, p_gains, p_caption, p_qkv, p_out, p_cross, p_cross_out, p_text, p_up, p_down):
        return forward(p_hidden, p_mask, p_gains, p_caption, p_qkv, p_out, p_cross, p_cross_out, p_text, p_up, p_down, masked)
    result, pull = jax.vjp(wrapped, floats[0], floats[1], floats[2], floats[3], floats[4], floats[5], floats[6], floats[7], floats[8], floats[9], floats[10])
    seed_grad = cotangent.astype(jnp.float32) * masked[:, :, None].astype(jnp.float32)
    grads = pull(seed_grad)
    return (result.astype(jnp.bfloat16), grads[0].astype(jnp.bfloat16), grads[3], grads[2], grads[1], grads[4], grads[5], grads[6], grads[7], grads[8], grads[9], grads[10])
```

```python
import math

import jax
import jax.numpy as jnp
from jax import lax
from jax.sharding import Mesh
from jax.sharding import PartitionSpec as P

HD = 128
EPS = 1e-05
BF = jnp.bfloat16
F32 = jnp.float32
PAIR = ((0, 1), (1, 0))
DIAG = ((0, 3), (1, 2), (2, 1), (3, 0))
DATA = ("z", "c")


def dot(a, b, dims):
    return lax.dot_general(a, b, (dims, ((), ())), preferred_element_type=F32)


def mm(a, b):
    return dot(a, b, ((1,), (0,)))


def mm_t(a, b):
    return dot(a, b, ((1,), (1,)))


def t_mm(a, b):
    return dot(a, b, ((0,), (0,)))


def normalize(values):
    centred = values - jnp.mean(values, axis=-1, keepdims=True)
    inv_std = lax.rsqrt(jnp.mean(centred * centred, axis=-1, keepdims=True) + EPS)
    return centred * inv_std, inv_std


def norm_back(grad_normed, normed, inv_std, gain):
    scaled = grad_normed * gain
    first_mean = jnp.mean(scaled, axis=-1, keepdims=True)
    second_mean = jnp.mean(scaled * normed, axis=-1, keepdims=True)
    return (
        inv_std * (scaled - first_mean - normed * second_mean),
        jnp.sum(grad_normed * normed, axis=0),
    )


def swap(values, axis):
    return lax.ppermute(values, axis, PAIR)


def swap_diag(values):
    return lax.ppermute(values, ("x", "y"), DIAG)


def gather_tokens(own):
    half = own.shape[0] // 2
    from_x = swap(own, "x")
    from_y = swap(own, "y")
    diag_low = swap(from_x[:half], "y")
    diag_high = swap(from_y[half:], "x")
    return jnp.concatenate([own, from_y, from_x, diag_low, diag_high], axis=0)


def scatter_tokens(partial):
    rows = partial.shape[0] // 4
    half = rows // 2
    own, for_y, for_x, for_diag = (partial[k * rows : (k + 1) * rows] for k in range(4))
    for_diag = for_diag.astype(BF)
    diag_low = swap(for_diag[:half], "y").astype(F32)
    diag_high = swap(for_diag[half:], "x").astype(F32)
    from_x = swap(
        jnp.concatenate([for_x[:half] + diag_low, for_x[half:]], axis=0).astype(BF), "x"
    )
    from_y = swap(
        jnp.concatenate([for_y[:half], for_y[half:] + diag_high], axis=0).astype(BF), "y"
    )
    return own + from_x.astype(F32) + from_y.astype(F32)


def exchange(blocks, rank):
    def pick(k):
        return lax.dynamic_index_in_dim(blocks, rank ^ k, 0, keepdims=True)

    parts = [pick(0), swap(pick(1), "y"), swap(pick(2), "x"), swap_diag(pick(3))]
    out = jnp.zeros_like(blocks)
    for k, part in enumerate(parts):
        out = lax.dynamic_update_slice_in_dim(out, part, rank ^ k, 0)
    return out


def column_blocks(weight, parts):
    rows = weight.shape[0]
    shaped = weight.reshape(rows, parts, 4, -1)
    return shaped.transpose(2, 0, 1, 3).reshape(4, rows, -1)


def weight_columns(blocks, rank):
    mine = exchange(blocks, rank)
    return lax.all_gather(mine.reshape(-1, mine.shape[-1]), DATA, axis=0, tiled=True)


def grad_rows(partial, rank):
    summed = lax.psum_scatter(partial, DATA, scatter_dimension=0, tiled=True)
    return exchange(summed.reshape(4, -1, summed.shape[-1]), rank)


def join_columns(blocks, parts):
    rows = blocks.shape[1]
    shaped = blocks.reshape(4, rows, parts, -1)
    return shaped.transpose(1, 2, 0, 3).reshape(rows, parts, -1)


def heads_of(values, images):
    return values.reshape(images, -1, values.shape[-1] // HD, HD)


def attend_forward(queries, keys, values, score_form, mix_form, scale):
    scores = jnp.einsum(score_form, queries, keys, preferred_element_type=F32) * scale
    row_peak = jnp.max(scores, axis=-1, keepdims=True)
    exp_terms = jnp.exp(scores - row_peak)
    probs = exp_terms / jnp.sum(exp_terms, axis=-1, keepdims=True)
    mixed = jnp.einsum(mix_form, probs.astype(BF), values, preferred_element_type=F32)
    return probs, mixed.astype(BF)


def attend_back(probs, queries, keys, values, grad_mixed, score_form, mix_form, key_form, scale):
    grad_probs = jnp.einsum(score_form, grad_mixed, values, preferred_element_type=F32)
    grad_scores = (
        probs * (grad_probs - jnp.sum(probs * grad_probs, axis=-1, keepdims=True))
    ).astype(BF)
    grad_queries = jnp.einsum(mix_form, grad_scores, keys, preferred_element_type=F32) * scale
    grad_keys = jnp.einsum(key_form, grad_scores, queries, preferred_element_type=F32) * scale
    grad_values = jnp.einsum(
        key_form, probs.astype(BF), grad_mixed, preferred_element_type=F32
    )
    return grad_queries, grad_keys, grad_values


def make_local(z_size):
    def sum_all(values):
        for axis in ("c", "x", "y"):
            values = values + swap(values, axis)
        step = 1
        while step < z_size:
            values = values + lax.ppermute(
                values, "z", tuple((k, k ^ step) for k in range(z_size))
            )
            step *= 2
        return values

    def feature_swap(values):
        lead = values.shape[:-1]
        shaped = values.reshape(lead + (z_size, 2, 2, -1))
        return jnp.swapaxes(shaped, -3, -2).reshape(values.shape)

    def local(
        hidden,
        mask_index,
        mask_count,
        mask_embed,
        norm_gains,
        caption,
        w_qkv,
        w_out,
        w_cross,
        w_cross_out,
        w_text,
        w_up,
        w_down,
        cotangent,
    ):
        images, local_rows, width = hidden.shape
        full_length = mask_index.shape[1]
        scale = 1.0 / math.sqrt(HD)
        shard_rows = w_qkv.shape[0]
        rank = lax.axis_index("x") * 2 + lax.axis_index("y")
        tokens = images * local_rows

        qkv = weight_columns(column_blocks(w_qkv.reshape(shard_rows, -1), 3), rank)
        mid = weight_columns(
            jnp.concatenate(
                [
                    column_blocks(w_out, 1),
                    column_blocks(w_cross[:, 0], 1),
                    column_blocks(w_cross_out, 1),
                ],
                axis=2,
            ),
            rank,
        )
        up = weight_columns(column_blocks(w_up, 1), rank)
        down = weight_columns(column_blocks(w_down, 1), rank)
        group = width // 4
        out_w, query_w, cross_out_w = (mid[:, k * group : (k + 1) * group] for k in range(3))

        own_text = mm_t(caption, w_text).astype(BF)
        kv_rows = w_cross[:, 1:].reshape(shard_rows, 2 * width)
        kv_part = mm(own_text, kv_rows)
        kv_part = exchange(column_blocks(kv_part, 2), rank).sum(axis=0)
        text_kv = lax.psum(kv_part, DATA).astype(BF)
        text_keys = text_kv[:, :group].reshape(-1, group // HD, HD)
        text_values = text_kv[:, group:].reshape(-1, group // HD, HD)

        positions = lax.axis_index("y") * local_rows + jnp.arange(local_rows, dtype=jnp.int32)
        ranks = jnp.arange(full_length, dtype=jnp.int32)
        matches = (mask_index[:, :, None] == positions[None, None, :]) & (
            ranks[None, :, None] < mask_count[:, None, None]
        )
        masked = jnp.any(matches, axis=1).reshape(tokens, 1)
        gains = feature_swap(norm_gains)
        start_x = jnp.where(
            masked,
            feature_swap(mask_embed),
            feature_swap(hidden.reshape(tokens, width)).astype(F32),
        )
        grad_top = feature_swap(cotangent.reshape(tokens, width)).astype(F32) * masked.astype(F32)
        grad_y = gather_tokens(grad_top.astype(BF))

        normed_a, inv_a = normalize(start_x)
        attn_in = gather_tokens((normed_a * gains[0]).astype(BF))
        projected = mm(attn_in, qkv).astype(BF)
        queries, keys, values = (
            heads_of(projected[:, k * group : (k + 1) * group], 2 * images) for k in range(3)
        )
        self_forms = ("bqhe,bkhe->bhqk", "bhqk,bkhe->bqhe")
        self_probs, self_mixed = attend_forward(queries, keys, values, *self_forms, scale)
        self_mixed = self_mixed.reshape(4 * tokens, group)
        after_attn = start_x + scatter_tokens(mm_t(self_mixed, out_w))

        normed_b, inv_b = normalize(after_attn)
        cross_in = gather_tokens((normed_b * gains[1]).astype(BF))
        cross_queries = heads_of(mm(cross_in, query_w).astype(BF), 2 * images)
        cross_forms = ("bqhe,khe->bhqk", "bhqk,khe->bqhe")
        cross_probs, cross_mixed = attend_forward(
            cross_queries, text_keys, text_values, *cross_forms, scale
        )
        cross_mixed = cross_mixed.reshape(4 * tokens, group)
        after_cross = after_attn + scatter_tokens(mm_t(cross_mixed, cross_out_w))

        normed_c, inv_c = normalize(after_cross)
        mlp_in = gather_tokens((normed_c * gains[2]).astype(BF))
        pre_act = mm(mlp_in, up)
        activated, gelu_pull = jax.vjp(jax.nn.gelu, pre_act)
        activated = activated.astype(BF)
        grad_pre = gelu_pull(mm(grad_y, down))[0].astype(BF)
        grad_mlp_in = scatter_tokens(mm_t(grad_pre, up))
        result = after_cross + scatter_tokens(mm_t(activated, down))
        output = feature_swap(result.astype(BF))
        down_grad = grad_rows(t_mm(grad_y, activated).astype(BF), rank)
        up_grad = grad_rows(t_mm(mlp_in, grad_pre).astype(BF), rank)
        back_c, gain_grad_c = norm_back(grad_mlp_in, normed_c, inv_c, gains[2])
        grad_after_cross = grad_top + back_c

        cross_branch = gather_tokens(grad_after_cross.astype(BF))
        grad_cross_mixed = heads_of(mm(cross_branch, cross_out_w).astype(BF), 2 * images)
        grad_cq, grad_tk, grad_tv = attend_back(
            cross_probs,
            cross_queries,
            text_keys,
            text_values,
            grad_cross_mixed,
            *cross_forms,
            "bhqk,bqhe->khe",
            scale,
        )
        grad_cq = grad_cq.astype(BF).reshape(4 * tokens, group)
        grad_cross_in = scatter_tokens(mm_t(grad_cq, query_w))
        back_b, gain_grad_b = norm_back(grad_cross_in, normed_b, inv_b, gains[1])
        grad_after_attn = grad_after_cross + back_b

        kv_grad = jnp.concatenate(
            [grad_tk.reshape(-1, group), grad_tv.reshape(-1, group)], axis=1
        )
        kv_grad = lax.psum(kv_grad, DATA).astype(BF)
        kv_grads = exchange(jnp.broadcast_to(kv_grad[None], (4,) + kv_grad.shape), rank)
        kv_grads = join_columns(kv_grads, 2).reshape(-1, 2 * width)
        kv_weight_grad = t_mm(own_text, kv_grads).reshape(shard_rows, 2, width)
        grad_text = mm_t(kv_grads, kv_rows).astype(BF)
        grad_text_w = t_mm(grad_text, caption)
        caption_part = mm(grad_text, w_text)
        caption_part = exchange(column_blocks(caption_part, 1), rank).sum(axis=0)
        caption_part = lax.psum(caption_part, DATA)
        caption_parts = exchange(
            jnp.broadcast_to(caption_part[None], (4,) + caption_part.shape), rank
        )
        grad_caption = join_columns(caption_parts, 1)[:, 0]

        attn_branch = gather_tokens(grad_after_attn.astype(BF))
        grad_self_mixed = heads_of(mm(attn_branch, out_w).astype(BF), 2 * images)
        grad_projected = attend_back(
            self_probs,
            queries,
            keys,
            values,
            grad_self_mixed,
            *self_forms,
            "bhqk,bqhe->bkhe",
            scale,
        )
        grad_projected = jnp.concatenate(
            [part.astype(BF).reshape(4 * tokens, group) for part in grad_projected], axis=1
        )
        mid_part = jnp.concatenate(
            [
                t_mm(attn_branch, self_mixed).astype(BF),
                t_mm(cross_in, grad_cq).astype(BF),
                t_mm(cross_branch, cross_mixed).astype(BF),
            ],
            axis=1,
        )
        mid_grad = join_columns(grad_rows(mid_part, rank), 3)
        qkv_grad = join_columns(
            grad_rows(t_mm(attn_in, grad_projected).astype(BF), rank), 3
        ).astype(F32)
        grad_attn_in = scatter_tokens(mm_t(grad_projected, qkv))
        back_a, gain_grad_a = norm_back(grad_attn_in, normed_a, inv_a, gains[0])
        grad_start = grad_after_attn + back_a

        grad_hidden = feature_swap(jnp.where(masked, 0.0, grad_start).astype(BF))
        mask_part = jnp.sum(jnp.where(masked, grad_start, 0.0), axis=0)
        sums = feature_swap(
            sum_all(jnp.stack([gain_grad_a, gain_grad_b, gain_grad_c, mask_part]))
        )
        mid_grad = mid_grad.astype(F32)
        grad_cross = jnp.concatenate([mid_grad[:, 1:2], kv_weight_grad], axis=1)
        return (
            output.reshape(hidden.shape),
            grad_hidden.reshape(hidden.shape),
            grad_caption,
            sums[:3],
            sums[3],
            qkv_grad,
            mid_grad[:, 0],
            grad_cross,
            mid_grad[:, 2],
            grad_text_w,
            join_columns(up_grad, 1)[:, 0].astype(F32),
            join_columns(down_grad, 1)[:, 0].astype(F32),
        )

    return local


def solution(mesh):
    z_size = mesh.shape["img"] // 4
    inner = Mesh(mesh.devices.reshape(z_size, 2, 2, 2), ("z", "x", "c", "y"))
    tokens = P(("z", "x", "c"), "y", None)
    rows = P(("z", "x", "c", "y"))
    in_specs = (
        tokens,
        P(("z", "x", "c"), None),
        P(("z", "x", "c")),
        P(),
        P(),
        P(),
        rows,
        rows,
        rows,
        rows,
        rows,
        rows,
        rows,
        tokens,
    )
    out_specs = (tokens, tokens, P(), P(), P()) + (rows,) * 7
    return jax.shard_map(
        make_local(z_size), mesh=inner, in_specs=in_specs, out_specs=out_specs, check_vma=False
    )
```

```python
import math

import jax
import jax.numpy as jnp
from jax import lax
from jax.experimental import pallas as pl
from jax.experimental.pallas import tpu as pltpu
from jax.sharding import Mesh
from jax.sharding import PartitionSpec as P

HD = 128
EPS = 1e-05
BF = jnp.bfloat16
F32 = jnp.float32
PAIR = ((0, 1), (1, 0))
DIAG = ((0, 3), (1, 2), (2, 1), (3, 0))
DATA = ("z", "c")
VMEM = 40 * 1024 * 1024


def dot(a, b, dims):
    return lax.dot_general(a, b, (dims, ((), ())), preferred_element_type=F32)


def mm(a, b):
    return dot(a, b, ((1,), (0,)))


def mm_t(a, b):
    return dot(a, b, ((1,), (1,)))


def t_mm(a, b):
    return dot(a, b, ((0,), (0,)))


def normalize(values):
    centred = values - jnp.mean(values, axis=-1, keepdims=True)
    inv_std = lax.rsqrt(jnp.mean(centred * centred, axis=-1, keepdims=True) + EPS)
    return centred * inv_std, inv_std


def norm_back(grad_normed, normed, inv_std, gain):
    scaled = grad_normed * gain
    first_mean = jnp.mean(scaled, axis=-1, keepdims=True)
    second_mean = jnp.mean(scaled * normed, axis=-1, keepdims=True)
    return (
        inv_std * (scaled - first_mean - normed * second_mean),
        jnp.sum(grad_normed * normed, axis=0),
    )


def swap(values, axis):
    return lax.ppermute(values, axis, PAIR)


def swap_diag(values):
    return lax.ppermute(values, ("x", "y"), DIAG)


def gather_tokens(own):
    half = own.shape[0] // 2
    from_x = swap(own, "x")
    from_y = swap(own, "y")
    diag_low = swap(from_x[:half], "y")
    diag_high = swap(from_y[half:], "x")
    return jnp.concatenate([own, from_y, from_x, diag_low, diag_high], axis=0)


def scatter_tokens(partial):
    rows = partial.shape[0] // 4
    half = rows // 2
    own, for_y, for_x, for_diag = (partial[k * rows : (k + 1) * rows] for k in range(4))
    for_diag = for_diag.astype(BF)
    diag_low = swap(for_diag[:half], "y").astype(F32)
    diag_high = swap(for_diag[half:], "x").astype(F32)
    from_x = swap(
        jnp.concatenate([for_x[:half] + diag_low, for_x[half:]], axis=0).astype(BF), "x"
    )
    from_y = swap(
        jnp.concatenate([for_y[:half], for_y[half:] + diag_high], axis=0).astype(BF), "y"
    )
    return own + from_x.astype(F32) + from_y.astype(F32)


def swap_all(parts):
    return [parts[0], swap(parts[1], "y"), swap(parts[2], "x"), swap_diag(parts[3])]


def pieces(values, rank, width):
    return [
        lax.dynamic_slice_in_dim(values, (rank ^ k) * width, width, 1) for k in range(4)
    ]


def grid_spec(in_specs, out_specs):
    return pltpu.PrefetchScalarGridSpec(
        num_scalar_prefetch=1, grid=(4,), in_specs=in_specs, out_specs=out_specs
    )


def pack(weights, rank):
    rows = weights[0].shape[0]
    widths = [w.shape[1] // 4 for w in weights]
    total = sum(widths)

    def kernel(rank_ref, *refs):
        step = pl.program_id(0)
        for k in range(4):

            @pl.when(step == k)
            def _():
                offset = 0
                for ref, width in zip(refs, widths):
                    refs[len(widths) + k][:, offset : offset + width] = ref[...]
                    offset += width

    return pl.pallas_call(
        kernel,
        out_shape=[jax.ShapeDtypeStruct((rows, total), BF)] * 4,
        grid_spec=grid_spec(
            [pl.BlockSpec((rows, w), lambda k, r: (0, k ^ r[0])) for w in widths],
            [pl.BlockSpec((rows, total), lambda k, r: (0, 0))] * 4,
        ),
        compiler_params=pltpu.CompilerParams(vmem_limit_bytes=VMEM),
        name="pack",
    )(rank.reshape(1), *weights)


def place(parts, rank, widths):
    rows, total = parts[0].shape

    def kernel(rank_ref, *refs):
        step = pl.program_id(0)
        for k in range(4):

            @pl.when(step == k)
            def _():
                offset = 0
                for ref, width in zip(refs[4:], widths):
                    ref[...] = refs[k][:, offset : offset + width]
                    offset += width

    return pl.pallas_call(
        kernel,
        out_shape=[jax.ShapeDtypeStruct((4 * rows, w), BF) for w in widths],
        grid_spec=grid_spec(
            [pl.BlockSpec((rows, total), lambda k, r: (0, 0))] * 4,
            [pl.BlockSpec((rows, w), lambda k, r: (k ^ r[0], 0)) for w in widths],
        ),
        compiler_params=pltpu.CompilerParams(vmem_limit_bytes=VMEM),
        name="place",
    )(rank.reshape(1), *parts)


def finish(parts, rank, widths):
    rows, total = parts[0].shape

    def kernel(rank_ref, *refs):
        step = pl.program_id(0)
        for k in range(4):

            @pl.when(step == k)
            def _():
                offset = 0
                for ref, width in zip(refs[4:], widths):
                    ref[...] = refs[k][:, offset : offset + width].astype(F32)
                    offset += width

    return pl.pallas_call(
        kernel,
        out_shape=[jax.ShapeDtypeStruct((rows, 4 * w), F32) for w in widths],
        grid_spec=grid_spec(
            [pl.BlockSpec((rows, total), lambda k, r: (0, 0))] * 4,
            [pl.BlockSpec((rows, w), lambda k, r: (0, k ^ r[0])) for w in widths],
        ),
        compiler_params=pltpu.CompilerParams(vmem_limit_bytes=VMEM),
        name="finish",
    )(rank.reshape(1), *parts)


def finish_three(parts, rank):
    rows, total = parts[0].shape
    width = total // 3

    def kernel(rank_ref, *refs):
        step = pl.program_id(0)
        for k in range(4):

            @pl.when(step == k)
            def _():
                for j in range(3):
                    refs[4][:, j, :] = refs[k][:, j * width : (j + 1) * width].astype(F32)

    return pl.pallas_call(
        kernel,
        out_shape=jax.ShapeDtypeStruct((rows, 3, 4 * width), F32),
        grid_spec=grid_spec(
            [pl.BlockSpec((rows, total), lambda k, r: (0, 0))] * 4,
            pl.BlockSpec((rows, 3, width), lambda k, r: (0, 0, k ^ r[0])),
        ),
        compiler_params=pltpu.CompilerParams(vmem_limit_bytes=VMEM),
        name="finish_three",
    )(rank.reshape(1), *parts)


def softmax(scores):
    exp_terms = jnp.exp(scores - jnp.max(scores, axis=-1, keepdims=True))
    return exp_terms / jnp.sum(exp_terms, axis=-1, keepdims=True)


def score_grad(probs, grad_probs):
    return (
        probs * (grad_probs - jnp.sum(probs * grad_probs, axis=-1, keepdims=True))
    ).astype(BF)


def head(ref, k):
    return ref[:, k * HD : (k + 1) * HD]


def kernel_call(kernel, out_shape, grid, in_specs, out_specs, flops, name):
    return pl.pallas_call(
        kernel,
        out_shape=out_shape,
        grid=grid,
        in_specs=in_specs,
        out_specs=out_specs,
        compiler_params=pltpu.CompilerParams(vmem_limit_bytes=VMEM),
        cost_estimate=pl.CostEstimate(flops=flops, bytes_accessed=1 << 22, transcendentals=0),
        name=name,
    )


def self_forward(projected, images):
    tokens, width = projected.shape
    rows, group = tokens // images, width // 3
    heads = group // HD
    scale = 1.0 / math.sqrt(HD)

    def kernel(proj, mixed):
        for k in range(heads):
            query, key, value = (head(proj, j * heads + k) for j in range(3))
            probs = softmax(mm_t(query, key) * scale).astype(BF)
            mixed[:, k * HD : (k + 1) * HD] = mm(probs, value).astype(BF)

    return kernel_call(
        kernel,
        jax.ShapeDtypeStruct((tokens, group), BF),
        (images,),
        [pl.BlockSpec((rows, width), lambda i: (i, 0))],
        pl.BlockSpec((rows, group), lambda i: (i, 0)),
        4 * tokens * rows * group,
        "self_forward",
    )(projected)


def self_back(projected, grad_mixed, images):
    tokens, width = projected.shape
    rows, group = tokens // images, width // 3
    heads = group // HD
    scale = 1.0 / math.sqrt(HD)

    def kernel(proj, grad, out):
        for k in range(heads):
            query, key, value = (head(proj, j * heads + k) for j in range(3))
            grad_head = head(grad, k)
            probs = softmax(mm_t(query, key) * scale)
            grad_scores = score_grad(probs, mm_t(grad_head, value))
            parts = (
                mm(grad_scores, key) * scale,
                t_mm(grad_scores, query) * scale,
                t_mm(probs.astype(BF), grad_head),
            )
            for j, part in enumerate(parts):
                at = (j * heads + k) * HD
                out[:, at : at + HD] = part.astype(BF)

    return kernel_call(
        kernel,
        jax.ShapeDtypeStruct((tokens, width), BF),
        (images,),
        [
            pl.BlockSpec((rows, width), lambda i: (i, 0)),
            pl.BlockSpec((rows, group), lambda i: (i, 0)),
        ],
        pl.BlockSpec((rows, width), lambda i: (i, 0)),
        10 * tokens * rows * group,
        "self_back",
    )(projected, grad_mixed)


def cross_forward(queries, text_kv):
    tokens, group = queries.shape
    context = text_kv.shape[0]
    heads = group // HD
    scale = 1.0 / math.sqrt(HD)

    def kernel(query, text, mixed):
        for k in range(heads):
            probs = softmax(mm_t(head(query, k), head(text, k)) * scale).astype(BF)
            mixed[:, k * HD : (k + 1) * HD] = mm(probs, head(text, heads + k)).astype(BF)

    return kernel_call(
        kernel,
        jax.ShapeDtypeStruct((tokens, group), BF),
        (1,),
        [
            pl.BlockSpec((tokens, group), lambda i: (0, 0)),
            pl.BlockSpec((context, 2 * group), lambda i: (0, 0)),
        ],
        pl.BlockSpec((tokens, group), lambda i: (0, 0)),
        4 * tokens * context * group,
        "cross_forward",
    )(queries, text_kv)


def cross_back(queries, text_kv, grad_mixed):
    tokens, group = queries.shape
    context = text_kv.shape[0]
    heads = group // HD
    scale = 1.0 / math.sqrt(HD)

    def kernel(query, text, grad, grad_query, grad_text):
        for k in range(heads):
            query_head, key, value = head(query, k), head(text, k), head(text, heads + k)
            grad_head = head(grad, k)
            probs = softmax(mm_t(query_head, key) * scale)
            grad_scores = score_grad(probs, mm_t(grad_head, value))
            grad_query[:, k * HD : (k + 1) * HD] = (mm(grad_scores, key) * scale).astype(BF)
            at = (heads + k) * HD
            grad_text[:, k * HD : (k + 1) * HD] = t_mm(grad_scores, query_head) * scale
            grad_text[:, at : at + HD] = t_mm(probs.astype(BF), grad_head)

    return kernel_call(
        kernel,
        [
            jax.ShapeDtypeStruct((tokens, group), BF),
            jax.ShapeDtypeStruct((context, 2 * group), F32),
        ],
        (1,),
        [
            pl.BlockSpec((tokens, group), lambda i: (0, 0)),
            pl.BlockSpec((context, 2 * group), lambda i: (0, 0)),
            pl.BlockSpec((tokens, group), lambda i: (0, 0)),
        ],
        [
            pl.BlockSpec((tokens, group), lambda i: (0, 0)),
            pl.BlockSpec((context, 2 * group), lambda i: (0, 0)),
        ],
        10 * tokens * context * group,
        "cross_back",
    )(queries, text_kv, grad_mixed)


def gather_rows(rows):
    return lax.all_gather(rows, DATA, axis=0, tiled=True)


def scatter_grad(partial):
    summed = lax.psum_scatter(partial, DATA, scatter_dimension=0, tiled=True)
    return summed.reshape(4, -1, summed.shape[-1])


def send_rows(blocks, rank):
    return swap_all(
        [lax.dynamic_index_in_dim(blocks, rank ^ k, 0, keepdims=False) for k in range(4)]
    )


def make_local(z_size):
    def sum_data(values):
        values = values + swap(values, "c")
        step = 1
        while step < z_size:
            sent = values.astype(BF)
            got = lax.ppermute(sent, "z", tuple((k, k ^ step) for k in range(z_size)))
            values = sent.astype(F32) + got.astype(F32)
            step *= 2
        return values

    def sum_all(values):
        for axis in ("c", "x", "y"):
            values = values + swap(values, axis)
        step = 1
        while step < z_size:
            values = values + lax.ppermute(
                values, "z", tuple((k, k ^ step) for k in range(z_size))
            )
            step *= 2
        return values

    def feature_swap(values):
        lead = values.shape[:-1]
        shaped = values.reshape(lead + (z_size, 2, 2, -1))
        return jnp.swapaxes(shaped, -3, -2).reshape(values.shape)

    def local(
        hidden,
        mask_index,
        mask_count,
        mask_embed,
        norm_gains,
        caption,
        w_qkv,
        w_out,
        w_cross,
        w_cross_out,
        w_text,
        w_up,
        w_down,
        cotangent,
    ):
        images, local_rows, width = hidden.shape
        full_length = mask_index.shape[1]
        shard_rows = w_qkv.shape[0]
        rank = lax.axis_index("x") * 2 + lax.axis_index("y")
        tokens = images * local_rows
        group = width // 4
        hidden_group = w_up.shape[1] // 4

        qkv_rows = w_qkv.reshape(shard_rows, 3 * width)
        qkv_parts = [
            pieces(qkv_rows[:, j * width : (j + 1) * width], rank, group) for j in range(3)
        ]
        qkv_parts = swap_all(
            [jnp.concatenate([part[k] for part in qkv_parts], axis=1) for k in range(4)]
        )
        qkv = gather_rows(place(qkv_parts, rank, [3 * group])[0])

        positions = lax.axis_index("y") * local_rows + jnp.arange(local_rows, dtype=jnp.int32)
        ranks = jnp.arange(full_length, dtype=jnp.int32)
        matches = (mask_index[:, :, None] == positions[None, None, :]) & (
            ranks[None, :, None] < mask_count[:, None, None]
        )
        masked = jnp.any(matches, axis=1).reshape(tokens, 1)
        gains = feature_swap(norm_gains)
        start_x = jnp.where(
            masked,
            feature_swap(mask_embed),
            feature_swap(hidden.reshape(tokens, width)).astype(F32),
        )
        grad_top = feature_swap(cotangent.reshape(tokens, width)).astype(F32) * masked.astype(F32)
        normed_a, inv_a = normalize(start_x)
        attn_in = gather_tokens((normed_a * gains[0]).astype(BF))

        rest = pack([w_out, w_cross[:, 0], w_cross_out, w_up, w_down], rank)
        mid, up, down = place(swap_all(rest), rank, [3 * group, hidden_group, hidden_group])
        mid = gather_rows(mid)
        up = gather_rows(up)
        down = gather_rows(down)
        out_w, query_w, cross_out_w = (mid[:, k * group : (k + 1) * group] for k in range(3))

        own_text = mm_t(caption, w_text).astype(BF)
        kv_rows = w_cross[:, 1:].reshape(shard_rows, 2 * width)
        kv_part = mm(own_text, kv_rows).astype(BF)
        kv_parts = [pieces(kv_part[:, j * width : (j + 1) * width], rank, group) for j in range(2)]
        kv_parts = swap_all(
            [jnp.concatenate([part[k] for part in kv_parts], axis=1) for k in range(4)]
        )
        text_kv = sum_data(sum(part.astype(F32) for part in kv_parts)).astype(BF)
        grad_y = gather_tokens(grad_top.astype(BF))

        projected = mm(attn_in, qkv).astype(BF)
        self_mixed = self_forward(projected, 2 * images)
        after_attn = start_x + scatter_tokens(mm_t(self_mixed, out_w))

        normed_b, inv_b = normalize(after_attn)
        cross_in = gather_tokens((normed_b * gains[1]).astype(BF))
        cross_queries = mm(cross_in, query_w).astype(BF)
        cross_mixed = cross_forward(cross_queries, text_kv)
        after_cross = after_attn + scatter_tokens(mm_t(cross_mixed, cross_out_w))

        normed_c, inv_c = normalize(after_cross)
        mlp_in = gather_tokens((normed_c * gains[2]).astype(BF))
        pre_act = mm(mlp_in, up)
        activated, gelu_pull = jax.vjp(jax.nn.gelu, pre_act)
        activated = activated.astype(BF)
        down_part = t_mm(grad_y, activated).astype(BF)
        grad_pre = gelu_pull(mm(grad_y, down))[0].astype(BF)
        grad_pre, down_part = lax.optimization_barrier((grad_pre, down_part))
        up_part = t_mm(mlp_in, grad_pre).astype(BF)
        back_part = mm_t(grad_pre, up)
        back_part, up_part = lax.optimization_barrier((back_part, up_part))
        down_rows = scatter_grad(down_part)
        up_rows = scatter_grad(up_part)
        grad_mlp_in = scatter_tokens(back_part)
        result = after_cross + scatter_tokens(mm_t(activated, down))
        output = feature_swap(result.astype(BF))
        back_c, gain_grad_c = norm_back(grad_mlp_in, normed_c, inv_c, gains[2])
        grad_after_cross = grad_top + back_c

        cross_branch = gather_tokens(grad_after_cross.astype(BF))
        grad_cross_mixed = mm(cross_branch, cross_out_w).astype(BF)
        grad_cq, kv_grad = cross_back(cross_queries, text_kv, grad_cross_mixed)
        grad_cross_in = scatter_tokens(mm_t(grad_cq, query_w))
        back_b, gain_grad_b = norm_back(grad_cross_in, normed_b, inv_b, gains[1])
        grad_after_attn = grad_after_cross + back_b

        attn_branch = gather_tokens(grad_after_attn.astype(BF))
        mid_part = jnp.concatenate(
            [
                t_mm(attn_branch, self_mixed).astype(BF),
                t_mm(cross_in, grad_cq).astype(BF),
                t_mm(cross_branch, cross_mixed).astype(BF),
            ],
            axis=1,
        )
        grad_self_mixed = mm(attn_branch, out_w).astype(BF)
        grad_self_mixed, mid_part = lax.optimization_barrier((grad_self_mixed, mid_part))
        mid_rows = scatter_grad(mid_part)
        grad_projected = self_back(projected, grad_self_mixed, 2 * images)
        qkv_part = t_mm(attn_in, grad_projected).astype(BF)
        grad_projected, qkv_part = lax.optimization_barrier((grad_projected, qkv_part))
        qkv_rows = scatter_grad(qkv_part)
        grad_attn_in = scatter_tokens(mm_t(grad_projected, qkv))
        back_a, gain_grad_a = norm_back(grad_attn_in, normed_a, inv_a, gains[0])
        grad_start = grad_after_attn + back_a

        kv_grad = sum_data(kv_grad).astype(BF)
        kv_grads = place(swap_all([kv_grad] * 4), rank, [group, group])
        kv_grads = [
            part.reshape(4, -1, group).transpose(1, 0, 2).reshape(-1, width) for part in kv_grads
        ]
        kv_grads = jnp.concatenate(kv_grads, axis=1)
        kv_weight_grad = t_mm(own_text, kv_grads).reshape(shard_rows, 2, width)
        grad_text = mm_t(kv_grads, kv_rows).astype(BF)
        grad_text_w = t_mm(grad_text, caption)
        caption_part = mm(grad_text, w_text).astype(BF)
        caption_parts = swap_all(pieces(caption_part, rank, caption.shape[1] // 4))
        caption_own = sum_data(sum(part.astype(F32) for part in caption_parts)).astype(BF)
        grad_caption = finish(swap_all([caption_own] * 4), rank, [caption_own.shape[1]])[0]

        down_grad, up_grad = (
            finish(send_rows(rows, rank), rank, [hidden_group])[0] for rows in (down_rows, up_rows)
        )
        out_grad, query_grad, cross_out_grad = finish(
            send_rows(mid_rows, rank), rank, [group] * 3
        )
        qkv_grad = finish_three(send_rows(qkv_rows, rank), rank)
        grad_hidden = feature_swap(jnp.where(masked, 0.0, grad_start).astype(BF))
        mask_part = jnp.sum(jnp.where(masked, grad_start, 0.0), axis=0)
        sums = feature_swap(
            sum_all(jnp.stack([gain_grad_a, gain_grad_b, gain_grad_c, mask_part]))
        )
        grad_cross = jnp.concatenate([query_grad[:, None], kv_weight_grad], axis=1)
        return (
            output.reshape(hidden.shape),
            grad_hidden.reshape(hidden.shape),
            grad_caption,
            sums[:3],
            sums[3],
            qkv_grad,
            out_grad,
            grad_cross,
            cross_out_grad,
            grad_text_w,
            up_grad,
            down_grad,
        )

    return local


def solution(mesh):
    z_size = mesh.shape["img"] // 4
    inner = Mesh(mesh.devices.reshape(z_size, 2, 2, 2), ("z", "x", "c", "y"))
    tokens = P(("z", "x", "c"), "y", None)
    rows = P(("z", "x", "c", "y"))
    in_specs = (
        tokens,
        P(("z", "x", "c"), None),
        P(("z", "x", "c")),
        P(),
        P(),
        P(),
        rows,
        rows,
        rows,
        rows,
        rows,
        rows,
        rows,
        tokens,
    )
    out_specs = (tokens, tokens, P(), P(), P()) + (rows,) * 7
    return jax.shard_map(
        make_local(z_size), mesh=inner, in_specs=in_specs, out_specs=out_specs, check_vma=False
    )
```

```python
import math

import jax
import jax.numpy as jnp
from jax import lax
from jax.experimental import pallas as pl
from jax.experimental.pallas import tpu as pltpu
from jax.sharding import Mesh
from jax.sharding import PartitionSpec as P

HD = 128
EPS = 1e-05
BF = jnp.bfloat16
F32 = jnp.float32
PAIR = ((0, 1), (1, 0))
DIAG = ((0, 3), (1, 2), (2, 1), (3, 0))
DATA = ("z", "c")
VMEM = 40 * 1024 * 1024


def dot(a, b, dims):
    return lax.dot_general(a, b, (dims, ((), ())), preferred_element_type=F32)


def mm(a, b):
    return dot(a, b, ((1,), (0,)))


def mm_t(a, b):
    return dot(a, b, ((1,), (1,)))


def t_mm(a, b):
    return dot(a, b, ((0,), (0,)))


def normalize(values):
    centred = values - jnp.mean(values, axis=-1, keepdims=True)
    inv_std = lax.rsqrt(jnp.mean(centred * centred, axis=-1, keepdims=True) + EPS)
    return centred * inv_std, inv_std


def norm_back(grad_normed, normed, inv_std, gain):
    scaled = grad_normed * gain
    first_mean = jnp.mean(scaled, axis=-1, keepdims=True)
    second_mean = jnp.mean(scaled * normed, axis=-1, keepdims=True)
    return (
        inv_std * (scaled - first_mean - normed * second_mean),
        jnp.sum(grad_normed * normed, axis=0),
    )


def swap(values, axis):
    return lax.ppermute(values, axis, PAIR)


def swap_diag(values):
    return lax.ppermute(values, ("x", "y"), DIAG)


def gather_tokens(own):
    half = own.shape[0] // 2
    from_x = swap(own, "x")
    from_y = swap(own, "y")
    diag_low = swap(from_x[:half], "y")
    diag_high = swap(from_y[half:], "x")
    return jnp.concatenate([own, from_y, from_x, diag_low, diag_high], axis=0)


def scatter_tokens(partial):
    rows = partial.shape[0] // 4
    half = rows // 2
    own, for_y, for_x, for_diag = (partial[k * rows : (k + 1) * rows] for k in range(4))
    for_diag = for_diag.astype(BF)
    diag_low = swap(for_diag[:half], "y").astype(F32)
    diag_high = swap(for_diag[half:], "x").astype(F32)
    from_x = swap(
        jnp.concatenate([for_x[:half] + diag_low, for_x[half:]], axis=0).astype(BF), "x"
    )
    from_y = swap(
        jnp.concatenate([for_y[:half], for_y[half:] + diag_high], axis=0).astype(BF), "y"
    )
    return own + from_x.astype(F32) + from_y.astype(F32)


def swap_all(parts):
    return [parts[0], swap(parts[1], "y"), swap(parts[2], "x"), swap_diag(parts[3])]


def pieces(values, rank, width):
    return [
        lax.dynamic_slice_in_dim(values, (rank ^ k) * width, width, 1) for k in range(4)
    ]


def grid_spec(in_specs, out_specs):
    return pltpu.PrefetchScalarGridSpec(
        num_scalar_prefetch=1, grid=(4,), in_specs=in_specs, out_specs=out_specs
    )


def pack(weights, rank):
    rows = weights[0].shape[0]
    widths = [w.shape[1] // 4 for w in weights]
    total = sum(widths)

    def kernel(rank_ref, *refs):
        step = pl.program_id(0)
        for k in range(4):

            @pl.when(step == k)
            def _():
                offset = 0
                for ref, width in zip(refs, widths):
                    refs[len(widths) + k][:, offset : offset + width] = ref[...]
                    offset += width

    return pl.pallas_call(
        kernel,
        out_shape=[jax.ShapeDtypeStruct((rows, total), BF)] * 4,
        grid_spec=grid_spec(
            [pl.BlockSpec((rows, w), lambda k, r: (0, k ^ r[0])) for w in widths],
            [pl.BlockSpec((rows, total), lambda k, r: (0, 0))] * 4,
        ),
        compiler_params=pltpu.CompilerParams(vmem_limit_bytes=VMEM),
        name="pack",
    )(rank.reshape(1), *weights)


def place(parts, rank, widths):
    rows, total = parts[0].shape

    def kernel(rank_ref, *refs):
        step = pl.program_id(0)
        for k in range(4):

            @pl.when(step == k)
            def _():
                offset = 0
                for ref, width in zip(refs[4:], widths):
                    ref[...] = refs[k][:, offset : offset + width]
                    offset += width

    return pl.pallas_call(
        kernel,
        out_shape=[jax.ShapeDtypeStruct((4 * rows, w), BF) for w in widths],
        grid_spec=grid_spec(
            [pl.BlockSpec((rows, total), lambda k, r: (0, 0))] * 4,
            [pl.BlockSpec((rows, w), lambda k, r: (k ^ r[0], 0)) for w in widths],
        ),
        compiler_params=pltpu.CompilerParams(vmem_limit_bytes=VMEM),
        name="place",
    )(rank.reshape(1), *parts)


def finish(parts, rank, widths, lead=0):
    rows, total = parts[0].shape
    first = widths[0]

    def kernel(rank_ref, *refs):
        step = pl.program_id(0)
        for k in range(4):

            @pl.when(step == k)
            def _():
                outs = refs[4:]
                offset = lead * first
                if lead:
                    for j in range(lead):
                        outs[0][:, j, :] = refs[k][:, j * first : (j + 1) * first].astype(F32)
                    outs = outs[1:]
                for ref, width in zip(outs, widths):
                    ref[...] = refs[k][:, offset : offset + width].astype(F32)
                    offset += width

    shapes = [jax.ShapeDtypeStruct((rows, 4 * w), F32) for w in widths]
    specs = [pl.BlockSpec((rows, w), lambda k, r: (0, k ^ r[0])) for w in widths]
    if lead:
        shapes = [jax.ShapeDtypeStruct((rows, lead, 4 * first), F32)] + shapes
        specs = [pl.BlockSpec((rows, lead, first), lambda k, r: (0, 0, k ^ r[0]))] + specs
    return pl.pallas_call(
        kernel,
        out_shape=shapes,
        grid_spec=grid_spec([pl.BlockSpec((rows, total), lambda k, r: (0, 0))] * 4, specs),
        compiler_params=pltpu.CompilerParams(vmem_limit_bytes=VMEM),
        name="finish",
    )(rank.reshape(1), *parts)


def softmax(scores):
    exp_terms = jnp.exp(scores - jnp.max(scores, axis=-1, keepdims=True))
    return exp_terms / jnp.sum(exp_terms, axis=-1, keepdims=True)


def score_grad(probs, grad_probs):
    return (
        probs * (grad_probs - jnp.sum(probs * grad_probs, axis=-1, keepdims=True))
    ).astype(BF)


def head(ref, k):
    return ref[:, k * HD : (k + 1) * HD]


def kernel_call(kernel, out_shape, grid, in_specs, out_specs, flops, name):
    return pl.pallas_call(
        kernel,
        out_shape=out_shape,
        grid=grid,
        in_specs=in_specs,
        out_specs=out_specs,
        compiler_params=pltpu.CompilerParams(vmem_limit_bytes=VMEM),
        cost_estimate=pl.CostEstimate(flops=flops, bytes_accessed=1 << 22, transcendentals=0),
        name=name,
    )


def self_forward(projected, images):
    tokens, width = projected.shape
    rows, group = tokens // images, width // 3
    heads = group // HD
    scale = 1.0 / math.sqrt(HD)

    def kernel(proj, mixed):
        for k in range(heads):
            query, key, value = (head(proj, j * heads + k) for j in range(3))
            probs = softmax(mm_t(query, key) * scale).astype(BF)
            mixed[:, k * HD : (k + 1) * HD] = mm(probs, value).astype(BF)

    return kernel_call(
        kernel,
        jax.ShapeDtypeStruct((tokens, group), BF),
        (images,),
        [pl.BlockSpec((rows, width), lambda i: (i, 0))],
        pl.BlockSpec((rows, group), lambda i: (i, 0)),
        4 * tokens * rows * group,
        "self_forward",
    )(projected)


def self_back(projected, grad_mixed, images):
    tokens, width = projected.shape
    rows, group = tokens // images, width // 3
    heads = group // HD
    scale = 1.0 / math.sqrt(HD)

    def kernel(proj, grad, out):
        for k in range(heads):
            query, key, value = (head(proj, j * heads + k) for j in range(3))
            grad_head = head(grad, k)
            probs = softmax(mm_t(query, key) * scale)
            grad_scores = score_grad(probs, mm_t(grad_head, value))
            parts = (
                mm(grad_scores, key) * scale,
                t_mm(grad_scores, query) * scale,
                t_mm(probs.astype(BF), grad_head),
            )
            for j, part in enumerate(parts):
                at = (j * heads + k) * HD
                out[:, at : at + HD] = part.astype(BF)

    return kernel_call(
        kernel,
        jax.ShapeDtypeStruct((tokens, width), BF),
        (images,),
        [
            pl.BlockSpec((rows, width), lambda i: (i, 0)),
            pl.BlockSpec((rows, group), lambda i: (i, 0)),
        ],
        pl.BlockSpec((rows, width), lambda i: (i, 0)),
        10 * tokens * rows * group,
        "self_back",
    )(projected, grad_mixed)


def cross_forward(queries, text_kv):
    tokens, group = queries.shape
    context = text_kv.shape[0]
    heads = group // HD
    scale = 1.0 / math.sqrt(HD)

    def kernel(query, text, mixed):
        for k in range(heads):
            probs = softmax(mm_t(head(query, k), head(text, k)) * scale).astype(BF)
            mixed[:, k * HD : (k + 1) * HD] = mm(probs, head(text, heads + k)).astype(BF)

    return kernel_call(
        kernel,
        jax.ShapeDtypeStruct((tokens, group), BF),
        (1,),
        [
            pl.BlockSpec((tokens, group), lambda i: (0, 0)),
            pl.BlockSpec((context, 2 * group), lambda i: (0, 0)),
        ],
        pl.BlockSpec((tokens, group), lambda i: (0, 0)),
        4 * tokens * context * group,
        "cross_forward",
    )(queries, text_kv)


def cross_back(queries, text_kv, grad_mixed):
    tokens, group = queries.shape
    context = text_kv.shape[0]
    heads = group // HD
    scale = 1.0 / math.sqrt(HD)

    def kernel(query, text, grad, grad_query, grad_text):
        for k in range(heads):
            query_head, key, value = head(query, k), head(text, k), head(text, heads + k)
            grad_head = head(grad, k)
            probs = softmax(mm_t(query_head, key) * scale)
            grad_scores = score_grad(probs, mm_t(grad_head, value))
            grad_query[:, k * HD : (k + 1) * HD] = (mm(grad_scores, key) * scale).astype(BF)
            at = (heads + k) * HD
            grad_text[:, k * HD : (k + 1) * HD] = t_mm(grad_scores, query_head) * scale
            grad_text[:, at : at + HD] = t_mm(probs.astype(BF), grad_head)

    return kernel_call(
        kernel,
        [
            jax.ShapeDtypeStruct((tokens, group), BF),
            jax.ShapeDtypeStruct((context, 2 * group), F32),
        ],
        (1,),
        [
            pl.BlockSpec((tokens, group), lambda i: (0, 0)),
            pl.BlockSpec((context, 2 * group), lambda i: (0, 0)),
            pl.BlockSpec((tokens, group), lambda i: (0, 0)),
        ],
        [
            pl.BlockSpec((tokens, group), lambda i: (0, 0)),
            pl.BlockSpec((context, 2 * group), lambda i: (0, 0)),
        ],
        10 * tokens * context * group,
        "cross_back",
    )(queries, text_kv, grad_mixed)


def grad_products(pairs):
    tokens, width = pairs[0][0].shape
    count = len(pairs)
    widths = [y.shape[1] for _, y in pairs]
    total = sum(widths)
    rows = 256
    step = 512

    def kernel(*refs):
        out = refs[2 * count]
        offset = 0
        for k, wide in enumerate(widths):
            left = refs[k][...].T
            for at in range(0, wide, step):
                out[:, offset + at : offset + at + step] = mm(
                    left, refs[count + k][:, at : at + step]
                ).astype(BF)
            offset += wide

    return kernel_call(
        kernel,
        jax.ShapeDtypeStruct((width, total), BF),
        (width // rows,),
        [pl.BlockSpec((tokens, rows), lambda i: (0, i))] * count
        + [pl.BlockSpec((tokens, w), lambda i: (0, 0)) for w in widths],
        pl.BlockSpec((rows, total), lambda i: (i, 0)),
        2 * tokens * width * total,
        "grad_products",
    )(*[x for x, _ in pairs], *[y for _, y in pairs])


def gather_rows(rows):
    return lax.all_gather(rows, DATA, axis=0, tiled=True)


def scatter_grad(partial):
    summed = lax.psum_scatter(partial, DATA, scatter_dimension=0, tiled=True)
    return summed.reshape(4, -1, summed.shape[-1])


def send_rows(blocks, rank):
    return swap_all(
        [lax.dynamic_index_in_dim(blocks, rank ^ k, 0, keepdims=False) for k in range(4)]
    )


def make_local(z_size):
    def sum_data(values):
        values = values + swap(values, "c")
        step = 1
        while step < z_size:
            sent = values.astype(BF)
            got = lax.ppermute(sent, "z", tuple((k, k ^ step) for k in range(z_size)))
            values = sent.astype(F32) + got.astype(F32)
            step *= 2
        return values

    def sum_all(values):
        for axis in ("c", "x", "y"):
            values = values + swap(values, axis)
        step = 1
        while step < z_size:
            values = values + lax.ppermute(
                values, "z", tuple((k, k ^ step) for k in range(z_size))
            )
            step *= 2
        return values

    def feature_swap(values):
        lead = values.shape[:-1]
        shaped = values.reshape(lead + (z_size, 2, 2, -1))
        return jnp.swapaxes(shaped, -3, -2).reshape(values.shape)

    def local(
        hidden,
        mask_index,
        mask_count,
        mask_embed,
        norm_gains,
        caption,
        w_qkv,
        w_out,
        w_cross,
        w_cross_out,
        w_text,
        w_up,
        w_down,
        cotangent,
    ):
        images, local_rows, width = hidden.shape
        full_length = mask_index.shape[1]
        shard_rows = w_qkv.shape[0]
        rank = lax.axis_index("x") * 2 + lax.axis_index("y")
        tokens = images * local_rows
        group = width // 4
        hidden_group = w_up.shape[1] // 4

        first = [w_qkv.reshape(shard_rows, 3 * width)[:, j * width : (j + 1) * width] for j in range(3)]
        first = [pieces(weight, rank, group) for weight in first + [w_out]]
        first = swap_all(
            [jnp.concatenate([part[k] for part in first], axis=1) for k in range(4)]
        )
        first = gather_rows(place(first, rank, [4 * group])[0])
        qkv, out_w = first[:, : 3 * group], first[:, 3 * group :]

        positions = lax.axis_index("y") * local_rows + jnp.arange(local_rows, dtype=jnp.int32)
        ranks = jnp.arange(full_length, dtype=jnp.int32)
        matches = (mask_index[:, :, None] == positions[None, None, :]) & (
            ranks[None, :, None] < mask_count[:, None, None]
        )
        masked = jnp.any(matches, axis=1).reshape(tokens, 1)
        gains = feature_swap(norm_gains)
        start_x = jnp.where(
            masked,
            feature_swap(mask_embed),
            feature_swap(hidden.reshape(tokens, width)).astype(F32),
        )
        grad_top = feature_swap(cotangent.reshape(tokens, width)).astype(F32) * masked.astype(F32)
        normed_a, inv_a = normalize(start_x)
        attn_in = gather_tokens((normed_a * gains[0]).astype(BF))

        rest = pack([w_cross[:, 0], w_cross_out, w_up, w_down], rank)
        mid, up, down = place(swap_all(rest), rank, [2 * group, hidden_group, hidden_group])
        mid = gather_rows(mid)
        up = gather_rows(up)
        down = gather_rows(down)
        query_w, cross_out_w = mid[:, :group], mid[:, group:]

        own_text = mm_t(caption, w_text).astype(BF)
        kv_rows = w_cross[:, 1:].reshape(shard_rows, 2 * width)
        kv_part = mm(own_text, kv_rows).astype(BF)
        kv_parts = [pieces(kv_part[:, j * width : (j + 1) * width], rank, group) for j in range(2)]
        kv_parts = swap_all(
            [jnp.concatenate([part[k] for part in kv_parts], axis=1) for k in range(4)]
        )
        text_kv = sum_data(sum(part.astype(F32) for part in kv_parts)).astype(BF)
        grad_y = gather_tokens(grad_top.astype(BF))
        attn_in, text_kv, grad_y = lax.optimization_barrier((attn_in, text_kv, grad_y))

        projected = mm(attn_in, qkv).astype(BF)
        self_mixed = self_forward(projected, 2 * images)
        after_attn = start_x + scatter_tokens(mm_t(self_mixed, out_w))

        normed_b, inv_b = normalize(after_attn)
        cross_in = gather_tokens((normed_b * gains[1]).astype(BF))
        cross_queries = mm(cross_in, query_w).astype(BF)
        cross_mixed = cross_forward(cross_queries, text_kv)
        after_cross = after_attn + scatter_tokens(mm_t(cross_mixed, cross_out_w))

        normed_c, inv_c = normalize(after_cross)
        mlp_in = gather_tokens((normed_c * gains[2]).astype(BF))
        pre_act = mm(mlp_in, up)
        activated, gelu_pull = jax.vjp(jax.nn.gelu, pre_act)
        activated = activated.astype(BF)
        grad_pre = gelu_pull(mm(grad_y, down))[0].astype(BF)
        back_part = mm_t(grad_pre, up)
        grad_pre, back_part = lax.optimization_barrier((grad_pre, back_part))
        mlp_part = grad_products([(grad_y, activated), (mlp_in, grad_pre)])
        mlp_rows = scatter_grad(mlp_part)
        grad_mlp_in = scatter_tokens(back_part)
        back_c, gain_grad_c = norm_back(grad_mlp_in, normed_c, inv_c, gains[2])
        grad_after_cross = grad_top + back_c

        cross_branch = gather_tokens(grad_after_cross.astype(BF))
        grad_cross_mixed = mm(cross_branch, cross_out_w).astype(BF)
        grad_cq, kv_grad = cross_back(cross_queries, text_kv, grad_cross_mixed)
        grad_cross_in = scatter_tokens(mm_t(grad_cq, query_w))
        back_b, gain_grad_b = norm_back(grad_cross_in, normed_b, inv_b, gains[1])
        grad_after_attn = grad_after_cross + back_b

        attn_branch = gather_tokens(grad_after_attn.astype(BF))
        grad_self_mixed = mm(attn_branch, out_w).astype(BF)
        grad_projected = self_back(projected, grad_self_mixed, 2 * images)
        attn_part = grad_products(
            [
                (attn_in, grad_projected),
                (attn_branch, self_mixed),
                (cross_in, grad_cq),
                (cross_branch, cross_mixed),
            ]
        )
        attn_part, mlp_rows = lax.optimization_barrier((attn_part, mlp_rows))
        attn_rows = scatter_grad(attn_part)
        grad_projected, activated, kv_grad, attn_part = lax.optimization_barrier(
            (grad_projected, activated, kv_grad, attn_part)
        )
        grad_attn_in = scatter_tokens(mm_t(grad_projected, qkv))
        back_a, gain_grad_a = norm_back(grad_attn_in, normed_a, inv_a, gains[0])
        grad_start = grad_after_attn + back_a
        result = after_cross + scatter_tokens(mm_t(activated, down))
        output = feature_swap(result.astype(BF))

        kv_grad = sum_data(kv_grad).astype(BF)
        kv_grads = place(swap_all([kv_grad] * 4), rank, [group, group])
        kv_grads = [
            part.reshape(4, -1, group).transpose(1, 0, 2).reshape(-1, width) for part in kv_grads
        ]
        kv_grads = jnp.concatenate(kv_grads, axis=1)
        kv_weight_grad = t_mm(own_text, kv_grads).reshape(shard_rows, 2, width)
        grad_text = mm_t(kv_grads, kv_rows).astype(BF)
        grad_text_w = t_mm(grad_text, caption)
        caption_part = mm(grad_text, w_text).astype(BF)
        caption_parts = swap_all(pieces(caption_part, rank, caption.shape[1] // 4))
        caption_own = sum_data(sum(part.astype(F32) for part in caption_parts)).astype(BF)
        grad_caption = finish(swap_all([caption_own] * 4), rank, [caption_own.shape[1]])[0]

        down_grad, up_grad = finish(send_rows(mlp_rows, rank), rank, [hidden_group] * 2)
        qkv_grad, out_grad, query_grad, cross_out_grad = finish(
            send_rows(attn_rows, rank), rank, [group] * 3, 3
        )
        grad_hidden = feature_swap(jnp.where(masked, 0.0, grad_start).astype(BF))
        mask_part = jnp.sum(jnp.where(masked, grad_start, 0.0), axis=0)
        sums = feature_swap(
            sum_all(jnp.stack([gain_grad_a, gain_grad_b, gain_grad_c, mask_part]))
        )
        grad_cross = jnp.concatenate([query_grad[:, None], kv_weight_grad], axis=1)
        return (
            output.reshape(hidden.shape),
            grad_hidden.reshape(hidden.shape),
            grad_caption,
            sums[:3],
            sums[3],
            qkv_grad,
            out_grad,
            grad_cross,
            cross_out_grad,
            grad_text_w,
            up_grad,
            down_grad,
        )

    return local


def solution(mesh):
    z_size = mesh.shape["img"] // 4
    inner = Mesh(mesh.devices.reshape(z_size, 2, 2, 2), ("z", "x", "c", "y"))
    tokens = P(("z", "x", "c"), "y", None)
    rows = P(("z", "x", "c", "y"))
    in_specs = (
        tokens,
        P(("z", "x", "c"), None),
        P(("z", "x", "c")),
        P(),
        P(),
        P(),
        rows,
        rows,
        rows,
        rows,
        rows,
        rows,
        rows,
        tokens,
    )
    out_specs = (tokens, tokens, P(), P(), P()) + (rows,) * 7
    return jax.shard_map(
        make_local(z_size), mesh=inner, in_specs=in_specs, out_specs=out_specs, check_vma=False
    )
```

```python
import math

import jax
import jax.numpy as jnp
from jax import lax
from jax.experimental import pallas as pl
from jax.experimental.pallas import tpu as pltpu
from jax.sharding import Mesh
from jax.sharding import PartitionSpec as P

HD = 128
EPS = 1e-05
BF = jnp.bfloat16
F32 = jnp.float32
PAIR = ((0, 1), (1, 0))
DIAG = ((0, 3), (1, 2), (2, 1), (3, 0))
DATA = ("w", "c", "z")
PAIR_DATA = ("w", "c")
VMEM = 40 * 1024 * 1024


def dot(a, b, dims):
    return lax.dot_general(a, b, (dims, ((), ())), preferred_element_type=F32)


def mm(a, b):
    return dot(a, b, ((1,), (0,)))


def mm_t(a, b):
    return dot(a, b, ((1,), (1,)))


def t_mm(a, b):
    return dot(a, b, ((0,), (0,)))


def normalize(values):
    centred = values - jnp.mean(values, axis=-1, keepdims=True)
    inv_std = lax.rsqrt(jnp.mean(centred * centred, axis=-1, keepdims=True) + EPS)
    return centred * inv_std, inv_std


def norm_back(grad_normed, normed, inv_std, gain):
    scaled = grad_normed * gain
    first_mean = jnp.mean(scaled, axis=-1, keepdims=True)
    second_mean = jnp.mean(scaled * normed, axis=-1, keepdims=True)
    return (
        inv_std * (scaled - first_mean - normed * second_mean),
        jnp.sum(grad_normed * normed, axis=0),
    )


def swap(values, axis):
    return lax.ppermute(values, axis, PAIR)


def swap_diag(values):
    return lax.ppermute(values, ("x", "y"), DIAG)


def gather_tokens(own):
    half = own.shape[0] // 2
    from_x = swap(own, "x")
    from_y = swap(own, "y")
    diag_low = swap(from_x[:half], "y")
    diag_high = swap(from_y[half:], "x")
    return jnp.concatenate([own, from_y, from_x, diag_low, diag_high], axis=0)


def scatter_tokens(partial):
    rows = partial.shape[0] // 4
    half = rows // 2
    own, for_y, for_x, for_diag = (partial[k * rows : (k + 1) * rows] for k in range(4))
    for_diag = for_diag.astype(BF)
    diag_low = swap(for_diag[:half], "y").astype(F32)
    diag_high = swap(for_diag[half:], "x").astype(F32)
    from_x = swap(
        jnp.concatenate([for_x[:half] + diag_low, for_x[half:]], axis=0).astype(BF), "x"
    )
    from_y = swap(
        jnp.concatenate([for_y[:half], for_y[half:] + diag_high], axis=0).astype(BF), "y"
    )
    return own + from_x.astype(F32) + from_y.astype(F32)


def gather_pair(own):
    return gather_tokens(own), gather_tokens(swap(own, "z"))


def scatter_pair(near, far):
    far = scatter_tokens(far).astype(BF)
    return scatter_tokens(near) + swap(far, "z").astype(F32)


def swap_all(parts):
    return [parts[0], swap(parts[1], "y"), swap(parts[2], "x"), swap_diag(parts[3])]


def pieces(values, rank, width):
    return [
        lax.dynamic_slice_in_dim(values, (rank ^ k) * width, width, 1) for k in range(4)
    ]


def block_call(kernel, steps, out_shape, in_specs, out_specs, rank, operands, name):
    return pl.pallas_call(
        kernel,
        out_shape=out_shape,
        grid_spec=pltpu.PrefetchScalarGridSpec(
            num_scalar_prefetch=1, grid=(steps,), in_specs=in_specs, out_specs=out_specs
        ),
        compiler_params=pltpu.CompilerParams(vmem_limit_bytes=VMEM),
        name=name,
    )(rank.reshape(1), *operands)


def whole(array):
    return pl.BlockSpec(array.shape, lambda k, r: (0,) * len(array.shape))


def pack(cross, wide, rank):
    rows = wide[0].shape[0]
    cross_width, width = cross[0].shape[1] // 4, wide[0].shape[1] // 8
    weights = cross + wide
    widths = [cross_width] * len(cross) + [width] * len(wide)
    total, far_total = sum(widths), width * len(wide)
    count = len(weights)

    def kernel(rank_ref, *refs):
        step = pl.program_id(0)
        for k in range(4):

            @pl.when(step == k)
            def _():
                offset = 0
                for ref, w in zip(refs, widths):
                    refs[count + k][:, offset : offset + w] = ref[...]
                    offset += w

            @pl.when(step == 4 + k)
            def _():
                for j in range(len(wide)):
                    refs[count + 4][k * rows : (k + 1) * rows, j * width : (j + 1) * width] = refs[
                        len(cross) + j
                    ][...]

    shapes = [jax.ShapeDtypeStruct((rows, total), BF)] * 4
    shapes.append(jax.ShapeDtypeStruct((4 * rows, far_total), BF))
    *near, far = block_call(
        kernel,
        8,
        shapes,
        [pl.BlockSpec((rows, cross_width), lambda k, r: (0, (k ^ r[0]) & 3))] * len(cross)
        + [pl.BlockSpec((rows, width), lambda k, r: (0, k ^ r[0]))] * len(wide),
        [whole(shape) for shape in shapes],
        rank,
        weights,
        "pack",
    )
    return near, far


def place(pieces, rank, widths):
    rows, starts, arrays = block_rows(pieces)
    count = len(arrays)

    def kernel(rank_ref, *refs):
        step = pl.program_id(0)
        for k, (which, row, offset) in enumerate(starts):

            @pl.when(step == k)
            def _():
                at = offset
                for ref, width in zip(refs[count:], widths):
                    ref[...] = refs[which][row : row + rows, at : at + width]
                    at += width

    return block_call(
        kernel,
        len(pieces),
        [jax.ShapeDtypeStruct((len(pieces) * rows, w), BF) for w in widths],
        [whole(array) for array in arrays],
        [pl.BlockSpec((rows, w), lambda k, r: (k ^ r[0], 0)) for w in widths],
        rank,
        arrays,
        "place",
    )


def block_rows(pieces):
    arrays, starts = [], []
    for array, row, column in pieces:
        found = [k for k, other in enumerate(arrays) if other is array]
        if not found:
            arrays.append(array)
        starts.append((found[0] if found else len(arrays) - 1, row, column))
    rows = min([array.shape[0] for array in arrays] + [s[1] for s in starts if s[1]])
    return rows, starts, arrays


def finish(pieces, rank, widths, lead=0):
    rows, starts, arrays = block_rows(pieces)
    blocks = len(pieces)
    first = widths[0]
    count = len(arrays)

    def kernel(rank_ref, *refs):
        step = pl.program_id(0)
        for k, (which, row, offset) in enumerate(starts):

            @pl.when(step == k)
            def _():
                outs = refs[count:]
                at = offset
                if lead:
                    for j in range(lead):
                        outs[0][:, j, :] = refs[which][row : row + rows, at : at + first].astype(F32)
                        at += first
                    outs = outs[1:]
                for ref, width in zip(outs, widths):
                    ref[...] = refs[which][row : row + rows, at : at + width].astype(F32)
                    at += width

    shapes = [jax.ShapeDtypeStruct((rows, blocks * w), F32) for w in widths]
    specs = [pl.BlockSpec((rows, w), lambda k, r: (0, k ^ r[0])) for w in widths]
    if lead:
        shapes = [jax.ShapeDtypeStruct((rows, lead, blocks * first), F32)] + shapes
        specs = [pl.BlockSpec((rows, lead, first), lambda k, r: (0, 0, k ^ r[0]))] + specs
    return block_call(
        kernel, blocks, shapes, [whole(a) for a in arrays], specs, rank, arrays, "finish"
    )


def softmax(scores):
    exp_terms = jnp.exp(scores - jnp.max(scores, axis=-1, keepdims=True))
    return exp_terms / jnp.sum(exp_terms, axis=-1, keepdims=True)


def score_grad(probs, grad_probs):
    return (
        probs * (grad_probs - jnp.sum(probs * grad_probs, axis=-1, keepdims=True))
    ).astype(BF)


def head(ref, k):
    return ref[:, k * HD : (k + 1) * HD]


def kernel_call(kernel, out_shape, grid, in_specs, out_specs, flops, name):
    return pl.pallas_call(
        kernel,
        out_shape=out_shape,
        grid=grid,
        in_specs=in_specs,
        out_specs=out_specs,
        compiler_params=pltpu.CompilerParams(vmem_limit_bytes=VMEM),
        cost_estimate=pl.CostEstimate(flops=flops, bytes_accessed=1 << 22, transcendentals=0),
        name=name,
    )


def self_forward(projected, images):
    tokens, width = projected.shape
    rows, group = tokens // images, width // 3
    heads = group // HD
    scale = 1.0 / math.sqrt(HD)

    def kernel(proj, mixed):
        for k in range(heads):
            query, key, value = (head(proj, j * heads + k) for j in range(3))
            probs = softmax(mm_t(query, key) * scale).astype(BF)
            mixed[:, k * HD : (k + 1) * HD] = mm(probs, value).astype(BF)

    return kernel_call(
        kernel,
        jax.ShapeDtypeStruct((tokens, group), BF),
        (images,),
        [pl.BlockSpec((rows, width), lambda i: (i, 0))],
        pl.BlockSpec((rows, group), lambda i: (i, 0)),
        4 * tokens * rows * group,
        "self_forward",
    )(projected)


def self_back(projected, grad_mixed, images):
    tokens, width = projected.shape
    rows, group = tokens // images, width // 3
    heads = group // HD
    scale = 1.0 / math.sqrt(HD)

    def kernel(proj, grad, out):
        for k in range(heads):
            query, key, value = (head(proj, j * heads + k) for j in range(3))
            grad_head = head(grad, k)
            probs = softmax(mm_t(query, key) * scale)
            grad_scores = score_grad(probs, mm_t(grad_head, value))
            parts = (
                mm(grad_scores, key) * scale,
                t_mm(grad_scores, query) * scale,
                t_mm(probs.astype(BF), grad_head),
            )
            for j, part in enumerate(parts):
                at = (j * heads + k) * HD
                out[:, at : at + HD] = part.astype(BF)

    return kernel_call(
        kernel,
        jax.ShapeDtypeStruct((tokens, width), BF),
        (images,),
        [
            pl.BlockSpec((rows, width), lambda i: (i, 0)),
            pl.BlockSpec((rows, group), lambda i: (i, 0)),
        ],
        pl.BlockSpec((rows, width), lambda i: (i, 0)),
        10 * tokens * rows * group,
        "self_back",
    )(projected, grad_mixed)


def cross_forward(queries, text_kv):
    tokens, group = queries.shape
    context = text_kv.shape[0]
    heads = group // HD
    scale = 1.0 / math.sqrt(HD)

    def kernel(query, text, mixed):
        for k in range(heads):
            probs = softmax(mm_t(head(query, k), head(text, k)) * scale).astype(BF)
            mixed[:, k * HD : (k + 1) * HD] = mm(probs, head(text, heads + k)).astype(BF)

    return kernel_call(
        kernel,
        jax.ShapeDtypeStruct((tokens, group), BF),
        (1,),
        [
            pl.BlockSpec((tokens, group), lambda i: (0, 0)),
            pl.BlockSpec((context, 2 * group), lambda i: (0, 0)),
        ],
        pl.BlockSpec((tokens, group), lambda i: (0, 0)),
        4 * tokens * context * group,
        "cross_forward",
    )(queries, text_kv)


def cross_back(queries, text_kv, grad_mixed):
    tokens, group = queries.shape
    context = text_kv.shape[0]
    heads = group // HD
    scale = 1.0 / math.sqrt(HD)

    def kernel(query, text, grad, grad_query, grad_text):
        for k in range(heads):
            query_head, key, value = head(query, k), head(text, k), head(text, heads + k)
            grad_head = head(grad, k)
            probs = softmax(mm_t(query_head, key) * scale)
            grad_scores = score_grad(probs, mm_t(grad_head, value))
            grad_query[:, k * HD : (k + 1) * HD] = (mm(grad_scores, key) * scale).astype(BF)
            at = (heads + k) * HD
            grad_text[:, k * HD : (k + 1) * HD] = t_mm(grad_scores, query_head) * scale
            grad_text[:, at : at + HD] = t_mm(probs.astype(BF), grad_head)

    return kernel_call(
        kernel,
        [
            jax.ShapeDtypeStruct((tokens, group), BF),
            jax.ShapeDtypeStruct((context, 2 * group), F32),
        ],
        (1,),
        [
            pl.BlockSpec((tokens, group), lambda i: (0, 0)),
            pl.BlockSpec((context, 2 * group), lambda i: (0, 0)),
            pl.BlockSpec((tokens, group), lambda i: (0, 0)),
        ],
        [
            pl.BlockSpec((tokens, group), lambda i: (0, 0)),
            pl.BlockSpec((context, 2 * group), lambda i: (0, 0)),
        ],
        10 * tokens * context * group,
        "cross_back",
    )(queries, text_kv, grad_mixed)


def grad_products(pairs):
    blocks = len(pairs[0][0])
    tokens, width = pairs[0][0][0].shape
    widths = [y[0].shape[1] for _, y in pairs]
    total = sum(widths)
    rows = 256
    step = 512
    count = len(pairs) * blocks

    def kernel(*refs):
        out = refs[2 * count]
        offset = 0
        for k, wide in enumerate(widths):
            left = [refs[k * blocks + b][...].T for b in range(blocks)]
            for at in range(0, wide, step):
                out[:, offset + at : offset + at + step] = sum(
                    mm(left[b], refs[count + k * blocks + b][:, at : at + step])
                    for b in range(blocks)
                ).astype(BF)
            offset += wide

    return kernel_call(
        kernel,
        jax.ShapeDtypeStruct((width, total), BF),
        (width // rows,),
        [pl.BlockSpec((tokens, rows), lambda i: (0, i))] * count
        + [pl.BlockSpec((tokens, w), lambda i: (0, 0)) for w in widths for _ in range(blocks)],
        pl.BlockSpec((rows, total), lambda i: (i, 0)),
        2 * tokens * blocks * width * total,
        "grad_products",
    )(*[b for x, _ in pairs for b in x], *[b for _, y in pairs for b in y])


def gather_rows(rows, axes):
    return lax.all_gather(rows, axes, axis=0, tiled=True)


def scatter_grad(partial, axes):
    return lax.psum_scatter(partial, axes, scatter_dimension=0, tiled=True)


def pick_rows(values, rank, count):
    rows = values.shape[0] // count
    return [
        lax.dynamic_slice_in_dim(values, (rank ^ k) * rows, rows, 0) for k in range(count)
    ]


def make_local(z_size):
    z_axes = ("w", "z")

    def sum_z(values):
        terms = [values] + [
            lax.ppermute(values, z_axes, tuple((k, k ^ m) for k in range(z_size)))
            for m in range(1, z_size)
        ]
        terms = [term.astype(F32) for term in terms]
        while len(terms) > 1:
            terms = [terms[k] + terms[k + 1] for k in range(0, len(terms), 2)]
        return terms[0]

    def sum_data(values):
        core = lax.axis_index("c")
        half = values.shape[0] // 2
        keep = lax.dynamic_slice_in_dim(values, core * half, half, 0)
        send = lax.dynamic_slice_in_dim(values, (1 - core) * half, half, 0)
        mine = sum_z((keep + swap(send, "c")).astype(BF)).astype(BF)
        other = swap(mine, "c")
        return jnp.concatenate(
            [jnp.where(core == 0, mine, other), jnp.where(core == 0, other, mine)], axis=0
        )

    def sum_all(values):
        for axis in ("c", "x", "y", "z"):
            values = values + swap(values, axis)
        step = 1
        while 2 * step < z_size:
            values = values + lax.ppermute(
                values, "w", tuple((k, k ^ step) for k in range(z_size // 2))
            )
            step *= 2
        return values

    def feature_order(values):
        lead = values.shape[:-1]
        shaped = values.reshape(lead + (z_size // 2, 2, 2, 2, -1))
        return jnp.moveaxis(shaped, -2, -4).reshape(values.shape)

    def natural_order(values):
        lead = values.shape[:-1]
        shaped = values.reshape(lead + (z_size // 2, 2, 2, 2, -1))
        return jnp.moveaxis(shaped, -4, -2).reshape(values.shape)

    def local(
        hidden,
        mask_index,
        mask_count,
        mask_embed,
        norm_gains,
        caption,
        w_qkv,
        w_out,
        w_cross,
        w_cross_out,
        w_text,
        w_up,
        w_down,
        cotangent,
    ):
        images, local_rows, width = hidden.shape
        full_length = mask_index.shape[1]
        shard_rows = w_qkv.shape[0]
        rank = lax.axis_index("x") * 2 + lax.axis_index("y")
        pair_rank = lax.axis_index("z") * 4 + rank
        tokens = images * local_rows
        group = width // 4
        hidden_group = w_up.shape[1] // 8

        first = [w_qkv.reshape(shard_rows, 3 * width)[:, j * width : (j + 1) * width] for j in range(3)]
        first = [pieces(weight, rank, group) for weight in first + [w_out]]
        first = swap_all(
            [jnp.concatenate([part[k] for part in first], axis=1) for k in range(4)]
        )
        first = gather_rows(place([(p, 0, 0) for p in first], rank, [4 * group])[0], DATA)
        qkv, out_w = first[:, : 3 * group], first[:, 3 * group :]

        positions = lax.axis_index("y") * local_rows + jnp.arange(local_rows, dtype=jnp.int32)
        ranks = jnp.arange(full_length, dtype=jnp.int32)
        matches = (mask_index[:, :, None] == positions[None, None, :]) & (
            ranks[None, :, None] < mask_count[:, None, None]
        )
        masked = jnp.any(matches, axis=1).reshape(tokens, 1)
        gains = feature_order(norm_gains)
        start_x = jnp.where(
            masked,
            feature_order(mask_embed),
            feature_order(hidden.reshape(tokens, width)).astype(F32),
        )
        grad_top = feature_order(cotangent.reshape(tokens, width)).astype(F32) * masked.astype(F32)
        normed_a, inv_a = normalize(start_x)
        attn_in = gather_tokens((normed_a * gains[0]).astype(BF))

        near, far = pack([w_cross[:, 0], w_cross_out], [w_up, w_down], pair_rank)
        far = swap(far, "z")
        near = swap_all(near)
        mid = gather_rows(place([(p, 0, 0) for p in near], rank, [2 * group])[0], DATA)
        far = swap_all([far[k * shard_rows : (k + 1) * shard_rows] for k in range(4)])
        mlp = place(
            [(p, 0, 2 * group) for p in near] + [(p, 0, 0) for p in far],
            pair_rank,
            [2 * hidden_group],
        )[0]
        mlp = gather_rows(mlp, PAIR_DATA)
        query_w, cross_out_w = mid[:, :group], mid[:, group:]
        up, down = mlp[:, :hidden_group], mlp[:, hidden_group:]

        own_text = mm_t(caption, w_text).astype(BF)
        kv_rows = w_cross[:, 1:].reshape(shard_rows, 2 * width)
        kv_part = mm(own_text, kv_rows).astype(BF)
        kv_parts = [pieces(kv_part[:, j * width : (j + 1) * width], rank, group) for j in range(2)]
        kv_parts = swap_all(
            [jnp.concatenate([part[k] for part in kv_parts], axis=1) for k in range(4)]
        )
        text_kv = sum_data(sum(part.astype(F32) for part in kv_parts))
        grad_y = gather_pair(grad_top.astype(BF))
        attn_in, text_kv = lax.optimization_barrier((attn_in, text_kv))

        projected = mm(attn_in, qkv).astype(BF)
        self_mixed = self_forward(projected, 2 * images)
        self_mixed, grad_y = lax.optimization_barrier((self_mixed, grad_y))
        after_attn = start_x + scatter_tokens(mm_t(self_mixed, out_w))

        normed_b, inv_b = normalize(after_attn)
        cross_in = gather_tokens((normed_b * gains[1]).astype(BF))
        cross_queries = mm(cross_in, query_w).astype(BF)
        cross_mixed = cross_forward(cross_queries, text_kv)
        after_cross = after_attn + scatter_tokens(mm_t(cross_mixed, cross_out_w))

        normed_c, inv_c = normalize(after_cross)
        mlp_in = gather_pair((normed_c * gains[2]).astype(BF))
        activated, grad_pre, back_part = [], [], []
        for side in range(2):
            pre_act = mm(mlp_in[side], up)
            active, gelu_pull = jax.vjp(jax.nn.gelu, pre_act)
            activated.append(active.astype(BF))
            grad_pre.append(gelu_pull(mm(grad_y[side], down))[0].astype(BF))
            back_part.append(mm_t(grad_pre[side], up))
        grad_pre, back_part = lax.optimization_barrier((grad_pre, back_part))
        mlp_part = grad_products([(grad_y, activated), (mlp_in, grad_pre)])
        mlp_rows = scatter_grad(mlp_part, PAIR_DATA)
        grad_mlp_in = scatter_pair(*back_part)
        back_c, gain_grad_c = norm_back(grad_mlp_in, normed_c, inv_c, gains[2])
        grad_after_cross = grad_top + back_c

        cross_branch = gather_tokens(grad_after_cross.astype(BF))
        grad_cross_mixed = mm(cross_branch, cross_out_w).astype(BF)
        grad_cq, kv_grad = cross_back(cross_queries, text_kv, grad_cross_mixed)
        cross_part = grad_products(
            [([cross_in], [grad_cq]), ([cross_branch], [cross_mixed])]
        )
        cross_part, mlp_rows = lax.optimization_barrier((cross_part, mlp_rows))
        cross_rows = scatter_grad(cross_part, DATA)
        grad_cross_in = scatter_tokens(mm_t(grad_cq, query_w))
        back_b, gain_grad_b = norm_back(grad_cross_in, normed_b, inv_b, gains[1])
        grad_after_attn = grad_after_cross + back_b

        attn_branch = gather_tokens(grad_after_attn.astype(BF))
        grad_self_mixed = mm(attn_branch, out_w).astype(BF)
        grad_projected = self_back(projected, grad_self_mixed, 2 * images)
        attn_part = grad_products(
            [([attn_in], [grad_projected]), ([attn_branch], [self_mixed])]
        )
        attn_part, cross_rows = lax.optimization_barrier((attn_part, cross_rows))
        attn_rows = scatter_grad(attn_part, DATA)
        grad_projected, activated, kv_grad, attn_part = lax.optimization_barrier(
            (grad_projected, activated, kv_grad, attn_part)
        )
        grad_attn_in = scatter_tokens(mm_t(grad_projected, qkv))
        back_a, gain_grad_a = norm_back(grad_attn_in, normed_a, inv_a, gains[0])
        grad_start = grad_after_attn + back_a
        result = after_cross + scatter_pair(*[mm_t(active, down) for active in activated])
        output = natural_order(result.astype(BF))

        kv_grad = sum_data(kv_grad)
        kv_grads = place([(p, 0, 0) for p in swap_all([kv_grad] * 4)], rank, [group, group])
        kv_grads = [
            part.reshape(4, -1, group).transpose(1, 0, 2).reshape(-1, width) for part in kv_grads
        ]
        kv_grads = jnp.concatenate(kv_grads, axis=1)
        kv_weight_grad = t_mm(own_text, kv_grads).reshape(shard_rows, 2, width)
        grad_text = mm_t(kv_grads, kv_rows).astype(BF)
        grad_text_w = t_mm(grad_text, caption)
        caption_part = mm(grad_text, w_text).astype(BF)
        caption_parts = swap_all(pieces(caption_part, rank, caption.shape[1] // 4))
        caption_own = sum_data(sum(part.astype(F32) for part in caption_parts))
        caption_parts = swap_all([caption_own] * 4)
        grad_caption = finish([(p, 0, 0) for p in caption_parts], rank, [caption_own.shape[1]])[0]

        picked = pick_rows(mlp_rows, pair_rank, 8)
        parts = swap_all([jnp.concatenate([picked[k], picked[4 + k]], axis=0) for k in range(4)])
        far = swap(jnp.concatenate([part[shard_rows:] for part in parts], axis=0), "z")
        down_grad, up_grad = finish(
            [(part, 0, 0) for part in parts] + [(far, k * shard_rows, 0) for k in range(4)],
            pair_rank,
            [hidden_group] * 2,
        )
        parts = swap_all(pick_rows(cross_rows, rank, 4))
        query_grad, cross_out_grad = finish([(p, 0, 0) for p in parts], rank, [group] * 2)
        parts = swap_all(pick_rows(attn_rows, rank, 4))
        qkv_grad, out_grad = finish([(p, 0, 0) for p in parts], rank, [group], 3)
        grad_hidden = natural_order(jnp.where(masked, 0.0, grad_start).astype(BF))
        mask_part = jnp.sum(jnp.where(masked, grad_start, 0.0), axis=0)
        sums = natural_order(
            sum_all(jnp.stack([gain_grad_a, gain_grad_b, gain_grad_c, mask_part]))
        )
        grad_cross = jnp.concatenate([query_grad[:, None], kv_weight_grad], axis=1)
        return (
            output.reshape(hidden.shape),
            grad_hidden.reshape(hidden.shape),
            grad_caption,
            sums[:3],
            sums[3],
            qkv_grad,
            out_grad,
            grad_cross,
            cross_out_grad,
            grad_text_w,
            up_grad,
            down_grad,
        )

    return local


def solution(mesh):
    z_size = mesh.shape["img"] // 4
    inner = Mesh(mesh.devices.reshape(z_size // 2, 2, 2, 2, 2), ("w", "z", "x", "c", "y"))
    image = ("w", "z", "x", "c")
    tokens = P(image, "y", None)
    rows = P(image + ("y",))
    in_specs = (tokens, P(image, None), P(image), P(), P(), P()) + (rows,) * 7 + (tokens,)
    out_specs = (tokens, tokens, P(), P(), P()) + (rows,) * 7
    return jax.shard_map(
        make_local(z_size), mesh=inner, in_specs=in_specs, out_specs=out_specs, check_vma=False
    )
```

```python
import math

import jax
import jax.numpy as jnp
from jax import lax
from jax.experimental import pallas as pl
from jax.experimental.pallas import tpu as pltpu
from jax.sharding import Mesh
from jax.sharding import PartitionSpec as P

HD = 128
EPS = 1e-05
BF = jnp.bfloat16
F32 = jnp.float32
PAIR = ((0, 1), (1, 0))
DIAG = ((0, 3), (1, 2), (2, 1), (3, 0))
DATA = ("w", "z", "c")
PAIR_DATA = ("w", "c")
VMEM = 40 * 1024 * 1024


def dot(a, b, dims):
    return lax.dot_general(a, b, (dims, ((), ())), preferred_element_type=F32)


def mm(a, b):
    return dot(a, b, ((1,), (0,)))


def mm_t(a, b):
    return dot(a, b, ((1,), (1,)))


def t_mm(a, b):
    return dot(a, b, ((0,), (0,)))


def normalize(values):
    centred = values - jnp.mean(values, axis=-1, keepdims=True)
    inv_std = lax.rsqrt(jnp.mean(centred * centred, axis=-1, keepdims=True) + EPS)
    return centred * inv_std, inv_std


def norm_back(grad_normed, normed, inv_std, gain):
    scaled = grad_normed * gain
    first_mean = jnp.mean(scaled, axis=-1, keepdims=True)
    second_mean = jnp.mean(scaled * normed, axis=-1, keepdims=True)
    return (
        inv_std * (scaled - first_mean - normed * second_mean),
        jnp.sum(grad_normed * normed, axis=0),
    )


def swap(values, axis):
    return lax.ppermute(values, axis, PAIR)


def swap_diag(values):
    return lax.ppermute(values, ("x", "y"), DIAG)


def gather_tokens(own):
    half = own.shape[0] // 2
    from_x = swap(own, "x")
    from_y = swap(own, "y")
    diag_low = swap(from_x[:half], "y")
    diag_high = swap(from_y[half:], "x")
    return jnp.concatenate([own, from_y, from_x, diag_low, diag_high], axis=0)


def scatter_tokens(partial):
    rows = partial.shape[0] // 4
    half = rows // 2
    own, for_y, for_x, for_diag = (partial[k * rows : (k + 1) * rows] for k in range(4))
    for_diag = for_diag.astype(BF)
    diag_low = swap(for_diag[:half], "y").astype(F32)
    diag_high = swap(for_diag[half:], "x").astype(F32)
    from_x = swap(
        jnp.concatenate([for_x[:half] + diag_low, for_x[half:]], axis=0).astype(BF), "x"
    )
    from_y = swap(
        jnp.concatenate([for_y[:half], for_y[half:] + diag_high], axis=0).astype(BF), "y"
    )
    return own + from_x.astype(F32) + from_y.astype(F32)


def gather_pair(own):
    return gather_tokens(own), gather_tokens(swap(own, "z"))


def scatter_pair(near, far):
    far = scatter_tokens(far).astype(BF)
    return scatter_tokens(near) + swap(far, "z").astype(F32)


def swap_all(parts):
    return [parts[0], swap(parts[1], "y"), swap(parts[2], "x"), swap_diag(parts[3])]


def pieces(values, rank, width):
    return [
        lax.dynamic_slice_in_dim(values, (rank ^ k) * width, width, 1) for k in range(4)
    ]


def block_call(kernel, steps, out_shape, in_specs, out_specs, rank, operands, name):
    return pl.pallas_call(
        kernel,
        out_shape=out_shape,
        grid_spec=pltpu.PrefetchScalarGridSpec(
            num_scalar_prefetch=1, grid=(steps,), in_specs=in_specs, out_specs=out_specs
        ),
        compiler_params=pltpu.CompilerParams(vmem_limit_bytes=VMEM),
        name=name,
    )(rank.reshape(1), *operands)


def whole(array):
    return pl.BlockSpec(array.shape, lambda k, r: (0,) * len(array.shape))


def pack(cross, wide, rank):
    rows = wide[0].shape[0]
    cross_width, width = cross[0].shape[1] // 4, wide[0].shape[1] // 8
    weights = cross + wide
    widths = [cross_width] * len(cross) + [width] * len(wide)
    total, far_total = sum(widths), width * len(wide)
    count = len(weights)

    def kernel(rank_ref, *refs):
        step = pl.program_id(0)
        for k in range(4):

            @pl.when(step == k)
            def _():
                offset = 0
                for ref, w in zip(refs, widths):
                    refs[count + k][:, offset : offset + w] = ref[...]
                    offset += w

            @pl.when(step == 4 + k)
            def _():
                for j in range(len(wide)):
                    refs[count + 4][k * rows : (k + 1) * rows, j * width : (j + 1) * width] = refs[
                        len(cross) + j
                    ][...]

    shapes = [jax.ShapeDtypeStruct((rows, total), BF)] * 4
    shapes.append(jax.ShapeDtypeStruct((4 * rows, far_total), BF))
    *near, far = block_call(
        kernel,
        8,
        shapes,
        [pl.BlockSpec((rows, cross_width), lambda k, r: (0, (k ^ r[0]) & 3))] * len(cross)
        + [pl.BlockSpec((rows, width), lambda k, r: (0, k ^ r[0]))] * len(wide),
        [whole(shape) for shape in shapes],
        rank,
        weights,
        "pack",
    )
    return near, far


def place(pieces, rank, widths):
    rows, starts, arrays = block_rows(pieces)
    count = len(arrays)

    def kernel(rank_ref, *refs):
        step = pl.program_id(0)
        for k, (which, row, offset) in enumerate(starts):

            @pl.when(step == k)
            def _():
                at = offset
                for ref, width in zip(refs[count:], widths):
                    ref[...] = refs[which][row : row + rows, at : at + width]
                    at += width

    return block_call(
        kernel,
        len(pieces),
        [jax.ShapeDtypeStruct((len(pieces) * rows, w), BF) for w in widths],
        [whole(array) for array in arrays],
        [pl.BlockSpec((rows, w), lambda k, r: (k ^ r[0], 0)) for w in widths],
        rank,
        arrays,
        "place",
    )


def block_rows(pieces):
    arrays, starts = [], []
    for array, row, column in pieces:
        found = [k for k, other in enumerate(arrays) if other is array]
        if not found:
            arrays.append(array)
        starts.append((found[0] if found else len(arrays) - 1, row, column))
    rows = min([array.shape[0] for array in arrays] + [s[1] for s in starts if s[1]])
    return rows, starts, arrays


def finish(pieces, rank, widths, lead=0):
    rows, starts, arrays = block_rows(pieces)
    blocks = len(pieces)
    first = widths[0]
    count = len(arrays)

    def kernel(rank_ref, *refs):
        step = pl.program_id(0)
        for k, (which, row, offset) in enumerate(starts):

            @pl.when(step == k)
            def _():
                outs = refs[count:]
                at = offset
                if lead:
                    for j in range(lead):
                        outs[0][:, j, :] = refs[which][row : row + rows, at : at + first].astype(F32)
                        at += first
                    outs = outs[1:]
                for ref, width in zip(outs, widths):
                    ref[...] = refs[which][row : row + rows, at : at + width].astype(F32)
                    at += width

    shapes = [jax.ShapeDtypeStruct((rows, blocks * w), F32) for w in widths]
    specs = [pl.BlockSpec((rows, w), lambda k, r: (0, k ^ r[0])) for w in widths]
    if lead:
        shapes = [jax.ShapeDtypeStruct((rows, lead, blocks * first), F32)] + shapes
        specs = [pl.BlockSpec((rows, lead, first), lambda k, r: (0, 0, k ^ r[0]))] + specs
    return block_call(
        kernel, blocks, shapes, [whole(a) for a in arrays], specs, rank, arrays, "finish"
    )


def softmax(scores):
    exp_terms = jnp.exp(scores - jnp.max(scores, axis=-1, keepdims=True))
    return exp_terms / jnp.sum(exp_terms, axis=-1, keepdims=True)


def score_grad(probs, grad_probs):
    return (
        probs * (grad_probs - jnp.sum(probs * grad_probs, axis=-1, keepdims=True))
    ).astype(BF)


def head(ref, k):
    return ref[:, k * HD : (k + 1) * HD]


def kernel_call(kernel, out_shape, grid, in_specs, out_specs, flops, name):
    return pl.pallas_call(
        kernel,
        out_shape=out_shape,
        grid=grid,
        in_specs=in_specs,
        out_specs=out_specs,
        compiler_params=pltpu.CompilerParams(vmem_limit_bytes=VMEM),
        cost_estimate=pl.CostEstimate(flops=flops, bytes_accessed=1 << 22, transcendentals=0),
        name=name,
    )


def self_forward(projected, images):
    tokens, width = projected.shape
    rows, group = tokens // images, width // 3
    heads = group // HD
    scale = 1.0 / math.sqrt(HD)

    def kernel(proj, mixed):
        for k in range(heads):
            query, key, value = (head(proj, j * heads + k) for j in range(3))
            probs = softmax(mm_t(query, key) * scale).astype(BF)
            mixed[:, k * HD : (k + 1) * HD] = mm(probs, value).astype(BF)

    return kernel_call(
        kernel,
        jax.ShapeDtypeStruct((tokens, group), BF),
        (images,),
        [pl.BlockSpec((rows, width), lambda i: (i, 0))],
        pl.BlockSpec((rows, group), lambda i: (i, 0)),
        4 * tokens * rows * group,
        "self_forward",
    )(projected)


def self_back(projected, grad_mixed, images):
    tokens, width = projected.shape
    rows, group = tokens // images, width // 3
    heads = group // HD
    scale = 1.0 / math.sqrt(HD)

    def kernel(proj, grad, out):
        for k in range(heads):
            query, key, value = (head(proj, j * heads + k) for j in range(3))
            grad_head = head(grad, k)
            probs = softmax(mm_t(query, key) * scale)
            grad_scores = score_grad(probs, mm_t(grad_head, value))
            parts = (
                mm(grad_scores, key) * scale,
                t_mm(grad_scores, query) * scale,
                t_mm(probs.astype(BF), grad_head),
            )
            for j, part in enumerate(parts):
                at = (j * heads + k) * HD
                out[:, at : at + HD] = part.astype(BF)

    return kernel_call(
        kernel,
        jax.ShapeDtypeStruct((tokens, width), BF),
        (images,),
        [
            pl.BlockSpec((rows, width), lambda i: (i, 0)),
            pl.BlockSpec((rows, group), lambda i: (i, 0)),
        ],
        pl.BlockSpec((rows, width), lambda i: (i, 0)),
        10 * tokens * rows * group,
        "self_back",
    )(projected, grad_mixed)


def cross_forward(queries, text_kv):
    tokens, group = queries.shape
    context = text_kv.shape[0]
    heads = group // HD
    scale = 1.0 / math.sqrt(HD)

    def kernel(query, text, mixed):
        for k in range(heads):
            probs = softmax(mm_t(head(query, k), head(text, k)) * scale).astype(BF)
            mixed[:, k * HD : (k + 1) * HD] = mm(probs, head(text, heads + k)).astype(BF)

    return kernel_call(
        kernel,
        jax.ShapeDtypeStruct((tokens, group), BF),
        (1,),
        [
            pl.BlockSpec((tokens, group), lambda i: (0, 0)),
            pl.BlockSpec((context, 2 * group), lambda i: (0, 0)),
        ],
        pl.BlockSpec((tokens, group), lambda i: (0, 0)),
        4 * tokens * context * group,
        "cross_forward",
    )(queries, text_kv)


def cross_back(queries, text_kv, grad_mixed):
    tokens, group = queries.shape
    context = text_kv.shape[0]
    heads = group // HD
    scale = 1.0 / math.sqrt(HD)

    def kernel(query, text, grad, grad_query, grad_text):
        for k in range(heads):
            query_head, key, value = head(query, k), head(text, k), head(text, heads + k)
            grad_head = head(grad, k)
            probs = softmax(mm_t(query_head, key) * scale)
            grad_scores = score_grad(probs, mm_t(grad_head, value))
            grad_query[:, k * HD : (k + 1) * HD] = (mm(grad_scores, key) * scale).astype(BF)
            at = (heads + k) * HD
            grad_text[:, k * HD : (k + 1) * HD] = t_mm(grad_scores, query_head) * scale
            grad_text[:, at : at + HD] = t_mm(probs.astype(BF), grad_head)

    return kernel_call(
        kernel,
        [
            jax.ShapeDtypeStruct((tokens, group), BF),
            jax.ShapeDtypeStruct((context, 2 * group), F32),
        ],
        (1,),
        [
            pl.BlockSpec((tokens, group), lambda i: (0, 0)),
            pl.BlockSpec((context, 2 * group), lambda i: (0, 0)),
            pl.BlockSpec((tokens, group), lambda i: (0, 0)),
        ],
        [
            pl.BlockSpec((tokens, group), lambda i: (0, 0)),
            pl.BlockSpec((context, 2 * group), lambda i: (0, 0)),
        ],
        10 * tokens * context * group,
        "cross_back",
    )(queries, text_kv, grad_mixed)


def grad_products(pairs):
    blocks = len(pairs[0][0])
    tokens, width = pairs[0][0][0].shape
    widths = [y[0].shape[1] for _, y in pairs]
    total = sum(widths)
    rows = 256
    step = 512
    count = len(pairs) * blocks

    def kernel(*refs):
        out = refs[2 * count]
        offset = 0
        for k, wide in enumerate(widths):
            left = [refs[k * blocks + b][...].T for b in range(blocks)]
            for at in range(0, wide, step):
                out[:, offset + at : offset + at + step] = sum(
                    mm(left[b], refs[count + k * blocks + b][:, at : at + step])
                    for b in range(blocks)
                ).astype(BF)
            offset += wide

    return kernel_call(
        kernel,
        jax.ShapeDtypeStruct((width, total), BF),
        (width // rows,),
        [pl.BlockSpec((tokens, rows), lambda i: (0, i))] * count
        + [pl.BlockSpec((tokens, w), lambda i: (0, 0)) for w in widths for _ in range(blocks)],
        pl.BlockSpec((rows, total), lambda i: (i, 0)),
        2 * tokens * blocks * width * total,
        "grad_products",
    )(*[b for x, _ in pairs for b in x], *[b for _, y in pairs for b in y])


def gather_rows(rows, axes):
    return lax.all_gather(rows, axes, axis=0, tiled=True)


def scatter_grad(partial, axes):
    return lax.psum_scatter(partial, axes, scatter_dimension=0, tiled=True)


def pick_rows(values, rank, count):
    rows = values.shape[0] // count
    return [
        lax.dynamic_slice_in_dim(values, (rank ^ k) * rows, rows, 0) for k in range(count)
    ]


def make_local(z_size):
    z_axes = ("w", "z")

    def sum_z(values):
        terms = [values] + [
            lax.ppermute(values, z_axes, tuple((k, k ^ m) for k in range(z_size)))
            for m in range(1, z_size)
        ]
        terms = [term.astype(F32) for term in terms]
        while len(terms) > 1:
            terms = [terms[k] + terms[k + 1] for k in range(0, len(terms), 2)]
        return terms[0]

    def sum_data(values):
        core = lax.axis_index("c")
        half = values.shape[0] // 2
        keep = lax.dynamic_slice_in_dim(values, core * half, half, 0)
        send = lax.dynamic_slice_in_dim(values, (1 - core) * half, half, 0)
        mine = sum_z((keep + swap(send, "c")).astype(BF)).astype(BF)
        other = swap(mine, "c")
        return jnp.concatenate(
            [jnp.where(core == 0, mine, other), jnp.where(core == 0, other, mine)], axis=0
        )

    def sum_all(values):
        for axis in ("c", "x", "y", "z"):
            values = values + swap(values, axis)
        step = 1
        while 2 * step < z_size:
            values = values + lax.ppermute(
                values, "w", tuple((k, k ^ step) for k in range(z_size // 2))
            )
            step *= 2
        return values

    def swap_dims(values, first):
        shaped = values.reshape(values.shape[:-1] + (z_size // 2, 2, 2, 2, -1))
        at = values.ndim - 1 + first
        return jnp.swapaxes(shaped, at, at + 1).reshape(values.shape)

    def layer_order(values):
        return swap_dims(values, 2)

    def pair_order(values):
        return swap_dims(values, 1)

    def local(
        hidden,
        mask_index,
        mask_count,
        mask_embed,
        norm_gains,
        caption,
        w_qkv,
        w_out,
        w_cross,
        w_cross_out,
        w_text,
        w_up,
        w_down,
        cotangent,
    ):
        images, local_rows, width = hidden.shape
        full_length = mask_index.shape[1]
        shard_rows = w_qkv.shape[0]
        rank = lax.axis_index("x") * 2 + lax.axis_index("y")
        pair_rank = lax.axis_index("z") * 4 + rank
        tokens = images * local_rows
        group = width // 4
        hidden_group = w_up.shape[1] // 8

        first = [w_qkv.reshape(shard_rows, 3 * width)[:, j * width : (j + 1) * width] for j in range(3)]
        first = [pieces(weight, rank, group) for weight in first + [w_out]]
        first = swap_all(
            [jnp.concatenate([part[k] for part in first], axis=1) for k in range(4)]
        )
        first = gather_rows(place([(p, 0, 0) for p in first], rank, [4 * group])[0], DATA)
        qkv, out_w = first[:, : 3 * group], first[:, 3 * group :]

        positions = lax.axis_index("y") * local_rows + jnp.arange(local_rows, dtype=jnp.int32)
        ranks = jnp.arange(full_length, dtype=jnp.int32)
        matches = (mask_index[:, :, None] == positions[None, None, :]) & (
            ranks[None, :, None] < mask_count[:, None, None]
        )
        masked = jnp.any(matches, axis=1).reshape(tokens, 1)
        gains = layer_order(norm_gains)
        start_x = jnp.where(
            masked,
            layer_order(mask_embed),
            layer_order(hidden.reshape(tokens, width)).astype(F32),
        )
        grad_top = layer_order(cotangent.reshape(tokens, width)).astype(F32) * masked.astype(F32)
        normed_a, inv_a = normalize(start_x)
        attn_in = gather_tokens((normed_a * gains[0]).astype(BF))

        near, far = pack([w_cross[:, 0], w_cross_out], [w_up, w_down], pair_rank)
        far = swap(far, "z")
        near = swap_all(near)
        mid = gather_rows(place([(p, 0, 0) for p in near], rank, [2 * group])[0], DATA)
        far = swap_all([far[k * shard_rows : (k + 1) * shard_rows] for k in range(4)])
        mlp = place(
            [(p, 0, 2 * group) for p in near] + [(p, 0, 0) for p in far],
            pair_rank,
            [2 * hidden_group],
        )[0]
        mlp = gather_rows(mlp, PAIR_DATA)
        query_w, cross_out_w = mid[:, :group], mid[:, group:]
        up, down = mlp[:, :hidden_group], mlp[:, hidden_group:]

        own_text = mm_t(caption, w_text).astype(BF)
        kv_rows = w_cross[:, 1:].reshape(shard_rows, 2 * width)
        kv_part = mm(own_text, kv_rows).astype(BF)
        kv_parts = [pieces(kv_part[:, j * width : (j + 1) * width], rank, group) for j in range(2)]
        kv_parts = swap_all(
            [jnp.concatenate([part[k] for part in kv_parts], axis=1) for k in range(4)]
        )
        text_kv = sum_data(sum(part.astype(F32) for part in kv_parts))
        grad_y = gather_pair(pair_order(grad_top.astype(BF)))
        attn_in, text_kv = lax.optimization_barrier((attn_in, text_kv))

        projected = mm(attn_in, qkv).astype(BF)
        self_mixed = self_forward(projected, 2 * images)
        self_mixed, grad_y = lax.optimization_barrier((self_mixed, grad_y))
        after_attn = start_x + scatter_tokens(mm_t(self_mixed, out_w))

        normed_b, inv_b = normalize(after_attn)
        cross_in = gather_tokens((normed_b * gains[1]).astype(BF))
        cross_queries = mm(cross_in, query_w).astype(BF)
        cross_mixed = cross_forward(cross_queries, text_kv)
        after_cross = after_attn + scatter_tokens(mm_t(cross_mixed, cross_out_w))

        normed_c, inv_c = normalize(after_cross)
        mlp_in = gather_pair(pair_order((normed_c * gains[2]).astype(BF)))
        activated, grad_pre, back_part = [], [], []
        for side in range(2):
            pre_act = mm(mlp_in[side], up)
            active, gelu_pull = jax.vjp(jax.nn.gelu, pre_act)
            activated.append(active.astype(BF))
            grad_pre.append(gelu_pull(mm(grad_y[side], down))[0].astype(BF))
            back_part.append(mm_t(grad_pre[side], up))
        grad_pre, back_part = lax.optimization_barrier((grad_pre, back_part))
        mlp_part = grad_products([(grad_y, activated), (mlp_in, grad_pre)])
        mlp_rows = scatter_grad(mlp_part, PAIR_DATA)
        grad_mlp_in = pair_order(scatter_pair(*back_part))
        back_c, gain_grad_c = norm_back(grad_mlp_in, normed_c, inv_c, gains[2])
        grad_after_cross = grad_top + back_c

        cross_branch = gather_tokens(grad_after_cross.astype(BF))
        grad_cross_mixed = mm(cross_branch, cross_out_w).astype(BF)
        grad_cq, kv_grad = cross_back(cross_queries, text_kv, grad_cross_mixed)
        cross_part = grad_products(
            [([cross_in], [grad_cq]), ([cross_branch], [cross_mixed])]
        )
        cross_part, mlp_rows = lax.optimization_barrier((cross_part, mlp_rows))
        cross_rows = scatter_grad(cross_part, DATA)
        grad_cross_in = scatter_tokens(mm_t(grad_cq, query_w))
        back_b, gain_grad_b = norm_back(grad_cross_in, normed_b, inv_b, gains[1])
        grad_after_attn = grad_after_cross + back_b

        attn_branch = gather_tokens(grad_after_attn.astype(BF))
        grad_self_mixed = mm(attn_branch, out_w).astype(BF)
        grad_projected = self_back(projected, grad_self_mixed, 2 * images)
        attn_part = grad_products(
            [([attn_in], [grad_projected]), ([attn_branch], [self_mixed])]
        )
        attn_part, cross_rows = lax.optimization_barrier((attn_part, cross_rows))
        attn_rows = scatter_grad(attn_part, DATA)
        grad_projected, activated, kv_grad, attn_part = lax.optimization_barrier(
            (grad_projected, activated, kv_grad, attn_part)
        )
        grad_attn_in = scatter_tokens(mm_t(grad_projected, qkv))
        back_a, gain_grad_a = norm_back(grad_attn_in, normed_a, inv_a, gains[0])
        grad_start = grad_after_attn + back_a
        result = after_cross + pair_order(
            scatter_pair(*[mm_t(active, down) for active in activated])
        )
        output = layer_order(result.astype(BF))

        kv_grad = sum_data(kv_grad)
        kv_grads = place([(p, 0, 0) for p in swap_all([kv_grad] * 4)], rank, [group, group])
        kv_grads = [
            part.reshape(4, -1, group).transpose(1, 0, 2).reshape(-1, width) for part in kv_grads
        ]
        kv_grads = jnp.concatenate(kv_grads, axis=1)
        kv_weight_grad = t_mm(own_text, kv_grads).reshape(shard_rows, 2, width)
        grad_text = mm_t(kv_grads, kv_rows).astype(BF)
        grad_text_w = t_mm(grad_text, caption)
        caption_part = mm(grad_text, w_text).astype(BF)
        caption_parts = swap_all(pieces(caption_part, rank, caption.shape[1] // 4))
        caption_own = sum_data(sum(part.astype(F32) for part in caption_parts))
        caption_parts = swap_all([caption_own] * 4)
        grad_caption = finish([(p, 0, 0) for p in caption_parts], rank, [caption_own.shape[1]])[0]

        picked = pick_rows(mlp_rows, pair_rank, 8)
        parts = swap_all([jnp.concatenate([picked[k], picked[4 + k]], axis=0) for k in range(4)])
        far = swap(jnp.concatenate([part[shard_rows:] for part in parts], axis=0), "z")
        down_grad, up_grad = finish(
            [(part, 0, 0) for part in parts] + [(far, k * shard_rows, 0) for k in range(4)],
            pair_rank,
            [hidden_group] * 2,
        )
        parts = swap_all(pick_rows(cross_rows, rank, 4))
        query_grad, cross_out_grad = finish([(p, 0, 0) for p in parts], rank, [group] * 2)
        parts = swap_all(pick_rows(attn_rows, rank, 4))
        qkv_grad, out_grad = finish([(p, 0, 0) for p in parts], rank, [group], 3)
        grad_hidden = layer_order(jnp.where(masked, 0.0, grad_start).astype(BF))
        mask_part = jnp.sum(jnp.where(masked, grad_start, 0.0), axis=0)
        sums = layer_order(
            sum_all(jnp.stack([gain_grad_a, gain_grad_b, gain_grad_c, mask_part]))
        )
        grad_cross = jnp.concatenate([query_grad[:, None], kv_weight_grad], axis=1)
        return (
            output.reshape(hidden.shape),
            grad_hidden.reshape(hidden.shape),
            grad_caption,
            sums[:3],
            sums[3],
            qkv_grad,
            out_grad,
            grad_cross,
            cross_out_grad,
            grad_text_w,
            up_grad,
            down_grad,
        )

    return local


def solution(mesh):
    z_size = mesh.shape["img"] // 4
    inner = Mesh(mesh.devices.reshape(z_size // 2, 2, 2, 2, 2), ("w", "z", "x", "c", "y"))
    image = ("w", "z", "x", "c")
    tokens = P(image, "y", None)
    rows = P(image + ("y",))
    in_specs = (tokens, P(image, None), P(image), P(), P(), P()) + (rows,) * 7 + (tokens,)
    out_specs = (tokens, tokens, P(), P(), P()) + (rows,) * 7
    return jax.shard_map(
        make_local(z_size), mesh=inner, in_specs=in_specs, out_specs=out_specs, check_vma=False
    )
```

```python
import math

import jax
import jax.numpy as jnp
from jax import lax
from jax.experimental import pallas as pl
from jax.experimental.pallas import tpu as pltpu
from jax.sharding import Mesh
from jax.sharding import PartitionSpec as P

HD = 128
EPS = 1e-05
BF = jnp.bfloat16
F32 = jnp.float32
PAIR = ((0, 1), (1, 0))
GROUP = ("x", "y")
DATA = ("w", "z", "c")
PAIR_DATA = ("w", "c")
VMEM = 48 * 1024 * 1024
SCALE = 1.0 / math.sqrt(HD)
SLOPE = math.sqrt(2.0 / math.pi)
CUBIC = 0.044715


def dot(a, b, dims):
    return lax.dot_general(a, b, (dims, ((), ())), preferred_element_type=F32)


def mm(a, b):
    return dot(a, b, ((1,), (0,)))


def mm_t(a, b):
    return dot(a, b, ((1,), (1,)))


def t_mm(a, b):
    return dot(a, b, ((0,), (0,)))


def shape(dims, dtype=BF):
    return jax.ShapeDtypeStruct(dims, dtype)


def swap(values, axis):
    return lax.ppermute(values, axis, PAIR)


def trade(blocks, axes=GROUP):
    return lax.all_to_all(blocks, axes, 0, 0, tiled=True)


def spread(values, axes=GROUP, count=4):
    return trade(jnp.broadcast_to(values[None], (count,) + values.shape), axes)


def gather_tokens(own):
    half = own.shape[0] // 2
    from_x = swap(own, "x")
    from_y = swap(own, "y")
    return own, from_y, from_x, swap(from_x[:half], "y"), swap(from_y[half:], "x")


def scatter_tokens(parts):
    own, for_y, for_x, for_low, for_high = parts
    half = for_low.shape[0]
    low = swap(for_low, "y").astype(F32) + for_x[:half].astype(F32)
    high = swap(for_high, "x").astype(F32) + for_y[half:].astype(F32)
    from_x = swap(jnp.concatenate([low.astype(BF), for_x[half:]], axis=0), "x")
    from_y = swap(jnp.concatenate([for_y[:half], high.astype(BF)], axis=0), "y")
    return [own, from_x, from_y]


def gather_rows(rows, axes):
    return lax.all_gather(rows, axes, axis=0, tiled=True)


def scatter_grad(partial, axes):
    return lax.psum_scatter(partial, axes, scatter_dimension=0, tiled=True)


def call(kernel, grid, in_specs, out_specs, out_shape, operands, name, flops=0, size=1 << 22,
         rank=None, scratch=()):
    options = dict(
        out_shape=out_shape,
        compiler_params=pltpu.CompilerParams(vmem_limit_bytes=VMEM),
        cost_estimate=pl.CostEstimate(flops=flops, bytes_accessed=size, transcendentals=0),
        name=name,
    )
    if rank is None:
        return pl.pallas_call(
            kernel, grid=grid, in_specs=in_specs, out_specs=out_specs, scratch_shapes=scratch,
            **options,
        )(*operands)
    spec = pltpu.PrefetchScalarGridSpec(
        num_scalar_prefetch=1,
        grid=grid,
        in_specs=in_specs,
        out_specs=out_specs,
        scratch_shapes=scratch,
    )
    return pl.pallas_call(kernel, grid_spec=spec, **options)(rank.reshape(1), *operands)


def whole(array):
    return pl.BlockSpec(array.shape, lambda *_: (0,) * len(array.shape))


def reorder(values, unit, order):
    if order is None:
        return values
    return jnp.concatenate([values[:, k * unit : (k + 1) * unit] for k in order], axis=1)


def assemble(target, pieces, rank, unit, order):
    rows, half = pieces[0].shape[0], pieces[3].shape[0]
    for k in range(3):
        at = pl.multiple_of((rank ^ k) * rows, rows)
        target[pl.ds(at, rows), :] = reorder(pieces[k][...], unit, order)
    at = pl.multiple_of((rank ^ 3) * rows, rows)
    target[pl.ds(at, half), :] = reorder(pieces[3][...], unit, order)
    target[pl.ds(pl.multiple_of(at + half, half), half), :] = reorder(pieces[4][...], unit, order)


def gather_mm(pieces, rank, weight, first, columns, name):
    rows, width = pieces[0].shape
    step = 256

    def kernel(r, *refs):
        tokens, out = refs[6], refs[7]

        @pl.when(pl.program_id(0) == 0)
        def _():
            assemble(tokens, refs[:5], r[0], width, None)

        out[...] = mm(tokens[...], refs[5][...]).astype(BF)

    return call(
        kernel,
        (columns // step,),
        [whole(p) for p in pieces]
        + [pl.BlockSpec((width, step), lambda j, r: (0, first // step + j))],
        [
            pl.BlockSpec((4 * rows, width), lambda j, r: (0, 0)),
            pl.BlockSpec((4 * rows, step), lambda j, r: (0, j)),
        ],
        [shape((4 * rows, width)), shape((4 * rows, columns))],
        [*pieces, weight],
        name,
        flops=8 * rows * width * columns,
        size=2 * width * (columns + 8 * rows),
        rank=rank,
    )


def mm_scatter(values, rank, weight, first, name, unit=0, order=None):
    tokens, depth = values.shape
    rows = tokens // 4
    width = weight.shape[0]
    step = unit if order is not None else 512
    place = (lambda j: j) if order is None else (lambda j: pair_index(j))

    def kernel(r, x, w, own, for_y, for_x, low, high, total):
        total[...] = mm_t(x[...], w[...])

        def block(k):
            return total[pl.ds(pl.multiple_of((r[0] ^ k) * rows, rows), rows), :]

        own[...] = block(0)
        for_y[...] = block(1).astype(BF)
        for_x[...] = block(2).astype(BF)
        diagonal = block(3).astype(BF)
        low[...] = diagonal[: rows // 2]
        high[...] = diagonal[rows // 2 :]

    sizes = [rows, rows, rows, rows // 2, rows // 2]
    return call(
        kernel,
        (width // step,),
        [
            pl.BlockSpec((tokens, depth), lambda j, r: (0, 0)),
            pl.BlockSpec((step, depth), lambda j, r: (j, first // depth)),
        ],
        [pl.BlockSpec((n, step), lambda j, r: (0, place(j))) for n in sizes],
        [shape((n, width), F32 if k == 0 else BF) for k, n in enumerate(sizes)],
        [values, weight],
        name,
        flops=2 * tokens * depth * width,
        size=2 * width * (depth + 6 * rows),
        rank=rank,
        scratch=[pltpu.VMEM((tokens, step), F32)],
    )


def pair_index(j):
    return ((j >> 2) << 2) | ((j & 1) << 1) | ((j >> 1) & 1)


def normalize(values):
    centred = values - jnp.mean(values, axis=-1, keepdims=True)
    inv_std = lax.rsqrt(jnp.mean(centred * centred, axis=-1, keepdims=True) + EPS)
    return centred * inv_std, inv_std


NORM_ROWS = 32


def row_spec(array, at=None):
    width = array.shape[-1]
    if at is None:
        return pl.BlockSpec((NORM_ROWS, width), lambda i: (i, 0))
    return pl.BlockSpec((1, NORM_ROWS, width), lambda i, at=at: (at, i, 0))


def terms_of(terms):
    arrays, specs = [], []
    for term in terms:
        array, at = term if isinstance(term, tuple) else (term, None)
        arrays.append(array)
        specs.append(row_spec(array, at))
    return arrays, specs


def total_of(refs):
    values = [ref[0] if len(ref.shape) == 3 else ref[...] for ref in refs]
    return sum(value.astype(F32) for value in values)


def add_norm(terms, gain):
    arrays, specs = terms_of(terms)
    tokens, width = arrays[0].shape[-2], arrays[0].shape[-1]
    tokens = min(a.shape[-2] for a in arrays)

    def kernel(*refs):
        gain_ref, x, out = refs[-3:]
        values = total_of(refs[:-3])
        x[...] = values
        out[...] = (normalize(values)[0] * gain_ref[...]).astype(BF)

    return call(
        kernel,
        (tokens // NORM_ROWS,),
        specs + [whole(gain)],
        [row_spec(shape((tokens, width)))] * 2,
        [shape((tokens, width), F32), shape((tokens, width))],
        [*arrays, gain],
        "add_norm",
    )


def norm_grad(grad, values, gain):
    normed, inv_std = normalize(values)
    scaled = grad * gain
    first_mean = jnp.mean(scaled, axis=-1, keepdims=True)
    second_mean = jnp.mean(scaled * normed, axis=-1, keepdims=True)
    return (
        inv_std * (scaled - first_mean - normed * second_mean),
        jnp.sum(grad * normed, axis=0, keepdims=True),
    )


def accumulate(ref, value):
    @pl.when(pl.program_id(0) == 0)
    def _():
        ref[...] = jnp.zeros_like(ref)

    ref[...] += value


def norm_back(terms, upper, values, gain):
    arrays, specs = terms_of(terms)
    tokens, width = values.shape

    def kernel(*refs):
        upper_ref, x, gain_ref, out, out_low, gain_grad = refs[-6:]
        back, part = norm_grad(total_of(refs[:-6]), x[...], gain_ref[...])
        result = upper_ref[...].astype(F32) + back
        out[...] = result
        out_low[...] = result.astype(BF)
        accumulate(gain_grad, part)

    return call(
        kernel,
        (tokens // NORM_ROWS,),
        specs + [row_spec(upper), row_spec(values), whole(gain)],
        [row_spec(values)] * 2 + [pl.BlockSpec((1, width), lambda i: (0, 0))],
        [shape((tokens, width), F32), shape((tokens, width)), shape((1, width), F32)],
        [*arrays, upper, values, gain],
        "norm_back",
    )


def last_back(terms, upper, values, gain, masked, unit, order):
    arrays, specs = terms_of(terms)
    tokens, width = values.shape

    def kernel(*refs):
        upper_ref, x, gain_ref, mask, out, gain_grad, mask_grad = refs[-7:]
        back, part = norm_grad(total_of(refs[:-7]), x[...], gain_ref[...])
        result = upper_ref[...].astype(F32) + back
        hit = mask[...] > 0.5
        out[...] = reorder(jnp.where(hit, 0.0, result).astype(BF), unit, order)
        accumulate(gain_grad, part)
        accumulate(mask_grad, jnp.sum(jnp.where(hit, result, 0.0), axis=0, keepdims=True))

    line = pl.BlockSpec((1, width), lambda i: (0, 0))
    return call(
        kernel,
        (tokens // NORM_ROWS,),
        specs + [row_spec(upper), row_spec(values), whole(gain), row_spec(masked)],
        [row_spec(values), line, line],
        [shape((tokens, width)), shape((1, width), F32), shape((1, width), F32)],
        [*arrays, upper, values, gain, masked],
        "last_back",
    )


def start(hidden, cotangent, masked, embed, gain, unit, order):
    tokens, width = hidden.shape

    def kernel(hid, cot, mask, embed_ref, gain_ref, x, out, grad):
        hit = mask[...] > 0.5
        values = jnp.where(
            hit, embed_ref[...], reorder(hid[...], unit, order).astype(F32)
        )
        x[...] = values
        out[...] = (normalize(values)[0] * gain_ref[...]).astype(BF)
        grad[...] = jnp.where(hit, reorder(cot[...], unit, order).astype(F32), 0.0).astype(BF)

    rows = row_spec(hidden)
    return call(
        kernel,
        (tokens // NORM_ROWS,),
        [rows, rows, row_spec(masked), whole(embed), whole(gain)],
        [rows] * 3,
        [shape((tokens, width), F32), shape((tokens, width)), shape((tokens, width))],
        [hidden, cotangent, masked, embed, gain],
        "start",
    )


def layer_output(upper, terms, pair_unit, pair_order, unit, order):
    arrays, specs = terms_of(terms)
    tokens, width = upper.shape

    def kernel(*refs):
        values = refs[-2][...] + reorder(total_of(refs[:-2]), pair_unit, pair_order)
        refs[-1][...] = reorder(values.astype(BF), unit, order)

    return call(
        kernel,
        (tokens // NORM_ROWS,),
        specs + [row_spec(upper)],
        row_spec(upper),
        shape((tokens, width)),
        [*arrays, upper],
        "layer_output",
    )


def feed_forward(pieces, grad_y, side, rank, weight, unit, order):
    rows, width = pieces[0].shape
    hidden = weight.shape[1] // 2
    step = 256

    def kernel(r, *refs):
        dy, up, down, tokens, grads, act, pre = refs[5:]

        @pl.when(pl.program_id(0) == 0)
        def _():
            assemble(tokens, refs[:5], r[0], unit, order)
            for k in range(4):
                grads[k * rows : (k + 1) * rows, :] = reorder(dy[k], unit, order)

        u = mm(tokens[...], up[...])
        square = u * u
        bend = jnp.tanh(SLOPE * u * (1.0 + CUBIC * square))
        half = 0.5 * (1.0 + bend)
        act[...] = (u * half).astype(BF)
        slope = half + 0.5 * u * (1.0 - bend * bend) * SLOPE * (1.0 + 3.0 * CUBIC * square)
        pre[...] = (mm(grads[...], down[...]) * slope).astype(BF)

    full = pl.BlockSpec((4 * rows, width), lambda j, r: (0, 0))
    part = pl.BlockSpec((4 * rows, step), lambda j, r: (0, j))
    return call(
        kernel,
        (hidden // step,),
        [whole(p) for p in pieces]
        + [
            pl.BlockSpec((4, rows, width), lambda j, r: (0, side, 0)),
            pl.BlockSpec((width, step), lambda j, r: (0, j)),
            pl.BlockSpec((width, step), lambda j, r: (0, hidden // step + j)),
        ],
        [full, full, part, part],
        [shape((4 * rows, width))] * 2 + [shape((4 * rows, hidden))] * 2,
        [*pieces, grad_y, weight, weight],
        "feed_forward",
        flops=16 * rows * width * hidden,
        size=4 * width * (hidden + 8 * rows),
        rank=rank,
    )


def softmax(scores):
    exp_terms = jnp.exp(scores - jnp.max(scores, axis=-1, keepdims=True))
    return exp_terms / jnp.sum(exp_terms, axis=-1, keepdims=True)


def score_grad(probs, grad_probs):
    return (
        probs * (grad_probs - jnp.sum(probs * grad_probs, axis=-1, keepdims=True))
    ).astype(BF)


def head(ref, k):
    return ref[:, k * HD : (k + 1) * HD]


def self_forward(projected, images):
    tokens, width = projected.shape
    rows, group = tokens // images, width // 3
    heads = group // HD

    def kernel(proj, mixed):
        for k in range(heads):
            query, key, value = (head(proj, j * heads + k) for j in range(3))
            probs = softmax(mm_t(query, key) * SCALE).astype(BF)
            mixed[:, k * HD : (k + 1) * HD] = mm(probs, value).astype(BF)

    return call(
        kernel,
        (images,),
        [pl.BlockSpec((rows, width), lambda i: (i, 0))],
        pl.BlockSpec((rows, group), lambda i: (i, 0)),
        shape((tokens, group)),
        [projected],
        "self_forward",
        flops=4 * tokens * rows * group,
    )


def self_back(projected, grad_mixed, images):
    tokens, width = projected.shape
    rows, group = tokens // images, width // 3
    heads = group // HD

    def kernel(proj, grad, out):
        for k in range(heads):
            query, key, value = (head(proj, j * heads + k) for j in range(3))
            grad_head = head(grad, k)
            probs = softmax(mm_t(query, key) * SCALE)
            grad_scores = score_grad(probs, mm_t(grad_head, value))
            parts = (
                mm(grad_scores, key) * SCALE,
                t_mm(grad_scores, query) * SCALE,
                t_mm(probs.astype(BF), grad_head),
            )
            for j, part in enumerate(parts):
                at = (j * heads + k) * HD
                out[:, at : at + HD] = part.astype(BF)

    return call(
        kernel,
        (images,),
        [
            pl.BlockSpec((rows, width), lambda i: (i, 0)),
            pl.BlockSpec((rows, group), lambda i: (i, 0)),
        ],
        pl.BlockSpec((rows, width), lambda i: (i, 0)),
        shape((tokens, width)),
        [projected, grad_mixed],
        "self_back",
        flops=10 * tokens * rows * group,
    )


def cross_forward(queries, text_kv):
    tokens, group = queries.shape
    heads = group // HD

    def kernel(query, text, mixed):
        for k in range(heads):
            probs = softmax(mm_t(head(query, k), head(text, k)) * SCALE).astype(BF)
            mixed[:, k * HD : (k + 1) * HD] = mm(probs, head(text, heads + k)).astype(BF)

    return call(
        kernel,
        (1,),
        [whole(queries), whole(text_kv)],
        whole(queries),
        shape((tokens, group)),
        [queries, text_kv],
        "cross_forward",
        flops=4 * tokens * text_kv.shape[0] * group,
    )


def cross_back(queries, text_kv, grad_mixed):
    tokens, group = queries.shape
    context = text_kv.shape[0]
    heads = group // HD

    def kernel(query, text, grad, grad_query, grad_text):
        for k in range(heads):
            query_head, key, value = head(query, k), head(text, k), head(text, heads + k)
            grad_head = head(grad, k)
            probs = softmax(mm_t(query_head, key) * SCALE)
            grad_scores = score_grad(probs, mm_t(grad_head, value))
            grad_query[:, k * HD : (k + 1) * HD] = (mm(grad_scores, key) * SCALE).astype(BF)
            at = (heads + k) * HD
            grad_text[:, k * HD : (k + 1) * HD] = t_mm(grad_scores, query_head) * SCALE
            grad_text[:, at : at + HD] = t_mm(probs.astype(BF), grad_head)

    return call(
        kernel,
        (1,),
        [whole(queries), whole(text_kv), whole(grad_mixed)],
        [whole(queries), whole(text_kv)],
        [shape((tokens, group)), shape((context, 2 * group), F32)],
        [queries, text_kv, grad_mixed],
        "cross_back",
        flops=10 * tokens * context * group,
    )


def grad_products(pairs, name):
    blocks = len(pairs[0][0])
    tokens, width = pairs[0][0][0].shape
    widths = [y[0].shape[1] for _, y in pairs]
    total = sum(widths)
    rows = 256
    step = 512
    count = len(pairs) * blocks

    def kernel(*refs):
        out = refs[2 * count]
        offset = 0
        for k, wide in enumerate(widths):
            left = [refs[k * blocks + b][...].T for b in range(blocks)]
            for at in range(0, wide, step):
                out[:, offset + at : offset + at + step] = sum(
                    mm(left[b], refs[count + k * blocks + b][:, at : at + step])
                    for b in range(blocks)
                ).astype(BF)
            offset += wide

    return call(
        kernel,
        (width // rows,),
        [pl.BlockSpec((tokens, rows), lambda i: (0, i))] * count
        + [pl.BlockSpec((tokens, w), lambda i: (0, 0)) for w in widths for _ in range(blocks)],
        pl.BlockSpec((rows, total), lambda i: (i, 0)),
        shape((width, total)),
        [b for x, _ in pairs for b in x] + [b for _, y in pairs for b in y],
        name,
        flops=2 * tokens * blocks * width * total,
        size=4 * width * total,
    )


def finish_pair(near, far, z):
    count, rows, total = near.shape
    width = total // 2

    def kernel(r, near_ref, far_ref, first, second):
        step = pl.program_id(0)
        for side, ref in enumerate((near_ref, far_ref)):

            @pl.when(step // count == side)
            def _():
                block = ref[lax.rem(step, count)].astype(F32)
                first[...] = block[:, :width]
                second[...] = block[:, width:]

    out = pl.BlockSpec((rows, width), lambda k, r: (0, ((k // count) ^ r[0]) * count + k % count))
    return call(
        kernel,
        (2 * count,),
        [whole(near), whole(far)],
        [out, out],
        [shape((rows, 2 * count * width), F32)] * 2,
        [near, far],
        "finish_pair",
        rank=z,
    )


def finish_attention(blocks):
    count, rows, total = blocks.shape
    width = total // 4

    def kernel(ref, three, one):
        for j in range(3):
            three[:, j, :] = ref[0, :, j * width : (j + 1) * width].astype(F32)
        one[...] = ref[0, :, 3 * width :].astype(F32)

    return call(
        kernel,
        (count,),
        [pl.BlockSpec((1, rows, total), lambda k: (k, 0, 0))],
        [
            pl.BlockSpec((rows, 3, width), lambda k: (0, 0, k)),
            pl.BlockSpec((rows, width), lambda k: (0, k)),
        ],
        [shape((rows, 3, count * width), F32), shape((rows, count * width), F32)],
        [blocks],
        "finish_attention",
    )


def finish_cross(blocks, text_grad):
    count, rows, total = blocks.shape
    width = total // 2

    def kernel(ref, key, value, three, one):
        three[:, 0, :] = ref[0, :, :width].astype(F32)
        three[:, 1, :] = key[...]
        three[:, 2, :] = value[...]
        one[...] = ref[0, :, width:].astype(F32)

    return call(
        kernel,
        (count,),
        [
            pl.BlockSpec((1, rows, total), lambda k: (k, 0, 0)),
            pl.BlockSpec((rows, width), lambda k: (0, k)),
            pl.BlockSpec((rows, width), lambda k: (0, count + k)),
        ],
        [
            pl.BlockSpec((rows, 3, width), lambda k: (0, 0, k)),
            pl.BlockSpec((rows, width), lambda k: (0, k)),
        ],
        [shape((rows, 3, count * width), F32), shape((rows, count * width), F32)],
        [blocks, text_grad, text_grad],
        "finish_cross",
    )


def column_blocks(weight, count):
    rows = weight.shape[0]
    return weight.reshape(rows, count, -1).transpose(1, 0, 2)


def make_local(z_size):
    z_axes = ("w", "z")

    def sum_data(values):
        rows, columns = values.shape
        core = lax.axis_index("c")
        halves = values.reshape(2, rows // 2, columns)
        keep = lax.dynamic_index_in_dim(halves, core, 0, keepdims=False)
        send = lax.dynamic_index_in_dim(halves, 1 - core, 0, keepdims=False)
        mine = (keep + swap(send, "c")).astype(BF).reshape(z_size, -1, columns)
        mine = trade(mine, z_axes).astype(F32).sum(axis=0).astype(BF)
        mine = spread(mine, z_axes, z_size).reshape(rows // 2, columns)
        other = swap(mine, "c")
        return jnp.concatenate(
            [jnp.where(core == 0, mine, other), jnp.where(core == 0, other, mine)], axis=0
        )

    def sum_all(values):
        for axis in ("c", "x", "y", "z"):
            values = values + swap(values, axis)
        step = 1
        while 2 * step < z_size:
            values = values + lax.ppermute(
                values, "w", tuple((k, k ^ step) for k in range(z_size // 2))
            )
            step *= 2
        return values

    def swap_dims(values, first):
        shaped = values.reshape(values.shape[:-1] + (z_size // 2, 2, 2, 2, -1))
        at = values.ndim - 1 + first
        return jnp.swapaxes(shaped, at, at + 1).reshape(values.shape)

    def layer_order(values):
        return swap_dims(values, 2)

    def pair_order(values):
        return swap_dims(values, 1)

    def local(
        hidden,
        mask_index,
        mask_count,
        mask_embed,
        norm_gains,
        caption,
        w_qkv,
        w_out,
        w_cross,
        w_cross_out,
        w_text,
        w_up,
        w_down,
        cotangent,
    ):
        images, local_rows, width = hidden.shape
        full_length = mask_index.shape[1]
        shard_rows = w_qkv.shape[0]
        rank = lax.axis_index("x") * 2 + lax.axis_index("y")
        z = lax.axis_index("z")
        tokens = images * local_rows
        group = width // 4
        text_width = caption.shape[1]

        unit, pair_unit = width // (4 * z_size), width // (2 * z_size)
        inside = unit % 128 == 0
        order = [pair_index(k) for k in range(4 * z_size)] if inside else None
        pair = [pair_index(k) for k in range(2 * z_size)] if inside else None

        def outer(values, change):
            return values if inside else change(values)

        first = jnp.concatenate(
            [
                w_qkv.reshape(shard_rows, 3, 4, group)
                .transpose(2, 0, 1, 3)
                .reshape(4, shard_rows, 3 * group),
                column_blocks(w_out, 4),
            ],
            axis=2,
        )
        first = gather_rows(trade(first).reshape(4 * shard_rows, 4 * group), DATA)
        wide = jnp.concatenate([column_blocks(w_up, 8), column_blocks(w_down, 8)], axis=2)
        wide = wide.reshape(2, 4, shard_rows, -1)
        wide_near = lax.dynamic_index_in_dim(wide, z, 0, keepdims=False)
        wide_far = swap(lax.dynamic_index_in_dim(wide, 1 - z, 0, keepdims=False), "z")
        mid = jnp.concatenate([column_blocks(w_cross[:, 0], 4), column_blocks(w_cross_out, 4)], axis=2)
        mid = gather_rows(trade(mid).reshape(4 * shard_rows, 2 * group), DATA)
        wide_near, wide_far = trade(wide_near), trade(wide_far)
        mlp = jnp.concatenate(
            [jnp.where(z == 0, wide_near, wide_far), jnp.where(z == 0, wide_far, wide_near)],
            axis=0,
        )
        mlp = gather_rows(mlp.reshape(8 * shard_rows, -1), PAIR_DATA)

        positions = lax.axis_index("y") * local_rows + jnp.arange(local_rows, dtype=jnp.int32)
        ranks = jnp.arange(full_length, dtype=jnp.int32)
        matches = (mask_index[:, :, None] == positions[None, None, :]) & (
            ranks[None, :, None] < mask_count[:, None, None]
        )
        masked = jnp.any(matches, axis=1).reshape(tokens, 1).astype(F32)
        gains = layer_order(norm_gains)
        gain_a, gain_b, gain_c = gains[:1], gains[1:2], gains[2:]
        start_x, attn_in, grad_top = start(
            outer(hidden.reshape(tokens, width), layer_order),
            outer(cotangent.reshape(tokens, width), layer_order),
            masked,
            layer_order(mask_embed)[None],
            gain_a,
            unit,
            order,
        )
        attn_in = gather_tokens(attn_in)

        own_text = mm_t(caption, w_text).astype(BF)
        kv_rows = w_cross[:, 1:].reshape(shard_rows, 2 * width)
        kv_part = mm(own_text, kv_rows).astype(BF)
        kv_part = kv_part.reshape(-1, 2, 4, group).transpose(2, 0, 1, 3).reshape(4, -1, 2 * group)
        text_kv = sum_data(trade(kv_part).astype(F32).sum(axis=0))
        attn_in, text_kv = lax.optimization_barrier((attn_in, text_kv))

        grad_y = outer(grad_top, pair_order)
        grad_y = jnp.concatenate([grad_y, swap(grad_y, "z")], axis=0)
        grad_y = spread(grad_y)

        attn_in, projected = gather_mm(attn_in, rank, first, 0, 3 * group, "qkv_mm")
        self_mixed = self_forward(projected, 2 * images)
        self_mixed, grad_y = lax.optimization_barrier((self_mixed, grad_y))
        parts = scatter_tokens(mm_scatter(self_mixed, rank, first, 3 * group, "out_mm"))
        after_attn, cross_in = add_norm([start_x] + parts, gain_b)

        cross_in, cross_queries = gather_mm(gather_tokens(cross_in), rank, mid, 0, group, "query_mm")
        cross_mixed = cross_forward(cross_queries, text_kv)
        parts = scatter_tokens(mm_scatter(cross_mixed, rank, mid, group, "cross_out_mm"))
        after_cross, mlp_in = add_norm([after_attn] + parts, gain_c)

        mlp_in = outer(mlp_in, pair_order)
        mlp_in = [gather_tokens(mlp_in), gather_tokens(swap(mlp_in, "z"))]
        runs = [
            feed_forward(mlp_in[side], grad_y, side, rank, mlp, pair_unit, pair)
            for side in range(2)
        ]
        mlp_in, mlp_grad_y, activated, grad_pre = zip(*runs)
        back = [mm_scatter(grad_pre[s], rank, mlp, 0, "up_back", pair_unit, pair) for s in range(2)]
        back, grad_pre = lax.optimization_barrier((back, grad_pre))
        mlp_part = grad_products([(mlp_grad_y, activated), (mlp_in, grad_pre)], "mlp_grads")
        mlp_rows = scatter_grad(mlp_part, PAIR_DATA)
        near = scatter_tokens(back[0])
        far = sum(part.astype(F32) for part in scatter_tokens(back[1])).astype(BF)
        terms = near + [swap(far, "z")]
        if not inside:
            terms = [pair_order(sum(part.astype(F32) for part in terms))]
        grad_after_cross, cross_branch, gain_grad_c = norm_back(terms, grad_top, after_cross, gain_c)

        cross_branch, grad_cross_mixed = gather_mm(
            gather_tokens(cross_branch), rank, mid, group, group, "cross_out_back"
        )
        grad_cq, kv_grad = cross_back(cross_queries, text_kv, grad_cross_mixed)
        parts = scatter_tokens(mm_scatter(grad_cq, rank, mid, 0, "query_back"))
        grad_after_attn, attn_branch, gain_grad_b = norm_back(
            parts, grad_after_cross, after_attn, gain_b
        )
        cross_part = grad_products(
            [([cross_in], [grad_cq]), ([cross_branch], [cross_mixed])], "cross_grads"
        )
        cross_part, mlp_rows = lax.optimization_barrier((cross_part, mlp_rows))
        cross_rows = scatter_grad(cross_part, DATA)

        attn_branch, grad_self_mixed = gather_mm(
            gather_tokens(attn_branch), rank, first, 3 * group, group, "out_back"
        )
        grad_projected = self_back(projected, grad_self_mixed, 2 * images)
        attn_part = grad_products(
            [([attn_in], [grad_projected]), ([attn_branch], [self_mixed])], "attn_grads"
        )
        attn_part, cross_rows = lax.optimization_barrier((attn_part, cross_rows))
        attn_rows = scatter_grad(attn_part, DATA)
        grad_projected, activated, kv_grad, mlp_rows, attn_part = lax.optimization_barrier(
            (grad_projected, activated, kv_grad, mlp_rows, attn_part)
        )
        grad_attn = mm_t(grad_projected, first[:, : 3 * group]).astype(BF)
        grad_attn = trade(grad_attn.reshape(4, tokens, width))
        grad_hidden, gain_grad_a, mask_grad = last_back(
            [(grad_attn, k) for k in range(4)],
            grad_after_attn,
            start_x,
            gain_a,
            masked,
            unit,
            order,
        )
        sums = jnp.concatenate([gain_grad_a, gain_grad_b, gain_grad_c, mask_grad], axis=0)
        sums = layer_order(sum_all(sums))

        active = jnp.concatenate([a.reshape(4, tokens, -1) for a in activated], axis=1)
        result = mm_t(active.reshape(8 * tokens, -1), mlp[:, mlp.shape[1] // 2 :]).astype(BF)
        result = trade(result.reshape(4, 2 * tokens, width))
        far = swap(result[:, tokens:].astype(F32).sum(axis=0).astype(BF), "z")
        terms = [(result, k) for k in range(4)] + [far]
        if not inside:
            near = result[:, :tokens].astype(F32).sum(axis=0)
            terms = [pair_order(near + far.astype(F32))]
        output = layer_output(after_cross, terms, pair_unit, pair, unit, order)

        kv_grads = spread(sum_data(kv_grad)).reshape(4, -1, 2, group)
        kv_grads = kv_grads.transpose(1, 2, 0, 3).reshape(-1, 2 * width)
        kv_weight_grad = t_mm(own_text, kv_grads)
        grad_text = mm_t(kv_grads, kv_rows).astype(BF)
        grad_text_w = t_mm(grad_text, caption)
        caption_part = column_blocks(mm(grad_text, w_text).astype(BF), 4)
        caption_own = sum_data(trade(caption_part).astype(F32).sum(axis=0))
        grad_caption = spread(caption_own).transpose(1, 0, 2).reshape(-1, text_width).astype(F32)

        half_rows = 4 * shard_rows
        near = lax.dynamic_slice_in_dim(mlp_rows, z * half_rows, half_rows, 0)
        far = swap(lax.dynamic_slice_in_dim(mlp_rows, (1 - z) * half_rows, half_rows, 0), "z")
        near, far = (trade(part.reshape(4, shard_rows, -1)) for part in (near, far))
        down_grad, up_grad = finish_pair(near, far, z)
        grad_cross, cross_out_grad = finish_cross(
            trade(cross_rows.reshape(4, shard_rows, -1)), kv_weight_grad
        )
        qkv_grad, out_grad = finish_attention(trade(attn_rows.reshape(4, shard_rows, -1)))
        return (
            outer(output, layer_order).reshape(hidden.shape),
            outer(grad_hidden, layer_order).reshape(hidden.shape),
            grad_caption,
            sums[:3],
            sums[3],
            qkv_grad,
            out_grad,
            grad_cross,
            cross_out_grad,
            grad_text_w,
            up_grad,
            down_grad,
        )

    return local


def solution(mesh):
    z_size = mesh.shape["img"] // 4
    inner = Mesh(mesh.devices.reshape(z_size // 2, 2, 2, 2, 2), ("w", "z", "x", "c", "y"))
    image = ("w", "z", "x", "c")
    tokens = P(image, "y", None)
    rows = P(image + ("y",))
    in_specs = (tokens, P(image, None), P(image), P(), P(), P()) + (rows,) * 7 + (tokens,)
    out_specs = (tokens, tokens, P(), P(), P()) + (rows,) * 7
    return jax.shard_map(
        make_local(z_size), mesh=inner, in_specs=in_specs, out_specs=out_specs, check_vma=False
    )
```

```python
import math

import jax
import jax.numpy as jnp
from jax import lax
from jax.experimental import pallas as pl
from jax.experimental.pallas import tpu as pltpu
from jax.sharding import Mesh
from jax.sharding import PartitionSpec as P

HD = 128
EPS = 1e-05
BF = jnp.bfloat16
F32 = jnp.float32
PAIR = ((0, 1), (1, 0))
GROUP = ("x", "y")
DATA = ("z", "c")
VMEM = 48 * 1024 * 1024
SCALE = 1.0 / math.sqrt(HD)
SLOPE = math.sqrt(2.0 / math.pi)
CUBIC = 0.044715


def dot(a, b, dims):
    return lax.dot_general(a, b, (dims, ((), ())), preferred_element_type=F32)


def mm(a, b):
    return dot(a, b, ((1,), (0,)))


def mm_t(a, b):
    return dot(a, b, ((1,), (1,)))


def t_mm(a, b):
    return dot(a, b, ((0,), (0,)))


def shape(dims, dtype=BF):
    return jax.ShapeDtypeStruct(dims, dtype)


def swap(values, axis):
    return lax.ppermute(values, axis, PAIR)


def trade(blocks, axes=GROUP):
    return lax.all_to_all(blocks, axes, 0, 0, tiled=True)


def spread(values, axes=GROUP, count=4):
    return trade(jnp.broadcast_to(values[None], (count,) + values.shape), axes)


def gather_tokens(own):
    half = own.shape[0] // 2
    from_x = swap(own, "x")
    from_y = swap(own, "y")
    return own, from_y, from_x, swap(from_x[:half], "y"), swap(from_y[half:], "x")


def scatter_tokens(parts):
    own, for_y, for_x, for_low, for_high = parts
    half = for_low.shape[0]
    low = swap(for_low, "y").astype(F32) + for_x[:half].astype(F32)
    high = swap(for_high, "x").astype(F32) + for_y[half:].astype(F32)
    from_x = swap(jnp.concatenate([low.astype(BF), for_x[half:]], axis=0), "x")
    from_y = swap(jnp.concatenate([for_y[:half], high.astype(BF)], axis=0), "y")
    return [own, from_x, from_y]


def swap_blocks(blocks, rank):
    parts = [lax.dynamic_index_in_dim(blocks, rank ^ k, 0, keepdims=False) for k in range(4)]
    return [
        parts[0],
        swap(parts[1], "y"),
        swap(parts[2], "x"),
        lax.ppermute(parts[3], GROUP, ((0, 3), (1, 2), (2, 1), (3, 0))),
    ]


def gather_rows(rows):
    return lax.all_gather(rows.reshape(-1, rows.shape[-1]), DATA, axis=0, tiled=True)


def scatter_grad(partial):
    summed = lax.psum_scatter(partial, DATA, scatter_dimension=0, tiled=True)
    return summed.reshape(4, -1, summed.shape[-1])


def call(kernel, grid, in_specs, out_specs, out_shape, operands, name, flops=0, size=1 << 22,
         rank=None, scratch=()):
    options = dict(
        out_shape=out_shape,
        compiler_params=pltpu.CompilerParams(vmem_limit_bytes=VMEM),
        cost_estimate=pl.CostEstimate(flops=flops, bytes_accessed=size, transcendentals=0),
        name=name,
    )
    if rank is None:
        return pl.pallas_call(
            kernel, grid=grid, in_specs=in_specs, out_specs=out_specs, scratch_shapes=scratch,
            **options,
        )(*operands)
    spec = pltpu.PrefetchScalarGridSpec(
        num_scalar_prefetch=1,
        grid=grid,
        in_specs=in_specs,
        out_specs=out_specs,
        scratch_shapes=scratch,
    )
    return pl.pallas_call(kernel, grid_spec=spec, **options)(rank.reshape(1), *operands)


def whole(array):
    return pl.BlockSpec(array.shape, lambda *_: (0,) * len(array.shape))


def reorder(values, unit, order):
    if order is None:
        return values
    return jnp.concatenate([values[:, k * unit : (k + 1) * unit] for k in order], axis=1)


def assemble(target, pieces, rank):
    rows, half = pieces[0].shape[0], pieces[3].shape[0]
    for k in range(3):
        target[pl.ds(pl.multiple_of((rank ^ k) * rows, rows), rows), :] = pieces[k][...]
    at = pl.multiple_of((rank ^ 3) * rows, rows)
    target[pl.ds(at, half), :] = pieces[3][...]
    target[pl.ds(pl.multiple_of(at + half, half), half), :] = pieces[4][...]


def gather_mm(pieces, rank, weight, first, columns, name):
    rows, width = pieces[0].shape
    step = 256

    def kernel(r, *refs):
        tokens, out = refs[6], refs[7]

        @pl.when(pl.program_id(0) == 0)
        def _():
            assemble(tokens, refs[:5], r[0])

        out[...] = mm(tokens[...], refs[5][...]).astype(BF)

    return call(
        kernel,
        (columns // step,),
        [whole(p) for p in pieces]
        + [pl.BlockSpec((width, step), lambda j, r: (0, first // step + j))],
        [
            pl.BlockSpec((4 * rows, width), lambda j, r: (0, 0)),
            pl.BlockSpec((4 * rows, step), lambda j, r: (0, j)),
        ],
        [shape((4 * rows, width)), shape((4 * rows, columns))],
        [*pieces, weight],
        name,
        flops=8 * rows * width * columns,
        size=2 * width * (columns + 8 * rows),
        rank=rank,
    )


def mm_scatter(values, rank, weight, first, name):
    tokens, depth = values.shape
    rows = tokens // 4
    width = weight.shape[0]
    step = 512

    def kernel(r, x, w, own, for_y, for_x, low, high, total):
        total[...] = mm_t(x[...], w[...])

        def block(k):
            return total[pl.ds(pl.multiple_of((r[0] ^ k) * rows, rows), rows), :]

        own[...] = block(0)
        for_y[...] = block(1).astype(BF)
        for_x[...] = block(2).astype(BF)
        diagonal = block(3).astype(BF)
        low[...] = diagonal[: rows // 2]
        high[...] = diagonal[rows // 2 :]

    sizes = [rows, rows, rows, rows // 2, rows // 2]
    return call(
        kernel,
        (width // step,),
        [
            pl.BlockSpec((tokens, depth), lambda j, r: (0, 0)),
            pl.BlockSpec((step, depth), lambda j, r: (j, first // depth)),
        ],
        [pl.BlockSpec((n, step), lambda j, r: (0, j)) for n in sizes],
        [shape((n, width), F32 if k == 0 else BF) for k, n in enumerate(sizes)],
        [values, weight],
        name,
        flops=2 * tokens * depth * width,
        size=2 * width * (depth + 6 * rows),
        rank=rank,
        scratch=[pltpu.VMEM((tokens, step), F32)],
    )


def normalize(values):
    centred = values - jnp.mean(values, axis=-1, keepdims=True)
    inv_std = lax.rsqrt(jnp.mean(centred * centred, axis=-1, keepdims=True) + EPS)
    return centred * inv_std, inv_std


NORM_ROWS = 32


def row_spec(array, at=None):
    width = array.shape[-1]
    if at is None:
        return pl.BlockSpec((NORM_ROWS, width), lambda i: (i, 0))
    return pl.BlockSpec((1, NORM_ROWS, width), lambda i, at=at: (at, i, 0))


def terms_of(terms):
    arrays, specs = [], []
    for term in terms:
        array, at = term if isinstance(term, tuple) else (term, None)
        arrays.append(array)
        specs.append(row_spec(array, at))
    return arrays, specs


def total_of(refs):
    values = [ref[0] if len(ref.shape) == 3 else ref[...] for ref in refs]
    return sum(value.astype(F32) for value in values)


def add_norm(terms, gain):
    arrays, specs = terms_of(terms)
    tokens, width = arrays[0].shape[-2], arrays[0].shape[-1]
    tokens = min(a.shape[-2] for a in arrays)

    def kernel(*refs):
        gain_ref, x, out = refs[-3:]
        values = total_of(refs[:-3])
        x[...] = values
        out[...] = (normalize(values)[0] * gain_ref[...]).astype(BF)

    return call(
        kernel,
        (tokens // NORM_ROWS,),
        specs + [whole(gain)],
        [row_spec(shape((tokens, width)))] * 2,
        [shape((tokens, width), F32), shape((tokens, width))],
        [*arrays, gain],
        "add_norm",
    )


def norm_grad(grad, values, gain):
    normed, inv_std = normalize(values)
    scaled = grad * gain
    first_mean = jnp.mean(scaled, axis=-1, keepdims=True)
    second_mean = jnp.mean(scaled * normed, axis=-1, keepdims=True)
    return (
        inv_std * (scaled - first_mean - normed * second_mean),
        jnp.sum(grad * normed, axis=0, keepdims=True),
    )


def accumulate(ref, value):
    @pl.when(pl.program_id(0) == 0)
    def _():
        ref[...] = jnp.zeros_like(ref)

    ref[...] += value


def norm_back(terms, upper, values, gain):
    arrays, specs = terms_of(terms)
    tokens, width = values.shape

    def kernel(*refs):
        upper_ref, x, gain_ref, out, out_low, gain_grad = refs[-6:]
        back, part = norm_grad(total_of(refs[:-6]), x[...], gain_ref[...])
        result = upper_ref[...].astype(F32) + back
        out[...] = result
        out_low[...] = result.astype(BF)
        accumulate(gain_grad, part)

    return call(
        kernel,
        (tokens // NORM_ROWS,),
        specs + [row_spec(upper), row_spec(values), whole(gain)],
        [row_spec(values)] * 2 + [pl.BlockSpec((1, width), lambda i: (0, 0))],
        [shape((tokens, width), F32), shape((tokens, width)), shape((1, width), F32)],
        [*arrays, upper, values, gain],
        "norm_back",
    )


def last_back(terms, upper, values, gain, masked, unit, order):
    arrays, specs = terms_of(terms)
    tokens, width = values.shape

    def kernel(*refs):
        upper_ref, x, gain_ref, mask, out, gain_grad, mask_grad = refs[-7:]
        back, part = norm_grad(total_of(refs[:-7]), x[...], gain_ref[...])
        result = upper_ref[...].astype(F32) + back
        hit = mask[...] > 0.5
        out[...] = reorder(jnp.where(hit, 0.0, result).astype(BF), unit, order)
        accumulate(gain_grad, part)
        accumulate(mask_grad, jnp.sum(jnp.where(hit, result, 0.0), axis=0, keepdims=True))

    line = pl.BlockSpec((1, width), lambda i: (0, 0))
    return call(
        kernel,
        (tokens // NORM_ROWS,),
        specs + [row_spec(upper), row_spec(values), whole(gain), row_spec(masked)],
        [row_spec(values), line, line],
        [shape((tokens, width)), shape((1, width), F32), shape((1, width), F32)],
        [*arrays, upper, values, gain, masked],
        "last_back",
    )


def start(hidden, cotangent, masked, embed, gain, unit, order):
    tokens, width = hidden.shape

    def kernel(hid, cot, mask, embed_ref, gain_ref, x, out, grad):
        hit = mask[...] > 0.5
        values = jnp.where(
            hit, embed_ref[...], reorder(hid[...], unit, order).astype(F32)
        )
        x[...] = values
        out[...] = (normalize(values)[0] * gain_ref[...]).astype(BF)
        grad[...] = jnp.where(hit, reorder(cot[...], unit, order).astype(F32), 0.0).astype(BF)

    rows = row_spec(hidden)
    return call(
        kernel,
        (tokens // NORM_ROWS,),
        [rows, rows, row_spec(masked), whole(embed), whole(gain)],
        [rows] * 3,
        [shape((tokens, width), F32), shape((tokens, width)), shape((tokens, width))],
        [hidden, cotangent, masked, embed, gain],
        "start",
    )


def layer_output(upper, terms, unit, order):
    arrays, specs = terms_of(terms)
    tokens, width = upper.shape

    def kernel(*refs):
        values = refs[-2][...] + total_of(refs[:-2])
        refs[-1][...] = reorder(values.astype(BF), unit, order)

    return call(
        kernel,
        (tokens // NORM_ROWS,),
        specs + [row_spec(upper)],
        row_spec(upper),
        shape((tokens, width)),
        [*arrays, upper],
        "layer_output",
    )


def feed_up(pieces, rank, weight):
    rows, width = pieces[0].shape
    hidden = weight.shape[1]
    step = 256

    def kernel(r, *refs):
        up, tokens, act, slope = refs[5:]

        @pl.when(pl.program_id(0) == 0)
        def _():
            assemble(tokens, refs[:5], r[0])

        u = mm(tokens[...], up[...])
        square = u * u
        bend = jnp.tanh(SLOPE * u * (1.0 + CUBIC * square))
        half = 0.5 * (1.0 + bend)
        act[...] = (u * half).astype(BF)
        slope[...] = half + 0.5 * u * (1.0 - bend * bend) * SLOPE * (1.0 + 3.0 * CUBIC * square)

    part = pl.BlockSpec((4 * rows, step), lambda j, r: (0, j))
    return call(
        kernel,
        (hidden // step,),
        [whole(p) for p in pieces] + [pl.BlockSpec((width, step), lambda j, r: (0, j))],
        [pl.BlockSpec((4 * rows, width), lambda j, r: (0, 0)), part, part],
        [shape((4 * rows, width)), shape((4 * rows, hidden)), shape((4 * rows, hidden), F32)],
        [*pieces, weight],
        "feed_up",
        flops=8 * rows * width * hidden,
        size=2 * width * (hidden + 8 * rows),
        rank=rank,
    )


def feed_down(grad_y, slope, weight):
    tokens, width = grad_y.shape
    hidden = weight.shape[1]
    step = 256

    def kernel(dy, slope_ref, down, out):
        out[...] = (mm(dy[...], down[...]) * slope_ref[...]).astype(BF)

    part = pl.BlockSpec((tokens, step), lambda j: (0, j))
    return call(
        kernel,
        (hidden // step,),
        [whole(grad_y), part, pl.BlockSpec((width, step), lambda j: (0, j))],
        part,
        shape((tokens, hidden)),
        [grad_y, slope, weight],
        "feed_down",
        flops=2 * tokens * width * hidden,
        size=2 * width * (hidden + 8 * tokens),
    )


def softmax(scores):
    exp_terms = jnp.exp(scores - jnp.max(scores, axis=-1, keepdims=True))
    return exp_terms / jnp.sum(exp_terms, axis=-1, keepdims=True)


def score_grad(probs, grad_probs):
    return (
        probs * (grad_probs - jnp.sum(probs * grad_probs, axis=-1, keepdims=True))
    ).astype(BF)


def head(ref, k):
    return ref[:, k * HD : (k + 1) * HD]


def self_forward(projected, images):
    tokens, width = projected.shape
    rows, group = tokens // images, width // 3
    heads = group // HD

    def kernel(proj, mixed):
        for k in range(heads):
            query, key, value = (head(proj, j * heads + k) for j in range(3))
            probs = softmax(mm_t(query, key) * SCALE).astype(BF)
            mixed[:, k * HD : (k + 1) * HD] = mm(probs, value).astype(BF)

    return call(
        kernel,
        (images,),
        [pl.BlockSpec((rows, width), lambda i: (i, 0))],
        pl.BlockSpec((rows, group), lambda i: (i, 0)),
        shape((tokens, group)),
        [projected],
        "self_forward",
        flops=4 * tokens * rows * group,
    )


def self_back(projected, grad_mixed, images):
    tokens, width = projected.shape
    rows, group = tokens // images, width // 3
    heads = group // HD

    def kernel(proj, grad, out):
        for k in range(heads):
            query, key, value = (head(proj, j * heads + k) for j in range(3))
            grad_head = head(grad, k)
            probs = softmax(mm_t(query, key) * SCALE)
            grad_scores = score_grad(probs, mm_t(grad_head, value))
            parts = (
                mm(grad_scores, key) * SCALE,
                t_mm(grad_scores, query) * SCALE,
                t_mm(probs.astype(BF), grad_head),
            )
            for j, part in enumerate(parts):
                at = (j * heads + k) * HD
                out[:, at : at + HD] = part.astype(BF)

    return call(
        kernel,
        (images,),
        [
            pl.BlockSpec((rows, width), lambda i: (i, 0)),
            pl.BlockSpec((rows, group), lambda i: (i, 0)),
        ],
        pl.BlockSpec((rows, width), lambda i: (i, 0)),
        shape((tokens, width)),
        [projected, grad_mixed],
        "self_back",
        flops=10 * tokens * rows * group,
    )


def cross_forward(queries, text_kv):
    tokens, group = queries.shape
    heads = group // HD

    def kernel(query, text, mixed):
        for k in range(heads):
            probs = softmax(mm_t(head(query, k), head(text, k)) * SCALE).astype(BF)
            mixed[:, k * HD : (k + 1) * HD] = mm(probs, head(text, heads + k)).astype(BF)

    return call(
        kernel,
        (1,),
        [whole(queries), whole(text_kv)],
        whole(queries),
        shape((tokens, group)),
        [queries, text_kv],
        "cross_forward",
        flops=4 * tokens * text_kv.shape[0] * group,
    )


def cross_back(queries, text_kv, grad_mixed):
    tokens, group = queries.shape
    context = text_kv.shape[0]
    heads = group // HD

    def kernel(query, text, grad, grad_query, grad_text):
        for k in range(heads):
            query_head, key, value = head(query, k), head(text, k), head(text, heads + k)
            grad_head = head(grad, k)
            probs = softmax(mm_t(query_head, key) * SCALE)
            grad_scores = score_grad(probs, mm_t(grad_head, value))
            grad_query[:, k * HD : (k + 1) * HD] = (mm(grad_scores, key) * SCALE).astype(BF)
            at = (heads + k) * HD
            grad_text[:, k * HD : (k + 1) * HD] = t_mm(grad_scores, query_head) * SCALE
            grad_text[:, at : at + HD] = t_mm(probs.astype(BF), grad_head)

    return call(
        kernel,
        (1,),
        [whole(queries), whole(text_kv), whole(grad_mixed)],
        [whole(queries), whole(text_kv)],
        [shape((tokens, group)), shape((context, 2 * group), F32)],
        [queries, text_kv, grad_mixed],
        "cross_back",
        flops=10 * tokens * context * group,
    )


def grad_products(pairs, name):
    blocks = len(pairs[0][0])
    tokens, width = pairs[0][0][0].shape
    widths = [y[0].shape[1] for _, y in pairs]
    total = sum(widths)
    rows = 256
    step = 512
    count = len(pairs) * blocks

    def kernel(*refs):
        out = refs[2 * count]
        offset = 0
        for k, wide in enumerate(widths):
            left = [refs[k * blocks + b][...].T for b in range(blocks)]
            for at in range(0, wide, step):
                out[:, offset + at : offset + at + step] = sum(
                    mm(left[b], refs[count + k * blocks + b][:, at : at + step])
                    for b in range(blocks)
                ).astype(BF)
            offset += wide

    return call(
        kernel,
        (width // rows,),
        [pl.BlockSpec((tokens, rows), lambda i: (0, i))] * count
        + [pl.BlockSpec((tokens, w), lambda i: (0, 0)) for w in widths for _ in range(blocks)],
        pl.BlockSpec((rows, total), lambda i: (i, 0)),
        shape((width, total)),
        [b for x, _ in pairs for b in x] + [b for _, y in pairs for b in y],
        name,
        flops=2 * tokens * blocks * width * total,
        size=4 * width * total,
    )


def place(parts, rank):
    def kernel(r, *refs):
        for k in range(4):

            @pl.when(pl.program_id(0) == k)
            def _():
                refs[4][0] = refs[k][...]

    rows, columns = parts[0].shape
    return call(
        kernel,
        (4,),
        [whole(p) for p in parts],
        pl.BlockSpec((1, rows, columns), lambda k, r: (k ^ r[0], 0, 0)),
        shape((4, rows, columns)),
        parts,
        "place",
        rank=rank,
    )


def finish_wide(blocks):
    count, rows, width = blocks.shape

    def kernel(ref, out):
        out[...] = ref[0].astype(F32)

    return call(
        kernel,
        (count,),
        [pl.BlockSpec((1, rows, width), lambda k: (k, 0, 0))],
        pl.BlockSpec((rows, width), lambda k: (0, k)),
        shape((rows, count * width), F32),
        [blocks],
        "finish_wide",
    )


def finish_all(parts, text_grad, rank):
    rows, total = parts[0].shape
    width = total // 6

    def kernel(r, *refs):
        key, value, three, out, cross, cross_out = refs[4:]
        for k in range(4):

            @pl.when(pl.program_id(0) == k)
            def _():
                def part(j):
                    return refs[k][:, j * width : (j + 1) * width].astype(F32)

                for j in range(3):
                    three[:, j, :] = part(j)
                out[...] = part(3)
                cross[:, 0, :] = part(4)
                cross_out[...] = part(5)

        cross[:, 1, :] = key[...]
        cross[:, 2, :] = value[...]

    wide = pl.BlockSpec((rows, 3, width), lambda k, r: (0, 0, k ^ r[0]))
    flat = pl.BlockSpec((rows, width), lambda k, r: (0, k ^ r[0]))
    return call(
        kernel,
        (4,),
        [whole(p) for p in parts]
        + [flat, pl.BlockSpec((rows, width), lambda k, r: (0, 4 + (k ^ r[0])))],
        [wide, flat, wide, flat],
        [shape((rows, 3, 4 * width), F32), shape((rows, 4 * width), F32)] * 2,
        [*parts, text_grad, text_grad],
        "finish_all",
        rank=rank,
    )


def column_blocks(weight, count):
    rows = weight.shape[0]
    return weight.reshape(rows, count, -1).transpose(1, 0, 2)


def make_local(z_size):
    def sum_data(values):
        rows, columns = values.shape
        core = lax.axis_index("c")
        halves = values.reshape(2, rows // 2, columns)
        keep = lax.dynamic_index_in_dim(halves, core, 0, keepdims=False)
        send = lax.dynamic_index_in_dim(halves, 1 - core, 0, keepdims=False)
        mine = (keep + swap(send, "c")).astype(BF).reshape(z_size, -1, columns)
        mine = trade(mine, "z").astype(F32).sum(axis=0).astype(BF)
        mine = spread(mine, "z", z_size).reshape(rows // 2, columns)
        other = swap(mine, "c")
        return jnp.concatenate(
            [jnp.where(core == 0, mine, other), jnp.where(core == 0, other, mine)], axis=0
        )

    def sum_all(values):
        for axis in ("c", "x", "y"):
            values = values + swap(values, axis)
        step = 1
        while step < z_size:
            values = values + lax.ppermute(
                values, "z", tuple((k, k ^ step) for k in range(z_size))
            )
            step *= 2
        return values

    def layer_order(values):
        shaped = values.reshape(values.shape[:-1] + (z_size, 2, 2, -1))
        return jnp.swapaxes(shaped, -3, -2).reshape(values.shape)

    def local(
        hidden,
        mask_index,
        mask_count,
        mask_embed,
        norm_gains,
        caption,
        w_qkv,
        w_out,
        w_cross,
        w_cross_out,
        w_text,
        w_up,
        w_down,
        cotangent,
    ):
        images, local_rows, width = hidden.shape
        full_length = mask_index.shape[1]
        shard_rows = w_qkv.shape[0]
        rank = lax.axis_index("x") * 2 + lax.axis_index("y")
        tokens = images * local_rows
        group = width // 4
        text_width = caption.shape[1]

        unit = width // (4 * z_size)
        inside = unit % 128 == 0
        order = [4 * k + j for k in range(z_size) for j in (0, 2, 1, 3)] if inside else None

        def outer(values):
            return values if inside else layer_order(values)

        first = jnp.concatenate(
            [
                w_qkv.reshape(shard_rows, 3, 4, group)
                .transpose(2, 0, 1, 3)
                .reshape(4, shard_rows, 3 * group),
                column_blocks(w_out, 4),
            ],
            axis=2,
        )
        first = gather_rows(place(swap_blocks(first, rank), rank))
        mid = jnp.concatenate([column_blocks(w_cross[:, 0], 4), column_blocks(w_cross_out, 4)], axis=2)
        mid = gather_rows(trade(mid))
        up = gather_rows(trade(column_blocks(w_up, 4)))
        down = gather_rows(trade(column_blocks(w_down, 4)))

        positions = lax.axis_index("y") * local_rows + jnp.arange(local_rows, dtype=jnp.int32)
        ranks = jnp.arange(full_length, dtype=jnp.int32)
        matches = (mask_index[:, :, None] == positions[None, None, :]) & (
            ranks[None, :, None] < mask_count[:, None, None]
        )
        masked = jnp.any(matches, axis=1).reshape(tokens, 1).astype(F32)
        gains = layer_order(norm_gains)
        gain_a, gain_b, gain_c = gains[:1], gains[1:2], gains[2:]
        start_x, attn_in, grad_top = start(
            outer(hidden.reshape(tokens, width)),
            outer(cotangent.reshape(tokens, width)),
            masked,
            layer_order(mask_embed)[None],
            gain_a,
            unit,
            order,
        )
        attn_in = gather_tokens(attn_in)

        own_text = mm_t(caption, w_text).astype(BF)
        kv_rows = w_cross[:, 1:].reshape(shard_rows, 2 * width)
        kv_part = mm(own_text, kv_rows).astype(BF)
        kv_part = kv_part.reshape(-1, 2, 4, group).transpose(2, 0, 1, 3).reshape(4, -1, 2 * group)
        text_kv = sum_data(trade(kv_part).astype(F32).sum(axis=0))
        attn_in, text_kv = lax.optimization_barrier((attn_in, text_kv))

        grad_y = spread(grad_top).reshape(4 * tokens, width)

        attn_in, projected = gather_mm(attn_in, rank, first, 0, 3 * group, "qkv_mm")
        self_mixed = self_forward(projected, 2 * images)
        self_mixed, grad_y = lax.optimization_barrier((self_mixed, grad_y))
        parts = scatter_tokens(mm_scatter(self_mixed, rank, first, 3 * group, "out_mm"))
        after_attn, cross_in = add_norm([start_x] + parts, gain_b)

        cross_in, cross_queries = gather_mm(gather_tokens(cross_in), rank, mid, 0, group, "query_mm")
        cross_mixed = cross_forward(cross_queries, text_kv)
        parts = scatter_tokens(mm_scatter(cross_mixed, rank, mid, group, "cross_out_mm"))
        after_cross, mlp_in = add_norm([after_attn] + parts, gain_c)

        mlp_in, activated, slope = feed_up(gather_tokens(mlp_in), rank, up)
        down_part = grad_products([([grad_y], [activated])], "down_grads")
        slope, down_part = lax.optimization_barrier((slope, down_part))
        down_rows = scatter_grad(down_part)
        grad_pre = feed_down(grad_y, slope, down)
        parts = mm_scatter(grad_pre, rank, up, 0, "up_back")
        parts, grad_pre = lax.optimization_barrier((parts, grad_pre))
        up_part = grad_products([([mlp_in], [grad_pre])], "up_grads")
        grad_after_cross, cross_branch, gain_grad_c = norm_back(
            scatter_tokens(parts), grad_top, after_cross, gain_c
        )

        cross_branch, grad_cross_mixed = gather_mm(
            gather_tokens(cross_branch), rank, mid, group, group, "cross_out_back"
        )
        grad_cq, kv_grad = cross_back(cross_queries, text_kv, grad_cross_mixed)
        up_part, down_rows, kv_grad = lax.optimization_barrier((up_part, down_rows, kv_grad))
        up_rows = scatter_grad(up_part)
        parts = scatter_tokens(mm_scatter(grad_cq, rank, mid, 0, "query_back"))
        grad_after_attn, attn_branch, gain_grad_b = norm_back(
            parts, grad_after_cross, after_attn, gain_b
        )

        attn_branch, grad_self_mixed = gather_mm(
            gather_tokens(attn_branch), rank, first, 3 * group, group, "out_back"
        )
        grad_projected = self_back(projected, grad_self_mixed, 2 * images)
        rest_part = grad_products(
            [
                ([attn_in], [grad_projected]),
                ([attn_branch], [self_mixed]),
                ([cross_in], [grad_cq]),
                ([cross_branch], [cross_mixed]),
            ],
            "attention_grads",
        )
        grad_projected, activated, kv_grad, rest_part = lax.optimization_barrier(
            (grad_projected, activated, kv_grad, rest_part)
        )
        rest_part, up_rows = lax.optimization_barrier((rest_part, up_rows))
        rest_rows = scatter_grad(rest_part)
        grad_attn = mm_t(grad_projected, first[:, : 3 * group]).astype(BF)
        grad_attn = trade(grad_attn.reshape(4, tokens, width))
        grad_hidden, gain_grad_a, mask_grad = last_back(
            [(grad_attn, k) for k in range(4)],
            grad_after_attn,
            start_x,
            gain_a,
            masked,
            unit,
            order,
        )
        sums = jnp.concatenate([gain_grad_a, gain_grad_b, gain_grad_c, mask_grad], axis=0)
        sums = layer_order(sum_all(sums))

        result = trade(mm_t(activated, down).astype(BF).reshape(4, tokens, width))
        output = layer_output(after_cross, [(result, k) for k in range(4)], unit, order)

        kv_grads = spread(sum_data(kv_grad)).reshape(4, -1, 2, group)
        kv_grads = kv_grads.transpose(1, 2, 0, 3).reshape(-1, 2 * width)
        kv_weight_grad = t_mm(own_text, kv_grads)
        grad_text = mm_t(kv_grads, kv_rows).astype(BF)
        grad_text_w = t_mm(grad_text, caption)
        caption_part = column_blocks(mm(grad_text, w_text).astype(BF), 4)
        caption_own = sum_data(trade(caption_part).astype(F32).sum(axis=0))
        grad_caption = spread(caption_own).transpose(1, 0, 2).reshape(-1, text_width).astype(F32)

        down_grad = finish_wide(trade(down_rows))
        up_grad = finish_wide(trade(up_rows))
        qkv_grad, out_grad, grad_cross, cross_out_grad = finish_all(
            swap_blocks(rest_rows, rank), kv_weight_grad, rank
        )
        return (
            outer(output).reshape(hidden.shape),
            outer(grad_hidden).reshape(hidden.shape),
            grad_caption,
            sums[:3],
            sums[3],
            qkv_grad,
            out_grad,
            grad_cross,
            cross_out_grad,
            grad_text_w,
            up_grad,
            down_grad,
        )

    return local


def solution(mesh):
    z_size = mesh.shape["img"] // 4
    inner = Mesh(mesh.devices.reshape(z_size, 2, 2, 2), ("z", "x", "c", "y"))
    image = ("z", "x", "c")
    tokens = P(image, "y", None)
    rows = P(image + ("y",))
    in_specs = (tokens, P(image, None), P(image), P(), P(), P()) + (rows,) * 7 + (tokens,)
    out_specs = (tokens, tokens, P(), P(), P()) + (rows,) * 7
    return jax.shard_map(
        make_local(z_size), mesh=inner, in_specs=in_specs, out_specs=out_specs, check_vma=False
    )
```

```python
import math

import jax
import jax.numpy as jnp
from jax import lax
from jax.experimental import pallas as pl
from jax.experimental.pallas import tpu as pltpu
from jax.sharding import Mesh
from jax.sharding import PartitionSpec as P

HD = 128
EPS = 1e-05
BF = jnp.bfloat16
F32 = jnp.float32
PAIR = ((0, 1), (1, 0))
GROUP = ("x", "y")
DATA = ("z", "c")
PLANE = ("x", "c", "y")
VMEM = 48 * 1024 * 1024
SCALE = 1.0 / math.sqrt(HD)
SLOPE = math.sqrt(2.0 / math.pi)
CUBIC = 0.044715


def dot(a, b, dims):
    return lax.dot_general(a, b, (dims, ((), ())), preferred_element_type=F32)


def mm(a, b):
    return dot(a, b, ((1,), (0,)))


def mm_t(a, b):
    return dot(a, b, ((1,), (1,)))


def t_mm(a, b):
    return dot(a, b, ((0,), (0,)))


def shape(dims, dtype=BF):
    return jax.ShapeDtypeStruct(dims, dtype)


def swap(values, axis):
    return lax.ppermute(values, axis, PAIR)


def trade(blocks, axes=GROUP):
    return lax.all_to_all(blocks, axes, 0, 0, tiled=True)


def spread(values, axes=GROUP, count=4):
    return trade(jnp.broadcast_to(values[None], (count,) + values.shape), axes)


def gather_tokens(own):
    half = own.shape[0] // 2
    from_x = swap(own, "x")
    from_y = swap(own, "y")
    return own, from_y, from_x, swap(from_x[:half], "y"), swap(from_y[half:], "x")


def scatter_tokens(parts):
    own, for_y, for_x, for_low, for_high = parts
    half = for_low.shape[0]
    low = swap(for_low, "y").astype(F32) + for_x[:half].astype(F32)
    high = swap(for_high, "x").astype(F32) + for_y[half:].astype(F32)
    from_x = swap(jnp.concatenate([low.astype(BF), for_x[half:]], axis=0), "x")
    from_y = swap(jnp.concatenate([for_y[:half], high.astype(BF)], axis=0), "y")
    return [own, from_x, from_y]


def swap_blocks(blocks, rank):
    parts = [lax.dynamic_index_in_dim(blocks, rank ^ k, 0, keepdims=False) for k in range(4)]
    return [
        parts[0],
        swap(parts[1], "y"),
        swap(parts[2], "x"),
        lax.ppermute(parts[3], GROUP, ((0, 3), (1, 2), (2, 1), (3, 0))),
    ]


def gather_rows(rows):
    return lax.all_gather(rows.reshape(-1, rows.shape[-1]), DATA, axis=0, tiled=True)


def scatter_grad(partial, axes):
    summed = lax.psum_scatter(partial, axes, scatter_dimension=0, tiled=True)
    return summed.reshape(4, -1, summed.shape[-1])


def call(kernel, grid, in_specs, out_specs, out_shape, operands, name, flops=0, size=1 << 22,
         rank=None, scratch=()):
    options = dict(
        out_shape=out_shape,
        compiler_params=pltpu.CompilerParams(vmem_limit_bytes=VMEM),
        cost_estimate=pl.CostEstimate(flops=flops, bytes_accessed=size, transcendentals=0),
        name=name,
    )
    if rank is None:
        return pl.pallas_call(
            kernel, grid=grid, in_specs=in_specs, out_specs=out_specs, scratch_shapes=scratch,
            **options,
        )(*operands)
    spec = pltpu.PrefetchScalarGridSpec(
        num_scalar_prefetch=1,
        grid=grid,
        in_specs=in_specs,
        out_specs=out_specs,
        scratch_shapes=scratch,
    )
    return pl.pallas_call(kernel, grid_spec=spec, **options)(rank.reshape(1), *operands)


def whole(array):
    return pl.BlockSpec(array.shape, lambda *_: (0,) * len(array.shape))


def reorder(values, unit, order):
    if order is None:
        return values
    return jnp.concatenate([values[:, k * unit : (k + 1) * unit] for k in order], axis=1)


def assemble(target, pieces, rank):
    rows, half = pieces[0].shape[0], pieces[3].shape[0]
    for k in range(3):
        target[pl.ds(pl.multiple_of((rank ^ k) * rows, rows), rows), :] = pieces[k][...]
    at = pl.multiple_of((rank ^ 3) * rows, rows)
    target[pl.ds(at, half), :] = pieces[3][...]
    target[pl.ds(pl.multiple_of(at + half, half), half), :] = pieces[4][...]


def gather_mm(pieces, rank, weight, first, columns, name):
    rows, width = pieces[0].shape
    step = 256

    def kernel(r, *refs):
        tokens, out = refs[6], refs[7]

        @pl.when(pl.program_id(0) == 0)
        def _():
            assemble(tokens, refs[:5], r[0])

        out[...] = mm(tokens[...], refs[5][...]).astype(BF)

    return call(
        kernel,
        (columns // step,),
        [whole(p) for p in pieces]
        + [pl.BlockSpec((width, step), lambda j, r: (0, first // step + j))],
        [
            pl.BlockSpec((4 * rows, width), lambda j, r: (0, 0)),
            pl.BlockSpec((4 * rows, step), lambda j, r: (0, j)),
        ],
        [shape((4 * rows, width)), shape((4 * rows, columns))],
        [*pieces, weight],
        name,
        flops=8 * rows * width * columns,
        size=2 * width * (columns + 8 * rows),
        rank=rank,
    )


def mm_scatter(values, rank, weight, first, name):
    tokens, depth = values.shape
    rows = tokens // 4
    width = weight.shape[0]
    step = 512

    def kernel(r, x, w, own, for_y, for_x, low, high, total):
        total[...] = mm_t(x[...], w[...])

        def block(k):
            return total[pl.ds(pl.multiple_of((r[0] ^ k) * rows, rows), rows), :]

        own[...] = block(0)
        for_y[...] = block(1).astype(BF)
        for_x[...] = block(2).astype(BF)
        diagonal = block(3).astype(BF)
        low[...] = diagonal[: rows // 2]
        high[...] = diagonal[rows // 2 :]

    sizes = [rows, rows, rows, rows // 2, rows // 2]
    return call(
        kernel,
        (width // step,),
        [
            pl.BlockSpec((tokens, depth), lambda j, r: (0, 0)),
            pl.BlockSpec((step, depth), lambda j, r: (j, first // depth)),
        ],
        [pl.BlockSpec((n, step), lambda j, r: (0, j)) for n in sizes],
        [shape((n, width), F32 if k == 0 else BF) for k, n in enumerate(sizes)],
        [values, weight],
        name,
        flops=2 * tokens * depth * width,
        size=2 * width * (depth + 6 * rows),
        rank=rank,
        scratch=[pltpu.VMEM((tokens, step), F32)],
    )


def normalize(values):
    centred = values - jnp.mean(values, axis=-1, keepdims=True)
    inv_std = lax.rsqrt(jnp.mean(centred * centred, axis=-1, keepdims=True) + EPS)
    return centred * inv_std, inv_std


NORM_ROWS = 32


def row_spec(array, at=None):
    width = array.shape[-1]
    if at is None:
        return pl.BlockSpec((NORM_ROWS, width), lambda i: (i, 0))
    return pl.BlockSpec((1, NORM_ROWS, width), lambda i, at=at: (at, i, 0))


def terms_of(terms):
    arrays, specs = [], []
    for term in terms:
        array, at = term if isinstance(term, tuple) else (term, None)
        arrays.append(array)
        specs.append(row_spec(array, at))
    return arrays, specs


def total_of(refs):
    values = [ref[0] if len(ref.shape) == 3 else ref[...] for ref in refs]
    return sum(value.astype(F32) for value in values)


def add_norm(terms, gain):
    arrays, specs = terms_of(terms)
    tokens, width = arrays[0].shape[-2], arrays[0].shape[-1]
    tokens = min(a.shape[-2] for a in arrays)

    def kernel(*refs):
        gain_ref, x, out = refs[-3:]
        values = total_of(refs[:-3])
        x[...] = values
        out[...] = (normalize(values)[0] * gain_ref[...]).astype(BF)

    return call(
        kernel,
        (tokens // NORM_ROWS,),
        specs + [whole(gain)],
        [row_spec(shape((tokens, width)))] * 2,
        [shape((tokens, width), F32), shape((tokens, width))],
        [*arrays, gain],
        "add_norm",
    )


def norm_grad(grad, values, gain):
    normed, inv_std = normalize(values)
    scaled = grad * gain
    first_mean = jnp.mean(scaled, axis=-1, keepdims=True)
    second_mean = jnp.mean(scaled * normed, axis=-1, keepdims=True)
    return (
        inv_std * (scaled - first_mean - normed * second_mean),
        jnp.sum(grad * normed, axis=0, keepdims=True),
    )


def accumulate(ref, value):
    @pl.when(pl.program_id(0) == 0)
    def _():
        ref[...] = jnp.zeros_like(ref)

    ref[...] += value


def norm_back(terms, upper, values, gain):
    arrays, specs = terms_of(terms)
    tokens, width = values.shape

    def kernel(*refs):
        upper_ref, x, gain_ref, out, out_low, gain_grad = refs[-6:]
        back, part = norm_grad(total_of(refs[:-6]), x[...], gain_ref[...])
        result = upper_ref[...].astype(F32) + back
        out[...] = result
        out_low[...] = result.astype(BF)
        accumulate(gain_grad, part)

    return call(
        kernel,
        (tokens // NORM_ROWS,),
        specs + [row_spec(upper), row_spec(values), whole(gain)],
        [row_spec(values)] * 2 + [pl.BlockSpec((1, width), lambda i: (0, 0))],
        [shape((tokens, width), F32), shape((tokens, width)), shape((1, width), F32)],
        [*arrays, upper, values, gain],
        "norm_back",
    )


def last_back(terms, upper, values, gain, masked, unit, order):
    arrays, specs = terms_of(terms)
    tokens, width = values.shape

    def kernel(*refs):
        upper_ref, x, gain_ref, mask, out, gain_grad, mask_grad = refs[-7:]
        back, part = norm_grad(total_of(refs[:-7]), x[...], gain_ref[...])
        result = upper_ref[...].astype(F32) + back
        hit = mask[...] > 0.5
        out[...] = reorder(jnp.where(hit, 0.0, result).astype(BF), unit, order)
        accumulate(gain_grad, part)
        accumulate(mask_grad, jnp.sum(jnp.where(hit, result, 0.0), axis=0, keepdims=True))

    line = pl.BlockSpec((1, width), lambda i: (0, 0))
    return call(
        kernel,
        (tokens // NORM_ROWS,),
        specs + [row_spec(upper), row_spec(values), whole(gain), row_spec(masked)],
        [row_spec(values), line, line],
        [shape((tokens, width)), shape((1, width), F32), shape((1, width), F32)],
        [*arrays, upper, values, gain, masked],
        "last_back",
    )


def start(hidden, cotangent, masked, embed, gain, unit, order):
    tokens, width = hidden.shape

    def kernel(hid, cot, mask, embed_ref, gain_ref, x, out, grad):
        hit = mask[...] > 0.5
        values = jnp.where(
            hit, embed_ref[...], reorder(hid[...], unit, order).astype(F32)
        )
        x[...] = values
        out[...] = (normalize(values)[0] * gain_ref[...]).astype(BF)
        grad[...] = jnp.where(hit, reorder(cot[...], unit, order).astype(F32), 0.0).astype(BF)

    rows = row_spec(hidden)
    return call(
        kernel,
        (tokens // NORM_ROWS,),
        [rows, rows, row_spec(masked), whole(embed), whole(gain)],
        [rows] * 3,
        [shape((tokens, width), F32), shape((tokens, width)), shape((tokens, width))],
        [hidden, cotangent, masked, embed, gain],
        "start",
    )


def layer_output(upper, terms, unit, order):
    arrays, specs = terms_of(terms)
    tokens, width = upper.shape

    def kernel(*refs):
        values = refs[-2][...] + total_of(refs[:-2])
        refs[-1][...] = reorder(values.astype(BF), unit, order)

    return call(
        kernel,
        (tokens // NORM_ROWS,),
        specs + [row_spec(upper)],
        row_spec(upper),
        shape((tokens, width)),
        [*arrays, upper],
        "layer_output",
    )


def feed_up(pieces, rank, weight):
    rows, width = pieces[0].shape
    hidden = weight.shape[1]
    step = 256

    def kernel(r, *refs):
        up, tokens, act, slope = refs[5:]

        @pl.when(pl.program_id(0) == 0)
        def _():
            assemble(tokens, refs[:5], r[0])

        u = mm(tokens[...], up[...])
        square = u * u
        bend = jnp.tanh(SLOPE * u * (1.0 + CUBIC * square))
        half = 0.5 * (1.0 + bend)
        act[...] = (u * half).astype(BF)
        slope[...] = half + 0.5 * u * (1.0 - bend * bend) * SLOPE * (1.0 + 3.0 * CUBIC * square)

    part = pl.BlockSpec((4 * rows, step), lambda j, r: (0, j))
    return call(
        kernel,
        (hidden // step,),
        [whole(p) for p in pieces] + [pl.BlockSpec((width, step), lambda j, r: (0, j))],
        [pl.BlockSpec((4 * rows, width), lambda j, r: (0, 0)), part, part],
        [shape((4 * rows, width)), shape((4 * rows, hidden)), shape((4 * rows, hidden), F32)],
        [*pieces, weight],
        "feed_up",
        flops=8 * rows * width * hidden,
        size=2 * width * (hidden + 8 * rows),
        rank=rank,
    )


def feed_down(grad_y, slope, weight):
    tokens, width = grad_y.shape
    hidden = weight.shape[1]
    step = 256

    def kernel(dy, slope_ref, down, out):
        out[...] = (mm(dy[...], down[...]) * slope_ref[...]).astype(BF)

    part = pl.BlockSpec((tokens, step), lambda j: (0, j))
    return call(
        kernel,
        (hidden // step,),
        [whole(grad_y), part, pl.BlockSpec((width, step), lambda j: (0, j))],
        part,
        shape((tokens, hidden)),
        [grad_y, slope, weight],
        "feed_down",
        flops=2 * tokens * width * hidden,
        size=2 * width * (hidden + 8 * tokens),
    )


def softmax(scores):
    exp_terms = jnp.exp(scores - jnp.max(scores, axis=-1, keepdims=True))
    return exp_terms / jnp.sum(exp_terms, axis=-1, keepdims=True)


def score_grad(probs, grad_probs):
    return (
        probs * (grad_probs - jnp.sum(probs * grad_probs, axis=-1, keepdims=True))
    ).astype(BF)


def head(ref, k):
    return ref[:, k * HD : (k + 1) * HD]


def self_forward(projected, images):
    tokens, width = projected.shape
    rows, group = tokens // images, width // 3
    heads = group // HD

    def kernel(proj, mixed):
        for k in range(heads):
            query, key, value = (head(proj, j * heads + k) for j in range(3))
            probs = softmax(mm_t(query, key) * SCALE).astype(BF)
            mixed[:, k * HD : (k + 1) * HD] = mm(probs, value).astype(BF)

    return call(
        kernel,
        (images,),
        [pl.BlockSpec((rows, width), lambda i: (i, 0))],
        pl.BlockSpec((rows, group), lambda i: (i, 0)),
        shape((tokens, group)),
        [projected],
        "self_forward",
        flops=4 * tokens * rows * group,
    )


def self_back(projected, grad_mixed, images):
    tokens, width = projected.shape
    rows, group = tokens // images, width // 3
    heads = group // HD

    def kernel(proj, grad, out):
        for k in range(heads):
            query, key, value = (head(proj, j * heads + k) for j in range(3))
            grad_head = head(grad, k)
            probs = softmax(mm_t(query, key) * SCALE)
            grad_scores = score_grad(probs, mm_t(grad_head, value))
            parts = (
                mm(grad_scores, key) * SCALE,
                t_mm(grad_scores, query) * SCALE,
                t_mm(probs.astype(BF), grad_head),
            )
            for j, part in enumerate(parts):
                at = (j * heads + k) * HD
                out[:, at : at + HD] = part.astype(BF)

    return call(
        kernel,
        (images,),
        [
            pl.BlockSpec((rows, width), lambda i: (i, 0)),
            pl.BlockSpec((rows, group), lambda i: (i, 0)),
        ],
        pl.BlockSpec((rows, width), lambda i: (i, 0)),
        shape((tokens, width)),
        [projected, grad_mixed],
        "self_back",
        flops=10 * tokens * rows * group,
    )


def cross_forward(queries, text_kv):
    tokens, group = queries.shape
    heads = group // HD

    def kernel(query, text, mixed):
        for k in range(heads):
            probs = softmax(mm_t(head(query, k), head(text, k)) * SCALE).astype(BF)
            mixed[:, k * HD : (k + 1) * HD] = mm(probs, head(text, heads + k)).astype(BF)

    return call(
        kernel,
        (1,),
        [whole(queries), whole(text_kv)],
        whole(queries),
        shape((tokens, group)),
        [queries, text_kv],
        "cross_forward",
        flops=4 * tokens * text_kv.shape[0] * group,
    )


def cross_back(queries, text_kv, grad_mixed):
    tokens, group = queries.shape
    context = text_kv.shape[0]
    heads = group // HD

    def kernel(query, text, grad, grad_query, grad_text):
        for k in range(heads):
            query_head, key, value = head(query, k), head(text, k), head(text, heads + k)
            grad_head = head(grad, k)
            probs = softmax(mm_t(query_head, key) * SCALE)
            grad_scores = score_grad(probs, mm_t(grad_head, value))
            grad_query[:, k * HD : (k + 1) * HD] = (mm(grad_scores, key) * SCALE).astype(BF)
            at = (heads + k) * HD
            grad_text[:, k * HD : (k + 1) * HD] = t_mm(grad_scores, query_head) * SCALE
            grad_text[:, at : at + HD] = t_mm(probs.astype(BF), grad_head)

    return call(
        kernel,
        (1,),
        [whole(queries), whole(text_kv), whole(grad_mixed)],
        [whole(queries), whole(text_kv)],
        [shape((tokens, group)), shape((context, 2 * group), F32)],
        [queries, text_kv, grad_mixed],
        "cross_back",
        flops=10 * tokens * context * group,
    )


def grad_products(pairs, name, core=None, blocks=0):
    count_in = len(pairs[0][0])
    tokens, width = pairs[0][0][0].shape
    widths = [y[0].shape[1] for _, y in pairs]
    total = sum(widths)
    rows = 256 if core is None else width // (2 * blocks)
    steps = width // rows if core is None else blocks
    step = 512
    count = len(pairs) * count_in

    def kernel(r, *refs):
        out = refs[2 * count]
        offset = 0
        for k, wide in enumerate(widths):
            left = [refs[k * count_in + b][...].T for b in range(count_in)]
            for at in range(0, wide, step):
                out[:, offset + at : offset + at + step] = sum(
                    mm(left[b], refs[count + k * count_in + b][:, at : at + step])
                    for b in range(count_in)
                ).astype(BF)
            offset += wide

    pick = (lambda i, r: (0, i)) if core is None else (lambda i, r: (0, 2 * i + r[0]))
    return call(
        kernel,
        (steps,),
        [pl.BlockSpec((tokens, rows), pick)] * count
        + [pl.BlockSpec((tokens, w), lambda i, r: (0, 0)) for w in widths for _ in range(count_in)],
        pl.BlockSpec((rows, total), lambda i, r: (i, 0)),
        shape((steps * rows, total)),
        [b for x, _ in pairs for b in x] + [b for _, y in pairs for b in y],
        name,
        flops=2 * tokens * count_in * steps * rows * total,
        size=4 * width * total,
        rank=jnp.zeros((), jnp.int32) if core is None else core,
    )


def place(parts, rank):
    def kernel(r, *refs):
        for k in range(4):

            @pl.when(pl.program_id(0) == k)
            def _():
                refs[4][0] = refs[k][...]

    rows, columns = parts[0].shape
    return call(
        kernel,
        (4,),
        [whole(p) for p in parts],
        pl.BlockSpec((1, rows, columns), lambda k, r: (k ^ r[0], 0, 0)),
        shape((4, rows, columns)),
        parts,
        "place",
        rank=rank,
    )


def finish_wide(blocks):
    count, rows, width = blocks.shape

    def kernel(ref, out):
        out[...] = ref[0].astype(F32)

    return call(
        kernel,
        (count,),
        [pl.BlockSpec((1, rows, width), lambda k: (k, 0, 0))],
        pl.BlockSpec((rows, width), lambda k: (0, k)),
        shape((rows, count * width), F32),
        [blocks],
        "finish_wide",
    )


def finish_all(parts, text_grad, rank):
    rows, total = parts[0].shape
    width = total // 6

    def kernel(r, *refs):
        key, value, three, out, cross, cross_out = refs[4:]
        for k in range(4):

            @pl.when(pl.program_id(0) == k)
            def _():
                def part(j):
                    return refs[k][:, j * width : (j + 1) * width].astype(F32)

                for j in range(3):
                    three[:, j, :] = part(j)
                out[...] = part(3)
                cross[:, 0, :] = part(4)
                cross_out[...] = part(5)

        cross[:, 1, :] = key[...]
        cross[:, 2, :] = value[...]

    wide = pl.BlockSpec((rows, 3, width), lambda k, r: (0, 0, k ^ r[0]))
    flat = pl.BlockSpec((rows, width), lambda k, r: (0, k ^ r[0]))
    return call(
        kernel,
        (4,),
        [whole(p) for p in parts]
        + [flat, pl.BlockSpec((rows, width), lambda k, r: (0, 4 + (k ^ r[0])))],
        [wide, flat, wide, flat],
        [shape((rows, 3, 4 * width), F32), shape((rows, 4 * width), F32)] * 2,
        [*parts, text_grad, text_grad],
        "finish_all",
        rank=rank,
    )


def column_blocks(weight, count):
    rows = weight.shape[0]
    return weight.reshape(rows, count, -1).transpose(1, 0, 2)


def make_local(z_size):
    def sum_z(values):
        return spread(values, "z", z_size).astype(F32).sum(axis=0)

    def by_plane(values, parts):
        rows = values.shape[0]
        shaped = values.reshape(2, rows // 2, parts, 2, 2, -1)
        return shaped.transpose(3, 0, 4, 1, 2, 5).reshape(8, rows // 2, -1)

    def from_plane(blocks, parts):
        rows = blocks.shape[1]
        shaped = blocks.reshape(2, 2, 2, rows, parts, -1)
        return shaped.transpose(1, 3, 4, 0, 2, 5).reshape(2 * rows, -1)

    def sum_all(values):
        return sum_z(spread(values, PLANE, 8).sum(axis=0))

    def layer_order(values):
        shaped = values.reshape(values.shape[:-1] + (z_size, 2, 2, -1))
        return jnp.swapaxes(shaped, -3, -2).reshape(values.shape)

    def local(
        hidden,
        mask_index,
        mask_count,
        mask_embed,
        norm_gains,
        caption,
        w_qkv,
        w_out,
        w_cross,
        w_cross_out,
        w_text,
        w_up,
        w_down,
        cotangent,
    ):
        images, local_rows, width = hidden.shape
        full_length = mask_index.shape[1]
        shard_rows = w_qkv.shape[0]
        rank = lax.axis_index("x") * 2 + lax.axis_index("y")
        core = lax.axis_index("c")
        tokens = images * local_rows
        group = width // 4
        text_width = caption.shape[1]

        unit = width // (4 * z_size)
        inside = unit % 128 == 0
        order = [4 * k + j for k in range(z_size) for j in (0, 2, 1, 3)] if inside else None

        def outer(values):
            return values if inside else layer_order(values)

        first = jnp.concatenate(
            [
                w_qkv.reshape(shard_rows, 3, 4, group)
                .transpose(2, 0, 1, 3)
                .reshape(4, shard_rows, 3 * group),
                column_blocks(w_out, 4),
            ],
            axis=2,
        )
        first = gather_rows(place(swap_blocks(first, rank), rank))
        positions = lax.axis_index("y") * local_rows + jnp.arange(local_rows, dtype=jnp.int32)
        ranks = jnp.arange(full_length, dtype=jnp.int32)
        matches = (mask_index[:, :, None] == positions[None, None, :]) & (
            ranks[None, :, None] < mask_count[:, None, None]
        )
        masked = jnp.any(matches, axis=1).reshape(tokens, 1).astype(F32)
        gains = layer_order(norm_gains)
        gain_a, gain_b, gain_c = gains[:1], gains[1:2], gains[2:]
        start_x, attn_in, grad_top = start(
            outer(hidden.reshape(tokens, width)),
            outer(cotangent.reshape(tokens, width)),
            masked,
            layer_order(mask_embed)[None],
            gain_a,
            unit,
            order,
        )
        attn_in = gather_tokens(attn_in)
        mid = jnp.concatenate([column_blocks(w_cross[:, 0], 4), column_blocks(w_cross_out, 4)], axis=2)
        attn_in, mid = lax.optimization_barrier((attn_in, mid))
        mid = gather_rows(trade(mid))

        own_text = mm_t(caption, w_text).astype(BF)
        kv_rows = w_cross[:, 1:].reshape(shard_rows, 2 * width)
        kv_part = by_plane(mm(own_text, kv_rows).astype(BF), 2)
        text_kv = trade(kv_part, PLANE).astype(F32).sum(axis=0).astype(BF)
        text_kv = sum_z(text_kv).astype(BF)
        other = swap(text_kv, "c")
        text_kv = jnp.concatenate(
            [jnp.where(core == 0, text_kv, other), jnp.where(core == 0, other, text_kv)], axis=0
        )
        up = column_blocks(w_up, 4)
        attn_in, text_kv, up = lax.optimization_barrier((attn_in, text_kv, up))
        up = gather_rows(trade(up))

        attn_in, projected = gather_mm(attn_in, rank, first, 0, 3 * group, "qkv_mm")
        down = column_blocks(w_down, 4)
        projected, down, grad_top = lax.optimization_barrier((projected, down, grad_top))
        down = gather_rows(trade(down))
        grad_y = spread(grad_top).reshape(4 * tokens, width)
        self_mixed = self_forward(projected, 2 * images)
        parts = scatter_tokens(mm_scatter(self_mixed, rank, first, 3 * group, "out_mm"))
        after_attn, cross_in = add_norm([start_x] + parts, gain_b)

        cross_in, cross_queries = gather_mm(gather_tokens(cross_in), rank, mid, 0, group, "query_mm")
        cross_mixed = cross_forward(cross_queries, text_kv)
        parts = scatter_tokens(mm_scatter(cross_mixed, rank, mid, group, "cross_out_mm"))
        after_cross, mlp_in = add_norm([after_attn] + parts, gain_c)

        mlp_in, activated, slope = feed_up(gather_tokens(mlp_in), rank, up)
        early = [attn_in, self_mixed, cross_in, cross_mixed]
        if inside:
            grad_axes, halves = "z", (core, z_size)

            def both(values):
                return [values, swap(values, "c")]

        else:
            grad_axes, halves = DATA, ()

            def both(values):
                return [values]

        early = [both(values) for values in early]
        down_part = grad_products([(both(grad_y), both(activated))], "down_grads", *halves)
        mlp_in = both(mlp_in)
        slope, down_part, early, mlp_in = lax.optimization_barrier((slope, down_part, early, mlp_in))
        down_rows = scatter_grad(down_part, grad_axes)
        grad_pre = feed_down(grad_y, slope, down)
        parts = mm_scatter(grad_pre, rank, up, 0, "up_back")
        parts, grad_pre = lax.optimization_barrier((parts, grad_pre))
        up_part = grad_products([(mlp_in, both(grad_pre))], "up_grads", *halves)
        grad_after_cross, cross_branch, gain_grad_c = norm_back(
            scatter_tokens(parts), grad_top, after_cross, gain_c
        )

        cross_branch, grad_cross_mixed = gather_mm(
            gather_tokens(cross_branch), rank, mid, group, group, "cross_out_back"
        )
        grad_cq, kv_grad = cross_back(cross_queries, text_kv, grad_cross_mixed)
        up_part, down_rows, kv_grad = lax.optimization_barrier((up_part, down_rows, kv_grad))
        up_rows = scatter_grad(up_part, grad_axes)
        cross_branch, grad_cq_both = both(cross_branch), both(grad_cq)
        parts = scatter_tokens(mm_scatter(grad_cq, rank, mid, 0, "query_back"))
        grad_after_attn, attn_branch, gain_grad_b = norm_back(
            parts, grad_after_cross, after_attn, gain_b
        )

        attn_branch, grad_self_mixed = gather_mm(
            gather_tokens(attn_branch), rank, first, 3 * group, group, "out_back"
        )
        grad_projected = self_back(projected, grad_self_mixed, 2 * images)
        kv_keep = lax.dynamic_index_in_dim(
            kv_grad.reshape(2, -1, 2 * group), core, 0, keepdims=False
        )
        kv_send = lax.dynamic_index_in_dim(
            kv_grad.reshape(2, -1, 2 * group), 1 - core, 0, keepdims=False
        )
        kv_sum = sum_z((kv_keep + swap(kv_send, "c")).astype(BF)).astype(BF)
        kv_grads = spread(kv_sum, PLANE, 8)
        down_rows = trade(down_rows)
        grad_projected, kv_grads, down_rows = lax.optimization_barrier(
            (grad_projected, kv_grads, down_rows)
        )
        rest_part = grad_products(
            [
                (early[0], both(grad_projected)),
                (both(attn_branch), early[1]),
                (early[2], grad_cq_both),
                (cross_branch, early[3]),
            ],
            "attention_grads",
            *halves,
        )
        grad_projected, activated, kv_grads, rest_part = lax.optimization_barrier(
            (grad_projected, activated, kv_grads, rest_part)
        )
        rest_part, up_rows = lax.optimization_barrier((rest_part, up_rows))
        rest_rows = scatter_grad(rest_part, grad_axes)
        grad_attn = mm_t(grad_projected, first[:, : 3 * group]).astype(BF)
        grad_attn = trade(grad_attn.reshape(4, tokens, width))
        grad_hidden, gain_grad_a, mask_grad = last_back(
            [(grad_attn, k) for k in range(4)],
            grad_after_attn,
            start_x,
            gain_a,
            masked,
            unit,
            order,
        )
        sums = jnp.concatenate([gain_grad_a, gain_grad_b, gain_grad_c, mask_grad], axis=0)
        sums = layer_order(sum_all(sums))

        result = trade(mm_t(activated, down).astype(BF).reshape(4, tokens, width))
        output = layer_output(after_cross, [(result, k) for k in range(4)], unit, order)

        kv_grads = from_plane(kv_grads, 2)
        kv_weight_grad = t_mm(own_text, kv_grads)
        grad_text = mm_t(kv_grads, kv_rows).astype(BF)
        grad_text_w = t_mm(grad_text, caption)
        caption_part = by_plane(mm(grad_text, w_text).astype(BF), 1)
        caption_own = trade(caption_part, PLANE).astype(F32).sum(axis=0).astype(BF)
        caption_own = sum_z(caption_own).astype(BF)
        grad_caption = from_plane(spread(caption_own, PLANE, 8), 1).astype(F32)

        down_grad = finish_wide(down_rows)
        up_grad = finish_wide(trade(up_rows))
        qkv_grad, out_grad, grad_cross, cross_out_grad = finish_all(
            swap_blocks(rest_rows, rank), kv_weight_grad, rank
        )
        return (
            outer(output).reshape(hidden.shape),
            outer(grad_hidden).reshape(hidden.shape),
            grad_caption,
            sums[:3],
            sums[3],
            qkv_grad,
            out_grad,
            grad_cross,
            cross_out_grad,
            grad_text_w,
            up_grad,
            down_grad,
        )

    return local


def solution(mesh):
    z_size = mesh.shape["img"] // 4
    inner = Mesh(mesh.devices.reshape(z_size, 2, 2, 2), ("z", "x", "c", "y"))
    image = ("z", "x", "c")
    tokens = P(image, "y", None)
    rows = P(image + ("y",))
    in_specs = (tokens, P(image, None), P(image), P(), P(), P()) + (rows,) * 7 + (tokens,)
    out_specs = (tokens, tokens, P(), P(), P()) + (rows,) * 7
    return jax.shard_map(
        make_local(z_size), mesh=inner, in_specs=in_specs, out_specs=out_specs, check_vma=False
    )
```

```python
import math

import jax
import jax.numpy as jnp
from jax import lax
from jax.experimental import pallas as pl
from jax.experimental.pallas import tpu as pltpu
from jax.sharding import Mesh
from jax.sharding import PartitionSpec as P

HD = 128
EPS = 1e-05
BF = jnp.bfloat16
F32 = jnp.float32
PAIR = ((0, 1), (1, 0))
GROUP = ("x", "y")
DATA = ("z", "c")
PLANE = ("x", "c", "y")
VMEM = 48 * 1024 * 1024
SCALE = 1.0 / math.sqrt(HD)
SLOPE = math.sqrt(2.0 / math.pi)
CUBIC = 0.044715


def dot(a, b, dims):
    return lax.dot_general(a, b, (dims, ((), ())), preferred_element_type=F32)


def mm(a, b):
    return dot(a, b, ((1,), (0,)))


def mm_t(a, b):
    return dot(a, b, ((1,), (1,)))


def t_mm(a, b):
    return dot(a, b, ((0,), (0,)))


def shape(dims, dtype=BF):
    return jax.ShapeDtypeStruct(dims, dtype)


def swap(values, axis):
    return lax.ppermute(values, axis, PAIR)


def trade(blocks, axes=GROUP):
    return lax.all_to_all(blocks, axes, 0, 0, tiled=True)


def spread(values, axes=GROUP, count=4):
    return trade(jnp.broadcast_to(values[None], (count,) + values.shape), axes)


def gather_tokens(own):
    half = own.shape[0] // 2
    from_x = swap(own, "x")
    from_y = swap(own, "y")
    return own, from_y, from_x, swap(from_x[:half], "y"), swap(from_y[half:], "x")


def scatter_tokens(parts):
    own, for_y, for_x, for_low, for_high = parts
    half = for_low.shape[0]
    low = swap(for_low, "y").astype(F32) + for_x[:half].astype(F32)
    high = swap(for_high, "x").astype(F32) + for_y[half:].astype(F32)
    from_x = swap(jnp.concatenate([low.astype(BF), for_x[half:]], axis=0), "x")
    from_y = swap(jnp.concatenate([for_y[:half], high.astype(BF)], axis=0), "y")
    return [own, from_x, from_y]


def swap_blocks(blocks, rank):
    parts = [lax.dynamic_index_in_dim(blocks, rank ^ k, 0, keepdims=False) for k in range(4)]
    return [
        parts[0],
        swap(parts[1], "y"),
        swap(parts[2], "x"),
        lax.ppermute(parts[3], GROUP, ((0, 3), (1, 2), (2, 1), (3, 0))),
    ]


def gather_rows(rows):
    return lax.all_gather(rows.reshape(-1, rows.shape[-1]), DATA, axis=0, tiled=True)


def scatter_grad(partial, axes):
    summed = lax.psum_scatter(partial, axes, scatter_dimension=0, tiled=True)
    return summed.reshape(4, -1, summed.shape[-1])


def call(kernel, grid, in_specs, out_specs, out_shape, operands, name, flops=0, size=1 << 22,
         rank=None, scratch=()):
    options = dict(
        out_shape=out_shape,
        compiler_params=pltpu.CompilerParams(vmem_limit_bytes=VMEM),
        cost_estimate=pl.CostEstimate(flops=flops, bytes_accessed=size, transcendentals=0),
        name=name,
    )
    if rank is None:
        return pl.pallas_call(
            kernel, grid=grid, in_specs=in_specs, out_specs=out_specs, scratch_shapes=scratch,
            **options,
        )(*operands)
    spec = pltpu.PrefetchScalarGridSpec(
        num_scalar_prefetch=1,
        grid=grid,
        in_specs=in_specs,
        out_specs=out_specs,
        scratch_shapes=scratch,
    )
    return pl.pallas_call(kernel, grid_spec=spec, **options)(rank.reshape(1), *operands)


def whole(array):
    return pl.BlockSpec(array.shape, lambda *_: (0,) * len(array.shape))


def reorder(values, unit, order):
    if order is None:
        return values
    return jnp.concatenate([values[:, k * unit : (k + 1) * unit] for k in order], axis=1)


def assemble(target, pieces, rank):
    rows, half = pieces[0].shape[0], pieces[3].shape[0]
    for k in range(3):
        target[pl.ds(pl.multiple_of((rank ^ k) * rows, rows), rows), :] = pieces[k][...]
    at = pl.multiple_of((rank ^ 3) * rows, rows)
    target[pl.ds(at, half), :] = pieces[3][...]
    target[pl.ds(pl.multiple_of(at + half, half), half), :] = pieces[4][...]


def gather_mm(pieces, rank, weight, first, columns, name):
    rows, width = pieces[0].shape
    step = 256

    def kernel(r, *refs):
        tokens, out = refs[6], refs[7]

        @pl.when(pl.program_id(0) == 0)
        def _():
            assemble(tokens, refs[:5], r[0])

        out[...] = mm(tokens[...], refs[5][...]).astype(BF)

    return call(
        kernel,
        (columns // step,),
        [whole(p) for p in pieces]
        + [pl.BlockSpec((width, step), lambda j, r: (0, first // step + j))],
        [
            pl.BlockSpec((4 * rows, width), lambda j, r: (0, 0)),
            pl.BlockSpec((4 * rows, step), lambda j, r: (0, j)),
        ],
        [shape((4 * rows, width)), shape((4 * rows, columns))],
        [*pieces, weight],
        name,
        flops=8 * rows * width * columns,
        size=2 * width * (columns + 8 * rows),
        rank=rank,
    )


def mm_scatter(values, rank, weight, first, name):
    tokens, depth = values.shape
    rows = tokens // 4
    width = weight.shape[0]
    step = 512

    def kernel(r, x, w, own, for_y, for_x, low, high, total):
        total[...] = mm_t(x[...], w[...])

        def block(k):
            return total[pl.ds(pl.multiple_of((r[0] ^ k) * rows, rows), rows), :]

        own[...] = block(0)
        for_y[...] = block(1).astype(BF)
        for_x[...] = block(2).astype(BF)
        diagonal = block(3).astype(BF)
        low[...] = diagonal[: rows // 2]
        high[...] = diagonal[rows // 2 :]

    sizes = [rows, rows, rows, rows // 2, rows // 2]
    return call(
        kernel,
        (width // step,),
        [
            pl.BlockSpec((tokens, depth), lambda j, r: (0, 0)),
            pl.BlockSpec((step, depth), lambda j, r: (j, first // depth)),
        ],
        [pl.BlockSpec((n, step), lambda j, r: (0, j)) for n in sizes],
        [shape((n, width), F32 if k == 0 else BF) for k, n in enumerate(sizes)],
        [values, weight],
        name,
        flops=2 * tokens * depth * width,
        size=2 * width * (depth + 6 * rows),
        rank=rank,
        scratch=[pltpu.VMEM((tokens, step), F32)],
    )


def normalize(values):
    centred = values - jnp.mean(values, axis=-1, keepdims=True)
    inv_std = lax.rsqrt(jnp.mean(centred * centred, axis=-1, keepdims=True) + EPS)
    return centred * inv_std, inv_std


NORM_ROWS = 32


def row_spec(array, at=None):
    width = array.shape[-1]
    if at is None:
        return pl.BlockSpec((NORM_ROWS, width), lambda i: (i, 0))
    return pl.BlockSpec((1, NORM_ROWS, width), lambda i, at=at: (at, i, 0))


def terms_of(terms):
    arrays, specs = [], []
    for term in terms:
        array, at = term if isinstance(term, tuple) else (term, None)
        arrays.append(array)
        specs.append(row_spec(array, at))
    return arrays, specs


def total_of(refs):
    values = [ref[0] if len(ref.shape) == 3 else ref[...] for ref in refs]
    return sum(value.astype(F32) for value in values)


def add_norm(terms, gain):
    arrays, specs = terms_of(terms)
    tokens, width = arrays[0].shape[-2], arrays[0].shape[-1]
    tokens = min(a.shape[-2] for a in arrays)

    def kernel(*refs):
        gain_ref, x, out = refs[-3:]
        values = total_of(refs[:-3])
        x[...] = values
        out[...] = (normalize(values)[0] * gain_ref[...]).astype(BF)

    return call(
        kernel,
        (tokens // NORM_ROWS,),
        specs + [whole(gain)],
        [row_spec(shape((tokens, width)))] * 2,
        [shape((tokens, width), F32), shape((tokens, width))],
        [*arrays, gain],
        "add_norm",
    )


def norm_grad(grad, values, gain):
    normed, inv_std = normalize(values)
    scaled = grad * gain
    first_mean = jnp.mean(scaled, axis=-1, keepdims=True)
    second_mean = jnp.mean(scaled * normed, axis=-1, keepdims=True)
    return (
        inv_std * (scaled - first_mean - normed * second_mean),
        jnp.sum(grad * normed, axis=0, keepdims=True),
    )


def accumulate(ref, value):
    @pl.when(pl.program_id(0) == 0)
    def _():
        ref[...] = jnp.zeros_like(ref)

    ref[...] += value


def norm_back(terms, upper, values, gain):
    arrays, specs = terms_of(terms)
    tokens, width = values.shape

    def kernel(*refs):
        upper_ref, x, gain_ref, out, out_low, gain_grad = refs[-6:]
        back, part = norm_grad(total_of(refs[:-6]), x[...], gain_ref[...])
        result = upper_ref[...].astype(F32) + back
        out[...] = result
        out_low[...] = result.astype(BF)
        accumulate(gain_grad, part)

    return call(
        kernel,
        (tokens // NORM_ROWS,),
        specs + [row_spec(upper), row_spec(values), whole(gain)],
        [row_spec(values)] * 2 + [pl.BlockSpec((1, width), lambda i: (0, 0))],
        [shape((tokens, width), F32), shape((tokens, width)), shape((1, width), F32)],
        [*arrays, upper, values, gain],
        "norm_back",
    )


def last_back(terms, upper, values, gain, masked, unit, order):
    arrays, specs = terms_of(terms)
    tokens, width = values.shape

    def kernel(*refs):
        upper_ref, x, gain_ref, mask, out, gain_grad, mask_grad = refs[-7:]
        back, part = norm_grad(total_of(refs[:-7]), x[...], gain_ref[...])
        result = upper_ref[...].astype(F32) + back
        hit = mask[...] > 0.5
        out[...] = reorder(jnp.where(hit, 0.0, result).astype(BF), unit, order)
        accumulate(gain_grad, part)
        accumulate(mask_grad, jnp.sum(jnp.where(hit, result, 0.0), axis=0, keepdims=True))

    line = pl.BlockSpec((1, width), lambda i: (0, 0))
    return call(
        kernel,
        (tokens // NORM_ROWS,),
        specs + [row_spec(upper), row_spec(values), whole(gain), row_spec(masked)],
        [row_spec(values), line, line],
        [shape((tokens, width)), shape((1, width), F32), shape((1, width), F32)],
        [*arrays, upper, values, gain, masked],
        "last_back",
    )


def start(hidden, cotangent, masked, embed, gain, unit, order):
    tokens, width = hidden.shape

    def kernel(hid, cot, mask, embed_ref, gain_ref, x, out, grad):
        hit = mask[...] > 0.5
        values = jnp.where(
            hit, embed_ref[...], reorder(hid[...], unit, order).astype(F32)
        )
        x[...] = values
        out[...] = (normalize(values)[0] * gain_ref[...]).astype(BF)
        grad[...] = jnp.where(hit, reorder(cot[...], unit, order).astype(F32), 0.0).astype(BF)

    rows = row_spec(hidden)
    return call(
        kernel,
        (tokens // NORM_ROWS,),
        [rows, rows, row_spec(masked), whole(embed), whole(gain)],
        [rows] * 3,
        [shape((tokens, width), F32), shape((tokens, width)), shape((tokens, width))],
        [hidden, cotangent, masked, embed, gain],
        "start",
    )


def layer_output(upper, terms, unit, order):
    arrays, specs = terms_of(terms)
    tokens, width = upper.shape

    def kernel(*refs):
        values = refs[-2][...] + total_of(refs[:-2])
        refs[-1][...] = reorder(values.astype(BF), unit, order)

    return call(
        kernel,
        (tokens // NORM_ROWS,),
        specs + [row_spec(upper)],
        row_spec(upper),
        shape((tokens, width)),
        [*arrays, upper],
        "layer_output",
    )


def feed_up(pieces, rank, weight):
    rows, width = pieces[0].shape
    hidden = weight.shape[1]
    step = 256

    def kernel(r, *refs):
        up, tokens, act, slope = refs[5:]

        @pl.when(pl.program_id(0) == 0)
        def _():
            assemble(tokens, refs[:5], r[0])

        u = mm(tokens[...], up[...])
        square = u * u
        bend = jnp.tanh(SLOPE * u * (1.0 + CUBIC * square))
        half = 0.5 * (1.0 + bend)
        act[...] = (u * half).astype(BF)
        slope[...] = half + 0.5 * u * (1.0 - bend * bend) * SLOPE * (1.0 + 3.0 * CUBIC * square)

    part = pl.BlockSpec((4 * rows, step), lambda j, r: (0, j))
    return call(
        kernel,
        (hidden // step,),
        [whole(p) for p in pieces] + [pl.BlockSpec((width, step), lambda j, r: (0, j))],
        [pl.BlockSpec((4 * rows, width), lambda j, r: (0, 0)), part, part],
        [shape((4 * rows, width)), shape((4 * rows, hidden)), shape((4 * rows, hidden), F32)],
        [*pieces, weight],
        "feed_up",
        flops=8 * rows * width * hidden,
        size=2 * width * (hidden + 8 * rows),
        rank=rank,
    )


def feed_down(grad_y, slope, weight):
    tokens, width = grad_y.shape
    hidden = weight.shape[1]
    step = 256

    def kernel(dy, slope_ref, down, out):
        out[...] = (mm(dy[...], down[...]) * slope_ref[...]).astype(BF)

    part = pl.BlockSpec((tokens, step), lambda j: (0, j))
    return call(
        kernel,
        (hidden // step,),
        [whole(grad_y), part, pl.BlockSpec((width, step), lambda j: (0, j))],
        part,
        shape((tokens, hidden)),
        [grad_y, slope, weight],
        "feed_down",
        flops=2 * tokens * width * hidden,
        size=2 * width * (hidden + 8 * tokens),
    )


def softmax(scores):
    exp_terms = jnp.exp(scores - jnp.max(scores, axis=-1, keepdims=True))
    return exp_terms / jnp.sum(exp_terms, axis=-1, keepdims=True)


def score_grad(probs, grad_probs):
    return (
        probs * (grad_probs - jnp.sum(probs * grad_probs, axis=-1, keepdims=True))
    ).astype(BF)


def head(ref, k):
    return ref[:, k * HD : (k + 1) * HD]


def self_forward(projected, images):
    tokens, width = projected.shape
    rows, group = tokens // images, width // 3
    heads = group // HD

    def kernel(proj, mixed):
        for k in range(heads):
            query, key, value = (head(proj, j * heads + k) for j in range(3))
            probs = softmax(mm_t(query, key) * SCALE).astype(BF)
            mixed[:, k * HD : (k + 1) * HD] = mm(probs, value).astype(BF)

    return call(
        kernel,
        (images,),
        [pl.BlockSpec((rows, width), lambda i: (i, 0))],
        pl.BlockSpec((rows, group), lambda i: (i, 0)),
        shape((tokens, group)),
        [projected],
        "self_forward",
        flops=4 * tokens * rows * group,
    )


def self_back(projected, grad_mixed, images):
    tokens, width = projected.shape
    rows, group = tokens // images, width // 3
    heads = group // HD

    def kernel(proj, grad, out):
        for k in range(heads):
            query, key, value = (head(proj, j * heads + k) for j in range(3))
            grad_head = head(grad, k)
            probs = softmax(mm_t(query, key) * SCALE)
            grad_scores = score_grad(probs, mm_t(grad_head, value))
            parts = (
                mm(grad_scores, key) * SCALE,
                t_mm(grad_scores, query) * SCALE,
                t_mm(probs.astype(BF), grad_head),
            )
            for j, part in enumerate(parts):
                at = (j * heads + k) * HD
                out[:, at : at + HD] = part.astype(BF)

    return call(
        kernel,
        (images,),
        [
            pl.BlockSpec((rows, width), lambda i: (i, 0)),
            pl.BlockSpec((rows, group), lambda i: (i, 0)),
        ],
        pl.BlockSpec((rows, width), lambda i: (i, 0)),
        shape((tokens, width)),
        [projected, grad_mixed],
        "self_back",
        flops=10 * tokens * rows * group,
    )


def cross_forward(queries, text_kv):
    tokens, group = queries.shape
    heads = group // HD

    def kernel(query, text, mixed):
        for k in range(heads):
            probs = softmax(mm_t(head(query, k), head(text, k)) * SCALE).astype(BF)
            mixed[:, k * HD : (k + 1) * HD] = mm(probs, head(text, heads + k)).astype(BF)

    return call(
        kernel,
        (1,),
        [whole(queries), whole(text_kv)],
        whole(queries),
        shape((tokens, group)),
        [queries, text_kv],
        "cross_forward",
        flops=4 * tokens * text_kv.shape[0] * group,
    )


def cross_back(queries, text_kv, grad_mixed):
    tokens, group = queries.shape
    context = text_kv.shape[0]
    heads = group // HD

    def kernel(query, text, grad, grad_query, grad_text):
        for k in range(heads):
            query_head, key, value = head(query, k), head(text, k), head(text, heads + k)
            grad_head = head(grad, k)
            probs = softmax(mm_t(query_head, key) * SCALE)
            grad_scores = score_grad(probs, mm_t(grad_head, value))
            grad_query[:, k * HD : (k + 1) * HD] = (mm(grad_scores, key) * SCALE).astype(BF)
            at = (heads + k) * HD
            grad_text[:, k * HD : (k + 1) * HD] = t_mm(grad_scores, query_head) * SCALE
            grad_text[:, at : at + HD] = t_mm(probs.astype(BF), grad_head)

    return call(
        kernel,
        (1,),
        [whole(queries), whole(text_kv), whole(grad_mixed)],
        [whole(queries), whole(text_kv)],
        [shape((tokens, group)), shape((context, 2 * group), F32)],
        [queries, text_kv, grad_mixed],
        "cross_back",
        flops=10 * tokens * context * group,
    )


def grad_products(pairs, name, core=None, blocks=0):
    count_in = len(pairs[0][0])
    tokens, width = pairs[0][0][0].shape
    widths = [y[0].shape[1] for _, y in pairs]
    total = sum(widths)
    rows = 256 if core is None else width // (2 * blocks)
    steps = width // rows if core is None else blocks
    step = 512
    count = len(pairs) * count_in

    def kernel(r, *refs):
        out = refs[2 * count]
        offset = 0
        for k, wide in enumerate(widths):
            left = [refs[k * count_in + b][...].T for b in range(count_in)]
            for at in range(0, wide, step):
                out[:, offset + at : offset + at + step] = sum(
                    mm(left[b], refs[count + k * count_in + b][:, at : at + step])
                    for b in range(count_in)
                ).astype(BF)
            offset += wide

    pick = (lambda i, r: (0, i)) if core is None else (lambda i, r: (0, 2 * i + r[0]))
    return call(
        kernel,
        (steps,),
        [pl.BlockSpec((tokens, rows), pick)] * count
        + [pl.BlockSpec((tokens, w), lambda i, r: (0, 0)) for w in widths for _ in range(count_in)],
        pl.BlockSpec((rows, total), lambda i, r: (i, 0)),
        shape((steps * rows, total)),
        [b for x, _ in pairs for b in x] + [b for _, y in pairs for b in y],
        name,
        flops=2 * tokens * count_in * steps * rows * total,
        size=4 * width * total,
        rank=jnp.zeros((), jnp.int32) if core is None else core,
    )


def place(parts, rank):
    def kernel(r, *refs):
        for k in range(4):

            @pl.when(pl.program_id(0) == k)
            def _():
                refs[4][0] = refs[k][...]

    rows, columns = parts[0].shape
    return call(
        kernel,
        (4,),
        [whole(p) for p in parts],
        pl.BlockSpec((1, rows, columns), lambda k, r: (k ^ r[0], 0, 0)),
        shape((4, rows, columns)),
        parts,
        "place",
        rank=rank,
    )


def finish_wide(parts, rank):
    rows, total = parts[0].shape
    width = total // 2

    def kernel(r, *refs):
        for k in range(4):

            @pl.when(pl.program_id(0) == k)
            def _():
                refs[4][...] = refs[k][:, :width].astype(F32)
                refs[5][...] = refs[k][:, width:].astype(F32)

    flat = pl.BlockSpec((rows, width), lambda k, r: (0, k ^ r[0]))
    return call(
        kernel,
        (4,),
        [whole(p) for p in parts],
        [flat, flat],
        [shape((rows, 4 * width), F32)] * 2,
        parts,
        "finish_wide",
        rank=rank,
    )


def finish_all(parts, text_grad, rank):
    rows, total = parts[0].shape
    width = total // 6

    def kernel(r, *refs):
        key, value, three, out, cross, cross_out = refs[4:]
        for k in range(4):

            @pl.when(pl.program_id(0) == k)
            def _():
                def part(j):
                    return refs[k][:, j * width : (j + 1) * width].astype(F32)

                for j in range(3):
                    three[:, j, :] = part(j)
                out[...] = part(3)
                cross[:, 0, :] = part(4)
                cross_out[...] = part(5)

        cross[:, 1, :] = key[...]
        cross[:, 2, :] = value[...]

    wide = pl.BlockSpec((rows, 3, width), lambda k, r: (0, 0, k ^ r[0]))
    flat = pl.BlockSpec((rows, width), lambda k, r: (0, k ^ r[0]))
    return call(
        kernel,
        (4,),
        [whole(p) for p in parts]
        + [flat, pl.BlockSpec((rows, width), lambda k, r: (0, 4 + (k ^ r[0])))],
        [wide, flat, wide, flat],
        [shape((rows, 3, 4 * width), F32), shape((rows, 4 * width), F32)] * 2,
        [*parts, text_grad, text_grad],
        "finish_all",
        rank=rank,
    )


def column_blocks(weight, count):
    rows = weight.shape[0]
    return weight.reshape(rows, count, -1).transpose(1, 0, 2)


def make_local(z_size):
    def sum_z(values):
        return spread(values, "z", z_size).astype(F32).sum(axis=0)

    def by_plane(values, parts):
        rows = values.shape[0]
        shaped = values.reshape(2, rows // 2, parts, 2, 2, -1)
        return shaped.transpose(3, 0, 4, 1, 2, 5).reshape(8, rows // 2, -1)

    def from_plane(blocks, parts):
        rows = blocks.shape[1]
        shaped = blocks.reshape(2, 2, 2, rows, parts, -1)
        return shaped.transpose(1, 3, 4, 0, 2, 5).reshape(2 * rows, -1)

    def sum_all(values):
        return sum_z(spread(values, PLANE, 8).sum(axis=0))

    def layer_order(values):
        shaped = values.reshape(values.shape[:-1] + (z_size, 2, 2, -1))
        return jnp.swapaxes(shaped, -3, -2).reshape(values.shape)

    def local(
        hidden,
        mask_index,
        mask_count,
        mask_embed,
        norm_gains,
        caption,
        w_qkv,
        w_out,
        w_cross,
        w_cross_out,
        w_text,
        w_up,
        w_down,
        cotangent,
    ):
        images, local_rows, width = hidden.shape
        full_length = mask_index.shape[1]
        shard_rows = w_qkv.shape[0]
        rank = lax.axis_index("x") * 2 + lax.axis_index("y")
        core = lax.axis_index("c")
        tokens = images * local_rows
        group = width // 4
        text_width = caption.shape[1]

        unit = width // (4 * z_size)
        inside = unit % 128 == 0
        order = [4 * k + j for k in range(z_size) for j in (0, 2, 1, 3)] if inside else None

        def outer(values):
            return values if inside else layer_order(values)

        first = jnp.concatenate(
            [
                w_qkv.reshape(shard_rows, 3, 4, group)
                .transpose(2, 0, 1, 3)
                .reshape(4, shard_rows, 3 * group),
                column_blocks(w_out, 4),
            ],
            axis=2,
        )
        first = gather_rows(place(swap_blocks(first, rank), rank))
        positions = lax.axis_index("y") * local_rows + jnp.arange(local_rows, dtype=jnp.int32)
        ranks = jnp.arange(full_length, dtype=jnp.int32)
        matches = (mask_index[:, :, None] == positions[None, None, :]) & (
            ranks[None, :, None] < mask_count[:, None, None]
        )
        masked = jnp.any(matches, axis=1).reshape(tokens, 1).astype(F32)
        gains = layer_order(norm_gains)
        gain_a, gain_b, gain_c = gains[:1], gains[1:2], gains[2:]
        start_x, attn_in, grad_top = start(
            outer(hidden.reshape(tokens, width)),
            outer(cotangent.reshape(tokens, width)),
            masked,
            layer_order(mask_embed)[None],
            gain_a,
            unit,
            order,
        )
        attn_in = gather_tokens(attn_in)
        mid = jnp.concatenate([column_blocks(w_cross[:, 0], 4), column_blocks(w_cross_out, 4)], axis=2)
        up = column_blocks(w_up, 4)
        attn_in, mid, up = lax.optimization_barrier((attn_in, mid, up))
        mid, up = gather_rows(trade(mid)), gather_rows(trade(up))

        own_text = mm_t(caption, w_text).astype(BF)
        kv_rows = w_cross[:, 1:].reshape(shard_rows, 2 * width)
        kv_part = by_plane(mm(own_text, kv_rows).astype(BF), 2)
        text_kv = trade(kv_part, PLANE).astype(F32).sum(axis=0).astype(BF)
        text_kv = sum_z(text_kv).astype(BF)
        other = swap(text_kv, "c")
        text_kv = jnp.concatenate(
            [jnp.where(core == 0, text_kv, other), jnp.where(core == 0, other, text_kv)], axis=0
        )
        attn_in, text_kv = lax.optimization_barrier((attn_in, text_kv))

        attn_in, projected = gather_mm(attn_in, rank, first, 0, 3 * group, "qkv_mm")
        down = column_blocks(w_down, 4)
        projected, down, grad_top = lax.optimization_barrier((projected, down, grad_top))
        down = gather_rows(trade(down))
        grad_y = spread(grad_top).reshape(4 * tokens, width)
        self_mixed = self_forward(projected, 2 * images)
        parts = scatter_tokens(mm_scatter(self_mixed, rank, first, 3 * group, "out_mm"))
        after_attn, cross_in = add_norm([start_x] + parts, gain_b)

        cross_in, cross_queries = gather_mm(gather_tokens(cross_in), rank, mid, 0, group, "query_mm")
        cross_mixed = cross_forward(cross_queries, text_kv)
        parts = scatter_tokens(mm_scatter(cross_mixed, rank, mid, group, "cross_out_mm"))
        after_cross, mlp_in = add_norm([after_attn] + parts, gain_c)

        mlp_in, activated, slope = feed_up(gather_tokens(mlp_in), rank, up)
        early = [attn_in, self_mixed, cross_in, cross_mixed]
        if inside:
            grad_axes, halves = "z", (core, z_size)

            def both(values):
                return [values, swap(values, "c")]

        else:
            grad_axes, halves = DATA, ()

            def both(values):
                return [values]

        early = [both(values) for values in early]
        down_part = grad_products([(both(grad_y), both(activated))], "down_grads", *halves)
        mlp_in = both(mlp_in)
        slope, down_part, early, mlp_in = lax.optimization_barrier((slope, down_part, early, mlp_in))
        down_rows = scatter_grad(down_part, grad_axes)
        grad_pre = feed_down(grad_y, slope, down)
        parts = mm_scatter(grad_pre, rank, up, 0, "up_back")
        parts, grad_pre = lax.optimization_barrier((parts, grad_pre))
        up_part = grad_products([(mlp_in, both(grad_pre))], "up_grads", *halves)
        grad_after_cross, cross_branch, gain_grad_c = norm_back(
            scatter_tokens(parts), grad_top, after_cross, gain_c
        )

        cross_branch, grad_cross_mixed = gather_mm(
            gather_tokens(cross_branch), rank, mid, group, group, "cross_out_back"
        )
        grad_cq, kv_grad = cross_back(cross_queries, text_kv, grad_cross_mixed)
        up_part, down_rows, kv_grad = lax.optimization_barrier((up_part, down_rows, kv_grad))
        up_rows = scatter_grad(up_part, grad_axes)
        cross_branch, grad_cq_both = both(cross_branch), both(grad_cq)
        parts = scatter_tokens(mm_scatter(grad_cq, rank, mid, 0, "query_back"))
        grad_after_attn, attn_branch, gain_grad_b = norm_back(
            parts, grad_after_cross, after_attn, gain_b
        )

        attn_branch, grad_self_mixed = gather_mm(
            gather_tokens(attn_branch), rank, first, 3 * group, group, "out_back"
        )
        grad_projected = self_back(projected, grad_self_mixed, 2 * images)
        rest_part = grad_products(
            [
                (early[0], both(grad_projected)),
                (both(attn_branch), early[1]),
                (early[2], grad_cq_both),
                (cross_branch, early[3]),
            ],
            "attention_grads",
            *halves,
        )
        grad_projected, activated, kv_grad, rest_part = lax.optimization_barrier(
            (grad_projected, activated, kv_grad, rest_part)
        )
        rest_part, up_rows = lax.optimization_barrier((rest_part, up_rows))
        rest_rows = scatter_grad(rest_part, grad_axes)
        parts = scatter_tokens(mm_scatter(grad_projected, rank, first, 0, "qkv_back"))
        grad_hidden, gain_grad_a, mask_grad = last_back(
            parts,
            grad_after_attn,
            start_x,
            gain_a,
            masked,
            unit,
            order,
        )
        sums = jnp.concatenate([gain_grad_a, gain_grad_b, gain_grad_c, mask_grad], axis=0)
        sums = layer_order(sum_all(sums))

        parts = scatter_tokens(mm_scatter(activated, rank, down, 0, "down_mm"))
        output = layer_output(after_cross, parts, unit, order)

        kv_halves = kv_grad.reshape(2, -1, 2 * group)
        kv_keep = lax.dynamic_index_in_dim(kv_halves, core, 0, keepdims=False)
        kv_send = lax.dynamic_index_in_dim(kv_halves, 1 - core, 0, keepdims=False)
        kv_sum = sum_z((kv_keep + swap(kv_send, "c")).astype(BF)).astype(BF)
        kv_grads = from_plane(spread(kv_sum, PLANE, 8), 2)
        kv_weight_grad = t_mm(own_text, kv_grads)
        grad_text = mm_t(kv_grads, kv_rows).astype(BF)
        grad_text_w = t_mm(grad_text, caption)
        caption_part = by_plane(mm(grad_text, w_text).astype(BF), 1)
        caption_own = trade(caption_part, PLANE).astype(F32).sum(axis=0).astype(BF)
        caption_own = sum_z(caption_own).astype(BF)
        grad_caption = from_plane(spread(caption_own, PLANE, 8), 1).astype(F32)

        wide_rows = jnp.concatenate([down_rows, up_rows], axis=2)
        down_grad, up_grad = finish_wide(swap_blocks(wide_rows, rank), rank)
        qkv_grad, out_grad, grad_cross, cross_out_grad = finish_all(
            swap_blocks(rest_rows, rank), kv_weight_grad, rank
        )
        return (
            outer(output).reshape(hidden.shape),
            outer(grad_hidden).reshape(hidden.shape),
            grad_caption,
            sums[:3],
            sums[3],
            qkv_grad,
            out_grad,
            grad_cross,
            cross_out_grad,
            grad_text_w,
            up_grad,
            down_grad,
        )

    return local


def solution(mesh):
    z_size = mesh.shape["img"] // 4
    inner = Mesh(mesh.devices.reshape(z_size, 2, 2, 2), ("z", "x", "c", "y"))
    image = ("z", "x", "c")
    tokens = P(image, "y", None)
    rows = P(image + ("y",))
    in_specs = (tokens, P(image, None), P(image), P(), P(), P()) + (rows,) * 7 + (tokens,)
    out_specs = (tokens, tokens, P(), P(), P()) + (rows,) * 7
    return jax.shard_map(
        make_local(z_size), mesh=inner, in_specs=in_specs, out_specs=out_specs, check_vma=False
    )
```

```python
import math

import jax
import jax.numpy as jnp
from jax import lax
from jax.experimental import pallas as pl
from jax.experimental.pallas import tpu as pltpu
from jax.sharding import Mesh
from jax.sharding import PartitionSpec as P

HD = 128
EPS = 1e-05
BF = jnp.bfloat16
F32 = jnp.float32
PAIR = ((0, 1), (1, 0))
GROUP = ("x", "y")
DATA = ("z", "c")
PLANE = ("x", "c", "y")
VMEM = 48 * 1024 * 1024
SCALE = 1.0 / math.sqrt(HD)
SLOPE = math.sqrt(2.0 / math.pi)
CUBIC = 0.044715


def dot(a, b, dims):
    return lax.dot_general(a, b, (dims, ((), ())), preferred_element_type=F32)


def mm(a, b):
    return dot(a, b, ((1,), (0,)))


def mm_t(a, b):
    return dot(a, b, ((1,), (1,)))


def t_mm(a, b):
    return dot(a, b, ((0,), (0,)))


def shape(dims, dtype=BF):
    return jax.ShapeDtypeStruct(dims, dtype)


def swap(values, axis):
    return lax.ppermute(values, axis, PAIR)


def trade(blocks, axes=GROUP):
    return lax.all_to_all(blocks, axes, 0, 0, tiled=True)


def spread(values, axes=GROUP, count=4):
    return trade(jnp.broadcast_to(values[None], (count,) + values.shape), axes)


def gather_tokens(own):
    half = own.shape[0] // 2
    from_x = swap(own, "x")
    from_y = swap(own, "y")
    return own, from_y, from_x, swap(from_x[:half], "y"), swap(from_y[half:], "x")


def scatter_tokens(parts):
    own, for_y, for_x, for_low, for_high = parts
    half = for_low.shape[0]
    low = swap(for_low, "y").astype(F32) + for_x[:half].astype(F32)
    high = swap(for_high, "x").astype(F32) + for_y[half:].astype(F32)
    from_x = swap(jnp.concatenate([low.astype(BF), for_x[half:]], axis=0), "x")
    from_y = swap(jnp.concatenate([for_y[:half], high.astype(BF)], axis=0), "y")
    return [own, from_x, from_y]


def swap_blocks(blocks, rank):
    parts = [lax.dynamic_index_in_dim(blocks, rank ^ k, 0, keepdims=False) for k in range(4)]
    return [
        parts[0],
        swap(parts[1], "y"),
        swap(parts[2], "x"),
        lax.ppermute(parts[3], GROUP, ((0, 3), (1, 2), (2, 1), (3, 0))),
    ]


def gather_rows(rows):
    return lax.all_gather(rows.reshape(-1, rows.shape[-1]), DATA, axis=0, tiled=True)


def scatter_grad(partial, axes):
    summed = lax.psum_scatter(partial, axes, scatter_dimension=0, tiled=True)
    return summed.reshape(4, -1, summed.shape[-1])


def call(kernel, grid, in_specs, out_specs, out_shape, operands, name, flops=0, size=1 << 22,
         rank=None, scratch=()):
    options = dict(
        out_shape=out_shape,
        compiler_params=pltpu.CompilerParams(vmem_limit_bytes=VMEM),
        cost_estimate=pl.CostEstimate(flops=flops, bytes_accessed=size, transcendentals=0),
        name=name,
    )
    if rank is None:
        return pl.pallas_call(
            kernel, grid=grid, in_specs=in_specs, out_specs=out_specs, scratch_shapes=scratch,
            **options,
        )(*operands)
    spec = pltpu.PrefetchScalarGridSpec(
        num_scalar_prefetch=1,
        grid=grid,
        in_specs=in_specs,
        out_specs=out_specs,
        scratch_shapes=scratch,
    )
    return pl.pallas_call(kernel, grid_spec=spec, **options)(rank.reshape(1), *operands)


def whole(array):
    return pl.BlockSpec(array.shape, lambda *_: (0,) * len(array.shape))


def reorder(values, unit, order):
    if order is None:
        return values
    return jnp.concatenate([values[:, k * unit : (k + 1) * unit] for k in order], axis=1)


def assemble(target, pieces):
    at = 0
    for piece in pieces:
        rows = piece.shape[0]
        target[at : at + rows, :] = piece[...]
        at += rows


def gather_mm(pieces, weight, first, columns, name):
    rows, width = pieces[0].shape
    step = 256

    def kernel(*refs):
        tokens, out = refs[6], refs[7]

        @pl.when(pl.program_id(0) == 0)
        def _():
            assemble(tokens, refs[:5])

        out[...] = mm(tokens[...], refs[5][...]).astype(BF)

    return call(
        kernel,
        (columns // step,),
        [whole(p) for p in pieces] + [pl.BlockSpec((width, step), lambda j: (0, first // step + j))],
        [
            pl.BlockSpec((4 * rows, width), lambda j: (0, 0)),
            pl.BlockSpec((4 * rows, step), lambda j: (0, j)),
        ],
        [shape((4 * rows, width)), shape((4 * rows, columns))],
        [*pieces, weight],
        name,
        flops=8 * rows * width * columns,
        size=2 * width * (columns + 8 * rows),
    )


def mm_scatter(values, weight):
    partial = mm_t(values, weight)
    rows = partial.shape[0] // 4
    low = partial[rows:].astype(BF)
    half = rows // 2
    cuts = [low[:rows], low[rows : 2 * rows], low[2 * rows : 2 * rows + half], low[2 * rows + half :]]
    return scatter_tokens([partial[:rows], *cuts])


def normalize(values):
    centred = values - jnp.mean(values, axis=-1, keepdims=True)
    inv_std = lax.rsqrt(jnp.mean(centred * centred, axis=-1, keepdims=True) + EPS)
    return centred * inv_std, inv_std


NORM_ROWS = 32


def row_spec(array, at=None):
    width = array.shape[-1]
    if at is None:
        return pl.BlockSpec((NORM_ROWS, width), lambda i: (i, 0))
    return pl.BlockSpec((1, NORM_ROWS, width), lambda i, at=at: (at, i, 0))


def terms_of(terms):
    arrays, specs = [], []
    for term in terms:
        array, at = term if isinstance(term, tuple) else (term, None)
        arrays.append(array)
        specs.append(row_spec(array, at))
    return arrays, specs


def total_of(refs):
    values = [ref[0] if len(ref.shape) == 3 else ref[...] for ref in refs]
    return sum(value.astype(F32) for value in values)


def add_norm(terms, gain):
    arrays, specs = terms_of(terms)
    tokens, width = arrays[0].shape[-2], arrays[0].shape[-1]
    tokens = min(a.shape[-2] for a in arrays)

    def kernel(*refs):
        gain_ref, x, out = refs[-3:]
        values = total_of(refs[:-3])
        x[...] = values
        out[...] = (normalize(values)[0] * gain_ref[...]).astype(BF)

    return call(
        kernel,
        (tokens // NORM_ROWS,),
        specs + [whole(gain)],
        [row_spec(shape((tokens, width)))] * 2,
        [shape((tokens, width), F32), shape((tokens, width))],
        [*arrays, gain],
        "add_norm",
    )


def norm_grad(grad, values, gain):
    normed, inv_std = normalize(values)
    scaled = grad * gain
    first_mean = jnp.mean(scaled, axis=-1, keepdims=True)
    second_mean = jnp.mean(scaled * normed, axis=-1, keepdims=True)
    return (
        inv_std * (scaled - first_mean - normed * second_mean),
        jnp.sum(grad * normed, axis=0, keepdims=True),
    )


def accumulate(ref, value):
    @pl.when(pl.program_id(0) == 0)
    def _():
        ref[...] = jnp.zeros_like(ref)

    ref[...] += value


def norm_back(terms, upper, values, gain):
    arrays, specs = terms_of(terms)
    tokens, width = values.shape

    def kernel(*refs):
        upper_ref, x, gain_ref, out, out_low, gain_grad = refs[-6:]
        back, part = norm_grad(total_of(refs[:-6]), x[...], gain_ref[...])
        result = upper_ref[...].astype(F32) + back
        out[...] = result
        out_low[...] = result.astype(BF)
        accumulate(gain_grad, part)

    return call(
        kernel,
        (tokens // NORM_ROWS,),
        specs + [row_spec(upper), row_spec(values), whole(gain)],
        [row_spec(values)] * 2 + [pl.BlockSpec((1, width), lambda i: (0, 0))],
        [shape((tokens, width), F32), shape((tokens, width)), shape((1, width), F32)],
        [*arrays, upper, values, gain],
        "norm_back",
    )


def last_back(terms, upper, values, gain, masked, unit, order):
    arrays, specs = terms_of(terms)
    tokens, width = values.shape

    def kernel(*refs):
        upper_ref, x, gain_ref, mask, out, gain_grad, mask_grad = refs[-7:]
        back, part = norm_grad(total_of(refs[:-7]), x[...], gain_ref[...])
        result = upper_ref[...].astype(F32) + back
        hit = mask[...] > 0.5
        out[...] = reorder(jnp.where(hit, 0.0, result).astype(BF), unit, order)
        accumulate(gain_grad, part)
        accumulate(mask_grad, jnp.sum(jnp.where(hit, result, 0.0), axis=0, keepdims=True))

    line = pl.BlockSpec((1, width), lambda i: (0, 0))
    return call(
        kernel,
        (tokens // NORM_ROWS,),
        specs + [row_spec(upper), row_spec(values), whole(gain), row_spec(masked)],
        [row_spec(values), line, line],
        [shape((tokens, width)), shape((1, width), F32), shape((1, width), F32)],
        [*arrays, upper, values, gain, masked],
        "last_back",
    )


def start(hidden, cotangent, masked, embed, gain, unit, order):
    tokens, width = hidden.shape

    def kernel(hid, cot, mask, embed_ref, gain_ref, x, out, grad):
        hit = mask[...] > 0.5
        values = jnp.where(
            hit, embed_ref[...], reorder(hid[...], unit, order).astype(F32)
        )
        x[...] = values
        out[...] = (normalize(values)[0] * gain_ref[...]).astype(BF)
        grad[...] = jnp.where(hit, reorder(cot[...], unit, order).astype(F32), 0.0).astype(BF)

    rows = row_spec(hidden)
    return call(
        kernel,
        (tokens // NORM_ROWS,),
        [rows, rows, row_spec(masked), whole(embed), whole(gain)],
        [rows] * 3,
        [shape((tokens, width), F32), shape((tokens, width)), shape((tokens, width))],
        [hidden, cotangent, masked, embed, gain],
        "start",
    )


def layer_output(upper, terms, unit, order):
    arrays, specs = terms_of(terms)
    tokens, width = upper.shape

    def kernel(*refs):
        values = refs[-2][...] + total_of(refs[:-2])
        refs[-1][...] = reorder(values.astype(BF), unit, order)

    return call(
        kernel,
        (tokens // NORM_ROWS,),
        specs + [row_spec(upper)],
        row_spec(upper),
        shape((tokens, width)),
        [*arrays, upper],
        "layer_output",
    )


def feed_up(pieces, weight):
    rows, width = pieces[0].shape
    hidden = weight.shape[1]
    step = 256

    def kernel(*refs):
        up, tokens, act, slope = refs[5:]

        @pl.when(pl.program_id(0) == 0)
        def _():
            assemble(tokens, refs[:5])

        u = mm(tokens[...], up[...])
        square = u * u
        bend = jnp.tanh(SLOPE * u * (1.0 + CUBIC * square))
        half = 0.5 * (1.0 + bend)
        act[...] = (u * half).astype(BF)
        slope[...] = half + 0.5 * u * (1.0 - bend * bend) * SLOPE * (1.0 + 3.0 * CUBIC * square)

    part = pl.BlockSpec((4 * rows, step), lambda j: (0, j))
    return call(
        kernel,
        (hidden // step,),
        [whole(p) for p in pieces] + [pl.BlockSpec((width, step), lambda j: (0, j))],
        [pl.BlockSpec((4 * rows, width), lambda j: (0, 0)), part, part],
        [shape((4 * rows, width)), shape((4 * rows, hidden)), shape((4 * rows, hidden), F32)],
        [*pieces, weight],
        "feed_up",
        flops=8 * rows * width * hidden,
        size=2 * width * (hidden + 8 * rows),
    )


def feed_down(grad_y, slope, weight):
    tokens, width = grad_y.shape
    hidden = weight.shape[1]
    step = 256

    def kernel(dy, slope_ref, down, out):
        out[...] = (mm(dy[...], down[...]) * slope_ref[...]).astype(BF)

    part = pl.BlockSpec((tokens, step), lambda j: (0, j))
    return call(
        kernel,
        (hidden // step,),
        [whole(grad_y), part, pl.BlockSpec((width, step), lambda j: (0, j))],
        part,
        shape((tokens, hidden)),
        [grad_y, slope, weight],
        "feed_down",
        flops=2 * tokens * width * hidden,
        size=2 * width * (hidden + 8 * tokens),
    )


def softmax(scores):
    exp_terms = jnp.exp(scores - jnp.max(scores, axis=-1, keepdims=True))
    return exp_terms / jnp.sum(exp_terms, axis=-1, keepdims=True)


def score_grad(probs, grad_probs):
    return (
        probs * (grad_probs - jnp.sum(probs * grad_probs, axis=-1, keepdims=True))
    ).astype(BF)


def head(ref, k):
    return ref[:, k * HD : (k + 1) * HD]


def self_forward(projected, images):
    tokens, width = projected.shape
    rows, group = tokens // images, width // 3
    heads = group // HD

    def kernel(proj, mixed):
        for k in range(heads):
            query, key, value = (head(proj, j * heads + k) for j in range(3))
            probs = softmax(mm_t(query, key) * SCALE).astype(BF)
            mixed[:, k * HD : (k + 1) * HD] = mm(probs, value).astype(BF)

    return call(
        kernel,
        (images,),
        [pl.BlockSpec((rows, width), lambda i: (i, 0))],
        pl.BlockSpec((rows, group), lambda i: (i, 0)),
        shape((tokens, group)),
        [projected],
        "self_forward",
        flops=4 * tokens * rows * group,
    )


def self_back(projected, grad_mixed, images):
    tokens, width = projected.shape
    rows, group = tokens // images, width // 3
    heads = group // HD

    def kernel(proj, grad, out):
        for k in range(heads):
            query, key, value = (head(proj, j * heads + k) for j in range(3))
            grad_head = head(grad, k)
            probs = softmax(mm_t(query, key) * SCALE)
            grad_scores = score_grad(probs, mm_t(grad_head, value))
            parts = (
                mm(grad_scores, key) * SCALE,
                t_mm(grad_scores, query) * SCALE,
                t_mm(probs.astype(BF), grad_head),
            )
            for j, part in enumerate(parts):
                at = (j * heads + k) * HD
                out[:, at : at + HD] = part.astype(BF)

    return call(
        kernel,
        (images,),
        [
            pl.BlockSpec((rows, width), lambda i: (i, 0)),
            pl.BlockSpec((rows, group), lambda i: (i, 0)),
        ],
        pl.BlockSpec((rows, width), lambda i: (i, 0)),
        shape((tokens, width)),
        [projected, grad_mixed],
        "self_back",
        flops=10 * tokens * rows * group,
    )


def cross_forward(queries, text_kv):
    tokens, group = queries.shape
    heads = group // HD

    def kernel(query, text, mixed):
        for k in range(heads):
            probs = softmax(mm_t(head(query, k), head(text, k)) * SCALE).astype(BF)
            mixed[:, k * HD : (k + 1) * HD] = mm(probs, head(text, heads + k)).astype(BF)

    return call(
        kernel,
        (1,),
        [whole(queries), whole(text_kv)],
        whole(queries),
        shape((tokens, group)),
        [queries, text_kv],
        "cross_forward",
        flops=4 * tokens * text_kv.shape[0] * group,
    )


def cross_back(queries, text_kv, grad_mixed):
    tokens, group = queries.shape
    context = text_kv.shape[0]
    heads = group // HD

    def kernel(query, text, grad, grad_query, grad_text):
        for k in range(heads):
            query_head, key, value = head(query, k), head(text, k), head(text, heads + k)
            grad_head = head(grad, k)
            probs = softmax(mm_t(query_head, key) * SCALE)
            grad_scores = score_grad(probs, mm_t(grad_head, value))
            grad_query[:, k * HD : (k + 1) * HD] = (mm(grad_scores, key) * SCALE).astype(BF)
            at = (heads + k) * HD
            grad_text[:, k * HD : (k + 1) * HD] = t_mm(grad_scores, query_head) * SCALE
            grad_text[:, at : at + HD] = t_mm(probs.astype(BF), grad_head)

    return call(
        kernel,
        (1,),
        [whole(queries), whole(text_kv), whole(grad_mixed)],
        [whole(queries), whole(text_kv)],
        [shape((tokens, group)), shape((context, 2 * group), F32)],
        [queries, text_kv, grad_mixed],
        "cross_back",
        flops=10 * tokens * context * group,
    )


def grad_products(pairs, name, core=None, blocks=0):
    count_in = len(pairs[0][0])
    tokens, width = pairs[0][0][0].shape
    widths = [y[0].shape[1] for _, y in pairs]
    total = sum(widths)
    rows = 256 if core is None else width // (2 * blocks)
    steps = width // rows if core is None else blocks
    step = 512
    count = len(pairs) * count_in

    def kernel(r, *refs):
        out = refs[2 * count]
        offset = 0
        for k, wide in enumerate(widths):
            left = [refs[k * count_in + b][...].T for b in range(count_in)]
            for at in range(0, wide, step):
                out[:, offset + at : offset + at + step] = sum(
                    mm(left[b], refs[count + k * count_in + b][:, at : at + step])
                    for b in range(count_in)
                ).astype(BF)
            offset += wide

    pick = (lambda i, r: (0, i)) if core is None else (lambda i, r: (0, 2 * i + r[0]))
    return call(
        kernel,
        (steps,),
        [pl.BlockSpec((tokens, rows), pick)] * count
        + [pl.BlockSpec((tokens, w), lambda i, r: (0, 0)) for w in widths for _ in range(count_in)],
        pl.BlockSpec((rows, total), lambda i, r: (i, 0)),
        shape((steps * rows, total)),
        [b for x, _ in pairs for b in x] + [b for _, y in pairs for b in y],
        name,
        flops=2 * tokens * count_in * steps * rows * total,
        size=4 * width * total,
        rank=jnp.zeros((), jnp.int32) if core is None else core,
    )


def place(parts, rank):
    def kernel(r, *refs):
        for k in range(4):

            @pl.when(pl.program_id(0) == k)
            def _():
                refs[4][0] = refs[k][...]

    rows, columns = parts[0].shape
    return call(
        kernel,
        (4,),
        [whole(p) for p in parts],
        pl.BlockSpec((1, rows, columns), lambda k, r: (k ^ r[0], 0, 0)),
        shape((4, rows, columns)),
        parts,
        "place",
        rank=rank,
    )


def finish_wide(parts, rank):
    rows, total = parts[0].shape
    width = total // 2

    def kernel(r, *refs):
        for k in range(4):

            @pl.when(pl.program_id(0) == k)
            def _():
                refs[4][...] = refs[k][:, :width].astype(F32)
                refs[5][...] = refs[k][:, width:].astype(F32)

    flat = pl.BlockSpec((rows, width), lambda k, r: (0, k ^ r[0]))
    return call(
        kernel,
        (4,),
        [whole(p) for p in parts],
        [flat, flat],
        [shape((rows, 4 * width), F32)] * 2,
        parts,
        "finish_wide",
        rank=rank,
    )


def finish_all(parts, text_grad, rank):
    rows, total = parts[0].shape
    width = total // 6

    def kernel(r, *refs):
        key, value, three, out, cross, cross_out = refs[4:]
        for k in range(4):

            @pl.when(pl.program_id(0) == k)
            def _():
                def part(j):
                    return refs[k][:, j * width : (j + 1) * width].astype(F32)

                for j in range(3):
                    three[:, j, :] = part(j)
                out[...] = part(3)
                cross[:, 0, :] = part(4)
                cross_out[...] = part(5)

        cross[:, 1, :] = key[...]
        cross[:, 2, :] = value[...]

    wide = pl.BlockSpec((rows, 3, width), lambda k, r: (0, 0, k ^ r[0]))
    flat = pl.BlockSpec((rows, width), lambda k, r: (0, k ^ r[0]))
    return call(
        kernel,
        (4,),
        [whole(p) for p in parts]
        + [flat, pl.BlockSpec((rows, width), lambda k, r: (0, 4 + (k ^ r[0])))],
        [wide, flat, wide, flat],
        [shape((rows, 3, 4 * width), F32), shape((rows, 4 * width), F32)] * 2,
        [*parts, text_grad, text_grad],
        "finish_all",
        rank=rank,
    )


def plane_block(k):
    return (k >> 1) & 1, (k >> 2) * 2 + (k & 1)


def text_forward(caption, w_text, kv_rows):
    context, rows = caption.shape[0], w_text.shape[0]
    half, width = context // 2, kv_rows.shape[1] // 8

    def kernel(cap, weight, kv, own, blocks):
        own[...] = mm_t(cap[...], weight[...]).astype(BF)
        part = mm(own[...], kv[...]).astype(BF)
        for k in range(8):
            core, group = plane_block(k)
            for j in range(2):
                at = (4 * j + group) * width
                blocks[k, :, j * width : (j + 1) * width] = part[
                    core * half : (core + 1) * half, at : at + width
                ]

    return call(
        kernel,
        (1,),
        [whole(caption), whole(w_text), whole(kv_rows)],
        [
            pl.BlockSpec((context, rows), lambda i: (0, 0)),
            pl.BlockSpec((8, half, 2 * width), lambda i: (0, 0, 0)),
        ],
        [shape((context, rows)), shape((8, half, 2 * width))],
        [caption, w_text, kv_rows],
        "text_forward",
    )


def text_back(blocks, own_text, kv_rows, caption, w_text, extra):
    context, rows = own_text.shape
    half, width = context // 2, kv_rows.shape[1] // 8
    wide = caption.shape[1] // 4
    tail = extra.shape[0]

    def kernel(block, own, kv, cap, weight, more, kv_grad, text_grad, out, grads):
        for k in range(8):
            core, group = plane_block(k)
            for j in range(2):
                at = (4 * j + group) * width
                grads[core * half : (core + 1) * half, at : at + width] = block[
                    k, :, j * width : (j + 1) * width
                ]
        kv_grad[...] = t_mm(own[...], grads[...])
        grad_text = mm_t(grads[...], kv[...]).astype(BF)
        text_grad[...] = t_mm(grad_text, cap[...])
        part = mm(grad_text, weight[...]).astype(BF)
        for k in range(8):
            core, group = plane_block(k)
            out[k, :half, :] = part[core * half : (core + 1) * half, group * wide : (group + 1) * wide]
            out[k, half:, :] = more[...]

    operands = [blocks, own_text, kv_rows, caption, w_text, extra]
    outs = [
        shape((rows, 8 * width), F32),
        shape((rows, 4 * wide), F32),
        shape((8, half + tail, wide)),
    ]
    return call(
        kernel,
        (1,),
        [whole(a) for a in operands],
        [whole(a) for a in outs],
        outs,
        operands,
        "text_back",
        scratch=[pltpu.VMEM((context, 8 * width), BF)],
    )


def caption_output(blocks):
    count, half, wide = blocks.shape

    def kernel(block, out):
        out[...] = block[0].astype(F32)

    return call(
        kernel,
        (count,),
        [pl.BlockSpec((1, half, wide), lambda k: (k, 0, 0))],
        pl.BlockSpec((half, wide), lambda k: plane_block(k)),
        shape((2 * half, 4 * wide), F32),
        [blocks],
        "caption_output",
    )


def column_blocks(weight, count):
    rows = weight.shape[0]
    return weight.reshape(rows, count, -1).transpose(1, 0, 2)


def halves_of(values, width):
    high = values.astype(BF)
    low = (values - high.astype(F32)).astype(BF)
    return jnp.concatenate([high.reshape(-1, width), low.reshape(-1, width)], axis=0)


def whole_of(halves, width):
    rows = halves.shape[0] // 2
    return (halves[:rows] + halves[rows:]).reshape(-1, width)


def make_local(z_size):
    def sum_z(values):
        return spread(values, "z", z_size).astype(F32).sum(axis=0)

    def layer_order(values):
        shaped = values.reshape(values.shape[:-1] + (z_size, 2, 2, -1))
        return jnp.swapaxes(shaped, -3, -2).reshape(values.shape)

    def local(
        hidden,
        mask_index,
        mask_count,
        mask_embed,
        norm_gains,
        caption,
        w_qkv,
        w_out,
        w_cross,
        w_cross_out,
        w_text,
        w_up,
        w_down,
        cotangent,
    ):
        images, local_rows, width = hidden.shape
        full_length = mask_index.shape[1]
        shard_rows = w_qkv.shape[0]
        rank = lax.axis_index("x") * 2 + lax.axis_index("y")
        core = lax.axis_index("c")
        tokens = images * local_rows
        group = width // 4
        text_width = caption.shape[1]

        unit = width // (4 * z_size)
        inside = unit % 128 == 0
        order = [4 * k + j for k in range(z_size) for j in (0, 2, 1, 3)] if inside else None

        def outer(values):
            return values if inside else layer_order(values)

        first = jnp.concatenate(
            [
                w_qkv.reshape(shard_rows, 3, 4, group)
                .transpose(2, 0, 1, 3)
                .reshape(4, shard_rows, 3 * group),
                column_blocks(w_out, 4),
            ],
            axis=2,
        )
        first = gather_rows(place(swap_blocks(first, rank), rank))
        positions = lax.axis_index("y") * local_rows + jnp.arange(local_rows, dtype=jnp.int32)
        ranks = jnp.arange(full_length, dtype=jnp.int32)
        matches = (mask_index[:, :, None] == positions[None, None, :]) & (
            ranks[None, :, None] < mask_count[:, None, None]
        )
        masked = jnp.any(matches, axis=1).reshape(tokens, 1).astype(F32)
        gains = layer_order(norm_gains)
        gain_a, gain_b, gain_c = gains[:1], gains[1:2], gains[2:]
        start_x, attn_in, grad_top = start(
            outer(hidden.reshape(tokens, width)),
            outer(cotangent.reshape(tokens, width)),
            masked,
            layer_order(mask_embed)[None],
            gain_a,
            unit,
            order,
        )
        attn_in = gather_tokens(attn_in)
        mid = jnp.concatenate([column_blocks(w_cross[:, 0], 4), column_blocks(w_cross_out, 4)], axis=2)
        up = column_blocks(w_up, 4)
        attn_in, mid, up = lax.optimization_barrier((attn_in, mid, up))
        mid, up = gather_rows(trade(mid)), gather_rows(trade(up))

        kv_rows = w_cross[:, 1:].reshape(shard_rows, 2 * width)
        own_text, kv_part = text_forward(caption, w_text, kv_rows)
        text_kv = trade(kv_part, PLANE).astype(F32).sum(axis=0).astype(BF)
        text_kv = sum_z(text_kv).astype(BF)
        other = swap(text_kv, "c")
        text_kv = jnp.concatenate(
            [jnp.where(core == 0, text_kv, other), jnp.where(core == 0, other, text_kv)], axis=0
        )
        attn_in, text_kv = lax.optimization_barrier((attn_in, text_kv))

        attn_in, projected = gather_mm(attn_in, first, 0, 3 * group, "qkv_mm")
        self_mixed = self_forward(projected, 2 * images)
        down = column_blocks(w_down, 4)
        self_mixed, down = lax.optimization_barrier((self_mixed, down))
        down = gather_rows(trade(down))
        parts = mm_scatter(self_mixed, first[:, 3 * group :])
        after_attn, cross_in = add_norm([start_x] + parts, gain_b)

        cross_in, cross_queries = gather_mm(gather_tokens(cross_in), mid, 0, group, "query_mm")
        cross_mixed = cross_forward(cross_queries, text_kv)
        parts = mm_scatter(cross_mixed, mid[:, group:])
        after_cross, mlp_in = add_norm([after_attn] + parts, gain_c)

        mlp_in = gather_tokens(mlp_in)
        mlp_in, grad_top = lax.optimization_barrier((mlp_in, grad_top))
        grad_y = jnp.concatenate(gather_tokens(grad_top), axis=0)
        mlp_in, activated, slope = feed_up(mlp_in, up)
        early = [attn_in, self_mixed, cross_in, cross_mixed]
        if inside:
            grad_axes, halves = "z", (core, z_size)

            def both(values):
                return [values, swap(values, "c")]

        else:
            grad_axes, halves = DATA, ()

            def both(values):
                return [values]

        early = [both(values) for values in early]
        down_part = grad_products([(both(grad_y), both(activated))], "down_grads", *halves)
        mlp_in = both(mlp_in)
        slope, down_part, early, mlp_in = lax.optimization_barrier((slope, down_part, early, mlp_in))
        down_rows = scatter_grad(down_part, grad_axes)
        grad_pre = feed_down(grad_y, slope, down)
        parts = mm_scatter(grad_pre, up)
        up_part = grad_products([(mlp_in, both(grad_pre))], "up_grads", *halves)
        grad_after_cross, cross_branch, gain_grad_c = norm_back(
            parts, grad_top, after_cross, gain_c
        )

        cross_branch, grad_cross_mixed = gather_mm(
            gather_tokens(cross_branch), mid, group, group, "cross_out_back"
        )
        grad_cq, kv_grad = cross_back(cross_queries, text_kv, grad_cross_mixed)
        up_part, down_rows, kv_grad = lax.optimization_barrier((up_part, down_rows, kv_grad))
        up_rows = scatter_grad(up_part, grad_axes)
        cross_branch, grad_cq_both = both(cross_branch), both(grad_cq)
        parts = mm_scatter(grad_cq, mid[:, :group])
        grad_after_attn, attn_branch, gain_grad_b = norm_back(
            parts, grad_after_cross, after_attn, gain_b
        )

        attn_branch, grad_self_mixed = gather_mm(
            gather_tokens(attn_branch), first, 3 * group, group, "out_back"
        )
        grad_projected = self_back(projected, grad_self_mixed, 2 * images)
        rest_part = grad_products(
            [
                (early[0], both(grad_projected)),
                (both(attn_branch), early[1]),
                (early[2], grad_cq_both),
                (cross_branch, early[3]),
            ],
            "attention_grads",
            *halves,
        )
        grad_projected, activated, kv_grad, rest_part = lax.optimization_barrier(
            (grad_projected, activated, kv_grad, rest_part)
        )
        rest_part, up_rows = lax.optimization_barrier((rest_part, up_rows))
        rest_rows = scatter_grad(rest_part, grad_axes)
        parts = mm_scatter(grad_projected, first[:, : 3 * group])
        grad_hidden, gain_grad_a, mask_grad = last_back(
            parts,
            grad_after_attn,
            start_x,
            gain_a,
            masked,
            unit,
            order,
        )
        sums = jnp.concatenate([gain_grad_a, gain_grad_b, gain_grad_c, mask_grad], axis=0)

        parts = mm_scatter(activated, down)
        output = layer_output(after_cross, parts, unit, order)

        kv_halves = kv_grad.reshape(2, -1, 2 * group)
        kv_keep = lax.dynamic_index_in_dim(kv_halves, core, 0, keepdims=False)
        kv_send = lax.dynamic_index_in_dim(kv_halves, 1 - core, 0, keepdims=False)
        kv_sum = sum_z((kv_keep + swap(kv_send, "c")).astype(BF)).astype(BF)
        kv_grads = spread(kv_sum, PLANE, 8)
        kv_weight_grad, grad_text_w, caption_part = text_back(
            kv_grads, own_text, kv_rows, caption, w_text, halves_of(sums, text_width // 4)
        )
        half_context = caption.shape[0] // 2

        def summed(total):
            return total[:half_context].astype(BF), whole_of(total[half_context:], width)

        caption_part, sums = summed(trade(caption_part, PLANE).astype(F32).sum(axis=0))
        both_parts = jnp.concatenate([caption_part, halves_of(sums, text_width // 4)], axis=0)
        caption_part, sums = summed(sum_z(both_parts))
        grad_caption = caption_output(spread(caption_part, PLANE, 8))
        sums = layer_order(sums)

        wide_rows = jnp.concatenate([down_rows, up_rows], axis=2)
        down_grad, up_grad = finish_wide(swap_blocks(wide_rows, rank), rank)
        qkv_grad, out_grad, grad_cross, cross_out_grad = finish_all(
            swap_blocks(rest_rows, rank), kv_weight_grad, rank
        )
        return (
            outer(output).reshape(hidden.shape),
            outer(grad_hidden).reshape(hidden.shape),
            grad_caption,
            sums[:3],
            sums[3],
            qkv_grad,
            out_grad,
            grad_cross,
            cross_out_grad,
            grad_text_w,
            up_grad,
            down_grad,
        )

    return local


def solution(mesh):
    z_size = mesh.shape["img"] // 4
    inner = Mesh(mesh.devices.reshape(z_size, 2, 2, 2), ("z", "x", "c", "y"))
    image = ("z", "x", "c")
    tokens = P(image, "y", None)
    rows = P(image + ("y",))
    in_specs = (tokens, P(image, None), P(image), P(), P(), P()) + (rows,) * 7 + (tokens,)
    out_specs = (tokens, tokens, P(), P(), P()) + (rows,) * 7
    return jax.shard_map(
        make_local(z_size), mesh=inner, in_specs=in_specs, out_specs=out_specs, check_vma=False
    )
```

```python
import math

import jax
import jax.numpy as jnp
from jax import lax
from jax.experimental import pallas as pl
from jax.experimental.pallas import tpu as pltpu
from jax.sharding import Mesh
from jax.sharding import PartitionSpec as P

HD = 128
EPS = 1e-05
BF = jnp.bfloat16
F32 = jnp.float32
PAIR = ((0, 1), (1, 0))
GROUP = ("x", "y")
DATA = ("z", "c")
PLANE = ("x", "c", "y")
VMEM = 48 * 1024 * 1024
SCALE = 1.0 / math.sqrt(HD)
SLOPE = math.sqrt(2.0 / math.pi)
CUBIC = 0.044715


def dot(a, b, dims):
    return lax.dot_general(a, b, (dims, ((), ())), preferred_element_type=F32)


def mm(a, b):
    return dot(a, b, ((1,), (0,)))


def mm_t(a, b):
    return dot(a, b, ((1,), (1,)))


def t_mm(a, b):
    return dot(a, b, ((0,), (0,)))


def shape(dims, dtype=BF):
    return jax.ShapeDtypeStruct(dims, dtype)


def swap(values, axis):
    return lax.ppermute(values, axis, PAIR)


def trade(blocks, axes=GROUP):
    return lax.all_to_all(blocks, axes, 0, 0, tiled=True)


def spread(values, axes=GROUP, count=4):
    return trade(jnp.broadcast_to(values[None], (count,) + values.shape), axes)


def gather_tokens(own):
    half = own.shape[0] // 2
    from_x = swap(own, "x")
    from_y = swap(own, "y")
    return own, from_y, from_x, swap(from_x[:half], "y"), swap(from_y[half:], "x")


def scatter_tokens(parts):
    own, for_y, for_x, for_low, for_high = parts
    half = for_low.shape[0]
    low = swap(for_low, "y").astype(F32) + for_x[:half].astype(F32)
    high = swap(for_high, "x").astype(F32) + for_y[half:].astype(F32)
    from_x = swap(jnp.concatenate([low.astype(BF), for_x[half:]], axis=0), "x")
    from_y = swap(jnp.concatenate([for_y[:half], high.astype(BF)], axis=0), "y")
    return [own, from_x, from_y]


def swap_blocks(blocks, rank):
    parts = [lax.dynamic_index_in_dim(blocks, rank ^ k, 0, keepdims=False) for k in range(4)]
    return [
        parts[0],
        swap(parts[1], "y"),
        swap(parts[2], "x"),
        lax.ppermute(parts[3], GROUP, ((0, 3), (1, 2), (2, 1), (3, 0))),
    ]


def gather_rows(rows):
    return lax.all_gather(rows.reshape(-1, rows.shape[-1]), DATA, axis=0, tiled=True)


def scatter_grad(partial, axes):
    summed = lax.psum_scatter(partial, axes, scatter_dimension=0, tiled=True)
    return summed.reshape(4, -1, summed.shape[-1])


def call(kernel, grid, in_specs, out_specs, out_shape, operands, name, flops=0, size=1 << 22,
         rank=None, scratch=()):
    options = dict(
        out_shape=out_shape,
        compiler_params=pltpu.CompilerParams(vmem_limit_bytes=VMEM),
        cost_estimate=pl.CostEstimate(flops=flops, bytes_accessed=size, transcendentals=0),
        name=name,
    )
    if rank is None:
        return pl.pallas_call(
            kernel, grid=grid, in_specs=in_specs, out_specs=out_specs, scratch_shapes=scratch,
            **options,
        )(*operands)
    spec = pltpu.PrefetchScalarGridSpec(
        num_scalar_prefetch=1,
        grid=grid,
        in_specs=in_specs,
        out_specs=out_specs,
        scratch_shapes=scratch,
    )
    return pl.pallas_call(kernel, grid_spec=spec, **options)(rank.reshape(1), *operands)


def whole(array):
    return pl.BlockSpec(array.shape, lambda *_: (0,) * len(array.shape))


def reorder(values, unit, order):
    if order is None:
        return values
    return jnp.concatenate([values[:, k * unit : (k + 1) * unit] for k in order], axis=1)


def assemble(target, pieces, sems):
    copies, at = [], 0
    for k, piece in enumerate(pieces):
        rows = piece.shape[0]
        copies.append(pltpu.make_async_copy(piece, target.at[at : at + rows], sems.at[k]))
        at += rows
    for copy in copies:
        copy.start()
    for copy in copies:
        copy.wait()


ANY = pl.BlockSpec(memory_space=pltpu.MemorySpace.HBM)


def gather_mm(pieces, weight, first, columns, name):
    rows, width = pieces[0].shape
    step = 256

    def kernel(*refs):
        tokens, out, sems = refs[6:]

        @pl.when(pl.program_id(0) == 0)
        def _():
            assemble(tokens, refs[:5], sems)

        out[...] = mm(tokens[...], refs[5][...]).astype(BF)

    return call(
        kernel,
        (columns // step,),
        [ANY] * 5 + [pl.BlockSpec((width, step), lambda j: (0, first // step + j))],
        [
            pl.BlockSpec((4 * rows, width), lambda j: (0, 0)),
            pl.BlockSpec((4 * rows, step), lambda j: (0, j)),
        ],
        [shape((4 * rows, width)), shape((4 * rows, columns))],
        [*pieces, weight],
        name,
        flops=8 * rows * width * columns,
        size=2 * width * (columns + 8 * rows),
        scratch=[pltpu.SemaphoreType.DMA((5,))],
    )


def mm_scatter(values, weight):
    partial = mm_t(values, weight)
    rows = partial.shape[0] // 4
    low = partial[rows:].astype(BF)
    half = rows // 2
    cuts = [low[:rows], low[rows : 2 * rows], low[2 * rows : 2 * rows + half], low[2 * rows + half :]]
    return scatter_tokens([partial[:rows], *cuts])


def normalize(values):
    centred = values - jnp.mean(values, axis=-1, keepdims=True)
    inv_std = lax.rsqrt(jnp.mean(centred * centred, axis=-1, keepdims=True) + EPS)
    return centred * inv_std, inv_std


NORM_ROWS = 32


def row_spec(array, at=None):
    width = array.shape[-1]
    if at is None:
        return pl.BlockSpec((NORM_ROWS, width), lambda i: (i, 0))
    return pl.BlockSpec((1, NORM_ROWS, width), lambda i, at=at: (at, i, 0))


def terms_of(terms):
    arrays, specs = [], []
    for term in terms:
        array, at = term if isinstance(term, tuple) else (term, None)
        arrays.append(array)
        specs.append(row_spec(array, at))
    return arrays, specs


def total_of(refs):
    values = [ref[0] if len(ref.shape) == 3 else ref[...] for ref in refs]
    return sum(value.astype(F32) for value in values)


def add_norm(terms, gain):
    arrays, specs = terms_of(terms)
    tokens, width = arrays[0].shape[-2], arrays[0].shape[-1]
    tokens = min(a.shape[-2] for a in arrays)

    def kernel(*refs):
        gain_ref, x, out = refs[-3:]
        values = total_of(refs[:-3])
        x[...] = values
        out[...] = (normalize(values)[0] * gain_ref[...]).astype(BF)

    return call(
        kernel,
        (tokens // NORM_ROWS,),
        specs + [whole(gain)],
        [row_spec(shape((tokens, width)))] * 2,
        [shape((tokens, width), F32), shape((tokens, width))],
        [*arrays, gain],
        "add_norm",
    )


def norm_grad(grad, values, gain):
    normed, inv_std = normalize(values)
    scaled = grad * gain
    first_mean = jnp.mean(scaled, axis=-1, keepdims=True)
    second_mean = jnp.mean(scaled * normed, axis=-1, keepdims=True)
    return (
        inv_std * (scaled - first_mean - normed * second_mean),
        jnp.sum(grad * normed, axis=0, keepdims=True),
    )


def accumulate(ref, value):
    @pl.when(pl.program_id(0) == 0)
    def _():
        ref[...] = jnp.zeros_like(ref)

    ref[...] += value


def norm_back(terms, upper, values, gain):
    arrays, specs = terms_of(terms)
    tokens, width = values.shape

    def kernel(*refs):
        upper_ref, x, gain_ref, out, out_low, gain_grad = refs[-6:]
        back, part = norm_grad(total_of(refs[:-6]), x[...], gain_ref[...])
        result = upper_ref[...].astype(F32) + back
        out[...] = result
        out_low[...] = result.astype(BF)
        accumulate(gain_grad, part)

    return call(
        kernel,
        (tokens // NORM_ROWS,),
        specs + [row_spec(upper), row_spec(values), whole(gain)],
        [row_spec(values)] * 2 + [pl.BlockSpec((1, width), lambda i: (0, 0))],
        [shape((tokens, width), F32), shape((tokens, width)), shape((1, width), F32)],
        [*arrays, upper, values, gain],
        "norm_back",
    )


def last_back(terms, upper, values, gain, masked, unit, order):
    arrays, specs = terms_of(terms)
    tokens, width = values.shape

    def kernel(*refs):
        upper_ref, x, gain_ref, mask, out, gain_grad, mask_grad = refs[-7:]
        back, part = norm_grad(total_of(refs[:-7]), x[...], gain_ref[...])
        result = upper_ref[...].astype(F32) + back
        hit = mask[...] > 0.5
        out[...] = reorder(jnp.where(hit, 0.0, result).astype(BF), unit, order)
        accumulate(gain_grad, part)
        accumulate(mask_grad, jnp.sum(jnp.where(hit, result, 0.0), axis=0, keepdims=True))

    line = pl.BlockSpec((1, width), lambda i: (0, 0))
    return call(
        kernel,
        (tokens // NORM_ROWS,),
        specs + [row_spec(upper), row_spec(values), whole(gain), row_spec(masked)],
        [row_spec(values), line, line],
        [shape((tokens, width)), shape((1, width), F32), shape((1, width), F32)],
        [*arrays, upper, values, gain, masked],
        "last_back",
    )


def start(hidden, cotangent, masked, embed, gain, unit, order):
    tokens, width = hidden.shape

    def kernel(hid, cot, mask, embed_ref, gain_ref, x, out, grad):
        hit = mask[...] > 0.5
        values = jnp.where(
            hit, embed_ref[...], reorder(hid[...], unit, order).astype(F32)
        )
        x[...] = values
        out[...] = (normalize(values)[0] * gain_ref[...]).astype(BF)
        grad[...] = jnp.where(hit, reorder(cot[...], unit, order).astype(F32), 0.0).astype(BF)

    rows = row_spec(hidden)
    return call(
        kernel,
        (tokens // NORM_ROWS,),
        [rows, rows, row_spec(masked), whole(embed), whole(gain)],
        [rows] * 3,
        [shape((tokens, width), F32), shape((tokens, width)), shape((tokens, width))],
        [hidden, cotangent, masked, embed, gain],
        "start",
    )


def layer_output(upper, terms, unit, order):
    arrays, specs = terms_of(terms)
    tokens, width = upper.shape

    def kernel(*refs):
        values = refs[-2][...] + total_of(refs[:-2])
        refs[-1][...] = reorder(values.astype(BF), unit, order)

    return call(
        kernel,
        (tokens // NORM_ROWS,),
        specs + [row_spec(upper)],
        row_spec(upper),
        shape((tokens, width)),
        [*arrays, upper],
        "layer_output",
    )


def feed_up(pieces, weight):
    rows, width = pieces[0].shape
    hidden = weight.shape[1]
    step = 256

    def kernel(*refs):
        up, tokens, act, slope, sems = refs[5:]

        @pl.when(pl.program_id(0) == 0)
        def _():
            assemble(tokens, refs[:5], sems)

        u = mm(tokens[...], up[...])
        square = u * u
        bend = jnp.tanh(SLOPE * u * (1.0 + CUBIC * square))
        half = 0.5 * (1.0 + bend)
        act[...] = (u * half).astype(BF)
        slope[...] = half + 0.5 * u * (1.0 - bend * bend) * SLOPE * (1.0 + 3.0 * CUBIC * square)

    part = pl.BlockSpec((4 * rows, step), lambda j: (0, j))
    return call(
        kernel,
        (hidden // step,),
        [ANY] * 5 + [pl.BlockSpec((width, step), lambda j: (0, j))],
        [pl.BlockSpec((4 * rows, width), lambda j: (0, 0)), part, part],
        [shape((4 * rows, width)), shape((4 * rows, hidden)), shape((4 * rows, hidden), F32)],
        [*pieces, weight],
        "feed_up",
        scratch=[pltpu.SemaphoreType.DMA((5,))],
        flops=8 * rows * width * hidden,
        size=2 * width * (hidden + 8 * rows),
    )


def feed_down(grad_y, slope, weight):
    tokens, width = grad_y.shape
    hidden = weight.shape[1]
    step = 256

    def kernel(dy, slope_ref, down, out):
        out[...] = (mm(dy[...], down[...]) * slope_ref[...]).astype(BF)

    part = pl.BlockSpec((tokens, step), lambda j: (0, j))
    return call(
        kernel,
        (hidden // step,),
        [whole(grad_y), part, pl.BlockSpec((width, step), lambda j: (0, j))],
        part,
        shape((tokens, hidden)),
        [grad_y, slope, weight],
        "feed_down",
        flops=2 * tokens * width * hidden,
        size=2 * width * (hidden + 8 * tokens),
    )


def softmax(scores):
    exp_terms = jnp.exp(scores - jnp.max(scores, axis=-1, keepdims=True))
    return exp_terms / jnp.sum(exp_terms, axis=-1, keepdims=True)


def score_grad(probs, grad_probs):
    return (
        probs * (grad_probs - jnp.sum(probs * grad_probs, axis=-1, keepdims=True))
    ).astype(BF)


def head(ref, k):
    return ref[:, k * HD : (k + 1) * HD]


def self_forward(projected, images):
    tokens, width = projected.shape
    rows, group = tokens // images, width // 3
    heads = group // HD

    def kernel(proj, mixed):
        for k in range(heads):
            query, key, value = (head(proj, j * heads + k) for j in range(3))
            probs = softmax(mm_t(query, key) * SCALE).astype(BF)
            mixed[:, k * HD : (k + 1) * HD] = mm(probs, value).astype(BF)

    return call(
        kernel,
        (images,),
        [pl.BlockSpec((rows, width), lambda i: (i, 0))],
        pl.BlockSpec((rows, group), lambda i: (i, 0)),
        shape((tokens, group)),
        [projected],
        "self_forward",
        flops=4 * tokens * rows * group,
    )


def self_back(projected, grad_mixed, images):
    tokens, width = projected.shape
    rows, group = tokens // images, width // 3
    heads = group // HD

    def kernel(proj, grad, out):
        for k in range(heads):
            query, key, value = (head(proj, j * heads + k) for j in range(3))
            grad_head = head(grad, k)
            probs = softmax(mm_t(query, key) * SCALE)
            grad_scores = score_grad(probs, mm_t(grad_head, value))
            parts = (
                mm(grad_scores, key) * SCALE,
                t_mm(grad_scores, query) * SCALE,
                t_mm(probs.astype(BF), grad_head),
            )
            for j, part in enumerate(parts):
                at = (j * heads + k) * HD
                out[:, at : at + HD] = part.astype(BF)

    return call(
        kernel,
        (images,),
        [
            pl.BlockSpec((rows, width), lambda i: (i, 0)),
            pl.BlockSpec((rows, group), lambda i: (i, 0)),
        ],
        pl.BlockSpec((rows, width), lambda i: (i, 0)),
        shape((tokens, width)),
        [projected, grad_mixed],
        "self_back",
        flops=10 * tokens * rows * group,
    )


def cross_forward(queries, text_kv):
    tokens, group = queries.shape
    heads = group // HD

    def kernel(query, text, mixed):
        for k in range(heads):
            probs = softmax(mm_t(head(query, k), head(text, k)) * SCALE).astype(BF)
            mixed[:, k * HD : (k + 1) * HD] = mm(probs, head(text, heads + k)).astype(BF)

    return call(
        kernel,
        (1,),
        [whole(queries), whole(text_kv)],
        whole(queries),
        shape((tokens, group)),
        [queries, text_kv],
        "cross_forward",
        flops=4 * tokens * text_kv.shape[0] * group,
    )


def cross_back(queries, text_kv, grad_mixed):
    tokens, group = queries.shape
    context = text_kv.shape[0]
    heads = group // HD

    def kernel(query, text, grad, grad_query, grad_text):
        for k in range(heads):
            query_head, key, value = head(query, k), head(text, k), head(text, heads + k)
            grad_head = head(grad, k)
            probs = softmax(mm_t(query_head, key) * SCALE)
            grad_scores = score_grad(probs, mm_t(grad_head, value))
            grad_query[:, k * HD : (k + 1) * HD] = (mm(grad_scores, key) * SCALE).astype(BF)
            at = (heads + k) * HD
            grad_text[:, k * HD : (k + 1) * HD] = t_mm(grad_scores, query_head) * SCALE
            grad_text[:, at : at + HD] = t_mm(probs.astype(BF), grad_head)

    return call(
        kernel,
        (1,),
        [whole(queries), whole(text_kv), whole(grad_mixed)],
        [whole(queries), whole(text_kv)],
        [shape((tokens, group)), shape((context, 2 * group), F32)],
        [queries, text_kv, grad_mixed],
        "cross_back",
        flops=10 * tokens * context * group,
    )


def grad_products(pairs, name, core=None, blocks=0):
    count_in = len(pairs[0][0])
    tokens, width = pairs[0][0][0].shape
    widths = [y[0].shape[1] for _, y in pairs]
    total = sum(widths)
    rows = 256 if core is None else width // (2 * blocks)
    steps = width // rows if core is None else blocks
    step = 512
    count = len(pairs) * count_in

    def kernel(r, *refs):
        out = refs[2 * count]
        offset = 0
        for k, wide in enumerate(widths):
            left = [refs[k * count_in + b][...].T for b in range(count_in)]
            for at in range(0, wide, step):
                out[:, offset + at : offset + at + step] = sum(
                    mm(left[b], refs[count + k * count_in + b][:, at : at + step])
                    for b in range(count_in)
                ).astype(BF)
            offset += wide

    pick = (lambda i, r: (0, i)) if core is None else (lambda i, r: (0, 2 * i + r[0]))
    return call(
        kernel,
        (steps,),
        [pl.BlockSpec((tokens, rows), pick)] * count
        + [pl.BlockSpec((tokens, w), lambda i, r: (0, 0)) for w in widths for _ in range(count_in)],
        pl.BlockSpec((rows, total), lambda i, r: (i, 0)),
        shape((steps * rows, total)),
        [b for x, _ in pairs for b in x] + [b for _, y in pairs for b in y],
        name,
        flops=2 * tokens * count_in * steps * rows * total,
        size=4 * width * total,
        rank=jnp.zeros((), jnp.int32) if core is None else core,
    )


def place(parts, rank):
    def kernel(r, *refs):
        for k in range(4):

            @pl.when(pl.program_id(0) == k)
            def _():
                refs[4][0] = refs[k][...]

    rows, columns = parts[0].shape
    return call(
        kernel,
        (4,),
        [whole(p) for p in parts],
        pl.BlockSpec((1, rows, columns), lambda k, r: (k ^ r[0], 0, 0)),
        shape((4, rows, columns)),
        parts,
        "place",
        rank=rank,
    )


def finish_wide(parts, rank):
    rows, total = parts[0].shape
    width = total // 2

    def kernel(r, *refs):
        for k in range(4):

            @pl.when(pl.program_id(0) == k)
            def _():
                refs[4][...] = refs[k][:, :width].astype(F32)
                refs[5][...] = refs[k][:, width:].astype(F32)

    flat = pl.BlockSpec((rows, width), lambda k, r: (0, k ^ r[0]))
    return call(
        kernel,
        (4,),
        [whole(p) for p in parts],
        [flat, flat],
        [shape((rows, 4 * width), F32)] * 2,
        parts,
        "finish_wide",
        rank=rank,
    )


def finish_all(parts, text_grad, rank):
    rows, total = parts[0].shape
    width = total // 6

    def kernel(r, *refs):
        key, value, three, out, cross, cross_out = refs[4:]
        for k in range(4):

            @pl.when(pl.program_id(0) == k)
            def _():
                def part(j):
                    return refs[k][:, j * width : (j + 1) * width].astype(F32)

                for j in range(3):
                    three[:, j, :] = part(j)
                out[...] = part(3)
                cross[:, 0, :] = part(4)
                cross_out[...] = part(5)

        cross[:, 1, :] = key[...]
        cross[:, 2, :] = value[...]

    wide = pl.BlockSpec((rows, 3, width), lambda k, r: (0, 0, k ^ r[0]))
    flat = pl.BlockSpec((rows, width), lambda k, r: (0, k ^ r[0]))
    return call(
        kernel,
        (4,),
        [whole(p) for p in parts]
        + [flat, pl.BlockSpec((rows, width), lambda k, r: (0, 4 + (k ^ r[0])))],
        [wide, flat, wide, flat],
        [shape((rows, 3, 4 * width), F32), shape((rows, 4 * width), F32)] * 2,
        [*parts, text_grad, text_grad],
        "finish_all",
        rank=rank,
    )


def plane_block(k):
    return (k >> 1) & 1, (k >> 2) * 2 + (k & 1)


def text_forward(caption, w_text, kv_rows):
    context, rows = caption.shape[0], w_text.shape[0]
    half, width = context // 2, kv_rows.shape[1] // 8

    def kernel(cap, weight, kv, own, blocks):
        own[...] = mm_t(cap[...], weight[...]).astype(BF)
        part = mm(own[...], kv[...]).astype(BF)
        for k in range(8):
            core, group = plane_block(k)
            for j in range(2):
                at = (4 * j + group) * width
                blocks[k, :, j * width : (j + 1) * width] = part[
                    core * half : (core + 1) * half, at : at + width
                ]

    return call(
        kernel,
        (1,),
        [whole(caption), whole(w_text), whole(kv_rows)],
        [
            pl.BlockSpec((context, rows), lambda i: (0, 0)),
            pl.BlockSpec((8, half, 2 * width), lambda i: (0, 0, 0)),
        ],
        [shape((context, rows)), shape((8, half, 2 * width))],
        [caption, w_text, kv_rows],
        "text_forward",
    )


def text_back(blocks, own_text, kv_rows, caption, w_text, extra):
    context, rows = own_text.shape
    half, width = context // 2, kv_rows.shape[1] // 8
    wide = caption.shape[1] // 4
    tail = extra.shape[0]

    def kernel(block, own, kv, cap, weight, more, kv_grad, text_grad, out, grads):
        for k in range(8):
            core, group = plane_block(k)
            for j in range(2):
                at = (4 * j + group) * width
                grads[core * half : (core + 1) * half, at : at + width] = block[
                    k, :, j * width : (j + 1) * width
                ]
        kv_grad[...] = t_mm(own[...], grads[...])
        grad_text = mm_t(grads[...], kv[...]).astype(BF)
        text_grad[...] = t_mm(grad_text, cap[...])
        part = mm(grad_text, weight[...]).astype(BF)
        for k in range(8):
            core, group = plane_block(k)
            out[k, :half, :] = part[core * half : (core + 1) * half, group * wide : (group + 1) * wide]
            out[k, half:, :] = more[...]

    operands = [blocks, own_text, kv_rows, caption, w_text, extra]
    outs = [
        shape((rows, 8 * width), F32),
        shape((rows, 4 * wide), F32),
        shape((8, half + tail, wide)),
    ]
    return call(
        kernel,
        (1,),
        [whole(a) for a in operands],
        [whole(a) for a in outs],
        outs,
        operands,
        "text_back",
        scratch=[pltpu.VMEM((context, 8 * width), BF)],
    )


def caption_output(blocks):
    count, half, wide = blocks.shape

    def kernel(block, out):
        out[...] = block[0].astype(F32)

    return call(
        kernel,
        (count,),
        [pl.BlockSpec((1, half, wide), lambda k: (k, 0, 0))],
        pl.BlockSpec((half, wide), lambda k: plane_block(k)),
        shape((2 * half, 4 * wide), F32),
        [blocks],
        "caption_output",
    )


def column_blocks(weight, count):
    rows = weight.shape[0]
    return weight.reshape(rows, count, -1).transpose(1, 0, 2)


def halves_of(values, width):
    high = values.astype(BF)
    low = (values - high.astype(F32)).astype(BF)
    return jnp.concatenate([high.reshape(-1, width), low.reshape(-1, width)], axis=0)


def whole_of(halves, width):
    rows = halves.shape[0] // 2
    return (halves[:rows] + halves[rows:]).reshape(-1, width)


def make_local(z_size):
    def sum_z(values):
        parts = values.reshape(z_size, -1, values.shape[-1])
        mine = trade(parts, "z").astype(F32).sum(axis=0).astype(BF)
        return spread(mine, "z", z_size).reshape(values.shape)

    def add_z(values):
        step = 1
        while step < z_size:
            values = values + lax.ppermute(
                values, "z", tuple((k, k ^ step) for k in range(z_size))
            )
            step *= 2
        return values

    def layer_order(values):
        shaped = values.reshape(values.shape[:-1] + (z_size, 2, 2, -1))
        return jnp.swapaxes(shaped, -3, -2).reshape(values.shape)

    def local(
        hidden,
        mask_index,
        mask_count,
        mask_embed,
        norm_gains,
        caption,
        w_qkv,
        w_out,
        w_cross,
        w_cross_out,
        w_text,
        w_up,
        w_down,
        cotangent,
    ):
        images, local_rows, width = hidden.shape
        full_length = mask_index.shape[1]
        shard_rows = w_qkv.shape[0]
        rank = lax.axis_index("x") * 2 + lax.axis_index("y")
        core = lax.axis_index("c")
        tokens = images * local_rows
        group = width // 4
        text_width = caption.shape[1]

        unit = width // (4 * z_size)
        inside = unit % 128 == 0
        order = [4 * k + j for k in range(z_size) for j in (0, 2, 1, 3)] if inside else None

        def outer(values):
            return values if inside else layer_order(values)

        first = jnp.concatenate(
            [
                w_qkv.reshape(shard_rows, 3, 4, group)
                .transpose(2, 0, 1, 3)
                .reshape(4, shard_rows, 3 * group),
                column_blocks(w_out, 4),
            ],
            axis=2,
        )
        first = gather_rows(place(swap_blocks(first, rank), rank))
        positions = lax.axis_index("y") * local_rows + jnp.arange(local_rows, dtype=jnp.int32)
        ranks = jnp.arange(full_length, dtype=jnp.int32)
        matches = (mask_index[:, :, None] == positions[None, None, :]) & (
            ranks[None, :, None] < mask_count[:, None, None]
        )
        masked = jnp.any(matches, axis=1).reshape(tokens, 1).astype(F32)
        gains = layer_order(norm_gains)
        gain_a, gain_b, gain_c = gains[:1], gains[1:2], gains[2:]
        start_x, attn_in, grad_top = start(
            outer(hidden.reshape(tokens, width)),
            outer(cotangent.reshape(tokens, width)),
            masked,
            layer_order(mask_embed)[None],
            gain_a,
            unit,
            order,
        )
        attn_in = gather_tokens(attn_in)
        mid = jnp.concatenate([column_blocks(w_cross[:, 0], 4), column_blocks(w_cross_out, 4)], axis=2)
        up = column_blocks(w_up, 4)
        attn_in, mid, up = lax.optimization_barrier((attn_in, mid, up))
        mid, up = gather_rows(trade(mid)), gather_rows(trade(up))

        kv_rows = w_cross[:, 1:].reshape(shard_rows, 2 * width)
        own_text, kv_part = text_forward(caption, w_text, kv_rows)
        text_kv = trade(kv_part, PLANE).astype(F32).sum(axis=0).astype(BF)
        text_kv = sum_z(text_kv)
        other = swap(text_kv, "c")
        text_kv = jnp.concatenate(
            [jnp.where(core == 0, text_kv, other), jnp.where(core == 0, other, text_kv)], axis=0
        )
        attn_in, text_kv = lax.optimization_barrier((attn_in, text_kv))

        attn_in, projected = gather_mm(attn_in, first, 0, 3 * group, "qkv_mm")
        self_mixed = self_forward(projected, 2 * images)
        down = column_blocks(w_down, 4)
        self_mixed, down = lax.optimization_barrier((self_mixed, down))
        down = gather_rows(trade(down))
        parts = mm_scatter(self_mixed, first[:, 3 * group :])
        after_attn, cross_in = add_norm([start_x] + parts, gain_b)

        cross_in, cross_queries = gather_mm(gather_tokens(cross_in), mid, 0, group, "query_mm")
        cross_mixed = cross_forward(cross_queries, text_kv)
        parts = mm_scatter(cross_mixed, mid[:, group:])
        after_cross, mlp_in = add_norm([after_attn] + parts, gain_c)

        mlp_in = gather_tokens(mlp_in)
        mlp_in, grad_top = lax.optimization_barrier((mlp_in, grad_top))
        grad_y = jnp.concatenate(gather_tokens(grad_top), axis=0)
        mlp_in, activated, slope = feed_up(mlp_in, up)
        early = [attn_in, self_mixed, cross_in, cross_mixed]
        if inside:
            grad_axes, halves = "z", (core, z_size)

            def both(values):
                return [values, swap(values, "c")]

        else:
            grad_axes, halves = DATA, ()

            def both(values):
                return [values]

        early = [both(values) for values in early]
        down_part = grad_products([(both(grad_y), both(activated))], "down_grads", *halves)
        mlp_in = both(mlp_in)
        slope, down_part, early, mlp_in = lax.optimization_barrier((slope, down_part, early, mlp_in))
        down_rows = scatter_grad(down_part, grad_axes)
        grad_pre = feed_down(grad_y, slope, down)
        parts = mm_scatter(grad_pre, up)
        up_part = grad_products([(mlp_in, both(grad_pre))], "up_grads", *halves)
        grad_after_cross, cross_branch, gain_grad_c = norm_back(
            parts, grad_top, after_cross, gain_c
        )

        cross_branch = gather_tokens(cross_branch)
        cross_branch, up_part = lax.optimization_barrier((cross_branch, up_part))
        cross_branch, grad_cross_mixed = gather_mm(
            cross_branch, mid, group, group, "cross_out_back"
        )
        grad_cq, kv_grad = cross_back(cross_queries, text_kv, grad_cross_mixed)
        up_part, down_rows, kv_grad = lax.optimization_barrier((up_part, down_rows, kv_grad))
        up_rows = scatter_grad(up_part, grad_axes)
        cross_branch, grad_cq_both = both(cross_branch), both(grad_cq)
        parts = mm_scatter(grad_cq, mid[:, :group])
        grad_after_attn, attn_branch, gain_grad_b = norm_back(
            parts, grad_after_cross, after_attn, gain_b
        )

        attn_branch, grad_self_mixed = gather_mm(
            gather_tokens(attn_branch), first, 3 * group, group, "out_back"
        )
        grad_projected = self_back(projected, grad_self_mixed, 2 * images)
        rest_part = grad_products(
            [
                (early[0], both(grad_projected)),
                (both(attn_branch), early[1]),
                (early[2], grad_cq_both),
                (cross_branch, early[3]),
            ],
            "attention_grads",
            *halves,
        )
        grad_projected, activated, kv_grad, rest_part = lax.optimization_barrier(
            (grad_projected, activated, kv_grad, rest_part)
        )
        rest_part, up_rows = lax.optimization_barrier((rest_part, up_rows))
        rest_rows = scatter_grad(rest_part, grad_axes)
        parts = mm_scatter(grad_projected, first[:, : 3 * group])
        grad_hidden, gain_grad_a, mask_grad = last_back(
            parts,
            grad_after_attn,
            start_x,
            gain_a,
            masked,
            unit,
            order,
        )
        sums = jnp.concatenate([gain_grad_a, gain_grad_b, gain_grad_c, mask_grad], axis=0)

        parts = mm_scatter(activated, down)
        output = layer_output(after_cross, parts, unit, order)

        kv_halves = kv_grad.reshape(2, -1, 2 * group)
        kv_keep = lax.dynamic_index_in_dim(kv_halves, core, 0, keepdims=False)
        kv_send = lax.dynamic_index_in_dim(kv_halves, 1 - core, 0, keepdims=False)
        kv_sum = sum_z((kv_keep + swap(kv_send, "c")).astype(BF))
        wide_rows = jnp.concatenate([down_rows, up_rows], axis=2)
        wide_rows = swap_blocks(wide_rows, rank)
        kv_sum, wide_rows = lax.optimization_barrier((kv_sum, wide_rows))
        kv_grads = spread(kv_sum, PLANE, 8)
        down_grad, up_grad = finish_wide(wide_rows, rank)
        kv_weight_grad, grad_text_w, caption_part = text_back(
            kv_grads, own_text, kv_rows, caption, w_text, halves_of(sums, text_width // 4)
        )
        half_context = caption.shape[0] // 2
        caption_part = trade(caption_part, PLANE).astype(F32).sum(axis=0)
        sums = layer_order(add_z(whole_of(caption_part[half_context:], width)))
        caption_part = sum_z(caption_part[:half_context].astype(BF))
        grad_caption = caption_output(spread(caption_part, PLANE, 8))

        qkv_grad, out_grad, grad_cross, cross_out_grad = finish_all(
            swap_blocks(rest_rows, rank), kv_weight_grad, rank
        )
        return (
            outer(output).reshape(hidden.shape),
            outer(grad_hidden).reshape(hidden.shape),
            grad_caption,
            sums[:3],
            sums[3],
            qkv_grad,
            out_grad,
            grad_cross,
            cross_out_grad,
            grad_text_w,
            up_grad,
            down_grad,
        )

    return local


def solution(mesh):
    z_size = mesh.shape["img"] // 4
    inner = Mesh(mesh.devices.reshape(z_size, 2, 2, 2), ("z", "x", "c", "y"))
    image = ("z", "x", "c")
    tokens = P(image, "y", None)
    rows = P(image + ("y",))
    in_specs = (tokens, P(image, None), P(image), P(), P(), P()) + (rows,) * 7 + (tokens,)
    out_specs = (tokens, tokens, P(), P(), P()) + (rows,) * 7
    return jax.shard_map(
        make_local(z_size), mesh=inner, in_specs=in_specs, out_specs=out_specs, check_vma=False
    )
```

```python
import math

import jax
import jax.numpy as jnp
from jax import lax
from jax.experimental import pallas as pl
from jax.experimental.pallas import tpu as pltpu
from jax.sharding import Mesh
from jax.sharding import PartitionSpec as P

HD = 128
EPS = 1e-05
BF = jnp.bfloat16
F32 = jnp.float32
PAIR = ((0, 1), (1, 0))
GROUP = ("x", "y")
DATA = ("z", "c")
PLANE = ("x", "c", "y")
VMEM = 48 * 1024 * 1024
SCALE = 1.0 / math.sqrt(HD)
SLOPE = math.sqrt(2.0 / math.pi)
CUBIC = 0.044715


def dot(a, b, dims):
    return lax.dot_general(a, b, (dims, ((), ())), preferred_element_type=F32)


def mm(a, b):
    return dot(a, b, ((1,), (0,)))


def mm_t(a, b):
    return dot(a, b, ((1,), (1,)))


def t_mm(a, b):
    return dot(a, b, ((0,), (0,)))


def shape(dims, dtype=BF):
    return jax.ShapeDtypeStruct(dims, dtype)


def swap(values, axis):
    return lax.ppermute(values, axis, PAIR)


def trade(blocks, axes=GROUP):
    return lax.all_to_all(blocks, axes, 0, 0, tiled=True)


def spread(values, axes=GROUP, count=4):
    return trade(jnp.broadcast_to(values[None], (count,) + values.shape), axes)


def gather_tokens(own):
    half = own.shape[0] // 2
    from_x = swap(own, "x")
    from_y = swap(own, "y")
    return own, from_y, from_x, swap(from_x[:half], "y"), swap(from_y[half:], "x")


def scatter_tokens(parts):
    own, for_y, for_x, for_low, for_high = parts
    half = for_low.shape[0]
    low = swap(for_low, "y").astype(F32) + for_x[:half].astype(F32)
    high = swap(for_high, "x").astype(F32) + for_y[half:].astype(F32)
    from_x = swap(jnp.concatenate([low.astype(BF), for_x[half:]], axis=0), "x")
    from_y = swap(jnp.concatenate([for_y[:half], high.astype(BF)], axis=0), "y")
    return [own, from_x, from_y]


def swap_parts(parts):
    return [
        parts[0],
        swap(parts[1], "y"),
        swap(parts[2], "x"),
        lax.ppermute(parts[3], GROUP, ((0, 3), (1, 2), (2, 1), (3, 0))),
    ]


def gather_rows(rows):
    return lax.all_gather(rows.reshape(-1, rows.shape[-1]), DATA, axis=0, tiled=True)


def scatter_grad(partial, axes):
    summed = lax.psum_scatter(partial, axes, scatter_dimension=0, tiled=True)
    return summed.reshape(4, -1, summed.shape[-1])


def call(kernel, grid, in_specs, out_specs, out_shape, operands, name, flops=0, size=1 << 22,
         rank=None, scratch=()):
    options = dict(
        out_shape=out_shape,
        compiler_params=pltpu.CompilerParams(vmem_limit_bytes=VMEM),
        cost_estimate=pl.CostEstimate(flops=flops, bytes_accessed=size, transcendentals=0),
        name=name,
    )
    if rank is None:
        return pl.pallas_call(
            kernel, grid=grid, in_specs=in_specs, out_specs=out_specs, scratch_shapes=scratch,
            **options,
        )(*operands)
    spec = pltpu.PrefetchScalarGridSpec(
        num_scalar_prefetch=1,
        grid=grid,
        in_specs=in_specs,
        out_specs=out_specs,
        scratch_shapes=scratch,
    )
    return pl.pallas_call(kernel, grid_spec=spec, **options)(rank.reshape(1), *operands)


def whole(array):
    return pl.BlockSpec(array.shape, lambda *_: (0,) * len(array.shape))


def reorder(values, unit, order):
    if order is None:
        return values
    return jnp.concatenate([values[:, k * unit : (k + 1) * unit] for k in order], axis=1)


def assemble(target, pieces, sems):
    copies, at = [], 0
    for k, piece in enumerate(pieces):
        rows = piece.shape[0]
        copies.append(pltpu.make_async_copy(piece, target.at[at : at + rows], sems.at[k]))
        at += rows
    for copy in copies:
        copy.start()
    for copy in copies:
        copy.wait()


ANY = pl.BlockSpec(memory_space=pl.ANY)


def gather_mm(pieces, weight, first, columns, name):
    rows, width = pieces[0].shape
    step = 256

    def kernel(*refs):
        tokens, out, sems = refs[6:]

        @pl.when(pl.program_id(0) == 0)
        def _():
            assemble(tokens, refs[:5], sems)

        out[...] = mm(tokens[...], refs[5][...]).astype(BF)

    return call(
        kernel,
        (columns // step,),
        [ANY] * 5 + [pl.BlockSpec((width, step), lambda j: (0, first // step + j))],
        [
            pl.BlockSpec((4 * rows, width), lambda j: (0, 0)),
            pl.BlockSpec((4 * rows, step), lambda j: (0, j)),
        ],
        [shape((4 * rows, width)), shape((4 * rows, columns))],
        [*pieces, weight],
        name,
        flops=8 * rows * width * columns,
        size=2 * width * (columns + 8 * rows),
        scratch=[pltpu.SemaphoreType.DMA((5,))],
    )


def mm_scatter(values, weight):
    partial = mm_t(values, weight).astype(BF)
    rows = partial.shape[0] // 4
    cuts = [0, rows, 2 * rows, 3 * rows, 3 * rows + rows // 2, 4 * rows]
    return scatter_tokens([partial[a:b] for a, b in zip(cuts, cuts[1:])])


def normalize(values):
    centred = values - jnp.mean(values, axis=-1, keepdims=True)
    inv_std = lax.rsqrt(jnp.mean(centred * centred, axis=-1, keepdims=True) + EPS)
    return centred * inv_std, inv_std


NORM_ROWS = 32


def row_spec(array, at=None):
    width = array.shape[-1]
    if at is None:
        return pl.BlockSpec((NORM_ROWS, width), lambda i: (i, 0))
    return pl.BlockSpec((1, NORM_ROWS, width), lambda i, at=at: (at, i, 0))


def terms_of(terms):
    arrays, specs = [], []
    for term in terms:
        array, at = term if isinstance(term, tuple) else (term, None)
        arrays.append(array)
        specs.append(row_spec(array, at))
    return arrays, specs


def total_of(refs):
    values = [ref[0] if len(ref.shape) == 3 else ref[...] for ref in refs]
    return sum(value.astype(F32) for value in values)


def add_norm(terms, gain):
    arrays, specs = terms_of(terms)
    tokens, width = arrays[0].shape[-2], arrays[0].shape[-1]
    tokens = min(a.shape[-2] for a in arrays)

    def kernel(*refs):
        gain_ref, x, out = refs[-3:]
        values = total_of(refs[:-3])
        x[...] = values
        out[...] = (normalize(values)[0] * gain_ref[...]).astype(BF)

    return call(
        kernel,
        (tokens // NORM_ROWS,),
        specs + [whole(gain)],
        [row_spec(shape((tokens, width)))] * 2,
        [shape((tokens, width), F32), shape((tokens, width))],
        [*arrays, gain],
        "add_norm",
    )


def norm_grad(grad, values, gain):
    normed, inv_std = normalize(values)
    scaled = grad * gain
    first_mean = jnp.mean(scaled, axis=-1, keepdims=True)
    second_mean = jnp.mean(scaled * normed, axis=-1, keepdims=True)
    return (
        inv_std * (scaled - first_mean - normed * second_mean),
        jnp.sum(grad * normed, axis=0, keepdims=True),
    )


def accumulate(ref, value):
    @pl.when(pl.program_id(0) == 0)
    def _():
        ref[...] = jnp.zeros_like(ref)

    ref[...] += value


def norm_back(terms, upper, values, gain):
    arrays, specs = terms_of(terms)
    tokens, width = values.shape

    def kernel(*refs):
        upper_ref, x, gain_ref, out, out_low, gain_grad = refs[-6:]
        back, part = norm_grad(total_of(refs[:-6]), x[...], gain_ref[...])
        result = upper_ref[...].astype(F32) + back
        out[...] = result
        out_low[...] = result.astype(BF)
        accumulate(gain_grad, part)

    return call(
        kernel,
        (tokens // NORM_ROWS,),
        specs + [row_spec(upper), row_spec(values), whole(gain)],
        [row_spec(values)] * 2 + [pl.BlockSpec((1, width), lambda i: (0, 0))],
        [shape((tokens, width), F32), shape((tokens, width)), shape((1, width), F32)],
        [*arrays, upper, values, gain],
        "norm_back",
    )


def last_back(terms, upper, values, gain, masked, unit, order):
    arrays, specs = terms_of(terms)
    tokens, width = values.shape

    def kernel(*refs):
        upper_ref, x, gain_ref, mask, out, gain_grad, mask_grad = refs[-7:]
        back, part = norm_grad(total_of(refs[:-7]), x[...], gain_ref[...])
        result = upper_ref[...].astype(F32) + back
        hit = mask[...] > 0.5
        out[...] = reorder(jnp.where(hit, 0.0, result).astype(BF), unit, order)
        accumulate(gain_grad, part)
        accumulate(mask_grad, jnp.sum(jnp.where(hit, result, 0.0), axis=0, keepdims=True))

    line = pl.BlockSpec((1, width), lambda i: (0, 0))
    return call(
        kernel,
        (tokens // NORM_ROWS,),
        specs + [row_spec(upper), row_spec(values), whole(gain), row_spec(masked)],
        [row_spec(values), line, line],
        [shape((tokens, width)), shape((1, width), F32), shape((1, width), F32)],
        [*arrays, upper, values, gain, masked],
        "last_back",
    )


def start(hidden, cotangent, masked, embed, gain, unit, order):
    tokens, width = hidden.shape

    def kernel(hid, cot, mask, embed_ref, gain_ref, x, out, grad):
        hit = mask[...] > 0.5
        values = jnp.where(
            hit, embed_ref[...], reorder(hid[...], unit, order).astype(F32)
        )
        x[...] = values
        out[...] = (normalize(values)[0] * gain_ref[...]).astype(BF)
        grad[...] = jnp.where(hit, reorder(cot[...], unit, order).astype(F32), 0.0).astype(BF)

    rows = row_spec(hidden)
    return call(
        kernel,
        (tokens // NORM_ROWS,),
        [rows, rows, row_spec(masked), whole(embed), whole(gain)],
        [rows] * 3,
        [shape((tokens, width), F32), shape((tokens, width)), shape((tokens, width))],
        [hidden, cotangent, masked, embed, gain],
        "start",
    )


def layer_output(upper, terms, unit, order):
    arrays, specs = terms_of(terms)
    tokens, width = upper.shape

    def kernel(*refs):
        values = refs[-2][...] + total_of(refs[:-2])
        refs[-1][...] = reorder(values.astype(BF), unit, order)

    return call(
        kernel,
        (tokens // NORM_ROWS,),
        specs + [row_spec(upper)],
        row_spec(upper),
        shape((tokens, width)),
        [*arrays, upper],
        "layer_output",
    )


def feed_up(pieces, weight):
    rows, width = pieces[0].shape
    hidden = weight.shape[1]
    step = 256

    def kernel(*refs):
        up, tokens, act, slope, sems = refs[5:]

        @pl.when(pl.program_id(0) == 0)
        def _():
            assemble(tokens, refs[:5], sems)

        u = mm(tokens[...], up[...])
        square = u * u
        bend = jnp.tanh(SLOPE * u * (1.0 + CUBIC * square))
        half = 0.5 * (1.0 + bend)
        act[...] = (u * half).astype(BF)
        slope[...] = half + 0.5 * u * (1.0 - bend * bend) * SLOPE * (1.0 + 3.0 * CUBIC * square)

    part = pl.BlockSpec((4 * rows, step), lambda j: (0, j))
    return call(
        kernel,
        (hidden // step,),
        [ANY] * 5 + [pl.BlockSpec((width, step), lambda j: (0, j))],
        [pl.BlockSpec((4 * rows, width), lambda j: (0, 0)), part, part],
        [shape((4 * rows, width)), shape((4 * rows, hidden)), shape((4 * rows, hidden), F32)],
        [*pieces, weight],
        "feed_up",
        scratch=[pltpu.SemaphoreType.DMA((5,))],
        flops=8 * rows * width * hidden,
        size=2 * width * (hidden + 8 * rows),
    )


def feed_down(grad_y, slope, weight):
    tokens, width = grad_y.shape
    hidden = weight.shape[1]
    step = 256

    def kernel(dy, slope_ref, down, out):
        out[...] = (mm(dy[...], down[...]) * slope_ref[...]).astype(BF)

    part = pl.BlockSpec((tokens, step), lambda j: (0, j))
    return call(
        kernel,
        (hidden // step,),
        [whole(grad_y), part, pl.BlockSpec((width, step), lambda j: (0, j))],
        part,
        shape((tokens, hidden)),
        [grad_y, slope, weight],
        "feed_down",
        flops=2 * tokens * width * hidden,
        size=2 * width * (hidden + 8 * tokens),
    )


def softmax(scores):
    exp_terms = jnp.exp(scores - jnp.max(scores, axis=-1, keepdims=True))
    return exp_terms / jnp.sum(exp_terms, axis=-1, keepdims=True)


def score_grad(probs, grad_probs):
    return (
        probs * (grad_probs - jnp.sum(probs * grad_probs, axis=-1, keepdims=True))
    ).astype(BF)


def head(ref, k):
    return ref[:, k * HD : (k + 1) * HD]


def self_forward(projected, images):
    tokens, width = projected.shape
    rows, group = tokens // images, width // 3
    heads = group // HD

    def kernel(proj, mixed):
        for k in range(heads):
            query, key, value = (head(proj, j * heads + k) for j in range(3))
            probs = softmax(mm_t(query, key) * SCALE).astype(BF)
            mixed[:, k * HD : (k + 1) * HD] = mm(probs, value).astype(BF)

    return call(
        kernel,
        (images,),
        [pl.BlockSpec((rows, width), lambda i: (i, 0))],
        pl.BlockSpec((rows, group), lambda i: (i, 0)),
        shape((tokens, group)),
        [projected],
        "self_forward",
        flops=4 * tokens * rows * group,
    )


def self_back(projected, grad_mixed, images):
    tokens, width = projected.shape
    rows, group = tokens // images, width // 3
    heads = group // HD

    def kernel(proj, grad, out):
        for k in range(heads):
            query, key, value = (head(proj, j * heads + k) for j in range(3))
            grad_head = head(grad, k)
            probs = softmax(mm_t(query, key) * SCALE)
            grad_scores = score_grad(probs, mm_t(grad_head, value))
            parts = (
                mm(grad_scores, key) * SCALE,
                t_mm(grad_scores, query) * SCALE,
                t_mm(probs.astype(BF), grad_head),
            )
            for j, part in enumerate(parts):
                at = (j * heads + k) * HD
                out[:, at : at + HD] = part.astype(BF)

    return call(
        kernel,
        (images,),
        [
            pl.BlockSpec((rows, width), lambda i: (i, 0)),
            pl.BlockSpec((rows, group), lambda i: (i, 0)),
        ],
        pl.BlockSpec((rows, width), lambda i: (i, 0)),
        shape((tokens, width)),
        [projected, grad_mixed],
        "self_back",
        flops=10 * tokens * rows * group,
    )


def cross_forward(queries, text_kv):
    tokens, group = queries.shape
    heads = group // HD

    def kernel(query, text, mixed):
        for k in range(heads):
            probs = softmax(mm_t(head(query, k), head(text, k)) * SCALE).astype(BF)
            mixed[:, k * HD : (k + 1) * HD] = mm(probs, head(text, heads + k)).astype(BF)

    return call(
        kernel,
        (1,),
        [whole(queries), whole(text_kv)],
        whole(queries),
        shape((tokens, group)),
        [queries, text_kv],
        "cross_forward",
        flops=4 * tokens * text_kv.shape[0] * group,
    )


def cross_back(queries, text_kv, grad_mixed):
    tokens, group = queries.shape
    context = text_kv.shape[0]
    heads = group // HD

    def kernel(query, text, grad, grad_query, grad_text):
        for k in range(heads):
            query_head, key, value = head(query, k), head(text, k), head(text, heads + k)
            grad_head = head(grad, k)
            probs = softmax(mm_t(query_head, key) * SCALE)
            grad_scores = score_grad(probs, mm_t(grad_head, value))
            grad_query[:, k * HD : (k + 1) * HD] = (mm(grad_scores, key) * SCALE).astype(BF)
            at = (heads + k) * HD
            grad_text[:, k * HD : (k + 1) * HD] = t_mm(grad_scores, query_head) * SCALE
            grad_text[:, at : at + HD] = t_mm(probs.astype(BF), grad_head)

    return call(
        kernel,
        (1,),
        [whole(queries), whole(text_kv), whole(grad_mixed)],
        [whole(queries), whole(text_kv)],
        [shape((tokens, group)), shape((context, 2 * group), F32)],
        [queries, text_kv, grad_mixed],
        "cross_back",
        flops=10 * tokens * context * group,
    )


def grad_products(pairs, name, core=None, blocks=0):
    count_in = len(pairs[0][0])
    tokens, width = pairs[0][0][0].shape
    widths = [y[0].shape[1] for _, y in pairs]
    total = sum(widths)
    rows = 256 if core is None else width // (2 * blocks)
    steps = width // rows if core is None else blocks
    step = 512
    count = len(pairs) * count_in

    def kernel(r, *refs):
        out = refs[2 * count]
        offset = 0
        for k, wide in enumerate(widths):
            left = [refs[k * count_in + b][...].T for b in range(count_in)]
            for at in range(0, wide, step):
                out[:, offset + at : offset + at + step] = sum(
                    mm(left[b], refs[count + k * count_in + b][:, at : at + step])
                    for b in range(count_in)
                ).astype(BF)
            offset += wide

    pick = (lambda i, r: (0, i)) if core is None else (lambda i, r: (0, 2 * i + r[0]))
    return call(
        kernel,
        (steps,),
        [pl.BlockSpec((tokens, rows), pick)] * count
        + [pl.BlockSpec((tokens, w), lambda i, r: (0, 0)) for w in widths for _ in range(count_in)],
        pl.BlockSpec((rows, total), lambda i, r: (i, 0)),
        shape((steps * rows, total)),
        [b for x, _ in pairs for b in x] + [b for _, y in pairs for b in y],
        name,
        flops=2 * tokens * count_in * steps * rows * total,
        size=4 * width * total,
        rank=jnp.zeros((), jnp.int32) if core is None else core,
    )


def pick_weights(three, one, rank):
    rows, width = one.shape[0], one.shape[1] // 4

    def kernel(r, three_ref, one_ref, *outs):
        for k in range(4):

            @pl.when(pl.program_id(0) == k)
            def _():
                for j in range(3):
                    outs[k][:, j * width : (j + 1) * width] = three_ref[j]
                outs[k][:, 3 * width :] = one_ref[...]

    outs = [shape((rows, 4 * width))] * 4
    return call(
        kernel,
        (4,),
        [
            pl.BlockSpec((3, rows, width), lambda k, r: (0, 0, k ^ r[0])),
            pl.BlockSpec((rows, width), lambda k, r: (0, k ^ r[0])),
        ],
        [whole(a) for a in outs],
        outs,
        [three, one],
        "pick_weights",
        rank=rank,
    )


def pick_rows(arrays, rank):
    rows = arrays[0].shape[1]
    widths = [a.shape[2] for a in arrays]
    count = len(arrays)

    def kernel(r, *refs):
        for k in range(4):

            @pl.when(pl.program_id(0) == k)
            def _():
                at = 0
                for ref, width in zip(refs, widths):
                    refs[count + k][:, at : at + width] = ref[0]
                    at += width

    outs = [shape((rows, sum(widths)))] * 4
    return call(
        kernel,
        (4,),
        [pl.BlockSpec((1, rows, w), lambda k, r: (k ^ r[0], 0, 0)) for w in widths],
        [whole(a) for a in outs],
        outs,
        arrays,
        "pick_rows",
        rank=rank,
    )


def place(parts, rank):
    def kernel(r, *refs):
        for k in range(4):

            @pl.when(pl.program_id(0) == k)
            def _():
                refs[4][0] = refs[k][...]

    rows, columns = parts[0].shape
    return call(
        kernel,
        (4,),
        [whole(p) for p in parts],
        pl.BlockSpec((1, rows, columns), lambda k, r: (k ^ r[0], 0, 0)),
        shape((4, rows, columns)),
        parts,
        "place",
        rank=rank,
    )


def finish_wide(parts, rank):
    rows, total = parts[0].shape
    width = total // 2

    def kernel(r, *refs):
        for k in range(4):

            @pl.when(pl.program_id(0) == k)
            def _():
                refs[4][...] = refs[k][:, :width].astype(F32)
                refs[5][...] = refs[k][:, width:].astype(F32)

    flat = pl.BlockSpec((rows, width), lambda k, r: (0, k ^ r[0]))
    return call(
        kernel,
        (4,),
        [whole(p) for p in parts],
        [flat, flat],
        [shape((rows, 4 * width), F32)] * 2,
        parts,
        "finish_wide",
        rank=rank,
    )


def finish_all(parts, text_grad, rank):
    rows, total = parts[0].shape
    width = total // 6

    def kernel(r, *refs):
        key, value, three, out, cross, cross_out = refs[4:]
        for k in range(4):

            @pl.when(pl.program_id(0) == k)
            def _():
                def part(j):
                    return refs[k][:, j * width : (j + 1) * width].astype(F32)

                for j in range(3):
                    three[j] = part(j)
                out[...] = part(3)
                cross[0] = part(4)
                cross_out[...] = part(5)

        cross[1] = key[...]
        cross[2] = value[...]

    wide = pl.BlockSpec((3, rows, width), lambda k, r: (0, 0, k ^ r[0]))
    flat = pl.BlockSpec((rows, width), lambda k, r: (0, k ^ r[0]))
    return call(
        kernel,
        (4,),
        [whole(p) for p in parts]
        + [flat, pl.BlockSpec((rows, width), lambda k, r: (0, 4 + (k ^ r[0])))],
        [wide, flat, wide, flat],
        [shape((3, rows, 4 * width), F32), shape((rows, 4 * width), F32)] * 2,
        [*parts, text_grad, text_grad],
        "finish_all",
        rank=rank,
    )


def plane_block(k):
    return (k >> 1) & 1, (k >> 2) * 2 + (k & 1)


def text_forward(caption, w_text, w_cross):
    context, rows = caption.shape[0], w_text.shape[0]
    half, width = context // 2, w_cross.shape[2] // 4

    def kernel(cap, weight, cross, own, blocks):
        own[...] = mm_t(cap[...], weight[...]).astype(BF)
        for j in range(2):
            part = mm(own[...], cross[1 + j]).astype(BF)
            for k in range(8):
                core, group = plane_block(k)
                blocks[k, :, j * width : (j + 1) * width] = part[
                    core * half : (core + 1) * half, group * width : (group + 1) * width
                ]

    return call(
        kernel,
        (1,),
        [whole(caption), whole(w_text), whole(w_cross)],
        [
            pl.BlockSpec((context, rows), lambda i: (0, 0)),
            pl.BlockSpec((8, half, 2 * width), lambda i: (0, 0, 0)),
        ],
        [shape((context, rows)), shape((8, half, 2 * width))],
        [caption, w_text, w_cross],
        "text_forward",
    )


def text_back(blocks, own_text, w_cross, caption, w_text, extra):
    context, rows = own_text.shape
    half, width = context // 2, w_cross.shape[2] // 4
    wide = caption.shape[1] // 4
    tail = extra.shape[0]

    def kernel(block, own, cross, cap, weight, more, kv_grad, text_grad, out, grads):
        for k in range(8):
            core, group = plane_block(k)
            for j in range(2):
                at = (4 * j + group) * width
                grads[core * half : (core + 1) * half, at : at + width] = block[
                    k, :, j * width : (j + 1) * width
                ]
        kv_grad[...] = t_mm(own[...], grads[...])
        grad_text = sum(
            mm_t(grads[:, 4 * j * width : 4 * (j + 1) * width], cross[1 + j]) for j in range(2)
        ).astype(BF)
        text_grad[...] = t_mm(grad_text, cap[...])
        part = mm(grad_text, weight[...]).astype(BF)
        for k in range(8):
            core, group = plane_block(k)
            out[k, :half, :] = part[core * half : (core + 1) * half, group * wide : (group + 1) * wide]
            out[k, half:, :] = more[...]

    operands = [blocks, own_text, w_cross, caption, w_text, extra]
    outs = [
        shape((rows, 8 * width), F32),
        shape((rows, 4 * wide), F32),
        shape((8, half + tail, wide)),
    ]
    return call(
        kernel,
        (1,),
        [whole(a) for a in operands],
        [whole(a) for a in outs],
        outs,
        operands,
        "text_back",
        scratch=[pltpu.VMEM((context, 8 * width), BF)],
    )


def caption_output(blocks):
    count, half, wide = blocks.shape

    def kernel(block, out):
        out[...] = block[0].astype(F32)

    return call(
        kernel,
        (count,),
        [pl.BlockSpec((1, half, wide), lambda k: (k, 0, 0))],
        pl.BlockSpec((half, wide), lambda k: plane_block(k)),
        shape((2 * half, 4 * wide), F32),
        [blocks],
        "caption_output",
    )


def column_blocks(weight, count):
    rows = weight.shape[0]
    return weight.reshape(rows, count, -1).transpose(1, 0, 2)


def halves_of(values, width):
    high = values.astype(BF)
    low = (values - high.astype(F32)).astype(BF)
    return jnp.concatenate([high.reshape(-1, width), low.reshape(-1, width)], axis=0)


def whole_of(halves, width):
    rows = halves.shape[0] // 2
    return (halves[:rows] + halves[rows:]).reshape(-1, width)


def make_local(z_size):
    def sum_z(values):
        parts = values.reshape(z_size, -1, values.shape[-1])
        mine = trade(parts, "z").astype(F32).sum(axis=0).astype(BF)
        return spread(mine, "z", z_size).reshape(values.shape)

    def add_z(values):
        step = 1
        while step < z_size:
            values = values + lax.ppermute(
                values, "z", tuple((k, k ^ step) for k in range(z_size))
            )
            step *= 2
        return values

    def layer_order(values):
        shaped = values.reshape(values.shape[:-1] + (z_size, 2, 2, -1))
        return jnp.swapaxes(shaped, -3, -2).reshape(values.shape)

    def local(
        hidden,
        mask_index,
        mask_count,
        mask_embed,
        norm_gains,
        caption,
        w_qkv,
        w_out,
        w_cross,
        w_cross_out,
        w_text,
        w_up,
        w_down,
        cotangent,
    ):
        images, local_rows, width = hidden.shape
        full_length = mask_index.shape[1]
        rank = lax.axis_index("x") * 2 + lax.axis_index("y")
        core = lax.axis_index("c")
        tokens = images * local_rows
        group = width // 4
        text_width = caption.shape[1]

        unit = width // (4 * z_size)
        inside = unit % 128 == 0
        order = [4 * k + j for k in range(z_size) for j in (0, 2, 1, 3)] if inside else None

        def outer(values):
            return values if inside else layer_order(values)

        w_qkv, w_cross = w_qkv.transpose(1, 0, 2), w_cross.transpose(1, 0, 2)
        first = swap_parts(pick_weights(w_qkv, w_out, rank))
        first = gather_rows(place(first, rank))

        positions = lax.axis_index("y") * local_rows + jnp.arange(local_rows, dtype=jnp.int32)
        ranks = jnp.arange(full_length, dtype=jnp.int32)
        matches = (mask_index[:, :, None] == positions[None, None, :]) & (
            ranks[None, :, None] < mask_count[:, None, None]
        )
        masked = jnp.any(matches, axis=1).reshape(tokens, 1).astype(F32)
        gains = layer_order(norm_gains)
        gain_a, gain_b, gain_c = gains[:1], gains[1:2], gains[2:]
        start_x, attn_in, grad_top = start(
            outer(hidden.reshape(tokens, width)),
            outer(cotangent.reshape(tokens, width)),
            masked,
            layer_order(mask_embed)[None],
            gain_a,
            unit,
            order,
        )
        attn_in = gather_tokens(attn_in)
        mid = jnp.concatenate([column_blocks(w_cross[0], 4), column_blocks(w_cross_out, 4)], axis=2)
        up = column_blocks(w_up, 4)
        attn_in, mid, up = lax.optimization_barrier((attn_in, mid, up))
        mid, up = gather_rows(trade(mid)), gather_rows(trade(up))

        own_text, kv_part = text_forward(caption, w_text, w_cross)
        text_kv = trade(kv_part, PLANE).astype(F32).sum(axis=0).astype(BF)
        text_kv = sum_z(text_kv)
        other = swap(text_kv, "c")
        text_kv = jnp.concatenate(
            [jnp.where(core == 0, text_kv, other), jnp.where(core == 0, other, text_kv)], axis=0
        )
        attn_in, text_kv = lax.optimization_barrier((attn_in, text_kv))

        attn_in, projected = gather_mm(attn_in, first, 0, 3 * group, "qkv_mm")
        self_mixed = self_forward(projected, 2 * images)
        down = column_blocks(w_down, 4)
        self_mixed, down = lax.optimization_barrier((self_mixed, down))
        down = gather_rows(trade(down))
        parts = mm_scatter(self_mixed, first[:, 3 * group :])
        after_attn, cross_in = add_norm([start_x] + parts, gain_b)

        cross_in, cross_queries = gather_mm(gather_tokens(cross_in), mid, 0, group, "query_mm")
        cross_mixed = cross_forward(cross_queries, text_kv)
        parts = mm_scatter(cross_mixed, mid[:, group:])
        after_cross, mlp_in = add_norm([after_attn] + parts, gain_c)

        mlp_in = gather_tokens(mlp_in)
        mlp_in, grad_top = lax.optimization_barrier((mlp_in, grad_top))
        grad_y = jnp.concatenate(gather_tokens(grad_top), axis=0)
        mlp_in, activated, slope = feed_up(mlp_in, up)
        early = [attn_in, self_mixed, cross_in, cross_mixed]
        if inside:
            grad_axes, halves = "z", (core, z_size)

            def both(values):
                return [values, swap(values, "c")]

        else:
            grad_axes, halves = DATA, ()

            def both(values):
                return [values]

        early = [both(values) for values in early]
        down_part = grad_products([(both(grad_y), both(activated))], "down_grads", *halves)
        mlp_in = both(mlp_in)
        slope, down_part, early, mlp_in = lax.optimization_barrier((slope, down_part, early, mlp_in))
        down_rows = scatter_grad(down_part, grad_axes)
        grad_pre = feed_down(grad_y, slope, down)
        parts = mm_scatter(grad_pre, up)
        up_part = grad_products([(mlp_in, both(grad_pre))], "up_grads", *halves)
        grad_after_cross, cross_branch, gain_grad_c = norm_back(
            parts, grad_top, after_cross, gain_c
        )

        cross_branch = gather_tokens(cross_branch)
        cross_branch, up_part = lax.optimization_barrier((cross_branch, up_part))
        cross_branch, grad_cross_mixed = gather_mm(
            cross_branch, mid, group, group, "cross_out_back"
        )
        grad_cq, kv_grad = cross_back(cross_queries, text_kv, grad_cross_mixed)
        up_part, down_rows, kv_grad = lax.optimization_barrier((up_part, down_rows, kv_grad))
        up_rows = scatter_grad(up_part, grad_axes)
        cross_branch, grad_cq_both = both(cross_branch), both(grad_cq)
        parts = mm_scatter(grad_cq, mid[:, :group])
        grad_after_attn, attn_branch, gain_grad_b = norm_back(
            parts, grad_after_cross, after_attn, gain_b
        )

        attn_branch, grad_self_mixed = gather_mm(
            gather_tokens(attn_branch), first, 3 * group, group, "out_back"
        )
        grad_projected = self_back(projected, grad_self_mixed, 2 * images)
        rest_part = grad_products(
            [
                (early[0], both(grad_projected)),
                (both(attn_branch), early[1]),
                (early[2], grad_cq_both),
                (cross_branch, early[3]),
            ],
            "attention_grads",
            *halves,
        )
        grad_projected, activated, kv_grad, rest_part = lax.optimization_barrier(
            (grad_projected, activated, kv_grad, rest_part)
        )
        rest_part, up_rows = lax.optimization_barrier((rest_part, up_rows))
        rest_rows = scatter_grad(rest_part, grad_axes)
        parts = mm_scatter(grad_projected, first[:, : 3 * group])
        grad_hidden, gain_grad_a, mask_grad = last_back(
            parts,
            grad_after_attn,
            start_x,
            gain_a,
            masked,
            unit,
            order,
        )
        sums = jnp.concatenate([gain_grad_a, gain_grad_b, gain_grad_c, mask_grad], axis=0)

        parts = mm_scatter(activated, down)
        output = layer_output(after_cross, parts, unit, order)

        kv_halves = kv_grad.reshape(2, -1, 2 * group)
        kv_keep = lax.dynamic_index_in_dim(kv_halves, core, 0, keepdims=False)
        kv_send = lax.dynamic_index_in_dim(kv_halves, 1 - core, 0, keepdims=False)
        kv_sum = sum_z((kv_keep + swap(kv_send, "c")).astype(BF))
        wide_rows = swap_parts(pick_rows([down_rows, up_rows], rank))
        kv_sum, wide_rows = lax.optimization_barrier((kv_sum, wide_rows))
        kv_grads = spread(kv_sum, PLANE, 8)
        down_grad, up_grad = finish_wide(wide_rows, rank)
        kv_weight_grad, grad_text_w, caption_part = text_back(
            kv_grads, own_text, w_cross, caption, w_text, halves_of(sums, text_width // 4)
        )
        half_context = caption.shape[0] // 2
        caption_part = trade(caption_part, PLANE).astype(F32).sum(axis=0)
        sums = layer_order(add_z(whole_of(caption_part[half_context:], width)))
        caption_part = sum_z(caption_part[:half_context].astype(BF))
        caption_part, rest_rows = lax.optimization_barrier((caption_part, rest_rows))
        grad_caption = caption_output(spread(caption_part, PLANE, 8))

        qkv_grad, out_grad, grad_cross, cross_out_grad = finish_all(
            swap_parts(pick_rows([rest_rows], rank)), kv_weight_grad, rank
        )
        return (
            outer(output).reshape(hidden.shape),
            outer(grad_hidden).reshape(hidden.shape),
            grad_caption,
            sums[:3],
            sums[3],
            qkv_grad.transpose(1, 0, 2),
            out_grad,
            grad_cross.transpose(1, 0, 2),
            cross_out_grad,
            grad_text_w,
            up_grad,
            down_grad,
        )

    return local


def solution(mesh):
    z_size = mesh.shape["img"] // 4
    inner = Mesh(mesh.devices.reshape(z_size, 2, 2, 2), ("z", "x", "c", "y"))
    image = ("z", "x", "c")
    tokens = P(image, "y", None)
    rows = P(image + ("y",))
    in_specs = (tokens, P(image, None), P(image), P(), P(), P()) + (rows,) * 7 + (tokens,)
    out_specs = (tokens, tokens, P(), P(), P()) + (rows,) * 7
    return jax.shard_map(
        make_local(z_size), mesh=inner, in_specs=in_specs, out_specs=out_specs, check_vma=False
    )
```

```python
import math

import jax
import jax.numpy as jnp
from jax import lax
from jax.experimental import pallas as pl
from jax.experimental.pallas import tpu as pltpu
from jax.sharding import Mesh
from jax.sharding import PartitionSpec as P

HD = 128
EPS = 1e-05
BF = jnp.bfloat16
F32 = jnp.float32
PAIR = ((0, 1), (1, 0))
GROUP = ("x", "y")
DATA = ("z", "c")
PLANE = ("x", "c", "y")
VMEM = 48 * 1024 * 1024
SCALE = 1.0 / math.sqrt(HD)
SLOPE = math.sqrt(2.0 / math.pi)
CUBIC = 0.044715


def dot(a, b, dims):
    return lax.dot_general(a, b, (dims, ((), ())), preferred_element_type=F32)


def mm(a, b):
    return dot(a, b, ((1,), (0,)))


def mm_t(a, b):
    return dot(a, b, ((1,), (1,)))


def t_mm(a, b):
    return dot(a, b, ((0,), (0,)))


def shape(dims, dtype=BF):
    return jax.ShapeDtypeStruct(dims, dtype)


def swap(values, axis):
    return lax.ppermute(values, axis, PAIR)


def trade(blocks, axes=GROUP):
    return lax.all_to_all(blocks, axes, 0, 0, tiled=True)


def spread(values, axes=GROUP, count=4):
    return trade(jnp.broadcast_to(values[None], (count,) + values.shape), axes)


def gather_tokens(own):
    half = own.shape[0] // 2
    from_x = swap(own, "x")
    from_y = swap(own, "y")
    return own, from_y, from_x, swap(from_x[:half], "y"), swap(from_y[half:], "x")


def scatter_tokens(parts):
    own, for_y, for_x, for_low, for_high = parts
    half = for_low.shape[0]
    low = swap(for_low, "y").astype(F32) + for_x[:half].astype(F32)
    high = swap(for_high, "x").astype(F32) + for_y[half:].astype(F32)
    from_x = swap(jnp.concatenate([low.astype(BF), for_x[half:]], axis=0), "x")
    from_y = swap(jnp.concatenate([for_y[:half], high.astype(BF)], axis=0), "y")
    return [own, from_x, from_y]


def swap_parts(parts):
    return [
        parts[0],
        swap(parts[1], "y"),
        swap(parts[2], "x"),
        lax.ppermute(parts[3], GROUP, ((0, 3), (1, 2), (2, 1), (3, 0))),
    ]


def gather_rows(rows):
    return lax.all_gather(rows.reshape(-1, rows.shape[-1]), DATA, axis=0, tiled=True)


def scatter_grad(partial, axes):
    summed = lax.psum_scatter(partial, axes, scatter_dimension=0, tiled=True)
    return summed.reshape(4, -1, summed.shape[-1])


def call(kernel, grid, in_specs, out_specs, out_shape, operands, name, flops=0, size=1 << 22,
         rank=None, scratch=(), aliases=None):
    options = dict(
        input_output_aliases=aliases or {},
        out_shape=out_shape,
        compiler_params=pltpu.CompilerParams(vmem_limit_bytes=VMEM),
        cost_estimate=pl.CostEstimate(flops=flops, bytes_accessed=size, transcendentals=0),
        name=name,
    )
    if rank is None:
        return pl.pallas_call(
            kernel, grid=grid, in_specs=in_specs, out_specs=out_specs, scratch_shapes=scratch,
            **options,
        )(*operands)
    spec = pltpu.PrefetchScalarGridSpec(
        num_scalar_prefetch=1,
        grid=grid,
        in_specs=in_specs,
        out_specs=out_specs,
        scratch_shapes=scratch,
    )
    return pl.pallas_call(kernel, grid_spec=spec, **options)(rank.reshape(1), *operands)


def whole(array):
    return pl.BlockSpec(array.shape, lambda *_: (0,) * len(array.shape))


def reorder(values, unit, order):
    if order is None:
        return values
    return jnp.concatenate([values[:, k * unit : (k + 1) * unit] for k in order], axis=1)


def assemble(target, pieces, sems):
    copies, at = [], 0
    for k, piece in enumerate(pieces):
        rows = piece.shape[0]
        copies.append(pltpu.make_async_copy(piece, target.at[at : at + rows], sems.at[k]))
        at += rows
    for copy in copies:
        copy.start()
    for copy in copies:
        copy.wait()


ANY = pl.BlockSpec(memory_space=pl.ANY)


def gather_mm(pieces, weight, first, columns, name):
    rows, width = pieces[0].shape
    step = 256

    def kernel(*refs):
        tokens, out, sems = refs[6:]

        @pl.when(pl.program_id(0) == 0)
        def _():
            assemble(tokens, refs[:5], sems)

        out[...] = mm(tokens[...], refs[5][...]).astype(BF)

    return call(
        kernel,
        (columns // step,),
        [ANY] * 5 + [pl.BlockSpec((width, step), lambda j: (0, first // step + j))],
        [
            pl.BlockSpec((4 * rows, width), lambda j: (0, 0)),
            pl.BlockSpec((4 * rows, step), lambda j: (0, j)),
        ],
        [shape((4 * rows, width)), shape((4 * rows, columns))],
        [*pieces, weight],
        name,
        flops=8 * rows * width * columns,
        size=2 * width * (columns + 8 * rows),
        scratch=[pltpu.SemaphoreType.DMA((5,))],
    )


def mm_scatter(values, weight):
    return scatter_partial(mm_t(values, weight).astype(BF))


def scatter_partial(partial):
    rows = partial.shape[0] // 4
    cuts = [0, rows, 2 * rows, 3 * rows, 3 * rows + rows // 2, 4 * rows]
    return scatter_tokens([partial[a:b] for a, b in zip(cuts, cuts[1:])])


def normalize(values):
    centred = values - jnp.mean(values, axis=-1, keepdims=True)
    inv_std = lax.rsqrt(jnp.mean(centred * centred, axis=-1, keepdims=True) + EPS)
    return centred * inv_std, inv_std


NORM_ROWS = 32


def row_spec(array, at=None):
    width = array.shape[-1]
    if at is None:
        return pl.BlockSpec((NORM_ROWS, width), lambda i: (i, 0))
    return pl.BlockSpec((1, NORM_ROWS, width), lambda i, at=at: (at, i, 0))


def terms_of(terms):
    arrays, specs = [], []
    for term in terms:
        array, at = term if isinstance(term, tuple) else (term, None)
        arrays.append(array)
        specs.append(row_spec(array, at))
    return arrays, specs


def total_of(refs):
    values = [ref[0] if len(ref.shape) == 3 else ref[...] for ref in refs]
    return sum(value.astype(F32) for value in values)


def add_norm(terms, gain):
    arrays, specs = terms_of(terms)
    tokens, width = arrays[0].shape[-2], arrays[0].shape[-1]
    tokens = min(a.shape[-2] for a in arrays)

    def kernel(*refs):
        gain_ref, x, out = refs[-3:]
        values = total_of(refs[:-3])
        x[...] = values
        out[...] = (normalize(values)[0] * gain_ref[...]).astype(BF)

    return call(
        kernel,
        (tokens // NORM_ROWS,),
        specs + [whole(gain)],
        [row_spec(shape((tokens, width)))] * 2,
        [shape((tokens, width), F32), shape((tokens, width))],
        [*arrays, gain],
        "add_norm",
    )


def norm_grad(grad, values, gain):
    normed, inv_std = normalize(values)
    scaled = grad * gain
    first_mean = jnp.mean(scaled, axis=-1, keepdims=True)
    second_mean = jnp.mean(scaled * normed, axis=-1, keepdims=True)
    return (
        inv_std * (scaled - first_mean - normed * second_mean),
        jnp.sum(grad * normed, axis=0, keepdims=True),
    )


def accumulate(ref, value):
    @pl.when(pl.program_id(0) == 0)
    def _():
        ref[...] = jnp.zeros_like(ref)

    ref[...] += value


def norm_back(terms, upper, values, gain):
    arrays, specs = terms_of(terms)
    tokens, width = values.shape

    def kernel(*refs):
        upper_ref, x, gain_ref, out, out_low, gain_grad = refs[-6:]
        back, part = norm_grad(total_of(refs[:-6]), x[...], gain_ref[...])
        result = upper_ref[...].astype(F32) + back
        out[...] = result
        out_low[...] = result.astype(BF)
        accumulate(gain_grad, part)

    return call(
        kernel,
        (tokens // NORM_ROWS,),
        specs + [row_spec(upper), row_spec(values), whole(gain)],
        [row_spec(values)] * 2 + [pl.BlockSpec((1, width), lambda i: (0, 0))],
        [shape((tokens, width), F32), shape((tokens, width)), shape((1, width), F32)],
        [*arrays, upper, values, gain],
        "norm_back",
    )


def last_back(terms, upper, values, gain, masked, unit, order):
    arrays, specs = terms_of(terms)
    tokens, width = values.shape

    def kernel(*refs):
        upper_ref, x, gain_ref, mask, out, gain_grad, mask_grad = refs[-7:]
        back, part = norm_grad(total_of(refs[:-7]), x[...], gain_ref[...])
        result = upper_ref[...].astype(F32) + back
        hit = mask[...] > 0.5
        out[...] = reorder(jnp.where(hit, 0.0, result).astype(BF), unit, order)
        accumulate(gain_grad, part)
        accumulate(mask_grad, jnp.sum(jnp.where(hit, result, 0.0), axis=0, keepdims=True))

    line = pl.BlockSpec((1, width), lambda i: (0, 0))
    return call(
        kernel,
        (tokens // NORM_ROWS,),
        specs + [row_spec(upper), row_spec(values), whole(gain), row_spec(masked)],
        [row_spec(values), line, line],
        [shape((tokens, width)), shape((1, width), F32), shape((1, width), F32)],
        [*arrays, upper, values, gain, masked],
        "last_back",
    )


def start(hidden, cotangent, masked, embed, gain, unit, order):
    tokens, width = hidden.shape

    def kernel(hid, cot, mask, embed_ref, gain_ref, x, out, grad):
        hit = mask[...] > 0.5
        values = jnp.where(
            hit, embed_ref[...], reorder(hid[...], unit, order).astype(F32)
        )
        x[...] = values
        out[...] = (normalize(values)[0] * gain_ref[...]).astype(BF)
        grad[...] = jnp.where(hit, reorder(cot[...], unit, order).astype(F32), 0.0).astype(BF)

    rows = row_spec(hidden)
    return call(
        kernel,
        (tokens // NORM_ROWS,),
        [rows, rows, row_spec(masked), whole(embed), whole(gain)],
        [rows] * 3,
        [shape((tokens, width), F32), shape((tokens, width)), shape((tokens, width))],
        [hidden, cotangent, masked, embed, gain],
        "start",
    )


def layer_output(upper, terms, unit, order):
    arrays, specs = terms_of(terms)
    tokens, width = upper.shape

    def kernel(*refs):
        values = refs[-2][...] + total_of(refs[:-2])
        refs[-1][...] = reorder(values.astype(BF), unit, order)

    return call(
        kernel,
        (tokens // NORM_ROWS,),
        specs + [row_spec(upper)],
        row_spec(upper),
        shape((tokens, width)),
        [*arrays, upper],
        "layer_output",
    )


def feed_up(pieces, weight):
    rows, width = pieces[0].shape
    hidden = weight.shape[1]
    step = 256

    def kernel(*refs):
        up, tokens, act, slope, sems = refs[5:]

        @pl.when(pl.program_id(0) == 0)
        def _():
            assemble(tokens, refs[:5], sems)

        u = mm(tokens[...], up[...])
        square = u * u
        bend = jnp.tanh(SLOPE * u * (1.0 + CUBIC * square))
        half = 0.5 * (1.0 + bend)
        act[...] = (u * half).astype(BF)
        slope[...] = half + 0.5 * u * (1.0 - bend * bend) * SLOPE * (1.0 + 3.0 * CUBIC * square)

    part = pl.BlockSpec((4 * rows, step), lambda j: (0, j))
    return call(
        kernel,
        (hidden // step,),
        [ANY] * 5 + [pl.BlockSpec((width, step), lambda j: (0, j))],
        [pl.BlockSpec((4 * rows, width), lambda j: (0, 0)), part, part],
        [shape((4 * rows, width)), shape((4 * rows, hidden)), shape((4 * rows, hidden), F32)],
        [*pieces, weight],
        "feed_up",
        scratch=[pltpu.SemaphoreType.DMA((5,))],
        flops=8 * rows * width * hidden,
        size=2 * width * (hidden + 8 * rows),
    )


def feed_down(grad_y, slope, weight):
    tokens, width = grad_y.shape
    hidden = weight.shape[1]
    step = 256

    def kernel(dy, slope_ref, down, out):
        out[...] = (mm(dy[...], down[...]) * slope_ref[...]).astype(BF)

    part = pl.BlockSpec((tokens, step), lambda j: (0, j))
    return call(
        kernel,
        (hidden // step,),
        [whole(grad_y), part, pl.BlockSpec((width, step), lambda j: (0, j))],
        part,
        shape((tokens, hidden)),
        [grad_y, slope, weight],
        "feed_down",
        flops=2 * tokens * width * hidden,
        size=2 * width * (hidden + 8 * tokens),
    )


def softmax(scores):
    exp_terms = jnp.exp(scores - jnp.max(scores, axis=-1, keepdims=True))
    return exp_terms / jnp.sum(exp_terms, axis=-1, keepdims=True)


def score_grad(probs, grad_probs):
    return (
        probs * (grad_probs - jnp.sum(probs * grad_probs, axis=-1, keepdims=True))
    ).astype(BF)


def head(ref, k):
    return ref[:, k * HD : (k + 1) * HD]


def self_forward(projected, images):
    tokens, width = projected.shape
    rows, group = tokens // images, width // 3
    heads = group // HD

    def kernel(proj, mixed):
        for k in range(heads):
            query, key, value = (head(proj, j * heads + k) for j in range(3))
            probs = softmax(mm_t(query, key) * SCALE).astype(BF)
            mixed[:, k * HD : (k + 1) * HD] = mm(probs, value).astype(BF)

    return call(
        kernel,
        (images,),
        [pl.BlockSpec((rows, width), lambda i: (i, 0))],
        pl.BlockSpec((rows, group), lambda i: (i, 0)),
        shape((tokens, group)),
        [projected],
        "self_forward",
        flops=4 * tokens * rows * group,
    )


def self_back(projected, grad_mixed, images):
    tokens, width = projected.shape
    rows, group = tokens // images, width // 3
    heads = group // HD

    def kernel(proj, grad, out):
        for k in range(heads):
            query, key, value = (head(proj, j * heads + k) for j in range(3))
            grad_head = head(grad, k)
            probs = softmax(mm_t(query, key) * SCALE)
            grad_scores = score_grad(probs, mm_t(grad_head, value))
            parts = (
                mm(grad_scores, key) * SCALE,
                t_mm(grad_scores, query) * SCALE,
                t_mm(probs.astype(BF), grad_head),
            )
            for j, part in enumerate(parts):
                at = (j * heads + k) * HD
                out[:, at : at + HD] = part.astype(BF)

    return call(
        kernel,
        (images,),
        [
            pl.BlockSpec((rows, width), lambda i: (i, 0)),
            pl.BlockSpec((rows, group), lambda i: (i, 0)),
        ],
        pl.BlockSpec((rows, width), lambda i: (i, 0)),
        shape((tokens, width)),
        [projected, grad_mixed],
        "self_back",
        flops=10 * tokens * rows * group,
    )


def cross_forward(queries, text_kv):
    tokens, group = queries.shape
    heads = group // HD

    def kernel(query, text, mixed):
        for k in range(heads):
            probs = softmax(mm_t(head(query, k), head(text, k)) * SCALE).astype(BF)
            mixed[:, k * HD : (k + 1) * HD] = mm(probs, head(text, heads + k)).astype(BF)

    return call(
        kernel,
        (1,),
        [whole(queries), whole(text_kv)],
        whole(queries),
        shape((tokens, group)),
        [queries, text_kv],
        "cross_forward",
        flops=4 * tokens * text_kv.shape[0] * group,
    )


def cross_back(queries, text_kv, grad_mixed):
    tokens, group = queries.shape
    context = text_kv.shape[0]
    heads = group // HD

    def kernel(query, text, grad, grad_query, grad_text):
        for k in range(heads):
            query_head, key, value = head(query, k), head(text, k), head(text, heads + k)
            grad_head = head(grad, k)
            probs = softmax(mm_t(query_head, key) * SCALE)
            grad_scores = score_grad(probs, mm_t(grad_head, value))
            grad_query[:, k * HD : (k + 1) * HD] = (mm(grad_scores, key) * SCALE).astype(BF)
            at = (heads + k) * HD
            grad_text[:, k * HD : (k + 1) * HD] = t_mm(grad_scores, query_head) * SCALE
            grad_text[:, at : at + HD] = t_mm(probs.astype(BF), grad_head)

    return call(
        kernel,
        (1,),
        [whole(queries), whole(text_kv), whole(grad_mixed)],
        [whole(queries), whole(text_kv)],
        [shape((tokens, group)), shape((context, 2 * group), F32)],
        [queries, text_kv, grad_mixed],
        "cross_back",
        flops=10 * tokens * context * group,
    )


def grad_products(pairs, name, core=None, blocks=0, columns=0, first=0, into=None):
    count_in = len(pairs[0][0])
    tokens, width = pairs[0][0][0].shape
    widths = [y[0].shape[1] for _, y in pairs]
    total = sum(widths)
    rows = 256 if core is None else width // (2 * blocks)
    steps = width // rows if core is None else blocks
    step = 512
    count = len(pairs) * count_in
    columns = columns or total
    extra = [] if into is None else [into]

    def kernel(r, *refs):
        out = refs[-1]
        offset = 0
        for k, wide in enumerate(widths):
            left = [refs[k * count_in + b][...].T for b in range(count_in)]
            for at in range(0, wide, step):
                out[:, offset + at : offset + at + step] = sum(
                    mm(left[b], refs[count + k * count_in + b][:, at : at + step])
                    for b in range(count_in)
                ).astype(BF)
            offset += wide

    pick = (lambda i, r: (0, i)) if core is None else (lambda i, r: (0, 2 * i + r[0]))
    return call(
        kernel,
        (steps,),
        [pl.BlockSpec((tokens, rows), pick)] * count
        + [pl.BlockSpec((tokens, w), lambda i, r: (0, 0)) for w in widths for _ in range(count_in)]
        + [ANY] * len(extra),
        pl.BlockSpec((rows, total), lambda i, r: (i, first // total)),
        shape((steps * rows, columns)),
        [b for x, _ in pairs for b in x] + [b for _, y in pairs for b in y] + extra,
        name,
        aliases={1 + 2 * count: 0} if extra else {},
        flops=2 * tokens * count_in * steps * rows * total,
        size=4 * width * total,
        rank=jnp.zeros((), jnp.int32) if core is None else core,
    )


def pick_weights(three, one, rank):
    rows, width = one.shape[0], one.shape[1] // 4

    def kernel(r, three_ref, one_ref, *outs):
        for k in range(4):

            @pl.when(pl.program_id(0) == k)
            def _():
                for j in range(3):
                    outs[k][:, j * width : (j + 1) * width] = three_ref[j]
                outs[k][:, 3 * width :] = one_ref[...]

    outs = [shape((rows, 4 * width))] * 4
    return call(
        kernel,
        (4,),
        [
            pl.BlockSpec((3, rows, width), lambda k, r: (0, 0, k ^ r[0])),
            pl.BlockSpec((rows, width), lambda k, r: (0, k ^ r[0])),
        ],
        [whole(a) for a in outs],
        outs,
        [three, one],
        "pick_weights",
        rank=rank,
    )


def pick_rows(arrays, rank):
    rows = arrays[0].shape[1]
    widths = [a.shape[2] for a in arrays]
    count = len(arrays)

    def kernel(r, *refs):
        for k in range(4):

            @pl.when(pl.program_id(0) == k)
            def _():
                at = 0
                for ref, width in zip(refs, widths):
                    refs[count + k][:, at : at + width] = ref[0]
                    at += width

    outs = [shape((rows, sum(widths)))] * 4
    return call(
        kernel,
        (4,),
        [pl.BlockSpec((1, rows, w), lambda k, r: (k ^ r[0], 0, 0)) for w in widths],
        [whole(a) for a in outs],
        outs,
        arrays,
        "pick_rows",
        rank=rank,
    )


def place(parts, rank):
    def kernel(r, *refs):
        for k in range(4):

            @pl.when(pl.program_id(0) == k)
            def _():
                refs[4][0] = refs[k][...]

    rows, columns = parts[0].shape
    return call(
        kernel,
        (4,),
        [whole(p) for p in parts],
        pl.BlockSpec((1, rows, columns), lambda k, r: (k ^ r[0], 0, 0)),
        shape((4, rows, columns)),
        parts,
        "place",
        rank=rank,
    )


def finish_wide(parts, rank):
    rows, total = parts[0].shape
    width = total // 2

    def kernel(r, *refs):
        for k in range(4):

            @pl.when(pl.program_id(0) == k)
            def _():
                refs[4][...] = refs[k][:, :width].astype(F32)
                refs[5][...] = refs[k][:, width:].astype(F32)

    flat = pl.BlockSpec((rows, width), lambda k, r: (0, k ^ r[0]))
    return call(
        kernel,
        (4,),
        [whole(p) for p in parts],
        [flat, flat],
        [shape((rows, 4 * width), F32)] * 2,
        parts,
        "finish_wide",
        rank=rank,
    )


def finish_all(parts, text_grad, rank):
    rows, total = parts[0].shape
    width = total // 6

    def kernel(r, *refs):
        key, value, three, out, cross, cross_out = refs[4:]
        for k in range(4):

            @pl.when(pl.program_id(0) == k)
            def _():
                def part(j):
                    return refs[k][:, j * width : (j + 1) * width].astype(F32)

                for j in range(3):
                    three[j] = part(j)
                out[...] = part(3)
                cross[0] = part(4)
                cross_out[...] = part(5)

        cross[1] = key[...]
        cross[2] = value[...]

    wide = pl.BlockSpec((3, rows, width), lambda k, r: (0, 0, k ^ r[0]))
    flat = pl.BlockSpec((rows, width), lambda k, r: (0, k ^ r[0]))
    return call(
        kernel,
        (4,),
        [whole(p) for p in parts]
        + [flat, pl.BlockSpec((rows, width), lambda k, r: (0, 4 + (k ^ r[0])))],
        [wide, flat, wide, flat],
        [shape((3, rows, 4 * width), F32), shape((rows, 4 * width), F32)] * 2,
        [*parts, text_grad, text_grad],
        "finish_all",
        rank=rank,
    )


def plane_block(k):
    return (k >> 1) & 1, (k >> 2) * 2 + (k & 1)


def text_forward(caption, w_text, w_cross):
    context, rows = caption.shape[0], w_text.shape[0]
    half, width = context // 2, w_cross.shape[2] // 4

    def kernel(cap, weight, cross, own, blocks):
        own[...] = mm_t(cap[...], weight[...]).astype(BF)
        for j in range(2):
            part = mm(own[...], cross[1 + j]).astype(BF)
            for k in range(8):
                core, group = plane_block(k)
                blocks[k, :, j * width : (j + 1) * width] = part[
                    core * half : (core + 1) * half, group * width : (group + 1) * width
                ]

    return call(
        kernel,
        (1,),
        [whole(caption), whole(w_text), whole(w_cross)],
        [
            pl.BlockSpec((context, rows), lambda i: (0, 0)),
            pl.BlockSpec((8, half, 2 * width), lambda i: (0, 0, 0)),
        ],
        [shape((context, rows)), shape((8, half, 2 * width))],
        [caption, w_text, w_cross],
        "text_forward",
    )


def text_back(blocks, own_text, w_cross, caption, w_text, extra):
    context, rows = own_text.shape
    half, width = context // 2, w_cross.shape[2] // 4
    wide = caption.shape[1] // 4
    tail = extra.shape[0]

    def kernel(block, own, cross, cap, weight, more, kv_grad, text_grad, out, grads):
        for k in range(8):
            core, group = plane_block(k)
            for j in range(2):
                at = (4 * j + group) * width
                grads[core * half : (core + 1) * half, at : at + width] = block[
                    k, :, j * width : (j + 1) * width
                ]
        kv_grad[...] = t_mm(own[...], grads[...])
        grad_text = sum(
            mm_t(grads[:, 4 * j * width : 4 * (j + 1) * width], cross[1 + j]) for j in range(2)
        ).astype(BF)
        text_grad[...] = t_mm(grad_text, cap[...])
        part = mm(grad_text, weight[...]).astype(BF)
        for k in range(8):
            core, group = plane_block(k)
            out[k, :half, :] = part[core * half : (core + 1) * half, group * wide : (group + 1) * wide]
            out[k, half:, :] = more[...]

    operands = [blocks, own_text, w_cross, caption, w_text, extra]
    outs = [
        shape((rows, 8 * width), F32),
        shape((rows, 4 * wide), F32),
        shape((8, half + tail, wide)),
    ]
    return call(
        kernel,
        (1,),
        [whole(a) for a in operands],
        [whole(a) for a in outs],
        outs,
        operands,
        "text_back",
        scratch=[pltpu.VMEM((context, 8 * width), BF)],
    )


def caption_output(blocks):
    count, half, wide = blocks.shape

    def kernel(block, out):
        out[...] = block[0].astype(F32)

    return call(
        kernel,
        (count,),
        [pl.BlockSpec((1, half, wide), lambda k: (k, 0, 0))],
        pl.BlockSpec((half, wide), lambda k: plane_block(k)),
        shape((2 * half, 4 * wide), F32),
        [blocks],
        "caption_output",
    )


def column_blocks(weight, count):
    rows = weight.shape[0]
    return weight.reshape(rows, count, -1).transpose(1, 0, 2)


def halves_of(values, width):
    high = values.astype(BF)
    low = (values - high.astype(F32)).astype(BF)
    return jnp.concatenate([high.reshape(-1, width), low.reshape(-1, width)], axis=0)


def whole_of(halves, width):
    rows = halves.shape[0] // 2
    return (halves[:rows] + halves[rows:]).reshape(-1, width)


def make_local(z_size):
    def sum_z(values):
        parts = values.reshape(z_size, -1, values.shape[-1])
        mine = trade(parts, "z").astype(F32).sum(axis=0).astype(BF)
        return spread(mine, "z", z_size).reshape(values.shape)

    def add_z(values):
        step = 1
        while step < z_size:
            values = values + lax.ppermute(
                values, "z", tuple((k, k ^ step) for k in range(z_size))
            )
            step *= 2
        return values

    def layer_order(values):
        shaped = values.reshape(values.shape[:-1] + (z_size, 2, 2, -1))
        return jnp.swapaxes(shaped, -3, -2).reshape(values.shape)

    def local(
        hidden,
        mask_index,
        mask_count,
        mask_embed,
        norm_gains,
        caption,
        w_qkv,
        w_out,
        w_cross,
        w_cross_out,
        w_text,
        w_up,
        w_down,
        cotangent,
    ):
        images, local_rows, width = hidden.shape
        full_length = mask_index.shape[1]
        rank = lax.axis_index("x") * 2 + lax.axis_index("y")
        core = lax.axis_index("c")
        tokens = images * local_rows
        group = width // 4
        text_width = caption.shape[1]

        unit = width // (4 * z_size)
        inside = unit % 128 == 0
        order = [4 * k + j for k in range(z_size) for j in (0, 2, 1, 3)] if inside else None

        def outer(values):
            return values if inside else layer_order(values)

        w_qkv, w_cross = w_qkv.transpose(1, 0, 2), w_cross.transpose(1, 0, 2)
        first = swap_parts(pick_weights(w_qkv, w_out, rank))
        first = gather_rows(place(first, rank))

        positions = lax.axis_index("y") * local_rows + jnp.arange(local_rows, dtype=jnp.int32)
        ranks = jnp.arange(full_length, dtype=jnp.int32)
        matches = (mask_index[:, :, None] == positions[None, None, :]) & (
            ranks[None, :, None] < mask_count[:, None, None]
        )
        masked = jnp.any(matches, axis=1).reshape(tokens, 1).astype(F32)
        gains = layer_order(norm_gains)
        gain_a, gain_b, gain_c = gains[:1], gains[1:2], gains[2:]
        start_x, attn_in, grad_top = start(
            outer(hidden.reshape(tokens, width)),
            outer(cotangent.reshape(tokens, width)),
            masked,
            layer_order(mask_embed)[None],
            gain_a,
            unit,
            order,
        )
        attn_in = gather_tokens(attn_in)
        mid = jnp.concatenate([column_blocks(w_cross[0], 4), column_blocks(w_cross_out, 4)], axis=2)
        up = column_blocks(w_up, 4)
        attn_in, mid, up = lax.optimization_barrier((attn_in, mid, up))
        mid, up = gather_rows(trade(mid)), gather_rows(trade(up))

        own_text, kv_part = text_forward(caption, w_text, w_cross)
        text_kv = trade(kv_part, PLANE).astype(F32).sum(axis=0).astype(BF)
        text_kv = sum_z(text_kv)
        other = swap(text_kv, "c")
        text_kv = jnp.concatenate(
            [jnp.where(core == 0, text_kv, other), jnp.where(core == 0, other, text_kv)], axis=0
        )
        attn_in, text_kv = lax.optimization_barrier((attn_in, text_kv))

        attn_in, projected = gather_mm(attn_in, first, 0, 3 * group, "qkv_mm")
        self_mixed = self_forward(projected, 2 * images)
        down = column_blocks(w_down, 4)
        self_mixed, down = lax.optimization_barrier((self_mixed, down))
        down = gather_rows(trade(down))
        parts = mm_scatter(self_mixed, first[:, 3 * group :])
        after_attn, cross_in = add_norm([start_x] + parts, gain_b)

        cross_in, cross_queries = gather_mm(gather_tokens(cross_in), mid, 0, group, "query_mm")
        cross_mixed = cross_forward(cross_queries, text_kv)
        parts = mm_scatter(cross_mixed, mid[:, group:])
        after_cross, mlp_in = add_norm([after_attn] + parts, gain_c)

        mlp_in = gather_tokens(mlp_in)
        mlp_in, grad_top = lax.optimization_barrier((mlp_in, grad_top))
        grad_y = jnp.concatenate(gather_tokens(grad_top), axis=0)
        mlp_in, activated, slope = feed_up(mlp_in, up)
        early = [attn_in, self_mixed, cross_in, cross_mixed]
        if inside:
            grad_axes, halves = "z", (core, z_size)

            def both(values):
                return [values, swap(values, "c")]

        else:
            grad_axes, halves = DATA, ()

            def both(values):
                return [values]

        early = [both(values) for values in early]
        down_part = grad_products([(both(grad_y), both(activated))], "down_grads", *halves)
        mlp_in = both(mlp_in)
        slope, down_part, early, mlp_in = lax.optimization_barrier((slope, down_part, early, mlp_in))
        down_rows = scatter_grad(down_part, grad_axes)
        grad_pre = feed_down(grad_y, slope, down)
        parts = mm_scatter(grad_pre, up)
        up_part = grad_products([(mlp_in, both(grad_pre))], "up_grads", *halves)
        grad_after_cross, cross_branch, gain_grad_c = norm_back(
            parts, grad_top, after_cross, gain_c
        )

        cross_branch = gather_tokens(cross_branch)
        activated, cross_own = lax.optimization_barrier((activated, cross_branch[0]))
        result = mm_t(activated, down).astype(BF)
        cross_branch, up_part, result = lax.optimization_barrier(
            ((cross_own,) + cross_branch[1:], up_part, result)
        )
        result = scatter_partial(result)
        cross_branch, grad_cross_mixed = gather_mm(
            cross_branch, mid, group, group, "cross_out_back"
        )
        grad_cq, kv_grad = cross_back(cross_queries, text_kv, grad_cross_mixed)
        up_part, down_rows, kv_grad = lax.optimization_barrier((up_part, down_rows, kv_grad))
        up_rows = scatter_grad(up_part, grad_axes)
        cross_branch, grad_cq_both = both(cross_branch), both(grad_cq)
        grad_cq, result = lax.optimization_barrier((grad_cq, result))
        parts = mm_scatter(grad_cq, mid[:, :group])
        grad_after_attn, attn_branch, gain_grad_b = norm_back(
            parts, grad_after_cross, after_attn, gain_b
        )

        attn_branch = gather_tokens(attn_branch)
        cross_part = grad_products(
            [(early[2], grad_cq_both), (cross_branch, early[3])],
            "cross_grads",
            *(halves or (None, 0)),
            6 * group,
            4 * group,
        )
        attn_branch, cross_part = lax.optimization_barrier((attn_branch, cross_part))
        attn_branch, grad_self_mixed = gather_mm(attn_branch, first, 3 * group, group, "out_back")
        grad_projected = self_back(projected, grad_self_mixed, 2 * images)
        rest_part = grad_products(
            [(early[0], both(grad_projected)), (both(attn_branch), early[1])],
            "attention_grads",
            *(halves or (None, 0)),
            6 * group,
            0,
            cross_part,
        )
        grad_projected, kv_grad, rest_part = lax.optimization_barrier(
            (grad_projected, kv_grad, rest_part)
        )
        rest_part, up_rows = lax.optimization_barrier((rest_part, up_rows))
        rest_rows = scatter_grad(rest_part, grad_axes)
        parts = mm_scatter(grad_projected, first[:, : 3 * group])
        grad_hidden, gain_grad_a, mask_grad = last_back(
            parts,
            grad_after_attn,
            start_x,
            gain_a,
            masked,
            unit,
            order,
        )
        sums = jnp.concatenate([gain_grad_a, gain_grad_b, gain_grad_c, mask_grad], axis=0)

        output = layer_output(after_cross, result, unit, order)

        kv_halves = kv_grad.reshape(2, -1, 2 * group)
        kv_keep = lax.dynamic_index_in_dim(kv_halves, core, 0, keepdims=False)
        kv_send = lax.dynamic_index_in_dim(kv_halves, 1 - core, 0, keepdims=False)
        kv_sum = sum_z((kv_keep + swap(kv_send, "c")).astype(BF))
        wide_rows = swap_parts(pick_rows([down_rows, up_rows], rank))
        kv_sum, wide_rows = lax.optimization_barrier((kv_sum, wide_rows))
        kv_grads = spread(kv_sum, PLANE, 8)
        down_grad, up_grad = finish_wide(wide_rows, rank)
        kv_weight_grad, grad_text_w, caption_part = text_back(
            kv_grads, own_text, w_cross, caption, w_text, halves_of(sums, text_width // 4)
        )
        half_context = caption.shape[0] // 2
        caption_part = trade(caption_part, PLANE).astype(F32).sum(axis=0)
        sums = layer_order(add_z(whole_of(caption_part[half_context:], width)))
        caption_part = sum_z(caption_part[:half_context].astype(BF))
        caption_part, rest_rows = lax.optimization_barrier((caption_part, rest_rows))
        grad_caption = caption_output(spread(caption_part, PLANE, 8))

        qkv_grad, out_grad, grad_cross, cross_out_grad = finish_all(
            swap_parts(pick_rows([rest_rows], rank)), kv_weight_grad, rank
        )
        return (
            outer(output).reshape(hidden.shape),
            outer(grad_hidden).reshape(hidden.shape),
            grad_caption,
            sums[:3],
            sums[3],
            qkv_grad.transpose(1, 0, 2),
            out_grad,
            grad_cross.transpose(1, 0, 2),
            cross_out_grad,
            grad_text_w,
            up_grad,
            down_grad,
        )

    return local


def solution(mesh):
    z_size = mesh.shape["img"] // 4
    inner = Mesh(mesh.devices.reshape(z_size, 2, 2, 2), ("z", "x", "c", "y"))
    image = ("z", "x", "c")
    tokens = P(image, "y", None)
    rows = P(image + ("y",))
    in_specs = (tokens, P(image, None), P(image), P(), P(), P()) + (rows,) * 7 + (tokens,)
    out_specs = (tokens, tokens, P(), P(), P()) + (rows,) * 7
    return jax.shard_map(
        make_local(z_size), mesh=inner, in_specs=in_specs, out_specs=out_specs, check_vma=False
    )
```

```python
import math

import jax
import jax.numpy as jnp
from jax import lax
from jax.experimental import pallas as pl
from jax.experimental.pallas import tpu as pltpu
from jax.sharding import Mesh
from jax.sharding import PartitionSpec as P

HD = 128
EPS = 1e-05
BF = jnp.bfloat16
F32 = jnp.float32
PAIR = ((0, 1), (1, 0))
GROUP = ("x", "y")
DATA = ("z", "c")
PLANE = ("x", "c", "y")
VMEM = 48 * 1024 * 1024
SCALE = 1.0 / math.sqrt(HD)
SLOPE = math.sqrt(2.0 / math.pi)
CUBIC = 0.044715


def dot(a, b, dims):
    return lax.dot_general(a, b, (dims, ((), ())), preferred_element_type=F32)


def mm(a, b):
    return dot(a, b, ((1,), (0,)))


def mm_t(a, b):
    return dot(a, b, ((1,), (1,)))


def t_mm(a, b):
    return dot(a, b, ((0,), (0,)))


def shape(dims, dtype=BF):
    return jax.ShapeDtypeStruct(dims, dtype)


def swap(values, axis):
    return lax.ppermute(values, axis, PAIR)


def trade(blocks, axes=GROUP):
    return lax.all_to_all(blocks, axes, 0, 0, tiled=True)


def spread(values, axes=GROUP, count=4):
    return trade(jnp.broadcast_to(values[None], (count,) + values.shape), axes)


def gather_tokens(own):
    half = own.shape[0] // 2
    from_x = swap(own, "x")
    from_y = swap(own, "y")
    return own, from_y, from_x, swap(from_x[:half], "y"), swap(from_y[half:], "x")


def scatter_tokens(parts):
    own, for_y, for_x, for_low, for_high = parts
    half = for_low.shape[0]
    low = swap(for_low, "y").astype(F32) + for_x[:half].astype(F32)
    high = swap(for_high, "x").astype(F32) + for_y[half:].astype(F32)
    from_x = swap(jnp.concatenate([low.astype(BF), for_x[half:]], axis=0), "x")
    from_y = swap(jnp.concatenate([for_y[:half], high.astype(BF)], axis=0), "y")
    return [own, from_x, from_y]


def swap_parts(parts):
    return [
        parts[0],
        swap(parts[1], "y"),
        swap(parts[2], "x"),
        lax.ppermute(parts[3], GROUP, ((0, 3), (1, 2), (2, 1), (3, 0))),
    ]


def gather_rows(rows):
    return lax.all_gather(rows.reshape(-1, rows.shape[-1]), DATA, axis=0, tiled=True)


def scatter_grad(partial, axes):
    summed = lax.psum_scatter(partial, axes, scatter_dimension=0, tiled=True)
    return summed.reshape(4, -1, summed.shape[-1])


def call(kernel, grid, in_specs, out_specs, out_shape, operands, name, flops=0, size=1 << 22,
         rank=None, scratch=()):
    options = dict(
        out_shape=out_shape,
        compiler_params=pltpu.CompilerParams(vmem_limit_bytes=VMEM),
        cost_estimate=pl.CostEstimate(flops=flops, bytes_accessed=size, transcendentals=0),
        name=name,
    )
    if rank is None:
        return pl.pallas_call(
            kernel, grid=grid, in_specs=in_specs, out_specs=out_specs, scratch_shapes=scratch,
            **options,
        )(*operands)
    spec = pltpu.PrefetchScalarGridSpec(
        num_scalar_prefetch=1,
        grid=grid,
        in_specs=in_specs,
        out_specs=out_specs,
        scratch_shapes=scratch,
    )
    return pl.pallas_call(kernel, grid_spec=spec, **options)(rank.reshape(1), *operands)


def whole(array):
    return pl.BlockSpec(array.shape, lambda *_: (0,) * len(array.shape))


def reorder(values, unit, order):
    if order is None:
        return values
    return jnp.concatenate([values[:, k * unit : (k + 1) * unit] for k in order], axis=1)


def assemble(target, pieces, sems):
    copies, at = [], 0
    for k, piece in enumerate(pieces):
        rows = piece.shape[0]
        copies.append(pltpu.make_async_copy(piece, target.at[at : at + rows], sems.at[k]))
        at += rows
    for copy in copies:
        copy.start()
    for copy in copies:
        copy.wait()


ANY = pl.BlockSpec(memory_space=pl.ANY)


def gather_mm(pieces, weight, first, columns, name):
    rows, width = pieces[0].shape
    step = 256

    def kernel(*refs):
        tokens, out, sems = refs[6:]

        @pl.when(pl.program_id(0) == 0)
        def _():
            assemble(tokens, refs[:5], sems)

        out[...] = mm(tokens[...], refs[5][...]).astype(BF)

    return call(
        kernel,
        (columns // step,),
        [ANY] * 5 + [pl.BlockSpec((width, step), lambda j: (0, first // step + j))],
        [
            pl.BlockSpec((4 * rows, width), lambda j: (0, 0)),
            pl.BlockSpec((4 * rows, step), lambda j: (0, j)),
        ],
        [shape((4 * rows, width)), shape((4 * rows, columns))],
        [*pieces, weight],
        name,
        flops=8 * rows * width * columns,
        size=2 * width * (columns + 8 * rows),
        scratch=[pltpu.SemaphoreType.DMA((5,))],
    )


def mm_scatter(values, weight):
    partial = mm_t(values, weight).astype(BF)
    rows = partial.shape[0] // 4
    cuts = [0, rows, 2 * rows, 3 * rows, 3 * rows + rows // 2, 4 * rows]
    return scatter_tokens([partial[a:b] for a, b in zip(cuts, cuts[1:])])


def normalize(values):
    centred = values - jnp.mean(values, axis=-1, keepdims=True)
    inv_std = lax.rsqrt(jnp.mean(centred * centred, axis=-1, keepdims=True) + EPS)
    return centred * inv_std, inv_std


NORM_ROWS = 32


def row_spec(array, at=None):
    width = array.shape[-1]
    if at is None:
        return pl.BlockSpec((NORM_ROWS, width), lambda i: (i, 0))
    return pl.BlockSpec((1, NORM_ROWS, width), lambda i, at=at: (at, i, 0))


def terms_of(terms):
    arrays, specs = [], []
    for term in terms:
        array, at = term if isinstance(term, tuple) else (term, None)
        arrays.append(array)
        specs.append(row_spec(array, at))
    return arrays, specs


def total_of(refs):
    values = [ref[0] if len(ref.shape) == 3 else ref[...] for ref in refs]
    return sum(value.astype(F32) for value in values)


def add_norm(terms, gain):
    arrays, specs = terms_of(terms)
    tokens, width = arrays[0].shape[-2], arrays[0].shape[-1]
    tokens = min(a.shape[-2] for a in arrays)

    def kernel(*refs):
        gain_ref, x, out = refs[-3:]
        values = total_of(refs[:-3])
        x[...] = values
        out[...] = (normalize(values)[0] * gain_ref[...]).astype(BF)

    return call(
        kernel,
        (tokens // NORM_ROWS,),
        specs + [whole(gain)],
        [row_spec(shape((tokens, width)))] * 2,
        [shape((tokens, width), F32), shape((tokens, width))],
        [*arrays, gain],
        "add_norm",
    )


def norm_grad(grad, values, gain):
    normed, inv_std = normalize(values)
    scaled = grad * gain
    first_mean = jnp.mean(scaled, axis=-1, keepdims=True)
    second_mean = jnp.mean(scaled * normed, axis=-1, keepdims=True)
    return (
        inv_std * (scaled - first_mean - normed * second_mean),
        jnp.sum(grad * normed, axis=0, keepdims=True),
    )


def accumulate(ref, value):
    @pl.when(pl.program_id(0) == 0)
    def _():
        ref[...] = jnp.zeros_like(ref)

    ref[...] += value


def norm_back(terms, upper, values, gain):
    arrays, specs = terms_of(terms)
    tokens, width = values.shape

    def kernel(*refs):
        upper_ref, x, gain_ref, out, out_low, gain_grad = refs[-6:]
        back, part = norm_grad(total_of(refs[:-6]), x[...], gain_ref[...])
        result = upper_ref[...].astype(F32) + back
        out[...] = result
        out_low[...] = result.astype(BF)
        accumulate(gain_grad, part)

    return call(
        kernel,
        (tokens // NORM_ROWS,),
        specs + [row_spec(upper), row_spec(values), whole(gain)],
        [row_spec(values)] * 2 + [pl.BlockSpec((1, width), lambda i: (0, 0))],
        [shape((tokens, width), F32), shape((tokens, width)), shape((1, width), F32)],
        [*arrays, upper, values, gain],
        "norm_back",
    )


def last_back(terms, upper, values, gain, masked, unit, order):
    arrays, specs = terms_of(terms)
    tokens, width = values.shape

    def kernel(*refs):
        upper_ref, x, gain_ref, mask, out, gain_grad, mask_grad = refs[-7:]
        back, part = norm_grad(total_of(refs[:-7]), x[...], gain_ref[...])
        result = upper_ref[...].astype(F32) + back
        hit = mask[...] > 0.5
        out[...] = reorder(jnp.where(hit, 0.0, result).astype(BF), unit, order)
        accumulate(gain_grad, part)
        accumulate(mask_grad, jnp.sum(jnp.where(hit, result, 0.0), axis=0, keepdims=True))

    line = pl.BlockSpec((1, width), lambda i: (0, 0))
    return call(
        kernel,
        (tokens // NORM_ROWS,),
        specs + [row_spec(upper), row_spec(values), whole(gain), row_spec(masked)],
        [row_spec(values), line, line],
        [shape((tokens, width)), shape((1, width), F32), shape((1, width), F32)],
        [*arrays, upper, values, gain, masked],
        "last_back",
    )


def start(hidden, cotangent, masked, embed, gain, unit, order):
    tokens, width = hidden.shape

    def kernel(hid, cot, mask, embed_ref, gain_ref, x, out, grad):
        hit = mask[...] > 0.5
        values = jnp.where(
            hit, embed_ref[...], reorder(hid[...], unit, order).astype(F32)
        )
        x[...] = values
        out[...] = (normalize(values)[0] * gain_ref[...]).astype(BF)
        grad[...] = jnp.where(hit, reorder(cot[...], unit, order).astype(F32), 0.0).astype(BF)

    rows = row_spec(hidden)
    return call(
        kernel,
        (tokens // NORM_ROWS,),
        [rows, rows, row_spec(masked), whole(embed), whole(gain)],
        [rows] * 3,
        [shape((tokens, width), F32), shape((tokens, width)), shape((tokens, width))],
        [hidden, cotangent, masked, embed, gain],
        "start",
    )


def layer_output(upper, terms, unit, order):
    arrays, specs = terms_of(terms)
    tokens, width = upper.shape

    def kernel(*refs):
        values = refs[-2][...] + total_of(refs[:-2])
        refs[-1][...] = reorder(values.astype(BF), unit, order)

    return call(
        kernel,
        (tokens // NORM_ROWS,),
        specs + [row_spec(upper)],
        row_spec(upper),
        shape((tokens, width)),
        [*arrays, upper],
        "layer_output",
    )


def feed_up(pieces, weight):
    rows, width = pieces[0].shape
    hidden = weight.shape[1]
    step = 256

    def kernel(*refs):
        up, tokens, act, slope, sems = refs[5:]

        @pl.when(pl.program_id(0) == 0)
        def _():
            assemble(tokens, refs[:5], sems)

        u = mm(tokens[...], up[...])
        square = u * u
        bend = jnp.tanh(SLOPE * u * (1.0 + CUBIC * square))
        half = 0.5 * (1.0 + bend)
        act[...] = (u * half).astype(BF)
        slope[...] = half + 0.5 * u * (1.0 - bend * bend) * SLOPE * (1.0 + 3.0 * CUBIC * square)

    part = pl.BlockSpec((4 * rows, step), lambda j: (0, j))
    return call(
        kernel,
        (hidden // step,),
        [ANY] * 5 + [pl.BlockSpec((width, step), lambda j: (0, j))],
        [pl.BlockSpec((4 * rows, width), lambda j: (0, 0)), part, part],
        [shape((4 * rows, width)), shape((4 * rows, hidden)), shape((4 * rows, hidden), F32)],
        [*pieces, weight],
        "feed_up",
        scratch=[pltpu.SemaphoreType.DMA((5,))],
        flops=8 * rows * width * hidden,
        size=2 * width * (hidden + 8 * rows),
    )


def feed_down(grad_y, slope, weight):
    tokens, width = grad_y.shape
    hidden = weight.shape[1]
    step = 256

    def kernel(dy, slope_ref, down, out):
        out[...] = (mm(dy[...], down[...]) * slope_ref[...]).astype(BF)

    part = pl.BlockSpec((tokens, step), lambda j: (0, j))
    return call(
        kernel,
        (hidden // step,),
        [whole(grad_y), part, pl.BlockSpec((width, step), lambda j: (0, j))],
        part,
        shape((tokens, hidden)),
        [grad_y, slope, weight],
        "feed_down",
        flops=2 * tokens * width * hidden,
        size=2 * width * (hidden + 8 * tokens),
    )


def softmax(scores):
    exp_terms = jnp.exp(scores - jnp.max(scores, axis=-1, keepdims=True))
    return exp_terms / jnp.sum(exp_terms, axis=-1, keepdims=True)


def score_grad(probs, grad_probs):
    return (
        probs * (grad_probs - jnp.sum(probs * grad_probs, axis=-1, keepdims=True))
    ).astype(BF)


def head(ref, k):
    return ref[:, k * HD : (k + 1) * HD]


def self_forward(projected, images):
    tokens, width = projected.shape
    rows, group = tokens // images, width // 3
    heads = group // HD

    def kernel(proj, mixed):
        for k in range(heads):
            query, key, value = (head(proj, j * heads + k) for j in range(3))
            probs = softmax(mm_t(query, key) * SCALE).astype(BF)
            mixed[:, k * HD : (k + 1) * HD] = mm(probs, value).astype(BF)

    return call(
        kernel,
        (images,),
        [pl.BlockSpec((rows, width), lambda i: (i, 0))],
        pl.BlockSpec((rows, group), lambda i: (i, 0)),
        shape((tokens, group)),
        [projected],
        "self_forward",
        flops=4 * tokens * rows * group,
    )


def self_back(projected, grad_mixed, images):
    tokens, width = projected.shape
    rows, group = tokens // images, width // 3
    heads = group // HD

    def kernel(proj, grad, out):
        for k in range(heads):
            query, key, value = (head(proj, j * heads + k) for j in range(3))
            grad_head = head(grad, k)
            probs = softmax(mm_t(query, key) * SCALE)
            grad_scores = score_grad(probs, mm_t(grad_head, value))
            parts = (
                mm(grad_scores, key) * SCALE,
                t_mm(grad_scores, query) * SCALE,
                t_mm(probs.astype(BF), grad_head),
            )
            for j, part in enumerate(parts):
                at = (j * heads + k) * HD
                out[:, at : at + HD] = part.astype(BF)

    return call(
        kernel,
        (images,),
        [
            pl.BlockSpec((rows, width), lambda i: (i, 0)),
            pl.BlockSpec((rows, group), lambda i: (i, 0)),
        ],
        pl.BlockSpec((rows, width), lambda i: (i, 0)),
        shape((tokens, width)),
        [projected, grad_mixed],
        "self_back",
        flops=10 * tokens * rows * group,
    )


def cross_forward(queries, text_kv):
    tokens, group = queries.shape
    heads = group // HD

    def kernel(query, text, mixed):
        for k in range(heads):
            probs = softmax(mm_t(head(query, k), head(text, k)) * SCALE).astype(BF)
            mixed[:, k * HD : (k + 1) * HD] = mm(probs, head(text, heads + k)).astype(BF)

    return call(
        kernel,
        (1,),
        [whole(queries), whole(text_kv)],
        whole(queries),
        shape((tokens, group)),
        [queries, text_kv],
        "cross_forward",
        flops=4 * tokens * text_kv.shape[0] * group,
    )


def cross_back(queries, text_kv, grad_mixed):
    tokens, group = queries.shape
    context = text_kv.shape[0]
    heads = group // HD

    def kernel(query, text, grad, grad_query, grad_text):
        for k in range(heads):
            query_head, key, value = head(query, k), head(text, k), head(text, heads + k)
            grad_head = head(grad, k)
            probs = softmax(mm_t(query_head, key) * SCALE)
            grad_scores = score_grad(probs, mm_t(grad_head, value))
            grad_query[:, k * HD : (k + 1) * HD] = (mm(grad_scores, key) * SCALE).astype(BF)
            at = (heads + k) * HD
            grad_text[:, k * HD : (k + 1) * HD] = t_mm(grad_scores, query_head) * SCALE
            grad_text[:, at : at + HD] = t_mm(probs.astype(BF), grad_head)

    return call(
        kernel,
        (1,),
        [whole(queries), whole(text_kv), whole(grad_mixed)],
        [whole(queries), whole(text_kv)],
        [shape((tokens, group)), shape((context, 2 * group), F32)],
        [queries, text_kv, grad_mixed],
        "cross_back",
        flops=10 * tokens * context * group,
    )


def grad_products(pairs, name, core=None, blocks=0):
    count_in = len(pairs[0][0])
    tokens, width = pairs[0][0][0].shape
    widths = [y[0].shape[1] for _, y in pairs]
    total = sum(widths)
    rows = 256 if core is None else width // (2 * blocks)
    steps = width // rows if core is None else blocks
    step = 512
    count = len(pairs) * count_in

    def kernel(r, *refs):
        out = refs[2 * count]
        offset = 0
        for k, wide in enumerate(widths):
            left = [refs[k * count_in + b][...].T for b in range(count_in)]
            for at in range(0, wide, step):
                out[:, offset + at : offset + at + step] = sum(
                    mm(left[b], refs[count + k * count_in + b][:, at : at + step])
                    for b in range(count_in)
                ).astype(BF)
            offset += wide

    pick = (lambda i, r: (0, i)) if core is None else (lambda i, r: (0, 2 * i + r[0]))
    return call(
        kernel,
        (steps,),
        [pl.BlockSpec((tokens, rows), pick)] * count
        + [pl.BlockSpec((tokens, w), lambda i, r: (0, 0)) for w in widths for _ in range(count_in)],
        pl.BlockSpec((rows, total), lambda i, r: (i, 0)),
        shape((steps * rows, total)),
        [b for x, _ in pairs for b in x] + [b for _, y in pairs for b in y],
        name,
        flops=2 * tokens * count_in * steps * rows * total,
        size=4 * width * total,
        rank=jnp.zeros((), jnp.int32) if core is None else core,
    )


def pick_weights(three, one, rank):
    rows, width = one.shape[0], one.shape[1] // 4

    def kernel(r, three_ref, one_ref, *outs):
        for k in range(4):

            @pl.when(pl.program_id(0) == k)
            def _():
                for j in range(3):
                    outs[k][:, j * width : (j + 1) * width] = three_ref[j]
                outs[k][:, 3 * width :] = one_ref[...]

    outs = [shape((rows, 4 * width))] * 4
    return call(
        kernel,
        (4,),
        [
            pl.BlockSpec((3, rows, width), lambda k, r: (0, 0, k ^ r[0])),
            pl.BlockSpec((rows, width), lambda k, r: (0, k ^ r[0])),
        ],
        [whole(a) for a in outs],
        outs,
        [three, one],
        "pick_weights",
        rank=rank,
    )


def pick_rows(arrays, rank):
    rows = arrays[0].shape[1]
    widths = [a.shape[2] for a in arrays]
    count = len(arrays)

    def kernel(r, *refs):
        for k in range(4):

            @pl.when(pl.program_id(0) == k)
            def _():
                at = 0
                for ref, width in zip(refs, widths):
                    refs[count + k][:, at : at + width] = ref[0]
                    at += width

    outs = [shape((rows, sum(widths)))] * 4
    return call(
        kernel,
        (4,),
        [pl.BlockSpec((1, rows, w), lambda k, r: (k ^ r[0], 0, 0)) for w in widths],
        [whole(a) for a in outs],
        outs,
        arrays,
        "pick_rows",
        rank=rank,
    )


def place(parts, rank):
    def kernel(r, *refs):
        for k in range(4):

            @pl.when(pl.program_id(0) == k)
            def _():
                refs[4][0] = refs[k][...]

    rows, columns = parts[0].shape
    return call(
        kernel,
        (4,),
        [whole(p) for p in parts],
        pl.BlockSpec((1, rows, columns), lambda k, r: (k ^ r[0], 0, 0)),
        shape((4, rows, columns)),
        parts,
        "place",
        rank=rank,
    )


def finish_wide(parts, rank):
    rows, total = parts[0].shape
    width = total // 2

    def kernel(r, *refs):
        for k in range(4):

            @pl.when(pl.program_id(0) == k)
            def _():
                refs[4][...] = refs[k][:, :width].astype(F32)
                refs[5][...] = refs[k][:, width:].astype(F32)

    flat = pl.BlockSpec((rows, width), lambda k, r: (0, k ^ r[0]))
    return call(
        kernel,
        (4,),
        [whole(p) for p in parts],
        [flat, flat],
        [shape((rows, 4 * width), F32)] * 2,
        parts,
        "finish_wide",
        rank=rank,
    )


def finish_all(parts, text_grad, rank):
    rows, total = parts[0].shape
    width = total // 6

    def kernel(r, *refs):
        key, value, three, out, cross, cross_out = refs[4:]
        for k in range(4):

            @pl.when(pl.program_id(0) == k)
            def _():
                def part(j):
                    return refs[k][:, j * width : (j + 1) * width].astype(F32)

                for j in range(3):
                    three[j] = part(j)
                out[...] = part(3)
                cross[0] = part(4)
                cross_out[...] = part(5)

        cross[1] = key[...]
        cross[2] = value[...]

    wide = pl.BlockSpec((3, rows, width), lambda k, r: (0, 0, k ^ r[0]))
    flat = pl.BlockSpec((rows, width), lambda k, r: (0, k ^ r[0]))
    return call(
        kernel,
        (4,),
        [whole(p) for p in parts]
        + [flat, pl.BlockSpec((rows, width), lambda k, r: (0, 4 + (k ^ r[0])))],
        [wide, flat, wide, flat],
        [shape((3, rows, 4 * width), F32), shape((rows, 4 * width), F32)] * 2,
        [*parts, text_grad, text_grad],
        "finish_all",
        rank=rank,
    )


def plane_block(k):
    return (k >> 1) & 1, (k >> 2) * 2 + (k & 1)


def text_forward(caption, w_text, w_cross):
    context, rows = caption.shape[0], w_text.shape[0]
    half, width = context // 2, w_cross.shape[2] // 4

    def kernel(cap, weight, cross, own, blocks):
        own[...] = mm_t(cap[...], weight[...]).astype(BF)
        for j in range(2):
            part = mm(own[...], cross[1 + j]).astype(BF)
            for k in range(8):
                core, group = plane_block(k)
                blocks[k, :, j * width : (j + 1) * width] = part[
                    core * half : (core + 1) * half, group * width : (group + 1) * width
                ]

    return call(
        kernel,
        (1,),
        [whole(caption), whole(w_text), whole(w_cross)],
        [
            pl.BlockSpec((context, rows), lambda i: (0, 0)),
            pl.BlockSpec((8, half, 2 * width), lambda i: (0, 0, 0)),
        ],
        [shape((context, rows)), shape((8, half, 2 * width))],
        [caption, w_text, w_cross],
        "text_forward",
    )


def text_back(blocks, own_text, w_cross, caption, w_text, extra):
    context, rows = own_text.shape
    half, width = context // 2, w_cross.shape[2] // 4
    wide = caption.shape[1] // 4
    tail = extra.shape[0]

    def kernel(block, own, cross, cap, weight, more, kv_grad, text_grad, out, grads):
        for k in range(8):
            core, group = plane_block(k)
            for j in range(2):
                at = (4 * j + group) * width
                grads[core * half : (core + 1) * half, at : at + width] = block[
                    k, :, j * width : (j + 1) * width
                ]
        kv_grad[...] = t_mm(own[...], grads[...])
        grad_text = sum(
            mm_t(grads[:, 4 * j * width : 4 * (j + 1) * width], cross[1 + j]) for j in range(2)
        ).astype(BF)
        text_grad[...] = t_mm(grad_text, cap[...])
        part = mm(grad_text, weight[...]).astype(BF)
        for k in range(8):
            core, group = plane_block(k)
            out[k, :half, :] = part[core * half : (core + 1) * half, group * wide : (group + 1) * wide]
            out[k, half:, :] = more[...]

    operands = [blocks, own_text, w_cross, caption, w_text, extra]
    outs = [
        shape((rows, 8 * width), F32),
        shape((rows, 4 * wide), F32),
        shape((8, half + tail, wide)),
    ]
    return call(
        kernel,
        (1,),
        [whole(a) for a in operands],
        [whole(a) for a in outs],
        outs,
        operands,
        "text_back",
        scratch=[pltpu.VMEM((context, 8 * width), BF)],
    )


def caption_output(blocks):
    count, half, wide = blocks.shape

    def kernel(block, out):
        out[...] = block[0].astype(F32)

    return call(
        kernel,
        (count,),
        [pl.BlockSpec((1, half, wide), lambda k: (k, 0, 0))],
        pl.BlockSpec((half, wide), lambda k: plane_block(k)),
        shape((2 * half, 4 * wide), F32),
        [blocks],
        "caption_output",
    )


def column_blocks(weight, count):
    rows = weight.shape[0]
    return weight.reshape(rows, count, -1).transpose(1, 0, 2)


def halves_of(values, width):
    high = values.astype(BF)
    low = (values - high.astype(F32)).astype(BF)
    return jnp.concatenate([high.reshape(-1, width), low.reshape(-1, width)], axis=0)


def whole_of(halves, width):
    rows = halves.shape[0] // 2
    return (halves[:rows] + halves[rows:]).reshape(-1, width)


def make_local(z_size):
    def sum_z(values):
        parts = values.reshape(z_size, -1, values.shape[-1])
        mine = trade(parts, "z").astype(F32).sum(axis=0).astype(BF)
        return spread(mine, "z", z_size).reshape(values.shape)

    def add_z(values):
        step = 1
        while step < z_size:
            values = values + lax.ppermute(
                values, "z", tuple((k, k ^ step) for k in range(z_size))
            )
            step *= 2
        return values

    def layer_order(values):
        shaped = values.reshape(values.shape[:-1] + (z_size, 2, 2, -1))
        return jnp.swapaxes(shaped, -3, -2).reshape(values.shape)

    def local(
        hidden,
        mask_index,
        mask_count,
        mask_embed,
        norm_gains,
        caption,
        w_qkv,
        w_out,
        w_cross,
        w_cross_out,
        w_text,
        w_up,
        w_down,
        cotangent,
    ):
        images, local_rows, width = hidden.shape
        full_length = mask_index.shape[1]
        rank = lax.axis_index("x") * 2 + lax.axis_index("y")
        core = lax.axis_index("c")
        tokens = images * local_rows
        group = width // 4
        text_width = caption.shape[1]

        unit = width // (4 * z_size)
        inside = unit % 128 == 0
        order = [4 * k + j for k in range(z_size) for j in (0, 2, 1, 3)] if inside else None

        def outer(values):
            return values if inside else layer_order(values)

        w_qkv, w_cross = w_qkv.transpose(1, 0, 2), w_cross.transpose(1, 0, 2)
        first = swap_parts(pick_weights(w_qkv, w_out, rank))
        first = gather_rows(place(first, rank))

        positions = lax.axis_index("y") * local_rows + jnp.arange(local_rows, dtype=jnp.int32)
        ranks = jnp.arange(full_length, dtype=jnp.int32)
        matches = (mask_index[:, :, None] == positions[None, None, :]) & (
            ranks[None, :, None] < mask_count[:, None, None]
        )
        masked = jnp.any(matches, axis=1).reshape(tokens, 1).astype(F32)
        gains = layer_order(norm_gains)
        gain_a, gain_b, gain_c = gains[:1], gains[1:2], gains[2:]
        start_x, attn_in, grad_top = start(
            outer(hidden.reshape(tokens, width)),
            outer(cotangent.reshape(tokens, width)),
            masked,
            layer_order(mask_embed)[None],
            gain_a,
            unit,
            order,
        )
        attn_in = gather_tokens(attn_in)
        mid = jnp.concatenate([column_blocks(w_cross[0], 4), column_blocks(w_cross_out, 4)], axis=2)
        up = column_blocks(w_up, 4)
        attn_in, mid, up = lax.optimization_barrier((attn_in, mid, up))
        mid, up = gather_rows(trade(mid)), gather_rows(trade(up))

        own_text, kv_part = text_forward(caption, w_text, w_cross)
        text_kv = trade(kv_part, PLANE).astype(F32).sum(axis=0).astype(BF)
        text_kv = sum_z(text_kv)
        other = swap(text_kv, "c")
        text_kv = jnp.concatenate(
            [jnp.where(core == 0, text_kv, other), jnp.where(core == 0, other, text_kv)], axis=0
        )
        attn_in, text_kv = lax.optimization_barrier((attn_in, text_kv))

        attn_in, projected = gather_mm(attn_in, first, 0, 3 * group, "qkv_mm")
        self_mixed = self_forward(projected, 2 * images)
        down = column_blocks(w_down, 4)
        self_mixed, down = lax.optimization_barrier((self_mixed, down))
        down = gather_rows(trade(down))
        parts = mm_scatter(self_mixed, first[:, 3 * group :])
        after_attn, cross_in = add_norm([start_x] + parts, gain_b)

        cross_in, cross_queries = gather_mm(gather_tokens(cross_in), mid, 0, group, "query_mm")
        cross_mixed = cross_forward(cross_queries, text_kv)
        parts = mm_scatter(cross_mixed, mid[:, group:])
        after_cross, mlp_in = add_norm([after_attn] + parts, gain_c)

        mlp_in = gather_tokens(mlp_in)
        mlp_in, grad_top = lax.optimization_barrier((mlp_in, grad_top))
        grad_y = jnp.concatenate(gather_tokens(grad_top), axis=0)
        mlp_in, activated, slope = feed_up(mlp_in, up)
        early = [attn_in, self_mixed, cross_in, cross_mixed]
        if inside:
            grad_axes, halves = "z", (core, z_size)

            def both(values):
                return [values, swap(values, "c")]

        else:
            grad_axes, halves = DATA, ()

            def both(values):
                return [values]

        early = [both(values) for values in early]
        down_part = grad_products([(both(grad_y), both(activated))], "down_grads", *halves)
        mlp_in = both(mlp_in)
        slope, down_part, early, mlp_in = lax.optimization_barrier((slope, down_part, early, mlp_in))
        down_rows = scatter_grad(down_part, grad_axes)
        grad_pre = feed_down(grad_y, slope, down)
        parts = mm_scatter(grad_pre, up)
        up_part = grad_products([(mlp_in, both(grad_pre))], "up_grads", *halves)
        grad_after_cross, cross_branch, gain_grad_c = norm_back(
            parts, grad_top, after_cross, gain_c
        )

        cross_branch = gather_tokens(cross_branch)
        cross_branch, up_part = lax.optimization_barrier((cross_branch, up_part))
        cross_branch, grad_cross_mixed = gather_mm(
            cross_branch, mid, group, group, "cross_out_back"
        )
        grad_cq, kv_grad = cross_back(cross_queries, text_kv, grad_cross_mixed)
        up_part, down_rows, kv_grad = lax.optimization_barrier((up_part, down_rows, kv_grad))
        up_rows = scatter_grad(up_part, grad_axes)
        cross_branch, grad_cq_both = both(cross_branch), both(grad_cq)
        parts = mm_scatter(grad_cq, mid[:, :group])
        grad_after_attn, attn_branch, gain_grad_b = norm_back(
            parts, grad_after_cross, after_attn, gain_b
        )

        attn_branch, grad_self_mixed = gather_mm(
            gather_tokens(attn_branch), first, 3 * group, group, "out_back"
        )
        grad_projected = self_back(projected, grad_self_mixed, 2 * images)
        rest_part = grad_products(
            [
                (early[0], both(grad_projected)),
                (both(attn_branch), early[1]),
                (early[2], grad_cq_both),
                (cross_branch, early[3]),
            ],
            "attention_grads",
            *halves,
        )
        grad_projected, activated, kv_grad, rest_part = lax.optimization_barrier(
            (grad_projected, activated, kv_grad, rest_part)
        )
        rest_part, up_rows = lax.optimization_barrier((rest_part, up_rows))
        rest_rows = scatter_grad(rest_part, grad_axes)
        parts = mm_scatter(grad_projected, first[:, : 3 * group])
        grad_hidden, gain_grad_a, mask_grad = last_back(
            parts,
            grad_after_attn,
            start_x,
            gain_a,
            masked,
            unit,
            order,
        )
        sums = jnp.concatenate([gain_grad_a, gain_grad_b, gain_grad_c, mask_grad], axis=0)

        result = mm_scatter(activated, down)

        kv_halves = kv_grad.reshape(2, -1, 2 * group)
        kv_keep = lax.dynamic_index_in_dim(kv_halves, core, 0, keepdims=False)
        kv_send = lax.dynamic_index_in_dim(kv_halves, 1 - core, 0, keepdims=False)
        kv_sum = sum_z((kv_keep + swap(kv_send, "c")).astype(BF))
        wide_rows = swap_parts(pick_rows([down_rows, up_rows], rank))
        kv_sum, wide_rows = lax.optimization_barrier((kv_sum, wide_rows))
        kv_grads = spread(kv_sum, PLANE, 8)
        kv_weight_grad, grad_text_w, caption_part = text_back(
            kv_grads, own_text, w_cross, caption, w_text, halves_of(sums, text_width // 4)
        )
        half_context = caption.shape[0] // 2
        caption_part = trade(caption_part, PLANE).astype(F32).sum(axis=0)
        sums = layer_order(add_z(whole_of(caption_part[half_context:], width)))
        caption_part = sum_z(caption_part[:half_context].astype(BF))
        output = layer_output(after_cross, result, unit, order)
        down_grad, up_grad = finish_wide(wide_rows, rank)
        caption_part, rest_rows, sums, output, down_grad, up_grad = lax.optimization_barrier(
            (caption_part, rest_rows, sums, output, down_grad, up_grad)
        )
        grad_caption = caption_output(spread(caption_part, PLANE, 8))

        qkv_grad, out_grad, grad_cross, cross_out_grad = finish_all(
            swap_parts(pick_rows([rest_rows], rank)), kv_weight_grad, rank
        )
        return (
            outer(output).reshape(hidden.shape),
            outer(grad_hidden).reshape(hidden.shape),
            grad_caption,
            sums[:3],
            sums[3],
            qkv_grad.transpose(1, 0, 2),
            out_grad,
            grad_cross.transpose(1, 0, 2),
            cross_out_grad,
            grad_text_w,
            up_grad,
            down_grad,
        )

    return local


def solution(mesh):
    z_size = mesh.shape["img"] // 4
    inner = Mesh(mesh.devices.reshape(z_size, 2, 2, 2), ("z", "x", "c", "y"))
    image = ("z", "x", "c")
    tokens = P(image, "y", None)
    rows = P(image + ("y",))
    in_specs = (tokens, P(image, None), P(image), P(), P(), P()) + (rows,) * 7 + (tokens,)
    out_specs = (tokens, tokens, P(), P(), P()) + (rows,) * 7
    return jax.shard_map(
        make_local(z_size), mesh=inner, in_specs=in_specs, out_specs=out_specs, check_vma=False
    )
```

```python
import math

import jax
import jax.numpy as jnp
from jax import lax
from jax.experimental import pallas as pl
from jax.experimental.pallas import tpu as pltpu
from jax.sharding import Mesh
from jax.sharding import PartitionSpec as P

HD = 128
EPS = 1e-05
BF = jnp.bfloat16
F32 = jnp.float32
PAIR = ((0, 1), (1, 0))
GROUP = ("x", "y")
DATA = ("z", "c")
PLANE = ("x", "c", "y")
VMEM = 48 * 1024 * 1024
SCALE = 1.0 / math.sqrt(HD)
SLOPE = math.sqrt(2.0 / math.pi)
CUBIC = 0.044715


def dot(a, b, dims):
    return lax.dot_general(a, b, (dims, ((), ())), preferred_element_type=F32)


def mm(a, b):
    return dot(a, b, ((1,), (0,)))


def mm_t(a, b):
    return dot(a, b, ((1,), (1,)))


def t_mm(a, b):
    return dot(a, b, ((0,), (0,)))


def shape(dims, dtype=BF):
    return jax.ShapeDtypeStruct(dims, dtype)


def swap(values, axis):
    return lax.ppermute(values, axis, PAIR)


def trade(blocks, axes=GROUP):
    return lax.all_to_all(blocks, axes, 0, 0, tiled=True)


def spread(values, axes=GROUP, count=4):
    return trade(jnp.broadcast_to(values[None], (count,) + values.shape), axes)


def gather_tokens(own):
    half = own.shape[0] // 2
    from_x = swap(own, "x")
    from_y = swap(own, "y")
    return own, from_y, from_x, swap(from_x[:half], "y"), swap(from_y[half:], "x")


def scatter_tokens(parts):
    own, for_y, for_x, for_low, for_high = parts
    half = for_low.shape[0]
    low = swap(for_low, "y").astype(F32) + for_x[:half].astype(F32)
    high = swap(for_high, "x").astype(F32) + for_y[half:].astype(F32)
    from_x = swap(jnp.concatenate([low.astype(BF), for_x[half:]], axis=0), "x")
    from_y = swap(jnp.concatenate([for_y[:half], high.astype(BF)], axis=0), "y")
    return [own, from_x, from_y]


def swap_parts(parts):
    return [
        parts[0],
        swap(parts[1], "y"),
        swap(parts[2], "x"),
        lax.ppermute(parts[3], GROUP, ((0, 3), (1, 2), (2, 1), (3, 0))),
    ]


def gather_rows(rows):
    return lax.all_gather(rows.reshape(-1, rows.shape[-1]), DATA, axis=0, tiled=True)


def scatter_grad(partial, axes):
    summed = lax.psum_scatter(partial, axes, scatter_dimension=0, tiled=True)
    return summed.reshape(4, -1, summed.shape[-1])


def call(kernel, grid, in_specs, out_specs, out_shape, operands, name, flops=0, size=1 << 22,
         rank=None, scratch=()):
    options = dict(
        out_shape=out_shape,
        compiler_params=pltpu.CompilerParams(vmem_limit_bytes=VMEM),
        cost_estimate=pl.CostEstimate(flops=flops, bytes_accessed=size, transcendentals=0),
        name=name,
    )
    if rank is None:
        return pl.pallas_call(
            kernel, grid=grid, in_specs=in_specs, out_specs=out_specs, scratch_shapes=scratch,
            **options,
        )(*operands)
    spec = pltpu.PrefetchScalarGridSpec(
        num_scalar_prefetch=1,
        grid=grid,
        in_specs=in_specs,
        out_specs=out_specs,
        scratch_shapes=scratch,
    )
    return pl.pallas_call(kernel, grid_spec=spec, **options)(rank.reshape(1), *operands)


def whole(array):
    return pl.BlockSpec(array.shape, lambda *_: (0,) * len(array.shape))


def reorder(values, unit, order):
    if order is None:
        return values
    return jnp.concatenate([values[:, k * unit : (k + 1) * unit] for k in order], axis=1)


def assemble(target, pieces, sems):
    copies, at = [], 0
    for k, piece in enumerate(pieces):
        rows = piece.shape[0]
        copies.append(pltpu.make_async_copy(piece, target.at[at : at + rows], sems.at[k]))
        at += rows
    for copy in copies:
        copy.start()
    for copy in copies:
        copy.wait()


ANY = pl.BlockSpec(memory_space=pl.ANY)


def gather_mm(pieces, weight, first, columns, name):
    rows, width = pieces[0].shape
    step = 256

    def kernel(*refs):
        tokens, out, sems = refs[6:]

        @pl.when(pl.program_id(0) == 0)
        def _():
            assemble(tokens, refs[:5], sems)

        out[...] = mm(tokens[...], refs[5][...]).astype(BF)

    return call(
        kernel,
        (columns // step,),
        [ANY] * 5 + [pl.BlockSpec((width, step), lambda j: (0, first // step + j))],
        [
            pl.BlockSpec((4 * rows, width), lambda j: (0, 0)),
            pl.BlockSpec((4 * rows, step), lambda j: (0, j)),
        ],
        [shape((4 * rows, width)), shape((4 * rows, columns))],
        [*pieces, weight],
        name,
        flops=8 * rows * width * columns,
        size=2 * width * (columns + 8 * rows),
        scratch=[pltpu.SemaphoreType.DMA((5,))],
    )


def mm_scatter(values, weight):
    partial = mm_t(values, weight).astype(BF)
    rows = partial.shape[0] // 4
    cuts = [0, rows, 2 * rows, 3 * rows, 3 * rows + rows // 2, 4 * rows]
    return scatter_tokens([partial[a:b] for a, b in zip(cuts, cuts[1:])])


def normalize(values):
    centred = values - jnp.mean(values, axis=-1, keepdims=True)
    inv_std = lax.rsqrt(jnp.mean(centred * centred, axis=-1, keepdims=True) + EPS)
    return centred * inv_std, inv_std


NORM_ROWS = 32


def row_spec(array, at=None):
    width = array.shape[-1]
    if at is None:
        return pl.BlockSpec((NORM_ROWS, width), lambda i: (i, 0))
    return pl.BlockSpec((1, NORM_ROWS, width), lambda i, at=at: (at, i, 0))


def terms_of(terms):
    arrays, specs = [], []
    for term in terms:
        array, at = term if isinstance(term, tuple) else (term, None)
        arrays.append(array)
        specs.append(row_spec(array, at))
    return arrays, specs


def total_of(refs):
    values = [ref[0] if len(ref.shape) == 3 else ref[...] for ref in refs]
    return sum(value.astype(F32) for value in values)


def add_norm(terms, gain):
    arrays, specs = terms_of(terms)
    tokens, width = arrays[0].shape[-2], arrays[0].shape[-1]
    tokens = min(a.shape[-2] for a in arrays)

    def kernel(*refs):
        gain_ref, x, out = refs[-3:]
        values = total_of(refs[:-3])
        x[...] = values
        out[...] = (normalize(values)[0] * gain_ref[...]).astype(BF)

    return call(
        kernel,
        (tokens // NORM_ROWS,),
        specs + [whole(gain)],
        [row_spec(shape((tokens, width)))] * 2,
        [shape((tokens, width), F32), shape((tokens, width))],
        [*arrays, gain],
        "add_norm",
    )


def norm_grad(grad, values, gain):
    normed, inv_std = normalize(values)
    scaled = grad * gain
    first_mean = jnp.mean(scaled, axis=-1, keepdims=True)
    second_mean = jnp.mean(scaled * normed, axis=-1, keepdims=True)
    return (
        inv_std * (scaled - first_mean - normed * second_mean),
        jnp.sum(grad * normed, axis=0, keepdims=True),
    )


def accumulate(ref, value):
    @pl.when(pl.program_id(0) == 0)
    def _():
        ref[...] = jnp.zeros_like(ref)

    ref[...] += value


def norm_back(terms, upper, values, gain):
    arrays, specs = terms_of(terms)
    tokens, width = values.shape

    def kernel(*refs):
        upper_ref, x, gain_ref, out, out_low, gain_grad = refs[-6:]
        back, part = norm_grad(total_of(refs[:-6]), x[...], gain_ref[...])
        result = upper_ref[...].astype(F32) + back
        out[...] = result
        out_low[...] = result.astype(BF)
        accumulate(gain_grad, part)

    return call(
        kernel,
        (tokens // NORM_ROWS,),
        specs + [row_spec(upper), row_spec(values), whole(gain)],
        [row_spec(values)] * 2 + [pl.BlockSpec((1, width), lambda i: (0, 0))],
        [shape((tokens, width), F32), shape((tokens, width)), shape((1, width), F32)],
        [*arrays, upper, values, gain],
        "norm_back",
    )


def last_back(terms, upper, values, gain, masked, unit, order):
    arrays, specs = terms_of(terms)
    tokens, width = values.shape

    def kernel(*refs):
        upper_ref, x, gain_ref, mask, out, gain_grad, mask_grad = refs[-7:]
        back, part = norm_grad(total_of(refs[:-7]), x[...], gain_ref[...])
        result = upper_ref[...].astype(F32) + back
        hit = mask[...] > 0.5
        out[...] = reorder(jnp.where(hit, 0.0, result).astype(BF), unit, order)
        accumulate(gain_grad, part)
        accumulate(mask_grad, jnp.sum(jnp.where(hit, result, 0.0), axis=0, keepdims=True))

    line = pl.BlockSpec((1, width), lambda i: (0, 0))
    return call(
        kernel,
        (tokens // NORM_ROWS,),
        specs + [row_spec(upper), row_spec(values), whole(gain), row_spec(masked)],
        [row_spec(values), line, line],
        [shape((tokens, width)), shape((1, width), F32), shape((1, width), F32)],
        [*arrays, upper, values, gain, masked],
        "last_back",
    )


def start(hidden, cotangent, masked, embed, gain, unit, order):
    tokens, width = hidden.shape

    def kernel(hid, cot, mask, embed_ref, gain_ref, x, out, grad):
        hit = mask[...] > 0.5
        values = jnp.where(
            hit, embed_ref[...], reorder(hid[...], unit, order).astype(F32)
        )
        x[...] = values
        out[...] = (normalize(values)[0] * gain_ref[...]).astype(BF)
        grad[...] = jnp.where(hit, reorder(cot[...], unit, order).astype(F32), 0.0).astype(BF)

    rows = row_spec(hidden)
    return call(
        kernel,
        (tokens // NORM_ROWS,),
        [rows, rows, row_spec(masked), whole(embed), whole(gain)],
        [rows] * 3,
        [shape((tokens, width), F32), shape((tokens, width)), shape((tokens, width))],
        [hidden, cotangent, masked, embed, gain],
        "start",
    )


def layer_output(upper, terms, unit, order):
    arrays, specs = terms_of(terms)
    tokens, width = upper.shape

    def kernel(*refs):
        values = refs[-2][...] + total_of(refs[:-2])
        refs[-1][...] = reorder(values.astype(BF), unit, order)

    return call(
        kernel,
        (tokens // NORM_ROWS,),
        specs + [row_spec(upper)],
        row_spec(upper),
        shape((tokens, width)),
        [*arrays, upper],
        "layer_output",
    )


def feed_up(pieces, weight):
    rows, width = pieces[0].shape
    hidden = weight.shape[1]
    step = 256

    def kernel(*refs):
        up, tokens, act, slope, sems = refs[5:]

        @pl.when(pl.program_id(0) == 0)
        def _():
            assemble(tokens, refs[:5], sems)

        u = mm(tokens[...], up[...])
        square = u * u
        bend = jnp.tanh(SLOPE * u * (1.0 + CUBIC * square))
        half = 0.5 * (1.0 + bend)
        act[...] = (u * half).astype(BF)
        slope[...] = half + 0.5 * u * (1.0 - bend * bend) * SLOPE * (1.0 + 3.0 * CUBIC * square)

    part = pl.BlockSpec((4 * rows, step), lambda j: (0, j))
    return call(
        kernel,
        (hidden // step,),
        [ANY] * 5 + [pl.BlockSpec((width, step), lambda j: (0, j))],
        [pl.BlockSpec((4 * rows, width), lambda j: (0, 0)), part, part],
        [shape((4 * rows, width)), shape((4 * rows, hidden)), shape((4 * rows, hidden), F32)],
        [*pieces, weight],
        "feed_up",
        scratch=[pltpu.SemaphoreType.DMA((5,))],
        flops=8 * rows * width * hidden,
        size=2 * width * (hidden + 8 * rows),
    )


def feed_down(grad_y, slope, weight):
    tokens, width = grad_y.shape
    hidden = weight.shape[1]
    step = 256

    def kernel(dy, slope_ref, down, out):
        out[...] = (mm(dy[...], down[...]) * slope_ref[...]).astype(BF)

    part = pl.BlockSpec((tokens, step), lambda j: (0, j))
    return call(
        kernel,
        (hidden // step,),
        [whole(grad_y), part, pl.BlockSpec((width, step), lambda j: (0, j))],
        part,
        shape((tokens, hidden)),
        [grad_y, slope, weight],
        "feed_down",
        flops=2 * tokens * width * hidden,
        size=2 * width * (hidden + 8 * tokens),
    )


def softmax(scores):
    exp_terms = jnp.exp(scores - jnp.max(scores, axis=-1, keepdims=True))
    return exp_terms / jnp.sum(exp_terms, axis=-1, keepdims=True)


def score_grad(probs, grad_probs):
    return (
        probs * (grad_probs - jnp.sum(probs * grad_probs, axis=-1, keepdims=True))
    ).astype(BF)


def head(ref, k):
    return ref[:, k * HD : (k + 1) * HD]


def self_forward(projected, images):
    tokens, width = projected.shape
    rows, group = tokens // images, width // 3
    heads = group // HD

    def kernel(proj, mixed):
        for k in range(heads):
            query, key, value = (head(proj, j * heads + k) for j in range(3))
            probs = softmax(mm_t(query, key) * SCALE).astype(BF)
            mixed[:, k * HD : (k + 1) * HD] = mm(probs, value).astype(BF)

    return call(
        kernel,
        (images,),
        [pl.BlockSpec((rows, width), lambda i: (i, 0))],
        pl.BlockSpec((rows, group), lambda i: (i, 0)),
        shape((tokens, group)),
        [projected],
        "self_forward",
        flops=4 * tokens * rows * group,
    )


def self_back(projected, grad_mixed, images):
    tokens, width = projected.shape
    rows, group = tokens // images, width // 3
    heads = group // HD

    def kernel(proj, grad, out):
        for k in range(heads):
            query, key, value = (head(proj, j * heads + k) for j in range(3))
            grad_head = head(grad, k)
            probs = softmax(mm_t(query, key) * SCALE)
            grad_scores = score_grad(probs, mm_t(grad_head, value))
            parts = (
                mm(grad_scores, key) * SCALE,
                t_mm(grad_scores, query) * SCALE,
                t_mm(probs.astype(BF), grad_head),
            )
            for j, part in enumerate(parts):
                at = (j * heads + k) * HD
                out[:, at : at + HD] = part.astype(BF)

    return call(
        kernel,
        (images,),
        [
            pl.BlockSpec((rows, width), lambda i: (i, 0)),
            pl.BlockSpec((rows, group), lambda i: (i, 0)),
        ],
        pl.BlockSpec((rows, width), lambda i: (i, 0)),
        shape((tokens, width)),
        [projected, grad_mixed],
        "self_back",
        flops=10 * tokens * rows * group,
    )


def cross_forward(queries, text_kv):
    tokens, group = queries.shape
    heads = group // HD

    def kernel(query, text, mixed):
        for k in range(heads):
            probs = softmax(mm_t(head(query, k), head(text, k)) * SCALE).astype(BF)
            mixed[:, k * HD : (k + 1) * HD] = mm(probs, head(text, heads + k)).astype(BF)

    return call(
        kernel,
        (1,),
        [whole(queries), whole(text_kv)],
        whole(queries),
        shape((tokens, group)),
        [queries, text_kv],
        "cross_forward",
        flops=4 * tokens * text_kv.shape[0] * group,
    )


def cross_back(queries, text_kv, grad_mixed):
    tokens, group = queries.shape
    context = text_kv.shape[0]
    heads = group // HD

    def kernel(query, text, grad, grad_query, grad_text):
        for k in range(heads):
            query_head, key, value = head(query, k), head(text, k), head(text, heads + k)
            grad_head = head(grad, k)
            probs = softmax(mm_t(query_head, key) * SCALE)
            grad_scores = score_grad(probs, mm_t(grad_head, value))
            grad_query[:, k * HD : (k + 1) * HD] = (mm(grad_scores, key) * SCALE).astype(BF)
            at = (heads + k) * HD
            grad_text[:, k * HD : (k + 1) * HD] = t_mm(grad_scores, query_head) * SCALE
            grad_text[:, at : at + HD] = t_mm(probs.astype(BF), grad_head)

    return call(
        kernel,
        (1,),
        [whole(queries), whole(text_kv), whole(grad_mixed)],
        [whole(queries), whole(text_kv)],
        [shape((tokens, group)), shape((context, 2 * group), F32)],
        [queries, text_kv, grad_mixed],
        "cross_back",
        flops=10 * tokens * context * group,
    )


def grad_products(pairs, name, core=None, blocks=0):
    count_in = len(pairs[0][0])
    tokens, width = pairs[0][0][0].shape
    widths = [y[0].shape[1] for _, y in pairs]
    total = sum(widths)
    rows = 256 if core is None else width // (2 * blocks)
    steps = width // rows if core is None else blocks
    step = 512
    count = len(pairs) * count_in

    def kernel(r, *refs):
        out = refs[2 * count]
        offset = 0
        for k, wide in enumerate(widths):
            left = [refs[k * count_in + b][...].T for b in range(count_in)]
            for at in range(0, wide, step):
                out[:, offset + at : offset + at + step] = sum(
                    mm(left[b], refs[count + k * count_in + b][:, at : at + step])
                    for b in range(count_in)
                ).astype(BF)
            offset += wide

    pick = (lambda i, r: (0, i)) if core is None else (lambda i, r: (0, 2 * i + r[0]))
    return call(
        kernel,
        (steps,),
        [pl.BlockSpec((tokens, rows), pick)] * count
        + [pl.BlockSpec((tokens, w), lambda i, r: (0, 0)) for w in widths for _ in range(count_in)],
        pl.BlockSpec((rows, total), lambda i, r: (i, 0)),
        shape((steps * rows, total)),
        [b for x, _ in pairs for b in x] + [b for _, y in pairs for b in y],
        name,
        flops=2 * tokens * count_in * steps * rows * total,
        size=4 * width * total,
        rank=jnp.zeros((), jnp.int32) if core is None else core,
    )


def pick_weights(three, one, rank):
    rows, width = one.shape[0], one.shape[1] // 4

    def kernel(r, three_ref, one_ref, *outs):
        for k in range(4):

            @pl.when(pl.program_id(0) == k)
            def _():
                for j in range(3):
                    outs[k][:, j * width : (j + 1) * width] = three_ref[j]
                outs[k][:, 3 * width :] = one_ref[...]

    outs = [shape((rows, 4 * width))] * 4
    return call(
        kernel,
        (4,),
        [
            pl.BlockSpec((3, rows, width), lambda k, r: (0, 0, k ^ r[0])),
            pl.BlockSpec((rows, width), lambda k, r: (0, k ^ r[0])),
        ],
        [whole(a) for a in outs],
        outs,
        [three, one],
        "pick_weights",
        rank=rank,
    )


def pick_rows(arrays, rank):
    rows = arrays[0].shape[1]
    widths = [a.shape[2] for a in arrays]
    count = len(arrays)

    def kernel(r, *refs):
        for k in range(4):

            @pl.when(pl.program_id(0) == k)
            def _():
                at = 0
                for ref, width in zip(refs, widths):
                    refs[count + k][:, at : at + width] = ref[0]
                    at += width

    outs = [shape((rows, sum(widths)))] * 4
    return call(
        kernel,
        (4,),
        [pl.BlockSpec((1, rows, w), lambda k, r: (k ^ r[0], 0, 0)) for w in widths],
        [whole(a) for a in outs],
        outs,
        arrays,
        "pick_rows",
        rank=rank,
    )


def place(parts, rank):
    def kernel(r, *refs):
        for k in range(4):

            @pl.when(pl.program_id(0) == k)
            def _():
                refs[4][0] = refs[k][...]

    rows, columns = parts[0].shape
    return call(
        kernel,
        (4,),
        [whole(p) for p in parts],
        pl.BlockSpec((1, rows, columns), lambda k, r: (k ^ r[0], 0, 0)),
        shape((4, rows, columns)),
        parts,
        "place",
        rank=rank,
    )


def finish_wide(parts, rank):
    rows, total = parts[0].shape
    width = total // 2

    def kernel(r, *refs):
        for k in range(4):

            @pl.when(pl.program_id(0) == k)
            def _():
                refs[4][...] = refs[k][:, :width].astype(F32)
                refs[5][...] = refs[k][:, width:].astype(F32)

    flat = pl.BlockSpec((rows, width), lambda k, r: (0, k ^ r[0]))
    return call(
        kernel,
        (4,),
        [whole(p) for p in parts],
        [flat, flat],
        [shape((rows, 4 * width), F32)] * 2,
        parts,
        "finish_wide",
        rank=rank,
    )


def finish_all(parts, text_grad, rank):
    rows, total = parts[0].shape
    width = total // 6

    def kernel(r, *refs):
        key, value, three, out, cross, cross_out = refs[4:]
        for k in range(4):

            @pl.when(pl.program_id(0) == k)
            def _():
                def part(j):
                    return refs[k][:, j * width : (j + 1) * width].astype(F32)

                for j in range(3):
                    three[j] = part(j)
                out[...] = part(3)
                cross[0] = part(4)
                cross_out[...] = part(5)

        cross[1] = key[...]
        cross[2] = value[...]

    wide = pl.BlockSpec((3, rows, width), lambda k, r: (0, 0, k ^ r[0]))
    flat = pl.BlockSpec((rows, width), lambda k, r: (0, k ^ r[0]))
    return call(
        kernel,
        (4,),
        [whole(p) for p in parts]
        + [flat, pl.BlockSpec((rows, width), lambda k, r: (0, 4 + (k ^ r[0])))],
        [wide, flat, wide, flat],
        [shape((3, rows, 4 * width), F32), shape((rows, 4 * width), F32)] * 2,
        [*parts, text_grad, text_grad],
        "finish_all",
        rank=rank,
    )


def plane_block(k):
    return (k >> 1) & 1, (k >> 2) * 2 + (k & 1)


def text_forward(caption, w_text, w_cross):
    context, rows = caption.shape[0], w_text.shape[0]
    half, width = context // 2, w_cross.shape[2] // 4

    def kernel(cap, weight, cross, own, blocks):
        own[...] = mm_t(cap[...], weight[...]).astype(BF)
        for j in range(2):
            part = mm(own[...], cross[1 + j]).astype(BF)
            for k in range(8):
                core, group = plane_block(k)
                blocks[k, :, j * width : (j + 1) * width] = part[
                    core * half : (core + 1) * half, group * width : (group + 1) * width
                ]

    return call(
        kernel,
        (1,),
        [whole(caption), whole(w_text), whole(w_cross)],
        [
            pl.BlockSpec((context, rows), lambda i: (0, 0)),
            pl.BlockSpec((8, half, 2 * width), lambda i: (0, 0, 0)),
        ],
        [shape((context, rows)), shape((8, half, 2 * width))],
        [caption, w_text, w_cross],
        "text_forward",
    )


def text_back(blocks, own_text, w_cross, caption, w_text, extra):
    context, rows = own_text.shape
    half, width = context // 2, w_cross.shape[2] // 4
    wide = caption.shape[1] // 4
    tail = extra.shape[0]

    def kernel(block, own, cross, cap, weight, more, kv_grad, text_grad, out, grads):
        for k in range(8):
            core, group = plane_block(k)
            for j in range(2):
                at = (4 * j + group) * width
                grads[core * half : (core + 1) * half, at : at + width] = block[
                    k, :, j * width : (j + 1) * width
                ]
        kv_grad[...] = t_mm(own[...], grads[...])
        grad_text = sum(
            mm_t(grads[:, 4 * j * width : 4 * (j + 1) * width], cross[1 + j]) for j in range(2)
        ).astype(BF)
        text_grad[...] = t_mm(grad_text, cap[...])
        part = mm(grad_text, weight[...]).astype(BF)
        for k in range(8):
            core, group = plane_block(k)
            out[k, :half, :] = part[core * half : (core + 1) * half, group * wide : (group + 1) * wide]
            out[k, half:, :] = more[...]

    operands = [blocks, own_text, w_cross, caption, w_text, extra]
    outs = [
        shape((rows, 8 * width), F32),
        shape((rows, 4 * wide), F32),
        shape((8, half + tail, wide)),
    ]
    return call(
        kernel,
        (1,),
        [whole(a) for a in operands],
        [whole(a) for a in outs],
        outs,
        operands,
        "text_back",
        scratch=[pltpu.VMEM((context, 8 * width), BF)],
    )


def caption_output(blocks):
    count, half, wide = blocks.shape

    def kernel(block, out):
        out[...] = block[0].astype(F32)

    return call(
        kernel,
        (count,),
        [pl.BlockSpec((1, half, wide), lambda k: (k, 0, 0))],
        pl.BlockSpec((half, wide), lambda k: plane_block(k)),
        shape((2 * half, 4 * wide), F32),
        [blocks],
        "caption_output",
    )


def column_blocks(weight, count):
    rows = weight.shape[0]
    return weight.reshape(rows, count, -1).transpose(1, 0, 2)


def halves_of(values, width):
    high = values.astype(BF)
    low = (values - high.astype(F32)).astype(BF)
    return jnp.concatenate([high.reshape(-1, width), low.reshape(-1, width)], axis=0)


def whole_of(halves, width):
    rows = halves.shape[0] // 2
    return (halves[:rows] + halves[rows:]).reshape(-1, width)


def make_local(z_size):
    def sum_z(values):
        parts = values.reshape(z_size, -1, values.shape[-1])
        mine = trade(parts, "z").astype(F32).sum(axis=0).astype(BF)
        return spread(mine, "z", z_size).reshape(values.shape)

    def add_z(values):
        step = 1
        while step < z_size:
            values = values + lax.ppermute(
                values, "z", tuple((k, k ^ step) for k in range(z_size))
            )
            step *= 2
        return values

    def layer_order(values):
        shaped = values.reshape(values.shape[:-1] + (z_size, 2, 2, -1))
        return jnp.swapaxes(shaped, -3, -2).reshape(values.shape)

    def local(
        hidden,
        mask_index,
        mask_count,
        mask_embed,
        norm_gains,
        caption,
        w_qkv,
        w_out,
        w_cross,
        w_cross_out,
        w_text,
        w_up,
        w_down,
        cotangent,
    ):
        images, local_rows, width = hidden.shape
        full_length = mask_index.shape[1]
        rank = lax.axis_index("x") * 2 + lax.axis_index("y")
        core = lax.axis_index("c")
        tokens = images * local_rows
        group = width // 4
        text_width = caption.shape[1]

        unit = width // (4 * z_size)
        inside = unit % 128 == 0
        order = [4 * k + j for k in range(z_size) for j in (0, 2, 1, 3)] if inside else None

        def outer(values):
            return values if inside else layer_order(values)

        w_qkv, w_cross = w_qkv.transpose(1, 0, 2), w_cross.transpose(1, 0, 2)
        first = swap_parts(pick_weights(w_qkv, w_out, rank))
        first = gather_rows(place(first, rank))

        positions = lax.axis_index("y") * local_rows + jnp.arange(local_rows, dtype=jnp.int32)
        ranks = jnp.arange(full_length, dtype=jnp.int32)
        matches = (mask_index[:, :, None] == positions[None, None, :]) & (
            ranks[None, :, None] < mask_count[:, None, None]
        )
        masked = jnp.any(matches, axis=1).reshape(tokens, 1).astype(F32)
        gains = layer_order(norm_gains)
        gain_a, gain_b, gain_c = gains[:1], gains[1:2], gains[2:]
        start_x, attn_in, grad_top = start(
            outer(hidden.reshape(tokens, width)),
            outer(cotangent.reshape(tokens, width)),
            masked,
            layer_order(mask_embed)[None],
            gain_a,
            unit,
            order,
        )
        attn_in = gather_tokens(attn_in)
        mid = jnp.concatenate([column_blocks(w_cross[0], 4), column_blocks(w_cross_out, 4)], axis=2)
        up = column_blocks(w_up, 4)
        attn_in, mid, up = lax.optimization_barrier((attn_in, mid, up))
        mid, up = gather_rows(trade(mid)), gather_rows(trade(up))

        own_text, kv_part = text_forward(caption, w_text, w_cross)
        text_kv = trade(kv_part, PLANE).astype(F32).sum(axis=0).astype(BF)
        text_kv = sum_z(text_kv)
        other = swap(text_kv, "c")
        text_kv = jnp.concatenate(
            [jnp.where(core == 0, text_kv, other), jnp.where(core == 0, other, text_kv)], axis=0
        )
        attn_in, text_kv = lax.optimization_barrier((attn_in, text_kv))

        attn_in, projected = gather_mm(attn_in, first, 0, 3 * group, "qkv_mm")
        self_mixed = self_forward(projected, 2 * images)
        down = column_blocks(w_down, 4)
        self_mixed, down = lax.optimization_barrier((self_mixed, down))
        down = gather_rows(trade(down))
        parts = mm_scatter(self_mixed, first[:, 3 * group :])
        after_attn, cross_in = add_norm([start_x] + parts, gain_b)

        cross_in, cross_queries = gather_mm(gather_tokens(cross_in), mid, 0, group, "query_mm")
        cross_mixed = cross_forward(cross_queries, text_kv)
        parts = mm_scatter(cross_mixed, mid[:, group:])
        after_cross, mlp_in = add_norm([after_attn] + parts, gain_c)

        mlp_in = gather_tokens(mlp_in)
        mlp_in, grad_top = lax.optimization_barrier((mlp_in, grad_top))
        grad_y = jnp.concatenate(gather_tokens(grad_top), axis=0)
        mlp_in, activated, slope = feed_up(mlp_in, up)
        early = [attn_in, self_mixed, cross_in, cross_mixed]
        if inside:
            grad_axes, halves = "z", (core, z_size)

            def both(values):
                return [values, swap(values, "c")]

        else:
            grad_axes, halves = DATA, ()

            def both(values):
                return [values]

        early = [both(values) for values in early]
        down_part = grad_products([(both(grad_y), both(activated))], "down_grads", *halves)
        mlp_in = both(mlp_in)
        slope, down_part, early, mlp_in = lax.optimization_barrier((slope, down_part, early, mlp_in))
        down_rows = scatter_grad(down_part, grad_axes)
        grad_pre = feed_down(grad_y, slope, down)
        parts = mm_scatter(grad_pre, up)
        up_part = grad_products([(mlp_in, both(grad_pre))], "up_grads", *halves)
        grad_after_cross, cross_branch, gain_grad_c = norm_back(
            parts, grad_top, after_cross, gain_c
        )

        cross_branch = gather_tokens(cross_branch)
        cross_branch, up_part = lax.optimization_barrier((cross_branch, up_part))
        cross_branch, grad_cross_mixed = gather_mm(
            cross_branch, mid, group, group, "cross_out_back"
        )
        grad_cq, kv_grad = cross_back(cross_queries, text_kv, grad_cross_mixed)
        up_part, down_rows, kv_grad = lax.optimization_barrier((up_part, down_rows, kv_grad))
        up_rows = scatter_grad(up_part, grad_axes)
        cross_branch, grad_cq_both = both(cross_branch), both(grad_cq)
        kv_part = kv_grad.astype(BF).reshape(2, z_size, -1, 2 * group)
        kv_part = kv_part.transpose(1, 0, 2, 3).reshape(2 * z_size, -1, 2 * group)
        parts = mm_scatter(grad_cq, mid[:, :group])
        kv_part = trade(kv_part, DATA).astype(F32).sum(axis=0).astype(BF)
        parts, kv_part = lax.optimization_barrier((parts, kv_part))
        grad_after_attn, attn_branch, gain_grad_b = norm_back(
            parts, grad_after_cross, after_attn, gain_b
        )

        attn_branch = gather_tokens(attn_branch)
        kv_part = spread(kv_part, "z", z_size).reshape(-1, 2 * group)
        attn_branch, kv_part = lax.optimization_barrier((attn_branch, kv_part))
        attn_branch, grad_self_mixed = gather_mm(attn_branch, first, 3 * group, group, "out_back")
        grad_projected = self_back(projected, grad_self_mixed, 2 * images)
        kv_grads = spread(kv_part, PLANE, 8)
        grad_projected, kv_grads = lax.optimization_barrier((grad_projected, kv_grads))
        rest_part = grad_products(
            [
                (early[0], both(grad_projected)),
                (both(attn_branch), early[1]),
                (early[2], grad_cq_both),
                (cross_branch, early[3]),
            ],
            "attention_grads",
            *halves,
        )
        grad_projected, activated, rest_part = lax.optimization_barrier(
            (grad_projected, activated, rest_part)
        )
        rest_part, up_rows = lax.optimization_barrier((rest_part, up_rows))
        rest_rows = scatter_grad(rest_part, grad_axes)
        parts = mm_scatter(grad_projected, first[:, : 3 * group])
        grad_hidden, gain_grad_a, mask_grad = last_back(
            parts,
            grad_after_attn,
            start_x,
            gain_a,
            masked,
            unit,
            order,
        )
        sums = jnp.concatenate([gain_grad_a, gain_grad_b, gain_grad_c, mask_grad], axis=0)

        result = mm_scatter(activated, down)

        wide_rows = swap_parts(pick_rows([down_rows, up_rows], rank))
        kv_weight_grad, grad_text_w, caption_part = text_back(
            kv_grads, own_text, w_cross, caption, w_text, halves_of(sums, text_width // 4)
        )
        half_context = caption.shape[0] // 2
        caption_part = trade(caption_part, PLANE).astype(F32).sum(axis=0)
        sums = layer_order(add_z(whole_of(caption_part[half_context:], width)))
        caption_part = sum_z(caption_part[:half_context].astype(BF))
        output = layer_output(after_cross, result, unit, order)
        down_grad, up_grad = finish_wide(wide_rows, rank)
        caption_part, rest_rows, sums, output, down_grad, up_grad = lax.optimization_barrier(
            (caption_part, rest_rows, sums, output, down_grad, up_grad)
        )
        grad_caption = caption_output(spread(caption_part, PLANE, 8))

        qkv_grad, out_grad, grad_cross, cross_out_grad = finish_all(
            swap_parts(pick_rows([rest_rows], rank)), kv_weight_grad, rank
        )
        return (
            outer(output).reshape(hidden.shape),
            outer(grad_hidden).reshape(hidden.shape),
            grad_caption,
            sums[:3],
            sums[3],
            qkv_grad.transpose(1, 0, 2),
            out_grad,
            grad_cross.transpose(1, 0, 2),
            cross_out_grad,
            grad_text_w,
            up_grad,
            down_grad,
        )

    return local


def solution(mesh):
    z_size = mesh.shape["img"] // 4
    inner = Mesh(mesh.devices.reshape(z_size, 2, 2, 2), ("z", "x", "c", "y"))
    image = ("z", "x", "c")
    tokens = P(image, "y", None)
    rows = P(image + ("y",))
    in_specs = (tokens, P(image, None), P(image), P(), P(), P()) + (rows,) * 7 + (tokens,)
    out_specs = (tokens, tokens, P(), P(), P()) + (rows,) * 7
    return jax.shard_map(
        make_local(z_size), mesh=inner, in_specs=in_specs, out_specs=out_specs, check_vma=False
    )
```

```python
import math

import jax
import jax.numpy as jnp
from jax import lax
from jax.experimental import pallas as pl
from jax.experimental.pallas import tpu as pltpu
from jax.sharding import Mesh
from jax.sharding import PartitionSpec as P

HD = 128
EPS = 1e-05
BF = jnp.bfloat16
F32 = jnp.float32
PAIR = ((0, 1), (1, 0))
GROUP = ("x", "y")
DATA = ("z", "c")
PLANE = ("x", "c", "y")
VMEM = 48 * 1024 * 1024
SCALE = 1.0 / math.sqrt(HD)
SLOPE = math.sqrt(2.0 / math.pi)
CUBIC = 0.044715


def dot(a, b, dims):
    return lax.dot_general(a, b, (dims, ((), ())), preferred_element_type=F32)


def mm(a, b):
    return dot(a, b, ((1,), (0,)))


def mm_t(a, b):
    return dot(a, b, ((1,), (1,)))


def t_mm(a, b):
    return dot(a, b, ((0,), (0,)))


def shape(dims, dtype=BF):
    return jax.ShapeDtypeStruct(dims, dtype)


def swap(values, axis):
    return lax.ppermute(values, axis, PAIR)


def trade(blocks, axes=GROUP):
    return lax.all_to_all(blocks, axes, 0, 0, tiled=True)


def spread(values, axes=GROUP, count=4):
    return trade(jnp.broadcast_to(values[None], (count,) + values.shape), axes)


def gather_tokens(own):
    half = own.shape[0] // 2
    from_x = swap(own, "x")
    from_y = swap(own, "y")
    return own, from_y, from_x, swap(from_x[:half], "y"), swap(from_y[half:], "x")


def scatter_first(parts):
    own, for_y, for_x, for_low, for_high = parts
    half = for_low.shape[0]
    low = swap(for_low, "y").astype(F32) + for_x[:half].astype(F32)
    high = swap(for_high, "x").astype(F32) + for_y[half:].astype(F32)
    return (
        own,
        jnp.concatenate([low.astype(BF), for_x[half:]], axis=0),
        jnp.concatenate([for_y[:half], high.astype(BF)], axis=0),
    )


def scatter_second(parts):
    own, for_x, for_y = parts
    return [own, swap(for_x, "x"), swap(for_y, "y")]


def scatter_tokens(parts):
    return scatter_second(scatter_first(parts))


def swap_parts(parts):
    return [
        parts[0],
        swap(parts[1], "y"),
        swap(parts[2], "x"),
        lax.ppermute(parts[3], GROUP, ((0, 3), (1, 2), (2, 1), (3, 0))),
    ]


def gather_rows(rows):
    return lax.all_gather(rows.reshape(-1, rows.shape[-1]), DATA, axis=0, tiled=True)


def scatter_grad(partial, axes):
    summed = lax.psum_scatter(partial, axes, scatter_dimension=0, tiled=True)
    return summed.reshape(4, -1, summed.shape[-1])


def call(kernel, grid, in_specs, out_specs, out_shape, operands, name, flops=0, size=1 << 22,
         rank=None, scratch=()):
    options = dict(
        out_shape=out_shape,
        compiler_params=pltpu.CompilerParams(vmem_limit_bytes=VMEM),
        cost_estimate=pl.CostEstimate(flops=flops, bytes_accessed=size, transcendentals=0),
        name=name,
    )
    if rank is None:
        return pl.pallas_call(
            kernel, grid=grid, in_specs=in_specs, out_specs=out_specs, scratch_shapes=scratch,
            **options,
        )(*operands)
    spec = pltpu.PrefetchScalarGridSpec(
        num_scalar_prefetch=1,
        grid=grid,
        in_specs=in_specs,
        out_specs=out_specs,
        scratch_shapes=scratch,
    )
    return pl.pallas_call(kernel, grid_spec=spec, **options)(rank.reshape(1), *operands)


def whole(array):
    return pl.BlockSpec(array.shape, lambda *_: (0,) * len(array.shape))


def reorder(values, unit, order):
    if order is None:
        return values
    return jnp.concatenate([values[:, k * unit : (k + 1) * unit] for k in order], axis=1)


def assemble(target, pieces, sems):
    copies, at = [], 0
    for k, piece in enumerate(pieces):
        rows = piece.shape[0]
        copies.append(pltpu.make_async_copy(piece, target.at[at : at + rows], sems.at[k]))
        at += rows
    for copy in copies:
        copy.start()
    for copy in copies:
        copy.wait()


ANY = pl.BlockSpec(memory_space=pl.ANY)


def gather_mm(pieces, weight, first, columns, name):
    rows, width = pieces[0].shape
    step = 256

    def kernel(*refs):
        tokens, out, sems = refs[6:]

        @pl.when(pl.program_id(0) == 0)
        def _():
            assemble(tokens, refs[:5], sems)

        out[...] = mm(tokens[...], refs[5][...]).astype(BF)

    return call(
        kernel,
        (columns // step,),
        [ANY] * 5 + [pl.BlockSpec((width, step), lambda j: (0, first // step + j))],
        [
            pl.BlockSpec((4 * rows, width), lambda j: (0, 0)),
            pl.BlockSpec((4 * rows, step), lambda j: (0, j)),
        ],
        [shape((4 * rows, width)), shape((4 * rows, columns))],
        [*pieces, weight],
        name,
        flops=8 * rows * width * columns,
        size=2 * width * (columns + 8 * rows),
        scratch=[pltpu.SemaphoreType.DMA((5,))],
    )


def mm_scatter(values, weight):
    return scatter_tokens(token_blocks(mm_t(values, weight).astype(BF)))


def token_blocks(partial):
    rows = partial.shape[0] // 4
    cuts = [0, rows, 2 * rows, 3 * rows, 3 * rows + rows // 2, 4 * rows]
    return [partial[a:b] for a, b in zip(cuts, cuts[1:])]


def normalize(values):
    centred = values - jnp.mean(values, axis=-1, keepdims=True)
    inv_std = lax.rsqrt(jnp.mean(centred * centred, axis=-1, keepdims=True) + EPS)
    return centred * inv_std, inv_std


NORM_ROWS = 32


def row_spec(array, at=None):
    width = array.shape[-1]
    if at is None:
        return pl.BlockSpec((NORM_ROWS, width), lambda i: (i, 0))
    return pl.BlockSpec((1, NORM_ROWS, width), lambda i, at=at: (at, i, 0))


def terms_of(terms):
    arrays, specs = [], []
    for term in terms:
        array, at = term if isinstance(term, tuple) else (term, None)
        arrays.append(array)
        specs.append(row_spec(array, at))
    return arrays, specs


def total_of(refs):
    values = [ref[0] if len(ref.shape) == 3 else ref[...] for ref in refs]
    return sum(value.astype(F32) for value in values)


def add_norm(terms, gain):
    arrays, specs = terms_of(terms)
    tokens, width = arrays[0].shape[-2], arrays[0].shape[-1]
    tokens = min(a.shape[-2] for a in arrays)

    def kernel(*refs):
        gain_ref, x, out = refs[-3:]
        values = total_of(refs[:-3])
        x[...] = values
        out[...] = (normalize(values)[0] * gain_ref[...]).astype(BF)

    return call(
        kernel,
        (tokens // NORM_ROWS,),
        specs + [whole(gain)],
        [row_spec(shape((tokens, width)))] * 2,
        [shape((tokens, width), F32), shape((tokens, width))],
        [*arrays, gain],
        "add_norm",
    )


def norm_grad(grad, values, gain):
    normed, inv_std = normalize(values)
    scaled = grad * gain
    first_mean = jnp.mean(scaled, axis=-1, keepdims=True)
    second_mean = jnp.mean(scaled * normed, axis=-1, keepdims=True)
    return (
        inv_std * (scaled - first_mean - normed * second_mean),
        jnp.sum(grad * normed, axis=0, keepdims=True),
    )


def accumulate(ref, value):
    @pl.when(pl.program_id(0) == 0)
    def _():
        ref[...] = jnp.zeros_like(ref)

    ref[...] += value


def norm_back(terms, upper, values, gain):
    arrays, specs = terms_of(terms)
    tokens, width = values.shape

    def kernel(*refs):
        upper_ref, x, gain_ref, out, out_low, gain_grad = refs[-6:]
        back, part = norm_grad(total_of(refs[:-6]), x[...], gain_ref[...])
        result = upper_ref[...].astype(F32) + back
        out[...] = result
        out_low[...] = result.astype(BF)
        accumulate(gain_grad, part)

    return call(
        kernel,
        (tokens // NORM_ROWS,),
        specs + [row_spec(upper), row_spec(values), whole(gain)],
        [row_spec(values)] * 2 + [pl.BlockSpec((1, width), lambda i: (0, 0))],
        [shape((tokens, width), F32), shape((tokens, width)), shape((1, width), F32)],
        [*arrays, upper, values, gain],
        "norm_back",
    )


def last_back(terms, upper, values, gain, masked, unit, order):
    arrays, specs = terms_of(terms)
    tokens, width = values.shape

    def kernel(*refs):
        upper_ref, x, gain_ref, mask, out, gain_grad, mask_grad = refs[-7:]
        back, part = norm_grad(total_of(refs[:-7]), x[...], gain_ref[...])
        result = upper_ref[...].astype(F32) + back
        hit = mask[...] > 0.5
        out[...] = reorder(jnp.where(hit, 0.0, result).astype(BF), unit, order)
        accumulate(gain_grad, part)
        accumulate(mask_grad, jnp.sum(jnp.where(hit, result, 0.0), axis=0, keepdims=True))

    line = pl.BlockSpec((1, width), lambda i: (0, 0))
    return call(
        kernel,
        (tokens // NORM_ROWS,),
        specs + [row_spec(upper), row_spec(values), whole(gain), row_spec(masked)],
        [row_spec(values), line, line],
        [shape((tokens, width)), shape((1, width), F32), shape((1, width), F32)],
        [*arrays, upper, values, gain, masked],
        "last_back",
    )


def start(hidden, cotangent, masked, embed, gain, unit, order):
    tokens, width = hidden.shape

    def kernel(hid, cot, mask, embed_ref, gain_ref, x, out, grad):
        hit = mask[...] > 0.5
        values = jnp.where(
            hit, embed_ref[...], reorder(hid[...], unit, order).astype(F32)
        )
        x[...] = values
        out[...] = (normalize(values)[0] * gain_ref[...]).astype(BF)
        grad[...] = jnp.where(hit, reorder(cot[...], unit, order).astype(F32), 0.0).astype(BF)

    rows = row_spec(hidden)
    return call(
        kernel,
        (tokens // NORM_ROWS,),
        [rows, rows, row_spec(masked), whole(embed), whole(gain)],
        [rows] * 3,
        [shape((tokens, width), F32), shape((tokens, width)), shape((tokens, width))],
        [hidden, cotangent, masked, embed, gain],
        "start",
    )


def layer_output(upper, terms, unit, order):
    arrays, specs = terms_of(terms)
    tokens, width = upper.shape

    def kernel(*refs):
        values = refs[-2][...] + total_of(refs[:-2])
        refs[-1][...] = reorder(values.astype(BF), unit, order)

    return call(
        kernel,
        (tokens // NORM_ROWS,),
        specs + [row_spec(upper)],
        row_spec(upper),
        shape((tokens, width)),
        [*arrays, upper],
        "layer_output",
    )


def feed_up(pieces, weight):
    rows, width = pieces[0].shape
    hidden = weight.shape[1]
    step = 256

    def kernel(*refs):
        up, tokens, act, slope, sems = refs[5:]

        @pl.when(pl.program_id(0) == 0)
        def _():
            assemble(tokens, refs[:5], sems)

        u = mm(tokens[...], up[...])
        square = u * u
        bend = jnp.tanh(SLOPE * u * (1.0 + CUBIC * square))
        half = 0.5 * (1.0 + bend)
        act[...] = (u * half).astype(BF)
        slope[...] = half + 0.5 * u * (1.0 - bend * bend) * SLOPE * (1.0 + 3.0 * CUBIC * square)

    part = pl.BlockSpec((4 * rows, step), lambda j: (0, j))
    return call(
        kernel,
        (hidden // step,),
        [ANY] * 5 + [pl.BlockSpec((width, step), lambda j: (0, j))],
        [pl.BlockSpec((4 * rows, width), lambda j: (0, 0)), part, part],
        [shape((4 * rows, width)), shape((4 * rows, hidden)), shape((4 * rows, hidden), F32)],
        [*pieces, weight],
        "feed_up",
        scratch=[pltpu.SemaphoreType.DMA((5,))],
        flops=8 * rows * width * hidden,
        size=2 * width * (hidden + 8 * rows),
    )


def feed_down(grad_y, slope, weight):
    tokens, width = grad_y.shape
    hidden = weight.shape[1]
    step = 256

    def kernel(dy, slope_ref, down, out):
        out[...] = (mm(dy[...], down[...]) * slope_ref[...]).astype(BF)

    part = pl.BlockSpec((tokens, step), lambda j: (0, j))
    return call(
        kernel,
        (hidden // step,),
        [whole(grad_y), part, pl.BlockSpec((width, step), lambda j: (0, j))],
        part,
        shape((tokens, hidden)),
        [grad_y, slope, weight],
        "feed_down",
        flops=2 * tokens * width * hidden,
        size=2 * width * (hidden + 8 * tokens),
    )


def softmax(scores):
    exp_terms = jnp.exp(scores - jnp.max(scores, axis=-1, keepdims=True))
    return exp_terms / jnp.sum(exp_terms, axis=-1, keepdims=True)


def score_grad(probs, grad_probs):
    return (
        probs * (grad_probs - jnp.sum(probs * grad_probs, axis=-1, keepdims=True))
    ).astype(BF)


def head(ref, k):
    return ref[:, k * HD : (k + 1) * HD]


def self_forward(projected, images):
    tokens, width = projected.shape
    rows, group = tokens // images, width // 3
    heads = group // HD

    def kernel(proj, mixed):
        for k in range(heads):
            query, key, value = (head(proj, j * heads + k) for j in range(3))
            probs = softmax(mm_t(query, key) * SCALE).astype(BF)
            mixed[:, k * HD : (k + 1) * HD] = mm(probs, value).astype(BF)

    return call(
        kernel,
        (images,),
        [pl.BlockSpec((rows, width), lambda i: (i, 0))],
        pl.BlockSpec((rows, group), lambda i: (i, 0)),
        shape((tokens, group)),
        [projected],
        "self_forward",
        flops=4 * tokens * rows * group,
    )


def self_back(projected, grad_mixed, images):
    tokens, width = projected.shape
    rows, group = tokens // images, width // 3
    heads = group // HD

    def kernel(proj, grad, out):
        for k in range(heads):
            query, key, value = (head(proj, j * heads + k) for j in range(3))
            grad_head = head(grad, k)
            probs = softmax(mm_t(query, key) * SCALE)
            grad_scores = score_grad(probs, mm_t(grad_head, value))
            parts = (
                mm(grad_scores, key) * SCALE,
                t_mm(grad_scores, query) * SCALE,
                t_mm(probs.astype(BF), grad_head),
            )
            for j, part in enumerate(parts):
                at = (j * heads + k) * HD
                out[:, at : at + HD] = part.astype(BF)

    return call(
        kernel,
        (images,),
        [
            pl.BlockSpec((rows, width), lambda i: (i, 0)),
            pl.BlockSpec((rows, group), lambda i: (i, 0)),
        ],
        pl.BlockSpec((rows, width), lambda i: (i, 0)),
        shape((tokens, width)),
        [projected, grad_mixed],
        "self_back",
        flops=10 * tokens * rows * group,
    )


def cross_forward(queries, text_kv):
    tokens, group = queries.shape
    heads = group // HD

    def kernel(query, text, mixed):
        for k in range(heads):
            probs = softmax(mm_t(head(query, k), head(text, k)) * SCALE).astype(BF)
            mixed[:, k * HD : (k + 1) * HD] = mm(probs, head(text, heads + k)).astype(BF)

    return call(
        kernel,
        (1,),
        [whole(queries), whole(text_kv)],
        whole(queries),
        shape((tokens, group)),
        [queries, text_kv],
        "cross_forward",
        flops=4 * tokens * text_kv.shape[0] * group,
    )


def cross_back(queries, text_kv, grad_mixed):
    tokens, group = queries.shape
    context = text_kv.shape[0]
    heads = group // HD

    def kernel(query, text, grad, grad_query, grad_text):
        for k in range(heads):
            query_head, key, value = head(query, k), head(text, k), head(text, heads + k)
            grad_head = head(grad, k)
            probs = softmax(mm_t(query_head, key) * SCALE)
            grad_scores = score_grad(probs, mm_t(grad_head, value))
            grad_query[:, k * HD : (k + 1) * HD] = (mm(grad_scores, key) * SCALE).astype(BF)
            at = (heads + k) * HD
            grad_text[:, k * HD : (k + 1) * HD] = t_mm(grad_scores, query_head) * SCALE
            grad_text[:, at : at + HD] = t_mm(probs.astype(BF), grad_head)

    return call(
        kernel,
        (1,),
        [whole(queries), whole(text_kv), whole(grad_mixed)],
        [whole(queries), whole(text_kv)],
        [shape((tokens, group)), shape((context, 2 * group), F32)],
        [queries, text_kv, grad_mixed],
        "cross_back",
        flops=10 * tokens * context * group,
    )


def grad_products(pairs, name, core=None, blocks=0):
    count_in = len(pairs[0][0])
    tokens, width = pairs[0][0][0].shape
    widths = [y[0].shape[1] for _, y in pairs]
    total = sum(widths)
    rows = 256 if core is None else width // (2 * blocks)
    steps = width // rows if core is None else blocks
    step = 512
    count = len(pairs) * count_in

    def kernel(r, *refs):
        out = refs[2 * count]
        offset = 0
        for k, wide in enumerate(widths):
            left = [refs[k * count_in + b][...].T for b in range(count_in)]
            for at in range(0, wide, step):
                out[:, offset + at : offset + at + step] = sum(
                    mm(left[b], refs[count + k * count_in + b][:, at : at + step])
                    for b in range(count_in)
                ).astype(BF)
            offset += wide

    pick = (lambda i, r: (0, i)) if core is None else (lambda i, r: (0, 2 * i + r[0]))
    return call(
        kernel,
        (steps,),
        [pl.BlockSpec((tokens, rows), pick)] * count
        + [pl.BlockSpec((tokens, w), lambda i, r: (0, 0)) for w in widths for _ in range(count_in)],
        pl.BlockSpec((rows, total), lambda i, r: (i, 0)),
        shape((steps * rows, total)),
        [b for x, _ in pairs for b in x] + [b for _, y in pairs for b in y],
        name,
        flops=2 * tokens * count_in * steps * rows * total,
        size=4 * width * total,
        rank=jnp.zeros((), jnp.int32) if core is None else core,
    )


def pick_weights(three, one, rank):
    rows, width = one.shape[0], one.shape[1] // 4

    def kernel(r, three_ref, one_ref, *outs):
        for k in range(4):

            @pl.when(pl.program_id(0) == k)
            def _():
                for j in range(3):
                    outs[k][:, j * width : (j + 1) * width] = three_ref[j]
                outs[k][:, 3 * width :] = one_ref[...]

    outs = [shape((rows, 4 * width))] * 4
    return call(
        kernel,
        (4,),
        [
            pl.BlockSpec((3, rows, width), lambda k, r: (0, 0, k ^ r[0])),
            pl.BlockSpec((rows, width), lambda k, r: (0, k ^ r[0])),
        ],
        [whole(a) for a in outs],
        outs,
        [three, one],
        "pick_weights",
        rank=rank,
    )


def pick_rows(arrays, rank):
    rows = arrays[0].shape[1]
    widths = [a.shape[2] for a in arrays]
    count = len(arrays)

    def kernel(r, *refs):
        for k in range(4):

            @pl.when(pl.program_id(0) == k)
            def _():
                at = 0
                for ref, width in zip(refs, widths):
                    refs[count + k][:, at : at + width] = ref[0]
                    at += width

    outs = [shape((rows, sum(widths)))] * 4
    return call(
        kernel,
        (4,),
        [pl.BlockSpec((1, rows, w), lambda k, r: (k ^ r[0], 0, 0)) for w in widths],
        [whole(a) for a in outs],
        outs,
        arrays,
        "pick_rows",
        rank=rank,
    )


def place(parts, rank):
    def kernel(r, *refs):
        for k in range(4):

            @pl.when(pl.program_id(0) == k)
            def _():
                refs[4][0] = refs[k][...]

    rows, columns = parts[0].shape
    return call(
        kernel,
        (4,),
        [whole(p) for p in parts],
        pl.BlockSpec((1, rows, columns), lambda k, r: (k ^ r[0], 0, 0)),
        shape((4, rows, columns)),
        parts,
        "place",
        rank=rank,
    )


def finish_wide(parts, rank):
    rows, width = parts[0].shape

    def kernel(r, *refs):
        for k in range(4):

            @pl.when(pl.program_id(0) == k)
            def _():
                refs[4][...] = refs[k][...].astype(F32)

    return call(
        kernel,
        (4,),
        [whole(p) for p in parts],
        pl.BlockSpec((rows, width), lambda k, r: (0, k ^ r[0])),
        shape((rows, 4 * width), F32),
        parts,
        "finish_wide",
        rank=rank,
    )


def finish_all(parts, text_grad, rank):
    rows, total = parts[0].shape
    width = total // 6

    def kernel(r, *refs):
        key, value, three, out, cross, cross_out = refs[4:]
        for k in range(4):

            @pl.when(pl.program_id(0) == k)
            def _():
                def part(j):
                    return refs[k][:, j * width : (j + 1) * width].astype(F32)

                for j in range(3):
                    three[j] = part(j)
                out[...] = part(3)
                cross[0] = part(4)
                cross_out[...] = part(5)

        cross[1] = key[...]
        cross[2] = value[...]

    wide = pl.BlockSpec((3, rows, width), lambda k, r: (0, 0, k ^ r[0]))
    flat = pl.BlockSpec((rows, width), lambda k, r: (0, k ^ r[0]))
    return call(
        kernel,
        (4,),
        [whole(p) for p in parts]
        + [flat, pl.BlockSpec((rows, width), lambda k, r: (0, 4 + (k ^ r[0])))],
        [wide, flat, wide, flat],
        [shape((3, rows, 4 * width), F32), shape((rows, 4 * width), F32)] * 2,
        [*parts, text_grad, text_grad],
        "finish_all",
        rank=rank,
    )


def plane_block(k):
    return (k >> 1) & 1, (k >> 2) * 2 + (k & 1)


def text_forward(caption, w_text, w_cross):
    context, rows = caption.shape[0], w_text.shape[0]
    half, width = context // 2, w_cross.shape[2] // 4

    def kernel(cap, weight, cross, own, blocks):
        own[...] = mm_t(cap[...], weight[...]).astype(BF)
        for j in range(2):
            part = mm(own[...], cross[1 + j]).astype(BF)
            for k in range(8):
                core, group = plane_block(k)
                blocks[k, :, j * width : (j + 1) * width] = part[
                    core * half : (core + 1) * half, group * width : (group + 1) * width
                ]

    return call(
        kernel,
        (1,),
        [whole(caption), whole(w_text), whole(w_cross)],
        [
            pl.BlockSpec((context, rows), lambda i: (0, 0)),
            pl.BlockSpec((8, half, 2 * width), lambda i: (0, 0, 0)),
        ],
        [shape((context, rows)), shape((8, half, 2 * width))],
        [caption, w_text, w_cross],
        "text_forward",
    )


def text_back(blocks, own_text, w_cross, caption, w_text):
    context, rows = own_text.shape
    half, width = context // 2, w_cross.shape[2] // 4
    wide = caption.shape[1] // 4

    def kernel(block, own, cross, cap, weight, kv_grad, text_grad, out, grads):
        for k in range(8):
            core, group = plane_block(k)
            for j in range(2):
                at = (4 * j + group) * width
                grads[core * half : (core + 1) * half, at : at + width] = block[
                    k, :, j * width : (j + 1) * width
                ]
        kv_grad[...] = t_mm(own[...], grads[...])
        grad_text = sum(
            mm_t(grads[:, 4 * j * width : 4 * (j + 1) * width], cross[1 + j]) for j in range(2)
        ).astype(BF)
        text_grad[...] = t_mm(grad_text, cap[...])
        part = mm(grad_text, weight[...]).astype(BF)
        for k in range(8):
            core, group = plane_block(k)
            out[k] = part[core * half : (core + 1) * half, group * wide : (group + 1) * wide]

    operands = [blocks, own_text, w_cross, caption, w_text]
    outs = [
        shape((rows, 8 * width), F32),
        shape((rows, 4 * wide), F32),
        shape((8, half, wide)),
    ]
    return call(
        kernel,
        (1,),
        [whole(a) for a in operands],
        [whole(a) for a in outs],
        outs,
        operands,
        "text_back",
        scratch=[pltpu.VMEM((context, 8 * width), BF)],
    )


def caption_output(blocks, half):
    count, _, wide = blocks.shape

    def kernel(block, out):
        out[...] = block[0].astype(F32)

    return call(
        kernel,
        (count,),
        [pl.BlockSpec((1, half, wide), lambda k: (k, 0, 0))],
        pl.BlockSpec((half, wide), lambda k: plane_block(k)),
        shape((2 * half, 4 * wide), F32),
        [blocks],
        "caption_output",
    )


def column_blocks(weight, count):
    rows = weight.shape[0]
    return weight.reshape(rows, count, -1).transpose(1, 0, 2)


def halves_of(values, width):
    high = values.astype(BF)
    low = (values - high.astype(F32)).astype(BF)
    return jnp.concatenate([high.reshape(-1, width), low.reshape(-1, width)], axis=0)


def whole_of(halves, width):
    rows = halves.shape[0] // 2
    return (halves[:rows] + halves[rows:]).reshape(-1, width)


def make_local(z_size):
    def sum_z(values):
        parts = values.reshape(z_size, -1, values.shape[-1])
        mine = trade(parts, "z").astype(F32).sum(axis=0).astype(BF)
        return spread(mine, "z", z_size).reshape(values.shape)

    def add_z(values):
        step = 1
        while step < z_size:
            values = values + lax.ppermute(
                values, "z", tuple((k, k ^ step) for k in range(z_size))
            )
            step *= 2
        return values

    def layer_order(values):
        shaped = values.reshape(values.shape[:-1] + (z_size, 2, 2, -1))
        return jnp.swapaxes(shaped, -3, -2).reshape(values.shape)

    def local(
        hidden,
        mask_index,
        mask_count,
        mask_embed,
        norm_gains,
        caption,
        w_qkv,
        w_out,
        w_cross,
        w_cross_out,
        w_text,
        w_up,
        w_down,
        cotangent,
    ):
        images, local_rows, width = hidden.shape
        full_length = mask_index.shape[1]
        rank = lax.axis_index("x") * 2 + lax.axis_index("y")
        core = lax.axis_index("c")
        tokens = images * local_rows
        group = width // 4
        text_width = caption.shape[1]

        unit = width // (4 * z_size)
        inside = unit % 128 == 0
        order = [4 * k + j for k in range(z_size) for j in (0, 2, 1, 3)] if inside else None

        def outer(values):
            return values if inside else layer_order(values)

        w_qkv, w_cross = w_qkv.transpose(1, 0, 2), w_cross.transpose(1, 0, 2)
        first = swap_parts(pick_weights(w_qkv, w_out, rank))
        first = gather_rows(place(first, rank))

        positions = lax.axis_index("y") * local_rows + jnp.arange(local_rows, dtype=jnp.int32)
        ranks = jnp.arange(full_length, dtype=jnp.int32)
        matches = (mask_index[:, :, None] == positions[None, None, :]) & (
            ranks[None, :, None] < mask_count[:, None, None]
        )
        masked = jnp.any(matches, axis=1).reshape(tokens, 1).astype(F32)
        gains = layer_order(norm_gains)
        gain_a, gain_b, gain_c = gains[:1], gains[1:2], gains[2:]
        start_x, attn_in, grad_top = start(
            outer(hidden.reshape(tokens, width)),
            outer(cotangent.reshape(tokens, width)),
            masked,
            layer_order(mask_embed)[None],
            gain_a,
            unit,
            order,
        )
        attn_in = gather_tokens(attn_in)
        mid = jnp.concatenate([column_blocks(w_cross[0], 4), column_blocks(w_cross_out, 4)], axis=2)
        up = column_blocks(w_up, 4)
        attn_in, mid, up = lax.optimization_barrier((attn_in, mid, up))
        mid, up = gather_rows(trade(mid)), gather_rows(trade(up))

        own_text, kv_part = text_forward(caption, w_text, w_cross)
        text_kv = trade(kv_part, PLANE).astype(F32).sum(axis=0).astype(BF)
        text_kv = sum_z(text_kv)
        other = swap(text_kv, "c")
        text_kv = jnp.concatenate(
            [jnp.where(core == 0, text_kv, other), jnp.where(core == 0, other, text_kv)], axis=0
        )
        attn_in, text_kv = lax.optimization_barrier((attn_in, text_kv))

        attn_in, projected = gather_mm(attn_in, first, 0, 3 * group, "qkv_mm")
        self_mixed = self_forward(projected, 2 * images)
        down = column_blocks(w_down, 4)
        self_mixed, down = lax.optimization_barrier((self_mixed, down))
        down = gather_rows(trade(down))
        parts = mm_scatter(self_mixed, first[:, 3 * group :])
        after_attn, cross_in = add_norm([start_x] + parts, gain_b)

        cross_in, cross_queries = gather_mm(gather_tokens(cross_in), mid, 0, group, "query_mm")
        cross_mixed = cross_forward(cross_queries, text_kv)
        parts = mm_scatter(cross_mixed, mid[:, group:])
        after_cross, mlp_in = add_norm([after_attn] + parts, gain_c)

        mlp_in = gather_tokens(mlp_in)
        mlp_in, grad_top = lax.optimization_barrier((mlp_in, grad_top))
        grad_y = jnp.concatenate(gather_tokens(grad_top), axis=0)
        mlp_in, activated, slope = feed_up(mlp_in, up)
        early = [attn_in, self_mixed, cross_in, cross_mixed]
        if inside:
            grad_axes, halves = "z", (core, z_size)

            def both(values):
                return [values, swap(values, "c")]

        else:
            grad_axes, halves = DATA, ()

            def both(values):
                return [values]

        early = [both(values) for values in early]
        down_part = grad_products([(both(grad_y), both(activated))], "down_grads", *halves)
        mlp_in = both(mlp_in)
        slope, down_part, early, mlp_in = lax.optimization_barrier((slope, down_part, early, mlp_in))
        down_rows = scatter_grad(down_part, grad_axes)
        grad_pre = feed_down(grad_y, slope, down)
        parts = mm_scatter(grad_pre, up)
        up_part = grad_products([(mlp_in, both(grad_pre))], "up_grads", *halves)
        grad_after_cross, cross_branch, gain_grad_c = norm_back(
            parts, grad_top, after_cross, gain_c
        )

        cross_branch = gather_tokens(cross_branch)
        cross_branch, up_part = lax.optimization_barrier((cross_branch, up_part))
        cross_branch, grad_cross_mixed = gather_mm(
            cross_branch, mid, group, group, "cross_out_back"
        )
        grad_cq, kv_grad = cross_back(cross_queries, text_kv, grad_cross_mixed)
        up_part, down_rows, kv_grad = lax.optimization_barrier((up_part, down_rows, kv_grad))
        up_rows = scatter_grad(up_part, grad_axes)
        cross_branch, grad_cq_both = both(cross_branch), both(grad_cq)
        parts = mm_scatter(grad_cq, mid[:, :group])
        grad_after_attn, attn_branch, gain_grad_b = norm_back(
            parts, grad_after_cross, after_attn, gain_b
        )

        attn_branch, grad_self_mixed = gather_mm(
            gather_tokens(attn_branch), first, 3 * group, group, "out_back"
        )
        grad_projected = self_back(projected, grad_self_mixed, 2 * images)
        rest_part = grad_products(
            [
                (early[0], both(grad_projected)),
                (both(attn_branch), early[1]),
                (early[2], grad_cq_both),
                (cross_branch, early[3]),
            ],
            "attention_grads",
            *halves,
        )
        kv_part = kv_grad.astype(BF).reshape(2, z_size, -1, 2 * group)
        kv_part = kv_part.transpose(1, 0, 2, 3).reshape(2 * z_size, -1, 2 * group)
        grad_projected, activated, kv_part, rest_part = lax.optimization_barrier(
            (grad_projected, activated, kv_part, rest_part)
        )
        rest_part, up_rows = lax.optimization_barrier((rest_part, up_rows))
        rest_rows = scatter_grad(rest_part, grad_axes)

        kv_part = trade(kv_part, DATA).astype(F32).sum(axis=0).astype(BF)
        grad_attn = mm_t(grad_projected, first[:, : 3 * group]).astype(BF)
        down_parts = swap_parts(pick_rows([down_rows], rank))
        kv_part, grad_attn, down_parts, activated = lax.optimization_barrier(
            (kv_part, grad_attn, down_parts, activated)
        )

        kv_part = spread(kv_part, "z", z_size).reshape(-1, 2 * group)
        grad_attn = scatter_first(token_blocks(grad_attn))
        result = mm_t(activated, down).astype(BF)
        kv_part, grad_attn, result = lax.optimization_barrier((kv_part, grad_attn, result))

        kv_grads = spread(kv_part, PLANE, 8)
        grad_attn = scatter_second(grad_attn)
        result = scatter_first(token_blocks(result))
        kv_grads, grad_attn, result = lax.optimization_barrier((kv_grads, grad_attn, result))

        kv_weight_grad, grad_text_w, caption_part = text_back(
            kv_grads, own_text, w_cross, caption, w_text
        )
        caption_part = trade(caption_part, PLANE).astype(F32).sum(axis=0).astype(BF)
        grad_hidden, gain_grad_a, mask_grad = last_back(
            grad_attn, grad_after_attn, start_x, gain_a, masked, unit, order
        )
        sums = jnp.concatenate([gain_grad_a, gain_grad_b, gain_grad_c, mask_grad], axis=0)
        result = scatter_second(result)
        caption_part, sums, result, up_rows = lax.optimization_barrier(
            (caption_part, sums, result, up_rows)
        )

        caption_part = caption_part.reshape(z_size, -1, text_width // 4)
        caption_part = trade(caption_part, "z").astype(F32).sum(axis=0).astype(BF)
        output = layer_output(after_cross, result, unit, order)
        up_parts = swap_parts(pick_rows([up_rows], rank))
        caption_part, output, up_parts = lax.optimization_barrier((caption_part, output, up_parts))

        half_context = caption.shape[0] // 2
        caption_part = spread(caption_part, "z", z_size).reshape(half_context, -1)
        down_grad, up_grad = finish_wide(down_parts, rank), finish_wide(up_parts, rank)
        caption_part, down_grad, up_grad = lax.optimization_barrier(
            (caption_part, down_grad, up_grad)
        )

        caption_part = jnp.concatenate([caption_part, halves_of(sums, text_width // 4)], axis=0)
        caption_part = spread(caption_part, PLANE, 8)
        caption_part, rest_rows = lax.optimization_barrier((caption_part, rest_rows))

        qkv_grad, out_grad, grad_cross, cross_out_grad = finish_all(
            swap_parts(pick_rows([rest_rows], rank)), kv_weight_grad, rank
        )
        sums = whole_of(caption_part[:, half_context:].astype(F32).sum(axis=0), width)
        sums = layer_order(add_z(sums))
        grad_caption = caption_output(caption_part, half_context)
        return (
            outer(output).reshape(hidden.shape),
            outer(grad_hidden).reshape(hidden.shape),
            grad_caption,
            sums[:3],
            sums[3],
            qkv_grad.transpose(1, 0, 2),
            out_grad,
            grad_cross.transpose(1, 0, 2),
            cross_out_grad,
            grad_text_w,
            up_grad,
            down_grad,
        )

    return local


def solution(mesh):
    z_size = mesh.shape["img"] // 4
    inner = Mesh(mesh.devices.reshape(z_size, 2, 2, 2), ("z", "x", "c", "y"))
    image = ("z", "x", "c")
    tokens = P(image, "y", None)
    rows = P(image + ("y",))
    in_specs = (tokens, P(image, None), P(image), P(), P(), P()) + (rows,) * 7 + (tokens,)
    out_specs = (tokens, tokens, P(), P(), P()) + (rows,) * 7
    return jax.shard_map(
        make_local(z_size), mesh=inner, in_specs=in_specs, out_specs=out_specs, check_vma=False
    )
```

```python
import math

import jax
import jax.numpy as jnp
from jax import lax
from jax.experimental import pallas as pl
from jax.experimental.pallas import tpu as pltpu
from jax.sharding import Mesh
from jax.sharding import PartitionSpec as P

HD = 128
EPS = 1e-05
BF = jnp.bfloat16
F32 = jnp.float32
PAIR = ((0, 1), (1, 0))
GROUP = ("x", "y")
DATA = ("z", "c")
PLANE = ("x", "c", "y")
VMEM = 48 * 1024 * 1024
SCALE = 1.0 / math.sqrt(HD)
SLOPE = math.sqrt(2.0 / math.pi)
CUBIC = 0.044715


def dot(a, b, dims):
    return lax.dot_general(a, b, (dims, ((), ())), preferred_element_type=F32)


def mm(a, b):
    return dot(a, b, ((1,), (0,)))


def mm_t(a, b):
    return dot(a, b, ((1,), (1,)))


def t_mm(a, b):
    return dot(a, b, ((0,), (0,)))


def shape(dims, dtype=BF):
    return jax.ShapeDtypeStruct(dims, dtype)


def swap(values, axis):
    return lax.ppermute(values, axis, PAIR)


def trade(blocks, axes=GROUP):
    return lax.all_to_all(blocks, axes, 0, 0, tiled=True)


def spread(values, axes=GROUP, count=4):
    return trade(jnp.broadcast_to(values[None], (count,) + values.shape), axes)


def gather_tokens(own):
    half = own.shape[0] // 2
    from_x = swap(own, "x")
    from_y = swap(own, "y")
    return own, from_y, from_x, swap(from_x[:half], "y"), swap(from_y[half:], "x")


def scatter_tokens(parts):
    own, for_y, for_x, for_low, for_high = parts
    half = for_low.shape[0]
    low = swap(for_low, "y").astype(F32) + for_x[:half].astype(F32)
    high = swap(for_high, "x").astype(F32) + for_y[half:].astype(F32)
    from_x = swap(jnp.concatenate([low.astype(BF), for_x[half:]], axis=0), "x")
    from_y = swap(jnp.concatenate([for_y[:half], high.astype(BF)], axis=0), "y")
    return [own, from_x, from_y]


def swap_parts(parts):
    return [
        parts[0],
        swap(parts[1], "y"),
        swap(parts[2], "x"),
        lax.ppermute(parts[3], GROUP, ((0, 3), (1, 2), (2, 1), (3, 0))),
    ]


def gather_rows(rows):
    return lax.all_gather(rows.reshape(-1, rows.shape[-1]), DATA, axis=0, tiled=True)


def scatter_grad(partial, axes):
    summed = lax.psum_scatter(partial, axes, scatter_dimension=0, tiled=True)
    return summed.reshape(4, -1, summed.shape[-1])


def call(kernel, grid, in_specs, out_specs, out_shape, operands, name, flops=0, size=1 << 22,
         rank=None, scratch=()):
    options = dict(
        out_shape=out_shape,
        compiler_params=pltpu.CompilerParams(vmem_limit_bytes=VMEM),
        cost_estimate=pl.CostEstimate(flops=flops, bytes_accessed=size, transcendentals=0),
        name=name,
    )
    if rank is None:
        return pl.pallas_call(
            kernel, grid=grid, in_specs=in_specs, out_specs=out_specs, scratch_shapes=scratch,
            **options,
        )(*operands)
    spec = pltpu.PrefetchScalarGridSpec(
        num_scalar_prefetch=1,
        grid=grid,
        in_specs=in_specs,
        out_specs=out_specs,
        scratch_shapes=scratch,
    )
    return pl.pallas_call(kernel, grid_spec=spec, **options)(rank.reshape(1), *operands)


def whole(array):
    return pl.BlockSpec(array.shape, lambda *_: (0,) * len(array.shape))


def reorder(values, unit, order):
    if order is None:
        return values
    return jnp.concatenate([values[:, k * unit : (k + 1) * unit] for k in order], axis=1)


def assemble(target, pieces, sems):
    copies, at = [], 0
    for k, piece in enumerate(pieces):
        rows = piece.shape[0]
        copies.append(pltpu.make_async_copy(piece, target.at[at : at + rows], sems.at[k]))
        at += rows
    for copy in copies:
        copy.start()
    for copy in copies:
        copy.wait()


ANY = pl.BlockSpec(memory_space=pl.ANY)


def gather_mm(pieces, weight, first, columns, name):
    rows, width = pieces[0].shape
    step = 256

    def kernel(*refs):
        tokens, out, sems = refs[6:]

        @pl.when(pl.program_id(0) == 0)
        def _():
            assemble(tokens, refs[:5], sems)

        out[...] = mm(tokens[...], refs[5][...]).astype(BF)

    return call(
        kernel,
        (columns // step,),
        [ANY] * 5 + [pl.BlockSpec((width, step), lambda j: (0, first // step + j))],
        [
            pl.BlockSpec((4 * rows, width), lambda j: (0, 0)),
            pl.BlockSpec((4 * rows, step), lambda j: (0, j)),
        ],
        [shape((4 * rows, width)), shape((4 * rows, columns))],
        [*pieces, weight],
        name,
        flops=8 * rows * width * columns,
        size=2 * width * (columns + 8 * rows),
        scratch=[pltpu.SemaphoreType.DMA((5,))],
    )


def mm_scatter(values, weight):
    partial = mm_t(values, weight).astype(BF)
    rows = partial.shape[0] // 4
    cuts = [0, rows, 2 * rows, 3 * rows, 3 * rows + rows // 2, 4 * rows]
    return scatter_tokens([partial[a:b] for a, b in zip(cuts, cuts[1:])])


def normalize(values):
    centred = values - jnp.mean(values, axis=-1, keepdims=True)
    inv_std = lax.rsqrt(jnp.mean(centred * centred, axis=-1, keepdims=True) + EPS)
    return centred * inv_std, inv_std


NORM_ROWS = 32


def row_spec(array, at=None):
    width = array.shape[-1]
    if at is None:
        return pl.BlockSpec((NORM_ROWS, width), lambda i: (i, 0))
    return pl.BlockSpec((1, NORM_ROWS, width), lambda i, at=at: (at, i, 0))


def terms_of(terms):
    arrays, specs = [], []
    for term in terms:
        array, at = term if isinstance(term, tuple) else (term, None)
        arrays.append(array)
        specs.append(row_spec(array, at))
    return arrays, specs


def total_of(refs):
    values = [ref[0] if len(ref.shape) == 3 else ref[...] for ref in refs]
    return sum(value.astype(F32) for value in values)


def add_norm(terms, gain):
    arrays, specs = terms_of(terms)
    tokens, width = arrays[0].shape[-2], arrays[0].shape[-1]
    tokens = min(a.shape[-2] for a in arrays)

    def kernel(*refs):
        gain_ref, x, out = refs[-3:]
        values = total_of(refs[:-3])
        x[...] = values
        out[...] = (normalize(values)[0] * gain_ref[...]).astype(BF)

    return call(
        kernel,
        (tokens // NORM_ROWS,),
        specs + [whole(gain)],
        [row_spec(shape((tokens, width)))] * 2,
        [shape((tokens, width), F32), shape((tokens, width))],
        [*arrays, gain],
        "add_norm",
    )


def norm_grad(grad, values, gain):
    normed, inv_std = normalize(values)
    scaled = grad * gain
    first_mean = jnp.mean(scaled, axis=-1, keepdims=True)
    second_mean = jnp.mean(scaled * normed, axis=-1, keepdims=True)
    return (
        inv_std * (scaled - first_mean - normed * second_mean),
        jnp.sum(grad * normed, axis=0, keepdims=True),
    )


def accumulate(ref, value):
    @pl.when(pl.program_id(0) == 0)
    def _():
        ref[...] = jnp.zeros_like(ref)

    ref[...] += value


def norm_back(terms, upper, values, gain):
    arrays, specs = terms_of(terms)
    tokens, width = values.shape

    def kernel(*refs):
        upper_ref, x, gain_ref, out, out_low, gain_grad = refs[-6:]
        back, part = norm_grad(total_of(refs[:-6]), x[...], gain_ref[...])
        result = upper_ref[...].astype(F32) + back
        out[...] = result
        out_low[...] = result.astype(BF)
        accumulate(gain_grad, part)

    return call(
        kernel,
        (tokens // NORM_ROWS,),
        specs + [row_spec(upper), row_spec(values), whole(gain)],
        [row_spec(values)] * 2 + [pl.BlockSpec((1, width), lambda i: (0, 0))],
        [shape((tokens, width), F32), shape((tokens, width)), shape((1, width), F32)],
        [*arrays, upper, values, gain],
        "norm_back",
    )


def last_back(terms, upper, values, gain, masked, unit, order):
    arrays, specs = terms_of(terms)
    tokens, width = values.shape

    def kernel(*refs):
        upper_ref, x, gain_ref, mask, out, gain_grad, mask_grad = refs[-7:]
        back, part = norm_grad(total_of(refs[:-7]), x[...], gain_ref[...])
        result = upper_ref[...].astype(F32) + back
        hit = mask[...] > 0.5
        out[...] = reorder(jnp.where(hit, 0.0, result).astype(BF), unit, order)
        accumulate(gain_grad, part)
        accumulate(mask_grad, jnp.sum(jnp.where(hit, result, 0.0), axis=0, keepdims=True))

    line = pl.BlockSpec((1, width), lambda i: (0, 0))
    return call(
        kernel,
        (tokens // NORM_ROWS,),
        specs + [row_spec(upper), row_spec(values), whole(gain), row_spec(masked)],
        [row_spec(values), line, line],
        [shape((tokens, width)), shape((1, width), F32), shape((1, width), F32)],
        [*arrays, upper, values, gain, masked],
        "last_back",
    )


def start(hidden, cotangent, masked, embed, gain, unit, order):
    tokens, width = hidden.shape

    def kernel(hid, cot, mask, embed_ref, gain_ref, x, out, grad):
        hit = mask[...] > 0.5
        values = jnp.where(
            hit, embed_ref[...], reorder(hid[...], unit, order).astype(F32)
        )
        x[...] = values
        out[...] = (normalize(values)[0] * gain_ref[...]).astype(BF)
        grad[...] = jnp.where(hit, reorder(cot[...], unit, order).astype(F32), 0.0).astype(BF)

    rows = row_spec(hidden)
    return call(
        kernel,
        (tokens // NORM_ROWS,),
        [rows, rows, row_spec(masked), whole(embed), whole(gain)],
        [rows] * 3,
        [shape((tokens, width), F32), shape((tokens, width)), shape((tokens, width))],
        [hidden, cotangent, masked, embed, gain],
        "start",
    )


def layer_output(upper, terms, unit, order):
    arrays, specs = terms_of(terms)
    tokens, width = upper.shape

    def kernel(*refs):
        values = refs[-2][...] + total_of(refs[:-2])
        refs[-1][...] = reorder(values.astype(BF), unit, order)

    return call(
        kernel,
        (tokens // NORM_ROWS,),
        specs + [row_spec(upper)],
        row_spec(upper),
        shape((tokens, width)),
        [*arrays, upper],
        "layer_output",
    )


def feed_up(pieces, weight):
    rows, width = pieces[0].shape
    hidden = weight.shape[1]
    step = 256

    def kernel(*refs):
        up, tokens, act, slope, sems = refs[5:]

        @pl.when(pl.program_id(0) == 0)
        def _():
            assemble(tokens, refs[:5], sems)

        u = mm(tokens[...], up[...])
        square = u * u
        bend = jnp.tanh(SLOPE * u * (1.0 + CUBIC * square))
        half = 0.5 * (1.0 + bend)
        act[...] = (u * half).astype(BF)
        slope[...] = half + 0.5 * u * (1.0 - bend * bend) * SLOPE * (1.0 + 3.0 * CUBIC * square)

    part = pl.BlockSpec((4 * rows, step), lambda j: (0, j))
    return call(
        kernel,
        (hidden // step,),
        [ANY] * 5 + [pl.BlockSpec((width, step), lambda j: (0, j))],
        [pl.BlockSpec((4 * rows, width), lambda j: (0, 0)), part, part],
        [shape((4 * rows, width)), shape((4 * rows, hidden)), shape((4 * rows, hidden), F32)],
        [*pieces, weight],
        "feed_up",
        scratch=[pltpu.SemaphoreType.DMA((5,))],
        flops=8 * rows * width * hidden,
        size=2 * width * (hidden + 8 * rows),
    )


def feed_down(grad_y, slope, weight):
    tokens, width = grad_y.shape
    hidden = weight.shape[1]
    step = 256

    def kernel(dy, slope_ref, down, out):
        out[...] = (mm(dy[...], down[...]) * slope_ref[...]).astype(BF)

    part = pl.BlockSpec((tokens, step), lambda j: (0, j))
    return call(
        kernel,
        (hidden // step,),
        [whole(grad_y), part, pl.BlockSpec((width, step), lambda j: (0, j))],
        part,
        shape((tokens, hidden)),
        [grad_y, slope, weight],
        "feed_down",
        flops=2 * tokens * width * hidden,
        size=2 * width * (hidden + 8 * tokens),
    )


def softmax(scores):
    exp_terms = jnp.exp(scores - jnp.max(scores, axis=-1, keepdims=True))
    return exp_terms / jnp.sum(exp_terms, axis=-1, keepdims=True)


def score_grad(probs, grad_probs):
    return (
        probs * (grad_probs - jnp.sum(probs * grad_probs, axis=-1, keepdims=True))
    ).astype(BF)


def head(ref, k):
    return ref[:, k * HD : (k + 1) * HD]


def self_forward(projected, images):
    tokens, width = projected.shape
    rows, group = tokens // images, width // 3
    heads = group // HD

    def kernel(proj, mixed):
        for k in range(heads):
            query, key, value = (head(proj, j * heads + k) for j in range(3))
            probs = softmax(mm_t(query, key) * SCALE).astype(BF)
            mixed[:, k * HD : (k + 1) * HD] = mm(probs, value).astype(BF)

    return call(
        kernel,
        (images,),
        [pl.BlockSpec((rows, width), lambda i: (i, 0))],
        pl.BlockSpec((rows, group), lambda i: (i, 0)),
        shape((tokens, group)),
        [projected],
        "self_forward",
        flops=4 * tokens * rows * group,
    )


def self_back(projected, grad_mixed, images):
    tokens, width = projected.shape
    rows, group = tokens // images, width // 3
    heads = group // HD

    def kernel(proj, grad, out):
        for k in range(heads):
            query, key, value = (head(proj, j * heads + k) for j in range(3))
            grad_head = head(grad, k)
            probs = softmax(mm_t(query, key) * SCALE)
            grad_scores = score_grad(probs, mm_t(grad_head, value))
            parts = (
                mm(grad_scores, key) * SCALE,
                t_mm(grad_scores, query) * SCALE,
                t_mm(probs.astype(BF), grad_head),
            )
            for j, part in enumerate(parts):
                at = (j * heads + k) * HD
                out[:, at : at + HD] = part.astype(BF)

    return call(
        kernel,
        (images,),
        [
            pl.BlockSpec((rows, width), lambda i: (i, 0)),
            pl.BlockSpec((rows, group), lambda i: (i, 0)),
        ],
        pl.BlockSpec((rows, width), lambda i: (i, 0)),
        shape((tokens, width)),
        [projected, grad_mixed],
        "self_back",
        flops=10 * tokens * rows * group,
    )


def cross_forward(queries, text_kv):
    tokens, group = queries.shape
    heads = group // HD

    def kernel(query, text, mixed):
        for k in range(heads):
            probs = softmax(mm_t(head(query, k), head(text, k)) * SCALE).astype(BF)
            mixed[:, k * HD : (k + 1) * HD] = mm(probs, head(text, heads + k)).astype(BF)

    return call(
        kernel,
        (1,),
        [whole(queries), whole(text_kv)],
        whole(queries),
        shape((tokens, group)),
        [queries, text_kv],
        "cross_forward",
        flops=4 * tokens * text_kv.shape[0] * group,
    )


def cross_back(queries, text_kv, grad_mixed):
    tokens, group = queries.shape
    context = text_kv.shape[0]
    heads = group // HD

    def kernel(query, text, grad, grad_query, grad_text):
        for k in range(heads):
            query_head, key, value = head(query, k), head(text, k), head(text, heads + k)
            grad_head = head(grad, k)
            probs = softmax(mm_t(query_head, key) * SCALE)
            grad_scores = score_grad(probs, mm_t(grad_head, value))
            grad_query[:, k * HD : (k + 1) * HD] = (mm(grad_scores, key) * SCALE).astype(BF)
            at = (heads + k) * HD
            grad_text[:, k * HD : (k + 1) * HD] = t_mm(grad_scores, query_head) * SCALE
            grad_text[:, at : at + HD] = t_mm(probs.astype(BF), grad_head)

    return call(
        kernel,
        (1,),
        [whole(queries), whole(text_kv), whole(grad_mixed)],
        [whole(queries), whole(text_kv)],
        [shape((tokens, group)), shape((context, 2 * group), F32)],
        [queries, text_kv, grad_mixed],
        "cross_back",
        flops=10 * tokens * context * group,
    )


def grad_products(pairs, name, core=None, blocks=0):
    count_in = len(pairs[0][0])
    tokens, width = pairs[0][0][0].shape
    widths = [y[0].shape[1] for _, y in pairs]
    total = sum(widths)
    rows = 256 if core is None else width // (2 * blocks)
    steps = width // rows if core is None else blocks
    step = 512
    count = len(pairs) * count_in

    def kernel(r, *refs):
        out = refs[2 * count]
        offset = 0
        for k, wide in enumerate(widths):
            left = [refs[k * count_in + b][...].T for b in range(count_in)]
            for at in range(0, wide, step):
                out[:, offset + at : offset + at + step] = sum(
                    mm(left[b], refs[count + k * count_in + b][:, at : at + step])
                    for b in range(count_in)
                ).astype(BF)
            offset += wide

    pick = (lambda i, r: (0, i)) if core is None else (lambda i, r: (0, 2 * i + r[0]))
    return call(
        kernel,
        (steps,),
        [pl.BlockSpec((tokens, rows), pick)] * count
        + [pl.BlockSpec((tokens, w), lambda i, r: (0, 0)) for w in widths for _ in range(count_in)],
        pl.BlockSpec((rows, total), lambda i, r: (i, 0)),
        shape((steps * rows, total)),
        [b for x, _ in pairs for b in x] + [b for _, y in pairs for b in y],
        name,
        flops=2 * tokens * count_in * steps * rows * total,
        size=4 * width * total,
        rank=jnp.zeros((), jnp.int32) if core is None else core,
    )


def pick_weights(three, one, rank):
    rows, width = one.shape[0], one.shape[1] // 4

    def kernel(r, three_ref, one_ref, *outs):
        for k in range(4):

            @pl.when(pl.program_id(0) == k)
            def _():
                for j in range(3):
                    outs[k][:, j * width : (j + 1) * width] = three_ref[j]
                outs[k][:, 3 * width :] = one_ref[...]

    outs = [shape((rows, 4 * width))] * 4
    return call(
        kernel,
        (4,),
        [
            pl.BlockSpec((3, rows, width), lambda k, r: (0, 0, k ^ r[0])),
            pl.BlockSpec((rows, width), lambda k, r: (0, k ^ r[0])),
        ],
        [whole(a) for a in outs],
        outs,
        [three, one],
        "pick_weights",
        rank=rank,
    )


def pick_rows(arrays, rank):
    rows = arrays[0].shape[1]
    widths = [a.shape[2] for a in arrays]
    count = len(arrays)

    def kernel(r, *refs):
        for k in range(4):

            @pl.when(pl.program_id(0) == k)
            def _():
                at = 0
                for ref, width in zip(refs, widths):
                    refs[count + k][:, at : at + width] = ref[0]
                    at += width

    outs = [shape((rows, sum(widths)))] * 4
    return call(
        kernel,
        (4,),
        [pl.BlockSpec((1, rows, w), lambda k, r: (k ^ r[0], 0, 0)) for w in widths],
        [whole(a) for a in outs],
        outs,
        arrays,
        "pick_rows",
        rank=rank,
    )


def place(parts, rank):
    def kernel(r, *refs):
        for k in range(4):

            @pl.when(pl.program_id(0) == k)
            def _():
                refs[4][0] = refs[k][...]

    rows, columns = parts[0].shape
    return call(
        kernel,
        (4,),
        [whole(p) for p in parts],
        pl.BlockSpec((1, rows, columns), lambda k, r: (k ^ r[0], 0, 0)),
        shape((4, rows, columns)),
        parts,
        "place",
        rank=rank,
    )


def finish_wide(parts, rank):
    rows, total = parts[0].shape
    width = total // 2

    def kernel(r, *refs):
        for k in range(4):

            @pl.when(pl.program_id(0) == k)
            def _():
                refs[4][...] = refs[k][:, :width].astype(F32)
                refs[5][...] = refs[k][:, width:].astype(F32)

    flat = pl.BlockSpec((rows, width), lambda k, r: (0, k ^ r[0]))
    return call(
        kernel,
        (4,),
        [whole(p) for p in parts],
        [flat, flat],
        [shape((rows, 4 * width), F32)] * 2,
        parts,
        "finish_wide",
        rank=rank,
    )


def finish_all(parts, text_grad, rank):
    rows, total = parts[0].shape
    width = total // 6

    def kernel(r, *refs):
        key, value, three, out, cross, cross_out = refs[4:]
        for k in range(4):

            @pl.when(pl.program_id(0) == k)
            def _():
                def part(j):
                    return refs[k][:, j * width : (j + 1) * width].astype(F32)

                for j in range(3):
                    three[j] = part(j)
                out[...] = part(3)
                cross[0] = part(4)
                cross_out[...] = part(5)

        cross[1] = key[...]
        cross[2] = value[...]

    wide = pl.BlockSpec((3, rows, width), lambda k, r: (0, 0, k ^ r[0]))
    flat = pl.BlockSpec((rows, width), lambda k, r: (0, k ^ r[0]))
    return call(
        kernel,
        (4,),
        [whole(p) for p in parts]
        + [flat, pl.BlockSpec((rows, width), lambda k, r: (0, 4 + (k ^ r[0])))],
        [wide, flat, wide, flat],
        [shape((3, rows, 4 * width), F32), shape((rows, 4 * width), F32)] * 2,
        [*parts, text_grad, text_grad],
        "finish_all",
        rank=rank,
    )


def plane_block(k):
    return (k >> 1) & 1, (k >> 2) * 2 + (k & 1)


def text_forward(caption, w_text, w_cross):
    context, rows = caption.shape[0], w_text.shape[0]
    half, width = context // 2, w_cross.shape[2] // 4

    def kernel(cap, weight, cross, own, blocks):
        own[...] = mm_t(cap[...], weight[...]).astype(BF)
        for j in range(2):
            part = mm(own[...], cross[1 + j]).astype(BF)
            for k in range(8):
                core, group = plane_block(k)
                blocks[k, :, j * width : (j + 1) * width] = part[
                    core * half : (core + 1) * half, group * width : (group + 1) * width
                ]

    return call(
        kernel,
        (1,),
        [whole(caption), whole(w_text), whole(w_cross)],
        [
            pl.BlockSpec((context, rows), lambda i: (0, 0)),
            pl.BlockSpec((8, half, 2 * width), lambda i: (0, 0, 0)),
        ],
        [shape((context, rows)), shape((8, half, 2 * width))],
        [caption, w_text, w_cross],
        "text_forward",
    )


def text_back(blocks, own_text, w_cross, caption, w_text, extra):
    context, rows = own_text.shape
    half, width = context // 2, w_cross.shape[2] // 4
    wide = caption.shape[1] // 4
    tail = extra.shape[0]

    def kernel(block, own, cross, cap, weight, more, kv_grad, text_grad, out, grads):
        for k in range(8):
            core, group = plane_block(k)
            for j in range(2):
                at = (4 * j + group) * width
                grads[core * half : (core + 1) * half, at : at + width] = block[
                    k, :, j * width : (j + 1) * width
                ]
        kv_grad[...] = t_mm(own[...], grads[...])
        grad_text = sum(
            mm_t(grads[:, 4 * j * width : 4 * (j + 1) * width], cross[1 + j]) for j in range(2)
        ).astype(BF)
        text_grad[...] = t_mm(grad_text, cap[...])
        part = mm(grad_text, weight[...]).astype(BF)
        for k in range(8):
            core, group = plane_block(k)
            out[k, :half, :] = part[core * half : (core + 1) * half, group * wide : (group + 1) * wide]
            out[k, half:, :] = more[...]

    operands = [blocks, own_text, w_cross, caption, w_text, extra]
    outs = [
        shape((rows, 8 * width), F32),
        shape((rows, 4 * wide), F32),
        shape((8, half + tail, wide)),
    ]
    return call(
        kernel,
        (1,),
        [whole(a) for a in operands],
        [whole(a) for a in outs],
        outs,
        operands,
        "text_back",
        scratch=[pltpu.VMEM((context, 8 * width), BF)],
    )


def caption_output(blocks):
    count, half, wide = blocks.shape

    def kernel(block, out):
        out[...] = block[0].astype(F32)

    return call(
        kernel,
        (count,),
        [pl.BlockSpec((1, half, wide), lambda k: (k, 0, 0))],
        pl.BlockSpec((half, wide), lambda k: plane_block(k)),
        shape((2 * half, 4 * wide), F32),
        [blocks],
        "caption_output",
    )


def column_blocks(weight, count):
    rows = weight.shape[0]
    return weight.reshape(rows, count, -1).transpose(1, 0, 2)


def halves_of(values, width):
    high = values.astype(BF)
    low = (values - high.astype(F32)).astype(BF)
    return jnp.concatenate([high.reshape(-1, width), low.reshape(-1, width)], axis=0)


def whole_of(halves, width):
    rows = halves.shape[0] // 2
    return (halves[:rows] + halves[rows:]).reshape(-1, width)


def make_local(z_size):
    def sum_z(values):
        parts = values.reshape(z_size, -1, values.shape[-1])
        mine = trade(parts, "z").astype(F32).sum(axis=0).astype(BF)
        return spread(mine, "z", z_size).reshape(values.shape)

    def add_z(values):
        step = 1
        while step < z_size:
            values = values + lax.ppermute(
                values, "z", tuple((k, k ^ step) for k in range(z_size))
            )
            step *= 2
        return values

    def layer_order(values):
        shaped = values.reshape(values.shape[:-1] + (z_size, 2, 2, -1))
        return jnp.swapaxes(shaped, -3, -2).reshape(values.shape)

    def local(
        hidden,
        mask_index,
        mask_count,
        mask_embed,
        norm_gains,
        caption,
        w_qkv,
        w_out,
        w_cross,
        w_cross_out,
        w_text,
        w_up,
        w_down,
        cotangent,
    ):
        images, local_rows, width = hidden.shape
        full_length = mask_index.shape[1]
        rank = lax.axis_index("x") * 2 + lax.axis_index("y")
        core = lax.axis_index("c")
        tokens = images * local_rows
        group = width // 4
        text_width = caption.shape[1]

        unit = width // (4 * z_size)
        inside = unit % 128 == 0
        order = [4 * k + j for k in range(z_size) for j in (0, 2, 1, 3)] if inside else None

        def outer(values):
            return values if inside else layer_order(values)

        w_qkv, w_cross = w_qkv.transpose(1, 0, 2), w_cross.transpose(1, 0, 2)
        first = swap_parts(pick_weights(w_qkv, w_out, rank))
        first = gather_rows(place(first, rank))

        positions = lax.axis_index("y") * local_rows + jnp.arange(local_rows, dtype=jnp.int32)
        ranks = jnp.arange(full_length, dtype=jnp.int32)
        matches = (mask_index[:, :, None] == positions[None, None, :]) & (
            ranks[None, :, None] < mask_count[:, None, None]
        )
        masked = jnp.any(matches, axis=1).reshape(tokens, 1).astype(F32)
        gains = layer_order(norm_gains)
        gain_a, gain_b, gain_c = gains[:1], gains[1:2], gains[2:]
        start_x, attn_in, grad_top = start(
            outer(hidden.reshape(tokens, width)),
            outer(cotangent.reshape(tokens, width)),
            masked,
            layer_order(mask_embed)[None],
            gain_a,
            unit,
            order,
        )
        attn_in = gather_tokens(attn_in)
        mid = jnp.concatenate([column_blocks(w_cross[0], 4), column_blocks(w_cross_out, 4)], axis=2)
        up = column_blocks(w_up, 4)
        attn_in, mid, up = lax.optimization_barrier((attn_in, mid, up))
        mid, up = gather_rows(trade(mid)), gather_rows(trade(up))

        own_text, kv_part = text_forward(caption, w_text, w_cross)
        text_kv = trade(kv_part, PLANE).astype(F32).sum(axis=0).astype(BF)
        text_kv = sum_z(text_kv)
        other = swap(text_kv, "c")
        text_kv = jnp.concatenate(
            [jnp.where(core == 0, text_kv, other), jnp.where(core == 0, other, text_kv)], axis=0
        )
        attn_in, text_kv = lax.optimization_barrier((attn_in, text_kv))

        attn_in, projected = gather_mm(attn_in, first, 0, 3 * group, "qkv_mm")
        self_mixed = self_forward(projected, 2 * images)
        down = column_blocks(w_down, 4)
        self_mixed, down = lax.optimization_barrier((self_mixed, down))
        down = gather_rows(trade(down))
        parts = mm_scatter(self_mixed, first[:, 3 * group :])
        after_attn, cross_in = add_norm([start_x] + parts, gain_b)

        cross_in, cross_queries = gather_mm(gather_tokens(cross_in), mid, 0, group, "query_mm")
        cross_mixed = cross_forward(cross_queries, text_kv)
        parts = mm_scatter(cross_mixed, mid[:, group:])
        after_cross, mlp_in = add_norm([after_attn] + parts, gain_c)

        mlp_in = gather_tokens(mlp_in)
        mlp_in, grad_top = lax.optimization_barrier((mlp_in, grad_top))
        grad_y = jnp.concatenate(gather_tokens(grad_top), axis=0)
        mlp_in, activated, slope = feed_up(mlp_in, up)
        early = [attn_in, self_mixed, cross_in, cross_mixed]
        if inside:
            grad_axes, halves = "z", (core, z_size)

            def both(values):
                return [values, swap(values, "c")]

        else:
            grad_axes, halves = DATA, ()

            def both(values):
                return [values]

        early = [both(values) for values in early]
        down_part = grad_products([(both(grad_y), both(activated))], "down_grads", *halves)
        mlp_in = both(mlp_in)
        slope, down_part, early, mlp_in = lax.optimization_barrier((slope, down_part, early, mlp_in))
        down_rows = scatter_grad(down_part, grad_axes)
        grad_pre = feed_down(grad_y, slope, down)
        parts = mm_scatter(grad_pre, up)
        up_part = grad_products([(mlp_in, both(grad_pre))], "up_grads", *halves)
        grad_after_cross, cross_branch, gain_grad_c = norm_back(
            parts, grad_top, after_cross, gain_c
        )

        cross_branch = gather_tokens(cross_branch)
        cross_branch, up_part = lax.optimization_barrier((cross_branch, up_part))
        cross_branch, grad_cross_mixed = gather_mm(
            cross_branch, mid, group, group, "cross_out_back"
        )
        grad_cq, kv_grad = cross_back(cross_queries, text_kv, grad_cross_mixed)
        up_part, down_rows, kv_grad = lax.optimization_barrier((up_part, down_rows, kv_grad))
        up_rows = scatter_grad(up_part, grad_axes)
        cross_branch, grad_cq_both = both(cross_branch), both(grad_cq)
        parts = mm_scatter(grad_cq, mid[:, :group])
        grad_after_attn, attn_branch, gain_grad_b = norm_back(
            parts, grad_after_cross, after_attn, gain_b
        )

        attn_branch, grad_self_mixed = gather_mm(
            gather_tokens(attn_branch), first, 3 * group, group, "out_back"
        )
        grad_projected = self_back(projected, grad_self_mixed, 2 * images)
        rest_part = grad_products(
            [
                (early[0], both(grad_projected)),
                (both(attn_branch), early[1]),
                (early[2], grad_cq_both),
                (cross_branch, early[3]),
            ],
            "attention_grads",
            *halves,
        )
        grad_projected, activated, kv_grad, rest_part = lax.optimization_barrier(
            (grad_projected, activated, kv_grad, rest_part)
        )
        rest_part, up_rows = lax.optimization_barrier((rest_part, up_rows))
        rest_rows = scatter_grad(rest_part, grad_axes)
        parts = mm_scatter(grad_projected, first[:, : 3 * group])
        grad_hidden, gain_grad_a, mask_grad = last_back(
            parts,
            grad_after_attn,
            start_x,
            gain_a,
            masked,
            unit,
            order,
        )
        sums = jnp.concatenate([gain_grad_a, gain_grad_b, gain_grad_c, mask_grad], axis=0)

        result = mm_scatter(activated, down)

        kv_halves = kv_grad.reshape(2, -1, 2 * group)
        kv_keep = lax.dynamic_index_in_dim(kv_halves, core, 0, keepdims=False)
        kv_send = lax.dynamic_index_in_dim(kv_halves, 1 - core, 0, keepdims=False)
        kv_sum = sum_z((kv_keep + swap(kv_send, "c")).astype(BF))
        wide_rows = swap_parts(pick_rows([down_rows, up_rows], rank))
        kv_sum, wide_rows = lax.optimization_barrier((kv_sum, wide_rows))
        kv_grads = spread(kv_sum, PLANE, 8)
        kv_weight_grad, grad_text_w, caption_part = text_back(
            kv_grads, own_text, w_cross, caption, w_text, halves_of(sums, text_width // 4)
        )
        half_context = caption.shape[0] // 2
        caption_part = trade(caption_part, PLANE).astype(F32).sum(axis=0)
        sums = layer_order(add_z(whole_of(caption_part[half_context:], width)))
        caption_part = caption_part[:half_context].astype(BF).reshape(z_size, -1, text_width // 4)
        caption_part = trade(caption_part, "z").astype(F32).sum(axis=0).astype(BF)
        output = layer_output(after_cross, result, unit, order)
        down_grad, up_grad = finish_wide(wide_rows, rank)
        rest_rows = pick_rows([rest_rows], rank)
        caption_part, rest_rows, sums, output, down_grad, up_grad = lax.optimization_barrier(
            (caption_part, rest_rows, sums, output, down_grad, up_grad)
        )
        caption_part = spread(caption_part, "z", z_size).reshape(half_context, -1)
        grad_caption = caption_output(spread(caption_part, PLANE, 8))

        qkv_grad, out_grad, grad_cross, cross_out_grad = finish_all(
            swap_parts(rest_rows), kv_weight_grad, rank
        )
        return (
            outer(output).reshape(hidden.shape),
            outer(grad_hidden).reshape(hidden.shape),
            grad_caption,
            sums[:3],
            sums[3],
            qkv_grad.transpose(1, 0, 2),
            out_grad,
            grad_cross.transpose(1, 0, 2),
            cross_out_grad,
            grad_text_w,
            up_grad,
            down_grad,
        )

    return local


def solution(mesh):
    z_size = mesh.shape["img"] // 4
    inner = Mesh(mesh.devices.reshape(z_size, 2, 2, 2), ("z", "x", "c", "y"))
    image = ("z", "x", "c")
    tokens = P(image, "y", None)
    rows = P(image + ("y",))
    in_specs = (tokens, P(image, None), P(image), P(), P(), P()) + (rows,) * 7 + (tokens,)
    out_specs = (tokens, tokens, P(), P(), P()) + (rows,) * 7
    return jax.shard_map(
        make_local(z_size), mesh=inner, in_specs=in_specs, out_specs=out_specs, check_vma=False
    )
```

```python
import math

import jax
import jax.numpy as jnp
from jax import lax
from jax.experimental import pallas as pl
from jax.experimental.pallas import tpu as pltpu
from jax.sharding import Mesh
from jax.sharding import PartitionSpec as P

HD = 128
EPS = 1e-05
BF = jnp.bfloat16
F32 = jnp.float32
PAIR = ((0, 1), (1, 0))
GROUP = ("x", "y")
DATA = ("z", "c")
PLANE = ("x", "c", "y")
VMEM = 48 * 1024 * 1024
SCALE = 1.0 / math.sqrt(HD)
SLOPE = math.sqrt(2.0 / math.pi)
CUBIC = 0.044715


def dot(a, b, dims):
    return lax.dot_general(a, b, (dims, ((), ())), preferred_element_type=F32)


def mm(a, b):
    return dot(a, b, ((1,), (0,)))


def mm_t(a, b):
    return dot(a, b, ((1,), (1,)))


def t_mm(a, b):
    return dot(a, b, ((0,), (0,)))


def shape(dims, dtype=BF):
    return jax.ShapeDtypeStruct(dims, dtype)


def swap(values, axis):
    return lax.ppermute(values, axis, PAIR)


def trade(blocks, axes=GROUP):
    return lax.all_to_all(blocks, axes, 0, 0, tiled=True)


def spread(values, axes=GROUP, count=4):
    return trade(jnp.broadcast_to(values[None], (count,) + values.shape), axes)


def gather_tokens(own):
    half = own.shape[0] // 2
    from_x = swap(own, "x")
    from_y = swap(own, "y")
    return own, from_y, from_x, swap(from_x[:half], "y"), swap(from_y[half:], "x")


def scatter_first(parts):
    own, for_y, for_x, for_low, for_high = parts
    half = for_low.shape[0]
    low = swap(for_low, "y").astype(F32) + for_x[:half].astype(F32)
    high = swap(for_high, "x").astype(F32) + for_y[half:].astype(F32)
    return (
        own,
        jnp.concatenate([low.astype(BF), for_x[half:]], axis=0),
        jnp.concatenate([for_y[:half], high.astype(BF)], axis=0),
    )


def scatter_second(parts):
    own, for_x, for_y = parts
    return [own, swap(for_x, "x"), swap(for_y, "y")]


def scatter_tokens(parts):
    return scatter_second(scatter_first(parts))


def swap_parts(parts):
    return [
        parts[0],
        swap(parts[1], "y"),
        swap(parts[2], "x"),
        lax.ppermute(parts[3], GROUP, ((0, 3), (1, 2), (2, 1), (3, 0))),
    ]


def gather_rows(rows):
    return lax.all_gather(rows.reshape(-1, rows.shape[-1]), DATA, axis=0, tiled=True)


def scatter_grad(partial, axes):
    summed = lax.psum_scatter(partial, axes, scatter_dimension=0, tiled=True)
    return summed.reshape(4, -1, summed.shape[-1])


def call(kernel, grid, in_specs, out_specs, out_shape, operands, name, flops=0, size=1 << 22,
         rank=None, scratch=()):
    options = dict(
        out_shape=out_shape,
        compiler_params=pltpu.CompilerParams(vmem_limit_bytes=VMEM),
        cost_estimate=pl.CostEstimate(flops=flops, bytes_accessed=size, transcendentals=0),
        name=name,
    )
    if rank is None:
        return pl.pallas_call(
            kernel, grid=grid, in_specs=in_specs, out_specs=out_specs, scratch_shapes=scratch,
            **options,
        )(*operands)
    spec = pltpu.PrefetchScalarGridSpec(
        num_scalar_prefetch=1,
        grid=grid,
        in_specs=in_specs,
        out_specs=out_specs,
        scratch_shapes=scratch,
    )
    return pl.pallas_call(kernel, grid_spec=spec, **options)(rank.reshape(1), *operands)


def whole(array):
    return pl.BlockSpec(array.shape, lambda *_: (0,) * len(array.shape))


def reorder(values, unit, order):
    if order is None:
        return values
    return jnp.concatenate([values[:, k * unit : (k + 1) * unit] for k in order], axis=1)


def assemble(target, pieces, sems):
    copies, at = [], 0
    for k, piece in enumerate(pieces):
        rows = piece.shape[0]
        copies.append(pltpu.make_async_copy(piece, target.at[at : at + rows], sems.at[k]))
        at += rows
    for copy in copies:
        copy.start()
    for copy in copies:
        copy.wait()


ANY = pl.BlockSpec(memory_space=pl.ANY)


def gather_mm(pieces, weight, first, columns, name):
    rows, width = pieces[0].shape
    step = 256

    def kernel(*refs):
        tokens, out, sems = refs[6:]

        @pl.when(pl.program_id(0) == 0)
        def _():
            assemble(tokens, refs[:5], sems)

        out[...] = mm(tokens[...], refs[5][...]).astype(BF)

    return call(
        kernel,
        (columns // step,),
        [ANY] * 5 + [pl.BlockSpec((width, step), lambda j: (0, first // step + j))],
        [
            pl.BlockSpec((4 * rows, width), lambda j: (0, 0)),
            pl.BlockSpec((4 * rows, step), lambda j: (0, j)),
        ],
        [shape((4 * rows, width)), shape((4 * rows, columns))],
        [*pieces, weight],
        name,
        flops=8 * rows * width * columns,
        size=2 * width * (columns + 8 * rows),
        scratch=[pltpu.SemaphoreType.DMA((5,))],
    )


def mm_scatter(values, weight):
    return scatter_tokens(token_blocks(mm_t(values, weight).astype(BF)))


def token_blocks(partial):
    rows = partial.shape[0] // 4
    cuts = [0, rows, 2 * rows, 3 * rows, 3 * rows + rows // 2, 4 * rows]
    return [partial[a:b] for a, b in zip(cuts, cuts[1:])]


def normalize(values):
    centred = values - jnp.mean(values, axis=-1, keepdims=True)
    inv_std = lax.rsqrt(jnp.mean(centred * centred, axis=-1, keepdims=True) + EPS)
    return centred * inv_std, inv_std


NORM_ROWS = 32


def row_spec(array, at=None):
    width = array.shape[-1]
    if at is None:
        return pl.BlockSpec((NORM_ROWS, width), lambda i: (i, 0))
    return pl.BlockSpec((1, NORM_ROWS, width), lambda i, at=at: (at, i, 0))


def terms_of(terms):
    arrays, specs = [], []
    for term in terms:
        array, at = term if isinstance(term, tuple) else (term, None)
        arrays.append(array)
        specs.append(row_spec(array, at))
    return arrays, specs


def total_of(refs):
    values = [ref[0] if len(ref.shape) == 3 else ref[...] for ref in refs]
    return sum(value.astype(F32) for value in values)


def add_norm(terms, gain):
    arrays, specs = terms_of(terms)
    tokens, width = arrays[0].shape[-2], arrays[0].shape[-1]
    tokens = min(a.shape[-2] for a in arrays)

    def kernel(*refs):
        gain_ref, x, out = refs[-3:]
        values = total_of(refs[:-3])
        x[...] = values
        out[...] = (normalize(values)[0] * gain_ref[...]).astype(BF)

    return call(
        kernel,
        (tokens // NORM_ROWS,),
        specs + [whole(gain)],
        [row_spec(shape((tokens, width)))] * 2,
        [shape((tokens, width), F32), shape((tokens, width))],
        [*arrays, gain],
        "add_norm",
    )


def norm_grad(grad, values, gain):
    normed, inv_std = normalize(values)
    scaled = grad * gain
    first_mean = jnp.mean(scaled, axis=-1, keepdims=True)
    second_mean = jnp.mean(scaled * normed, axis=-1, keepdims=True)
    return (
        inv_std * (scaled - first_mean - normed * second_mean),
        jnp.sum(grad * normed, axis=0, keepdims=True),
    )


def accumulate(ref, value):
    @pl.when(pl.program_id(0) == 0)
    def _():
        ref[...] = jnp.zeros_like(ref)

    ref[...] += value


def norm_back(terms, upper, values, gain):
    arrays, specs = terms_of(terms)
    tokens, width = values.shape

    def kernel(*refs):
        upper_ref, x, gain_ref, out, out_low, gain_grad = refs[-6:]
        back, part = norm_grad(total_of(refs[:-6]), x[...], gain_ref[...])
        result = upper_ref[...].astype(F32) + back
        out[...] = result
        out_low[...] = result.astype(BF)
        accumulate(gain_grad, part)

    return call(
        kernel,
        (tokens // NORM_ROWS,),
        specs + [row_spec(upper), row_spec(values), whole(gain)],
        [row_spec(values)] * 2 + [pl.BlockSpec((1, width), lambda i: (0, 0))],
        [shape((tokens, width), F32), shape((tokens, width)), shape((1, width), F32)],
        [*arrays, upper, values, gain],
        "norm_back",
    )


def last_back(terms, upper, values, gain, masked, unit, order):
    arrays, specs = terms_of(terms)
    tokens, width = values.shape

    def kernel(*refs):
        upper_ref, x, gain_ref, mask, out, gain_grad, mask_grad = refs[-7:]
        back, part = norm_grad(total_of(refs[:-7]), x[...], gain_ref[...])
        result = upper_ref[...].astype(F32) + back
        hit = mask[...] > 0.5
        out[...] = reorder(jnp.where(hit, 0.0, result).astype(BF), unit, order)
        accumulate(gain_grad, part)
        accumulate(mask_grad, jnp.sum(jnp.where(hit, result, 0.0), axis=0, keepdims=True))

    line = pl.BlockSpec((1, width), lambda i: (0, 0))
    return call(
        kernel,
        (tokens // NORM_ROWS,),
        specs + [row_spec(upper), row_spec(values), whole(gain), row_spec(masked)],
        [row_spec(values), line, line],
        [shape((tokens, width)), shape((1, width), F32), shape((1, width), F32)],
        [*arrays, upper, values, gain, masked],
        "last_back",
    )


def start(hidden, cotangent, masked, embed, gain, unit, order):
    tokens, width = hidden.shape

    def kernel(hid, cot, mask, embed_ref, gain_ref, x, out, grad):
        hit = mask[...] > 0.5
        values = jnp.where(
            hit, embed_ref[...], reorder(hid[...], unit, order).astype(F32)
        )
        x[...] = values
        out[...] = (normalize(values)[0] * gain_ref[...]).astype(BF)
        grad[...] = jnp.where(hit, reorder(cot[...], unit, order).astype(F32), 0.0).astype(BF)

    rows = row_spec(hidden)
    return call(
        kernel,
        (tokens // NORM_ROWS,),
        [rows, rows, row_spec(masked), whole(embed), whole(gain)],
        [rows] * 3,
        [shape((tokens, width), F32), shape((tokens, width)), shape((tokens, width))],
        [hidden, cotangent, masked, embed, gain],
        "start",
    )


def layer_output(upper, terms, unit, order):
    arrays, specs = terms_of(terms)
    tokens, width = upper.shape

    def kernel(*refs):
        values = refs[-2][...] + total_of(refs[:-2])
        refs[-1][...] = reorder(values.astype(BF), unit, order)

    return call(
        kernel,
        (tokens // NORM_ROWS,),
        specs + [row_spec(upper)],
        row_spec(upper),
        shape((tokens, width)),
        [*arrays, upper],
        "layer_output",
    )


def feed_up(pieces, weight):
    rows, width = pieces[0].shape
    hidden = weight.shape[1]
    step = 256

    def kernel(*refs):
        up, tokens, act, slope, sems = refs[5:]

        @pl.when(pl.program_id(0) == 0)
        def _():
            assemble(tokens, refs[:5], sems)

        u = mm(tokens[...], up[...])
        square = u * u
        bend = jnp.tanh(SLOPE * u * (1.0 + CUBIC * square))
        half = 0.5 * (1.0 + bend)
        act[...] = (u * half).astype(BF)
        slope[...] = half + 0.5 * u * (1.0 - bend * bend) * SLOPE * (1.0 + 3.0 * CUBIC * square)

    part = pl.BlockSpec((4 * rows, step), lambda j: (0, j))
    return call(
        kernel,
        (hidden // step,),
        [ANY] * 5 + [pl.BlockSpec((width, step), lambda j: (0, j))],
        [pl.BlockSpec((4 * rows, width), lambda j: (0, 0)), part, part],
        [shape((4 * rows, width)), shape((4 * rows, hidden)), shape((4 * rows, hidden), F32)],
        [*pieces, weight],
        "feed_up",
        scratch=[pltpu.SemaphoreType.DMA((5,))],
        flops=8 * rows * width * hidden,
        size=2 * width * (hidden + 8 * rows),
    )


def feed_down(grad_y, slope, weight):
    tokens, width = grad_y.shape
    hidden = weight.shape[1]
    step = 256

    def kernel(dy, slope_ref, down, out):
        out[...] = (mm(dy[...], down[...]) * slope_ref[...]).astype(BF)

    part = pl.BlockSpec((tokens, step), lambda j: (0, j))
    return call(
        kernel,
        (hidden // step,),
        [whole(grad_y), part, pl.BlockSpec((width, step), lambda j: (0, j))],
        part,
        shape((tokens, hidden)),
        [grad_y, slope, weight],
        "feed_down",
        flops=2 * tokens * width * hidden,
        size=2 * width * (hidden + 8 * tokens),
    )


def softmax(scores):
    exp_terms = jnp.exp(scores - jnp.max(scores, axis=-1, keepdims=True))
    return exp_terms / jnp.sum(exp_terms, axis=-1, keepdims=True)


def score_grad(probs, grad_probs):
    return (
        probs * (grad_probs - jnp.sum(probs * grad_probs, axis=-1, keepdims=True))
    ).astype(BF)


def head(ref, k):
    return ref[:, k * HD : (k + 1) * HD]


def self_forward(projected, images):
    tokens, width = projected.shape
    rows, group = tokens // images, width // 3
    heads = group // HD

    def kernel(proj, mixed):
        for k in range(heads):
            query, key, value = (head(proj, j * heads + k) for j in range(3))
            probs = softmax(mm_t(query, key) * SCALE).astype(BF)
            mixed[:, k * HD : (k + 1) * HD] = mm(probs, value).astype(BF)

    return call(
        kernel,
        (images,),
        [pl.BlockSpec((rows, width), lambda i: (i, 0))],
        pl.BlockSpec((rows, group), lambda i: (i, 0)),
        shape((tokens, group)),
        [projected],
        "self_forward",
        flops=4 * tokens * rows * group,
    )


def self_back(projected, grad_mixed, images):
    tokens, width = projected.shape
    rows, group = tokens // images, width // 3
    heads = group // HD

    def kernel(proj, grad, out):
        for k in range(heads):
            query, key, value = (head(proj, j * heads + k) for j in range(3))
            grad_head = head(grad, k)
            probs = softmax(mm_t(query, key) * SCALE)
            grad_scores = score_grad(probs, mm_t(grad_head, value))
            parts = (
                mm(grad_scores, key) * SCALE,
                t_mm(grad_scores, query) * SCALE,
                t_mm(probs.astype(BF), grad_head),
            )
            for j, part in enumerate(parts):
                at = (j * heads + k) * HD
                out[:, at : at + HD] = part.astype(BF)

    return call(
        kernel,
        (images,),
        [
            pl.BlockSpec((rows, width), lambda i: (i, 0)),
            pl.BlockSpec((rows, group), lambda i: (i, 0)),
        ],
        pl.BlockSpec((rows, width), lambda i: (i, 0)),
        shape((tokens, width)),
        [projected, grad_mixed],
        "self_back",
        flops=10 * tokens * rows * group,
    )


def cross_forward(queries, text_kv):
    tokens, group = queries.shape
    heads = group // HD

    def kernel(query, text, mixed):
        for k in range(heads):
            probs = softmax(mm_t(head(query, k), head(text, k)) * SCALE).astype(BF)
            mixed[:, k * HD : (k + 1) * HD] = mm(probs, head(text, heads + k)).astype(BF)

    return call(
        kernel,
        (1,),
        [whole(queries), whole(text_kv)],
        whole(queries),
        shape((tokens, group)),
        [queries, text_kv],
        "cross_forward",
        flops=4 * tokens * text_kv.shape[0] * group,
    )


def cross_back(queries, text_kv, grad_mixed):
    tokens, group = queries.shape
    context = text_kv.shape[0]
    heads = group // HD

    def kernel(query, text, grad, grad_query, grad_text):
        for k in range(heads):
            query_head, key, value = head(query, k), head(text, k), head(text, heads + k)
            grad_head = head(grad, k)
            probs = softmax(mm_t(query_head, key) * SCALE)
            grad_scores = score_grad(probs, mm_t(grad_head, value))
            grad_query[:, k * HD : (k + 1) * HD] = (mm(grad_scores, key) * SCALE).astype(BF)
            at = (heads + k) * HD
            grad_text[:, k * HD : (k + 1) * HD] = t_mm(grad_scores, query_head) * SCALE
            grad_text[:, at : at + HD] = t_mm(probs.astype(BF), grad_head)

    return call(
        kernel,
        (1,),
        [whole(queries), whole(text_kv), whole(grad_mixed)],
        [whole(queries), whole(text_kv)],
        [shape((tokens, group)), shape((context, 2 * group), F32)],
        [queries, text_kv, grad_mixed],
        "cross_back",
        flops=10 * tokens * context * group,
    )


def grad_products(pairs, name, core=None, blocks=0):
    count_in = len(pairs[0][0])
    tokens, width = pairs[0][0][0].shape
    widths = [y[0].shape[1] for _, y in pairs]
    total = sum(widths)
    rows = 256 if core is None else width // (2 * blocks)
    steps = width // rows if core is None else blocks
    step = 512
    count = len(pairs) * count_in

    def kernel(r, *refs):
        out = refs[2 * count]
        offset = 0
        for k, wide in enumerate(widths):
            left = [refs[k * count_in + b][...].T for b in range(count_in)]
            for at in range(0, wide, step):
                out[:, offset + at : offset + at + step] = sum(
                    mm(left[b], refs[count + k * count_in + b][:, at : at + step])
                    for b in range(count_in)
                ).astype(BF)
            offset += wide

    pick = (lambda i, r: (0, i)) if core is None else (lambda i, r: (0, 2 * i + r[0]))
    return call(
        kernel,
        (steps,),
        [pl.BlockSpec((tokens, rows), pick)] * count
        + [pl.BlockSpec((tokens, w), lambda i, r: (0, 0)) for w in widths for _ in range(count_in)],
        pl.BlockSpec((rows, total), lambda i, r: (i, 0)),
        shape((steps * rows, total)),
        [b for x, _ in pairs for b in x] + [b for _, y in pairs for b in y],
        name,
        flops=2 * tokens * count_in * steps * rows * total,
        size=4 * width * total,
        rank=jnp.zeros((), jnp.int32) if core is None else core,
    )


def pick_weights(three, one, rank):
    rows, width = one.shape[0], one.shape[1] // 4

    def kernel(r, three_ref, one_ref, *outs):
        for k in range(4):

            @pl.when(pl.program_id(0) == k)
            def _():
                for j in range(3):
                    outs[k][:, j * width : (j + 1) * width] = three_ref[j]
                outs[k][:, 3 * width :] = one_ref[...]

    outs = [shape((rows, 4 * width))] * 4
    return call(
        kernel,
        (4,),
        [
            pl.BlockSpec((3, rows, width), lambda k, r: (0, 0, k ^ r[0])),
            pl.BlockSpec((rows, width), lambda k, r: (0, k ^ r[0])),
        ],
        [whole(a) for a in outs],
        outs,
        [three, one],
        "pick_weights",
        rank=rank,
    )


def pick_rows(arrays, rank):
    rows = arrays[0].shape[1]
    widths = [a.shape[2] for a in arrays]
    count = len(arrays)

    def kernel(r, *refs):
        for k in range(4):

            @pl.when(pl.program_id(0) == k)
            def _():
                at = 0
                for ref, width in zip(refs, widths):
                    refs[count + k][:, at : at + width] = ref[0]
                    at += width

    outs = [shape((rows, sum(widths)))] * 4
    return call(
        kernel,
        (4,),
        [pl.BlockSpec((1, rows, w), lambda k, r: (k ^ r[0], 0, 0)) for w in widths],
        [whole(a) for a in outs],
        outs,
        arrays,
        "pick_rows",
        rank=rank,
    )


def place(parts, rank):
    def kernel(r, *refs):
        for k in range(4):

            @pl.when(pl.program_id(0) == k)
            def _():
                refs[4][0] = refs[k][...]

    rows, columns = parts[0].shape
    return call(
        kernel,
        (4,),
        [whole(p) for p in parts],
        pl.BlockSpec((1, rows, columns), lambda k, r: (k ^ r[0], 0, 0)),
        shape((4, rows, columns)),
        parts,
        "place",
        rank=rank,
    )


def finish_wide(parts, rank):
    rows, total = parts[0].shape
    width = total // 2

    def kernel(r, *refs):
        for k in range(4):

            @pl.when(pl.program_id(0) == k)
            def _():
                refs[4][...] = refs[k][:, :width].astype(F32)
                refs[5][...] = refs[k][:, width:].astype(F32)

    flat = pl.BlockSpec((rows, width), lambda k, r: (0, k ^ r[0]))
    return call(
        kernel,
        (4,),
        [whole(p) for p in parts],
        [flat, flat],
        [shape((rows, 4 * width), F32)] * 2,
        parts,
        "finish_wide",
        rank=rank,
    )


def finish_all(parts, text_grad, rank):
    rows, total = parts[0].shape
    width = total // 6

    def kernel(r, *refs):
        key, value, three, out, cross, cross_out = refs[4:]
        for k in range(4):

            @pl.when(pl.program_id(0) == k)
            def _():
                def part(j):
                    return refs[k][:, j * width : (j + 1) * width].astype(F32)

                for j in range(3):
                    three[j] = part(j)
                out[...] = part(3)
                cross[0] = part(4)
                cross_out[...] = part(5)

        cross[1] = key[...]
        cross[2] = value[...]

    wide = pl.BlockSpec((3, rows, width), lambda k, r: (0, 0, k ^ r[0]))
    flat = pl.BlockSpec((rows, width), lambda k, r: (0, k ^ r[0]))
    return call(
        kernel,
        (4,),
        [whole(p) for p in parts]
        + [flat, pl.BlockSpec((rows, width), lambda k, r: (0, 4 + (k ^ r[0])))],
        [wide, flat, wide, flat],
        [shape((3, rows, 4 * width), F32), shape((rows, 4 * width), F32)] * 2,
        [*parts, text_grad, text_grad],
        "finish_all",
        rank=rank,
    )


def plane_block(k):
    return (k >> 1) & 1, (k >> 2) * 2 + (k & 1)


def text_forward(caption, w_text, w_cross):
    context, rows = caption.shape[0], w_text.shape[0]
    half, width = context // 2, w_cross.shape[2] // 4

    def kernel(cap, weight, cross, own, blocks):
        own[...] = mm_t(cap[...], weight[...]).astype(BF)
        for j in range(2):
            part = mm(own[...], cross[1 + j]).astype(BF)
            for k in range(8):
                core, group = plane_block(k)
                blocks[k, :, j * width : (j + 1) * width] = part[
                    core * half : (core + 1) * half, group * width : (group + 1) * width
                ]

    return call(
        kernel,
        (1,),
        [whole(caption), whole(w_text), whole(w_cross)],
        [
            pl.BlockSpec((context, rows), lambda i: (0, 0)),
            pl.BlockSpec((8, half, 2 * width), lambda i: (0, 0, 0)),
        ],
        [shape((context, rows)), shape((8, half, 2 * width))],
        [caption, w_text, w_cross],
        "text_forward",
    )


def text_back(blocks, own_text, w_cross, caption, w_text, extra):
    context, rows = own_text.shape
    half, width = context // 2, w_cross.shape[2] // 4
    wide = caption.shape[1] // 4
    tail = extra.shape[0]

    def kernel(block, own, cross, cap, weight, more, kv_grad, text_grad, out, grads):
        for k in range(8):
            core, group = plane_block(k)
            for j in range(2):
                at = (4 * j + group) * width
                grads[core * half : (core + 1) * half, at : at + width] = block[
                    k, :, j * width : (j + 1) * width
                ]
        kv_grad[...] = t_mm(own[...], grads[...])
        grad_text = sum(
            mm_t(grads[:, 4 * j * width : 4 * (j + 1) * width], cross[1 + j]) for j in range(2)
        ).astype(BF)
        text_grad[...] = t_mm(grad_text, cap[...])
        part = mm(grad_text, weight[...]).astype(BF)
        for k in range(8):
            core, group = plane_block(k)
            out[k, :half, :] = part[core * half : (core + 1) * half, group * wide : (group + 1) * wide]
            out[k, half:, :] = more[...]

    operands = [blocks, own_text, w_cross, caption, w_text, extra]
    outs = [
        shape((rows, 8 * width), F32),
        shape((rows, 4 * wide), F32),
        shape((8, half + tail, wide)),
    ]
    return call(
        kernel,
        (1,),
        [whole(a) for a in operands],
        [whole(a) for a in outs],
        outs,
        operands,
        "text_back",
        scratch=[pltpu.VMEM((context, 8 * width), BF)],
    )


def caption_output(blocks):
    count, half, wide = blocks.shape

    def kernel(block, out):
        out[...] = block[0].astype(F32)

    return call(
        kernel,
        (count,),
        [pl.BlockSpec((1, half, wide), lambda k: (k, 0, 0))],
        pl.BlockSpec((half, wide), lambda k: plane_block(k)),
        shape((2 * half, 4 * wide), F32),
        [blocks],
        "caption_output",
    )


def column_blocks(weight, count):
    rows = weight.shape[0]
    return weight.reshape(rows, count, -1).transpose(1, 0, 2)


def halves_of(values, width):
    high = values.astype(BF)
    low = (values - high.astype(F32)).astype(BF)
    return jnp.concatenate([high.reshape(-1, width), low.reshape(-1, width)], axis=0)


def whole_of(halves, width):
    rows = halves.shape[0] // 2
    return (halves[:rows] + halves[rows:]).reshape(-1, width)


def make_local(z_size):
    def sum_z(values):
        parts = values.reshape(z_size, -1, values.shape[-1])
        mine = trade(parts, "z").astype(F32).sum(axis=0).astype(BF)
        return spread(mine, "z", z_size).reshape(values.shape)

    def add_z(values):
        step = 1
        while step < z_size:
            values = values + lax.ppermute(
                values, "z", tuple((k, k ^ step) for k in range(z_size))
            )
            step *= 2
        return values

    def layer_order(values):
        shaped = values.reshape(values.shape[:-1] + (z_size, 2, 2, -1))
        return jnp.swapaxes(shaped, -3, -2).reshape(values.shape)

    def local(
        hidden,
        mask_index,
        mask_count,
        mask_embed,
        norm_gains,
        caption,
        w_qkv,
        w_out,
        w_cross,
        w_cross_out,
        w_text,
        w_up,
        w_down,
        cotangent,
    ):
        images, local_rows, width = hidden.shape
        full_length = mask_index.shape[1]
        rank = lax.axis_index("x") * 2 + lax.axis_index("y")
        core = lax.axis_index("c")
        tokens = images * local_rows
        group = width // 4
        text_width = caption.shape[1]

        unit = width // (4 * z_size)
        inside = unit % 128 == 0
        order = [4 * k + j for k in range(z_size) for j in (0, 2, 1, 3)] if inside else None

        def outer(values):
            return values if inside else layer_order(values)

        w_qkv, w_cross = w_qkv.transpose(1, 0, 2), w_cross.transpose(1, 0, 2)
        first = swap_parts(pick_weights(w_qkv, w_out, rank))
        first = gather_rows(place(first, rank))

        positions = lax.axis_index("y") * local_rows + jnp.arange(local_rows, dtype=jnp.int32)
        ranks = jnp.arange(full_length, dtype=jnp.int32)
        matches = (mask_index[:, :, None] == positions[None, None, :]) & (
            ranks[None, :, None] < mask_count[:, None, None]
        )
        masked = jnp.any(matches, axis=1).reshape(tokens, 1).astype(F32)
        gains = layer_order(norm_gains)
        gain_a, gain_b, gain_c = gains[:1], gains[1:2], gains[2:]
        start_x, attn_in, grad_top = start(
            outer(hidden.reshape(tokens, width)),
            outer(cotangent.reshape(tokens, width)),
            masked,
            layer_order(mask_embed)[None],
            gain_a,
            unit,
            order,
        )
        attn_in = gather_tokens(attn_in)
        mid = jnp.concatenate([column_blocks(w_cross[0], 4), column_blocks(w_cross_out, 4)], axis=2)
        up = column_blocks(w_up, 4)
        attn_in, mid, up = lax.optimization_barrier((attn_in, mid, up))
        mid, up = gather_rows(trade(mid)), gather_rows(trade(up))

        own_text, kv_part = text_forward(caption, w_text, w_cross)
        text_kv = trade(kv_part, PLANE).astype(F32).sum(axis=0).astype(BF)
        text_kv = sum_z(text_kv)
        other = swap(text_kv, "c")
        text_kv = jnp.concatenate(
            [jnp.where(core == 0, text_kv, other), jnp.where(core == 0, other, text_kv)], axis=0
        )
        attn_in, text_kv = lax.optimization_barrier((attn_in, text_kv))

        attn_in, projected = gather_mm(attn_in, first, 0, 3 * group, "qkv_mm")
        self_mixed = self_forward(projected, 2 * images)
        down = column_blocks(w_down, 4)
        self_mixed, down = lax.optimization_barrier((self_mixed, down))
        down = gather_rows(trade(down))
        parts = mm_scatter(self_mixed, first[:, 3 * group :])
        after_attn, cross_in = add_norm([start_x] + parts, gain_b)

        cross_in, cross_queries = gather_mm(gather_tokens(cross_in), mid, 0, group, "query_mm")
        cross_mixed = cross_forward(cross_queries, text_kv)
        parts = mm_scatter(cross_mixed, mid[:, group:])
        after_cross, mlp_in = add_norm([after_attn] + parts, gain_c)

        mlp_in = gather_tokens(mlp_in)
        mlp_in, grad_top = lax.optimization_barrier((mlp_in, grad_top))
        grad_y = jnp.concatenate(gather_tokens(grad_top), axis=0)
        mlp_in, activated, slope = feed_up(mlp_in, up)
        early = [attn_in, self_mixed, cross_in, cross_mixed]
        if inside:
            grad_axes, halves = "z", (core, z_size)

            def both(values):
                return [values, swap(values, "c")]

        else:
            grad_axes, halves = DATA, ()

            def both(values):
                return [values]

        early = [both(values) for values in early]
        down_part = grad_products([(both(grad_y), both(activated))], "down_grads", *halves)
        mlp_in = both(mlp_in)
        slope, down_part, early, mlp_in = lax.optimization_barrier((slope, down_part, early, mlp_in))
        down_rows = scatter_grad(down_part, grad_axes)
        grad_pre = feed_down(grad_y, slope, down)
        parts = mm_scatter(grad_pre, up)
        up_part = grad_products([(mlp_in, both(grad_pre))], "up_grads", *halves)
        grad_after_cross, cross_branch, gain_grad_c = norm_back(
            parts, grad_top, after_cross, gain_c
        )

        cross_branch = gather_tokens(cross_branch)
        activated, cross_own = lax.optimization_barrier((activated, cross_branch[0]))
        result = mm_t(activated, down).astype(BF)
        cross_branch, up_part, result = lax.optimization_barrier(
            ((cross_own,) + cross_branch[1:], up_part, result)
        )
        cross_branch, grad_cross_mixed = gather_mm(
            cross_branch, mid, group, group, "cross_out_back"
        )
        grad_cq, kv_grad = cross_back(cross_queries, text_kv, grad_cross_mixed)
        up_part, down_rows, kv_grad = lax.optimization_barrier((up_part, down_rows, kv_grad))
        up_rows = scatter_grad(up_part, grad_axes)
        cross_branch, grad_cq_both = both(cross_branch), both(grad_cq)
        parts = mm_scatter(grad_cq, mid[:, :group])
        grad_after_attn, attn_branch, gain_grad_b = norm_back(
            parts, grad_after_cross, after_attn, gain_b
        )

        attn_branch, result = lax.optimization_barrier((gather_tokens(attn_branch), result))
        result = scatter_first(token_blocks(result))
        attn_branch, grad_self_mixed = gather_mm(attn_branch, first, 3 * group, group, "out_back")
        grad_projected = self_back(projected, grad_self_mixed, 2 * images)
        grad_projected, result = lax.optimization_barrier((grad_projected, result))
        result = scatter_second(result)
        rest_part = grad_products(
            [
                (early[0], both(grad_projected)),
                (both(attn_branch), early[1]),
                (early[2], grad_cq_both),
                (cross_branch, early[3]),
            ],
            "attention_grads",
            *halves,
        )
        grad_projected, result, kv_grad, rest_part = lax.optimization_barrier(
            (grad_projected, result, kv_grad, rest_part)
        )
        rest_part, up_rows = lax.optimization_barrier((rest_part, up_rows))
        rest_rows = scatter_grad(rest_part, grad_axes)
        parts = mm_scatter(grad_projected, first[:, : 3 * group])
        grad_hidden, gain_grad_a, mask_grad = last_back(
            parts,
            grad_after_attn,
            start_x,
            gain_a,
            masked,
            unit,
            order,
        )
        sums = jnp.concatenate([gain_grad_a, gain_grad_b, gain_grad_c, mask_grad], axis=0)


        kv_halves = kv_grad.reshape(2, -1, 2 * group)
        kv_keep = lax.dynamic_index_in_dim(kv_halves, core, 0, keepdims=False)
        kv_send = lax.dynamic_index_in_dim(kv_halves, 1 - core, 0, keepdims=False)
        kv_sum = sum_z((kv_keep + swap(kv_send, "c")).astype(BF))
        wide_rows = swap_parts(pick_rows([down_rows, up_rows], rank))
        kv_sum, wide_rows = lax.optimization_barrier((kv_sum, wide_rows))
        kv_grads = spread(kv_sum, PLANE, 8)
        kv_weight_grad, grad_text_w, caption_part = text_back(
            kv_grads, own_text, w_cross, caption, w_text, halves_of(sums, text_width // 4)
        )
        half_context = caption.shape[0] // 2
        caption_part = trade(caption_part, PLANE).astype(F32).sum(axis=0)
        sums = layer_order(add_z(whole_of(caption_part[half_context:], width)))
        caption_part = caption_part[:half_context].astype(BF).reshape(z_size, -1, text_width // 4)
        caption_part = trade(caption_part, "z").astype(F32).sum(axis=0).astype(BF)
        output = layer_output(after_cross, result, unit, order)
        down_grad, up_grad = finish_wide(wide_rows, rank)
        rest_rows = pick_rows([rest_rows], rank)
        caption_part, rest_rows, sums, output, down_grad, up_grad = lax.optimization_barrier(
            (caption_part, rest_rows, sums, output, down_grad, up_grad)
        )
        caption_part = spread(caption_part, "z", z_size).reshape(half_context, -1)
        grad_caption = caption_output(spread(caption_part, PLANE, 8))

        qkv_grad, out_grad, grad_cross, cross_out_grad = finish_all(
            swap_parts(rest_rows), kv_weight_grad, rank
        )
        return (
            outer(output).reshape(hidden.shape),
            outer(grad_hidden).reshape(hidden.shape),
            grad_caption,
            sums[:3],
            sums[3],
            qkv_grad.transpose(1, 0, 2),
            out_grad,
            grad_cross.transpose(1, 0, 2),
            cross_out_grad,
            grad_text_w,
            up_grad,
            down_grad,
        )

    return local


def solution(mesh):
    z_size = mesh.shape["img"] // 4
    inner = Mesh(mesh.devices.reshape(z_size, 2, 2, 2), ("z", "x", "c", "y"))
    image = ("z", "x", "c")
    tokens = P(image, "y", None)
    rows = P(image + ("y",))
    in_specs = (tokens, P(image, None), P(image), P(), P(), P()) + (rows,) * 7 + (tokens,)
    out_specs = (tokens, tokens, P(), P(), P()) + (rows,) * 7
    return jax.shard_map(
        make_local(z_size), mesh=inner, in_specs=in_specs, out_specs=out_specs, check_vma=False
    )
```

```python
import math

import jax
import jax.numpy as jnp
from jax import lax
from jax.experimental import pallas as pl
from jax.experimental.pallas import tpu as pltpu
from jax.sharding import Mesh
from jax.sharding import PartitionSpec as P

HD = 128
EPS = 1e-05
BF = jnp.bfloat16
F32 = jnp.float32
PAIR = ((0, 1), (1, 0))
GROUP = ("x", "y")
DATA = ("z", "c")
PLANE = ("x", "c", "y")
VMEM = 48 * 1024 * 1024
SCALE = 1.0 / math.sqrt(HD)
SLOPE = math.sqrt(2.0 / math.pi)
CUBIC = 0.044715


def dot(a, b, dims):
    return lax.dot_general(a, b, (dims, ((), ())), preferred_element_type=F32)


def mm(a, b):
    return dot(a, b, ((1,), (0,)))


def mm_t(a, b):
    return dot(a, b, ((1,), (1,)))


def t_mm(a, b):
    return dot(a, b, ((0,), (0,)))


def shape(dims, dtype=BF):
    return jax.ShapeDtypeStruct(dims, dtype)


def swap(values, axis):
    return lax.ppermute(values, axis, PAIR)


def trade(blocks, axes=GROUP):
    return lax.all_to_all(blocks, axes, 0, 0, tiled=True)


def spread(values, axes=GROUP, count=4):
    return trade(jnp.broadcast_to(values[None], (count,) + values.shape), axes)


def gather_tokens(own):
    half = own.shape[0] // 2
    from_x = swap(own, "x")
    from_y = swap(own, "y")
    return own, from_y, from_x, swap(from_x[:half], "y"), swap(from_y[half:], "x")


def scatter_first(parts):
    own, for_y, for_x, for_low, for_high = parts
    half = for_low.shape[0]
    low = swap(for_low, "y").astype(F32) + for_x[:half].astype(F32)
    high = swap(for_high, "x").astype(F32) + for_y[half:].astype(F32)
    return (
        own,
        jnp.concatenate([low.astype(BF), for_x[half:]], axis=0),
        jnp.concatenate([for_y[:half], high.astype(BF)], axis=0),
    )


def scatter_second(parts):
    own, for_x, for_y = parts
    return [own, swap(for_x, "x"), swap(for_y, "y")]


def scatter_tokens(parts):
    return scatter_second(scatter_first(parts))


def swap_parts(parts):
    return [
        parts[0],
        swap(parts[1], "y"),
        swap(parts[2], "x"),
        lax.ppermute(parts[3], GROUP, ((0, 3), (1, 2), (2, 1), (3, 0))),
    ]


def gather_rows(rows):
    return lax.all_gather(rows.reshape(-1, rows.shape[-1]), DATA, axis=0, tiled=True)


def scatter_grad(partial, axes):
    summed = lax.psum_scatter(partial, axes, scatter_dimension=0, tiled=True)
    return summed.reshape(4, -1, summed.shape[-1])


def call(kernel, grid, in_specs, out_specs, out_shape, operands, name, flops=0, size=1 << 22,
         rank=None, scratch=()):
    options = dict(
        out_shape=out_shape,
        compiler_params=pltpu.CompilerParams(vmem_limit_bytes=VMEM),
        cost_estimate=pl.CostEstimate(flops=flops, bytes_accessed=size, transcendentals=0),
        name=name,
    )
    if rank is None:
        return pl.pallas_call(
            kernel, grid=grid, in_specs=in_specs, out_specs=out_specs, scratch_shapes=scratch,
            **options,
        )(*operands)
    spec = pltpu.PrefetchScalarGridSpec(
        num_scalar_prefetch=1,
        grid=grid,
        in_specs=in_specs,
        out_specs=out_specs,
        scratch_shapes=scratch,
    )
    return pl.pallas_call(kernel, grid_spec=spec, **options)(rank.reshape(1), *operands)


def whole(array):
    return pl.BlockSpec(array.shape, lambda *_: (0,) * len(array.shape))


def reorder(values, unit, order):
    if order is None:
        return values
    return jnp.concatenate([values[:, k * unit : (k + 1) * unit] for k in order], axis=1)


def assemble(target, pieces, sems):
    copies, at = [], 0
    for k, piece in enumerate(pieces):
        rows = piece.shape[0]
        copies.append(pltpu.make_async_copy(piece, target.at[at : at + rows], sems.at[k]))
        at += rows
    for copy in copies:
        copy.start()
    for copy in copies:
        copy.wait()


ANY = pl.BlockSpec(memory_space=pl.ANY)


def gather_mm(pieces, weight, first, columns, name):
    rows, width = pieces[0].shape
    step = 256

    def kernel(*refs):
        tokens, out, sems = refs[6:]

        @pl.when(pl.program_id(0) == 0)
        def _():
            assemble(tokens, refs[:5], sems)

        out[...] = mm(tokens[...], refs[5][...]).astype(BF)

    return call(
        kernel,
        (columns // step,),
        [ANY] * 5 + [pl.BlockSpec((width, step), lambda j: (0, first // step + j))],
        [
            pl.BlockSpec((4 * rows, width), lambda j: (0, 0)),
            pl.BlockSpec((4 * rows, step), lambda j: (0, j)),
        ],
        [shape((4 * rows, width)), shape((4 * rows, columns))],
        [*pieces, weight],
        name,
        flops=8 * rows * width * columns,
        size=2 * width * (columns + 8 * rows),
        scratch=[pltpu.SemaphoreType.DMA((5,))],
    )


def mm_scatter(values, weight):
    return scatter_tokens(token_blocks(mm_t(values, weight).astype(BF)))


def token_blocks(partial):
    rows = partial.shape[0] // 4
    cuts = [0, rows, 2 * rows, 3 * rows, 3 * rows + rows // 2, 4 * rows]
    return [partial[a:b] for a, b in zip(cuts, cuts[1:])]


def normalize(values):
    centred = values - jnp.mean(values, axis=-1, keepdims=True)
    inv_std = lax.rsqrt(jnp.mean(centred * centred, axis=-1, keepdims=True) + EPS)
    return centred * inv_std, inv_std


NORM_ROWS = 32


def row_spec(array, at=None):
    width = array.shape[-1]
    if at is None:
        return pl.BlockSpec((NORM_ROWS, width), lambda i: (i, 0))
    return pl.BlockSpec((1, NORM_ROWS, width), lambda i, at=at: (at, i, 0))


def terms_of(terms):
    arrays, specs = [], []
    for term in terms:
        array, at = term if isinstance(term, tuple) else (term, None)
        arrays.append(array)
        specs.append(row_spec(array, at))
    return arrays, specs


def total_of(refs):
    values = [ref[0] if len(ref.shape) == 3 else ref[...] for ref in refs]
    return sum(value.astype(F32) for value in values)


def add_norm(terms, gain):
    arrays, specs = terms_of(terms)
    tokens, width = arrays[0].shape[-2], arrays[0].shape[-1]
    tokens = min(a.shape[-2] for a in arrays)

    def kernel(*refs):
        gain_ref, x, out = refs[-3:]
        values = total_of(refs[:-3])
        x[...] = values
        out[...] = (normalize(values)[0] * gain_ref[...]).astype(BF)

    return call(
        kernel,
        (tokens // NORM_ROWS,),
        specs + [whole(gain)],
        [row_spec(shape((tokens, width)))] * 2,
        [shape((tokens, width), F32), shape((tokens, width))],
        [*arrays, gain],
        "add_norm",
    )


def norm_grad(grad, values, gain):
    normed, inv_std = normalize(values)
    scaled = grad * gain
    first_mean = jnp.mean(scaled, axis=-1, keepdims=True)
    second_mean = jnp.mean(scaled * normed, axis=-1, keepdims=True)
    return (
        inv_std * (scaled - first_mean - normed * second_mean),
        jnp.sum(grad * normed, axis=0, keepdims=True),
    )


def accumulate(ref, value):
    @pl.when(pl.program_id(0) == 0)
    def _():
        ref[...] = jnp.zeros_like(ref)

    ref[...] += value


def norm_back(terms, upper, values, gain):
    arrays, specs = terms_of(terms)
    tokens, width = values.shape

    def kernel(*refs):
        upper_ref, x, gain_ref, out, out_low, gain_grad = refs[-6:]
        back, part = norm_grad(total_of(refs[:-6]), x[...], gain_ref[...])
        result = upper_ref[...].astype(F32) + back
        out[...] = result
        out_low[...] = result.astype(BF)
        accumulate(gain_grad, part)

    return call(
        kernel,
        (tokens // NORM_ROWS,),
        specs + [row_spec(upper), row_spec(values), whole(gain)],
        [row_spec(values)] * 2 + [pl.BlockSpec((1, width), lambda i: (0, 0))],
        [shape((tokens, width), F32), shape((tokens, width)), shape((1, width), F32)],
        [*arrays, upper, values, gain],
        "norm_back",
    )


def last_back(terms, upper, values, gain, masked, unit, order):
    arrays, specs = terms_of(terms)
    tokens, width = values.shape

    def kernel(*refs):
        upper_ref, x, gain_ref, mask, out, gain_grad, mask_grad = refs[-7:]
        back, part = norm_grad(total_of(refs[:-7]), x[...], gain_ref[...])
        result = upper_ref[...].astype(F32) + back
        hit = mask[...] > 0.5
        out[...] = reorder(jnp.where(hit, 0.0, result).astype(BF), unit, order)
        accumulate(gain_grad, part)
        accumulate(mask_grad, jnp.sum(jnp.where(hit, result, 0.0), axis=0, keepdims=True))

    line = pl.BlockSpec((1, width), lambda i: (0, 0))
    return call(
        kernel,
        (tokens // NORM_ROWS,),
        specs + [row_spec(upper), row_spec(values), whole(gain), row_spec(masked)],
        [row_spec(values), line, line],
        [shape((tokens, width)), shape((1, width), F32), shape((1, width), F32)],
        [*arrays, upper, values, gain, masked],
        "last_back",
    )


def start(hidden, cotangent, masked, embed, gain, unit, order):
    tokens, width = hidden.shape

    def kernel(hid, cot, mask, embed_ref, gain_ref, x, out, grad):
        hit = mask[...] > 0.5
        values = jnp.where(
            hit, embed_ref[...], reorder(hid[...], unit, order).astype(F32)
        )
        x[...] = values
        out[...] = (normalize(values)[0] * gain_ref[...]).astype(BF)
        grad[...] = jnp.where(hit, reorder(cot[...], unit, order).astype(F32), 0.0).astype(BF)

    rows = row_spec(hidden)
    return call(
        kernel,
        (tokens // NORM_ROWS,),
        [rows, rows, row_spec(masked), whole(embed), whole(gain)],
        [rows] * 3,
        [shape((tokens, width), F32), shape((tokens, width)), shape((tokens, width))],
        [hidden, cotangent, masked, embed, gain],
        "start",
    )


def layer_output(upper, terms, unit, order):
    arrays, specs = terms_of(terms)
    tokens, width = upper.shape

    def kernel(*refs):
        values = refs[-2][...] + total_of(refs[:-2])
        refs[-1][...] = reorder(values.astype(BF), unit, order)

    return call(
        kernel,
        (tokens // NORM_ROWS,),
        specs + [row_spec(upper)],
        row_spec(upper),
        shape((tokens, width)),
        [*arrays, upper],
        "layer_output",
    )


def feed_up(pieces, weight):
    rows, width = pieces[0].shape
    hidden = weight.shape[1]
    step = 256

    def kernel(*refs):
        up, tokens, act, slope, sems = refs[5:]

        @pl.when(pl.program_id(0) == 0)
        def _():
            assemble(tokens, refs[:5], sems)

        u = mm(tokens[...], up[...])
        square = u * u
        bend = jnp.tanh(SLOPE * u * (1.0 + CUBIC * square))
        half = 0.5 * (1.0 + bend)
        act[...] = (u * half).astype(BF)
        slope[...] = half + 0.5 * u * (1.0 - bend * bend) * SLOPE * (1.0 + 3.0 * CUBIC * square)

    part = pl.BlockSpec((4 * rows, step), lambda j: (0, j))
    return call(
        kernel,
        (hidden // step,),
        [ANY] * 5 + [pl.BlockSpec((width, step), lambda j: (0, j))],
        [pl.BlockSpec((4 * rows, width), lambda j: (0, 0)), part, part],
        [shape((4 * rows, width)), shape((4 * rows, hidden)), shape((4 * rows, hidden), F32)],
        [*pieces, weight],
        "feed_up",
        scratch=[pltpu.SemaphoreType.DMA((5,))],
        flops=8 * rows * width * hidden,
        size=2 * width * (hidden + 8 * rows),
    )


def feed_down(grad_y, slope, weight):
    tokens, width = grad_y.shape
    hidden = weight.shape[1]
    step = 256

    def kernel(dy, slope_ref, down, out):
        out[...] = (mm(dy[...], down[...]) * slope_ref[...]).astype(BF)

    part = pl.BlockSpec((tokens, step), lambda j: (0, j))
    return call(
        kernel,
        (hidden // step,),
        [whole(grad_y), part, pl.BlockSpec((width, step), lambda j: (0, j))],
        part,
        shape((tokens, hidden)),
        [grad_y, slope, weight],
        "feed_down",
        flops=2 * tokens * width * hidden,
        size=2 * width * (hidden + 8 * tokens),
    )


def softmax(scores):
    exp_terms = jnp.exp(scores - jnp.max(scores, axis=-1, keepdims=True))
    return exp_terms / jnp.sum(exp_terms, axis=-1, keepdims=True)


def score_grad(probs, grad_probs):
    return (
        probs * (grad_probs - jnp.sum(probs * grad_probs, axis=-1, keepdims=True))
    ).astype(BF)


def head(ref, k):
    return ref[:, k * HD : (k + 1) * HD]


def self_forward(projected, images):
    tokens, width = projected.shape
    rows, group = tokens // images, width // 3
    heads = group // HD

    def kernel(proj, mixed):
        for k in range(heads):
            query, key, value = (head(proj, j * heads + k) for j in range(3))
            probs = softmax(mm_t(query, key) * SCALE).astype(BF)
            mixed[:, k * HD : (k + 1) * HD] = mm(probs, value).astype(BF)

    return call(
        kernel,
        (images,),
        [pl.BlockSpec((rows, width), lambda i: (i, 0))],
        pl.BlockSpec((rows, group), lambda i: (i, 0)),
        shape((tokens, group)),
        [projected],
        "self_forward",
        flops=4 * tokens * rows * group,
    )


def self_back(projected, grad_mixed, images):
    tokens, width = projected.shape
    rows, group = tokens // images, width // 3
    heads = group // HD

    def kernel(proj, grad, out):
        for k in range(heads):
            query, key, value = (head(proj, j * heads + k) for j in range(3))
            grad_head = head(grad, k)
            probs = softmax(mm_t(query, key) * SCALE)
            grad_scores = score_grad(probs, mm_t(grad_head, value))
            parts = (
                mm(grad_scores, key) * SCALE,
                t_mm(grad_scores, query) * SCALE,
                t_mm(probs.astype(BF), grad_head),
            )
            for j, part in enumerate(parts):
                at = (j * heads + k) * HD
                out[:, at : at + HD] = part.astype(BF)

    return call(
        kernel,
        (images,),
        [
            pl.BlockSpec((rows, width), lambda i: (i, 0)),
            pl.BlockSpec((rows, group), lambda i: (i, 0)),
        ],
        pl.BlockSpec((rows, width), lambda i: (i, 0)),
        shape((tokens, width)),
        [projected, grad_mixed],
        "self_back",
        flops=10 * tokens * rows * group,
    )


def cross_forward(queries, text_kv):
    tokens, group = queries.shape
    heads = group // HD

    def kernel(query, text, mixed):
        for k in range(heads):
            probs = softmax(mm_t(head(query, k), head(text, k)) * SCALE).astype(BF)
            mixed[:, k * HD : (k + 1) * HD] = mm(probs, head(text, heads + k)).astype(BF)

    return call(
        kernel,
        (1,),
        [whole(queries), whole(text_kv)],
        whole(queries),
        shape((tokens, group)),
        [queries, text_kv],
        "cross_forward",
        flops=4 * tokens * text_kv.shape[0] * group,
    )


def cross_back(queries, text_kv, grad_mixed):
    tokens, group = queries.shape
    context = text_kv.shape[0]
    heads = group // HD

    def kernel(query, text, grad, grad_query, grad_text):
        for k in range(heads):
            query_head, key, value = head(query, k), head(text, k), head(text, heads + k)
            grad_head = head(grad, k)
            probs = softmax(mm_t(query_head, key) * SCALE)
            grad_scores = score_grad(probs, mm_t(grad_head, value))
            grad_query[:, k * HD : (k + 1) * HD] = (mm(grad_scores, key) * SCALE).astype(BF)
            at = (heads + k) * HD
            grad_text[:, k * HD : (k + 1) * HD] = t_mm(grad_scores, query_head) * SCALE
            grad_text[:, at : at + HD] = t_mm(probs.astype(BF), grad_head)

    return call(
        kernel,
        (1,),
        [whole(queries), whole(text_kv), whole(grad_mixed)],
        [whole(queries), whole(text_kv)],
        [shape((tokens, group)), shape((context, 2 * group), F32)],
        [queries, text_kv, grad_mixed],
        "cross_back",
        flops=10 * tokens * context * group,
    )


def grad_products(pairs, name, core=None, blocks=0):
    count_in = len(pairs[0][0])
    tokens, width = pairs[0][0][0].shape
    widths = [y[0].shape[1] for _, y in pairs]
    total = sum(widths)
    rows = 256 if core is None else width // (2 * blocks)
    steps = width // rows if core is None else blocks
    step = 512
    count = len(pairs) * count_in

    def kernel(r, *refs):
        out = refs[2 * count]
        offset = 0
        for k, wide in enumerate(widths):
            left = [refs[k * count_in + b][...].T for b in range(count_in)]
            for at in range(0, wide, step):
                out[:, offset + at : offset + at + step] = sum(
                    mm(left[b], refs[count + k * count_in + b][:, at : at + step])
                    for b in range(count_in)
                ).astype(BF)
            offset += wide

    pick = (lambda i, r: (0, i)) if core is None else (lambda i, r: (0, 2 * i + r[0]))
    return call(
        kernel,
        (steps,),
        [pl.BlockSpec((tokens, rows), pick)] * count
        + [pl.BlockSpec((tokens, w), lambda i, r: (0, 0)) for w in widths for _ in range(count_in)],
        pl.BlockSpec((rows, total), lambda i, r: (i, 0)),
        shape((steps * rows, total)),
        [b for x, _ in pairs for b in x] + [b for _, y in pairs for b in y],
        name,
        flops=2 * tokens * count_in * steps * rows * total,
        size=4 * width * total,
        rank=jnp.zeros((), jnp.int32) if core is None else core,
    )


def pick_weights(three, one, rank):
    rows, width = one.shape[0], one.shape[1] // 4

    def kernel(r, three_ref, one_ref, *outs):
        for k in range(4):

            @pl.when(pl.program_id(0) == k)
            def _():
                for j in range(3):
                    outs[k][:, j * width : (j + 1) * width] = three_ref[j]
                outs[k][:, 3 * width :] = one_ref[...]

    outs = [shape((rows, 4 * width))] * 4
    return call(
        kernel,
        (4,),
        [
            pl.BlockSpec((3, rows, width), lambda k, r: (0, 0, k ^ r[0])),
            pl.BlockSpec((rows, width), lambda k, r: (0, k ^ r[0])),
        ],
        [whole(a) for a in outs],
        outs,
        [three, one],
        "pick_weights",
        rank=rank,
    )


def pick_rows(arrays, rank):
    rows = arrays[0].shape[1]
    widths = [a.shape[2] for a in arrays]
    count = len(arrays)

    def kernel(r, *refs):
        for k in range(4):

            @pl.when(pl.program_id(0) == k)
            def _():
                at = 0
                for ref, width in zip(refs, widths):
                    refs[count + k][:, at : at + width] = ref[0]
                    at += width

    outs = [shape((rows, sum(widths)))] * 4
    return call(
        kernel,
        (4,),
        [pl.BlockSpec((1, rows, w), lambda k, r: (k ^ r[0], 0, 0)) for w in widths],
        [whole(a) for a in outs],
        outs,
        arrays,
        "pick_rows",
        rank=rank,
    )


def place(parts, rank):
    def kernel(r, *refs):
        for k in range(4):

            @pl.when(pl.program_id(0) == k)
            def _():
                refs[4][0] = refs[k][...]

    rows, columns = parts[0].shape
    return call(
        kernel,
        (4,),
        [whole(p) for p in parts],
        pl.BlockSpec((1, rows, columns), lambda k, r: (k ^ r[0], 0, 0)),
        shape((4, rows, columns)),
        parts,
        "place",
        rank=rank,
    )


def finish_wide(parts, rank):
    rows, total = parts[0].shape
    width = total // 2

    def kernel(r, *refs):
        for k in range(4):

            @pl.when(pl.program_id(0) == k)
            def _():
                refs[4][...] = refs[k][:, :width].astype(F32)
                refs[5][...] = refs[k][:, width:].astype(F32)

    flat = pl.BlockSpec((rows, width), lambda k, r: (0, k ^ r[0]))
    return call(
        kernel,
        (4,),
        [whole(p) for p in parts],
        [flat, flat],
        [shape((rows, 4 * width), F32)] * 2,
        parts,
        "finish_wide",
        rank=rank,
    )


def finish_all(parts, text_grad, rank):
    rows, total = parts[0].shape
    width = total // 6

    def kernel(r, *refs):
        key, value, three, out, cross, cross_out = refs[4:]
        for k in range(4):

            @pl.when(pl.program_id(0) == k)
            def _():
                def part(j):
                    return refs[k][:, j * width : (j + 1) * width].astype(F32)

                for j in range(3):
                    three[j] = part(j)
                out[...] = part(3)
                cross[0] = part(4)
                cross_out[...] = part(5)

        cross[1] = key[...]
        cross[2] = value[...]

    wide = pl.BlockSpec((3, rows, width), lambda k, r: (0, 0, k ^ r[0]))
    flat = pl.BlockSpec((rows, width), lambda k, r: (0, k ^ r[0]))
    return call(
        kernel,
        (4,),
        [whole(p) for p in parts]
        + [flat, pl.BlockSpec((rows, width), lambda k, r: (0, 4 + (k ^ r[0])))],
        [wide, flat, wide, flat],
        [shape((3, rows, 4 * width), F32), shape((rows, 4 * width), F32)] * 2,
        [*parts, text_grad, text_grad],
        "finish_all",
        rank=rank,
    )


def plane_block(k):
    return (k >> 1) & 1, (k >> 2) * 2 + (k & 1)


def text_forward(caption, w_text, w_cross):
    context, rows = caption.shape[0], w_text.shape[0]
    half, width = context // 2, w_cross.shape[2] // 4

    def kernel(cap, weight, cross, own, blocks):
        own[...] = mm_t(cap[...], weight[...]).astype(BF)
        for j in range(2):
            part = mm(own[...], cross[1 + j]).astype(BF)
            for k in range(8):
                core, group = plane_block(k)
                blocks[k, :, j * width : (j + 1) * width] = part[
                    core * half : (core + 1) * half, group * width : (group + 1) * width
                ]

    return call(
        kernel,
        (1,),
        [whole(caption), whole(w_text), whole(w_cross)],
        [
            pl.BlockSpec((context, rows), lambda i: (0, 0)),
            pl.BlockSpec((8, half, 2 * width), lambda i: (0, 0, 0)),
        ],
        [shape((context, rows)), shape((8, half, 2 * width))],
        [caption, w_text, w_cross],
        "text_forward",
    )


def text_back(blocks, own_text, w_cross, caption, w_text, extra):
    context, rows = own_text.shape
    half, width = context // 2, w_cross.shape[2] // 4
    wide = caption.shape[1] // 4
    tail = extra.shape[0]

    def kernel(block, own, cross, cap, weight, more, kv_grad, text_grad, out, grads):
        for k in range(8):
            core, group = plane_block(k)
            for j in range(2):
                at = (4 * j + group) * width
                grads[core * half : (core + 1) * half, at : at + width] = block[
                    k, :, j * width : (j + 1) * width
                ]
        kv_grad[...] = t_mm(own[...], grads[...])
        grad_text = sum(
            mm_t(grads[:, 4 * j * width : 4 * (j + 1) * width], cross[1 + j]) for j in range(2)
        ).astype(BF)
        text_grad[...] = t_mm(grad_text, cap[...])
        part = mm(grad_text, weight[...]).astype(BF)
        for k in range(8):
            core, group = plane_block(k)
            out[k, :half, :] = part[core * half : (core + 1) * half, group * wide : (group + 1) * wide]
            out[k, half:, :] = more[...]

    operands = [blocks, own_text, w_cross, caption, w_text, extra]
    outs = [
        shape((rows, 8 * width), F32),
        shape((rows, 4 * wide), F32),
        shape((8, half + tail, wide)),
    ]
    return call(
        kernel,
        (1,),
        [whole(a) for a in operands],
        [whole(a) for a in outs],
        outs,
        operands,
        "text_back",
        scratch=[pltpu.VMEM((context, 8 * width), BF)],
    )


def caption_output(blocks):
    count, half, wide = blocks.shape

    def kernel(block, out):
        out[...] = block[0].astype(F32)

    return call(
        kernel,
        (count,),
        [pl.BlockSpec((1, half, wide), lambda k: (k, 0, 0))],
        pl.BlockSpec((half, wide), lambda k: plane_block(k)),
        shape((2 * half, 4 * wide), F32),
        [blocks],
        "caption_output",
    )


def column_blocks(weight, count):
    rows = weight.shape[0]
    return weight.reshape(rows, count, -1).transpose(1, 0, 2)


def halves_of(values, width):
    high = values.astype(BF)
    low = (values - high.astype(F32)).astype(BF)
    return jnp.concatenate([high.reshape(-1, width), low.reshape(-1, width)], axis=0)


def whole_of(halves, width):
    rows = halves.shape[0] // 2
    return (halves[:rows] + halves[rows:]).reshape(-1, width)


def make_local(z_size):
    def sum_z(values):
        parts = values.reshape(z_size, -1, values.shape[-1])
        mine = trade(parts, "z").astype(F32).sum(axis=0).astype(BF)
        return spread(mine, "z", z_size).reshape(values.shape)

    def add_z(values):
        step = 1
        while step < z_size:
            values = values + lax.ppermute(
                values, "z", tuple((k, k ^ step) for k in range(z_size))
            )
            step *= 2
        return values

    def layer_order(values):
        shaped = values.reshape(values.shape[:-1] + (z_size, 2, 2, -1))
        return jnp.swapaxes(shaped, -3, -2).reshape(values.shape)

    def local(
        hidden,
        mask_index,
        mask_count,
        mask_embed,
        norm_gains,
        caption,
        w_qkv,
        w_out,
        w_cross,
        w_cross_out,
        w_text,
        w_up,
        w_down,
        cotangent,
    ):
        images, local_rows, width = hidden.shape
        full_length = mask_index.shape[1]
        rank = lax.axis_index("x") * 2 + lax.axis_index("y")
        core = lax.axis_index("c")
        tokens = images * local_rows
        group = width // 4
        text_width = caption.shape[1]

        unit = width // (4 * z_size)
        inside = unit % 128 == 0
        order = [4 * k + j for k in range(z_size) for j in (0, 2, 1, 3)] if inside else None

        def outer(values):
            return values if inside else layer_order(values)

        w_qkv, w_cross = w_qkv.transpose(1, 0, 2), w_cross.transpose(1, 0, 2)
        first = swap_parts(pick_weights(w_qkv, w_out, rank))
        first = gather_rows(place(first, rank))

        positions = lax.axis_index("y") * local_rows + jnp.arange(local_rows, dtype=jnp.int32)
        ranks = jnp.arange(full_length, dtype=jnp.int32)
        matches = (mask_index[:, :, None] == positions[None, None, :]) & (
            ranks[None, :, None] < mask_count[:, None, None]
        )
        masked = jnp.any(matches, axis=1).reshape(tokens, 1).astype(F32)
        gains = layer_order(norm_gains)
        gain_a, gain_b, gain_c = gains[:1], gains[1:2], gains[2:]
        start_x, attn_in, grad_top = start(
            outer(hidden.reshape(tokens, width)),
            outer(cotangent.reshape(tokens, width)),
            masked,
            layer_order(mask_embed)[None],
            gain_a,
            unit,
            order,
        )
        attn_in = gather_tokens(attn_in)
        mid = jnp.concatenate([column_blocks(w_cross[0], 4), column_blocks(w_cross_out, 4)], axis=2)
        up = column_blocks(w_up, 4)
        attn_in, mid, up = lax.optimization_barrier((attn_in, mid, up))
        mid, up = gather_rows(trade(mid)), gather_rows(trade(up))

        own_text, kv_part = text_forward(caption, w_text, w_cross)
        text_kv = trade(kv_part, PLANE).astype(F32).sum(axis=0).astype(BF)
        text_kv = sum_z(text_kv)
        other = swap(text_kv, "c")
        text_kv = jnp.concatenate(
            [jnp.where(core == 0, text_kv, other), jnp.where(core == 0, other, text_kv)], axis=0
        )
        attn_in, text_kv = lax.optimization_barrier((attn_in, text_kv))

        attn_in, projected = gather_mm(attn_in, first, 0, 3 * group, "qkv_mm")
        self_mixed = self_forward(projected, 2 * images)
        down = column_blocks(w_down, 4)
        self_mixed, down = lax.optimization_barrier((self_mixed, down))
        down = gather_rows(trade(down))
        parts = mm_scatter(self_mixed, first[:, 3 * group :])
        after_attn, cross_in = add_norm([start_x] + parts, gain_b)

        cross_in, cross_queries = gather_mm(gather_tokens(cross_in), mid, 0, group, "query_mm")
        cross_mixed = cross_forward(cross_queries, text_kv)
        parts = mm_scatter(cross_mixed, mid[:, group:])
        after_cross, mlp_in = add_norm([after_attn] + parts, gain_c)

        mlp_in = gather_tokens(mlp_in)
        mlp_in, grad_top = lax.optimization_barrier((mlp_in, grad_top))
        grad_y = jnp.concatenate(gather_tokens(grad_top), axis=0)
        mlp_in, activated, slope = feed_up(mlp_in, up)
        early = [attn_in, self_mixed, cross_in, cross_mixed]
        if inside:
            grad_axes, halves = "z", (core, z_size)

            def both(values):
                return [values, swap(values, "c")]

        else:
            grad_axes, halves = DATA, ()

            def both(values):
                return [values]

        early = [both(values) for values in early]
        down_part = grad_products([(both(grad_y), both(activated))], "down_grads", *halves)
        mlp_in = both(mlp_in)
        slope, down_part, early, mlp_in = lax.optimization_barrier((slope, down_part, early, mlp_in))
        down_rows = scatter_grad(down_part, grad_axes)
        grad_pre = feed_down(grad_y, slope, down)
        parts = mm_scatter(grad_pre, up)
        up_part = grad_products([(mlp_in, both(grad_pre))], "up_grads", *halves)
        grad_after_cross, cross_branch, gain_grad_c = norm_back(
            parts, grad_top, after_cross, gain_c
        )

        cross_branch = gather_tokens(cross_branch)
        activated, cross_own = lax.optimization_barrier((activated, cross_branch[0]))
        result = mm_t(activated, down).astype(BF)
        cross_branch, up_part, result = lax.optimization_barrier(
            ((cross_own,) + cross_branch[1:], up_part, result)
        )
        cross_branch, grad_cross_mixed = gather_mm(
            cross_branch, mid, group, group, "cross_out_back"
        )
        grad_cq, kv_grad = cross_back(cross_queries, text_kv, grad_cross_mixed)
        up_part, down_rows, kv_grad = lax.optimization_barrier((up_part, down_rows, kv_grad))
        up_rows = scatter_grad(up_part, grad_axes)
        cross_branch, grad_cq_both = both(cross_branch), both(grad_cq)
        parts = mm_scatter(grad_cq, mid[:, :group])
        grad_after_attn, attn_branch, gain_grad_b = norm_back(
            parts, grad_after_cross, after_attn, gain_b
        )

        attn_branch, result = lax.optimization_barrier((gather_tokens(attn_branch), result))
        result = scatter_first(token_blocks(result))
        attn_branch, grad_self_mixed = gather_mm(attn_branch, first, 3 * group, group, "out_back")
        grad_projected = self_back(projected, grad_self_mixed, 2 * images)
        grad_projected, result = lax.optimization_barrier((grad_projected, result))
        result = scatter_second(result)
        rest_part = grad_products(
            [
                (early[0], both(grad_projected)),
                (both(attn_branch), early[1]),
                (early[2], grad_cq_both),
                (cross_branch, early[3]),
            ],
            "attention_grads",
            *halves,
        )
        grad_projected, result, kv_grad, rest_part = lax.optimization_barrier(
            (grad_projected, result, kv_grad, rest_part)
        )
        rest_part, up_rows = lax.optimization_barrier((rest_part, up_rows))
        rest_rows = scatter_grad(rest_part, grad_axes)
        parts = mm_scatter(grad_projected, first[:, : 3 * group])
        grad_hidden, gain_grad_a, mask_grad = last_back(
            parts,
            grad_after_attn,
            start_x,
            gain_a,
            masked,
            unit,
            order,
        )
        sums = jnp.concatenate([gain_grad_a, gain_grad_b, gain_grad_c, mask_grad], axis=0)


        kv_part = kv_grad.astype(BF).reshape(2, z_size, -1, 2 * group)
        kv_part = kv_part.transpose(1, 0, 2, 3).reshape(2 * z_size, -1, 2 * group)
        kv_part = trade(kv_part, DATA).astype(F32).sum(axis=0).astype(BF)
        kv_sum = spread(kv_part, "z", z_size).reshape(-1, 2 * group)
        wide_rows = swap_parts(pick_rows([down_rows, up_rows], rank))
        kv_sum, wide_rows = lax.optimization_barrier((kv_sum, wide_rows))
        kv_grads = spread(kv_sum, PLANE, 8)
        kv_weight_grad, grad_text_w, caption_part = text_back(
            kv_grads, own_text, w_cross, caption, w_text, halves_of(sums, text_width // 4)
        )
        half_context = caption.shape[0] // 2
        caption_part = trade(caption_part, PLANE)
        output = layer_output(after_cross, result, unit, order)
        down_grad, up_grad = finish_wide(wide_rows, rank)
        caption_part, output, down_grad, up_grad = lax.optimization_barrier(
            (caption_part, output, down_grad, up_grad)
        )
        caption_part = caption_part.astype(F32).sum(axis=0)
        sums = layer_order(add_z(whole_of(caption_part[half_context:], width)))
        caption_part = caption_part[:half_context].astype(BF).reshape(z_size, -1, text_width // 4)
        caption_part = trade(caption_part, "z").astype(F32).sum(axis=0).astype(BF)
        rest_rows = pick_rows([rest_rows], rank)
        caption_part, rest_rows = lax.optimization_barrier((caption_part, rest_rows))
        caption_part = spread(caption_part, "z", z_size).reshape(half_context, -1)
        rest_rows = swap_parts(rest_rows)
        caption_part, rest_rows = lax.optimization_barrier((caption_part, rest_rows))
        grad_caption = caption_output(spread(caption_part, PLANE, 8))
        qkv_grad, out_grad, grad_cross, cross_out_grad = finish_all(
            rest_rows, kv_weight_grad, rank
        )
        return (
            outer(output).reshape(hidden.shape),
            outer(grad_hidden).reshape(hidden.shape),
            grad_caption,
            sums[:3],
            sums[3],
            qkv_grad.transpose(1, 0, 2),
            out_grad,
            grad_cross.transpose(1, 0, 2),
            cross_out_grad,
            grad_text_w,
            up_grad,
            down_grad,
        )

    return local


def solution(mesh):
    z_size = mesh.shape["img"] // 4
    inner = Mesh(mesh.devices.reshape(z_size, 2, 2, 2), ("z", "x", "c", "y"))
    image = ("z", "x", "c")
    tokens = P(image, "y", None)
    rows = P(image + ("y",))
    in_specs = (tokens, P(image, None), P(image), P(), P(), P()) + (rows,) * 7 + (tokens,)
    out_specs = (tokens, tokens, P(), P(), P()) + (rows,) * 7
    return jax.shard_map(
        make_local(z_size), mesh=inner, in_specs=in_specs, out_specs=out_specs, check_vma=False
    )
```

```python
import math

import jax
import jax.numpy as jnp
from jax import lax
from jax.experimental import pallas as pl
from jax.experimental.pallas import tpu as pltpu
from jax.sharding import Mesh
from jax.sharding import PartitionSpec as P

HD = 128
EPS = 1e-05
BF = jnp.bfloat16
F32 = jnp.float32
PAIR = ((0, 1), (1, 0))
GROUP = ("x", "y")
DATA = ("z", "c")
PLANE = ("x", "c", "y")
VMEM = 48 * 1024 * 1024
SCALE = 1.0 / math.sqrt(HD)
SLOPE = math.sqrt(2.0 / math.pi)
CUBIC = 0.044715


def dot(a, b, dims):
    return lax.dot_general(a, b, (dims, ((), ())), preferred_element_type=F32)


def mm(a, b):
    return dot(a, b, ((1,), (0,)))


def mm_t(a, b):
    return dot(a, b, ((1,), (1,)))


def t_mm(a, b):
    return dot(a, b, ((0,), (0,)))


def shape(dims, dtype=BF):
    return jax.ShapeDtypeStruct(dims, dtype)


def swap(values, axis):
    return lax.ppermute(values, axis, PAIR)


def trade(blocks, axes=GROUP):
    return lax.all_to_all(blocks, axes, 0, 0, tiled=True)


def spread(values, axes=GROUP, count=4):
    return trade(jnp.broadcast_to(values[None], (count,) + values.shape), axes)


def gather_tokens(own):
    half = own.shape[0] // 2
    from_x = swap(own, "x")
    from_y = swap(own, "y")
    return own, from_y, from_x, swap(from_x[:half], "y"), swap(from_y[half:], "x")


def scatter_first(parts):
    own, for_y, for_x, for_low, for_high = parts
    half = for_low.shape[0]
    low = swap(for_low, "y").astype(F32) + for_x[:half].astype(F32)
    high = swap(for_high, "x").astype(F32) + for_y[half:].astype(F32)
    return (
        own,
        jnp.concatenate([low.astype(BF), for_x[half:]], axis=0),
        jnp.concatenate([for_y[:half], high.astype(BF)], axis=0),
    )


def scatter_second(parts):
    own, for_x, for_y = parts
    return [own, swap(for_x, "x"), swap(for_y, "y")]


def scatter_tokens(parts):
    return scatter_second(scatter_first(parts))


def swap_parts(parts):
    return [
        parts[0],
        swap(parts[1], "y"),
        swap(parts[2], "x"),
        lax.ppermute(parts[3], GROUP, ((0, 3), (1, 2), (2, 1), (3, 0))),
    ]


def gather_rows(rows):
    return lax.all_gather(rows.reshape(-1, rows.shape[-1]), DATA, axis=0, tiled=True)


def scatter_grad(partial, axes):
    summed = lax.psum_scatter(partial, axes, scatter_dimension=0, tiled=True)
    return summed.reshape(4, -1, summed.shape[-1])


def call(kernel, grid, in_specs, out_specs, out_shape, operands, name, flops=0, size=1 << 22,
         rank=None, scratch=()):
    options = dict(
        out_shape=out_shape,
        compiler_params=pltpu.CompilerParams(vmem_limit_bytes=VMEM),
        cost_estimate=pl.CostEstimate(flops=flops, bytes_accessed=size, transcendentals=0),
        name=name,
    )
    if rank is None:
        return pl.pallas_call(
            kernel, grid=grid, in_specs=in_specs, out_specs=out_specs, scratch_shapes=scratch,
            **options,
        )(*operands)
    spec = pltpu.PrefetchScalarGridSpec(
        num_scalar_prefetch=1,
        grid=grid,
        in_specs=in_specs,
        out_specs=out_specs,
        scratch_shapes=scratch,
    )
    return pl.pallas_call(kernel, grid_spec=spec, **options)(rank.reshape(1), *operands)


def whole(array):
    return pl.BlockSpec(array.shape, lambda *_: (0,) * len(array.shape))


def reorder(values, unit, order):
    if order is None:
        return values
    return jnp.concatenate([values[:, k * unit : (k + 1) * unit] for k in order], axis=1)


def assemble(target, pieces, sems):
    copies, at = [], 0
    for k, piece in enumerate(pieces):
        rows = piece.shape[0]
        copies.append(pltpu.make_async_copy(piece, target.at[at : at + rows], sems.at[k]))
        at += rows
    for copy in copies:
        copy.start()
    for copy in copies:
        copy.wait()


ANY = pl.BlockSpec(memory_space=pl.ANY)


def gather_mm(pieces, weight, first, columns, name):
    rows, width = pieces[0].shape
    step = 256

    def kernel(*refs):
        tokens, out, sems = refs[6:]

        @pl.when(pl.program_id(0) == 0)
        def _():
            assemble(tokens, refs[:5], sems)

        out[...] = mm(tokens[...], refs[5][...]).astype(BF)

    return call(
        kernel,
        (columns // step,),
        [ANY] * 5 + [pl.BlockSpec((width, step), lambda j: (0, first // step + j))],
        [
            pl.BlockSpec((4 * rows, width), lambda j: (0, 0)),
            pl.BlockSpec((4 * rows, step), lambda j: (0, j)),
        ],
        [shape((4 * rows, width)), shape((4 * rows, columns))],
        [*pieces, weight],
        name,
        flops=8 * rows * width * columns,
        size=2 * width * (columns + 8 * rows),
        scratch=[pltpu.SemaphoreType.DMA((5,))],
    )


def mm_scatter(values, weight):
    return scatter_tokens(token_blocks(mm_t(values, weight).astype(BF)))


def token_blocks(partial):
    rows = partial.shape[0] // 4
    cuts = [0, rows, 2 * rows, 3 * rows, 3 * rows + rows // 2, 4 * rows]
    return [partial[a:b] for a, b in zip(cuts, cuts[1:])]


def normalize(values):
    centred = values - jnp.mean(values, axis=-1, keepdims=True)
    inv_std = lax.rsqrt(jnp.mean(centred * centred, axis=-1, keepdims=True) + EPS)
    return centred * inv_std, inv_std


NORM_ROWS = 32


def row_spec(array, at=None):
    width = array.shape[-1]
    if at is None:
        return pl.BlockSpec((NORM_ROWS, width), lambda i: (i, 0))
    return pl.BlockSpec((1, NORM_ROWS, width), lambda i, at=at: (at, i, 0))


def terms_of(terms):
    arrays, specs = [], []
    for term in terms:
        array, at = term if isinstance(term, tuple) else (term, None)
        arrays.append(array)
        specs.append(row_spec(array, at))
    return arrays, specs


def total_of(refs):
    values = [ref[0] if len(ref.shape) == 3 else ref[...] for ref in refs]
    return sum(value.astype(F32) for value in values)


def add_norm(terms, gain):
    arrays, specs = terms_of(terms)
    tokens, width = arrays[0].shape[-2], arrays[0].shape[-1]
    tokens = min(a.shape[-2] for a in arrays)

    def kernel(*refs):
        gain_ref, x, out = refs[-3:]
        values = total_of(refs[:-3])
        x[...] = values
        out[...] = (normalize(values)[0] * gain_ref[...]).astype(BF)

    return call(
        kernel,
        (tokens // NORM_ROWS,),
        specs + [whole(gain)],
        [row_spec(shape((tokens, width)))] * 2,
        [shape((tokens, width), F32), shape((tokens, width))],
        [*arrays, gain],
        "add_norm",
    )


def norm_grad(grad, values, gain):
    normed, inv_std = normalize(values)
    scaled = grad * gain
    first_mean = jnp.mean(scaled, axis=-1, keepdims=True)
    second_mean = jnp.mean(scaled * normed, axis=-1, keepdims=True)
    return (
        inv_std * (scaled - first_mean - normed * second_mean),
        jnp.sum(grad * normed, axis=0, keepdims=True),
    )


def accumulate(ref, value):
    @pl.when(pl.program_id(0) == 0)
    def _():
        ref[...] = jnp.zeros_like(ref)

    ref[...] += value


def norm_back(terms, upper, values, gain):
    arrays, specs = terms_of(terms)
    tokens, width = values.shape

    def kernel(*refs):
        upper_ref, x, gain_ref, out, out_low, gain_grad = refs[-6:]
        back, part = norm_grad(total_of(refs[:-6]), x[...], gain_ref[...])
        result = upper_ref[...].astype(F32) + back
        out[...] = result
        out_low[...] = result.astype(BF)
        accumulate(gain_grad, part)

    return call(
        kernel,
        (tokens // NORM_ROWS,),
        specs + [row_spec(upper), row_spec(values), whole(gain)],
        [row_spec(values)] * 2 + [pl.BlockSpec((1, width), lambda i: (0, 0))],
        [shape((tokens, width), F32), shape((tokens, width)), shape((1, width), F32)],
        [*arrays, upper, values, gain],
        "norm_back",
    )


def last_back(terms, upper, values, gain, masked, unit, order):
    arrays, specs = terms_of(terms)
    tokens, width = values.shape

    def kernel(*refs):
        upper_ref, x, gain_ref, mask, out, gain_grad, mask_grad = refs[-7:]
        back, part = norm_grad(total_of(refs[:-7]), x[...], gain_ref[...])
        result = upper_ref[...].astype(F32) + back
        hit = mask[...] > 0.5
        out[...] = reorder(jnp.where(hit, 0.0, result).astype(BF), unit, order)
        accumulate(gain_grad, part)
        accumulate(mask_grad, jnp.sum(jnp.where(hit, result, 0.0), axis=0, keepdims=True))

    line = pl.BlockSpec((1, width), lambda i: (0, 0))
    return call(
        kernel,
        (tokens // NORM_ROWS,),
        specs + [row_spec(upper), row_spec(values), whole(gain), row_spec(masked)],
        [row_spec(values), line, line],
        [shape((tokens, width)), shape((1, width), F32), shape((1, width), F32)],
        [*arrays, upper, values, gain, masked],
        "last_back",
    )


def start(hidden, cotangent, masked, embed, gain, unit, order):
    tokens, width = hidden.shape

    def kernel(hid, cot, mask, embed_ref, gain_ref, x, out, grad):
        hit = mask[...] > 0.5
        values = jnp.where(
            hit, embed_ref[...], reorder(hid[...], unit, order).astype(F32)
        )
        x[...] = values
        out[...] = (normalize(values)[0] * gain_ref[...]).astype(BF)
        grad[...] = jnp.where(hit, reorder(cot[...], unit, order).astype(F32), 0.0).astype(BF)

    rows = row_spec(hidden)
    return call(
        kernel,
        (tokens // NORM_ROWS,),
        [rows, rows, row_spec(masked), whole(embed), whole(gain)],
        [rows] * 3,
        [shape((tokens, width), F32), shape((tokens, width)), shape((tokens, width))],
        [hidden, cotangent, masked, embed, gain],
        "start",
    )


def layer_output(upper, terms, unit, order):
    arrays, specs = terms_of(terms)
    tokens, width = upper.shape

    def kernel(*refs):
        values = refs[-2][...] + total_of(refs[:-2])
        refs[-1][...] = reorder(values.astype(BF), unit, order)

    return call(
        kernel,
        (tokens // NORM_ROWS,),
        specs + [row_spec(upper)],
        row_spec(upper),
        shape((tokens, width)),
        [*arrays, upper],
        "layer_output",
    )


def feed_up(pieces, weight):
    rows, width = pieces[0].shape
    hidden = weight.shape[1]
    step = 256

    def kernel(*refs):
        up, tokens, act, slope, sems = refs[5:]

        @pl.when(pl.program_id(0) == 0)
        def _():
            assemble(tokens, refs[:5], sems)

        u = mm(tokens[...], up[...])
        square = u * u
        bend = jnp.tanh(SLOPE * u * (1.0 + CUBIC * square))
        half = 0.5 * (1.0 + bend)
        act[...] = (u * half).astype(BF)
        slope[...] = half + 0.5 * u * (1.0 - bend * bend) * SLOPE * (1.0 + 3.0 * CUBIC * square)

    part = pl.BlockSpec((4 * rows, step), lambda j: (0, j))
    return call(
        kernel,
        (hidden // step,),
        [ANY] * 5 + [pl.BlockSpec((width, step), lambda j: (0, j))],
        [pl.BlockSpec((4 * rows, width), lambda j: (0, 0)), part, part],
        [shape((4 * rows, width)), shape((4 * rows, hidden)), shape((4 * rows, hidden), F32)],
        [*pieces, weight],
        "feed_up",
        scratch=[pltpu.SemaphoreType.DMA((5,))],
        flops=8 * rows * width * hidden,
        size=2 * width * (hidden + 8 * rows),
    )


def feed_down(grad_y, slope, weight):
    tokens, width = grad_y.shape
    hidden = weight.shape[1]
    step = 256

    def kernel(dy, slope_ref, down, out):
        out[...] = (mm(dy[...], down[...]) * slope_ref[...]).astype(BF)

    part = pl.BlockSpec((tokens, step), lambda j: (0, j))
    return call(
        kernel,
        (hidden // step,),
        [whole(grad_y), part, pl.BlockSpec((width, step), lambda j: (0, j))],
        part,
        shape((tokens, hidden)),
        [grad_y, slope, weight],
        "feed_down",
        flops=2 * tokens * width * hidden,
        size=2 * width * (hidden + 8 * tokens),
    )


def softmax(scores):
    exp_terms = jnp.exp(scores - jnp.max(scores, axis=-1, keepdims=True))
    return exp_terms / jnp.sum(exp_terms, axis=-1, keepdims=True)


def score_grad(probs, grad_probs):
    return (
        probs * (grad_probs - jnp.sum(probs * grad_probs, axis=-1, keepdims=True))
    ).astype(BF)


def head(ref, k):
    return ref[:, k * HD : (k + 1) * HD]


def self_forward(projected, images):
    tokens, width = projected.shape
    rows, group = tokens // images, width // 3
    heads = group // HD

    def kernel(proj, mixed):
        for k in range(heads):
            query, key, value = (head(proj, j * heads + k) for j in range(3))
            probs = softmax(mm_t(query, key) * SCALE).astype(BF)
            mixed[:, k * HD : (k + 1) * HD] = mm(probs, value).astype(BF)

    return call(
        kernel,
        (images,),
        [pl.BlockSpec((rows, width), lambda i: (i, 0))],
        pl.BlockSpec((rows, group), lambda i: (i, 0)),
        shape((tokens, group)),
        [projected],
        "self_forward",
        flops=4 * tokens * rows * group,
    )


def self_back(projected, grad_mixed, images):
    tokens, width = projected.shape
    rows, group = tokens // images, width // 3
    heads = group // HD

    def kernel(proj, grad, out):
        for k in range(heads):
            query, key, value = (head(proj, j * heads + k) for j in range(3))
            grad_head = head(grad, k)
            probs = softmax(mm_t(query, key) * SCALE)
            grad_scores = score_grad(probs, mm_t(grad_head, value))
            parts = (
                mm(grad_scores, key) * SCALE,
                t_mm(grad_scores, query) * SCALE,
                t_mm(probs.astype(BF), grad_head),
            )
            for j, part in enumerate(parts):
                at = (j * heads + k) * HD
                out[:, at : at + HD] = part.astype(BF)

    return call(
        kernel,
        (images,),
        [
            pl.BlockSpec((rows, width), lambda i: (i, 0)),
            pl.BlockSpec((rows, group), lambda i: (i, 0)),
        ],
        pl.BlockSpec((rows, width), lambda i: (i, 0)),
        shape((tokens, width)),
        [projected, grad_mixed],
        "self_back",
        flops=10 * tokens * rows * group,
    )


def cross_forward(queries, text_kv):
    tokens, group = queries.shape
    heads = group // HD

    def kernel(query, text, mixed):
        for k in range(heads):
            probs = softmax(mm_t(head(query, k), head(text, k)) * SCALE).astype(BF)
            mixed[:, k * HD : (k + 1) * HD] = mm(probs, head(text, heads + k)).astype(BF)

    return call(
        kernel,
        (1,),
        [whole(queries), whole(text_kv)],
        whole(queries),
        shape((tokens, group)),
        [queries, text_kv],
        "cross_forward",
        flops=4 * tokens * text_kv.shape[0] * group,
    )


def cross_back(queries, text_kv, grad_mixed):
    tokens, group = queries.shape
    context = text_kv.shape[0]
    heads = group // HD

    def kernel(query, text, grad, grad_query, grad_text):
        for k in range(heads):
            query_head, key, value = head(query, k), head(text, k), head(text, heads + k)
            grad_head = head(grad, k)
            probs = softmax(mm_t(query_head, key) * SCALE)
            grad_scores = score_grad(probs, mm_t(grad_head, value))
            grad_query[:, k * HD : (k + 1) * HD] = (mm(grad_scores, key) * SCALE).astype(BF)
            at = (heads + k) * HD
            grad_text[:, k * HD : (k + 1) * HD] = t_mm(grad_scores, query_head) * SCALE
            grad_text[:, at : at + HD] = t_mm(probs.astype(BF), grad_head)

    return call(
        kernel,
        (1,),
        [whole(queries), whole(text_kv), whole(grad_mixed)],
        [whole(queries), whole(text_kv)],
        [shape((tokens, group)), shape((context, 2 * group), F32)],
        [queries, text_kv, grad_mixed],
        "cross_back",
        flops=10 * tokens * context * group,
    )


def grad_products(pairs, name, core=None, blocks=0):
    count_in = len(pairs[0][0])
    tokens, width = pairs[0][0][0].shape
    widths = [y[0].shape[1] for _, y in pairs]
    total = sum(widths)
    rows = 256 if core is None else width // (2 * blocks)
    steps = width // rows if core is None else blocks
    step = 512
    count = len(pairs) * count_in

    def kernel(r, *refs):
        out = refs[2 * count]
        offset = 0
        for k, wide in enumerate(widths):
            left = [refs[k * count_in + b][...].T for b in range(count_in)]
            for at in range(0, wide, step):
                out[:, offset + at : offset + at + step] = sum(
                    mm(left[b], refs[count + k * count_in + b][:, at : at + step])
                    for b in range(count_in)
                ).astype(BF)
            offset += wide

    pick = (lambda i, r: (0, i)) if core is None else (lambda i, r: (0, 2 * i + r[0]))
    return call(
        kernel,
        (steps,),
        [pl.BlockSpec((tokens, rows), pick)] * count
        + [pl.BlockSpec((tokens, w), lambda i, r: (0, 0)) for w in widths for _ in range(count_in)],
        pl.BlockSpec((rows, total), lambda i, r: (i, 0)),
        shape((steps * rows, total)),
        [b for x, _ in pairs for b in x] + [b for _, y in pairs for b in y],
        name,
        flops=2 * tokens * count_in * steps * rows * total,
        size=4 * width * total,
        rank=jnp.zeros((), jnp.int32) if core is None else core,
    )


def pick_weights(three, one, rank):
    rows, width = one.shape[0], one.shape[1] // 4

    def kernel(r, three_ref, one_ref, *outs):
        for k in range(4):

            @pl.when(pl.program_id(0) == k)
            def _():
                for j in range(3):
                    outs[k][:, j * width : (j + 1) * width] = three_ref[j]
                outs[k][:, 3 * width :] = one_ref[...]

    outs = [shape((rows, 4 * width))] * 4
    return call(
        kernel,
        (4,),
        [
            pl.BlockSpec((3, rows, width), lambda k, r: (0, 0, k ^ r[0])),
            pl.BlockSpec((rows, width), lambda k, r: (0, k ^ r[0])),
        ],
        [whole(a) for a in outs],
        outs,
        [three, one],
        "pick_weights",
        rank=rank,
    )


def pick_rows(arrays, rank):
    rows = arrays[0].shape[1]
    widths = [a.shape[2] for a in arrays]
    count = len(arrays)

    def kernel(r, *refs):
        for k in range(4):

            @pl.when(pl.program_id(0) == k)
            def _():
                at = 0
                for ref, width in zip(refs, widths):
                    refs[count + k][:, at : at + width] = ref[0]
                    at += width

    outs = [shape((rows, sum(widths)))] * 4
    return call(
        kernel,
        (4,),
        [pl.BlockSpec((1, rows, w), lambda k, r: (k ^ r[0], 0, 0)) for w in widths],
        [whole(a) for a in outs],
        outs,
        arrays,
        "pick_rows",
        rank=rank,
    )


def place(parts, rank):
    def kernel(r, *refs):
        for k in range(4):

            @pl.when(pl.program_id(0) == k)
            def _():
                refs[4][0] = refs[k][...]

    rows, columns = parts[0].shape
    return call(
        kernel,
        (4,),
        [whole(p) for p in parts],
        pl.BlockSpec((1, rows, columns), lambda k, r: (k ^ r[0], 0, 0)),
        shape((4, rows, columns)),
        parts,
        "place",
        rank=rank,
    )


def finish_wide(parts, rank):
    rows, total = parts[0].shape
    width = total // 2

    def kernel(r, *refs):
        for k in range(4):

            @pl.when(pl.program_id(0) == k)
            def _():
                refs[4][...] = refs[k][:, :width].astype(F32)
                refs[5][...] = refs[k][:, width:].astype(F32)

    flat = pl.BlockSpec((rows, width), lambda k, r: (0, k ^ r[0]))
    return call(
        kernel,
        (4,),
        [whole(p) for p in parts],
        [flat, flat],
        [shape((rows, 4 * width), F32)] * 2,
        parts,
        "finish_wide",
        rank=rank,
    )


def finish_all(parts, text_grad, rank):
    rows, total = parts[0].shape
    width = total // 6

    def kernel(r, *refs):
        key, value, three, out, cross, cross_out = refs[4:]
        for k in range(4):

            @pl.when(pl.program_id(0) == k)
            def _():
                def part(j):
                    return refs[k][:, j * width : (j + 1) * width].astype(F32)

                for j in range(3):
                    three[j] = part(j)
                out[...] = part(3)
                cross[0] = part(4)
                cross_out[...] = part(5)

        cross[1] = key[...]
        cross[2] = value[...]

    wide = pl.BlockSpec((3, rows, width), lambda k, r: (0, 0, k ^ r[0]))
    flat = pl.BlockSpec((rows, width), lambda k, r: (0, k ^ r[0]))
    return call(
        kernel,
        (4,),
        [whole(p) for p in parts]
        + [flat, pl.BlockSpec((rows, width), lambda k, r: (0, 4 + (k ^ r[0])))],
        [wide, flat, wide, flat],
        [shape((3, rows, 4 * width), F32), shape((rows, 4 * width), F32)] * 2,
        [*parts, text_grad, text_grad],
        "finish_all",
        rank=rank,
    )


def plane_block(k):
    return (k >> 1) & 1, (k >> 2) * 2 + (k & 1)


def text_forward(caption, w_text, w_cross):
    context, rows = caption.shape[0], w_text.shape[0]
    half, width = context // 2, w_cross.shape[2] // 4

    def kernel(cap, weight, cross, own, blocks):
        own[...] = mm_t(cap[...], weight[...]).astype(BF)
        for j in range(2):
            part = mm(own[...], cross[1 + j]).astype(BF)
            for k in range(8):
                core, group = plane_block(k)
                blocks[k, :, j * width : (j + 1) * width] = part[
                    core * half : (core + 1) * half, group * width : (group + 1) * width
                ]

    return call(
        kernel,
        (1,),
        [whole(caption), whole(w_text), whole(w_cross)],
        [
            pl.BlockSpec((context, rows), lambda i: (0, 0)),
            pl.BlockSpec((8, half, 2 * width), lambda i: (0, 0, 0)),
        ],
        [shape((context, rows)), shape((8, half, 2 * width))],
        [caption, w_text, w_cross],
        "text_forward",
    )


def text_back(blocks, own_text, w_cross, caption, w_text, extra):
    context, rows = own_text.shape
    half, width = context // 2, w_cross.shape[2] // 4
    wide = caption.shape[1] // 4
    tail = extra.shape[0]

    def kernel(block, own, cross, cap, weight, more, kv_grad, text_grad, out, grads):
        for k in range(8):
            core, group = plane_block(k)
            for j in range(2):
                at = (4 * j + group) * width
                grads[core * half : (core + 1) * half, at : at + width] = block[
                    k, :, j * width : (j + 1) * width
                ]
        kv_grad[...] = t_mm(own[...], grads[...])
        grad_text = sum(
            mm_t(grads[:, 4 * j * width : 4 * (j + 1) * width], cross[1 + j]) for j in range(2)
        ).astype(BF)
        text_grad[...] = t_mm(grad_text, cap[...])
        part = mm(grad_text, weight[...]).astype(BF)
        for k in range(8):
            core, group = plane_block(k)
            out[k, :half, :] = part[core * half : (core + 1) * half, group * wide : (group + 1) * wide]
            out[k, half:, :] = more[...]

    operands = [blocks, own_text, w_cross, caption, w_text, extra]
    outs = [
        shape((rows, 8 * width), F32),
        shape((rows, 4 * wide), F32),
        shape((8, half + tail, wide)),
    ]
    return call(
        kernel,
        (1,),
        [whole(a) for a in operands],
        [whole(a) for a in outs],
        outs,
        operands,
        "text_back",
        scratch=[pltpu.VMEM((context, 8 * width), BF)],
    )


def caption_output(blocks):
    count, half, wide = blocks.shape

    def kernel(block, out):
        out[...] = block[0].astype(F32)

    return call(
        kernel,
        (count,),
        [pl.BlockSpec((1, half, wide), lambda k: (k, 0, 0))],
        pl.BlockSpec((half, wide), lambda k: plane_block(k)),
        shape((2 * half, 4 * wide), F32),
        [blocks],
        "caption_output",
    )


def column_blocks(weight, count):
    rows = weight.shape[0]
    return weight.reshape(rows, count, -1).transpose(1, 0, 2)


def halves_of(values, width):
    high = values.astype(BF)
    low = (values - high.astype(F32)).astype(BF)
    return jnp.concatenate([high.reshape(-1, width), low.reshape(-1, width)], axis=0)


def whole_of(halves, width):
    rows = halves.shape[0] // 2
    return (halves[:rows] + halves[rows:]).reshape(-1, width)


def make_local(z_size):
    def sum_z(values):
        parts = values.reshape(z_size, -1, values.shape[-1])
        mine = trade(parts, "z").astype(F32).sum(axis=0).astype(BF)
        return spread(mine, "z", z_size).reshape(values.shape)

    def add_z(values):
        step = 1
        while step < z_size:
            values = values + lax.ppermute(
                values, "z", tuple((k, k ^ step) for k in range(z_size))
            )
            step *= 2
        return values

    def layer_order(values):
        shaped = values.reshape(values.shape[:-1] + (z_size, 2, 2, -1))
        return jnp.swapaxes(shaped, -3, -2).reshape(values.shape)

    def local(
        hidden,
        mask_index,
        mask_count,
        mask_embed,
        norm_gains,
        caption,
        w_qkv,
        w_out,
        w_cross,
        w_cross_out,
        w_text,
        w_up,
        w_down,
        cotangent,
    ):
        images, local_rows, width = hidden.shape
        full_length = mask_index.shape[1]
        rank = lax.axis_index("x") * 2 + lax.axis_index("y")
        core = lax.axis_index("c")
        tokens = images * local_rows
        group = width // 4
        text_width = caption.shape[1]

        unit = width // (4 * z_size)
        inside = unit % 128 == 0
        order = [4 * k + j for k in range(z_size) for j in (0, 2, 1, 3)] if inside else None

        def outer(values):
            return values if inside else layer_order(values)

        w_qkv, w_cross = w_qkv.transpose(1, 0, 2), w_cross.transpose(1, 0, 2)
        first = swap_parts(pick_weights(w_qkv, w_out, rank))
        first = gather_rows(place(first, rank))

        positions = lax.axis_index("y") * local_rows + jnp.arange(local_rows, dtype=jnp.int32)
        ranks = jnp.arange(full_length, dtype=jnp.int32)
        matches = (mask_index[:, :, None] == positions[None, None, :]) & (
            ranks[None, :, None] < mask_count[:, None, None]
        )
        masked = jnp.any(matches, axis=1).reshape(tokens, 1).astype(F32)
        gains = layer_order(norm_gains)
        gain_a, gain_b, gain_c = gains[:1], gains[1:2], gains[2:]
        start_x, attn_in, grad_top = start(
            outer(hidden.reshape(tokens, width)),
            outer(cotangent.reshape(tokens, width)),
            masked,
            layer_order(mask_embed)[None],
            gain_a,
            unit,
            order,
        )
        attn_in = gather_tokens(attn_in)
        mid = jnp.concatenate([column_blocks(w_cross[0], 4), column_blocks(w_cross_out, 4)], axis=2)
        up = column_blocks(w_up, 4)
        attn_in, mid, up = lax.optimization_barrier((attn_in, mid, up))
        mid, up = gather_rows(trade(mid)), gather_rows(trade(up))

        own_text, kv_part = text_forward(caption, w_text, w_cross)
        text_kv = trade(kv_part, PLANE).astype(F32).sum(axis=0).astype(BF)
        text_kv = sum_z(text_kv)
        other = swap(text_kv, "c")
        text_kv = jnp.concatenate(
            [jnp.where(core == 0, text_kv, other), jnp.where(core == 0, other, text_kv)], axis=0
        )
        attn_in, text_kv = lax.optimization_barrier((attn_in, text_kv))

        attn_in, projected = gather_mm(attn_in, first, 0, 3 * group, "qkv_mm")
        self_mixed = self_forward(projected, 2 * images)
        down = column_blocks(w_down, 4)
        self_mixed, down = lax.optimization_barrier((self_mixed, down))
        down = gather_rows(trade(down))
        parts = mm_scatter(self_mixed, first[:, 3 * group :])
        after_attn, cross_in = add_norm([start_x] + parts, gain_b)

        cross_in, cross_queries = gather_mm(gather_tokens(cross_in), mid, 0, group, "query_mm")
        cross_mixed = cross_forward(cross_queries, text_kv)
        parts = mm_scatter(cross_mixed, mid[:, group:])
        after_cross, mlp_in = add_norm([after_attn] + parts, gain_c)

        mlp_in = gather_tokens(mlp_in)
        mlp_in, grad_top = lax.optimization_barrier((mlp_in, grad_top))
        grad_y = jnp.concatenate(gather_tokens(grad_top), axis=0)
        mlp_in, activated, slope = feed_up(mlp_in, up)
        early = [attn_in, self_mixed, cross_in, cross_mixed]
        if inside:
            grad_axes, halves = "z", (core, z_size)

            def both(values):
                return [values, swap(values, "c")]

        else:
            grad_axes, halves = DATA, ()

            def both(values):
                return [values]

        early = [both(values) for values in early]
        down_part = grad_products([(both(grad_y), both(activated))], "down_grads", *halves)
        mlp_in = both(mlp_in)
        slope, down_part, early, mlp_in = lax.optimization_barrier((slope, down_part, early, mlp_in))
        down_rows = scatter_grad(down_part, grad_axes)
        grad_pre = feed_down(grad_y, slope, down)
        parts = mm_scatter(grad_pre, up)
        up_part = grad_products([(mlp_in, both(grad_pre))], "up_grads", *halves)
        grad_after_cross, cross_branch, gain_grad_c = norm_back(
            parts, grad_top, after_cross, gain_c
        )

        cross_branch = gather_tokens(cross_branch)
        activated, cross_own = lax.optimization_barrier((activated, cross_branch[0]))
        result = mm_t(activated, down).astype(BF)
        cross_branch, up_part, result = lax.optimization_barrier(
            ((cross_own,) + cross_branch[1:], up_part, result)
        )
        cross_branch, grad_cross_mixed = gather_mm(
            cross_branch, mid, group, group, "cross_out_back"
        )
        grad_cq, kv_grad = cross_back(cross_queries, text_kv, grad_cross_mixed)
        up_part, down_rows, kv_grad = lax.optimization_barrier((up_part, down_rows, kv_grad))
        up_rows = scatter_grad(up_part, grad_axes)
        cross_branch, grad_cq_both = both(cross_branch), both(grad_cq)
        parts = mm_scatter(grad_cq, mid[:, :group])
        grad_after_attn, attn_branch, gain_grad_b = norm_back(
            parts, grad_after_cross, after_attn, gain_b
        )

        attn_branch, result = lax.optimization_barrier((gather_tokens(attn_branch), result))
        result = scatter_first(token_blocks(result))
        attn_branch, grad_self_mixed = gather_mm(attn_branch, first, 3 * group, group, "out_back")
        grad_projected = self_back(projected, grad_self_mixed, 2 * images)
        kv_part = kv_grad.astype(BF).reshape(2, z_size, -1, 2 * group)
        kv_part = kv_part.transpose(1, 0, 2, 3).reshape(2 * z_size, -1, 2 * group)
        grad_projected, result, kv_part = lax.optimization_barrier(
            (grad_projected, result, kv_part)
        )
        kv_part = trade(kv_part, DATA)
        result = scatter_second(result)
        rest_part = grad_products(
            [
                (early[0], both(grad_projected)),
                (both(attn_branch), early[1]),
                (early[2], grad_cq_both),
                (cross_branch, early[3]),
            ],
            "attention_grads",
            *halves,
        )
        grad_projected, result, kv_part, rest_part = lax.optimization_barrier(
            (grad_projected, result, kv_part, rest_part)
        )
        rest_part, up_rows = lax.optimization_barrier((rest_part, up_rows))
        rest_rows = scatter_grad(rest_part, grad_axes)
        parts = mm_scatter(grad_projected, first[:, : 3 * group])
        grad_hidden, gain_grad_a, mask_grad = last_back(
            parts,
            grad_after_attn,
            start_x,
            gain_a,
            masked,
            unit,
            order,
        )
        sums = jnp.concatenate([gain_grad_a, gain_grad_b, gain_grad_c, mask_grad], axis=0)


        kv_part = kv_part.astype(F32).sum(axis=0).astype(BF)
        kv_sum = spread(kv_part, "z", z_size).reshape(-1, 2 * group)
        wide_rows = swap_parts(pick_rows([down_rows, up_rows], rank))
        kv_sum, wide_rows = lax.optimization_barrier((kv_sum, wide_rows))
        kv_grads = spread(kv_sum, PLANE, 8)
        kv_weight_grad, grad_text_w, caption_part = text_back(
            kv_grads, own_text, w_cross, caption, w_text, halves_of(sums, text_width // 4)
        )
        half_context = caption.shape[0] // 2
        caption_part = trade(caption_part, PLANE)
        output = layer_output(after_cross, result, unit, order)
        down_grad, up_grad = finish_wide(wide_rows, rank)
        caption_part, output, down_grad, up_grad = lax.optimization_barrier(
            (caption_part, output, down_grad, up_grad)
        )
        caption_part = caption_part.astype(F32).sum(axis=0)
        sums = layer_order(add_z(whole_of(caption_part[half_context:], width)))
        caption_part = caption_part[:half_context].astype(BF).reshape(z_size, -1, text_width // 4)
        caption_part = trade(caption_part, "z").astype(F32).sum(axis=0).astype(BF)
        caption_part = spread(caption_part, "z", z_size).reshape(half_context, -1)
        caption_part = spread(caption_part, PLANE, 8)
        caption_part, rest_rows = lax.optimization_barrier((caption_part, rest_rows))
        grad_caption = caption_output(caption_part)
        rest_rows = swap_parts(pick_rows([rest_rows], rank))
        qkv_grad, out_grad, grad_cross, cross_out_grad = finish_all(
            rest_rows, kv_weight_grad, rank
        )
        return (
            outer(output).reshape(hidden.shape),
            outer(grad_hidden).reshape(hidden.shape),
            grad_caption,
            sums[:3],
            sums[3],
            qkv_grad.transpose(1, 0, 2),
            out_grad,
            grad_cross.transpose(1, 0, 2),
            cross_out_grad,
            grad_text_w,
            up_grad,
            down_grad,
        )

    return local


def solution(mesh):
    z_size = mesh.shape["img"] // 4
    inner = Mesh(mesh.devices.reshape(z_size, 2, 2, 2), ("z", "x", "c", "y"))
    image = ("z", "x", "c")
    tokens = P(image, "y", None)
    rows = P(image + ("y",))
    in_specs = (tokens, P(image, None), P(image), P(), P(), P()) + (rows,) * 7 + (tokens,)
    out_specs = (tokens, tokens, P(), P(), P()) + (rows,) * 7
    return jax.shard_map(
        make_local(z_size), mesh=inner, in_specs=in_specs, out_specs=out_specs, check_vma=False
    )
```

```python
import math

import jax
import jax.numpy as jnp
from jax import lax
from jax.experimental import pallas as pl
from jax.experimental.pallas import tpu as pltpu
from jax.sharding import Mesh
from jax.sharding import PartitionSpec as P

HD = 128
EPS = 1e-05
BF = jnp.bfloat16
F32 = jnp.float32
PAIR = ((0, 1), (1, 0))
GROUP = ("x", "y")
DATA = ("z", "c")
PLANE = ("x", "c", "y")
VMEM = 48 * 1024 * 1024
SCALE = 1.0 / math.sqrt(HD)
SLOPE = math.sqrt(2.0 / math.pi)
CUBIC = 0.044715


def dot(a, b, dims):
    return lax.dot_general(a, b, (dims, ((), ())), preferred_element_type=F32)


def mm(a, b):
    return dot(a, b, ((1,), (0,)))


def mm_t(a, b):
    return dot(a, b, ((1,), (1,)))


def t_mm(a, b):
    return dot(a, b, ((0,), (0,)))


def shape(dims, dtype=BF):
    return jax.ShapeDtypeStruct(dims, dtype)


def swap(values, axis):
    return lax.ppermute(values, axis, PAIR)


def trade(blocks, axes=GROUP):
    return lax.all_to_all(blocks, axes, 0, 0, tiled=True)


def spread(values, axes=GROUP, count=4):
    return trade(jnp.broadcast_to(values[None], (count,) + values.shape), axes)


def gather_tokens(own):
    half = own.shape[0] // 2
    from_x = swap(own, "x")
    from_y = swap(own, "y")
    return own, from_y, from_x, swap(from_x[:half], "y"), swap(from_y[half:], "x")


def scatter_first(parts):
    own, for_y, for_x, for_low, for_high = parts
    half = for_low.shape[0]
    low = swap(for_low, "y").astype(F32) + for_x[:half].astype(F32)
    high = swap(for_high, "x").astype(F32) + for_y[half:].astype(F32)
    return (
        own,
        jnp.concatenate([low.astype(BF), for_x[half:]], axis=0),
        jnp.concatenate([for_y[:half], high.astype(BF)], axis=0),
    )


def scatter_second(parts):
    own, for_x, for_y = parts
    return [own, swap(for_x, "x"), swap(for_y, "y")]


def scatter_tokens(parts):
    return scatter_second(scatter_first(parts))


def swap_parts(parts):
    return [
        parts[0],
        swap(parts[1], "y"),
        swap(parts[2], "x"),
        lax.ppermute(parts[3], GROUP, ((0, 3), (1, 2), (2, 1), (3, 0))),
    ]


def gather_rows(rows):
    return lax.all_gather(rows.reshape(-1, rows.shape[-1]), DATA, axis=0, tiled=True)


def scatter_grad(partial, axes):
    summed = lax.psum_scatter(partial, axes, scatter_dimension=0, tiled=True)
    return summed.reshape(4, -1, summed.shape[-1])


def call(kernel, grid, in_specs, out_specs, out_shape, operands, name, flops=0, size=1 << 22,
         rank=None, scratch=()):
    options = dict(
        out_shape=out_shape,
        compiler_params=pltpu.CompilerParams(vmem_limit_bytes=VMEM),
        cost_estimate=pl.CostEstimate(flops=flops, bytes_accessed=size, transcendentals=0),
        name=name,
    )
    if rank is None:
        return pl.pallas_call(
            kernel, grid=grid, in_specs=in_specs, out_specs=out_specs, scratch_shapes=scratch,
            **options,
        )(*operands)
    spec = pltpu.PrefetchScalarGridSpec(
        num_scalar_prefetch=1,
        grid=grid,
        in_specs=in_specs,
        out_specs=out_specs,
        scratch_shapes=scratch,
    )
    return pl.pallas_call(kernel, grid_spec=spec, **options)(rank.reshape(1), *operands)


def whole(array):
    return pl.BlockSpec(array.shape, lambda *_: (0,) * len(array.shape))


def reorder(values, unit, order):
    if order is None:
        return values
    return jnp.concatenate([values[:, k * unit : (k + 1) * unit] for k in order], axis=1)


def assemble(target, pieces, sems):
    copies, at = [], 0
    for k, piece in enumerate(pieces):
        rows = piece.shape[0]
        copies.append(pltpu.make_async_copy(piece, target.at[at : at + rows], sems.at[k]))
        at += rows
    for copy in copies:
        copy.start()
    for copy in copies:
        copy.wait()


ANY = pl.BlockSpec(memory_space=pl.ANY)


def gather_mm(pieces, weight, first, columns, name):
    rows, width = pieces[0].shape
    step = 256

    def kernel(*refs):
        tokens, out, sems = refs[6:]

        @pl.when(pl.program_id(0) == 0)
        def _():
            assemble(tokens, refs[:5], sems)

        out[...] = mm(tokens[...], refs[5][...]).astype(BF)

    return call(
        kernel,
        (columns // step,),
        [ANY] * 5 + [pl.BlockSpec((width, step), lambda j: (0, first // step + j))],
        [
            pl.BlockSpec((4 * rows, width), lambda j: (0, 0)),
            pl.BlockSpec((4 * rows, step), lambda j: (0, j)),
        ],
        [shape((4 * rows, width)), shape((4 * rows, columns))],
        [*pieces, weight],
        name,
        flops=8 * rows * width * columns,
        size=2 * width * (columns + 8 * rows),
        scratch=[pltpu.SemaphoreType.DMA((5,))],
    )


def mm_scatter(values, weight):
    return scatter_tokens(token_blocks(mm_t(values, weight).astype(BF)))


def token_blocks(partial):
    rows = partial.shape[0] // 4
    cuts = [0, rows, 2 * rows, 3 * rows, 3 * rows + rows // 2, 4 * rows]
    return [partial[a:b] for a, b in zip(cuts, cuts[1:])]


def normalize(values):
    centred = values - jnp.mean(values, axis=-1, keepdims=True)
    inv_std = lax.rsqrt(jnp.mean(centred * centred, axis=-1, keepdims=True) + EPS)
    return centred * inv_std, inv_std


NORM_ROWS = 32


def row_spec(array, at=None):
    width = array.shape[-1]
    if at is None:
        return pl.BlockSpec((NORM_ROWS, width), lambda i: (i, 0))
    return pl.BlockSpec((1, NORM_ROWS, width), lambda i, at=at: (at, i, 0))


def terms_of(terms):
    arrays, specs = [], []
    for term in terms:
        array, at = term if isinstance(term, tuple) else (term, None)
        arrays.append(array)
        specs.append(row_spec(array, at))
    return arrays, specs


def total_of(refs):
    values = [ref[0] if len(ref.shape) == 3 else ref[...] for ref in refs]
    return sum(value.astype(F32) for value in values)


def add_norm(terms, gain):
    arrays, specs = terms_of(terms)
    tokens, width = arrays[0].shape[-2], arrays[0].shape[-1]
    tokens = min(a.shape[-2] for a in arrays)

    def kernel(*refs):
        gain_ref, x, out = refs[-3:]
        values = total_of(refs[:-3])
        x[...] = values
        out[...] = (normalize(values)[0] * gain_ref[...]).astype(BF)

    return call(
        kernel,
        (tokens // NORM_ROWS,),
        specs + [whole(gain)],
        [row_spec(shape((tokens, width)))] * 2,
        [shape((tokens, width), F32), shape((tokens, width))],
        [*arrays, gain],
        "add_norm",
    )


def norm_grad(grad, values, gain):
    normed, inv_std = normalize(values)
    scaled = grad * gain
    first_mean = jnp.mean(scaled, axis=-1, keepdims=True)
    second_mean = jnp.mean(scaled * normed, axis=-1, keepdims=True)
    return (
        inv_std * (scaled - first_mean - normed * second_mean),
        jnp.sum(grad * normed, axis=0, keepdims=True),
    )


def accumulate(ref, value):
    @pl.when(pl.program_id(0) == 0)
    def _():
        ref[...] = jnp.zeros_like(ref)

    ref[...] += value


def norm_back(terms, upper, values, gain):
    arrays, specs = terms_of(terms)
    tokens, width = values.shape

    def kernel(*refs):
        upper_ref, x, gain_ref, out, out_low, gain_grad = refs[-6:]
        back, part = norm_grad(total_of(refs[:-6]), x[...], gain_ref[...])
        result = upper_ref[...].astype(F32) + back
        out[...] = result
        out_low[...] = result.astype(BF)
        accumulate(gain_grad, part)

    return call(
        kernel,
        (tokens // NORM_ROWS,),
        specs + [row_spec(upper), row_spec(values), whole(gain)],
        [row_spec(values)] * 2 + [pl.BlockSpec((1, width), lambda i: (0, 0))],
        [shape((tokens, width), F32), shape((tokens, width)), shape((1, width), F32)],
        [*arrays, upper, values, gain],
        "norm_back",
    )


def last_back(terms, upper, values, gain, masked, unit, order):
    arrays, specs = terms_of(terms)
    tokens, width = values.shape

    def kernel(*refs):
        upper_ref, x, gain_ref, mask, out, gain_grad, mask_grad = refs[-7:]
        back, part = norm_grad(total_of(refs[:-7]), x[...], gain_ref[...])
        result = upper_ref[...].astype(F32) + back
        hit = mask[...] > 0.5
        out[...] = reorder(jnp.where(hit, 0.0, result).astype(BF), unit, order)
        accumulate(gain_grad, part)
        accumulate(mask_grad, jnp.sum(jnp.where(hit, result, 0.0), axis=0, keepdims=True))

    line = pl.BlockSpec((1, width), lambda i: (0, 0))
    return call(
        kernel,
        (tokens // NORM_ROWS,),
        specs + [row_spec(upper), row_spec(values), whole(gain), row_spec(masked)],
        [row_spec(values), line, line],
        [shape((tokens, width)), shape((1, width), F32), shape((1, width), F32)],
        [*arrays, upper, values, gain, masked],
        "last_back",
    )


def start(hidden, cotangent, masked, embed, gain, unit, order):
    tokens, width = hidden.shape

    def kernel(hid, cot, mask, embed_ref, gain_ref, x, out, grad):
        hit = mask[...] > 0.5
        values = jnp.where(
            hit, embed_ref[...], reorder(hid[...], unit, order).astype(F32)
        )
        x[...] = values
        out[...] = (normalize(values)[0] * gain_ref[...]).astype(BF)
        grad[...] = jnp.where(hit, reorder(cot[...], unit, order).astype(F32), 0.0).astype(BF)

    rows = row_spec(hidden)
    return call(
        kernel,
        (tokens // NORM_ROWS,),
        [rows, rows, row_spec(masked), whole(embed), whole(gain)],
        [rows] * 3,
        [shape((tokens, width), F32), shape((tokens, width)), shape((tokens, width))],
        [hidden, cotangent, masked, embed, gain],
        "start",
    )


def layer_output(upper, terms, unit, order):
    arrays, specs = terms_of(terms)
    tokens, width = upper.shape

    def kernel(*refs):
        values = refs[-2][...] + total_of(refs[:-2])
        refs[-1][...] = reorder(values.astype(BF), unit, order)

    return call(
        kernel,
        (tokens // NORM_ROWS,),
        specs + [row_spec(upper)],
        row_spec(upper),
        shape((tokens, width)),
        [*arrays, upper],
        "layer_output",
    )


def feed_up(pieces, weight):
    rows, width = pieces[0].shape
    hidden = weight.shape[1]
    step = 256

    def kernel(*refs):
        up, tokens, act, slope, sems = refs[5:]

        @pl.when(pl.program_id(0) == 0)
        def _():
            assemble(tokens, refs[:5], sems)

        u = mm(tokens[...], up[...])
        square = u * u
        bend = jnp.tanh(SLOPE * u * (1.0 + CUBIC * square))
        half = 0.5 * (1.0 + bend)
        act[...] = (u * half).astype(BF)
        slope[...] = half + 0.5 * u * (1.0 - bend * bend) * SLOPE * (1.0 + 3.0 * CUBIC * square)

    part = pl.BlockSpec((4 * rows, step), lambda j: (0, j))
    return call(
        kernel,
        (hidden // step,),
        [ANY] * 5 + [pl.BlockSpec((width, step), lambda j: (0, j))],
        [pl.BlockSpec((4 * rows, width), lambda j: (0, 0)), part, part],
        [shape((4 * rows, width)), shape((4 * rows, hidden)), shape((4 * rows, hidden), F32)],
        [*pieces, weight],
        "feed_up",
        scratch=[pltpu.SemaphoreType.DMA((5,))],
        flops=8 * rows * width * hidden,
        size=2 * width * (hidden + 8 * rows),
    )


def feed_down(grad_y, slope, weight):
    tokens, width = grad_y.shape
    hidden = weight.shape[1]
    step = 256

    def kernel(dy, slope_ref, down, out):
        out[...] = (mm(dy[...], down[...]) * slope_ref[...]).astype(BF)

    part = pl.BlockSpec((tokens, step), lambda j: (0, j))
    return call(
        kernel,
        (hidden // step,),
        [whole(grad_y), part, pl.BlockSpec((width, step), lambda j: (0, j))],
        part,
        shape((tokens, hidden)),
        [grad_y, slope, weight],
        "feed_down",
        flops=2 * tokens * width * hidden,
        size=2 * width * (hidden + 8 * tokens),
    )


def softmax(scores):
    exp_terms = jnp.exp(scores - jnp.max(scores, axis=-1, keepdims=True))
    return exp_terms / jnp.sum(exp_terms, axis=-1, keepdims=True)


def score_grad(probs, grad_probs):
    return (
        probs * (grad_probs - jnp.sum(probs * grad_probs, axis=-1, keepdims=True))
    ).astype(BF)


def head(ref, k):
    return ref[:, k * HD : (k + 1) * HD]


def self_forward(projected, images):
    tokens, width = projected.shape
    rows, group = tokens // images, width // 3
    heads = group // HD

    def kernel(proj, mixed):
        for k in range(heads):
            query, key, value = (head(proj, j * heads + k) for j in range(3))
            probs = softmax(mm_t(query, key) * SCALE).astype(BF)
            mixed[:, k * HD : (k + 1) * HD] = mm(probs, value).astype(BF)

    return call(
        kernel,
        (images,),
        [pl.BlockSpec((rows, width), lambda i: (i, 0))],
        pl.BlockSpec((rows, group), lambda i: (i, 0)),
        shape((tokens, group)),
        [projected],
        "self_forward",
        flops=4 * tokens * rows * group,
    )


def self_back(projected, grad_mixed, images):
    tokens, width = projected.shape
    rows, group = tokens // images, width // 3
    heads = group // HD

    def kernel(proj, grad, out):
        for k in range(heads):
            query, key, value = (head(proj, j * heads + k) for j in range(3))
            grad_head = head(grad, k)
            probs = softmax(mm_t(query, key) * SCALE)
            grad_scores = score_grad(probs, mm_t(grad_head, value))
            parts = (
                mm(grad_scores, key) * SCALE,
                t_mm(grad_scores, query) * SCALE,
                t_mm(probs.astype(BF), grad_head),
            )
            for j, part in enumerate(parts):
                at = (j * heads + k) * HD
                out[:, at : at + HD] = part.astype(BF)

    return call(
        kernel,
        (images,),
        [
            pl.BlockSpec((rows, width), lambda i: (i, 0)),
            pl.BlockSpec((rows, group), lambda i: (i, 0)),
        ],
        pl.BlockSpec((rows, width), lambda i: (i, 0)),
        shape((tokens, width)),
        [projected, grad_mixed],
        "self_back",
        flops=10 * tokens * rows * group,
    )


def cross_forward(queries, text_kv):
    tokens, group = queries.shape
    heads = group // HD

    def kernel(query, text, mixed):
        for k in range(heads):
            probs = softmax(mm_t(head(query, k), head(text, k)) * SCALE).astype(BF)
            mixed[:, k * HD : (k + 1) * HD] = mm(probs, head(text, heads + k)).astype(BF)

    return call(
        kernel,
        (1,),
        [whole(queries), whole(text_kv)],
        whole(queries),
        shape((tokens, group)),
        [queries, text_kv],
        "cross_forward",
        flops=4 * tokens * text_kv.shape[0] * group,
    )


def cross_back(queries, text_kv, grad_mixed):
    tokens, group = queries.shape
    context = text_kv.shape[0]
    heads = group // HD

    def kernel(query, text, grad, grad_query, grad_text):
        for k in range(heads):
            query_head, key, value = head(query, k), head(text, k), head(text, heads + k)
            grad_head = head(grad, k)
            probs = softmax(mm_t(query_head, key) * SCALE)
            grad_scores = score_grad(probs, mm_t(grad_head, value))
            grad_query[:, k * HD : (k + 1) * HD] = (mm(grad_scores, key) * SCALE).astype(BF)
            at = (heads + k) * HD
            grad_text[:, k * HD : (k + 1) * HD] = t_mm(grad_scores, query_head) * SCALE
            grad_text[:, at : at + HD] = t_mm(probs.astype(BF), grad_head)

    return call(
        kernel,
        (1,),
        [whole(queries), whole(text_kv), whole(grad_mixed)],
        [whole(queries), whole(text_kv)],
        [shape((tokens, group)), shape((context, 2 * group), F32)],
        [queries, text_kv, grad_mixed],
        "cross_back",
        flops=10 * tokens * context * group,
    )


def grad_products(pairs, name, core=None, blocks=0):
    count_in = len(pairs[0][0])
    tokens, width = pairs[0][0][0].shape
    widths = [y[0].shape[1] for _, y in pairs]
    total = sum(widths)
    rows = 256 if core is None else width // (2 * blocks)
    steps = width // rows if core is None else blocks
    step = 512
    count = len(pairs) * count_in

    def kernel(r, *refs):
        out = refs[2 * count]
        offset = 0
        for k, wide in enumerate(widths):
            left = [refs[k * count_in + b][...].T for b in range(count_in)]
            for at in range(0, wide, step):
                out[:, offset + at : offset + at + step] = sum(
                    mm(left[b], refs[count + k * count_in + b][:, at : at + step])
                    for b in range(count_in)
                ).astype(BF)
            offset += wide

    pick = (lambda i, r: (0, i)) if core is None else (lambda i, r: (0, 2 * i + r[0]))
    return call(
        kernel,
        (steps,),
        [pl.BlockSpec((tokens, rows), pick)] * count
        + [pl.BlockSpec((tokens, w), lambda i, r: (0, 0)) for w in widths for _ in range(count_in)],
        pl.BlockSpec((rows, total), lambda i, r: (i, 0)),
        shape((steps * rows, total)),
        [b for x, _ in pairs for b in x] + [b for _, y in pairs for b in y],
        name,
        flops=2 * tokens * count_in * steps * rows * total,
        size=4 * width * total,
        rank=jnp.zeros((), jnp.int32) if core is None else core,
    )


def pick_weights(three, one, rank):
    rows, width = one.shape[0], one.shape[1] // 4

    def kernel(r, three_ref, one_ref, *outs):
        for k in range(4):

            @pl.when(pl.program_id(0) == k)
            def _():
                for j in range(3):
                    outs[k][:, j * width : (j + 1) * width] = three_ref[j]
                outs[k][:, 3 * width :] = one_ref[...]

    outs = [shape((rows, 4 * width))] * 4
    return call(
        kernel,
        (4,),
        [
            pl.BlockSpec((3, rows, width), lambda k, r: (0, 0, k ^ r[0])),
            pl.BlockSpec((rows, width), lambda k, r: (0, k ^ r[0])),
        ],
        [whole(a) for a in outs],
        outs,
        [three, one],
        "pick_weights",
        rank=rank,
    )


def pick_rows(arrays, rank):
    rows = arrays[0].shape[1]
    widths = [a.shape[2] for a in arrays]
    count = len(arrays)

    def kernel(r, *refs):
        for k in range(4):

            @pl.when(pl.program_id(0) == k)
            def _():
                at = 0
                for ref, width in zip(refs, widths):
                    refs[count + k][:, at : at + width] = ref[0]
                    at += width

    outs = [shape((rows, sum(widths)))] * 4
    return call(
        kernel,
        (4,),
        [pl.BlockSpec((1, rows, w), lambda k, r: (k ^ r[0], 0, 0)) for w in widths],
        [whole(a) for a in outs],
        outs,
        arrays,
        "pick_rows",
        rank=rank,
    )


def place(parts, rank):
    def kernel(r, *refs):
        for k in range(4):

            @pl.when(pl.program_id(0) == k)
            def _():
                refs[4][0] = refs[k][...]

    rows, columns = parts[0].shape
    return call(
        kernel,
        (4,),
        [whole(p) for p in parts],
        pl.BlockSpec((1, rows, columns), lambda k, r: (k ^ r[0], 0, 0)),
        shape((4, rows, columns)),
        parts,
        "place",
        rank=rank,
    )


def finish_wide(parts, rank):
    rows, total = parts[0].shape
    width = total // 2

    def kernel(r, *refs):
        for k in range(4):

            @pl.when(pl.program_id(0) == k)
            def _():
                refs[4][...] = refs[k][:, :width].astype(F32)
                refs[5][...] = refs[k][:, width:].astype(F32)

    flat = pl.BlockSpec((rows, width), lambda k, r: (0, k ^ r[0]))
    return call(
        kernel,
        (4,),
        [whole(p) for p in parts],
        [flat, flat],
        [shape((rows, 4 * width), F32)] * 2,
        parts,
        "finish_wide",
        rank=rank,
    )


def finish_all(parts, text_grad, rank):
    rows, total = parts[0].shape
    width = total // 6

    def kernel(r, *refs):
        key, value, three, out, cross, cross_out = refs[4:]
        for k in range(4):

            @pl.when(pl.program_id(0) == k)
            def _():
                def part(j):
                    return refs[k][:, j * width : (j + 1) * width].astype(F32)

                for j in range(3):
                    three[j] = part(j)
                out[...] = part(3)
                cross[0] = part(4)
                cross_out[...] = part(5)

        cross[1] = key[...]
        cross[2] = value[...]

    wide = pl.BlockSpec((3, rows, width), lambda k, r: (0, 0, k ^ r[0]))
    flat = pl.BlockSpec((rows, width), lambda k, r: (0, k ^ r[0]))
    return call(
        kernel,
        (4,),
        [whole(p) for p in parts]
        + [flat, pl.BlockSpec((rows, width), lambda k, r: (0, 4 + (k ^ r[0])))],
        [wide, flat, wide, flat],
        [shape((3, rows, 4 * width), F32), shape((rows, 4 * width), F32)] * 2,
        [*parts, text_grad, text_grad],
        "finish_all",
        rank=rank,
    )


def plane_block(k):
    return (k >> 1) & 1, (k >> 2) * 2 + (k & 1)


def text_forward(caption, w_text, w_cross):
    context, rows = caption.shape[0], w_text.shape[0]
    half, width = context // 2, w_cross.shape[2] // 4

    def kernel(cap, weight, cross, own, blocks):
        own[...] = mm_t(cap[...], weight[...]).astype(BF)
        for j in range(2):
            part = mm(own[...], cross[1 + j]).astype(BF)
            for k in range(8):
                core, group = plane_block(k)
                blocks[k, :, j * width : (j + 1) * width] = part[
                    core * half : (core + 1) * half, group * width : (group + 1) * width
                ]

    return call(
        kernel,
        (1,),
        [whole(caption), whole(w_text), whole(w_cross)],
        [
            pl.BlockSpec((context, rows), lambda i: (0, 0)),
            pl.BlockSpec((8, half, 2 * width), lambda i: (0, 0, 0)),
        ],
        [shape((context, rows)), shape((8, half, 2 * width))],
        [caption, w_text, w_cross],
        "text_forward",
    )


def text_back(blocks, own_text, w_cross, caption, w_text, extra):
    context, rows = own_text.shape
    half, width = context // 2, w_cross.shape[2] // 4
    wide = caption.shape[1] // 4
    tail = extra.shape[0]

    def kernel(block, own, cross, cap, weight, more, kv_grad, text_grad, out, grads):
        for k in range(8):
            core, group = plane_block(k)
            for j in range(2):
                at = (4 * j + group) * width
                grads[core * half : (core + 1) * half, at : at + width] = block[
                    k, :, j * width : (j + 1) * width
                ]
        kv_grad[...] = t_mm(own[...], grads[...])
        grad_text = sum(
            mm_t(grads[:, 4 * j * width : 4 * (j + 1) * width], cross[1 + j]) for j in range(2)
        ).astype(BF)
        text_grad[...] = t_mm(grad_text, cap[...])
        part = mm(grad_text, weight[...]).astype(BF)
        for k in range(8):
            core, group = plane_block(k)
            out[k, :half, :] = part[core * half : (core + 1) * half, group * wide : (group + 1) * wide]
            out[k, half:, :] = more[...]

    operands = [blocks, own_text, w_cross, caption, w_text, extra]
    outs = [
        shape((rows, 8 * width), F32),
        shape((rows, 4 * wide), F32),
        shape((8, half + tail, wide)),
    ]
    return call(
        kernel,
        (1,),
        [whole(a) for a in operands],
        [whole(a) for a in outs],
        outs,
        operands,
        "text_back",
        scratch=[pltpu.VMEM((context, 8 * width), BF)],
    )


def caption_output(own, other, core):
    count, half, wide = own.shape

    def kernel(r, own_ref, other_ref, out):
        block = jnp.where(pl.program_id(0) == r[0], own_ref[0], other_ref[0])
        out[...] = block.astype(F32)

    block = pl.BlockSpec((1, half, wide), lambda i, k, r: (k, 0, 0))
    return call(
        kernel,
        (2, count),
        [block, block],
        pl.BlockSpec((half, wide), lambda i, k, r: (i, k)),
        shape((2 * half, 4 * wide), F32),
        [own, other],
        "caption_output",
        rank=core,
    )


def column_blocks(weight, count):
    rows = weight.shape[0]
    return weight.reshape(rows, count, -1).transpose(1, 0, 2)


def halves_of(values, width):
    high = values.astype(BF)
    low = (values - high.astype(F32)).astype(BF)
    return jnp.concatenate([high.reshape(-1, width), low.reshape(-1, width)], axis=0)


def whole_of(halves, width):
    rows = halves.shape[0] // 2
    return (halves[:rows] + halves[rows:]).reshape(-1, width)


def make_local(z_size):
    def sum_z(values):
        parts = values.reshape(z_size, -1, values.shape[-1])
        mine = trade(parts, "z").astype(F32).sum(axis=0).astype(BF)
        return spread(mine, "z", z_size).reshape(values.shape)

    def add_z(values):
        step = 1
        while step < z_size:
            values = values + lax.ppermute(
                values, "z", tuple((k, k ^ step) for k in range(z_size))
            )
            step *= 2
        return values

    def layer_order(values):
        shaped = values.reshape(values.shape[:-1] + (z_size, 2, 2, -1))
        return jnp.swapaxes(shaped, -3, -2).reshape(values.shape)

    def local(
        hidden,
        mask_index,
        mask_count,
        mask_embed,
        norm_gains,
        caption,
        w_qkv,
        w_out,
        w_cross,
        w_cross_out,
        w_text,
        w_up,
        w_down,
        cotangent,
    ):
        images, local_rows, width = hidden.shape
        full_length = mask_index.shape[1]
        rank = lax.axis_index("x") * 2 + lax.axis_index("y")
        core = lax.axis_index("c")
        tokens = images * local_rows
        group = width // 4
        text_width = caption.shape[1]

        unit = width // (4 * z_size)
        inside = unit % 128 == 0
        order = [4 * k + j for k in range(z_size) for j in (0, 2, 1, 3)] if inside else None

        def outer(values):
            return values if inside else layer_order(values)

        w_qkv, w_cross = w_qkv.transpose(1, 0, 2), w_cross.transpose(1, 0, 2)
        first = swap_parts(pick_weights(w_qkv, w_out, rank))
        first = gather_rows(place(first, rank))

        positions = lax.axis_index("y") * local_rows + jnp.arange(local_rows, dtype=jnp.int32)
        ranks = jnp.arange(full_length, dtype=jnp.int32)
        matches = (mask_index[:, :, None] == positions[None, None, :]) & (
            ranks[None, :, None] < mask_count[:, None, None]
        )
        masked = jnp.any(matches, axis=1).reshape(tokens, 1).astype(F32)
        gains = layer_order(norm_gains)
        gain_a, gain_b, gain_c = gains[:1], gains[1:2], gains[2:]
        start_x, attn_in, grad_top = start(
            outer(hidden.reshape(tokens, width)),
            outer(cotangent.reshape(tokens, width)),
            masked,
            layer_order(mask_embed)[None],
            gain_a,
            unit,
            order,
        )
        attn_in = gather_tokens(attn_in)
        mid = jnp.concatenate([column_blocks(w_cross[0], 4), column_blocks(w_cross_out, 4)], axis=2)
        up = column_blocks(w_up, 4)
        attn_in, mid, up = lax.optimization_barrier((attn_in, mid, up))
        mid, up = gather_rows(trade(mid)), gather_rows(trade(up))

        own_text, kv_part = text_forward(caption, w_text, w_cross)
        text_kv = trade(kv_part, PLANE).astype(F32).sum(axis=0).astype(BF)
        text_kv = sum_z(text_kv)
        other = swap(text_kv, "c")
        text_kv = jnp.concatenate(
            [jnp.where(core == 0, text_kv, other), jnp.where(core == 0, other, text_kv)], axis=0
        )
        attn_in, text_kv = lax.optimization_barrier((attn_in, text_kv))

        attn_in, projected = gather_mm(attn_in, first, 0, 3 * group, "qkv_mm")
        self_mixed = self_forward(projected, 2 * images)
        down = column_blocks(w_down, 4)
        self_mixed, down = lax.optimization_barrier((self_mixed, down))
        down = gather_rows(trade(down))
        parts = mm_scatter(self_mixed, first[:, 3 * group :])
        after_attn, cross_in = add_norm([start_x] + parts, gain_b)

        cross_in, cross_queries = gather_mm(gather_tokens(cross_in), mid, 0, group, "query_mm")
        cross_mixed = cross_forward(cross_queries, text_kv)
        parts = mm_scatter(cross_mixed, mid[:, group:])
        after_cross, mlp_in = add_norm([after_attn] + parts, gain_c)

        mlp_in = gather_tokens(mlp_in)
        mlp_in, grad_top = lax.optimization_barrier((mlp_in, grad_top))
        grad_y = jnp.concatenate(gather_tokens(grad_top), axis=0)
        mlp_in, activated, slope = feed_up(mlp_in, up)
        early = [attn_in, self_mixed, cross_in, cross_mixed]
        if inside:
            grad_axes, halves = "z", (core, z_size)

            def both(values):
                return [values, swap(values, "c")]

        else:
            grad_axes, halves = DATA, ()

            def both(values):
                return [values]

        early = [both(values) for values in early]
        down_part = grad_products([(both(grad_y), both(activated))], "down_grads", *halves)
        mlp_in = both(mlp_in)
        slope, down_part, early, mlp_in = lax.optimization_barrier((slope, down_part, early, mlp_in))
        down_rows = scatter_grad(down_part, grad_axes)
        grad_pre = feed_down(grad_y, slope, down)
        parts = mm_scatter(grad_pre, up)
        up_part = grad_products([(mlp_in, both(grad_pre))], "up_grads", *halves)
        grad_after_cross, cross_branch, gain_grad_c = norm_back(
            parts, grad_top, after_cross, gain_c
        )

        cross_branch = gather_tokens(cross_branch)
        activated, cross_own = lax.optimization_barrier((activated, cross_branch[0]))
        result = mm_t(activated, down).astype(BF)
        cross_branch, up_part, result = lax.optimization_barrier(
            ((cross_own,) + cross_branch[1:], up_part, result)
        )
        cross_branch, grad_cross_mixed = gather_mm(
            cross_branch, mid, group, group, "cross_out_back"
        )
        grad_cq, kv_grad = cross_back(cross_queries, text_kv, grad_cross_mixed)
        up_part, down_rows, kv_grad = lax.optimization_barrier((up_part, down_rows, kv_grad))
        up_rows = scatter_grad(up_part, grad_axes)
        cross_branch, grad_cq_both = both(cross_branch), both(grad_cq)
        parts = mm_scatter(grad_cq, mid[:, :group])
        grad_after_attn, attn_branch, gain_grad_b = norm_back(
            parts, grad_after_cross, after_attn, gain_b
        )

        attn_branch, result = lax.optimization_barrier((gather_tokens(attn_branch), result))
        result = scatter_first(token_blocks(result))
        attn_branch, grad_self_mixed = gather_mm(attn_branch, first, 3 * group, group, "out_back")
        grad_projected = self_back(projected, grad_self_mixed, 2 * images)
        grad_projected, result = lax.optimization_barrier((grad_projected, result))
        result = scatter_second(result)
        rest_part = grad_products(
            [
                (early[0], both(grad_projected)),
                (both(attn_branch), early[1]),
                (early[2], grad_cq_both),
                (cross_branch, early[3]),
            ],
            "attention_grads",
            *halves,
        )
        grad_projected, result, kv_grad, rest_part = lax.optimization_barrier(
            (grad_projected, result, kv_grad, rest_part)
        )
        rest_part, up_rows = lax.optimization_barrier((rest_part, up_rows))
        rest_rows = scatter_grad(rest_part, grad_axes)
        parts = mm_scatter(grad_projected, first[:, : 3 * group])
        grad_hidden, gain_grad_a, mask_grad = last_back(
            parts,
            grad_after_attn,
            start_x,
            gain_a,
            masked,
            unit,
            order,
        )
        sums = jnp.concatenate([gain_grad_a, gain_grad_b, gain_grad_c, mask_grad], axis=0)


        kv_part = kv_grad.astype(BF).reshape(2, z_size, -1, 2 * group)
        kv_part = kv_part.transpose(1, 0, 2, 3).reshape(2 * z_size, -1, 2 * group)
        kv_part = trade(kv_part, DATA).astype(F32).sum(axis=0).astype(BF)
        kv_sum = spread(kv_part, "z", z_size).reshape(-1, 2 * group)
        wide_rows = swap_parts(pick_rows([down_rows, up_rows], rank))
        kv_sum, wide_rows = lax.optimization_barrier((kv_sum, wide_rows))
        kv_grads = spread(kv_sum, PLANE, 8)
        kv_weight_grad, grad_text_w, caption_part = text_back(
            kv_grads, own_text, w_cross, caption, w_text, halves_of(sums, text_width // 4)
        )
        half_context = caption.shape[0] // 2
        caption_part = trade(caption_part, PLANE)
        output = layer_output(after_cross, result, unit, order)
        down_grad, up_grad = finish_wide(wide_rows, rank)
        caption_part, output, down_grad, up_grad = lax.optimization_barrier(
            (caption_part, output, down_grad, up_grad)
        )
        caption_part = caption_part.astype(F32).sum(axis=0)
        sums = layer_order(add_z(whole_of(caption_part[half_context:], width)))
        caption_part = caption_part[:half_context].astype(BF).reshape(z_size, -1, text_width // 4)
        caption_part = trade(caption_part, "z").astype(F32).sum(axis=0).astype(BF)
        rest_rows = pick_rows([rest_rows], rank)
        caption_part = spread(caption_part, "z", z_size).reshape(half_context, -1)
        caption_part, rest_rows = lax.optimization_barrier((caption_part, rest_rows))
        rest_rows = swap_parts(rest_rows)
        caption_part = spread(caption_part)
        grad_caption = caption_output(caption_part, swap(caption_part, "c"), core)
        qkv_grad, out_grad, grad_cross, cross_out_grad = finish_all(
            rest_rows, kv_weight_grad, rank
        )
        return (
            outer(output).reshape(hidden.shape),
            outer(grad_hidden).reshape(hidden.shape),
            grad_caption,
            sums[:3],
            sums[3],
            qkv_grad.transpose(1, 0, 2),
            out_grad,
            grad_cross.transpose(1, 0, 2),
            cross_out_grad,
            grad_text_w,
            up_grad,
            down_grad,
        )

    return local


def solution(mesh):
    z_size = mesh.shape["img"] // 4
    inner = Mesh(mesh.devices.reshape(z_size, 2, 2, 2), ("z", "x", "c", "y"))
    image = ("z", "x", "c")
    tokens = P(image, "y", None)
    rows = P(image + ("y",))
    in_specs = (tokens, P(image, None), P(image), P(), P(), P()) + (rows,) * 7 + (tokens,)
    out_specs = (tokens, tokens, P(), P(), P()) + (rows,) * 7
    return jax.shard_map(
        make_local(z_size), mesh=inner, in_specs=in_specs, out_specs=out_specs, check_vma=False
    )
```

```python
import math

import jax
import jax.numpy as jnp
from jax import lax
from jax.experimental import pallas as pl
from jax.experimental.pallas import tpu as pltpu
from jax.sharding import Mesh
from jax.sharding import PartitionSpec as P

HD = 128
EPS = 1e-05
BF = jnp.bfloat16
F32 = jnp.float32
PAIR = ((0, 1), (1, 0))
GROUP = ("x", "y")
DATA = ("z", "c")
PLANE = ("x", "c", "y")
VMEM = 48 * 1024 * 1024
SCALE = 1.0 / math.sqrt(HD)
SLOPE = math.sqrt(2.0 / math.pi)
CUBIC = 0.044715


def dot(a, b, dims):
    return lax.dot_general(a, b, (dims, ((), ())), preferred_element_type=F32)


def mm(a, b):
    return dot(a, b, ((1,), (0,)))


def mm_t(a, b):
    return dot(a, b, ((1,), (1,)))


def t_mm(a, b):
    return dot(a, b, ((0,), (0,)))


def shape(dims, dtype=BF):
    return jax.ShapeDtypeStruct(dims, dtype)


def swap(values, axis):
    return lax.ppermute(values, axis, PAIR)


def trade(blocks, axes=GROUP):
    return lax.all_to_all(blocks, axes, 0, 0, tiled=True)


def spread(values, axes=GROUP, count=4):
    return trade(jnp.broadcast_to(values[None], (count,) + values.shape), axes)


def gather_tokens(own):
    half = own.shape[0] // 2
    from_x = swap(own, "x")
    from_y = swap(own, "y")
    return own, from_y, from_x, swap(from_x[:half], "y"), swap(from_y[half:], "x")


def scatter_first(parts):
    own, for_y, for_x, for_low, for_high = parts
    half = for_low.shape[0]
    low = swap(for_low, "y").astype(F32) + for_x[:half].astype(F32)
    high = swap(for_high, "x").astype(F32) + for_y[half:].astype(F32)
    return (
        own,
        jnp.concatenate([low.astype(BF), for_x[half:]], axis=0),
        jnp.concatenate([for_y[:half], high.astype(BF)], axis=0),
    )


def scatter_second(parts):
    own, for_x, for_y = parts
    return [own, swap(for_x, "x"), swap(for_y, "y")]


def scatter_tokens(parts):
    return scatter_second(scatter_first(parts))


def swap_parts(parts):
    return [
        parts[0],
        swap(parts[1], "y"),
        swap(parts[2], "x"),
        lax.ppermute(parts[3], GROUP, ((0, 3), (1, 2), (2, 1), (3, 0))),
    ]


def gather_rows(rows):
    return lax.all_gather(rows.reshape(-1, rows.shape[-1]), DATA, axis=0, tiled=True)


def scatter_grad(partial, axes):
    summed = lax.psum_scatter(partial, axes, scatter_dimension=0, tiled=True)
    return summed.reshape(4, -1, summed.shape[-1])


def call(kernel, grid, in_specs, out_specs, out_shape, operands, name, flops=0, size=1 << 22,
         rank=None, scratch=()):
    options = dict(
        out_shape=out_shape,
        compiler_params=pltpu.CompilerParams(vmem_limit_bytes=VMEM),
        cost_estimate=pl.CostEstimate(flops=flops, bytes_accessed=size, transcendentals=0),
        name=name,
    )
    if rank is None:
        return pl.pallas_call(
            kernel, grid=grid, in_specs=in_specs, out_specs=out_specs, scratch_shapes=scratch,
            **options,
        )(*operands)
    spec = pltpu.PrefetchScalarGridSpec(
        num_scalar_prefetch=1,
        grid=grid,
        in_specs=in_specs,
        out_specs=out_specs,
        scratch_shapes=scratch,
    )
    return pl.pallas_call(kernel, grid_spec=spec, **options)(rank.reshape(1), *operands)


def whole(array):
    return pl.BlockSpec(array.shape, lambda *_: (0,) * len(array.shape))


def reorder(values, unit, order):
    if order is None:
        return values
    return jnp.concatenate([values[:, k * unit : (k + 1) * unit] for k in order], axis=1)


def assemble(target, pieces, sems):
    copies, at = [], 0
    for k, piece in enumerate(pieces):
        rows = piece.shape[0]
        copies.append(pltpu.make_async_copy(piece, target.at[at : at + rows], sems.at[k]))
        at += rows
    for copy in copies:
        copy.start()
    for copy in copies:
        copy.wait()


ANY = pl.BlockSpec(memory_space=pl.ANY)


def gather_mm(pieces, weight, first, columns, name):
    rows, width = pieces[0].shape
    step = 256

    def kernel(*refs):
        tokens, out, sems = refs[6:]

        @pl.when(pl.program_id(0) == 0)
        def _():
            assemble(tokens, refs[:5], sems)

        out[...] = mm(tokens[...], refs[5][...]).astype(BF)

    return call(
        kernel,
        (columns // step,),
        [ANY] * 5 + [pl.BlockSpec((width, step), lambda j: (0, first // step + j))],
        [
            pl.BlockSpec((4 * rows, width), lambda j: (0, 0)),
            pl.BlockSpec((4 * rows, step), lambda j: (0, j)),
        ],
        [shape((4 * rows, width)), shape((4 * rows, columns))],
        [*pieces, weight],
        name,
        flops=8 * rows * width * columns,
        size=2 * width * (columns + 8 * rows),
        scratch=[pltpu.SemaphoreType.DMA((5,))],
    )


def mm_scatter(values, weight):
    return scatter_tokens(token_blocks(mm_t(values, weight).astype(BF)))


def token_blocks(partial):
    rows = partial.shape[0] // 4
    cuts = [0, rows, 2 * rows, 3 * rows, 3 * rows + rows // 2, 4 * rows]
    return [partial[a:b] for a, b in zip(cuts, cuts[1:])]


def normalize(values):
    centred = values - jnp.mean(values, axis=-1, keepdims=True)
    inv_std = lax.rsqrt(jnp.mean(centred * centred, axis=-1, keepdims=True) + EPS)
    return centred * inv_std, inv_std


NORM_ROWS = 32


def row_spec(array, at=None):
    width = array.shape[-1]
    if at is None:
        return pl.BlockSpec((NORM_ROWS, width), lambda i: (i, 0))
    return pl.BlockSpec((1, NORM_ROWS, width), lambda i, at=at: (at, i, 0))


def terms_of(terms):
    arrays, specs = [], []
    for term in terms:
        array, at = term if isinstance(term, tuple) else (term, None)
        arrays.append(array)
        specs.append(row_spec(array, at))
    return arrays, specs


def total_of(refs):
    values = [ref[0] if len(ref.shape) == 3 else ref[...] for ref in refs]
    return sum(value.astype(F32) for value in values)


def add_norm(terms, gain):
    arrays, specs = terms_of(terms)
    tokens, width = arrays[0].shape[-2], arrays[0].shape[-1]
    tokens = min(a.shape[-2] for a in arrays)

    def kernel(*refs):
        gain_ref, x, out = refs[-3:]
        values = total_of(refs[:-3])
        x[...] = values
        out[...] = (normalize(values)[0] * gain_ref[...]).astype(BF)

    return call(
        kernel,
        (tokens // NORM_ROWS,),
        specs + [whole(gain)],
        [row_spec(shape((tokens, width)))] * 2,
        [shape((tokens, width), F32), shape((tokens, width))],
        [*arrays, gain],
        "add_norm",
    )


def norm_grad(grad, values, gain):
    normed, inv_std = normalize(values)
    scaled = grad * gain
    first_mean = jnp.mean(scaled, axis=-1, keepdims=True)
    second_mean = jnp.mean(scaled * normed, axis=-1, keepdims=True)
    return (
        inv_std * (scaled - first_mean - normed * second_mean),
        jnp.sum(grad * normed, axis=0, keepdims=True),
    )


def accumulate(ref, value):
    @pl.when(pl.program_id(0) == 0)
    def _():
        ref[...] = jnp.zeros_like(ref)

    ref[...] += value


def norm_back(terms, upper, values, gain):
    arrays, specs = terms_of(terms)
    tokens, width = values.shape

    def kernel(*refs):
        upper_ref, x, gain_ref, out, out_low, gain_grad = refs[-6:]
        back, part = norm_grad(total_of(refs[:-6]), x[...], gain_ref[...])
        result = upper_ref[...].astype(F32) + back
        out[...] = result
        out_low[...] = result.astype(BF)
        accumulate(gain_grad, part)

    return call(
        kernel,
        (tokens // NORM_ROWS,),
        specs + [row_spec(upper), row_spec(values), whole(gain)],
        [row_spec(values)] * 2 + [pl.BlockSpec((1, width), lambda i: (0, 0))],
        [shape((tokens, width), F32), shape((tokens, width)), shape((1, width), F32)],
        [*arrays, upper, values, gain],
        "norm_back",
    )


def last_back(terms, upper, values, gain, masked, unit, order):
    arrays, specs = terms_of(terms)
    tokens, width = values.shape

    def kernel(*refs):
        upper_ref, x, gain_ref, mask, out, gain_grad, mask_grad = refs[-7:]
        back, part = norm_grad(total_of(refs[:-7]), x[...], gain_ref[...])
        result = upper_ref[...].astype(F32) + back
        hit = mask[...] > 0.5
        out[...] = reorder(jnp.where(hit, 0.0, result).astype(BF), unit, order)
        accumulate(gain_grad, part)
        accumulate(mask_grad, jnp.sum(jnp.where(hit, result, 0.0), axis=0, keepdims=True))

    line = pl.BlockSpec((1, width), lambda i: (0, 0))
    return call(
        kernel,
        (tokens // NORM_ROWS,),
        specs + [row_spec(upper), row_spec(values), whole(gain), row_spec(masked)],
        [row_spec(values), line, line],
        [shape((tokens, width)), shape((1, width), F32), shape((1, width), F32)],
        [*arrays, upper, values, gain, masked],
        "last_back",
    )


def start(hidden, cotangent, masked, embed, gain, unit, order):
    tokens, width = hidden.shape

    def kernel(hid, cot, mask, embed_ref, gain_ref, x, out, grad):
        hit = mask[...] > 0.5
        values = jnp.where(
            hit, embed_ref[...], reorder(hid[...], unit, order).astype(F32)
        )
        x[...] = values
        out[...] = (normalize(values)[0] * gain_ref[...]).astype(BF)
        grad[...] = jnp.where(hit, reorder(cot[...], unit, order).astype(F32), 0.0).astype(BF)

    rows = row_spec(hidden)
    return call(
        kernel,
        (tokens // NORM_ROWS,),
        [rows, rows, row_spec(masked), whole(embed), whole(gain)],
        [rows] * 3,
        [shape((tokens, width), F32), shape((tokens, width)), shape((tokens, width))],
        [hidden, cotangent, masked, embed, gain],
        "start",
    )


def layer_output(upper, terms, unit, order):
    arrays, specs = terms_of(terms)
    tokens, width = upper.shape

    def kernel(*refs):
        values = refs[-2][...] + total_of(refs[:-2])
        refs[-1][...] = reorder(values.astype(BF), unit, order)

    return call(
        kernel,
        (tokens // NORM_ROWS,),
        specs + [row_spec(upper)],
        row_spec(upper),
        shape((tokens, width)),
        [*arrays, upper],
        "layer_output",
    )


def feed_up(pieces, weight):
    rows, width = pieces[0].shape
    hidden = weight.shape[1]
    step = 256

    def kernel(*refs):
        up, tokens, act, slope, sems = refs[5:]

        @pl.when(pl.program_id(0) == 0)
        def _():
            assemble(tokens, refs[:5], sems)

        u = mm(tokens[...], up[...])
        square = u * u
        bend = jnp.tanh(SLOPE * u * (1.0 + CUBIC * square))
        half = 0.5 * (1.0 + bend)
        act[...] = (u * half).astype(BF)
        slope[...] = half + 0.5 * u * (1.0 - bend * bend) * SLOPE * (1.0 + 3.0 * CUBIC * square)

    part = pl.BlockSpec((4 * rows, step), lambda j: (0, j))
    return call(
        kernel,
        (hidden // step,),
        [ANY] * 5 + [pl.BlockSpec((width, step), lambda j: (0, j))],
        [pl.BlockSpec((4 * rows, width), lambda j: (0, 0)), part, part],
        [shape((4 * rows, width)), shape((4 * rows, hidden)), shape((4 * rows, hidden), F32)],
        [*pieces, weight],
        "feed_up",
        scratch=[pltpu.SemaphoreType.DMA((5,))],
        flops=8 * rows * width * hidden,
        size=2 * width * (hidden + 8 * rows),
    )


def feed_down(grad_y, slope, weight):
    tokens, width = grad_y.shape
    hidden = weight.shape[1]
    step = 256

    def kernel(dy, slope_ref, down, out):
        out[...] = (mm(dy[...], down[...]) * slope_ref[...]).astype(BF)

    part = pl.BlockSpec((tokens, step), lambda j: (0, j))
    return call(
        kernel,
        (hidden // step,),
        [whole(grad_y), part, pl.BlockSpec((width, step), lambda j: (0, j))],
        part,
        shape((tokens, hidden)),
        [grad_y, slope, weight],
        "feed_down",
        flops=2 * tokens * width * hidden,
        size=2 * width * (hidden + 8 * tokens),
    )


def softmax(scores):
    exp_terms = jnp.exp(scores - jnp.max(scores, axis=-1, keepdims=True))
    return exp_terms / jnp.sum(exp_terms, axis=-1, keepdims=True)


def score_grad(probs, grad_probs):
    return (
        probs * (grad_probs - jnp.sum(probs * grad_probs, axis=-1, keepdims=True))
    ).astype(BF)


def head(ref, k):
    return ref[:, k * HD : (k + 1) * HD]


def self_forward(projected, images):
    tokens, width = projected.shape
    rows, group = tokens // images, width // 3
    heads = group // HD

    def kernel(proj, mixed):
        for k in range(heads):
            query, key, value = (head(proj, j * heads + k) for j in range(3))
            probs = softmax(mm_t(query, key) * SCALE).astype(BF)
            mixed[:, k * HD : (k + 1) * HD] = mm(probs, value).astype(BF)

    return call(
        kernel,
        (images,),
        [pl.BlockSpec((rows, width), lambda i: (i, 0))],
        pl.BlockSpec((rows, group), lambda i: (i, 0)),
        shape((tokens, group)),
        [projected],
        "self_forward",
        flops=4 * tokens * rows * group,
    )


def self_back(projected, grad_mixed, images):
    tokens, width = projected.shape
    rows, group = tokens // images, width // 3
    heads = group // HD

    def kernel(proj, grad, out):
        for k in range(heads):
            query, key, value = (head(proj, j * heads + k) for j in range(3))
            grad_head = head(grad, k)
            probs = softmax(mm_t(query, key) * SCALE)
            grad_scores = score_grad(probs, mm_t(grad_head, value))
            parts = (
                mm(grad_scores, key) * SCALE,
                t_mm(grad_scores, query) * SCALE,
                t_mm(probs.astype(BF), grad_head),
            )
            for j, part in enumerate(parts):
                at = (j * heads + k) * HD
                out[:, at : at + HD] = part.astype(BF)

    return call(
        kernel,
        (images,),
        [
            pl.BlockSpec((rows, width), lambda i: (i, 0)),
            pl.BlockSpec((rows, group), lambda i: (i, 0)),
        ],
        pl.BlockSpec((rows, width), lambda i: (i, 0)),
        shape((tokens, width)),
        [projected, grad_mixed],
        "self_back",
        flops=10 * tokens * rows * group,
    )


def cross_forward(queries, text_kv):
    tokens, group = queries.shape
    heads = group // HD

    def kernel(query, text, mixed):
        for k in range(heads):
            probs = softmax(mm_t(head(query, k), head(text, k)) * SCALE).astype(BF)
            mixed[:, k * HD : (k + 1) * HD] = mm(probs, head(text, heads + k)).astype(BF)

    return call(
        kernel,
        (1,),
        [whole(queries), whole(text_kv)],
        whole(queries),
        shape((tokens, group)),
        [queries, text_kv],
        "cross_forward",
        flops=4 * tokens * text_kv.shape[0] * group,
    )


def cross_back(queries, text_kv, grad_mixed):
    tokens, group = queries.shape
    context = text_kv.shape[0]
    heads = group // HD

    def kernel(query, text, grad, grad_query, grad_text):
        for k in range(heads):
            query_head, key, value = head(query, k), head(text, k), head(text, heads + k)
            grad_head = head(grad, k)
            probs = softmax(mm_t(query_head, key) * SCALE)
            grad_scores = score_grad(probs, mm_t(grad_head, value))
            grad_query[:, k * HD : (k + 1) * HD] = (mm(grad_scores, key) * SCALE).astype(BF)
            at = (heads + k) * HD
            grad_text[:, k * HD : (k + 1) * HD] = t_mm(grad_scores, query_head) * SCALE
            grad_text[:, at : at + HD] = t_mm(probs.astype(BF), grad_head)

    return call(
        kernel,
        (1,),
        [whole(queries), whole(text_kv), whole(grad_mixed)],
        [whole(queries), whole(text_kv)],
        [shape((tokens, group)), shape((context, 2 * group), F32)],
        [queries, text_kv, grad_mixed],
        "cross_back",
        flops=10 * tokens * context * group,
    )


def grad_products(pairs, name, core=None, blocks=0):
    count_in = len(pairs[0][0])
    tokens, width = pairs[0][0][0].shape
    widths = [y[0].shape[1] for _, y in pairs]
    total = sum(widths)
    rows = 256 if core is None else width // (2 * blocks)
    steps = width // rows if core is None else blocks
    step = 512
    count = len(pairs) * count_in

    def kernel(r, *refs):
        out = refs[2 * count]
        offset = 0
        for k, wide in enumerate(widths):
            left = [refs[k * count_in + b][...].T for b in range(count_in)]
            for at in range(0, wide, step):
                out[:, offset + at : offset + at + step] = sum(
                    mm(left[b], refs[count + k * count_in + b][:, at : at + step])
                    for b in range(count_in)
                ).astype(BF)
            offset += wide

    pick = (lambda i, r: (0, i)) if core is None else (lambda i, r: (0, 2 * i + r[0]))
    return call(
        kernel,
        (steps,),
        [pl.BlockSpec((tokens, rows), pick)] * count
        + [pl.BlockSpec((tokens, w), lambda i, r: (0, 0)) for w in widths for _ in range(count_in)],
        pl.BlockSpec((rows, total), lambda i, r: (i, 0)),
        shape((steps * rows, total)),
        [b for x, _ in pairs for b in x] + [b for _, y in pairs for b in y],
        name,
        flops=2 * tokens * count_in * steps * rows * total,
        size=4 * width * total,
        rank=jnp.zeros((), jnp.int32) if core is None else core,
    )


def pick_weights(three, one, rank):
    rows, width = one.shape[0], one.shape[1] // 4

    def kernel(r, three_ref, one_ref, *outs):
        for k in range(4):

            @pl.when(pl.program_id(0) == k)
            def _():
                for j in range(3):
                    outs[k][:, j * width : (j + 1) * width] = three_ref[j]
                outs[k][:, 3 * width :] = one_ref[...]

    outs = [shape((rows, 4 * width))] * 4
    return call(
        kernel,
        (4,),
        [
            pl.BlockSpec((3, rows, width), lambda k, r: (0, 0, k ^ r[0])),
            pl.BlockSpec((rows, width), lambda k, r: (0, k ^ r[0])),
        ],
        [whole(a) for a in outs],
        outs,
        [three, one],
        "pick_weights",
        rank=rank,
    )


def pick_rows(arrays, rank):
    rows = arrays[0].shape[1]
    widths = [a.shape[2] for a in arrays]
    count = len(arrays)

    def kernel(r, *refs):
        for k in range(4):

            @pl.when(pl.program_id(0) == k)
            def _():
                at = 0
                for ref, width in zip(refs, widths):
                    refs[count + k][:, at : at + width] = ref[0]
                    at += width

    outs = [shape((rows, sum(widths)))] * 4
    return call(
        kernel,
        (4,),
        [pl.BlockSpec((1, rows, w), lambda k, r: (k ^ r[0], 0, 0)) for w in widths],
        [whole(a) for a in outs],
        outs,
        arrays,
        "pick_rows",
        rank=rank,
    )


def place(parts, rank):
    def kernel(r, *refs):
        for k in range(4):

            @pl.when(pl.program_id(0) == k)
            def _():
                refs[4][0] = refs[k][...]

    rows, columns = parts[0].shape
    return call(
        kernel,
        (4,),
        [whole(p) for p in parts],
        pl.BlockSpec((1, rows, columns), lambda k, r: (k ^ r[0], 0, 0)),
        shape((4, rows, columns)),
        parts,
        "place",
        rank=rank,
    )


def finish_wide(parts, rank):
    rows, total = parts[0].shape
    width = total // 2

    def kernel(r, *refs):
        for k in range(4):

            @pl.when(pl.program_id(0) == k)
            def _():
                refs[4][...] = refs[k][:, :width].astype(F32)
                refs[5][...] = refs[k][:, width:].astype(F32)

    flat = pl.BlockSpec((rows, width), lambda k, r: (0, k ^ r[0]))
    return call(
        kernel,
        (4,),
        [whole(p) for p in parts],
        [flat, flat],
        [shape((rows, 4 * width), F32)] * 2,
        parts,
        "finish_wide",
        rank=rank,
    )


def finish_all(parts, text_grad, rank):
    rows, total = parts[0].shape
    width = total // 6

    def kernel(r, *refs):
        key, value, three, out, cross, cross_out = refs[4:]
        for k in range(4):

            @pl.when(pl.program_id(0) == k)
            def _():
                def part(j):
                    return refs[k][:, j * width : (j + 1) * width].astype(F32)

                for j in range(3):
                    three[j] = part(j)
                out[...] = part(3)
                cross[0] = part(4)
                cross_out[...] = part(5)

        cross[1] = key[...]
        cross[2] = value[...]

    wide = pl.BlockSpec((3, rows, width), lambda k, r: (0, 0, k ^ r[0]))
    flat = pl.BlockSpec((rows, width), lambda k, r: (0, k ^ r[0]))
    return call(
        kernel,
        (4,),
        [whole(p) for p in parts]
        + [flat, pl.BlockSpec((rows, width), lambda k, r: (0, 4 + (k ^ r[0])))],
        [wide, flat, wide, flat],
        [shape((3, rows, 4 * width), F32), shape((rows, 4 * width), F32)] * 2,
        [*parts, text_grad, text_grad],
        "finish_all",
        rank=rank,
    )


def plane_block(k):
    return (k >> 1) & 1, (k >> 2) * 2 + (k & 1)


def text_forward(caption, w_text, w_cross):
    context, rows = caption.shape[0], w_text.shape[0]
    half, width = context // 2, w_cross.shape[2] // 4

    def kernel(cap, weight, cross, own, blocks):
        own[...] = mm_t(cap[...], weight[...]).astype(BF)
        for j in range(2):
            part = mm(own[...], cross[1 + j]).astype(BF)
            for k in range(8):
                core, group = plane_block(k)
                blocks[k, :, j * width : (j + 1) * width] = part[
                    core * half : (core + 1) * half, group * width : (group + 1) * width
                ]

    return call(
        kernel,
        (1,),
        [whole(caption), whole(w_text), whole(w_cross)],
        [
            pl.BlockSpec((context, rows), lambda i: (0, 0)),
            pl.BlockSpec((8, half, 2 * width), lambda i: (0, 0, 0)),
        ],
        [shape((context, rows)), shape((8, half, 2 * width))],
        [caption, w_text, w_cross],
        "text_forward",
    )


def text_back(own_blocks, other_blocks, own_text, w_cross, caption, w_text, core):
    context, rows = own_text.shape
    half, width = context // 2, w_cross.shape[2] // 4
    wide = caption.shape[1] // 4

    def kernel(r, mine, other, own, cross, cap, weight, kv_grad, text_grad, near, far, grads, part):
        spans = [pl.ds(pl.multiple_of((r[0] ^ c) * half, half), half) for c in range(2)]
        for k in range(4):
            for j in range(2):
                at = (4 * j + k) * width
                for c, ref in enumerate((mine, other)):
                    grads[spans[c], at : at + width] = ref[k, :, j * width : (j + 1) * width]
        kv_grad[...] = t_mm(own[...], grads[...])
        grad_text = sum(
            mm_t(grads[:, 4 * j * width : 4 * (j + 1) * width], cross[1 + j]) for j in range(2)
        ).astype(BF)
        text_grad[...] = t_mm(grad_text, cap[...])
        part[...] = mm(grad_text, weight[...]).astype(BF)
        for k in range(4):
            for c, ref in enumerate((near, far)):
                ref[k] = part[spans[c], k * wide : (k + 1) * wide]

    operands = [own_blocks, other_blocks, own_text, w_cross, caption, w_text]
    outs = [
        shape((rows, 8 * width), F32),
        shape((rows, 4 * wide), F32),
        shape((4, half, wide)),
        shape((4, half, wide)),
    ]
    return call(
        kernel,
        (1,),
        [whole(a) for a in operands],
        [whole(a) for a in outs],
        outs,
        operands,
        "text_back",
        rank=core,
        scratch=[pltpu.VMEM((context, 8 * width), BF), pltpu.VMEM((context, 4 * wide), BF)],
    )


def caption_output(own, other, core):
    count, half, wide = own.shape

    def kernel(r, own_ref, other_ref, out):
        block = jnp.where(pl.program_id(0) == r[0], own_ref[0], other_ref[0])
        out[...] = block.astype(F32)

    block = pl.BlockSpec((1, half, wide), lambda i, k, r: (k, 0, 0))
    return call(
        kernel,
        (2, count),
        [block, block],
        pl.BlockSpec((half, wide), lambda i, k, r: (i, k)),
        shape((2 * half, 4 * wide), F32),
        [own, other],
        "caption_output",
        rank=core,
    )


def column_blocks(weight, count):
    rows = weight.shape[0]
    return weight.reshape(rows, count, -1).transpose(1, 0, 2)


def make_local(z_size):
    def sum_z(values):
        parts = values.reshape(z_size, -1, values.shape[-1])
        mine = trade(parts, "z").astype(F32).sum(axis=0).astype(BF)
        return spread(mine, "z", z_size).reshape(values.shape)

    def sum_all(values):
        for axis in ("c", "x", "y"):
            values = values + swap(values, axis)
        step = 1
        while step < z_size:
            values = values + lax.ppermute(
                values, "z", tuple((k, k ^ step) for k in range(z_size))
            )
            step *= 2
        return values

    def layer_order(values):
        shaped = values.reshape(values.shape[:-1] + (z_size, 2, 2, -1))
        return jnp.swapaxes(shaped, -3, -2).reshape(values.shape)

    def local(
        hidden,
        mask_index,
        mask_count,
        mask_embed,
        norm_gains,
        caption,
        w_qkv,
        w_out,
        w_cross,
        w_cross_out,
        w_text,
        w_up,
        w_down,
        cotangent,
    ):
        images, local_rows, width = hidden.shape
        full_length = mask_index.shape[1]
        rank = lax.axis_index("x") * 2 + lax.axis_index("y")
        core = lax.axis_index("c")
        tokens = images * local_rows
        group = width // 4
        text_width = caption.shape[1]

        unit = width // (4 * z_size)
        inside = unit % 128 == 0
        order = [4 * k + j for k in range(z_size) for j in (0, 2, 1, 3)] if inside else None

        def outer(values):
            return values if inside else layer_order(values)

        w_qkv, w_cross = w_qkv.transpose(1, 0, 2), w_cross.transpose(1, 0, 2)
        first = swap_parts(pick_weights(w_qkv, w_out, rank))
        first = gather_rows(place(first, rank))

        positions = lax.axis_index("y") * local_rows + jnp.arange(local_rows, dtype=jnp.int32)
        ranks = jnp.arange(full_length, dtype=jnp.int32)
        matches = (mask_index[:, :, None] == positions[None, None, :]) & (
            ranks[None, :, None] < mask_count[:, None, None]
        )
        masked = jnp.any(matches, axis=1).reshape(tokens, 1).astype(F32)
        gains = layer_order(norm_gains)
        gain_a, gain_b, gain_c = gains[:1], gains[1:2], gains[2:]
        start_x, attn_in, grad_top = start(
            outer(hidden.reshape(tokens, width)),
            outer(cotangent.reshape(tokens, width)),
            masked,
            layer_order(mask_embed)[None],
            gain_a,
            unit,
            order,
        )
        attn_in = gather_tokens(attn_in)
        mid = jnp.concatenate([column_blocks(w_cross[0], 4), column_blocks(w_cross_out, 4)], axis=2)
        up = column_blocks(w_up, 4)
        attn_in, mid, up = lax.optimization_barrier((attn_in, mid, up))
        mid, up = gather_rows(trade(mid)), gather_rows(trade(up))

        own_text, kv_part = text_forward(caption, w_text, w_cross)
        text_kv = trade(kv_part, PLANE).astype(F32).sum(axis=0).astype(BF)
        text_kv = sum_z(text_kv)
        other = swap(text_kv, "c")
        text_kv = jnp.concatenate(
            [jnp.where(core == 0, text_kv, other), jnp.where(core == 0, other, text_kv)], axis=0
        )
        attn_in, text_kv = lax.optimization_barrier((attn_in, text_kv))

        attn_in, projected = gather_mm(attn_in, first, 0, 3 * group, "qkv_mm")
        self_mixed = self_forward(projected, 2 * images)
        down = column_blocks(w_down, 4)
        self_mixed, down = lax.optimization_barrier((self_mixed, down))
        down = gather_rows(trade(down))
        parts = mm_scatter(self_mixed, first[:, 3 * group :])
        after_attn, cross_in = add_norm([start_x] + parts, gain_b)

        cross_in, cross_queries = gather_mm(gather_tokens(cross_in), mid, 0, group, "query_mm")
        cross_mixed = cross_forward(cross_queries, text_kv)
        parts = mm_scatter(cross_mixed, mid[:, group:])
        after_cross, mlp_in = add_norm([after_attn] + parts, gain_c)

        mlp_in = gather_tokens(mlp_in)
        mlp_in, grad_top = lax.optimization_barrier((mlp_in, grad_top))
        grad_y = jnp.concatenate(gather_tokens(grad_top), axis=0)
        mlp_in, activated, slope = feed_up(mlp_in, up)
        early = [attn_in, self_mixed, cross_in, cross_mixed]
        if inside:
            grad_axes, halves = "z", (core, z_size)

            def both(values):
                return [values, swap(values, "c")]

        else:
            grad_axes, halves = DATA, ()

            def both(values):
                return [values]

        early = [both(values) for values in early]
        down_part = grad_products([(both(grad_y), both(activated))], "down_grads", *halves)
        mlp_in = both(mlp_in)
        slope, down_part, early, mlp_in = lax.optimization_barrier((slope, down_part, early, mlp_in))
        down_rows = scatter_grad(down_part, grad_axes)
        grad_pre = feed_down(grad_y, slope, down)
        parts = mm_scatter(grad_pre, up)
        up_part = grad_products([(mlp_in, both(grad_pre))], "up_grads", *halves)
        grad_after_cross, cross_branch, gain_grad_c = norm_back(
            parts, grad_top, after_cross, gain_c
        )

        cross_branch = gather_tokens(cross_branch)
        activated, cross_own = lax.optimization_barrier((activated, cross_branch[0]))
        result = mm_t(activated, down).astype(BF)
        cross_branch, up_part, result = lax.optimization_barrier(
            ((cross_own,) + cross_branch[1:], up_part, result)
        )
        cross_branch, grad_cross_mixed = gather_mm(
            cross_branch, mid, group, group, "cross_out_back"
        )
        grad_cq, kv_grad = cross_back(cross_queries, text_kv, grad_cross_mixed)
        up_part, down_rows, kv_grad = lax.optimization_barrier((up_part, down_rows, kv_grad))
        up_rows = scatter_grad(up_part, grad_axes)
        cross_branch, grad_cq_both = both(cross_branch), both(grad_cq)
        parts = mm_scatter(grad_cq, mid[:, :group])
        grad_after_attn, attn_branch, gain_grad_b = norm_back(
            parts, grad_after_cross, after_attn, gain_b
        )

        attn_branch, result = lax.optimization_barrier((gather_tokens(attn_branch), result))
        result = scatter_first(token_blocks(result))
        attn_branch, grad_self_mixed = gather_mm(attn_branch, first, 3 * group, group, "out_back")
        grad_projected = self_back(projected, grad_self_mixed, 2 * images)
        grad_projected, result = lax.optimization_barrier((grad_projected, result))
        result = scatter_second(result)
        rest_part = grad_products(
            [
                (early[0], both(grad_projected)),
                (both(attn_branch), early[1]),
                (early[2], grad_cq_both),
                (cross_branch, early[3]),
            ],
            "attention_grads",
            *halves,
        )
        grad_projected, result, kv_grad, rest_part = lax.optimization_barrier(
            (grad_projected, result, kv_grad, rest_part)
        )
        rest_part, up_rows = lax.optimization_barrier((rest_part, up_rows))
        rest_rows = scatter_grad(rest_part, grad_axes)
        kv_part = kv_grad.astype(BF).reshape(2, z_size, -1, 2 * group)
        kv_part = kv_part.transpose(1, 0, 2, 3).reshape(2 * z_size, -1, 2 * group)
        kv_part = trade(kv_part, DATA).astype(F32).sum(axis=0).astype(BF)
        kv_part, grad_projected = lax.optimization_barrier((kv_part, grad_projected))
        kv_part = spread(spread(kv_part, "z", z_size).reshape(-1, 2 * group))
        wide_rows = swap_parts(pick_rows([down_rows, up_rows], rank))
        kv_part, wide_rows = lax.optimization_barrier((kv_part, wide_rows))
        kv_weight_grad, grad_text_w, caption_part, caption_far = text_back(
            kv_part, swap(kv_part, "c"), own_text, w_cross, caption, w_text, core
        )
        caption_part = caption_part.astype(F32) + swap(caption_far, "c").astype(F32)
        caption_part = trade(caption_part.astype(BF))
        parts = mm_scatter(grad_projected, first[:, : 3 * group])
        grad_hidden, gain_grad_a, mask_grad = last_back(
            parts, grad_after_attn, start_x, gain_a, masked, unit, order
        )
        sums = jnp.concatenate([gain_grad_a, gain_grad_b, gain_grad_c, mask_grad], axis=0)
        output = layer_output(after_cross, result, unit, order)
        down_grad, up_grad = finish_wide(wide_rows, rank)
        caption_part, sums, output, down_grad, up_grad = lax.optimization_barrier(
            (caption_part, sums, output, down_grad, up_grad)
        )
        caption_part = caption_part.astype(F32).sum(axis=0).astype(BF)
        caption_part = trade(caption_part.reshape(z_size, -1, text_width // 4), "z")
        caption_part = caption_part.astype(F32).sum(axis=0).astype(BF)
        half_context = caption.shape[0] // 2
        caption_part = spread(spread(caption_part, "z", z_size).reshape(half_context, -1))
        caption_part, rest_rows = lax.optimization_barrier((caption_part, rest_rows))
        rest_rows = swap_parts(pick_rows([rest_rows], rank))
        grad_caption = caption_output(caption_part, swap(caption_part, "c"), core)
        sums = layer_order(sum_all(sums))
        qkv_grad, out_grad, grad_cross, cross_out_grad = finish_all(
            rest_rows, kv_weight_grad, rank
        )
        return (
            outer(output).reshape(hidden.shape),
            outer(grad_hidden).reshape(hidden.shape),
            grad_caption,
            sums[:3],
            sums[3],
            qkv_grad.transpose(1, 0, 2),
            out_grad,
            grad_cross.transpose(1, 0, 2),
            cross_out_grad,
            grad_text_w,
            up_grad,
            down_grad,
        )

    return local


def solution(mesh):
    z_size = mesh.shape["img"] // 4
    inner = Mesh(mesh.devices.reshape(z_size, 2, 2, 2), ("z", "x", "c", "y"))
    image = ("z", "x", "c")
    tokens = P(image, "y", None)
    rows = P(image + ("y",))
    in_specs = (tokens, P(image, None), P(image), P(), P(), P()) + (rows,) * 7 + (tokens,)
    out_specs = (tokens, tokens, P(), P(), P()) + (rows,) * 7
    return jax.shard_map(
        make_local(z_size), mesh=inner, in_specs=in_specs, out_specs=out_specs, check_vma=False
    )
```

```python
import math

import jax
import jax.numpy as jnp
from jax import lax
from jax.experimental import pallas as pl
from jax.experimental.pallas import tpu as pltpu
from jax.sharding import Mesh
from jax.sharding import PartitionSpec as P

HD = 128
EPS = 1e-05
BF = jnp.bfloat16
F32 = jnp.float32
PAIR = ((0, 1), (1, 0))
GROUP = ("x", "y")
DATA = ("z", "c")
PLANE = ("x", "c", "y")
VMEM = 48 * 1024 * 1024
SCALE = 1.0 / math.sqrt(HD)
SLOPE = math.sqrt(2.0 / math.pi)
CUBIC = 0.044715


def dot(a, b, dims):
    return lax.dot_general(a, b, (dims, ((), ())), preferred_element_type=F32)


def mm(a, b):
    return dot(a, b, ((1,), (0,)))


def mm_t(a, b):
    return dot(a, b, ((1,), (1,)))


def t_mm(a, b):
    return dot(a, b, ((0,), (0,)))


def shape(dims, dtype=BF):
    return jax.ShapeDtypeStruct(dims, dtype)


def swap(values, axis):
    return lax.ppermute(values, axis, PAIR)


def trade(blocks, axes=GROUP):
    return lax.all_to_all(blocks, axes, 0, 0, tiled=True)


def spread(values, axes=GROUP, count=4):
    return trade(jnp.broadcast_to(values[None], (count,) + values.shape), axes)


def gather_tokens(own):
    half = own.shape[0] // 2
    from_x = swap(own, "x")
    from_y = swap(own, "y")
    return own, from_y, from_x, swap(from_x[:half], "y"), swap(from_y[half:], "x")


def scatter_first(parts):
    own, for_y, for_x, for_low, for_high = parts
    half = for_low.shape[0]
    low = swap(for_low, "y").astype(F32) + for_x[:half].astype(F32)
    high = swap(for_high, "x").astype(F32) + for_y[half:].astype(F32)
    return (
        own,
        jnp.concatenate([low.astype(BF), for_x[half:]], axis=0),
        jnp.concatenate([for_y[:half], high.astype(BF)], axis=0),
    )


def scatter_second(parts):
    own, for_x, for_y = parts
    return [own, swap(for_x, "x"), swap(for_y, "y")]


def scatter_tokens(parts):
    return scatter_second(scatter_first(parts))


def swap_parts(parts):
    return [
        parts[0],
        swap(parts[1], "y"),
        swap(parts[2], "x"),
        lax.ppermute(parts[3], GROUP, ((0, 3), (1, 2), (2, 1), (3, 0))),
    ]


def gather_rows(rows):
    return lax.all_gather(rows.reshape(-1, rows.shape[-1]), DATA, axis=0, tiled=True)


def scatter_grad(partial, axes):
    summed = lax.psum_scatter(partial, axes, scatter_dimension=0, tiled=True)
    return summed.reshape(4, -1, summed.shape[-1])


def call(kernel, grid, in_specs, out_specs, out_shape, operands, name, flops=0, size=1 << 22,
         rank=None, scratch=()):
    options = dict(
        out_shape=out_shape,
        compiler_params=pltpu.CompilerParams(vmem_limit_bytes=VMEM),
        cost_estimate=pl.CostEstimate(flops=flops, bytes_accessed=size, transcendentals=0),
        name=name,
    )
    if rank is None:
        return pl.pallas_call(
            kernel, grid=grid, in_specs=in_specs, out_specs=out_specs, scratch_shapes=scratch,
            **options,
        )(*operands)
    spec = pltpu.PrefetchScalarGridSpec(
        num_scalar_prefetch=1,
        grid=grid,
        in_specs=in_specs,
        out_specs=out_specs,
        scratch_shapes=scratch,
    )
    return pl.pallas_call(kernel, grid_spec=spec, **options)(rank.reshape(1), *operands)


def whole(array):
    return pl.BlockSpec(array.shape, lambda *_: (0,) * len(array.shape))


def reorder(values, unit, order):
    if order is None:
        return values
    return jnp.concatenate([values[:, k * unit : (k + 1) * unit] for k in order], axis=1)


def assemble(target, pieces, sems):
    copies, at = [], 0
    for k, piece in enumerate(pieces):
        rows = piece.shape[0]
        copies.append(pltpu.make_async_copy(piece, target.at[at : at + rows], sems.at[k]))
        at += rows
    for copy in copies:
        copy.start()
    for copy in copies:
        copy.wait()


ANY = pl.BlockSpec(memory_space=pl.ANY)


def gather_mm(pieces, weight, first, columns, name):
    rows, width = pieces[0].shape
    step = 256

    def kernel(*refs):
        tokens, out, sems = refs[6:]

        @pl.when(pl.program_id(0) == 0)
        def _():
            assemble(tokens, refs[:5], sems)

        out[...] = mm(tokens[...], refs[5][...]).astype(BF)

    return call(
        kernel,
        (columns // step,),
        [ANY] * 5 + [pl.BlockSpec((width, step), lambda j: (0, first // step + j))],
        [
            pl.BlockSpec((4 * rows, width), lambda j: (0, 0)),
            pl.BlockSpec((4 * rows, step), lambda j: (0, j)),
        ],
        [shape((4 * rows, width)), shape((4 * rows, columns))],
        [*pieces, weight],
        name,
        flops=8 * rows * width * columns,
        size=2 * width * (columns + 8 * rows),
        scratch=[pltpu.SemaphoreType.DMA((5,))],
    )


def mm_scatter(values, weight):
    return scatter_tokens(token_blocks(mm_t(values, weight).astype(BF)))


def token_blocks(partial):
    rows = partial.shape[0] // 4
    cuts = [0, rows, 2 * rows, 3 * rows, 3 * rows + rows // 2, 4 * rows]
    return [partial[a:b] for a, b in zip(cuts, cuts[1:])]


def normalize(values):
    centred = values - jnp.mean(values, axis=-1, keepdims=True)
    inv_std = lax.rsqrt(jnp.mean(centred * centred, axis=-1, keepdims=True) + EPS)
    return centred * inv_std, inv_std


NORM_ROWS = 32


def row_spec(array, at=None):
    width = array.shape[-1]
    if at is None:
        return pl.BlockSpec((NORM_ROWS, width), lambda i: (i, 0))
    return pl.BlockSpec((1, NORM_ROWS, width), lambda i, at=at: (at, i, 0))


def terms_of(terms):
    arrays, specs = [], []
    for term in terms:
        array, at = term if isinstance(term, tuple) else (term, None)
        arrays.append(array)
        specs.append(row_spec(array, at))
    return arrays, specs


def total_of(refs):
    values = [ref[0] if len(ref.shape) == 3 else ref[...] for ref in refs]
    return sum(value.astype(F32) for value in values)


def add_norm(terms, gain):
    arrays, specs = terms_of(terms)
    tokens, width = arrays[0].shape[-2], arrays[0].shape[-1]
    tokens = min(a.shape[-2] for a in arrays)

    def kernel(*refs):
        gain_ref, x, out = refs[-3:]
        values = total_of(refs[:-3])
        x[...] = values
        out[...] = (normalize(values)[0] * gain_ref[...]).astype(BF)

    return call(
        kernel,
        (tokens // NORM_ROWS,),
        specs + [whole(gain)],
        [row_spec(shape((tokens, width)))] * 2,
        [shape((tokens, width), F32), shape((tokens, width))],
        [*arrays, gain],
        "add_norm",
    )


def norm_grad(grad, values, gain):
    normed, inv_std = normalize(values)
    scaled = grad * gain
    first_mean = jnp.mean(scaled, axis=-1, keepdims=True)
    second_mean = jnp.mean(scaled * normed, axis=-1, keepdims=True)
    return (
        inv_std * (scaled - first_mean - normed * second_mean),
        jnp.sum(grad * normed, axis=0, keepdims=True),
    )


def accumulate(ref, value):
    @pl.when(pl.program_id(0) == 0)
    def _():
        ref[...] = jnp.zeros_like(ref)

    ref[...] += value


def norm_back(terms, upper, values, gain):
    arrays, specs = terms_of(terms)
    tokens, width = values.shape

    def kernel(*refs):
        upper_ref, x, gain_ref, out, out_low, gain_grad = refs[-6:]
        back, part = norm_grad(total_of(refs[:-6]), x[...], gain_ref[...])
        result = upper_ref[...].astype(F32) + back
        out[...] = result
        out_low[...] = result.astype(BF)
        accumulate(gain_grad, part)

    return call(
        kernel,
        (tokens // NORM_ROWS,),
        specs + [row_spec(upper), row_spec(values), whole(gain)],
        [row_spec(values)] * 2 + [pl.BlockSpec((1, width), lambda i: (0, 0))],
        [shape((tokens, width), F32), shape((tokens, width)), shape((1, width), F32)],
        [*arrays, upper, values, gain],
        "norm_back",
    )


def last_back(terms, upper, values, gain, masked, unit, order):
    arrays, specs = terms_of(terms)
    tokens, width = values.shape

    def kernel(*refs):
        upper_ref, x, gain_ref, mask, out, gain_grad, mask_grad = refs[-7:]
        back, part = norm_grad(total_of(refs[:-7]), x[...], gain_ref[...])
        result = upper_ref[...].astype(F32) + back
        hit = mask[...] > 0.5
        out[...] = reorder(jnp.where(hit, 0.0, result).astype(BF), unit, order)
        accumulate(gain_grad, part)
        accumulate(mask_grad, jnp.sum(jnp.where(hit, result, 0.0), axis=0, keepdims=True))

    line = pl.BlockSpec((1, width), lambda i: (0, 0))
    return call(
        kernel,
        (tokens // NORM_ROWS,),
        specs + [row_spec(upper), row_spec(values), whole(gain), row_spec(masked)],
        [row_spec(values), line, line],
        [shape((tokens, width)), shape((1, width), F32), shape((1, width), F32)],
        [*arrays, upper, values, gain, masked],
        "last_back",
    )


def start(hidden, cotangent, masked, embed, gain, unit, order):
    tokens, width = hidden.shape

    def kernel(hid, cot, mask, embed_ref, gain_ref, x, out, grad):
        hit = mask[...] > 0.5
        values = jnp.where(
            hit, embed_ref[...], reorder(hid[...], unit, order).astype(F32)
        )
        x[...] = values
        out[...] = (normalize(values)[0] * gain_ref[...]).astype(BF)
        grad[...] = jnp.where(hit, reorder(cot[...], unit, order).astype(F32), 0.0).astype(BF)

    rows = row_spec(hidden)
    return call(
        kernel,
        (tokens // NORM_ROWS,),
        [rows, rows, row_spec(masked), whole(embed), whole(gain)],
        [rows] * 3,
        [shape((tokens, width), F32), shape((tokens, width)), shape((tokens, width))],
        [hidden, cotangent, masked, embed, gain],
        "start",
    )


def layer_output(upper, terms, unit, order):
    arrays, specs = terms_of(terms)
    tokens, width = upper.shape

    def kernel(*refs):
        values = refs[-2][...] + total_of(refs[:-2])
        refs[-1][...] = reorder(values.astype(BF), unit, order)

    return call(
        kernel,
        (tokens // NORM_ROWS,),
        specs + [row_spec(upper)],
        row_spec(upper),
        shape((tokens, width)),
        [*arrays, upper],
        "layer_output",
    )


def feed_up(pieces, weight):
    rows, width = pieces[0].shape
    hidden = weight.shape[1]
    step = 256

    def kernel(*refs):
        up, tokens, act, slope, sems = refs[5:]

        @pl.when(pl.program_id(0) == 0)
        def _():
            assemble(tokens, refs[:5], sems)

        u = mm(tokens[...], up[...])
        square = u * u
        bend = jnp.tanh(SLOPE * u * (1.0 + CUBIC * square))
        half = 0.5 * (1.0 + bend)
        act[...] = (u * half).astype(BF)
        slope[...] = half + 0.5 * u * (1.0 - bend * bend) * SLOPE * (1.0 + 3.0 * CUBIC * square)

    part = pl.BlockSpec((4 * rows, step), lambda j: (0, j))
    return call(
        kernel,
        (hidden // step,),
        [ANY] * 5 + [pl.BlockSpec((width, step), lambda j: (0, j))],
        [pl.BlockSpec((4 * rows, width), lambda j: (0, 0)), part, part],
        [shape((4 * rows, width)), shape((4 * rows, hidden)), shape((4 * rows, hidden), F32)],
        [*pieces, weight],
        "feed_up",
        scratch=[pltpu.SemaphoreType.DMA((5,))],
        flops=8 * rows * width * hidden,
        size=2 * width * (hidden + 8 * rows),
    )


def feed_down(grad_y, slope, weight):
    tokens, width = grad_y.shape
    hidden = weight.shape[1]
    step = 256

    def kernel(dy, slope_ref, down, out):
        out[...] = (mm(dy[...], down[...]) * slope_ref[...]).astype(BF)

    part = pl.BlockSpec((tokens, step), lambda j: (0, j))
    return call(
        kernel,
        (hidden // step,),
        [whole(grad_y), part, pl.BlockSpec((width, step), lambda j: (0, j))],
        part,
        shape((tokens, hidden)),
        [grad_y, slope, weight],
        "feed_down",
        flops=2 * tokens * width * hidden,
        size=2 * width * (hidden + 8 * tokens),
    )


def softmax(scores):
    exp_terms = jnp.exp(scores - jnp.max(scores, axis=-1, keepdims=True))
    return exp_terms / jnp.sum(exp_terms, axis=-1, keepdims=True)


def score_grad(probs, grad_probs):
    return (
        probs * (grad_probs - jnp.sum(probs * grad_probs, axis=-1, keepdims=True))
    ).astype(BF)


def head(ref, k):
    return ref[:, k * HD : (k + 1) * HD]


def self_forward(projected, images):
    tokens, width = projected.shape
    rows, group = tokens // images, width // 3
    heads = group // HD

    def kernel(proj, mixed):
        for k in range(heads):
            query, key, value = (head(proj, j * heads + k) for j in range(3))
            probs = softmax(mm_t(query, key) * SCALE).astype(BF)
            mixed[:, k * HD : (k + 1) * HD] = mm(probs, value).astype(BF)

    return call(
        kernel,
        (images,),
        [pl.BlockSpec((rows, width), lambda i: (i, 0))],
        pl.BlockSpec((rows, group), lambda i: (i, 0)),
        shape((tokens, group)),
        [projected],
        "self_forward",
        flops=4 * tokens * rows * group,
    )


def self_back(projected, grad_mixed, images):
    tokens, width = projected.shape
    rows, group = tokens // images, width // 3
    heads = group // HD

    def kernel(proj, grad, out):
        for k in range(heads):
            query, key, value = (head(proj, j * heads + k) for j in range(3))
            grad_head = head(grad, k)
            probs = softmax(mm_t(query, key) * SCALE)
            grad_scores = score_grad(probs, mm_t(grad_head, value))
            parts = (
                mm(grad_scores, key) * SCALE,
                t_mm(grad_scores, query) * SCALE,
                t_mm(probs.astype(BF), grad_head),
            )
            for j, part in enumerate(parts):
                at = (j * heads + k) * HD
                out[:, at : at + HD] = part.astype(BF)

    return call(
        kernel,
        (images,),
        [
            pl.BlockSpec((rows, width), lambda i: (i, 0)),
            pl.BlockSpec((rows, group), lambda i: (i, 0)),
        ],
        pl.BlockSpec((rows, width), lambda i: (i, 0)),
        shape((tokens, width)),
        [projected, grad_mixed],
        "self_back",
        flops=10 * tokens * rows * group,
    )


def cross_forward(queries, text_kv):
    tokens, group = queries.shape
    heads = group // HD

    def kernel(query, text, mixed):
        for k in range(heads):
            probs = softmax(mm_t(head(query, k), head(text, k)) * SCALE).astype(BF)
            mixed[:, k * HD : (k + 1) * HD] = mm(probs, head(text, heads + k)).astype(BF)

    return call(
        kernel,
        (1,),
        [whole(queries), whole(text_kv)],
        whole(queries),
        shape((tokens, group)),
        [queries, text_kv],
        "cross_forward",
        flops=4 * tokens * text_kv.shape[0] * group,
    )


def cross_back(queries, text_kv, grad_mixed):
    tokens, group = queries.shape
    context = text_kv.shape[0]
    heads = group // HD

    def kernel(query, text, grad, grad_query, grad_text):
        for k in range(heads):
            query_head, key, value = head(query, k), head(text, k), head(text, heads + k)
            grad_head = head(grad, k)
            probs = softmax(mm_t(query_head, key) * SCALE)
            grad_scores = score_grad(probs, mm_t(grad_head, value))
            grad_query[:, k * HD : (k + 1) * HD] = (mm(grad_scores, key) * SCALE).astype(BF)
            at = (heads + k) * HD
            grad_text[:, k * HD : (k + 1) * HD] = t_mm(grad_scores, query_head) * SCALE
            grad_text[:, at : at + HD] = t_mm(probs.astype(BF), grad_head)

    return call(
        kernel,
        (1,),
        [whole(queries), whole(text_kv), whole(grad_mixed)],
        [whole(queries), whole(text_kv)],
        [shape((tokens, group)), shape((context, 2 * group), F32)],
        [queries, text_kv, grad_mixed],
        "cross_back",
        flops=10 * tokens * context * group,
    )


def grad_products(pairs, name, core=None, blocks=0):
    count_in = len(pairs[0][0])
    tokens, width = pairs[0][0][0].shape
    widths = [y[0].shape[1] for _, y in pairs]
    total = sum(widths)
    rows = 256 if core is None else width // (2 * blocks)
    steps = width // rows if core is None else blocks
    step = 512
    count = len(pairs) * count_in

    def kernel(r, *refs):
        out = refs[2 * count]
        offset = 0
        for k, wide in enumerate(widths):
            left = [refs[k * count_in + b][...].T for b in range(count_in)]
            for at in range(0, wide, step):
                out[:, offset + at : offset + at + step] = sum(
                    mm(left[b], refs[count + k * count_in + b][:, at : at + step])
                    for b in range(count_in)
                ).astype(BF)
            offset += wide

    pick = (lambda i, r: (0, i)) if core is None else (lambda i, r: (0, 2 * i + r[0]))
    return call(
        kernel,
        (steps,),
        [pl.BlockSpec((tokens, rows), pick)] * count
        + [pl.BlockSpec((tokens, w), lambda i, r: (0, 0)) for w in widths for _ in range(count_in)],
        pl.BlockSpec((rows, total), lambda i, r: (i, 0)),
        shape((steps * rows, total)),
        [b for x, _ in pairs for b in x] + [b for _, y in pairs for b in y],
        name,
        flops=2 * tokens * count_in * steps * rows * total,
        size=4 * width * total,
        rank=jnp.zeros((), jnp.int32) if core is None else core,
    )


def pick_weights(three, one, rank):
    rows, width = one.shape[0], one.shape[1] // 4

    def kernel(r, three_ref, one_ref, *outs):
        for k in range(4):

            @pl.when(pl.program_id(0) == k)
            def _():
                for j in range(3):
                    outs[k][:, j * width : (j + 1) * width] = three_ref[j]
                outs[k][:, 3 * width :] = one_ref[...]

    outs = [shape((rows, 4 * width))] * 4
    return call(
        kernel,
        (4,),
        [
            pl.BlockSpec((3, rows, width), lambda k, r: (0, 0, k ^ r[0])),
            pl.BlockSpec((rows, width), lambda k, r: (0, k ^ r[0])),
        ],
        [whole(a) for a in outs],
        outs,
        [three, one],
        "pick_weights",
        rank=rank,
    )


def pick_rows(arrays, rank):
    rows = arrays[0].shape[1]
    widths = [a.shape[2] for a in arrays]
    count = len(arrays)

    def kernel(r, *refs):
        for k in range(4):

            @pl.when(pl.program_id(0) == k)
            def _():
                at = 0
                for ref, width in zip(refs, widths):
                    refs[count + k][:, at : at + width] = ref[0]
                    at += width

    outs = [shape((rows, sum(widths)))] * 4
    return call(
        kernel,
        (4,),
        [pl.BlockSpec((1, rows, w), lambda k, r: (k ^ r[0], 0, 0)) for w in widths],
        [whole(a) for a in outs],
        outs,
        arrays,
        "pick_rows",
        rank=rank,
    )


def place(parts, rank):
    def kernel(r, *refs):
        for k in range(4):

            @pl.when(pl.program_id(0) == k)
            def _():
                refs[4][0] = refs[k][...]

    rows, columns = parts[0].shape
    return call(
        kernel,
        (4,),
        [whole(p) for p in parts],
        pl.BlockSpec((1, rows, columns), lambda k, r: (k ^ r[0], 0, 0)),
        shape((4, rows, columns)),
        parts,
        "place",
        rank=rank,
    )


def finish_wide(parts, rank):
    rows, total = parts[0].shape
    width = total // 2

    def kernel(r, *refs):
        for k in range(4):

            @pl.when(pl.program_id(0) == k)
            def _():
                refs[4][...] = refs[k][:, :width].astype(F32)
                refs[5][...] = refs[k][:, width:].astype(F32)

    flat = pl.BlockSpec((rows, width), lambda k, r: (0, k ^ r[0]))
    return call(
        kernel,
        (4,),
        [whole(p) for p in parts],
        [flat, flat],
        [shape((rows, 4 * width), F32)] * 2,
        parts,
        "finish_wide",
        rank=rank,
    )


def finish_all(parts, text_grad, rank):
    rows, total = parts[0].shape
    width = total // 6

    def kernel(r, *refs):
        key, value, three, out, cross, cross_out = refs[4:]
        for k in range(4):

            @pl.when(pl.program_id(0) == k)
            def _():
                def part(j):
                    return refs[k][:, j * width : (j + 1) * width].astype(F32)

                for j in range(3):
                    three[j] = part(j)
                out[...] = part(3)
                cross[0] = part(4)
                cross_out[...] = part(5)

        cross[1] = key[...]
        cross[2] = value[...]

    wide = pl.BlockSpec((3, rows, width), lambda k, r: (0, 0, k ^ r[0]))
    flat = pl.BlockSpec((rows, width), lambda k, r: (0, k ^ r[0]))
    return call(
        kernel,
        (4,),
        [whole(p) for p in parts]
        + [flat, pl.BlockSpec((rows, width), lambda k, r: (0, 4 + (k ^ r[0])))],
        [wide, flat, wide, flat],
        [shape((3, rows, 4 * width), F32), shape((rows, 4 * width), F32)] * 2,
        [*parts, text_grad, text_grad],
        "finish_all",
        rank=rank,
    )


def plane_block(k):
    return (k >> 1) & 1, (k >> 2) * 2 + (k & 1)


def text_forward(caption, w_text, w_cross):
    context, rows = caption.shape[0], w_text.shape[0]
    half, width = context // 2, w_cross.shape[2] // 4

    def kernel(cap, weight, cross, own, blocks):
        own[...] = mm_t(cap[...], weight[...]).astype(BF)
        for j in range(2):
            part = mm(own[...], cross[1 + j]).astype(BF)
            for k in range(8):
                core, group = plane_block(k)
                blocks[k, :, j * width : (j + 1) * width] = part[
                    core * half : (core + 1) * half, group * width : (group + 1) * width
                ]

    return call(
        kernel,
        (1,),
        [whole(caption), whole(w_text), whole(w_cross)],
        [
            pl.BlockSpec((context, rows), lambda i: (0, 0)),
            pl.BlockSpec((8, half, 2 * width), lambda i: (0, 0, 0)),
        ],
        [shape((context, rows)), shape((8, half, 2 * width))],
        [caption, w_text, w_cross],
        "text_forward",
    )


def text_back(blocks, own_text, w_cross, caption, w_text, extra):
    context, rows = own_text.shape
    half, width = context // 2, w_cross.shape[2] // 4
    wide = caption.shape[1] // 4
    tail = extra.shape[0]

    def kernel(block, own, cross, cap, weight, more, kv_grad, text_grad, out, grads):
        for k in range(8):
            core, group = plane_block(k)
            for j in range(2):
                at = (4 * j + group) * width
                grads[core * half : (core + 1) * half, at : at + width] = block[
                    k, :, j * width : (j + 1) * width
                ]
        kv_grad[...] = t_mm(own[...], grads[...])
        grad_text = sum(
            mm_t(grads[:, 4 * j * width : 4 * (j + 1) * width], cross[1 + j]) for j in range(2)
        ).astype(BF)
        text_grad[...] = t_mm(grad_text, cap[...])
        part = mm(grad_text, weight[...]).astype(BF)
        for k in range(8):
            core, group = plane_block(k)
            out[k, :half, :] = part[core * half : (core + 1) * half, group * wide : (group + 1) * wide]
            out[k, half:, :] = more[...]

    operands = [blocks, own_text, w_cross, caption, w_text, extra]
    outs = [
        shape((rows, 8 * width), F32),
        shape((rows, 4 * wide), F32),
        shape((8, half + tail, wide)),
    ]
    return call(
        kernel,
        (1,),
        [whole(a) for a in operands],
        [whole(a) for a in outs],
        outs,
        operands,
        "text_back",
        scratch=[pltpu.VMEM((context, 8 * width), BF)],
    )


def caption_output(own, other, core):
    count, half, wide = own.shape

    def kernel(r, own_ref, other_ref, out):
        block = jnp.where(pl.program_id(0) == r[0], own_ref[0], other_ref[0])
        out[...] = block.astype(F32)

    block = pl.BlockSpec((1, half, wide), lambda i, k, r: (k, 0, 0))
    return call(
        kernel,
        (2, count),
        [block, block],
        pl.BlockSpec((half, wide), lambda i, k, r: (i, k)),
        shape((2 * half, 4 * wide), F32),
        [own, other],
        "caption_output",
        rank=core,
    )


def column_blocks(weight, count):
    rows = weight.shape[0]
    return weight.reshape(rows, count, -1).transpose(1, 0, 2)


def halves_of(values, width):
    high = values.astype(BF)
    low = (values - high.astype(F32)).astype(BF)
    return jnp.concatenate([high.reshape(-1, width), low.reshape(-1, width)], axis=0)


def whole_of(halves, width):
    rows = halves.shape[0] // 2
    return (halves[:rows] + halves[rows:]).reshape(-1, width)


def make_local(z_size):
    def sum_z(values):
        parts = values.reshape(z_size, -1, values.shape[-1])
        mine = trade(parts, "z").astype(F32).sum(axis=0).astype(BF)
        return spread(mine, "z", z_size).reshape(values.shape)

    def add_z(values):
        step = 1
        while step < z_size:
            values = values + lax.ppermute(
                values, "z", tuple((k, k ^ step) for k in range(z_size))
            )
            step *= 2
        return values

    def layer_order(values):
        shaped = values.reshape(values.shape[:-1] + (z_size, 2, 2, -1))
        return jnp.swapaxes(shaped, -3, -2).reshape(values.shape)

    def local(
        hidden,
        mask_index,
        mask_count,
        mask_embed,
        norm_gains,
        caption,
        w_qkv,
        w_out,
        w_cross,
        w_cross_out,
        w_text,
        w_up,
        w_down,
        cotangent,
    ):
        images, local_rows, width = hidden.shape
        full_length = mask_index.shape[1]
        rank = lax.axis_index("x") * 2 + lax.axis_index("y")
        core = lax.axis_index("c")
        tokens = images * local_rows
        group = width // 4
        text_width = caption.shape[1]

        unit = width // (4 * z_size)
        inside = unit % 128 == 0
        order = [4 * k + j for k in range(z_size) for j in (0, 2, 1, 3)] if inside else None

        def outer(values):
            return values if inside else layer_order(values)

        w_qkv, w_cross = w_qkv.transpose(1, 0, 2), w_cross.transpose(1, 0, 2)
        first = swap_parts(pick_weights(w_qkv, w_out, rank))
        first = gather_rows(place(first, rank))

        positions = lax.axis_index("y") * local_rows + jnp.arange(local_rows, dtype=jnp.int32)
        ranks = jnp.arange(full_length, dtype=jnp.int32)
        matches = (mask_index[:, :, None] == positions[None, None, :]) & (
            ranks[None, :, None] < mask_count[:, None, None]
        )
        masked = jnp.any(matches, axis=1).reshape(tokens, 1).astype(F32)
        gains = layer_order(norm_gains)
        gain_a, gain_b, gain_c = gains[:1], gains[1:2], gains[2:]
        start_x, attn_in, grad_top = start(
            outer(hidden.reshape(tokens, width)),
            outer(cotangent.reshape(tokens, width)),
            masked,
            layer_order(mask_embed)[None],
            gain_a,
            unit,
            order,
        )
        attn_in = gather_tokens(attn_in)
        mid = jnp.concatenate([column_blocks(w_cross[0], 4), column_blocks(w_cross_out, 4)], axis=2)
        up = column_blocks(w_up, 4)
        attn_in, mid, up = lax.optimization_barrier((attn_in, mid, up))
        mid, up = gather_rows(trade(mid)), gather_rows(trade(up))

        own_text, kv_part = text_forward(caption, w_text, w_cross)
        text_kv = trade(kv_part, PLANE).astype(F32).sum(axis=0).astype(BF)
        text_kv = sum_z(text_kv)
        other = swap(text_kv, "c")
        text_kv = jnp.concatenate(
            [jnp.where(core == 0, text_kv, other), jnp.where(core == 0, other, text_kv)], axis=0
        )
        attn_in, text_kv = lax.optimization_barrier((attn_in, text_kv))

        attn_in, projected = gather_mm(attn_in, first, 0, 3 * group, "qkv_mm")
        self_mixed = self_forward(projected, 2 * images)
        down = column_blocks(w_down, 4)
        self_mixed, down = lax.optimization_barrier((self_mixed, down))
        down = gather_rows(trade(down))
        parts = mm_scatter(self_mixed, first[:, 3 * group :])
        after_attn, cross_in = add_norm([start_x] + parts, gain_b)

        cross_in, cross_queries = gather_mm(gather_tokens(cross_in), mid, 0, group, "query_mm")
        cross_mixed = cross_forward(cross_queries, text_kv)
        parts = mm_scatter(cross_mixed, mid[:, group:])
        after_cross, mlp_in = add_norm([after_attn] + parts, gain_c)

        mlp_in = gather_tokens(mlp_in)
        mlp_in, grad_top = lax.optimization_barrier((mlp_in, grad_top))
        grad_y = jnp.concatenate(gather_tokens(grad_top), axis=0)
        mlp_in, activated, slope = feed_up(mlp_in, up)
        early = [attn_in, self_mixed, cross_in, cross_mixed]
        if inside:
            grad_axes, halves = "z", (core, z_size)

            def both(values):
                return [values, swap(values, "c")]

        else:
            grad_axes, halves = DATA, ()

            def both(values):
                return [values]

        early = [both(values) for values in early]
        down_part = grad_products([(both(grad_y), both(activated))], "down_grads", *halves)
        mlp_in = both(mlp_in)
        slope, down_part, early, mlp_in = lax.optimization_barrier((slope, down_part, early, mlp_in))
        down_rows = scatter_grad(down_part, grad_axes)
        grad_pre = feed_down(grad_y, slope, down)
        parts = mm_scatter(grad_pre, up)
        up_part = grad_products([(mlp_in, both(grad_pre))], "up_grads", *halves)
        grad_after_cross, cross_branch, gain_grad_c = norm_back(
            parts, grad_top, after_cross, gain_c
        )

        cross_branch = gather_tokens(cross_branch)
        activated, cross_own = lax.optimization_barrier((activated, cross_branch[0]))
        result = mm_t(activated, down).astype(BF)
        cross_branch, up_part, result = lax.optimization_barrier(
            ((cross_own,) + cross_branch[1:], up_part, result)
        )
        cross_branch, grad_cross_mixed = gather_mm(
            cross_branch, mid, group, group, "cross_out_back"
        )
        grad_cq, kv_grad = cross_back(cross_queries, text_kv, grad_cross_mixed)
        up_part, down_rows, kv_grad = lax.optimization_barrier((up_part, down_rows, kv_grad))
        up_rows = scatter_grad(up_part, grad_axes)
        cross_branch, grad_cq_both = both(cross_branch), both(grad_cq)
        parts = mm_scatter(grad_cq, mid[:, :group])
        grad_after_attn, attn_branch, gain_grad_b = norm_back(
            parts, grad_after_cross, after_attn, gain_b
        )

        attn_branch, result = lax.optimization_barrier((gather_tokens(attn_branch), result))
        result = scatter_first(token_blocks(result))
        attn_branch, grad_self_mixed = gather_mm(attn_branch, first, 3 * group, group, "out_back")
        grad_projected = self_back(projected, grad_self_mixed, 2 * images)
        kv_part = kv_grad.astype(BF).reshape(2, z_size, -1, 2 * group)
        kv_part = kv_part.transpose(1, 0, 2, 3).reshape(2 * z_size, -1, 2 * group)
        grad_projected, result, kv_part = lax.optimization_barrier(
            (grad_projected, result, kv_part)
        )
        kv_part = trade(kv_part, DATA)
        result = scatter_second(result)
        rest_part = grad_products(
            [
                (early[0], both(grad_projected)),
                (both(attn_branch), early[1]),
                (early[2], grad_cq_both),
                (cross_branch, early[3]),
            ],
            "attention_grads",
            *halves,
        )
        grad_projected, result, kv_part, rest_part = lax.optimization_barrier(
            (grad_projected, result, kv_part, rest_part)
        )
        rest_part, up_rows = lax.optimization_barrier((rest_part, up_rows))
        rest_rows = scatter_grad(rest_part, grad_axes)
        parts = mm_scatter(grad_projected, first[:, : 3 * group])
        grad_hidden, gain_grad_a, mask_grad = last_back(
            parts,
            grad_after_attn,
            start_x,
            gain_a,
            masked,
            unit,
            order,
        )
        sums = jnp.concatenate([gain_grad_a, gain_grad_b, gain_grad_c, mask_grad], axis=0)


        kv_part = kv_part.astype(F32).sum(axis=0).astype(BF)
        kv_sum = spread(kv_part, "z", z_size).reshape(-1, 2 * group)
        wide_rows = swap_parts(pick_rows([down_rows, up_rows], rank))
        kv_grads = spread(kv_sum, PLANE, 8)
        kv_grads, wide_rows = lax.optimization_barrier((kv_grads, wide_rows))
        kv_weight_grad, grad_text_w, caption_part = text_back(
            kv_grads, own_text, w_cross, caption, w_text, halves_of(sums, text_width // 4)
        )
        half_context = caption.shape[0] // 2
        caption_part = trade(caption_part, PLANE)
        output = layer_output(after_cross, result, unit, order)
        down_grad, up_grad = finish_wide(wide_rows, rank)
        caption_part, output, down_grad, up_grad = lax.optimization_barrier(
            (caption_part, output, down_grad, up_grad)
        )
        caption_part = caption_part.astype(F32).sum(axis=0)
        sums = layer_order(add_z(whole_of(caption_part[half_context:], width)))
        caption_part = caption_part[:half_context].astype(BF).reshape(z_size, -1, text_width // 4)
        caption_part = trade(caption_part, "z").astype(F32).sum(axis=0).astype(BF)
        caption_part = spread(caption_part, "z", z_size).reshape(half_context, -1)
        caption_part = spread(caption_part)
        caption_part, rest_rows = lax.optimization_barrier((caption_part, rest_rows))
        grad_caption = caption_output(caption_part, swap(caption_part, "c"), core)
        rest_rows = swap_parts(pick_rows([rest_rows], rank))
        qkv_grad, out_grad, grad_cross, cross_out_grad = finish_all(
            rest_rows, kv_weight_grad, rank
        )
        return (
            outer(output).reshape(hidden.shape),
            outer(grad_hidden).reshape(hidden.shape),
            grad_caption,
            sums[:3],
            sums[3],
            qkv_grad.transpose(1, 0, 2),
            out_grad,
            grad_cross.transpose(1, 0, 2),
            cross_out_grad,
            grad_text_w,
            up_grad,
            down_grad,
        )

    return local


def solution(mesh):
    z_size = mesh.shape["img"] // 4
    inner = Mesh(mesh.devices.reshape(z_size, 2, 2, 2), ("z", "x", "c", "y"))
    image = ("z", "x", "c")
    tokens = P(image, "y", None)
    rows = P(image + ("y",))
    in_specs = (tokens, P(image, None), P(image), P(), P(), P()) + (rows,) * 7 + (tokens,)
    out_specs = (tokens, tokens, P(), P(), P()) + (rows,) * 7
    return jax.shard_map(
        make_local(z_size), mesh=inner, in_specs=in_specs, out_specs=out_specs, check_vma=False
    )
```

```python
import math

import jax
import jax.numpy as jnp
from jax import lax
from jax.experimental import pallas as pl
from jax.experimental.pallas import tpu as pltpu
from jax.sharding import Mesh
from jax.sharding import PartitionSpec as P

HD = 128
EPS = 1e-05
BF = jnp.bfloat16
F32 = jnp.float32
PAIR = ((0, 1), (1, 0))
GROUP = ("x", "y")
DATA = ("z", "c")
PLANE = ("x", "c", "y")
VMEM = 48 * 1024 * 1024
SCALE = 1.0 / math.sqrt(HD)
SLOPE = math.sqrt(2.0 / math.pi)
CUBIC = 0.044715


def dot(a, b, dims):
    return lax.dot_general(a, b, (dims, ((), ())), preferred_element_type=F32)


def mm(a, b):
    return dot(a, b, ((1,), (0,)))


def mm_t(a, b):
    return dot(a, b, ((1,), (1,)))


def t_mm(a, b):
    return dot(a, b, ((0,), (0,)))


def shape(dims, dtype=BF):
    return jax.ShapeDtypeStruct(dims, dtype)


def swap(values, axis):
    return lax.ppermute(values, axis, PAIR)


def trade(blocks, axes=GROUP):
    return lax.all_to_all(blocks, axes, 0, 0, tiled=True)


def spread(values, axes=GROUP, count=4):
    return trade(jnp.broadcast_to(values[None], (count,) + values.shape), axes)


def gather_tokens(own):
    half = own.shape[0] // 2
    from_x = swap(own, "x")
    from_y = swap(own, "y")
    return own, from_y, from_x, swap(from_x[:half], "y"), swap(from_y[half:], "x")


def scatter_first(parts):
    own, for_y, for_x, for_low, for_high = parts
    half = for_low.shape[0]
    low = swap(for_low, "y").astype(F32) + for_x[:half].astype(F32)
    high = swap(for_high, "x").astype(F32) + for_y[half:].astype(F32)
    return (
        own,
        jnp.concatenate([low.astype(BF), for_x[half:]], axis=0),
        jnp.concatenate([for_y[:half], high.astype(BF)], axis=0),
    )


def scatter_second(parts):
    own, for_x, for_y = parts
    return [own, swap(for_x, "x"), swap(for_y, "y")]


def scatter_tokens(parts):
    return scatter_second(scatter_first(parts))


def swap_parts(parts):
    return [
        parts[0],
        swap(parts[1], "y"),
        swap(parts[2], "x"),
        lax.ppermute(parts[3], GROUP, ((0, 3), (1, 2), (2, 1), (3, 0))),
    ]


def gather_rows(rows):
    return lax.all_gather(rows.reshape(-1, rows.shape[-1]), DATA, axis=0, tiled=True)


def scatter_grad(partial, axes):
    summed = lax.psum_scatter(partial, axes, scatter_dimension=0, tiled=True)
    return summed.reshape(4, -1, summed.shape[-1])


def call(kernel, grid, in_specs, out_specs, out_shape, operands, name, flops=0, size=1 << 22,
         rank=None, scratch=()):
    options = dict(
        out_shape=out_shape,
        compiler_params=pltpu.CompilerParams(vmem_limit_bytes=VMEM),
        cost_estimate=pl.CostEstimate(flops=flops, bytes_accessed=size, transcendentals=0),
        name=name,
    )
    if rank is None:
        return pl.pallas_call(
            kernel, grid=grid, in_specs=in_specs, out_specs=out_specs, scratch_shapes=scratch,
            **options,
        )(*operands)
    spec = pltpu.PrefetchScalarGridSpec(
        num_scalar_prefetch=1,
        grid=grid,
        in_specs=in_specs,
        out_specs=out_specs,
        scratch_shapes=scratch,
    )
    return pl.pallas_call(kernel, grid_spec=spec, **options)(rank.reshape(1), *operands)


def whole(array):
    return pl.BlockSpec(array.shape, lambda *_: (0,) * len(array.shape))


def reorder(values, unit, order):
    if order is None:
        return values
    return jnp.concatenate([values[:, k * unit : (k + 1) * unit] for k in order], axis=1)


def assemble(target, pieces, sems):
    copies, at = [], 0
    for k, piece in enumerate(pieces):
        rows = piece.shape[0]
        copies.append(pltpu.make_async_copy(piece, target.at[at : at + rows], sems.at[k]))
        at += rows
    for copy in copies:
        copy.start()
    for copy in copies:
        copy.wait()


ANY = pl.BlockSpec(memory_space=pl.ANY)


def gather_mm(pieces, weight, first, columns, name):
    rows, width = pieces[0].shape
    step = 256

    def kernel(*refs):
        tokens, out, sems = refs[6:]

        @pl.when(pl.program_id(0) == 0)
        def _():
            assemble(tokens, refs[:5], sems)

        out[...] = mm(tokens[...], refs[5][...]).astype(BF)

    return call(
        kernel,
        (columns // step,),
        [ANY] * 5 + [pl.BlockSpec((width, step), lambda j: (0, first // step + j))],
        [
            pl.BlockSpec((4 * rows, width), lambda j: (0, 0)),
            pl.BlockSpec((4 * rows, step), lambda j: (0, j)),
        ],
        [shape((4 * rows, width)), shape((4 * rows, columns))],
        [*pieces, weight],
        name,
        flops=8 * rows * width * columns,
        size=2 * width * (columns + 8 * rows),
        scratch=[pltpu.SemaphoreType.DMA((5,))],
    )


def mm_scatter(values, weight):
    return scatter_tokens(token_blocks(mm_t(values, weight).astype(BF)))


def token_blocks(partial):
    rows = partial.shape[0] // 4
    cuts = [0, rows, 2 * rows, 3 * rows, 3 * rows + rows // 2, 4 * rows]
    return [partial[a:b] for a, b in zip(cuts, cuts[1:])]


def normalize(values):
    centred = values - jnp.mean(values, axis=-1, keepdims=True)
    inv_std = lax.rsqrt(jnp.mean(centred * centred, axis=-1, keepdims=True) + EPS)
    return centred * inv_std, inv_std


NORM_ROWS = 32


def row_spec(array, at=None):
    width = array.shape[-1]
    if at is None:
        return pl.BlockSpec((NORM_ROWS, width), lambda i: (i, 0))
    return pl.BlockSpec((1, NORM_ROWS, width), lambda i, at=at: (at, i, 0))


def terms_of(terms):
    arrays, specs = [], []
    for term in terms:
        array, at = term if isinstance(term, tuple) else (term, None)
        arrays.append(array)
        specs.append(row_spec(array, at))
    return arrays, specs


def total_of(refs):
    values = [ref[0] if len(ref.shape) == 3 else ref[...] for ref in refs]
    return sum(value.astype(F32) for value in values)


def add_norm(terms, gain):
    arrays, specs = terms_of(terms)
    tokens, width = arrays[0].shape[-2], arrays[0].shape[-1]
    tokens = min(a.shape[-2] for a in arrays)

    def kernel(*refs):
        gain_ref, x, out = refs[-3:]
        values = total_of(refs[:-3])
        x[...] = values
        out[...] = (normalize(values)[0] * gain_ref[...]).astype(BF)

    return call(
        kernel,
        (tokens // NORM_ROWS,),
        specs + [whole(gain)],
        [row_spec(shape((tokens, width)))] * 2,
        [shape((tokens, width), F32), shape((tokens, width))],
        [*arrays, gain],
        "add_norm",
    )


def norm_grad(grad, values, gain):
    normed, inv_std = normalize(values)
    scaled = grad * gain
    first_mean = jnp.mean(scaled, axis=-1, keepdims=True)
    second_mean = jnp.mean(scaled * normed, axis=-1, keepdims=True)
    return (
        inv_std * (scaled - first_mean - normed * second_mean),
        jnp.sum(grad * normed, axis=0, keepdims=True),
    )


def accumulate(ref, value):
    @pl.when(pl.program_id(0) == 0)
    def _():
        ref[...] = jnp.zeros_like(ref)

    ref[...] += value


def norm_back(terms, upper, values, gain):
    arrays, specs = terms_of(terms)
    tokens, width = values.shape

    def kernel(*refs):
        upper_ref, x, gain_ref, out, out_low, gain_grad = refs[-6:]
        back, part = norm_grad(total_of(refs[:-6]), x[...], gain_ref[...])
        result = upper_ref[...].astype(F32) + back
        out[...] = result
        out_low[...] = result.astype(BF)
        accumulate(gain_grad, part)

    return call(
        kernel,
        (tokens // NORM_ROWS,),
        specs + [row_spec(upper), row_spec(values), whole(gain)],
        [row_spec(values)] * 2 + [pl.BlockSpec((1, width), lambda i: (0, 0))],
        [shape((tokens, width), F32), shape((tokens, width)), shape((1, width), F32)],
        [*arrays, upper, values, gain],
        "norm_back",
    )


def last_back(terms, upper, values, gain, masked, unit, order):
    arrays, specs = terms_of(terms)
    tokens, width = values.shape

    def kernel(*refs):
        upper_ref, x, gain_ref, mask, out, gain_grad, mask_grad = refs[-7:]
        back, part = norm_grad(total_of(refs[:-7]), x[...], gain_ref[...])
        result = upper_ref[...].astype(F32) + back
        hit = mask[...] > 0.5
        out[...] = reorder(jnp.where(hit, 0.0, result).astype(BF), unit, order)
        accumulate(gain_grad, part)
        accumulate(mask_grad, jnp.sum(jnp.where(hit, result, 0.0), axis=0, keepdims=True))

    line = pl.BlockSpec((1, width), lambda i: (0, 0))
    return call(
        kernel,
        (tokens // NORM_ROWS,),
        specs + [row_spec(upper), row_spec(values), whole(gain), row_spec(masked)],
        [row_spec(values), line, line],
        [shape((tokens, width)), shape((1, width), F32), shape((1, width), F32)],
        [*arrays, upper, values, gain, masked],
        "last_back",
    )


def start(hidden, cotangent, masked, embed, gain, unit, order):
    tokens, width = hidden.shape

    def kernel(hid, cot, mask, embed_ref, gain_ref, x, out, grad):
        hit = mask[...] > 0.5
        values = jnp.where(
            hit, embed_ref[...], reorder(hid[...], unit, order).astype(F32)
        )
        x[...] = values
        out[...] = (normalize(values)[0] * gain_ref[...]).astype(BF)
        grad[...] = jnp.where(hit, reorder(cot[...], unit, order).astype(F32), 0.0).astype(BF)

    rows = row_spec(hidden)
    return call(
        kernel,
        (tokens // NORM_ROWS,),
        [rows, rows, row_spec(masked), whole(embed), whole(gain)],
        [rows] * 3,
        [shape((tokens, width), F32), shape((tokens, width)), shape((tokens, width))],
        [hidden, cotangent, masked, embed, gain],
        "start",
    )


def layer_output(upper, terms, unit, order):
    arrays, specs = terms_of(terms)
    tokens, width = upper.shape

    def kernel(*refs):
        values = refs[-2][...] + total_of(refs[:-2])
        refs[-1][...] = reorder(values.astype(BF), unit, order)

    return call(
        kernel,
        (tokens // NORM_ROWS,),
        specs + [row_spec(upper)],
        row_spec(upper),
        shape((tokens, width)),
        [*arrays, upper],
        "layer_output",
    )


def feed_up(pieces, weight):
    rows, width = pieces[0].shape
    hidden = weight.shape[1]
    step = 256

    def kernel(*refs):
        up, tokens, act, slope, sems = refs[5:]

        @pl.when(pl.program_id(0) == 0)
        def _():
            assemble(tokens, refs[:5], sems)

        u = mm(tokens[...], up[...])
        square = u * u
        bend = jnp.tanh(SLOPE * u * (1.0 + CUBIC * square))
        half = 0.5 * (1.0 + bend)
        act[...] = (u * half).astype(BF)
        slope[...] = half + 0.5 * u * (1.0 - bend * bend) * SLOPE * (1.0 + 3.0 * CUBIC * square)

    part = pl.BlockSpec((4 * rows, step), lambda j: (0, j))
    return call(
        kernel,
        (hidden // step,),
        [ANY] * 5 + [pl.BlockSpec((width, step), lambda j: (0, j))],
        [pl.BlockSpec((4 * rows, width), lambda j: (0, 0)), part, part],
        [shape((4 * rows, width)), shape((4 * rows, hidden)), shape((4 * rows, hidden), F32)],
        [*pieces, weight],
        "feed_up",
        scratch=[pltpu.SemaphoreType.DMA((5,))],
        flops=8 * rows * width * hidden,
        size=2 * width * (hidden + 8 * rows),
    )


def feed_down(grad_y, slope, weight):
    tokens, width = grad_y.shape
    hidden = weight.shape[1]
    step = 256

    def kernel(dy, slope_ref, down, out):
        out[...] = (mm(dy[...], down[...]) * slope_ref[...]).astype(BF)

    part = pl.BlockSpec((tokens, step), lambda j: (0, j))
    return call(
        kernel,
        (hidden // step,),
        [whole(grad_y), part, pl.BlockSpec((width, step), lambda j: (0, j))],
        part,
        shape((tokens, hidden)),
        [grad_y, slope, weight],
        "feed_down",
        flops=2 * tokens * width * hidden,
        size=2 * width * (hidden + 8 * tokens),
    )


def softmax(scores):
    exp_terms = jnp.exp(scores - jnp.max(scores, axis=-1, keepdims=True))
    return exp_terms / jnp.sum(exp_terms, axis=-1, keepdims=True)


def score_grad(probs, grad_probs):
    return (
        probs * (grad_probs - jnp.sum(probs * grad_probs, axis=-1, keepdims=True))
    ).astype(BF)


def head(ref, k):
    return ref[:, k * HD : (k + 1) * HD]


def self_forward(projected, images):
    tokens, width = projected.shape
    rows, group = tokens // images, width // 3
    heads = group // HD

    def kernel(proj, mixed):
        for k in range(heads):
            query, key, value = (head(proj, j * heads + k) for j in range(3))
            probs = softmax(mm_t(query, key) * SCALE).astype(BF)
            mixed[:, k * HD : (k + 1) * HD] = mm(probs, value).astype(BF)

    return call(
        kernel,
        (images,),
        [pl.BlockSpec((rows, width), lambda i: (i, 0))],
        pl.BlockSpec((rows, group), lambda i: (i, 0)),
        shape((tokens, group)),
        [projected],
        "self_forward",
        flops=4 * tokens * rows * group,
    )


def self_back(projected, grad_mixed, images):
    tokens, width = projected.shape
    rows, group = tokens // images, width // 3
    heads = group // HD

    def kernel(proj, grad, out):
        for k in range(heads):
            query, key, value = (head(proj, j * heads + k) for j in range(3))
            grad_head = head(grad, k)
            probs = softmax(mm_t(query, key) * SCALE)
            grad_scores = score_grad(probs, mm_t(grad_head, value))
            parts = (
                mm(grad_scores, key) * SCALE,
                t_mm(grad_scores, query) * SCALE,
                t_mm(probs.astype(BF), grad_head),
            )
            for j, part in enumerate(parts):
                at = (j * heads + k) * HD
                out[:, at : at + HD] = part.astype(BF)

    return call(
        kernel,
        (images,),
        [
            pl.BlockSpec((rows, width), lambda i: (i, 0)),
            pl.BlockSpec((rows, group), lambda i: (i, 0)),
        ],
        pl.BlockSpec((rows, width), lambda i: (i, 0)),
        shape((tokens, width)),
        [projected, grad_mixed],
        "self_back",
        flops=10 * tokens * rows * group,
    )


def cross_forward(queries, text_kv):
    tokens, group = queries.shape
    heads = group // HD

    def kernel(query, text, mixed):
        for k in range(heads):
            probs = softmax(mm_t(head(query, k), head(text, k)) * SCALE).astype(BF)
            mixed[:, k * HD : (k + 1) * HD] = mm(probs, head(text, heads + k)).astype(BF)

    return call(
        kernel,
        (1,),
        [whole(queries), whole(text_kv)],
        whole(queries),
        shape((tokens, group)),
        [queries, text_kv],
        "cross_forward",
        flops=4 * tokens * text_kv.shape[0] * group,
    )


def cross_back(queries, text_kv, grad_mixed):
    tokens, group = queries.shape
    context = text_kv.shape[0]
    heads = group // HD

    def kernel(query, text, grad, grad_query, grad_text):
        for k in range(heads):
            query_head, key, value = head(query, k), head(text, k), head(text, heads + k)
            grad_head = head(grad, k)
            probs = softmax(mm_t(query_head, key) * SCALE)
            grad_scores = score_grad(probs, mm_t(grad_head, value))
            grad_query[:, k * HD : (k + 1) * HD] = (mm(grad_scores, key) * SCALE).astype(BF)
            at = (heads + k) * HD
            grad_text[:, k * HD : (k + 1) * HD] = t_mm(grad_scores, query_head) * SCALE
            grad_text[:, at : at + HD] = t_mm(probs.astype(BF), grad_head)

    return call(
        kernel,
        (1,),
        [whole(queries), whole(text_kv), whole(grad_mixed)],
        [whole(queries), whole(text_kv)],
        [shape((tokens, group)), shape((context, 2 * group), F32)],
        [queries, text_kv, grad_mixed],
        "cross_back",
        flops=10 * tokens * context * group,
    )


def grad_products(pairs, name, core=None, blocks=0):
    count_in = len(pairs[0][0])
    tokens, width = pairs[0][0][0].shape
    widths = [y[0].shape[1] for _, y in pairs]
    total = sum(widths)
    rows = 256 if core is None else width // (2 * blocks)
    steps = width // rows if core is None else blocks
    step = 512
    count = len(pairs) * count_in

    def kernel(r, *refs):
        out = refs[2 * count]
        offset = 0
        for k, wide in enumerate(widths):
            left = [refs[k * count_in + b][...].T for b in range(count_in)]
            for at in range(0, wide, step):
                out[:, offset + at : offset + at + step] = sum(
                    mm(left[b], refs[count + k * count_in + b][:, at : at + step])
                    for b in range(count_in)
                ).astype(BF)
            offset += wide

    pick = (lambda i, r: (0, i)) if core is None else (lambda i, r: (0, 2 * i + r[0]))
    return call(
        kernel,
        (steps,),
        [pl.BlockSpec((tokens, rows), pick)] * count
        + [pl.BlockSpec((tokens, w), lambda i, r: (0, 0)) for w in widths for _ in range(count_in)],
        pl.BlockSpec((rows, total), lambda i, r: (i, 0)),
        shape((steps * rows, total)),
        [b for x, _ in pairs for b in x] + [b for _, y in pairs for b in y],
        name,
        flops=2 * tokens * count_in * steps * rows * total,
        size=4 * width * total,
        rank=jnp.zeros((), jnp.int32) if core is None else core,
    )


def pick_weights(three, one, rank):
    rows, width = one.shape[0], one.shape[1] // 4

    def kernel(r, three_ref, one_ref, *outs):
        for k in range(4):

            @pl.when(pl.program_id(0) == k)
            def _():
                for j in range(3):
                    outs[k][:, j * width : (j + 1) * width] = three_ref[j]
                outs[k][:, 3 * width :] = one_ref[...]

    outs = [shape((rows, 4 * width))] * 4
    return call(
        kernel,
        (4,),
        [
            pl.BlockSpec((3, rows, width), lambda k, r: (0, 0, k ^ r[0])),
            pl.BlockSpec((rows, width), lambda k, r: (0, k ^ r[0])),
        ],
        [whole(a) for a in outs],
        outs,
        [three, one],
        "pick_weights",
        rank=rank,
    )


def pick_rows(arrays, rank):
    rows = arrays[0].shape[1]
    widths = [a.shape[2] for a in arrays]
    count = len(arrays)

    def kernel(r, *refs):
        for k in range(4):

            @pl.when(pl.program_id(0) == k)
            def _():
                at = 0
                for ref, width in zip(refs, widths):
                    refs[count + k][:, at : at + width] = ref[0]
                    at += width

    outs = [shape((rows, sum(widths)))] * 4
    return call(
        kernel,
        (4,),
        [pl.BlockSpec((1, rows, w), lambda k, r: (k ^ r[0], 0, 0)) for w in widths],
        [whole(a) for a in outs],
        outs,
        arrays,
        "pick_rows",
        rank=rank,
    )


def place(parts, rank):
    def kernel(r, *refs):
        for k in range(4):

            @pl.when(pl.program_id(0) == k)
            def _():
                refs[4][0] = refs[k][...]

    rows, columns = parts[0].shape
    return call(
        kernel,
        (4,),
        [whole(p) for p in parts],
        pl.BlockSpec((1, rows, columns), lambda k, r: (k ^ r[0], 0, 0)),
        shape((4, rows, columns)),
        parts,
        "place",
        rank=rank,
    )


def finish_wide(parts, rank):
    rows, width = parts[0].shape

    def kernel(r, *refs):
        for k in range(4):

            @pl.when(pl.program_id(0) == k)
            def _():
                refs[4][...] = refs[k][...].astype(F32)

    return call(
        kernel,
        (4,),
        [whole(p) for p in parts],
        pl.BlockSpec((rows, width), lambda k, r: (0, k ^ r[0])),
        shape((rows, 4 * width), F32),
        parts,
        "finish_wide",
        rank=rank,
    )


def finish_all(parts, text_grad, rank):
    rows, total = parts[0].shape
    width = total // 6

    def kernel(r, *refs):
        key, value, three, out, cross, cross_out = refs[4:]
        for k in range(4):

            @pl.when(pl.program_id(0) == k)
            def _():
                def part(j):
                    return refs[k][:, j * width : (j + 1) * width].astype(F32)

                for j in range(3):
                    three[j] = part(j)
                out[...] = part(3)
                cross[0] = part(4)
                cross_out[...] = part(5)

        cross[1] = key[...]
        cross[2] = value[...]

    wide = pl.BlockSpec((3, rows, width), lambda k, r: (0, 0, k ^ r[0]))
    flat = pl.BlockSpec((rows, width), lambda k, r: (0, k ^ r[0]))
    return call(
        kernel,
        (4,),
        [whole(p) for p in parts]
        + [flat, pl.BlockSpec((rows, width), lambda k, r: (0, 4 + (k ^ r[0])))],
        [wide, flat, wide, flat],
        [shape((3, rows, 4 * width), F32), shape((rows, 4 * width), F32)] * 2,
        [*parts, text_grad, text_grad],
        "finish_all",
        rank=rank,
    )


def plane_block(k):
    return (k >> 1) & 1, (k >> 2) * 2 + (k & 1)


def text_forward(caption, w_text, w_cross):
    context, rows = caption.shape[0], w_text.shape[0]
    half, width = context // 2, w_cross.shape[2] // 4

    def kernel(cap, weight, cross, own, blocks):
        own[...] = mm_t(cap[...], weight[...]).astype(BF)
        for j in range(2):
            part = mm(own[...], cross[1 + j]).astype(BF)
            for k in range(8):
                core, group = plane_block(k)
                blocks[k, :, j * width : (j + 1) * width] = part[
                    core * half : (core + 1) * half, group * width : (group + 1) * width
                ]

    return call(
        kernel,
        (1,),
        [whole(caption), whole(w_text), whole(w_cross)],
        [
            pl.BlockSpec((context, rows), lambda i: (0, 0)),
            pl.BlockSpec((8, half, 2 * width), lambda i: (0, 0, 0)),
        ],
        [shape((context, rows)), shape((8, half, 2 * width))],
        [caption, w_text, w_cross],
        "text_forward",
    )


def text_back(blocks, own_text, w_cross, caption, w_text, extra):
    context, rows = own_text.shape
    half, width = context // 2, w_cross.shape[2] // 4
    wide = caption.shape[1] // 4
    tail = extra.shape[0]

    def kernel(block, own, cross, cap, weight, more, kv_grad, text_grad, out, grads):
        for k in range(8):
            core, group = plane_block(k)
            for j in range(2):
                at = (4 * j + group) * width
                grads[core * half : (core + 1) * half, at : at + width] = block[
                    k, :, j * width : (j + 1) * width
                ]
        kv_grad[...] = t_mm(own[...], grads[...])
        grad_text = sum(
            mm_t(grads[:, 4 * j * width : 4 * (j + 1) * width], cross[1 + j]) for j in range(2)
        ).astype(BF)
        text_grad[...] = t_mm(grad_text, cap[...])
        part = mm(grad_text, weight[...]).astype(BF)
        for k in range(8):
            core, group = plane_block(k)
            out[k, :half, :] = part[core * half : (core + 1) * half, group * wide : (group + 1) * wide]
            out[k, half:, :] = more[...]

    operands = [blocks, own_text, w_cross, caption, w_text, extra]
    outs = [
        shape((rows, 8 * width), F32),
        shape((rows, 4 * wide), F32),
        shape((8, half + tail, wide)),
    ]
    return call(
        kernel,
        (1,),
        [whole(a) for a in operands],
        [whole(a) for a in outs],
        outs,
        operands,
        "text_back",
        scratch=[pltpu.VMEM((context, 8 * width), BF)],
    )


def caption_output(own, other, core):
    count, half, wide = own.shape

    def kernel(r, own_ref, other_ref, out):
        block = jnp.where(pl.program_id(0) == r[0], own_ref[0], other_ref[0])
        out[...] = block.astype(F32)

    block = pl.BlockSpec((1, half, wide), lambda i, k, r: (k, 0, 0))
    return call(
        kernel,
        (2, count),
        [block, block],
        pl.BlockSpec((half, wide), lambda i, k, r: (i, k)),
        shape((2 * half, 4 * wide), F32),
        [own, other],
        "caption_output",
        rank=core,
    )


def column_blocks(weight, count):
    rows = weight.shape[0]
    return weight.reshape(rows, count, -1).transpose(1, 0, 2)


def halves_of(values, width):
    high = values.astype(BF)
    low = (values - high.astype(F32)).astype(BF)
    return jnp.concatenate([high.reshape(-1, width), low.reshape(-1, width)], axis=0)


def whole_of(halves, width):
    rows = halves.shape[0] // 2
    return (halves[:rows] + halves[rows:]).reshape(-1, width)


def make_local(z_size):
    def sum_z(values):
        parts = values.reshape(z_size, -1, values.shape[-1])
        mine = trade(parts, "z").astype(F32).sum(axis=0).astype(BF)
        return spread(mine, "z", z_size).reshape(values.shape)

    def add_z(values):
        step = 1
        while step < z_size:
            values = values + lax.ppermute(
                values, "z", tuple((k, k ^ step) for k in range(z_size))
            )
            step *= 2
        return values

    def layer_order(values):
        shaped = values.reshape(values.shape[:-1] + (z_size, 2, 2, -1))
        return jnp.swapaxes(shaped, -3, -2).reshape(values.shape)

    def local(
        hidden,
        mask_index,
        mask_count,
        mask_embed,
        norm_gains,
        caption,
        w_qkv,
        w_out,
        w_cross,
        w_cross_out,
        w_text,
        w_up,
        w_down,
        cotangent,
    ):
        images, local_rows, width = hidden.shape
        full_length = mask_index.shape[1]
        rank = lax.axis_index("x") * 2 + lax.axis_index("y")
        core = lax.axis_index("c")
        tokens = images * local_rows
        group = width // 4
        text_width = caption.shape[1]

        unit = width // (4 * z_size)
        inside = unit % 128 == 0
        order = [4 * k + j for k in range(z_size) for j in (0, 2, 1, 3)] if inside else None

        def outer(values):
            return values if inside else layer_order(values)

        w_qkv, w_cross = w_qkv.transpose(1, 0, 2), w_cross.transpose(1, 0, 2)
        first = swap_parts(pick_weights(w_qkv, w_out, rank))
        first = gather_rows(place(first, rank))

        positions = lax.axis_index("y") * local_rows + jnp.arange(local_rows, dtype=jnp.int32)
        ranks = jnp.arange(full_length, dtype=jnp.int32)
        matches = (mask_index[:, :, None] == positions[None, None, :]) & (
            ranks[None, :, None] < mask_count[:, None, None]
        )
        masked = jnp.any(matches, axis=1).reshape(tokens, 1).astype(F32)
        gains = layer_order(norm_gains)
        gain_a, gain_b, gain_c = gains[:1], gains[1:2], gains[2:]
        start_x, attn_in, grad_top = start(
            outer(hidden.reshape(tokens, width)),
            outer(cotangent.reshape(tokens, width)),
            masked,
            layer_order(mask_embed)[None],
            gain_a,
            unit,
            order,
        )
        attn_in = gather_tokens(attn_in)
        mid = jnp.concatenate([column_blocks(w_cross[0], 4), column_blocks(w_cross_out, 4)], axis=2)
        up = column_blocks(w_up, 4)
        attn_in, mid, up = lax.optimization_barrier((attn_in, mid, up))
        mid, up = gather_rows(trade(mid)), gather_rows(trade(up))

        own_text, kv_part = text_forward(caption, w_text, w_cross)
        text_kv = trade(kv_part, PLANE).astype(F32).sum(axis=0).astype(BF)
        text_kv = sum_z(text_kv)
        other = swap(text_kv, "c")
        text_kv = jnp.concatenate(
            [jnp.where(core == 0, text_kv, other), jnp.where(core == 0, other, text_kv)], axis=0
        )
        attn_in, text_kv = lax.optimization_barrier((attn_in, text_kv))

        attn_in, projected = gather_mm(attn_in, first, 0, 3 * group, "qkv_mm")
        self_mixed = self_forward(projected, 2 * images)
        down = column_blocks(w_down, 4)
        self_mixed, down = lax.optimization_barrier((self_mixed, down))
        down = gather_rows(trade(down))
        parts = mm_scatter(self_mixed, first[:, 3 * group :])
        after_attn, cross_in = add_norm([start_x] + parts, gain_b)

        cross_in, cross_queries = gather_mm(gather_tokens(cross_in), mid, 0, group, "query_mm")
        cross_mixed = cross_forward(cross_queries, text_kv)
        parts = mm_scatter(cross_mixed, mid[:, group:])
        after_cross, mlp_in = add_norm([after_attn] + parts, gain_c)

        mlp_in = gather_tokens(mlp_in)
        mlp_in, grad_top = lax.optimization_barrier((mlp_in, grad_top))
        grad_y = jnp.concatenate(gather_tokens(grad_top), axis=0)
        mlp_in, activated, slope = feed_up(mlp_in, up)
        early = [attn_in, self_mixed, cross_in, cross_mixed]
        if inside:
            grad_axes, halves = "z", (core, z_size)

            def both(values):
                return [values, swap(values, "c")]

        else:
            grad_axes, halves = DATA, ()

            def both(values):
                return [values]

        early = [both(values) for values in early]
        down_part = grad_products([(both(grad_y), both(activated))], "down_grads", *halves)
        mlp_in = both(mlp_in)
        slope, down_part, early, mlp_in = lax.optimization_barrier((slope, down_part, early, mlp_in))
        down_rows = scatter_grad(down_part, grad_axes)
        grad_pre = feed_down(grad_y, slope, down)
        parts = mm_scatter(grad_pre, up)
        up_part = grad_products([(mlp_in, both(grad_pre))], "up_grads", *halves)
        grad_after_cross, cross_branch, gain_grad_c = norm_back(
            parts, grad_top, after_cross, gain_c
        )

        cross_branch = gather_tokens(cross_branch)
        activated, cross_own = lax.optimization_barrier((activated, cross_branch[0]))
        result = mm_t(activated, down).astype(BF)
        cross_branch, up_part, result = lax.optimization_barrier(
            ((cross_own,) + cross_branch[1:], up_part, result)
        )
        cross_branch, grad_cross_mixed = gather_mm(
            cross_branch, mid, group, group, "cross_out_back"
        )
        grad_cq, kv_grad = cross_back(cross_queries, text_kv, grad_cross_mixed)
        up_part, down_rows, kv_grad = lax.optimization_barrier((up_part, down_rows, kv_grad))
        up_rows = scatter_grad(up_part, grad_axes)
        cross_branch, grad_cq_both = both(cross_branch), both(grad_cq)
        parts = mm_scatter(grad_cq, mid[:, :group])
        grad_after_attn, attn_branch, gain_grad_b = norm_back(
            parts, grad_after_cross, after_attn, gain_b
        )

        attn_branch, result = lax.optimization_barrier((gather_tokens(attn_branch), result))
        result = scatter_first(token_blocks(result))
        attn_branch, grad_self_mixed = gather_mm(attn_branch, first, 3 * group, group, "out_back")
        grad_projected = self_back(projected, grad_self_mixed, 2 * images)
        kv_part = kv_grad.astype(BF).reshape(2, z_size, -1, 2 * group)
        kv_part = kv_part.transpose(1, 0, 2, 3).reshape(2 * z_size, -1, 2 * group)
        grad_projected, result, kv_part = lax.optimization_barrier(
            (grad_projected, result, kv_part)
        )
        kv_part = trade(kv_part, DATA)
        result = scatter_second(result)
        rest_part = grad_products(
            [
                (early[0], both(grad_projected)),
                (both(attn_branch), early[1]),
                (early[2], grad_cq_both),
                (cross_branch, early[3]),
            ],
            "attention_grads",
            *halves,
        )
        grad_projected, result, kv_part, rest_part = lax.optimization_barrier(
            (grad_projected, result, kv_part, rest_part)
        )
        rest_part, up_rows = lax.optimization_barrier((rest_part, up_rows))
        rest_rows = scatter_grad(rest_part, grad_axes)
        parts = mm_scatter(grad_projected, first[:, : 3 * group])
        grad_hidden, gain_grad_a, mask_grad = last_back(
            parts,
            grad_after_attn,
            start_x,
            gain_a,
            masked,
            unit,
            order,
        )
        sums = jnp.concatenate([gain_grad_a, gain_grad_b, gain_grad_c, mask_grad], axis=0)


        kv_part = kv_part.astype(F32).sum(axis=0).astype(BF)
        kv_sum = spread(kv_part, "z", z_size).reshape(-1, 2 * group)
        kv_grads = spread(kv_sum, PLANE, 8)
        kv_weight_grad, grad_text_w, caption_part = text_back(
            kv_grads, own_text, w_cross, caption, w_text, halves_of(sums, text_width // 4)
        )
        half_context = caption.shape[0] // 2
        caption_part = trade(caption_part, PLANE)
        output = layer_output(after_cross, result, unit, order)
        caption_part, output, down_rows, up_rows = lax.optimization_barrier(
            (caption_part, output, down_rows, up_rows)
        )

        caption_part = caption_part.astype(F32).sum(axis=0)
        sums = layer_order(add_z(whole_of(caption_part[half_context:], width)))
        caption_part = caption_part[:half_context].astype(BF).reshape(z_size, -1, text_width // 4)
        caption_part = trade(caption_part, "z")
        down_parts = swap_parts(pick_rows([down_rows], rank))
        caption_part, down_parts, up_rows = lax.optimization_barrier(
            (caption_part, down_parts, up_rows)
        )

        caption_part = caption_part.astype(F32).sum(axis=0).astype(BF)
        caption_part = spread(caption_part, "z", z_size).reshape(half_context, -1)
        up_parts = swap_parts(pick_rows([up_rows], rank))
        down_grad = finish_wide(down_parts, rank)
        caption_part, up_parts, down_grad = lax.optimization_barrier(
            (caption_part, up_parts, down_grad)
        )

        caption_part = spread(caption_part)
        up_grad = finish_wide(up_parts, rank)
        caption_part, rest_rows, up_grad = lax.optimization_barrier(
            (caption_part, rest_rows, up_grad)
        )
        grad_caption = caption_output(caption_part, swap(caption_part, "c"), core)
        rest_rows = swap_parts(pick_rows([rest_rows], rank))
        qkv_grad, out_grad, grad_cross, cross_out_grad = finish_all(
            rest_rows, kv_weight_grad, rank
        )
        return (
            outer(output).reshape(hidden.shape),
            outer(grad_hidden).reshape(hidden.shape),
            grad_caption,
            sums[:3],
            sums[3],
            qkv_grad.transpose(1, 0, 2),
            out_grad,
            grad_cross.transpose(1, 0, 2),
            cross_out_grad,
            grad_text_w,
            up_grad,
            down_grad,
        )

    return local


def solution(mesh):
    z_size = mesh.shape["img"] // 4
    inner = Mesh(mesh.devices.reshape(z_size, 2, 2, 2), ("z", "x", "c", "y"))
    image = ("z", "x", "c")
    tokens = P(image, "y", None)
    rows = P(image + ("y",))
    in_specs = (tokens, P(image, None), P(image), P(), P(), P()) + (rows,) * 7 + (tokens,)
    out_specs = (tokens, tokens, P(), P(), P()) + (rows,) * 7
    return jax.shard_map(
        make_local(z_size), mesh=inner, in_specs=in_specs, out_specs=out_specs, check_vma=False
    )
```

```python
import math

import jax
import jax.numpy as jnp
from jax import lax
from jax.experimental import pallas as pl
from jax.experimental.pallas import tpu as pltpu
from jax.sharding import Mesh
from jax.sharding import PartitionSpec as P

HD = 128
EPS = 1e-05
BF = jnp.bfloat16
F32 = jnp.float32
PAIR = ((0, 1), (1, 0))
GROUP = ("x", "y")
DATA = ("z", "c")
PLANE = ("x", "c", "y")
VMEM = 48 * 1024 * 1024
SCALE = 1.0 / math.sqrt(HD)
SLOPE = math.sqrt(2.0 / math.pi)
CUBIC = 0.044715


def dot(a, b, dims):
    return lax.dot_general(a, b, (dims, ((), ())), preferred_element_type=F32)


def mm(a, b):
    return dot(a, b, ((1,), (0,)))


def mm_t(a, b):
    return dot(a, b, ((1,), (1,)))


def t_mm(a, b):
    return dot(a, b, ((0,), (0,)))


def shape(dims, dtype=BF):
    return jax.ShapeDtypeStruct(dims, dtype)


def swap(values, axis):
    return lax.ppermute(values, axis, PAIR)


def trade(blocks, axes=GROUP):
    return lax.all_to_all(blocks, axes, 0, 0, tiled=True)


def spread(values, axes=GROUP, count=4):
    return trade(jnp.broadcast_to(values[None], (count,) + values.shape), axes)


def gather_tokens(own):
    half = own.shape[0] // 2
    from_x = swap(own, "x")
    from_y = swap(own, "y")
    return own, from_y, from_x, swap(from_x[:half], "y"), swap(from_y[half:], "x")


def scatter_first(parts):
    own, for_y, for_x, for_low, for_high = parts
    half = for_low.shape[0]
    low = swap(for_low, "y").astype(F32) + for_x[:half].astype(F32)
    high = swap(for_high, "x").astype(F32) + for_y[half:].astype(F32)
    return (
        own,
        jnp.concatenate([low.astype(BF), for_x[half:]], axis=0),
        jnp.concatenate([for_y[:half], high.astype(BF)], axis=0),
    )


def scatter_second(parts):
    own, for_x, for_y = parts
    return [own, swap(for_x, "x"), swap(for_y, "y")]


def scatter_tokens(parts):
    return scatter_second(scatter_first(parts))


def swap_parts(parts):
    return [
        parts[0],
        swap(parts[1], "y"),
        swap(parts[2], "x"),
        lax.ppermute(parts[3], GROUP, ((0, 3), (1, 2), (2, 1), (3, 0))),
    ]


def gather_rows(rows):
    return lax.all_gather(rows.reshape(-1, rows.shape[-1]), DATA, axis=0, tiled=True)


def scatter_grad(partial, axes):
    summed = lax.psum_scatter(partial, axes, scatter_dimension=0, tiled=True)
    return summed.reshape(4, -1, summed.shape[-1])


def call(kernel, grid, in_specs, out_specs, out_shape, operands, name, flops=0, size=1 << 22,
         rank=None, scratch=()):
    options = dict(
        out_shape=out_shape,
        compiler_params=pltpu.CompilerParams(vmem_limit_bytes=VMEM),
        cost_estimate=pl.CostEstimate(flops=flops, bytes_accessed=size, transcendentals=0),
        name=name,
    )
    if rank is None:
        return pl.pallas_call(
            kernel, grid=grid, in_specs=in_specs, out_specs=out_specs, scratch_shapes=scratch,
            **options,
        )(*operands)
    spec = pltpu.PrefetchScalarGridSpec(
        num_scalar_prefetch=1,
        grid=grid,
        in_specs=in_specs,
        out_specs=out_specs,
        scratch_shapes=scratch,
    )
    return pl.pallas_call(kernel, grid_spec=spec, **options)(rank.reshape(1), *operands)


def whole(array):
    return pl.BlockSpec(array.shape, lambda *_: (0,) * len(array.shape))


def reorder(values, unit, order):
    if order is None:
        return values
    return jnp.concatenate([values[:, k * unit : (k + 1) * unit] for k in order], axis=1)


def assemble(target, pieces, sems):
    copies, at = [], 0
    for k, piece in enumerate(pieces):
        rows = piece.shape[0]
        copies.append(pltpu.make_async_copy(piece, target.at[at : at + rows], sems.at[k]))
        at += rows
    for copy in copies:
        copy.start()
    for copy in copies:
        copy.wait()


ANY = pl.BlockSpec(memory_space=pl.ANY)


def gather_mm(pieces, weight, first, columns, name):
    rows, width = pieces[0].shape
    step = 256

    def kernel(*refs):
        tokens, out, sems = refs[6:]

        @pl.when(pl.program_id(0) == 0)
        def _():
            assemble(tokens, refs[:5], sems)

        out[...] = mm(tokens[...], refs[5][...]).astype(BF)

    return call(
        kernel,
        (columns // step,),
        [ANY] * 5 + [pl.BlockSpec((width, step), lambda j: (0, first // step + j))],
        [
            pl.BlockSpec((4 * rows, width), lambda j: (0, 0)),
            pl.BlockSpec((4 * rows, step), lambda j: (0, j)),
        ],
        [shape((4 * rows, width)), shape((4 * rows, columns))],
        [*pieces, weight],
        name,
        flops=8 * rows * width * columns,
        size=2 * width * (columns + 8 * rows),
        scratch=[pltpu.SemaphoreType.DMA((5,))],
    )


def mm_scatter(values, weight):
    return scatter_tokens(token_blocks(mm_t(values, weight).astype(BF)))


def token_blocks(partial):
    rows = partial.shape[0] // 4
    cuts = [0, rows, 2 * rows, 3 * rows, 3 * rows + rows // 2, 4 * rows]
    return [partial[a:b] for a, b in zip(cuts, cuts[1:])]


def normalize(values):
    centred = values - jnp.mean(values, axis=-1, keepdims=True)
    inv_std = lax.rsqrt(jnp.mean(centred * centred, axis=-1, keepdims=True) + EPS)
    return centred * inv_std, inv_std


NORM_ROWS = 32


def row_spec(array, at=None):
    width = array.shape[-1]
    if at is None:
        return pl.BlockSpec((NORM_ROWS, width), lambda i: (i, 0))
    return pl.BlockSpec((1, NORM_ROWS, width), lambda i, at=at: (at, i, 0))


def terms_of(terms):
    arrays, specs = [], []
    for term in terms:
        array, at = term if isinstance(term, tuple) else (term, None)
        arrays.append(array)
        specs.append(row_spec(array, at))
    return arrays, specs


def total_of(refs):
    values = [ref[0] if len(ref.shape) == 3 else ref[...] for ref in refs]
    return sum(value.astype(F32) for value in values)


def add_norm(terms, gain):
    arrays, specs = terms_of(terms)
    tokens, width = arrays[0].shape[-2], arrays[0].shape[-1]
    tokens = min(a.shape[-2] for a in arrays)

    def kernel(*refs):
        gain_ref, x, out = refs[-3:]
        values = total_of(refs[:-3])
        x[...] = values
        out[...] = (normalize(values)[0] * gain_ref[...]).astype(BF)

    return call(
        kernel,
        (tokens // NORM_ROWS,),
        specs + [whole(gain)],
        [row_spec(shape((tokens, width)))] * 2,
        [shape((tokens, width), F32), shape((tokens, width))],
        [*arrays, gain],
        "add_norm",
    )


def norm_grad(grad, values, gain):
    normed, inv_std = normalize(values)
    scaled = grad * gain
    first_mean = jnp.mean(scaled, axis=-1, keepdims=True)
    second_mean = jnp.mean(scaled * normed, axis=-1, keepdims=True)
    return (
        inv_std * (scaled - first_mean - normed * second_mean),
        jnp.sum(grad * normed, axis=0, keepdims=True),
    )


def accumulate(ref, value):
    @pl.when(pl.program_id(0) == 0)
    def _():
        ref[...] = jnp.zeros_like(ref)

    ref[...] += value


def norm_back(terms, upper, values, gain):
    arrays, specs = terms_of(terms)
    tokens, width = values.shape

    def kernel(*refs):
        upper_ref, x, gain_ref, out, out_low, gain_grad = refs[-6:]
        back, part = norm_grad(total_of(refs[:-6]), x[...], gain_ref[...])
        result = upper_ref[...].astype(F32) + back
        out[...] = result
        out_low[...] = result.astype(BF)
        accumulate(gain_grad, part)

    return call(
        kernel,
        (tokens // NORM_ROWS,),
        specs + [row_spec(upper), row_spec(values), whole(gain)],
        [row_spec(values)] * 2 + [pl.BlockSpec((1, width), lambda i: (0, 0))],
        [shape((tokens, width), F32), shape((tokens, width)), shape((1, width), F32)],
        [*arrays, upper, values, gain],
        "norm_back",
    )


def last_back(terms, upper, values, gain, masked, unit, order):
    arrays, specs = terms_of(terms)
    tokens, width = values.shape

    def kernel(*refs):
        upper_ref, x, gain_ref, mask, out, gain_grad, mask_grad = refs[-7:]
        back, part = norm_grad(total_of(refs[:-7]), x[...], gain_ref[...])
        result = upper_ref[...].astype(F32) + back
        hit = mask[...] > 0.5
        out[...] = reorder(jnp.where(hit, 0.0, result).astype(BF), unit, order)
        accumulate(gain_grad, part)
        accumulate(mask_grad, jnp.sum(jnp.where(hit, result, 0.0), axis=0, keepdims=True))

    line = pl.BlockSpec((1, width), lambda i: (0, 0))
    return call(
        kernel,
        (tokens // NORM_ROWS,),
        specs + [row_spec(upper), row_spec(values), whole(gain), row_spec(masked)],
        [row_spec(values), line, line],
        [shape((tokens, width)), shape((1, width), F32), shape((1, width), F32)],
        [*arrays, upper, values, gain, masked],
        "last_back",
    )


def start(hidden, cotangent, masked, embed, gain, unit, order):
    tokens, width = hidden.shape

    def kernel(hid, cot, mask, embed_ref, gain_ref, x, out, grad):
        hit = mask[...] > 0.5
        values = jnp.where(
            hit, embed_ref[...], reorder(hid[...], unit, order).astype(F32)
        )
        x[...] = values
        out[...] = (normalize(values)[0] * gain_ref[...]).astype(BF)
        grad[...] = jnp.where(hit, reorder(cot[...], unit, order).astype(F32), 0.0).astype(BF)

    rows = row_spec(hidden)
    return call(
        kernel,
        (tokens // NORM_ROWS,),
        [rows, rows, row_spec(masked), whole(embed), whole(gain)],
        [rows] * 3,
        [shape((tokens, width), F32), shape((tokens, width)), shape((tokens, width))],
        [hidden, cotangent, masked, embed, gain],
        "start",
    )


def layer_output(upper, terms, unit, order):
    arrays, specs = terms_of(terms)
    tokens, width = upper.shape

    def kernel(*refs):
        values = refs[-2][...] + total_of(refs[:-2])
        refs[-1][...] = reorder(values.astype(BF), unit, order)

    return call(
        kernel,
        (tokens // NORM_ROWS,),
        specs + [row_spec(upper)],
        row_spec(upper),
        shape((tokens, width)),
        [*arrays, upper],
        "layer_output",
    )


def feed_up(pieces, weight):
    rows, width = pieces[0].shape
    hidden = weight.shape[1]
    step = 256

    def kernel(*refs):
        up, tokens, act, slope, sems = refs[5:]

        @pl.when(pl.program_id(0) == 0)
        def _():
            assemble(tokens, refs[:5], sems)

        u = mm(tokens[...], up[...])
        square = u * u
        bend = jnp.tanh(SLOPE * u * (1.0 + CUBIC * square))
        half = 0.5 * (1.0 + bend)
        act[...] = (u * half).astype(BF)
        slope[...] = half + 0.5 * u * (1.0 - bend * bend) * SLOPE * (1.0 + 3.0 * CUBIC * square)

    part = pl.BlockSpec((4 * rows, step), lambda j: (0, j))
    return call(
        kernel,
        (hidden // step,),
        [ANY] * 5 + [pl.BlockSpec((width, step), lambda j: (0, j))],
        [pl.BlockSpec((4 * rows, width), lambda j: (0, 0)), part, part],
        [shape((4 * rows, width)), shape((4 * rows, hidden)), shape((4 * rows, hidden), F32)],
        [*pieces, weight],
        "feed_up",
        scratch=[pltpu.SemaphoreType.DMA((5,))],
        flops=8 * rows * width * hidden,
        size=2 * width * (hidden + 8 * rows),
    )


def feed_down(grad_y, slope, weight):
    tokens, width = grad_y.shape
    hidden = weight.shape[1]
    step = 256

    def kernel(dy, slope_ref, down, out):
        out[...] = (mm(dy[...], down[...]) * slope_ref[...]).astype(BF)

    part = pl.BlockSpec((tokens, step), lambda j: (0, j))
    return call(
        kernel,
        (hidden // step,),
        [whole(grad_y), part, pl.BlockSpec((width, step), lambda j: (0, j))],
        part,
        shape((tokens, hidden)),
        [grad_y, slope, weight],
        "feed_down",
        flops=2 * tokens * width * hidden,
        size=2 * width * (hidden + 8 * tokens),
    )


def softmax(scores):
    exp_terms = jnp.exp(scores - jnp.max(scores, axis=-1, keepdims=True))
    return exp_terms / jnp.sum(exp_terms, axis=-1, keepdims=True)


def score_grad(probs, grad_probs):
    return (
        probs * (grad_probs - jnp.sum(probs * grad_probs, axis=-1, keepdims=True))
    ).astype(BF)


def head(ref, k):
    return ref[:, k * HD : (k + 1) * HD]


def self_forward(projected, images):
    tokens, width = projected.shape
    rows, group = tokens // images, width // 3
    heads = group // HD

    def kernel(proj, mixed):
        for k in range(heads):
            query, key, value = (head(proj, j * heads + k) for j in range(3))
            probs = softmax(mm_t(query, key) * SCALE).astype(BF)
            mixed[:, k * HD : (k + 1) * HD] = mm(probs, value).astype(BF)

    return call(
        kernel,
        (images,),
        [pl.BlockSpec((rows, width), lambda i: (i, 0))],
        pl.BlockSpec((rows, group), lambda i: (i, 0)),
        shape((tokens, group)),
        [projected],
        "self_forward",
        flops=4 * tokens * rows * group,
    )


def self_back(projected, grad_mixed, images):
    tokens, width = projected.shape
    rows, group = tokens // images, width // 3
    heads = group // HD

    def kernel(proj, grad, out):
        for k in range(heads):
            query, key, value = (head(proj, j * heads + k) for j in range(3))
            grad_head = head(grad, k)
            probs = softmax(mm_t(query, key) * SCALE)
            grad_scores = score_grad(probs, mm_t(grad_head, value))
            parts = (
                mm(grad_scores, key) * SCALE,
                t_mm(grad_scores, query) * SCALE,
                t_mm(probs.astype(BF), grad_head),
            )
            for j, part in enumerate(parts):
                at = (j * heads + k) * HD
                out[:, at : at + HD] = part.astype(BF)

    return call(
        kernel,
        (images,),
        [
            pl.BlockSpec((rows, width), lambda i: (i, 0)),
            pl.BlockSpec((rows, group), lambda i: (i, 0)),
        ],
        pl.BlockSpec((rows, width), lambda i: (i, 0)),
        shape((tokens, width)),
        [projected, grad_mixed],
        "self_back",
        flops=10 * tokens * rows * group,
    )


def cross_forward(queries, text_kv):
    tokens, group = queries.shape
    heads = group // HD

    def kernel(query, text, mixed):
        for k in range(heads):
            probs = softmax(mm_t(head(query, k), head(text, k)) * SCALE).astype(BF)
            mixed[:, k * HD : (k + 1) * HD] = mm(probs, head(text, heads + k)).astype(BF)

    return call(
        kernel,
        (1,),
        [whole(queries), whole(text_kv)],
        whole(queries),
        shape((tokens, group)),
        [queries, text_kv],
        "cross_forward",
        flops=4 * tokens * text_kv.shape[0] * group,
    )


def cross_back(queries, text_kv, grad_mixed):
    tokens, group = queries.shape
    context = text_kv.shape[0]
    heads = group // HD

    def kernel(query, text, grad, grad_query, grad_text):
        for k in range(heads):
            query_head, key, value = head(query, k), head(text, k), head(text, heads + k)
            grad_head = head(grad, k)
            probs = softmax(mm_t(query_head, key) * SCALE)
            grad_scores = score_grad(probs, mm_t(grad_head, value))
            grad_query[:, k * HD : (k + 1) * HD] = (mm(grad_scores, key) * SCALE).astype(BF)
            at = (heads + k) * HD
            grad_text[:, k * HD : (k + 1) * HD] = t_mm(grad_scores, query_head) * SCALE
            grad_text[:, at : at + HD] = t_mm(probs.astype(BF), grad_head)

    return call(
        kernel,
        (1,),
        [whole(queries), whole(text_kv), whole(grad_mixed)],
        [whole(queries), whole(text_kv)],
        [shape((tokens, group)), shape((context, 2 * group), F32)],
        [queries, text_kv, grad_mixed],
        "cross_back",
        flops=10 * tokens * context * group,
    )


def grad_products(pairs, name, core=None, blocks=0):
    count_in = len(pairs[0][0])
    tokens, width = pairs[0][0][0].shape
    widths = [y[0].shape[1] for _, y in pairs]
    total = sum(widths)
    rows = 256 if core is None else width // (2 * blocks)
    steps = width // rows if core is None else blocks
    step = 512
    count = len(pairs) * count_in

    def kernel(r, *refs):
        out = refs[2 * count]
        offset = 0
        for k, wide in enumerate(widths):
            left = [refs[k * count_in + b][...].T for b in range(count_in)]
            for at in range(0, wide, step):
                out[:, offset + at : offset + at + step] = sum(
                    mm(left[b], refs[count + k * count_in + b][:, at : at + step])
                    for b in range(count_in)
                ).astype(BF)
            offset += wide

    pick = (lambda i, r: (0, i)) if core is None else (lambda i, r: (0, 2 * i + r[0]))
    return call(
        kernel,
        (steps,),
        [pl.BlockSpec((tokens, rows), pick)] * count
        + [pl.BlockSpec((tokens, w), lambda i, r: (0, 0)) for w in widths for _ in range(count_in)],
        pl.BlockSpec((rows, total), lambda i, r: (i, 0)),
        shape((steps * rows, total)),
        [b for x, _ in pairs for b in x] + [b for _, y in pairs for b in y],
        name,
        flops=2 * tokens * count_in * steps * rows * total,
        size=4 * width * total,
        rank=jnp.zeros((), jnp.int32) if core is None else core,
    )


def pick_weights(three, one, rank):
    rows, width = one.shape[0], one.shape[1] // 4

    def kernel(r, three_ref, one_ref, *outs):
        for k in range(4):

            @pl.when(pl.program_id(0) == k)
            def _():
                for j in range(3):
                    outs[k][:, j * width : (j + 1) * width] = three_ref[j]
                outs[k][:, 3 * width :] = one_ref[...]

    outs = [shape((rows, 4 * width))] * 4
    return call(
        kernel,
        (4,),
        [
            pl.BlockSpec((3, rows, width), lambda k, r: (0, 0, k ^ r[0])),
            pl.BlockSpec((rows, width), lambda k, r: (0, k ^ r[0])),
        ],
        [whole(a) for a in outs],
        outs,
        [three, one],
        "pick_weights",
        rank=rank,
    )


def pick_rows(arrays, rank):
    rows = arrays[0].shape[1]
    widths = [a.shape[2] for a in arrays]
    count = len(arrays)

    def kernel(r, *refs):
        for k in range(4):

            @pl.when(pl.program_id(0) == k)
            def _():
                at = 0
                for ref, width in zip(refs, widths):
                    refs[count + k][:, at : at + width] = ref[0]
                    at += width

    outs = [shape((rows, sum(widths)))] * 4
    return call(
        kernel,
        (4,),
        [pl.BlockSpec((1, rows, w), lambda k, r: (k ^ r[0], 0, 0)) for w in widths],
        [whole(a) for a in outs],
        outs,
        arrays,
        "pick_rows",
        rank=rank,
    )


def place(parts, rank):
    def kernel(r, *refs):
        for k in range(4):

            @pl.when(pl.program_id(0) == k)
            def _():
                refs[4][0] = refs[k][...]

    rows, columns = parts[0].shape
    return call(
        kernel,
        (4,),
        [whole(p) for p in parts],
        pl.BlockSpec((1, rows, columns), lambda k, r: (k ^ r[0], 0, 0)),
        shape((4, rows, columns)),
        parts,
        "place",
        rank=rank,
    )


def finish_wide(parts, rank):
    rows, width = parts[0].shape

    def kernel(r, *refs):
        for k in range(4):

            @pl.when(pl.program_id(0) == k)
            def _():
                refs[4][...] = refs[k][...].astype(F32)

    return call(
        kernel,
        (4,),
        [whole(p) for p in parts],
        pl.BlockSpec((rows, width), lambda k, r: (0, k ^ r[0])),
        shape((rows, 4 * width), F32),
        parts,
        "finish_wide",
        rank=rank,
    )


def finish_all(parts, text_grad, rank):
    rows, total = parts[0].shape
    width = total // 6

    def kernel(r, *refs):
        key, value, three, out, cross, cross_out = refs[4:]
        for k in range(4):

            @pl.when(pl.program_id(0) == k)
            def _():
                def part(j):
                    return refs[k][:, j * width : (j + 1) * width].astype(F32)

                for j in range(3):
                    three[j] = part(j)
                out[...] = part(3)
                cross[0] = part(4)
                cross_out[...] = part(5)

        cross[1] = key[...]
        cross[2] = value[...]

    wide = pl.BlockSpec((3, rows, width), lambda k, r: (0, 0, k ^ r[0]))
    flat = pl.BlockSpec((rows, width), lambda k, r: (0, k ^ r[0]))
    return call(
        kernel,
        (4,),
        [whole(p) for p in parts]
        + [flat, pl.BlockSpec((rows, width), lambda k, r: (0, 4 + (k ^ r[0])))],
        [wide, flat, wide, flat],
        [shape((3, rows, 4 * width), F32), shape((rows, 4 * width), F32)] * 2,
        [*parts, text_grad, text_grad],
        "finish_all",
        rank=rank,
    )


def plane_block(k):
    return (k >> 1) & 1, (k >> 2) * 2 + (k & 1)


def text_forward(caption, w_text, w_cross):
    context, rows = caption.shape[0], w_text.shape[0]
    half, width = context // 2, w_cross.shape[2] // 4

    def kernel(cap, weight, cross, own, blocks):
        own[...] = mm_t(cap[...], weight[...]).astype(BF)
        for j in range(2):
            part = mm(own[...], cross[1 + j]).astype(BF)
            for k in range(8):
                core, group = plane_block(k)
                blocks[k, :, j * width : (j + 1) * width] = part[
                    core * half : (core + 1) * half, group * width : (group + 1) * width
                ]

    return call(
        kernel,
        (1,),
        [whole(caption), whole(w_text), whole(w_cross)],
        [
            pl.BlockSpec((context, rows), lambda i: (0, 0)),
            pl.BlockSpec((8, half, 2 * width), lambda i: (0, 0, 0)),
        ],
        [shape((context, rows)), shape((8, half, 2 * width))],
        [caption, w_text, w_cross],
        "text_forward",
    )


def text_back(blocks, own_text, w_cross, caption, w_text, extra):
    context, rows = own_text.shape
    half, width = context // 2, w_cross.shape[2] // 4
    wide = caption.shape[1] // 4
    tail = extra.shape[0]

    def kernel(block, own, cross, cap, weight, more, kv_grad, text_grad, out, grads):
        for k in range(8):
            core, group = plane_block(k)
            for j in range(2):
                at = (4 * j + group) * width
                grads[core * half : (core + 1) * half, at : at + width] = block[
                    k, :, j * width : (j + 1) * width
                ]
        kv_grad[...] = t_mm(own[...], grads[...])
        grad_text = sum(
            mm_t(grads[:, 4 * j * width : 4 * (j + 1) * width], cross[1 + j]) for j in range(2)
        ).astype(BF)
        text_grad[...] = t_mm(grad_text, cap[...])
        part = mm(grad_text, weight[...]).astype(BF)
        for k in range(8):
            core, group = plane_block(k)
            out[k, :half, :] = part[core * half : (core + 1) * half, group * wide : (group + 1) * wide]
            out[k, half:, :] = more[...]

    operands = [blocks, own_text, w_cross, caption, w_text, extra]
    outs = [
        shape((rows, 8 * width), F32),
        shape((rows, 4 * wide), F32),
        shape((8, half + tail, wide)),
    ]
    return call(
        kernel,
        (1,),
        [whole(a) for a in operands],
        [whole(a) for a in outs],
        outs,
        operands,
        "text_back",
        scratch=[pltpu.VMEM((context, 8 * width), BF)],
    )


def caption_output(own, other, core):
    count, half, wide = own.shape

    def kernel(r, own_ref, other_ref, out):
        block = jnp.where(pl.program_id(0) == r[0], own_ref[0], other_ref[0])
        out[...] = block.astype(F32)

    block = pl.BlockSpec((1, half, wide), lambda i, k, r: (k, 0, 0))
    return call(
        kernel,
        (2, count),
        [block, block],
        pl.BlockSpec((half, wide), lambda i, k, r: (i, k)),
        shape((2 * half, 4 * wide), F32),
        [own, other],
        "caption_output",
        rank=core,
    )


def column_blocks(weight, count):
    rows = weight.shape[0]
    return weight.reshape(rows, count, -1).transpose(1, 0, 2)


def halves_of(values, width):
    high = values.astype(BF)
    low = (values - high.astype(F32)).astype(BF)
    return jnp.concatenate([high.reshape(-1, width), low.reshape(-1, width)], axis=0)


def whole_of(halves, width):
    rows = halves.shape[0] // 2
    return (halves[:rows] + halves[rows:]).reshape(-1, width)


def make_local(z_size):
    def sum_z(values):
        parts = values.reshape(z_size, -1, values.shape[-1])
        mine = trade(parts, "z").astype(F32).sum(axis=0).astype(BF)
        return spread(mine, "z", z_size).reshape(values.shape)

    def add_z(values):
        step = 1
        while step < z_size:
            values = values + lax.ppermute(
                values, "z", tuple((k, k ^ step) for k in range(z_size))
            )
            step *= 2
        return values

    def layer_order(values):
        shaped = values.reshape(values.shape[:-1] + (z_size, 2, 2, -1))
        return jnp.swapaxes(shaped, -3, -2).reshape(values.shape)

    def local(
        hidden,
        mask_index,
        mask_count,
        mask_embed,
        norm_gains,
        caption,
        w_qkv,
        w_out,
        w_cross,
        w_cross_out,
        w_text,
        w_up,
        w_down,
        cotangent,
    ):
        images, local_rows, width = hidden.shape
        full_length = mask_index.shape[1]
        rank = lax.axis_index("x") * 2 + lax.axis_index("y")
        core = lax.axis_index("c")
        tokens = images * local_rows
        group = width // 4
        text_width = caption.shape[1]

        unit = width // (4 * z_size)
        inside = unit % 128 == 0
        order = [4 * k + j for k in range(z_size) for j in (0, 2, 1, 3)] if inside else None

        def outer(values):
            return values if inside else layer_order(values)

        w_qkv, w_cross = w_qkv.transpose(1, 0, 2), w_cross.transpose(1, 0, 2)
        first = swap_parts(pick_weights(w_qkv, w_out, rank))
        first = gather_rows(place(first, rank))

        positions = lax.axis_index("y") * local_rows + jnp.arange(local_rows, dtype=jnp.int32)
        ranks = jnp.arange(full_length, dtype=jnp.int32)
        matches = (mask_index[:, :, None] == positions[None, None, :]) & (
            ranks[None, :, None] < mask_count[:, None, None]
        )
        masked = jnp.any(matches, axis=1).reshape(tokens, 1).astype(F32)
        gains = layer_order(norm_gains)
        gain_a, gain_b, gain_c = gains[:1], gains[1:2], gains[2:]
        start_x, attn_in, grad_top = start(
            outer(hidden.reshape(tokens, width)),
            outer(cotangent.reshape(tokens, width)),
            masked,
            layer_order(mask_embed)[None],
            gain_a,
            unit,
            order,
        )
        attn_in = gather_tokens(attn_in)
        mid = jnp.concatenate([column_blocks(w_cross[0], 4), column_blocks(w_cross_out, 4)], axis=2)
        up = column_blocks(w_up, 4)
        attn_in, mid, up = lax.optimization_barrier((attn_in, mid, up))
        mid, up = gather_rows(trade(mid)), gather_rows(trade(up))

        own_text, kv_part = text_forward(caption, w_text, w_cross)
        text_kv = trade(kv_part, PLANE).astype(F32).sum(axis=0).astype(BF)
        text_kv = sum_z(text_kv)
        other = swap(text_kv, "c")
        text_kv = jnp.concatenate(
            [jnp.where(core == 0, text_kv, other), jnp.where(core == 0, other, text_kv)], axis=0
        )
        attn_in, text_kv = lax.optimization_barrier((attn_in, text_kv))

        attn_in, projected = gather_mm(attn_in, first, 0, 3 * group, "qkv_mm")
        self_mixed = self_forward(projected, 2 * images)
        down = column_blocks(w_down, 4)
        self_mixed, down = lax.optimization_barrier((self_mixed, down))
        down = gather_rows(trade(down))
        parts = mm_scatter(self_mixed, first[:, 3 * group :])
        after_attn, cross_in = add_norm([start_x] + parts, gain_b)

        cross_in, cross_queries = gather_mm(gather_tokens(cross_in), mid, 0, group, "query_mm")
        cross_mixed = cross_forward(cross_queries, text_kv)
        parts = mm_scatter(cross_mixed, mid[:, group:])
        after_cross, mlp_in = add_norm([after_attn] + parts, gain_c)

        mlp_in = gather_tokens(mlp_in)
        mlp_in, grad_top = lax.optimization_barrier((mlp_in, grad_top))
        grad_y = jnp.concatenate(gather_tokens(grad_top), axis=0)
        mlp_in, activated, slope = feed_up(mlp_in, up)
        early = [attn_in, self_mixed, cross_in, cross_mixed]
        if inside:
            grad_axes, halves = "z", (core, z_size)

            def both(values):
                return [values, swap(values, "c")]

        else:
            grad_axes, halves = DATA, ()

            def both(values):
                return [values]

        early = [both(values) for values in early]
        down_part = grad_products([(both(grad_y), both(activated))], "down_grads", *halves)
        mlp_in = both(mlp_in)
        slope, down_part, early, mlp_in = lax.optimization_barrier((slope, down_part, early, mlp_in))
        down_rows = scatter_grad(down_part, grad_axes)
        grad_pre = feed_down(grad_y, slope, down)
        parts = mm_scatter(grad_pre, up)
        up_part = grad_products([(mlp_in, both(grad_pre))], "up_grads", *halves)
        grad_after_cross, cross_branch, gain_grad_c = norm_back(
            parts, grad_top, after_cross, gain_c
        )

        cross_branch = gather_tokens(cross_branch)
        cross_branch, up_part = lax.optimization_barrier((cross_branch, up_part))
        cross_branch, grad_cross_mixed = gather_mm(
            cross_branch, mid, group, group, "cross_out_back"
        )
        grad_cq, kv_grad = cross_back(cross_queries, text_kv, grad_cross_mixed)
        up_part, down_rows, kv_grad = lax.optimization_barrier((up_part, down_rows, kv_grad))
        up_rows = scatter_grad(up_part, grad_axes)
        cross_branch, grad_cq_both = both(cross_branch), both(grad_cq)
        parts = mm_scatter(grad_cq, mid[:, :group])
        grad_after_attn, attn_branch, gain_grad_b = norm_back(
            parts, grad_after_cross, after_attn, gain_b
        )

        activated, attn_branch = lax.optimization_barrier((activated, attn_branch))
        result = mm_t(activated, down).astype(BF)
        attn_branch, result = lax.optimization_barrier((gather_tokens(attn_branch), result))
        result = scatter_first(token_blocks(result))
        attn_branch, grad_self_mixed = gather_mm(attn_branch, first, 3 * group, group, "out_back")
        grad_projected = self_back(projected, grad_self_mixed, 2 * images)
        kv_part = kv_grad.astype(BF).reshape(2, z_size, -1, 2 * group)
        kv_part = kv_part.transpose(1, 0, 2, 3).reshape(2 * z_size, -1, 2 * group)
        grad_projected, result, kv_part = lax.optimization_barrier(
            (grad_projected, result, kv_part)
        )
        kv_part = trade(kv_part, DATA)
        result = scatter_second(result)
        rest_part = grad_products(
            [
                (early[0], both(grad_projected)),
                (both(attn_branch), early[1]),
                (early[2], grad_cq_both),
                (cross_branch, early[3]),
            ],
            "attention_grads",
            *halves,
        )
        grad_projected, result, kv_part, rest_part = lax.optimization_barrier(
            (grad_projected, result, kv_part, rest_part)
        )
        rest_part, up_rows = lax.optimization_barrier((rest_part, up_rows))
        rest_rows = scatter_grad(rest_part, grad_axes)
        parts = mm_scatter(grad_projected, first[:, : 3 * group])
        grad_hidden, gain_grad_a, mask_grad = last_back(
            parts,
            grad_after_attn,
            start_x,
            gain_a,
            masked,
            unit,
            order,
        )
        sums = jnp.concatenate([gain_grad_a, gain_grad_b, gain_grad_c, mask_grad], axis=0)


        kv_part = kv_part.astype(F32).sum(axis=0).astype(BF)
        kv_sum = spread(kv_part, "z", z_size).reshape(-1, 2 * group)
        kv_grads = spread(kv_sum, PLANE, 8)
        kv_weight_grad, grad_text_w, caption_part = text_back(
            kv_grads, own_text, w_cross, caption, w_text, halves_of(sums, text_width // 4)
        )
        half_context = caption.shape[0] // 2
        caption_part = trade(caption_part, PLANE)
        output = layer_output(after_cross, result, unit, order)
        caption_part, output, down_rows, up_rows = lax.optimization_barrier(
            (caption_part, output, down_rows, up_rows)
        )

        caption_part = caption_part.astype(F32).sum(axis=0)
        sums = layer_order(add_z(whole_of(caption_part[half_context:], width)))
        caption_part = caption_part[:half_context].astype(BF).reshape(z_size, -1, text_width // 4)
        caption_part = trade(caption_part, "z")
        down_parts = swap_parts(pick_rows([down_rows], rank))
        caption_part, down_parts, up_rows = lax.optimization_barrier(
            (caption_part, down_parts, up_rows)
        )

        caption_part = caption_part.astype(F32).sum(axis=0).astype(BF)
        caption_part = spread(caption_part, "z", z_size).reshape(half_context, -1)
        up_parts = swap_parts(pick_rows([up_rows], rank))
        down_grad = finish_wide(down_parts, rank)
        caption_part, up_parts, down_grad = lax.optimization_barrier(
            (caption_part, up_parts, down_grad)
        )

        caption_part = spread(caption_part)
        up_grad = finish_wide(up_parts, rank)
        caption_part, rest_rows, up_grad = lax.optimization_barrier(
            (caption_part, rest_rows, up_grad)
        )
        grad_caption = caption_output(caption_part, swap(caption_part, "c"), core)
        rest_rows = swap_parts(pick_rows([rest_rows], rank))
        grad_caption, rest_rows = lax.optimization_barrier((grad_caption, rest_rows))
        qkv_grad, out_grad, grad_cross, cross_out_grad = finish_all(
            rest_rows, kv_weight_grad, rank
        )
        return (
            outer(output).reshape(hidden.shape),
            outer(grad_hidden).reshape(hidden.shape),
            grad_caption,
            sums[:3],
            sums[3],
            qkv_grad.transpose(1, 0, 2),
            out_grad,
            grad_cross.transpose(1, 0, 2),
            cross_out_grad,
            grad_text_w,
            up_grad,
            down_grad,
        )

    return local


def solution(mesh):
    z_size = mesh.shape["img"] // 4
    inner = Mesh(mesh.devices.reshape(z_size, 2, 2, 2), ("z", "x", "c", "y"))
    image = ("z", "x", "c")
    tokens = P(image, "y", None)
    rows = P(image + ("y",))
    in_specs = (tokens, P(image, None), P(image), P(), P(), P()) + (rows,) * 7 + (tokens,)
    out_specs = (tokens, tokens, P(), P(), P()) + (rows,) * 7
    return jax.shard_map(
        make_local(z_size), mesh=inner, in_specs=in_specs, out_specs=out_specs, check_vma=False
    )
```

```python
import math

import jax
import jax.numpy as jnp
from jax import lax
from jax.experimental import pallas as pl
from jax.experimental.pallas import tpu as pltpu
from jax.sharding import Mesh
from jax.sharding import PartitionSpec as P

HD = 128
EPS = 1e-05
BF = jnp.bfloat16
F32 = jnp.float32
PAIR = ((0, 1), (1, 0))
GROUP = ("x", "y")
DATA = ("z", "c")
PLANE = ("x", "c", "y")
VMEM = 48 * 1024 * 1024
SCALE = 1.0 / math.sqrt(HD)
SLOPE = math.sqrt(2.0 / math.pi)
CUBIC = 0.044715


def dot(a, b, dims):
    return lax.dot_general(a, b, (dims, ((), ())), preferred_element_type=F32)


def mm(a, b):
    return dot(a, b, ((1,), (0,)))


def mm_t(a, b):
    return dot(a, b, ((1,), (1,)))


def t_mm(a, b):
    return dot(a, b, ((0,), (0,)))


def shape(dims, dtype=BF):
    return jax.ShapeDtypeStruct(dims, dtype)


def swap(values, axis):
    return lax.ppermute(values, axis, PAIR)


def trade(blocks, axes=GROUP):
    return lax.all_to_all(blocks, axes, 0, 0, tiled=True)


def spread(values, axes=GROUP, count=4):
    return trade(jnp.broadcast_to(values[None], (count,) + values.shape), axes)


def gather_tokens(own):
    half = own.shape[0] // 2
    from_x = swap(own, "x")
    from_y = swap(own, "y")
    return own, from_y, from_x, swap(from_x[:half], "y"), swap(from_y[half:], "x")


def gather_beside(own, work):
    half = own.shape[0] // 2
    from_x, from_y, work = lax.optimization_barrier((swap(own, "x"), swap(own, "y"), work))
    return (own, from_y, from_x, swap(from_x[:half], "y"), swap(from_y[half:], "x")), work


def scatter_first(parts):
    own, for_y, for_x, for_low, for_high = parts
    half = for_low.shape[0]
    low = swap(for_low, "y").astype(F32) + for_x[:half].astype(F32)
    high = swap(for_high, "x").astype(F32) + for_y[half:].astype(F32)
    return (
        own,
        jnp.concatenate([low.astype(BF), for_x[half:]], axis=0),
        jnp.concatenate([for_y[:half], high.astype(BF)], axis=0),
    )


def scatter_second(parts):
    own, for_x, for_y = parts
    return [own, swap(for_x, "x"), swap(for_y, "y")]


def scatter_tokens(parts):
    return scatter_second(scatter_first(parts))


def swap_parts(parts):
    return [
        parts[0],
        swap(parts[1], "y"),
        swap(parts[2], "x"),
        lax.ppermute(parts[3], GROUP, ((0, 3), (1, 2), (2, 1), (3, 0))),
    ]


def gather_rows(rows):
    return lax.all_gather(rows.reshape(-1, rows.shape[-1]), DATA, axis=0, tiled=True)


def scatter_grad(partial, axes):
    summed = lax.psum_scatter(partial, axes, scatter_dimension=0, tiled=True)
    return summed.reshape(4, -1, summed.shape[-1])


def call(kernel, grid, in_specs, out_specs, out_shape, operands, name, flops=0, size=1 << 22,
         rank=None, scratch=()):
    options = dict(
        out_shape=out_shape,
        compiler_params=pltpu.CompilerParams(vmem_limit_bytes=VMEM),
        cost_estimate=pl.CostEstimate(flops=flops, bytes_accessed=size, transcendentals=0),
        name=name,
    )
    if rank is None:
        return pl.pallas_call(
            kernel, grid=grid, in_specs=in_specs, out_specs=out_specs, scratch_shapes=scratch,
            **options,
        )(*operands)
    spec = pltpu.PrefetchScalarGridSpec(
        num_scalar_prefetch=1,
        grid=grid,
        in_specs=in_specs,
        out_specs=out_specs,
        scratch_shapes=scratch,
    )
    return pl.pallas_call(kernel, grid_spec=spec, **options)(rank.reshape(1), *operands)


def whole(array):
    return pl.BlockSpec(array.shape, lambda *_: (0,) * len(array.shape))


def reorder(values, unit, order):
    if order is None:
        return values
    return jnp.concatenate([values[:, k * unit : (k + 1) * unit] for k in order], axis=1)


def assemble(target, pieces, sems):
    copies, at = [], 0
    for k, piece in enumerate(pieces):
        rows = piece.shape[0]
        copies.append(pltpu.make_async_copy(piece, target.at[at : at + rows], sems.at[k]))
        at += rows
    for copy in copies:
        copy.start()
    for copy in copies:
        copy.wait()


ANY = pl.BlockSpec(memory_space=pl.ANY)


def gather_mm(pieces, weight, first, columns, name):
    rows, width = pieces[0].shape
    step = 256

    def kernel(*refs):
        tokens, out, sems = refs[6:]

        @pl.when(pl.program_id(0) == 0)
        def _():
            assemble(tokens, refs[:5], sems)

        out[...] = mm(tokens[...], refs[5][...]).astype(BF)

    return call(
        kernel,
        (columns // step,),
        [ANY] * 5 + [pl.BlockSpec((width, step), lambda j: (0, first // step + j))],
        [
            pl.BlockSpec((4 * rows, width), lambda j: (0, 0)),
            pl.BlockSpec((4 * rows, step), lambda j: (0, j)),
        ],
        [shape((4 * rows, width)), shape((4 * rows, columns))],
        [*pieces, weight],
        name,
        flops=8 * rows * width * columns,
        size=2 * width * (columns + 8 * rows),
        scratch=[pltpu.SemaphoreType.DMA((5,))],
    )


def mm_scatter(values, weight):
    return scatter_tokens(token_blocks(mm_t(values, weight).astype(BF)))


def token_blocks(partial):
    rows = partial.shape[0] // 4
    cuts = [0, rows, 2 * rows, 3 * rows, 3 * rows + rows // 2, 4 * rows]
    return [partial[a:b] for a, b in zip(cuts, cuts[1:])]


def normalize(values):
    centred = values - jnp.mean(values, axis=-1, keepdims=True)
    inv_std = lax.rsqrt(jnp.mean(centred * centred, axis=-1, keepdims=True) + EPS)
    return centred * inv_std, inv_std


NORM_ROWS = 32


def row_spec(array, at=None):
    width = array.shape[-1]
    if at is None:
        return pl.BlockSpec((NORM_ROWS, width), lambda i: (i, 0))
    return pl.BlockSpec((1, NORM_ROWS, width), lambda i, at=at: (at, i, 0))


def terms_of(terms):
    arrays, specs = [], []
    for term in terms:
        array, at = term if isinstance(term, tuple) else (term, None)
        arrays.append(array)
        specs.append(row_spec(array, at))
    return arrays, specs


def total_of(refs):
    values = [ref[0] if len(ref.shape) == 3 else ref[...] for ref in refs]
    return sum(value.astype(F32) for value in values)


def add_norm(terms, gain):
    arrays, specs = terms_of(terms)
    tokens, width = arrays[0].shape[-2], arrays[0].shape[-1]
    tokens = min(a.shape[-2] for a in arrays)

    def kernel(*refs):
        gain_ref, x, out = refs[-3:]
        values = total_of(refs[:-3])
        x[...] = values
        out[...] = (normalize(values)[0] * gain_ref[...]).astype(BF)

    return call(
        kernel,
        (tokens // NORM_ROWS,),
        specs + [whole(gain)],
        [row_spec(shape((tokens, width)))] * 2,
        [shape((tokens, width), F32), shape((tokens, width))],
        [*arrays, gain],
        "add_norm",
    )


def norm_grad(grad, values, gain):
    normed, inv_std = normalize(values)
    scaled = grad * gain
    first_mean = jnp.mean(scaled, axis=-1, keepdims=True)
    second_mean = jnp.mean(scaled * normed, axis=-1, keepdims=True)
    return (
        inv_std * (scaled - first_mean - normed * second_mean),
        jnp.sum(grad * normed, axis=0, keepdims=True),
    )


def accumulate(ref, value):
    @pl.when(pl.program_id(0) == 0)
    def _():
        ref[...] = jnp.zeros_like(ref)

    ref[...] += value


def norm_back(terms, upper, values, gain):
    arrays, specs = terms_of(terms)
    tokens, width = values.shape

    def kernel(*refs):
        upper_ref, x, gain_ref, out, out_low, gain_grad = refs[-6:]
        back, part = norm_grad(total_of(refs[:-6]), x[...], gain_ref[...])
        result = upper_ref[...].astype(F32) + back
        out[...] = result
        out_low[...] = result.astype(BF)
        accumulate(gain_grad, part)

    return call(
        kernel,
        (tokens // NORM_ROWS,),
        specs + [row_spec(upper), row_spec(values), whole(gain)],
        [row_spec(values)] * 2 + [pl.BlockSpec((1, width), lambda i: (0, 0))],
        [shape((tokens, width), F32), shape((tokens, width)), shape((1, width), F32)],
        [*arrays, upper, values, gain],
        "norm_back",
    )


def last_back(terms, upper, values, gain, masked, unit, order):
    arrays, specs = terms_of(terms)
    tokens, width = values.shape

    def kernel(*refs):
        upper_ref, x, gain_ref, mask, out, gain_grad, mask_grad = refs[-7:]
        back, part = norm_grad(total_of(refs[:-7]), x[...], gain_ref[...])
        result = upper_ref[...].astype(F32) + back
        hit = mask[...] > 0.5
        out[...] = reorder(jnp.where(hit, 0.0, result).astype(BF), unit, order)
        accumulate(gain_grad, part)
        accumulate(mask_grad, jnp.sum(jnp.where(hit, result, 0.0), axis=0, keepdims=True))

    line = pl.BlockSpec((1, width), lambda i: (0, 0))
    return call(
        kernel,
        (tokens // NORM_ROWS,),
        specs + [row_spec(upper), row_spec(values), whole(gain), row_spec(masked)],
        [row_spec(values), line, line],
        [shape((tokens, width)), shape((1, width), F32), shape((1, width), F32)],
        [*arrays, upper, values, gain, masked],
        "last_back",
    )


def start(hidden, cotangent, masked, embed, gain, unit, order):
    tokens, width = hidden.shape

    def kernel(hid, cot, mask, embed_ref, gain_ref, x, out, grad):
        hit = mask[...] > 0.5
        values = jnp.where(
            hit, embed_ref[...], reorder(hid[...], unit, order).astype(F32)
        )
        x[...] = values
        out[...] = (normalize(values)[0] * gain_ref[...]).astype(BF)
        grad[...] = jnp.where(hit, reorder(cot[...], unit, order).astype(F32), 0.0).astype(BF)

    rows = row_spec(hidden)
    return call(
        kernel,
        (tokens // NORM_ROWS,),
        [rows, rows, row_spec(masked), whole(embed), whole(gain)],
        [rows] * 3,
        [shape((tokens, width), F32), shape((tokens, width)), shape((tokens, width))],
        [hidden, cotangent, masked, embed, gain],
        "start",
    )


def layer_output(upper, terms, unit, order):
    arrays, specs = terms_of(terms)
    tokens, width = upper.shape

    def kernel(*refs):
        values = refs[-2][...] + total_of(refs[:-2])
        refs[-1][...] = reorder(values.astype(BF), unit, order)

    return call(
        kernel,
        (tokens // NORM_ROWS,),
        specs + [row_spec(upper)],
        row_spec(upper),
        shape((tokens, width)),
        [*arrays, upper],
        "layer_output",
    )


def feed_up(pieces, weight):
    rows, width = pieces[0].shape
    hidden = weight.shape[1]
    step = 256

    def kernel(*refs):
        up, tokens, act, slope, sems = refs[5:]

        @pl.when(pl.program_id(0) == 0)
        def _():
            assemble(tokens, refs[:5], sems)

        u = mm(tokens[...], up[...])
        square = u * u
        bend = jnp.tanh(SLOPE * u * (1.0 + CUBIC * square))
        half = 0.5 * (1.0 + bend)
        act[...] = (u * half).astype(BF)
        slope[...] = half + 0.5 * u * (1.0 - bend * bend) * SLOPE * (1.0 + 3.0 * CUBIC * square)

    part = pl.BlockSpec((4 * rows, step), lambda j: (0, j))
    return call(
        kernel,
        (hidden // step,),
        [ANY] * 5 + [pl.BlockSpec((width, step), lambda j: (0, j))],
        [pl.BlockSpec((4 * rows, width), lambda j: (0, 0)), part, part],
        [shape((4 * rows, width)), shape((4 * rows, hidden)), shape((4 * rows, hidden), F32)],
        [*pieces, weight],
        "feed_up",
        scratch=[pltpu.SemaphoreType.DMA((5,))],
        flops=8 * rows * width * hidden,
        size=2 * width * (hidden + 8 * rows),
    )


def feed_down(grad_y, slope, weight):
    tokens, width = grad_y.shape
    hidden = weight.shape[1]
    step = 256

    def kernel(dy, slope_ref, down, out):
        out[...] = (mm(dy[...], down[...]) * slope_ref[...]).astype(BF)

    part = pl.BlockSpec((tokens, step), lambda j: (0, j))
    return call(
        kernel,
        (hidden // step,),
        [whole(grad_y), part, pl.BlockSpec((width, step), lambda j: (0, j))],
        part,
        shape((tokens, hidden)),
        [grad_y, slope, weight],
        "feed_down",
        flops=2 * tokens * width * hidden,
        size=2 * width * (hidden + 8 * tokens),
    )


def softmax(scores):
    exp_terms = jnp.exp(scores - jnp.max(scores, axis=-1, keepdims=True))
    return exp_terms / jnp.sum(exp_terms, axis=-1, keepdims=True)


def score_grad(probs, grad_probs):
    return (
        probs * (grad_probs - jnp.sum(probs * grad_probs, axis=-1, keepdims=True))
    ).astype(BF)


def head(ref, k):
    return ref[:, k * HD : (k + 1) * HD]


def self_forward(projected, images):
    tokens, width = projected.shape
    rows, group = tokens // images, width // 3
    heads = group // HD

    def kernel(proj, mixed):
        for k in range(heads):
            query, key, value = (head(proj, j * heads + k) for j in range(3))
            probs = softmax(mm_t(query, key) * SCALE).astype(BF)
            mixed[:, k * HD : (k + 1) * HD] = mm(probs, value).astype(BF)

    return call(
        kernel,
        (images,),
        [pl.BlockSpec((rows, width), lambda i: (i, 0))],
        pl.BlockSpec((rows, group), lambda i: (i, 0)),
        shape((tokens, group)),
        [projected],
        "self_forward",
        flops=4 * tokens * rows * group,
    )


def self_back(projected, grad_mixed, images):
    tokens, width = projected.shape
    rows, group = tokens // images, width // 3
    heads = group // HD

    def kernel(proj, grad, out):
        for k in range(heads):
            query, key, value = (head(proj, j * heads + k) for j in range(3))
            grad_head = head(grad, k)
            probs = softmax(mm_t(query, key) * SCALE)
            grad_scores = score_grad(probs, mm_t(grad_head, value))
            parts = (
                mm(grad_scores, key) * SCALE,
                t_mm(grad_scores, query) * SCALE,
                t_mm(probs.astype(BF), grad_head),
            )
            for j, part in enumerate(parts):
                at = (j * heads + k) * HD
                out[:, at : at + HD] = part.astype(BF)

    return call(
        kernel,
        (images,),
        [
            pl.BlockSpec((rows, width), lambda i: (i, 0)),
            pl.BlockSpec((rows, group), lambda i: (i, 0)),
        ],
        pl.BlockSpec((rows, width), lambda i: (i, 0)),
        shape((tokens, width)),
        [projected, grad_mixed],
        "self_back",
        flops=10 * tokens * rows * group,
    )


def cross_forward(queries, text_kv):
    tokens, group = queries.shape
    heads = group // HD

    def kernel(query, text, mixed):
        for k in range(heads):
            probs = softmax(mm_t(head(query, k), head(text, k)) * SCALE).astype(BF)
            mixed[:, k * HD : (k + 1) * HD] = mm(probs, head(text, heads + k)).astype(BF)

    return call(
        kernel,
        (1,),
        [whole(queries), whole(text_kv)],
        whole(queries),
        shape((tokens, group)),
        [queries, text_kv],
        "cross_forward",
        flops=4 * tokens * text_kv.shape[0] * group,
    )


def cross_back(queries, text_kv, grad_mixed):
    tokens, group = queries.shape
    context = text_kv.shape[0]
    heads = group // HD

    def kernel(query, text, grad, grad_query, grad_text):
        for k in range(heads):
            query_head, key, value = head(query, k), head(text, k), head(text, heads + k)
            grad_head = head(grad, k)
            probs = softmax(mm_t(query_head, key) * SCALE)
            grad_scores = score_grad(probs, mm_t(grad_head, value))
            grad_query[:, k * HD : (k + 1) * HD] = (mm(grad_scores, key) * SCALE).astype(BF)
            at = (heads + k) * HD
            grad_text[:, k * HD : (k + 1) * HD] = t_mm(grad_scores, query_head) * SCALE
            grad_text[:, at : at + HD] = t_mm(probs.astype(BF), grad_head)

    return call(
        kernel,
        (1,),
        [whole(queries), whole(text_kv), whole(grad_mixed)],
        [whole(queries), whole(text_kv)],
        [shape((tokens, group)), shape((context, 2 * group), F32)],
        [queries, text_kv, grad_mixed],
        "cross_back",
        flops=10 * tokens * context * group,
    )


def grad_products(pairs, name, core=None, blocks=0):
    count_in = len(pairs[0][0])
    tokens, width = pairs[0][0][0].shape
    widths = [y[0].shape[1] for _, y in pairs]
    total = sum(widths)
    rows = 256 if core is None else width // (2 * blocks)
    steps = width // rows if core is None else blocks
    step = 512
    count = len(pairs) * count_in

    def kernel(r, *refs):
        out = refs[2 * count]
        offset = 0
        for k, wide in enumerate(widths):
            left = [refs[k * count_in + b][...].T for b in range(count_in)]
            for at in range(0, wide, step):
                out[:, offset + at : offset + at + step] = sum(
                    mm(left[b], refs[count + k * count_in + b][:, at : at + step])
                    for b in range(count_in)
                ).astype(BF)
            offset += wide

    pick = (lambda i, r: (0, i)) if core is None else (lambda i, r: (0, 2 * i + r[0]))
    return call(
        kernel,
        (steps,),
        [pl.BlockSpec((tokens, rows), pick)] * count
        + [pl.BlockSpec((tokens, w), lambda i, r: (0, 0)) for w in widths for _ in range(count_in)],
        pl.BlockSpec((rows, total), lambda i, r: (i, 0)),
        shape((steps * rows, total)),
        [b for x, _ in pairs for b in x] + [b for _, y in pairs for b in y],
        name,
        flops=2 * tokens * count_in * steps * rows * total,
        size=4 * width * total,
        rank=jnp.zeros((), jnp.int32) if core is None else core,
    )


def pick_weights(three, one, rank):
    rows, width = one.shape[0], one.shape[1] // 4

    def kernel(r, three_ref, one_ref, *outs):
        for k in range(4):

            @pl.when(pl.program_id(0) == k)
            def _():
                for j in range(3):
                    outs[k][:, j * width : (j + 1) * width] = three_ref[j]
                outs[k][:, 3 * width :] = one_ref[...]

    outs = [shape((rows, 4 * width))] * 4
    return call(
        kernel,
        (4,),
        [
            pl.BlockSpec((3, rows, width), lambda k, r: (0, 0, k ^ r[0])),
            pl.BlockSpec((rows, width), lambda k, r: (0, k ^ r[0])),
        ],
        [whole(a) for a in outs],
        outs,
        [three, one],
        "pick_weights",
        rank=rank,
    )


def pick_rows(arrays, rank):
    rows = arrays[0].shape[1]
    widths = [a.shape[2] for a in arrays]
    count = len(arrays)

    def kernel(r, *refs):
        for k in range(4):

            @pl.when(pl.program_id(0) == k)
            def _():
                at = 0
                for ref, width in zip(refs, widths):
                    refs[count + k][:, at : at + width] = ref[0]
                    at += width

    outs = [shape((rows, sum(widths)))] * 4
    return call(
        kernel,
        (4,),
        [pl.BlockSpec((1, rows, w), lambda k, r: (k ^ r[0], 0, 0)) for w in widths],
        [whole(a) for a in outs],
        outs,
        arrays,
        "pick_rows",
        rank=rank,
    )


def place(parts, rank):
    def kernel(r, *refs):
        for k in range(4):

            @pl.when(pl.program_id(0) == k)
            def _():
                refs[4][0] = refs[k][...]

    rows, columns = parts[0].shape
    return call(
        kernel,
        (4,),
        [whole(p) for p in parts],
        pl.BlockSpec((1, rows, columns), lambda k, r: (k ^ r[0], 0, 0)),
        shape((4, rows, columns)),
        parts,
        "place",
        rank=rank,
    )


def finish_wide(parts, rank):
    rows, width = parts[0].shape

    def kernel(r, *refs):
        for k in range(4):

            @pl.when(pl.program_id(0) == k)
            def _():
                refs[4][...] = refs[k][...].astype(F32)

    return call(
        kernel,
        (4,),
        [whole(p) for p in parts],
        pl.BlockSpec((rows, width), lambda k, r: (0, k ^ r[0])),
        shape((rows, 4 * width), F32),
        parts,
        "finish_wide",
        rank=rank,
    )


def finish_all(parts, text_grad, rank):
    rows, total = parts[0].shape
    width = total // 6

    def kernel(r, *refs):
        key, value, three, out, cross, cross_out = refs[4:]
        for k in range(4):

            @pl.when(pl.program_id(0) == k)
            def _():
                def part(j):
                    return refs[k][:, j * width : (j + 1) * width].astype(F32)

                for j in range(3):
                    three[j] = part(j)
                out[...] = part(3)
                cross[0] = part(4)
                cross_out[...] = part(5)

        cross[1] = key[...]
        cross[2] = value[...]

    wide = pl.BlockSpec((3, rows, width), lambda k, r: (0, 0, k ^ r[0]))
    flat = pl.BlockSpec((rows, width), lambda k, r: (0, k ^ r[0]))
    return call(
        kernel,
        (4,),
        [whole(p) for p in parts]
        + [flat, pl.BlockSpec((rows, width), lambda k, r: (0, 4 + (k ^ r[0])))],
        [wide, flat, wide, flat],
        [shape((3, rows, 4 * width), F32), shape((rows, 4 * width), F32)] * 2,
        [*parts, text_grad, text_grad],
        "finish_all",
        rank=rank,
    )


def plane_block(k):
    return (k >> 1) & 1, (k >> 2) * 2 + (k & 1)


def text_forward(caption, w_text, w_cross):
    context, rows = caption.shape[0], w_text.shape[0]
    half, width = context // 2, w_cross.shape[2] // 4

    def kernel(cap, weight, cross, own, blocks):
        own[...] = mm_t(cap[...], weight[...]).astype(BF)
        for j in range(2):
            part = mm(own[...], cross[1 + j]).astype(BF)
            for k in range(8):
                core, group = plane_block(k)
                blocks[k, :, j * width : (j + 1) * width] = part[
                    core * half : (core + 1) * half, group * width : (group + 1) * width
                ]

    return call(
        kernel,
        (1,),
        [whole(caption), whole(w_text), whole(w_cross)],
        [
            pl.BlockSpec((context, rows), lambda i: (0, 0)),
            pl.BlockSpec((8, half, 2 * width), lambda i: (0, 0, 0)),
        ],
        [shape((context, rows)), shape((8, half, 2 * width))],
        [caption, w_text, w_cross],
        "text_forward",
    )


def text_back(blocks, own_text, w_cross, caption, w_text, extra):
    context, rows = own_text.shape
    half, width = context // 2, w_cross.shape[2] // 4
    wide = caption.shape[1] // 4
    tail = extra.shape[0]

    def kernel(block, own, cross, cap, weight, more, kv_grad, text_grad, out, grads):
        for k in range(8):
            core, group = plane_block(k)
            for j in range(2):
                at = (4 * j + group) * width
                grads[core * half : (core + 1) * half, at : at + width] = block[
                    k, :, j * width : (j + 1) * width
                ]
        kv_grad[...] = t_mm(own[...], grads[...])
        grad_text = sum(
            mm_t(grads[:, 4 * j * width : 4 * (j + 1) * width], cross[1 + j]) for j in range(2)
        ).astype(BF)
        text_grad[...] = t_mm(grad_text, cap[...])
        part = mm(grad_text, weight[...]).astype(BF)
        for k in range(8):
            core, group = plane_block(k)
            out[k, :half, :] = part[core * half : (core + 1) * half, group * wide : (group + 1) * wide]
            out[k, half:, :] = more[...]

    operands = [blocks, own_text, w_cross, caption, w_text, extra]
    outs = [
        shape((rows, 8 * width), F32),
        shape((rows, 4 * wide), F32),
        shape((8, half + tail, wide)),
    ]
    return call(
        kernel,
        (1,),
        [whole(a) for a in operands],
        [whole(a) for a in outs],
        outs,
        operands,
        "text_back",
        scratch=[pltpu.VMEM((context, 8 * width), BF)],
    )


def caption_output(own, other, core):
    count, half, wide = own.shape

    def kernel(r, own_ref, other_ref, out):
        block = jnp.where(pl.program_id(0) == r[0], own_ref[0], other_ref[0])
        out[...] = block.astype(F32)

    block = pl.BlockSpec((1, half, wide), lambda i, k, r: (k, 0, 0))
    return call(
        kernel,
        (2, count),
        [block, block],
        pl.BlockSpec((half, wide), lambda i, k, r: (i, k)),
        shape((2 * half, 4 * wide), F32),
        [own, other],
        "caption_output",
        rank=core,
    )


def column_blocks(weight, count):
    rows = weight.shape[0]
    return weight.reshape(rows, count, -1).transpose(1, 0, 2)


def halves_of(values, width):
    high = values.astype(BF)
    low = (values - high.astype(F32)).astype(BF)
    return jnp.concatenate([high.reshape(-1, width), low.reshape(-1, width)], axis=0)


def whole_of(halves, width):
    rows = halves.shape[0] // 2
    return (halves[:rows] + halves[rows:]).reshape(-1, width)


def make_local(z_size):
    def sum_z(values):
        parts = values.reshape(z_size, -1, values.shape[-1])
        mine = trade(parts, "z").astype(F32).sum(axis=0).astype(BF)
        return spread(mine, "z", z_size).reshape(values.shape)

    def add_z(values):
        step = 1
        while step < z_size:
            values = values + lax.ppermute(
                values, "z", tuple((k, k ^ step) for k in range(z_size))
            )
            step *= 2
        return values

    def layer_order(values):
        shaped = values.reshape(values.shape[:-1] + (z_size, 2, 2, -1))
        return jnp.swapaxes(shaped, -3, -2).reshape(values.shape)

    def local(
        hidden,
        mask_index,
        mask_count,
        mask_embed,
        norm_gains,
        caption,
        w_qkv,
        w_out,
        w_cross,
        w_cross_out,
        w_text,
        w_up,
        w_down,
        cotangent,
    ):
        images, local_rows, width = hidden.shape
        full_length = mask_index.shape[1]
        rank = lax.axis_index("x") * 2 + lax.axis_index("y")
        core = lax.axis_index("c")
        tokens = images * local_rows
        group = width // 4
        text_width = caption.shape[1]

        unit = width // (4 * z_size)
        inside = unit % 128 == 0
        order = [4 * k + j for k in range(z_size) for j in (0, 2, 1, 3)] if inside else None

        def outer(values):
            return values if inside else layer_order(values)

        w_qkv, w_cross = w_qkv.transpose(1, 0, 2), w_cross.transpose(1, 0, 2)
        first = swap_parts(pick_weights(w_qkv, w_out, rank))
        first = gather_rows(place(first, rank))

        positions = lax.axis_index("y") * local_rows + jnp.arange(local_rows, dtype=jnp.int32)
        ranks = jnp.arange(full_length, dtype=jnp.int32)
        matches = (mask_index[:, :, None] == positions[None, None, :]) & (
            ranks[None, :, None] < mask_count[:, None, None]
        )
        masked = jnp.any(matches, axis=1).reshape(tokens, 1).astype(F32)
        gains = layer_order(norm_gains)
        gain_a, gain_b, gain_c = gains[:1], gains[1:2], gains[2:]
        start_x, attn_in, grad_top = start(
            outer(hidden.reshape(tokens, width)),
            outer(cotangent.reshape(tokens, width)),
            masked,
            layer_order(mask_embed)[None],
            gain_a,
            unit,
            order,
        )
        attn_in = gather_tokens(attn_in)
        mid = jnp.concatenate([column_blocks(w_cross[0], 4), column_blocks(w_cross_out, 4)], axis=2)
        up = column_blocks(w_up, 4)
        attn_in, mid, up = lax.optimization_barrier((attn_in, mid, up))
        mid, up = gather_rows(trade(mid)), gather_rows(trade(up))

        own_text, kv_part = text_forward(caption, w_text, w_cross)
        text_kv = trade(kv_part, PLANE).astype(F32).sum(axis=0).astype(BF)
        text_kv = sum_z(text_kv)
        other = swap(text_kv, "c")
        text_kv = jnp.concatenate(
            [jnp.where(core == 0, text_kv, other), jnp.where(core == 0, other, text_kv)], axis=0
        )
        attn_in, text_kv = lax.optimization_barrier((attn_in, text_kv))

        attn_in, projected = gather_mm(attn_in, first, 0, 3 * group, "qkv_mm")
        self_mixed = self_forward(projected, 2 * images)
        down = column_blocks(w_down, 4)
        self_mixed, down = lax.optimization_barrier((self_mixed, down))
        down = gather_rows(trade(down))
        parts = mm_scatter(self_mixed, first[:, 3 * group :])
        after_attn, cross_in = add_norm([start_x] + parts, gain_b)

        cross_in, cross_queries = gather_mm(gather_tokens(cross_in), mid, 0, group, "query_mm")
        cross_mixed = cross_forward(cross_queries, text_kv)
        parts = mm_scatter(cross_mixed, mid[:, group:])
        after_cross, mlp_in = add_norm([after_attn] + parts, gain_c)

        mlp_in = gather_tokens(mlp_in)
        mlp_in, grad_top = lax.optimization_barrier((mlp_in, grad_top))
        grad_y = jnp.concatenate(gather_tokens(grad_top), axis=0)
        mlp_in, activated, slope = feed_up(mlp_in, up)
        early = [attn_in, self_mixed, cross_in, cross_mixed]
        if inside:
            grad_axes, halves = "z", (core, z_size)

            def both(values):
                return [values, swap(values, "c")]

        else:
            grad_axes, halves = DATA, ()

            def both(values):
                return [values]

        early = [both(values) for values in early]
        down_part = grad_products([(both(grad_y), both(activated))], "down_grads", *halves)
        mlp_in = both(mlp_in)
        slope, down_part, early, mlp_in = lax.optimization_barrier((slope, down_part, early, mlp_in))
        down_rows = scatter_grad(down_part, grad_axes)
        grad_pre = feed_down(grad_y, slope, down)
        parts = mm_scatter(grad_pre, up)
        up_part = grad_products([(mlp_in, both(grad_pre))], "up_grads", *halves)
        grad_after_cross, cross_branch, gain_grad_c = norm_back(
            parts, grad_top, after_cross, gain_c
        )

        cross_branch, up_part = gather_beside(cross_branch, up_part)
        cross_branch, grad_cross_mixed = gather_mm(
            cross_branch, mid, group, group, "cross_out_back"
        )
        grad_cq, kv_grad = cross_back(cross_queries, text_kv, grad_cross_mixed)
        up_part, down_rows, kv_grad = lax.optimization_barrier((up_part, down_rows, kv_grad))
        up_rows = scatter_grad(up_part, grad_axes)
        cross_branch, grad_cq_both = both(cross_branch), both(grad_cq)
        parts = mm_scatter(grad_cq, mid[:, :group])
        grad_after_attn, attn_branch, gain_grad_b = norm_back(
            parts, grad_after_cross, after_attn, gain_b
        )

        activated, attn_branch = lax.optimization_barrier((activated, attn_branch))
        result = mm_t(activated, down).astype(BF)
        attn_branch, result = gather_beside(attn_branch, result)
        attn_branch, result = lax.optimization_barrier((attn_branch, result))
        result = scatter_first(token_blocks(result))
        attn_branch, grad_self_mixed = gather_mm(attn_branch, first, 3 * group, group, "out_back")
        grad_projected = self_back(projected, grad_self_mixed, 2 * images)
        kv_part = kv_grad.astype(BF).reshape(2, z_size, -1, 2 * group)
        kv_part = kv_part.transpose(1, 0, 2, 3).reshape(2 * z_size, -1, 2 * group)
        grad_projected, result, kv_part = lax.optimization_barrier(
            (grad_projected, result, kv_part)
        )
        kv_part = trade(kv_part, DATA)
        result = scatter_second(result)
        rest_part = grad_products(
            [
                (early[0], both(grad_projected)),
                (both(attn_branch), early[1]),
                (early[2], grad_cq_both),
                (cross_branch, early[3]),
            ],
            "attention_grads",
            *halves,
        )
        grad_projected, result, kv_part, rest_part = lax.optimization_barrier(
            (grad_projected, result, kv_part, rest_part)
        )
        rest_part, up_rows = lax.optimization_barrier((rest_part, up_rows))
        rest_rows = scatter_grad(rest_part, grad_axes)
        parts = mm_scatter(grad_projected, first[:, : 3 * group])
        grad_hidden, gain_grad_a, mask_grad = last_back(
            parts,
            grad_after_attn,
            start_x,
            gain_a,
            masked,
            unit,
            order,
        )
        sums = jnp.concatenate([gain_grad_a, gain_grad_b, gain_grad_c, mask_grad], axis=0)


        kv_part = kv_part.astype(F32).sum(axis=0).astype(BF)
        kv_sum = spread(kv_part, "z", z_size).reshape(-1, 2 * group)
        kv_grads = spread(kv_sum, PLANE, 8)
        kv_weight_grad, grad_text_w, caption_part = text_back(
            kv_grads, own_text, w_cross, caption, w_text, halves_of(sums, text_width // 4)
        )
        half_context = caption.shape[0] // 2
        caption_part = trade(caption_part, PLANE)
        output = layer_output(after_cross, result, unit, order)
        caption_part, output, down_rows, up_rows = lax.optimization_barrier(
            (caption_part, output, down_rows, up_rows)
        )

        caption_part = caption_part.astype(F32).sum(axis=0)
        sums = layer_order(add_z(whole_of(caption_part[half_context:], width)))
        caption_part = caption_part[:half_context].astype(BF).reshape(z_size, -1, text_width // 4)
        caption_part = trade(caption_part, "z")
        down_parts = swap_parts(pick_rows([down_rows], rank))
        caption_part, down_parts, up_rows = lax.optimization_barrier(
            (caption_part, down_parts, up_rows)
        )

        caption_part = caption_part.astype(F32).sum(axis=0).astype(BF)
        caption_part = spread(caption_part, "z", z_size).reshape(half_context, -1)
        up_parts = swap_parts(pick_rows([up_rows], rank))
        down_grad = finish_wide(down_parts, rank)
        caption_part, up_parts, down_grad = lax.optimization_barrier(
            (caption_part, up_parts, down_grad)
        )

        caption_part = spread(caption_part)
        up_grad = finish_wide(up_parts, rank)
        caption_part, rest_rows, up_grad = lax.optimization_barrier(
            (caption_part, rest_rows, up_grad)
        )
        grad_caption = caption_output(caption_part, swap(caption_part, "c"), core)
        rest_rows = swap_parts(pick_rows([rest_rows], rank))
        grad_caption, rest_rows = lax.optimization_barrier((grad_caption, rest_rows))
        qkv_grad, out_grad, grad_cross, cross_out_grad = finish_all(
            rest_rows, kv_weight_grad, rank
        )
        return (
            outer(output).reshape(hidden.shape),
            outer(grad_hidden).reshape(hidden.shape),
            grad_caption,
            sums[:3],
            sums[3],
            qkv_grad.transpose(1, 0, 2),
            out_grad,
            grad_cross.transpose(1, 0, 2),
            cross_out_grad,
            grad_text_w,
            up_grad,
            down_grad,
        )

    return local


def solution(mesh):
    z_size = mesh.shape["img"] // 4
    inner = Mesh(mesh.devices.reshape(z_size, 2, 2, 2), ("z", "x", "c", "y"))
    image = ("z", "x", "c")
    tokens = P(image, "y", None)
    rows = P(image + ("y",))
    in_specs = (tokens, P(image, None), P(image), P(), P(), P()) + (rows,) * 7 + (tokens,)
    out_specs = (tokens, tokens, P(), P(), P()) + (rows,) * 7
    return jax.shard_map(
        make_local(z_size), mesh=inner, in_specs=in_specs, out_specs=out_specs, check_vma=False
    )
```

```python
import math

import jax
import jax.numpy as jnp
from jax import lax
from jax.experimental import pallas as pl
from jax.experimental.pallas import tpu as pltpu
from jax.sharding import Mesh
from jax.sharding import PartitionSpec as P

HD = 128
EPS = 1e-05
BF = jnp.bfloat16
F32 = jnp.float32
PAIR = ((0, 1), (1, 0))
GROUP = ("x", "y")
DATA = ("z", "c")
PLANE = ("x", "c", "y")
VMEM = 48 * 1024 * 1024
SCALE = 1.0 / math.sqrt(HD)
SLOPE = math.sqrt(2.0 / math.pi)
CUBIC = 0.044715


def dot(a, b, dims):
    return lax.dot_general(a, b, (dims, ((), ())), preferred_element_type=F32)


def mm(a, b):
    return dot(a, b, ((1,), (0,)))


def mm_t(a, b):
    return dot(a, b, ((1,), (1,)))


def t_mm(a, b):
    return dot(a, b, ((0,), (0,)))


def shape(dims, dtype=BF):
    return jax.ShapeDtypeStruct(dims, dtype)


def swap(values, axis):
    return lax.ppermute(values, axis, PAIR)


def trade(blocks, axes=GROUP):
    return lax.all_to_all(blocks, axes, 0, 0, tiled=True)


def spread(values, axes=GROUP, count=4):
    return trade(jnp.broadcast_to(values[None], (count,) + values.shape), axes)


def gather_tokens(own):
    half = own.shape[0] // 2
    from_x = swap(own, "x")
    from_y = swap(own, "y")
    return own, from_y, from_x, swap(from_x[:half], "y"), swap(from_y[half:], "x")


def gather_beside(own, work):
    half = own.shape[0] // 2
    from_x, from_y, work = lax.optimization_barrier((swap(own, "x"), swap(own, "y"), work))
    return (own, from_y, from_x, swap(from_x[:half], "y"), swap(from_y[half:], "x")), work


def scatter_first(parts):
    own, for_y, for_x, for_low, for_high = parts
    half = for_low.shape[0]
    low = swap(for_low, "y").astype(F32) + for_x[:half].astype(F32)
    high = swap(for_high, "x").astype(F32) + for_y[half:].astype(F32)
    return (
        own,
        jnp.concatenate([low.astype(BF), for_x[half:]], axis=0),
        jnp.concatenate([for_y[:half], high.astype(BF)], axis=0),
    )


def scatter_second(parts):
    own, for_x, for_y = parts
    return [own, swap(for_x, "x"), swap(for_y, "y")]


def scatter_tokens(parts):
    return scatter_second(scatter_first(parts))


def swap_parts(parts):
    return [
        parts[0],
        swap(parts[1], "y"),
        swap(parts[2], "x"),
        lax.ppermute(parts[3], GROUP, ((0, 3), (1, 2), (2, 1), (3, 0))),
    ]


def gather_rows(rows):
    return lax.all_gather(rows.reshape(-1, rows.shape[-1]), DATA, axis=0, tiled=True)


def scatter_grad(partial, axes):
    summed = lax.psum_scatter(partial, axes, scatter_dimension=0, tiled=True)
    return summed.reshape(4, -1, summed.shape[-1])


def call(kernel, grid, in_specs, out_specs, out_shape, operands, name, flops=0, size=1 << 22,
         rank=None, scratch=()):
    options = dict(
        out_shape=out_shape,
        compiler_params=pltpu.CompilerParams(vmem_limit_bytes=VMEM),
        cost_estimate=pl.CostEstimate(flops=flops, bytes_accessed=size, transcendentals=0),
        name=name,
    )
    if rank is None:
        return pl.pallas_call(
            kernel, grid=grid, in_specs=in_specs, out_specs=out_specs, scratch_shapes=scratch,
            **options,
        )(*operands)
    spec = pltpu.PrefetchScalarGridSpec(
        num_scalar_prefetch=1,
        grid=grid,
        in_specs=in_specs,
        out_specs=out_specs,
        scratch_shapes=scratch,
    )
    return pl.pallas_call(kernel, grid_spec=spec, **options)(rank.reshape(1), *operands)


def whole(array):
    return pl.BlockSpec(array.shape, lambda *_: (0,) * len(array.shape))


def reorder(values, unit, order):
    if order is None:
        return values
    return jnp.concatenate([values[:, k * unit : (k + 1) * unit] for k in order], axis=1)


def assemble(target, pieces, sems):
    copies, at = [], 0
    for k, piece in enumerate(pieces):
        rows = piece.shape[0]
        copies.append(pltpu.make_async_copy(piece, target.at[at : at + rows], sems.at[k]))
        at += rows
    for copy in copies:
        copy.start()
    for copy in copies:
        copy.wait()


ANY = pl.BlockSpec(memory_space=pl.ANY)


def gather_mm(pieces, weight, first, columns, name):
    rows, width = pieces[0].shape
    step = 256

    def kernel(*refs):
        tokens, out, sems = refs[6:]

        @pl.when(pl.program_id(0) == 0)
        def _():
            assemble(tokens, refs[:5], sems)

        out[...] = mm(tokens[...], refs[5][...]).astype(BF)

    return call(
        kernel,
        (columns // step,),
        [ANY] * 5 + [pl.BlockSpec((width, step), lambda j: (0, first // step + j))],
        [
            pl.BlockSpec((4 * rows, width), lambda j: (0, 0)),
            pl.BlockSpec((4 * rows, step), lambda j: (0, j)),
        ],
        [shape((4 * rows, width)), shape((4 * rows, columns))],
        [*pieces, weight],
        name,
        flops=8 * rows * width * columns,
        size=2 * width * (columns + 8 * rows),
        scratch=[pltpu.SemaphoreType.DMA((5,))],
    )


def mm_scatter(values, weight):
    return scatter_tokens(token_blocks(mm_t(values, weight).astype(BF)))


def token_blocks(partial):
    rows = partial.shape[0] // 4
    cuts = [0, rows, 2 * rows, 3 * rows, 3 * rows + rows // 2, 4 * rows]
    return [partial[a:b] for a, b in zip(cuts, cuts[1:])]


def normalize(values):
    centred = values - jnp.mean(values, axis=-1, keepdims=True)
    inv_std = lax.rsqrt(jnp.mean(centred * centred, axis=-1, keepdims=True) + EPS)
    return centred * inv_std, inv_std


NORM_ROWS = 32


def row_spec(array, at=None):
    width = array.shape[-1]
    if at is None:
        return pl.BlockSpec((NORM_ROWS, width), lambda i: (i, 0))
    return pl.BlockSpec((1, NORM_ROWS, width), lambda i, at=at: (at, i, 0))


def terms_of(terms):
    arrays, specs = [], []
    for term in terms:
        array, at = term if isinstance(term, tuple) else (term, None)
        arrays.append(array)
        specs.append(row_spec(array, at))
    return arrays, specs


def total_of(refs):
    values = [ref[0] if len(ref.shape) == 3 else ref[...] for ref in refs]
    return sum(value.astype(F32) for value in values)


def add_norm(terms, gain):
    arrays, specs = terms_of(terms)
    tokens, width = arrays[0].shape[-2], arrays[0].shape[-1]
    tokens = min(a.shape[-2] for a in arrays)

    def kernel(*refs):
        gain_ref, x, out = refs[-3:]
        values = total_of(refs[:-3])
        x[...] = values
        out[...] = (normalize(values)[0] * gain_ref[...]).astype(BF)

    return call(
        kernel,
        (tokens // NORM_ROWS,),
        specs + [whole(gain)],
        [row_spec(shape((tokens, width)))] * 2,
        [shape((tokens, width), F32), shape((tokens, width))],
        [*arrays, gain],
        "add_norm",
    )


def norm_grad(grad, values, gain):
    normed, inv_std = normalize(values)
    scaled = grad * gain
    first_mean = jnp.mean(scaled, axis=-1, keepdims=True)
    second_mean = jnp.mean(scaled * normed, axis=-1, keepdims=True)
    return (
        inv_std * (scaled - first_mean - normed * second_mean),
        jnp.sum(grad * normed, axis=0, keepdims=True),
    )


def accumulate(ref, value):
    @pl.when(pl.program_id(0) == 0)
    def _():
        ref[...] = jnp.zeros_like(ref)

    ref[...] += value


def norm_back(terms, upper, values, gain):
    arrays, specs = terms_of(terms)
    tokens, width = values.shape

    def kernel(*refs):
        upper_ref, x, gain_ref, out, out_low, gain_grad = refs[-6:]
        back, part = norm_grad(total_of(refs[:-6]), x[...], gain_ref[...])
        result = upper_ref[...].astype(F32) + back
        out[...] = result
        out_low[...] = result.astype(BF)
        accumulate(gain_grad, part)

    return call(
        kernel,
        (tokens // NORM_ROWS,),
        specs + [row_spec(upper), row_spec(values), whole(gain)],
        [row_spec(values)] * 2 + [pl.BlockSpec((1, width), lambda i: (0, 0))],
        [shape((tokens, width), F32), shape((tokens, width)), shape((1, width), F32)],
        [*arrays, upper, values, gain],
        "norm_back",
    )


def last_back(terms, upper, values, gain, masked, unit, order):
    arrays, specs = terms_of(terms)
    tokens, width = values.shape

    def kernel(*refs):
        upper_ref, x, gain_ref, mask, out, gain_grad, mask_grad = refs[-7:]
        back, part = norm_grad(total_of(refs[:-7]), x[...], gain_ref[...])
        result = upper_ref[...].astype(F32) + back
        hit = mask[...] > 0.5
        out[...] = reorder(jnp.where(hit, 0.0, result).astype(BF), unit, order)
        accumulate(gain_grad, part)
        accumulate(mask_grad, jnp.sum(jnp.where(hit, result, 0.0), axis=0, keepdims=True))

    line = pl.BlockSpec((1, width), lambda i: (0, 0))
    return call(
        kernel,
        (tokens // NORM_ROWS,),
        specs + [row_spec(upper), row_spec(values), whole(gain), row_spec(masked)],
        [row_spec(values), line, line],
        [shape((tokens, width)), shape((1, width), F32), shape((1, width), F32)],
        [*arrays, upper, values, gain, masked],
        "last_back",
    )


def start(hidden, cotangent, masked, embed, gain, unit, order):
    tokens, width = hidden.shape

    def kernel(hid, cot, mask, embed_ref, gain_ref, x, out, grad):
        hit = mask[...] > 0.5
        values = jnp.where(
            hit, embed_ref[...], reorder(hid[...], unit, order).astype(F32)
        )
        x[...] = values
        out[...] = (normalize(values)[0] * gain_ref[...]).astype(BF)
        grad[...] = jnp.where(hit, reorder(cot[...], unit, order).astype(F32), 0.0).astype(BF)

    rows = row_spec(hidden)
    return call(
        kernel,
        (tokens // NORM_ROWS,),
        [rows, rows, row_spec(masked), whole(embed), whole(gain)],
        [rows] * 3,
        [shape((tokens, width), F32), shape((tokens, width)), shape((tokens, width))],
        [hidden, cotangent, masked, embed, gain],
        "start",
    )


def layer_output(upper, terms, unit, order):
    arrays, specs = terms_of(terms)
    tokens, width = upper.shape

    def kernel(*refs):
        values = refs[-2][...] + total_of(refs[:-2])
        refs[-1][...] = reorder(values.astype(BF), unit, order)

    return call(
        kernel,
        (tokens // NORM_ROWS,),
        specs + [row_spec(upper)],
        row_spec(upper),
        shape((tokens, width)),
        [*arrays, upper],
        "layer_output",
    )


def feed_up(pieces, weight):
    rows, width = pieces[0].shape
    hidden = weight.shape[1]
    step = 256

    def kernel(*refs):
        up, tokens, act, slope, sems = refs[5:]

        @pl.when(pl.program_id(0) == 0)
        def _():
            assemble(tokens, refs[:5], sems)

        u = mm(tokens[...], up[...])
        square = u * u
        bend = jnp.tanh(SLOPE * u * (1.0 + CUBIC * square))
        half = 0.5 * (1.0 + bend)
        act[...] = (u * half).astype(BF)
        slope[...] = half + 0.5 * u * (1.0 - bend * bend) * SLOPE * (1.0 + 3.0 * CUBIC * square)

    part = pl.BlockSpec((4 * rows, step), lambda j: (0, j))
    return call(
        kernel,
        (hidden // step,),
        [ANY] * 5 + [pl.BlockSpec((width, step), lambda j: (0, j))],
        [pl.BlockSpec((4 * rows, width), lambda j: (0, 0)), part, part],
        [shape((4 * rows, width)), shape((4 * rows, hidden)), shape((4 * rows, hidden), F32)],
        [*pieces, weight],
        "feed_up",
        scratch=[pltpu.SemaphoreType.DMA((5,))],
        flops=8 * rows * width * hidden,
        size=2 * width * (hidden + 8 * rows),
    )


def feed_down(grad_y, slope, weight):
    tokens, width = grad_y.shape
    hidden = weight.shape[1]
    step = 256

    def kernel(dy, slope_ref, down, out):
        out[...] = (mm(dy[...], down[...]) * slope_ref[...]).astype(BF)

    part = pl.BlockSpec((tokens, step), lambda j: (0, j))
    return call(
        kernel,
        (hidden // step,),
        [whole(grad_y), part, pl.BlockSpec((width, step), lambda j: (0, j))],
        part,
        shape((tokens, hidden)),
        [grad_y, slope, weight],
        "feed_down",
        flops=2 * tokens * width * hidden,
        size=2 * width * (hidden + 8 * tokens),
    )


def softmax(scores):
    exp_terms = jnp.exp(scores - jnp.max(scores, axis=-1, keepdims=True))
    return exp_terms / jnp.sum(exp_terms, axis=-1, keepdims=True)


def score_grad(probs, grad_probs):
    return (
        probs * (grad_probs - jnp.sum(probs * grad_probs, axis=-1, keepdims=True))
    ).astype(BF)


def head(ref, k):
    return ref[:, k * HD : (k + 1) * HD]


def self_forward(projected, images):
    tokens, width = projected.shape
    rows, group = tokens // images, width // 3
    heads = group // HD

    def kernel(proj, mixed):
        for k in range(heads):
            query, key, value = (head(proj, j * heads + k) for j in range(3))
            probs = softmax(mm_t(query, key) * SCALE).astype(BF)
            mixed[:, k * HD : (k + 1) * HD] = mm(probs, value).astype(BF)

    return call(
        kernel,
        (images,),
        [pl.BlockSpec((rows, width), lambda i: (i, 0))],
        pl.BlockSpec((rows, group), lambda i: (i, 0)),
        shape((tokens, group)),
        [projected],
        "self_forward",
        flops=4 * tokens * rows * group,
    )


def self_back(projected, grad_mixed, images):
    tokens, width = projected.shape
    rows, group = tokens // images, width // 3
    heads = group // HD

    def kernel(proj, grad, out):
        for k in range(heads):
            query, key, value = (head(proj, j * heads + k) for j in range(3))
            grad_head = head(grad, k)
            probs = softmax(mm_t(query, key) * SCALE)
            grad_scores = score_grad(probs, mm_t(grad_head, value))
            parts = (
                mm(grad_scores, key) * SCALE,
                t_mm(grad_scores, query) * SCALE,
                t_mm(probs.astype(BF), grad_head),
            )
            for j, part in enumerate(parts):
                at = (j * heads + k) * HD
                out[:, at : at + HD] = part.astype(BF)

    return call(
        kernel,
        (images,),
        [
            pl.BlockSpec((rows, width), lambda i: (i, 0)),
            pl.BlockSpec((rows, group), lambda i: (i, 0)),
        ],
        pl.BlockSpec((rows, width), lambda i: (i, 0)),
        shape((tokens, width)),
        [projected, grad_mixed],
        "self_back",
        flops=10 * tokens * rows * group,
    )


def cross_forward(queries, text_kv):
    tokens, group = queries.shape
    heads = group // HD

    def kernel(query, text, mixed):
        for k in range(heads):
            probs = softmax(mm_t(head(query, k), head(text, k)) * SCALE).astype(BF)
            mixed[:, k * HD : (k + 1) * HD] = mm(probs, head(text, heads + k)).astype(BF)

    return call(
        kernel,
        (1,),
        [whole(queries), whole(text_kv)],
        whole(queries),
        shape((tokens, group)),
        [queries, text_kv],
        "cross_forward",
        flops=4 * tokens * text_kv.shape[0] * group,
    )


def cross_back(queries, text_kv, grad_mixed):
    tokens, group = queries.shape
    context = text_kv.shape[0]
    heads = group // HD

    def kernel(query, text, grad, grad_query, grad_text):
        for k in range(heads):
            query_head, key, value = head(query, k), head(text, k), head(text, heads + k)
            grad_head = head(grad, k)
            probs = softmax(mm_t(query_head, key) * SCALE)
            grad_scores = score_grad(probs, mm_t(grad_head, value))
            grad_query[:, k * HD : (k + 1) * HD] = (mm(grad_scores, key) * SCALE).astype(BF)
            at = (heads + k) * HD
            grad_text[:, k * HD : (k + 1) * HD] = t_mm(grad_scores, query_head) * SCALE
            grad_text[:, at : at + HD] = t_mm(probs.astype(BF), grad_head)

    return call(
        kernel,
        (1,),
        [whole(queries), whole(text_kv), whole(grad_mixed)],
        [whole(queries), whole(text_kv)],
        [shape((tokens, group)), shape((context, 2 * group), F32)],
        [queries, text_kv, grad_mixed],
        "cross_back",
        flops=10 * tokens * context * group,
    )


def grad_products(pairs, name, core=None, blocks=0):
    count_in = len(pairs[0][0])
    tokens, width = pairs[0][0][0].shape
    widths = [y[0].shape[1] for _, y in pairs]
    total = sum(widths)
    rows = 256 if core is None else width // (2 * blocks)
    steps = width // rows if core is None else blocks
    step = 512
    count = len(pairs) * count_in

    def kernel(r, *refs):
        out = refs[2 * count]
        offset = 0
        for k, wide in enumerate(widths):
            left = [refs[k * count_in + b][...].T for b in range(count_in)]
            for at in range(0, wide, step):
                out[:, offset + at : offset + at + step] = sum(
                    mm(left[b], refs[count + k * count_in + b][:, at : at + step])
                    for b in range(count_in)
                ).astype(BF)
            offset += wide

    pick = (lambda i, r: (0, i)) if core is None else (lambda i, r: (0, 2 * i + r[0]))
    return call(
        kernel,
        (steps,),
        [pl.BlockSpec((tokens, rows), pick)] * count
        + [pl.BlockSpec((tokens, w), lambda i, r: (0, 0)) for w in widths for _ in range(count_in)],
        pl.BlockSpec((rows, total), lambda i, r: (i, 0)),
        shape((steps * rows, total)),
        [b for x, _ in pairs for b in x] + [b for _, y in pairs for b in y],
        name,
        flops=2 * tokens * count_in * steps * rows * total,
        size=4 * width * total,
        rank=jnp.zeros((), jnp.int32) if core is None else core,
    )


def pick_weights(three, rank):
    rows, width = three.shape[1], three.shape[2] // 4

    def kernel(r, three_ref, *outs):
        for k in range(4):

            @pl.when(pl.program_id(0) == k)
            def _():
                for j in range(3):
                    outs[k][:, j * width : (j + 1) * width] = three_ref[j]

    outs = [shape((rows, 3 * width))] * 4
    return call(
        kernel,
        (4,),
        [pl.BlockSpec((3, rows, width), lambda k, r: (0, 0, k ^ r[0]))],
        [whole(a) for a in outs],
        outs,
        [three],
        "pick_weights",
        rank=rank,
    )


def pick_rows(arrays, rank):
    rows = arrays[0].shape[1]
    widths = [a.shape[2] for a in arrays]
    count = len(arrays)

    def kernel(r, *refs):
        for k in range(4):

            @pl.when(pl.program_id(0) == k)
            def _():
                at = 0
                for ref, width in zip(refs, widths):
                    refs[count + k][:, at : at + width] = ref[0]
                    at += width

    outs = [shape((rows, sum(widths)))] * 4
    return call(
        kernel,
        (4,),
        [pl.BlockSpec((1, rows, w), lambda k, r: (k ^ r[0], 0, 0)) for w in widths],
        [whole(a) for a in outs],
        outs,
        arrays,
        "pick_rows",
        rank=rank,
    )


def place(parts, rank):
    def kernel(r, *refs):
        for k in range(4):

            @pl.when(pl.program_id(0) == k)
            def _():
                refs[4][0] = refs[k][...]

    rows, columns = parts[0].shape
    return call(
        kernel,
        (4,),
        [whole(p) for p in parts],
        pl.BlockSpec((1, rows, columns), lambda k, r: (k ^ r[0], 0, 0)),
        shape((4, rows, columns)),
        parts,
        "place",
        rank=rank,
    )


def finish_wide(parts, rank):
    rows, width = parts[0].shape

    def kernel(r, *refs):
        for k in range(4):

            @pl.when(pl.program_id(0) == k)
            def _():
                refs[4][...] = refs[k][...].astype(F32)

    return call(
        kernel,
        (4,),
        [whole(p) for p in parts],
        pl.BlockSpec((rows, width), lambda k, r: (0, k ^ r[0])),
        shape((rows, 4 * width), F32),
        parts,
        "finish_wide",
        rank=rank,
    )


def finish_all(parts, text_grad, rank):
    rows, total = parts[0].shape
    width = total // 6

    def kernel(r, *refs):
        key, value, three, out, cross, cross_out = refs[4:]
        for k in range(4):

            @pl.when(pl.program_id(0) == k)
            def _():
                def part(j):
                    return refs[k][:, j * width : (j + 1) * width].astype(F32)

                for j in range(3):
                    three[j] = part(j)
                out[...] = part(3)
                cross[0] = part(4)
                cross_out[...] = part(5)

        cross[1] = key[...]
        cross[2] = value[...]

    wide = pl.BlockSpec((3, rows, width), lambda k, r: (0, 0, k ^ r[0]))
    flat = pl.BlockSpec((rows, width), lambda k, r: (0, k ^ r[0]))
    return call(
        kernel,
        (4,),
        [whole(p) for p in parts]
        + [flat, pl.BlockSpec((rows, width), lambda k, r: (0, 4 + (k ^ r[0])))],
        [wide, flat, wide, flat],
        [shape((3, rows, 4 * width), F32), shape((rows, 4 * width), F32)] * 2,
        [*parts, text_grad, text_grad],
        "finish_all",
        rank=rank,
    )


def plane_block(k):
    return (k >> 1) & 1, (k >> 2) * 2 + (k & 1)


def text_forward(caption, w_text, w_cross):
    context, rows = caption.shape[0], w_text.shape[0]
    half, width = context // 2, w_cross.shape[2] // 4

    def kernel(cap, weight, cross, own, blocks):
        own[...] = mm_t(cap[...], weight[...]).astype(BF)
        for j in range(2):
            part = mm(own[...], cross[1 + j]).astype(BF)
            for k in range(8):
                core, group = plane_block(k)
                blocks[k, :, j * width : (j + 1) * width] = part[
                    core * half : (core + 1) * half, group * width : (group + 1) * width
                ]

    return call(
        kernel,
        (1,),
        [whole(caption), whole(w_text), whole(w_cross)],
        [
            pl.BlockSpec((context, rows), lambda i: (0, 0)),
            pl.BlockSpec((8, half, 2 * width), lambda i: (0, 0, 0)),
        ],
        [shape((context, rows)), shape((8, half, 2 * width))],
        [caption, w_text, w_cross],
        "text_forward",
    )


def text_back(blocks, own_text, w_cross, caption, w_text, extra):
    context, rows = own_text.shape
    half, width = context // 2, w_cross.shape[2] // 4
    wide = caption.shape[1] // 4
    tail = extra.shape[0]

    def kernel(block, own, cross, cap, weight, more, kv_grad, text_grad, out, grads):
        for k in range(8):
            core, group = plane_block(k)
            for j in range(2):
                at = (4 * j + group) * width
                grads[core * half : (core + 1) * half, at : at + width] = block[
                    k, :, j * width : (j + 1) * width
                ]
        kv_grad[...] = t_mm(own[...], grads[...])
        grad_text = sum(
            mm_t(grads[:, 4 * j * width : 4 * (j + 1) * width], cross[1 + j]) for j in range(2)
        ).astype(BF)
        text_grad[...] = t_mm(grad_text, cap[...])
        part = mm(grad_text, weight[...]).astype(BF)
        for k in range(8):
            core, group = plane_block(k)
            out[k, :half, :] = part[core * half : (core + 1) * half, group * wide : (group + 1) * wide]
            out[k, half:, :] = more[...]

    operands = [blocks, own_text, w_cross, caption, w_text, extra]
    outs = [
        shape((rows, 8 * width), F32),
        shape((rows, 4 * wide), F32),
        shape((8, half + tail, wide)),
    ]
    return call(
        kernel,
        (1,),
        [whole(a) for a in operands],
        [whole(a) for a in outs],
        outs,
        operands,
        "text_back",
        scratch=[pltpu.VMEM((context, 8 * width), BF)],
    )


def caption_output(own, other, core):
    count, half, wide = own.shape

    def kernel(r, own_ref, other_ref, out):
        block = jnp.where(pl.program_id(0) == r[0], own_ref[0], other_ref[0])
        out[...] = block.astype(F32)

    block = pl.BlockSpec((1, half, wide), lambda i, k, r: (k, 0, 0))
    return call(
        kernel,
        (2, count),
        [block, block],
        pl.BlockSpec((half, wide), lambda i, k, r: (i, k)),
        shape((2 * half, 4 * wide), F32),
        [own, other],
        "caption_output",
        rank=core,
    )


def column_blocks(weight, count):
    rows = weight.shape[0]
    return weight.reshape(rows, count, -1).transpose(1, 0, 2)


def halves_of(values, width):
    high = values.astype(BF)
    low = (values - high.astype(F32)).astype(BF)
    return jnp.concatenate([high.reshape(-1, width), low.reshape(-1, width)], axis=0)


def whole_of(halves, width):
    rows = halves.shape[0] // 2
    return (halves[:rows] + halves[rows:]).reshape(-1, width)


def make_local(z_size):
    def sum_z(values):
        parts = values.reshape(z_size, -1, values.shape[-1])
        mine = trade(parts, "z").astype(F32).sum(axis=0).astype(BF)
        return spread(mine, "z", z_size).reshape(values.shape)

    def add_z(values):
        step = 1
        while step < z_size:
            values = values + lax.ppermute(
                values, "z", tuple((k, k ^ step) for k in range(z_size))
            )
            step *= 2
        return values

    def layer_order(values):
        shaped = values.reshape(values.shape[:-1] + (z_size, 2, 2, -1))
        return jnp.swapaxes(shaped, -3, -2).reshape(values.shape)

    def local(
        hidden,
        mask_index,
        mask_count,
        mask_embed,
        norm_gains,
        caption,
        w_qkv,
        w_out,
        w_cross,
        w_cross_out,
        w_text,
        w_up,
        w_down,
        cotangent,
    ):
        images, local_rows, width = hidden.shape
        full_length = mask_index.shape[1]
        rank = lax.axis_index("x") * 2 + lax.axis_index("y")
        core = lax.axis_index("c")
        tokens = images * local_rows
        group = width // 4
        text_width = caption.shape[1]

        unit = width // (4 * z_size)
        inside = unit % 128 == 0
        order = [4 * k + j for k in range(z_size) for j in (0, 2, 1, 3)] if inside else None

        def outer(values):
            return values if inside else layer_order(values)

        w_qkv, w_cross = w_qkv.transpose(1, 0, 2), w_cross.transpose(1, 0, 2)
        first = swap_parts(pick_weights(w_qkv, rank))
        first = gather_rows(place(first, rank))

        positions = lax.axis_index("y") * local_rows + jnp.arange(local_rows, dtype=jnp.int32)
        ranks = jnp.arange(full_length, dtype=jnp.int32)
        matches = (mask_index[:, :, None] == positions[None, None, :]) & (
            ranks[None, :, None] < mask_count[:, None, None]
        )
        masked = jnp.any(matches, axis=1).reshape(tokens, 1).astype(F32)
        gains = layer_order(norm_gains)
        gain_a, gain_b, gain_c = gains[:1], gains[1:2], gains[2:]
        start_x, attn_in, grad_top = start(
            outer(hidden.reshape(tokens, width)),
            outer(cotangent.reshape(tokens, width)),
            masked,
            layer_order(mask_embed)[None],
            gain_a,
            unit,
            order,
        )
        attn_in = gather_tokens(attn_in)
        mid = [column_blocks(weight, 4) for weight in (w_out, w_cross[0], w_cross_out)]
        mid = jnp.concatenate(mid, axis=2)
        up = column_blocks(w_up, 4)
        attn_in, mid, up = lax.optimization_barrier((attn_in, mid, up))
        mid, up = gather_rows(trade(mid)), gather_rows(trade(up))

        own_text, kv_part = text_forward(caption, w_text, w_cross)
        text_kv = trade(kv_part, PLANE).astype(F32).sum(axis=0).astype(BF)
        text_kv = sum_z(text_kv)
        other = swap(text_kv, "c")
        text_kv = jnp.concatenate(
            [jnp.where(core == 0, text_kv, other), jnp.where(core == 0, other, text_kv)], axis=0
        )
        attn_in, text_kv = lax.optimization_barrier((attn_in, text_kv))

        attn_in, projected = gather_mm(attn_in, first, 0, 3 * group, "qkv_mm")
        self_mixed = self_forward(projected, 2 * images)
        down = column_blocks(w_down, 4)
        self_mixed, down = lax.optimization_barrier((self_mixed, down))
        down = gather_rows(trade(down))
        parts = mm_scatter(self_mixed, mid[:, :group])
        after_attn, cross_in = add_norm([start_x] + parts, gain_b)

        cross_in, cross_queries = gather_mm(
            gather_tokens(cross_in), mid, group, group, "query_mm"
        )
        cross_mixed = cross_forward(cross_queries, text_kv)
        parts = mm_scatter(cross_mixed, mid[:, 2 * group :])
        after_cross, mlp_in = add_norm([after_attn] + parts, gain_c)

        mlp_in = gather_tokens(mlp_in)
        mlp_in, grad_top = lax.optimization_barrier((mlp_in, grad_top))
        grad_y = jnp.concatenate(gather_tokens(grad_top), axis=0)
        mlp_in, activated, slope = feed_up(mlp_in, up)
        early = [attn_in, self_mixed, cross_in, cross_mixed]
        if inside:
            grad_axes, halves = "z", (core, z_size)

            def both(values):
                return [values, swap(values, "c")]

        else:
            grad_axes, halves = DATA, ()

            def both(values):
                return [values]

        early = [both(values) for values in early]
        down_part = grad_products([(both(grad_y), both(activated))], "down_grads", *halves)
        mlp_in = both(mlp_in)
        slope, down_part, early, mlp_in = lax.optimization_barrier((slope, down_part, early, mlp_in))
        down_rows = scatter_grad(down_part, grad_axes)
        grad_pre = feed_down(grad_y, slope, down)
        parts = mm_scatter(grad_pre, up)
        up_part = grad_products([(mlp_in, both(grad_pre))], "up_grads", *halves)
        grad_after_cross, cross_branch, gain_grad_c = norm_back(
            parts, grad_top, after_cross, gain_c
        )

        cross_branch, up_part = gather_beside(cross_branch, up_part)
        cross_branch, grad_cross_mixed = gather_mm(
            cross_branch, mid, 2 * group, group, "cross_out_back"
        )
        grad_cq, kv_grad = cross_back(cross_queries, text_kv, grad_cross_mixed)
        up_part, down_rows, kv_grad = lax.optimization_barrier((up_part, down_rows, kv_grad))
        up_rows = scatter_grad(up_part, grad_axes)
        cross_branch, grad_cq_both = both(cross_branch), both(grad_cq)
        parts = mm_scatter(grad_cq, mid[:, group : 2 * group])
        grad_after_attn, attn_branch, gain_grad_b = norm_back(
            parts, grad_after_cross, after_attn, gain_b
        )

        activated, attn_branch = lax.optimization_barrier((activated, attn_branch))
        result = mm_t(activated, down).astype(BF)
        attn_branch, result = gather_beside(attn_branch, result)
        attn_branch, result = lax.optimization_barrier((attn_branch, result))
        result = scatter_first(token_blocks(result))
        attn_branch, grad_self_mixed = gather_mm(attn_branch, mid, 0, group, "out_back")
        grad_projected = self_back(projected, grad_self_mixed, 2 * images)
        kv_part = kv_grad.astype(BF).reshape(2, z_size, -1, 2 * group)
        kv_part = kv_part.transpose(1, 0, 2, 3).reshape(2 * z_size, -1, 2 * group)
        grad_projected, result, kv_part = lax.optimization_barrier(
            (grad_projected, result, kv_part)
        )
        kv_part = trade(kv_part, DATA)
        result = scatter_second(result)
        rest_part = grad_products(
            [
                (early[0], both(grad_projected)),
                (both(attn_branch), early[1]),
                (early[2], grad_cq_both),
                (cross_branch, early[3]),
            ],
            "attention_grads",
            *halves,
        )
        grad_projected, result, kv_part, rest_part = lax.optimization_barrier(
            (grad_projected, result, kv_part, rest_part)
        )
        rest_part, up_rows = lax.optimization_barrier((rest_part, up_rows))
        rest_rows = scatter_grad(rest_part, grad_axes)
        parts = mm_scatter(grad_projected, first)
        grad_hidden, gain_grad_a, mask_grad = last_back(
            parts,
            grad_after_attn,
            start_x,
            gain_a,
            masked,
            unit,
            order,
        )
        sums = jnp.concatenate([gain_grad_a, gain_grad_b, gain_grad_c, mask_grad], axis=0)


        kv_part = kv_part.astype(F32).sum(axis=0).astype(BF)
        kv_sum = spread(kv_part, "z", z_size).reshape(-1, 2 * group)
        kv_grads = spread(kv_sum, PLANE, 8)
        kv_weight_grad, grad_text_w, caption_part = text_back(
            kv_grads, own_text, w_cross, caption, w_text, halves_of(sums, text_width // 4)
        )
        half_context = caption.shape[0] // 2
        caption_part = trade(caption_part, PLANE)
        output = layer_output(after_cross, result, unit, order)
        caption_part, output, down_rows, up_rows = lax.optimization_barrier(
            (caption_part, output, down_rows, up_rows)
        )

        caption_part = caption_part.astype(F32).sum(axis=0)
        sums = layer_order(add_z(whole_of(caption_part[half_context:], width)))
        caption_part = caption_part[:half_context].astype(BF).reshape(z_size, -1, text_width // 4)
        caption_part = trade(caption_part, "z")
        down_parts = swap_parts(pick_rows([down_rows], rank))
        caption_part, down_parts, up_rows = lax.optimization_barrier(
            (caption_part, down_parts, up_rows)
        )

        caption_part = caption_part.astype(F32).sum(axis=0).astype(BF)
        caption_part = spread(caption_part, "z", z_size).reshape(half_context, -1)
        up_parts = swap_parts(pick_rows([up_rows], rank))
        down_grad = finish_wide(down_parts, rank)
        caption_part, up_parts, down_grad = lax.optimization_barrier(
            (caption_part, up_parts, down_grad)
        )

        caption_part = spread(caption_part)
        up_grad = finish_wide(up_parts, rank)
        caption_part, rest_rows, up_grad = lax.optimization_barrier(
            (caption_part, rest_rows, up_grad)
        )
        grad_caption = caption_output(caption_part, swap(caption_part, "c"), core)
        rest_rows = swap_parts(pick_rows([rest_rows], rank))
        grad_caption, rest_rows = lax.optimization_barrier((grad_caption, rest_rows))
        qkv_grad, out_grad, grad_cross, cross_out_grad = finish_all(
            rest_rows, kv_weight_grad, rank
        )
        return (
            outer(output).reshape(hidden.shape),
            outer(grad_hidden).reshape(hidden.shape),
            grad_caption,
            sums[:3],
            sums[3],
            qkv_grad.transpose(1, 0, 2),
            out_grad,
            grad_cross.transpose(1, 0, 2),
            cross_out_grad,
            grad_text_w,
            up_grad,
            down_grad,
        )

    return local


def solution(mesh):
    z_size = mesh.shape["img"] // 4
    inner = Mesh(mesh.devices.reshape(z_size, 2, 2, 2), ("z", "x", "c", "y"))
    image = ("z", "x", "c")
    tokens = P(image, "y", None)
    rows = P(image + ("y",))
    in_specs = (tokens, P(image, None), P(image), P(), P(), P()) + (rows,) * 7 + (tokens,)
    out_specs = (tokens, tokens, P(), P(), P()) + (rows,) * 7
    return jax.shard_map(
        make_local(z_size), mesh=inner, in_specs=in_specs, out_specs=out_specs, check_vma=False
    )
```

```python
import math

import jax
import jax.numpy as jnp
from jax import lax
from jax.experimental import pallas as pl
from jax.experimental.pallas import tpu as pltpu
from jax.sharding import Mesh
from jax.sharding import PartitionSpec as P

HD = 128
EPS = 1e-05
BF = jnp.bfloat16
F32 = jnp.float32
PAIR = ((0, 1), (1, 0))
GROUP = ("x", "y")
DATA = ("z", "c")
PLANE = ("x", "c", "y")
VMEM = 48 * 1024 * 1024
SCALE = 1.0 / math.sqrt(HD)
SLOPE = math.sqrt(2.0 / math.pi)
CUBIC = 0.044715


def dot(a, b, dims):
    return lax.dot_general(a, b, (dims, ((), ())), preferred_element_type=F32)


def mm(a, b):
    return dot(a, b, ((1,), (0,)))


def mm_t(a, b):
    return dot(a, b, ((1,), (1,)))


def t_mm(a, b):
    return dot(a, b, ((0,), (0,)))


def shape(dims, dtype=BF):
    return jax.ShapeDtypeStruct(dims, dtype)


def swap(values, axis):
    return lax.ppermute(values, axis, PAIR)


def trade(blocks, axes=GROUP):
    return lax.all_to_all(blocks, axes, 0, 0, tiled=True)


def spread(values, axes=GROUP, count=4):
    return trade(jnp.broadcast_to(values[None], (count,) + values.shape), axes)


def gather_tokens(own):
    half = own.shape[0] // 2
    from_x = swap(own, "x")
    from_y = swap(own, "y")
    return own, from_y, from_x, swap(from_x[:half], "y"), swap(from_y[half:], "x")


def gather_beside(own, work):
    half = own.shape[0] // 2
    from_x, from_y, work = lax.optimization_barrier((swap(own, "x"), swap(own, "y"), work))
    return (own, from_y, from_x, swap(from_x[:half], "y"), swap(from_y[half:], "x")), work


def scatter_first(parts):
    own, for_y, for_x, for_low, for_high = parts
    half = for_low.shape[0]
    low = swap(for_low, "y").astype(F32) + for_x[:half].astype(F32)
    high = swap(for_high, "x").astype(F32) + for_y[half:].astype(F32)
    return (
        own,
        jnp.concatenate([low.astype(BF), for_x[half:]], axis=0),
        jnp.concatenate([for_y[:half], high.astype(BF)], axis=0),
    )


def scatter_second(parts):
    own, for_x, for_y = parts
    return [own, swap(for_x, "x"), swap(for_y, "y")]


def scatter_tokens(parts):
    return scatter_second(scatter_first(parts))


def swap_parts(parts):
    return [
        parts[0],
        swap(parts[1], "y"),
        swap(parts[2], "x"),
        lax.ppermute(parts[3], GROUP, ((0, 3), (1, 2), (2, 1), (3, 0))),
    ]


def gather_rows(rows):
    return lax.all_gather(rows.reshape(-1, rows.shape[-1]), DATA, axis=0, tiled=True)


def scatter_grad(partial, axes):
    summed = lax.psum_scatter(partial, axes, scatter_dimension=0, tiled=True)
    return summed.reshape(4, -1, summed.shape[-1])


def call(kernel, grid, in_specs, out_specs, out_shape, operands, name, flops=0, size=1 << 22,
         rank=None, scratch=()):
    options = dict(
        out_shape=out_shape,
        compiler_params=pltpu.CompilerParams(vmem_limit_bytes=VMEM),
        cost_estimate=pl.CostEstimate(flops=flops, bytes_accessed=size, transcendentals=0),
        name=name,
    )
    if rank is None:
        return pl.pallas_call(
            kernel, grid=grid, in_specs=in_specs, out_specs=out_specs, scratch_shapes=scratch,
            **options,
        )(*operands)
    spec = pltpu.PrefetchScalarGridSpec(
        num_scalar_prefetch=1,
        grid=grid,
        in_specs=in_specs,
        out_specs=out_specs,
        scratch_shapes=scratch,
    )
    return pl.pallas_call(kernel, grid_spec=spec, **options)(rank.reshape(1), *operands)


def whole(array):
    return pl.BlockSpec(array.shape, lambda *_: (0,) * len(array.shape))


def reorder(values, unit, order):
    if order is None:
        return values
    return jnp.concatenate([values[:, k * unit : (k + 1) * unit] for k in order], axis=1)


def assemble(target, pieces, sems):
    copies, at = [], 0
    for k, piece in enumerate(pieces):
        rows = piece.shape[0]
        copies.append(pltpu.make_async_copy(piece, target.at[at : at + rows], sems.at[k]))
        at += rows
    for copy in copies:
        copy.start()
    for copy in copies:
        copy.wait()


ANY = pl.BlockSpec(memory_space=pl.ANY)


def gather_mm(pieces, weight, first, columns, name):
    rows, width = pieces[0].shape
    step = 256

    def kernel(*refs):
        tokens, out, sems = refs[6:]

        @pl.when(pl.program_id(0) == 0)
        def _():
            assemble(tokens, refs[:5], sems)

        out[...] = mm(tokens[...], refs[5][...]).astype(BF)

    return call(
        kernel,
        (columns // step,),
        [ANY] * 5 + [pl.BlockSpec((width, step), lambda j: (0, first // step + j))],
        [
            pl.BlockSpec((4 * rows, width), lambda j: (0, 0)),
            pl.BlockSpec((4 * rows, step), lambda j: (0, j)),
        ],
        [shape((4 * rows, width)), shape((4 * rows, columns))],
        [*pieces, weight],
        name,
        flops=8 * rows * width * columns,
        size=2 * width * (columns + 8 * rows),
        scratch=[pltpu.SemaphoreType.DMA((5,))],
    )


def mm_scatter(values, weight):
    return scatter_tokens(token_blocks(mm_t(values, weight).astype(BF)))


def token_blocks(partial):
    rows = partial.shape[0] // 4
    cuts = [0, rows, 2 * rows, 3 * rows, 3 * rows + rows // 2, 4 * rows]
    return [partial[a:b] for a, b in zip(cuts, cuts[1:])]


def normalize(values):
    centred = values - jnp.mean(values, axis=-1, keepdims=True)
    inv_std = lax.rsqrt(jnp.mean(centred * centred, axis=-1, keepdims=True) + EPS)
    return centred * inv_std, inv_std


NORM_ROWS = 32


def row_spec(array, at=None):
    width = array.shape[-1]
    if at is None:
        return pl.BlockSpec((NORM_ROWS, width), lambda i: (i, 0))
    return pl.BlockSpec((1, NORM_ROWS, width), lambda i, at=at: (at, i, 0))


def terms_of(terms):
    arrays, specs = [], []
    for term in terms:
        array, at = term if isinstance(term, tuple) else (term, None)
        arrays.append(array)
        specs.append(row_spec(array, at))
    return arrays, specs


def total_of(refs):
    values = [ref[0] if len(ref.shape) == 3 else ref[...] for ref in refs]
    return sum(value.astype(F32) for value in values)


def add_norm(terms, gain):
    arrays, specs = terms_of(terms)
    tokens, width = arrays[0].shape[-2], arrays[0].shape[-1]
    tokens = min(a.shape[-2] for a in arrays)

    def kernel(*refs):
        gain_ref, x, out = refs[-3:]
        values = total_of(refs[:-3])
        x[...] = values
        out[...] = (normalize(values)[0] * gain_ref[...]).astype(BF)

    return call(
        kernel,
        (tokens // NORM_ROWS,),
        specs + [whole(gain)],
        [row_spec(shape((tokens, width)))] * 2,
        [shape((tokens, width), F32), shape((tokens, width))],
        [*arrays, gain],
        "add_norm",
    )


def norm_grad(grad, values, gain):
    normed, inv_std = normalize(values)
    scaled = grad * gain
    first_mean = jnp.mean(scaled, axis=-1, keepdims=True)
    second_mean = jnp.mean(scaled * normed, axis=-1, keepdims=True)
    return (
        inv_std * (scaled - first_mean - normed * second_mean),
        jnp.sum(grad * normed, axis=0, keepdims=True),
    )


def accumulate(ref, value):
    @pl.when(pl.program_id(0) == 0)
    def _():
        ref[...] = jnp.zeros_like(ref)

    ref[...] += value


def norm_back(terms, upper, values, gain):
    arrays, specs = terms_of(terms)
    tokens, width = values.shape

    def kernel(*refs):
        upper_ref, x, gain_ref, out, out_low, gain_grad = refs[-6:]
        back, part = norm_grad(total_of(refs[:-6]), x[...], gain_ref[...])
        result = upper_ref[...].astype(F32) + back
        out[...] = result
        out_low[...] = result.astype(BF)
        accumulate(gain_grad, part)

    return call(
        kernel,
        (tokens // NORM_ROWS,),
        specs + [row_spec(upper), row_spec(values), whole(gain)],
        [row_spec(values)] * 2 + [pl.BlockSpec((1, width), lambda i: (0, 0))],
        [shape((tokens, width), F32), shape((tokens, width)), shape((1, width), F32)],
        [*arrays, upper, values, gain],
        "norm_back",
    )


def last_back(terms, upper, values, gain, masked, unit, order):
    arrays, specs = terms_of(terms)
    tokens, width = values.shape

    def kernel(*refs):
        upper_ref, x, gain_ref, mask, out, gain_grad, mask_grad = refs[-7:]
        back, part = norm_grad(total_of(refs[:-7]), x[...], gain_ref[...])
        result = upper_ref[...].astype(F32) + back
        hit = mask[...] > 0.5
        out[...] = reorder(jnp.where(hit, 0.0, result).astype(BF), unit, order)
        accumulate(gain_grad, part)
        accumulate(mask_grad, jnp.sum(jnp.where(hit, result, 0.0), axis=0, keepdims=True))

    line = pl.BlockSpec((1, width), lambda i: (0, 0))
    return call(
        kernel,
        (tokens // NORM_ROWS,),
        specs + [row_spec(upper), row_spec(values), whole(gain), row_spec(masked)],
        [row_spec(values), line, line],
        [shape((tokens, width)), shape((1, width), F32), shape((1, width), F32)],
        [*arrays, upper, values, gain, masked],
        "last_back",
    )


def start(hidden, cotangent, masked, embed, gain, unit, order):
    tokens, width = hidden.shape

    def kernel(hid, cot, mask, embed_ref, gain_ref, x, out, grad):
        hit = mask[...] > 0.5
        values = jnp.where(
            hit, embed_ref[...], reorder(hid[...], unit, order).astype(F32)
        )
        x[...] = values
        out[...] = (normalize(values)[0] * gain_ref[...]).astype(BF)
        grad[...] = jnp.where(hit, reorder(cot[...], unit, order).astype(F32), 0.0).astype(BF)

    rows = row_spec(hidden)
    return call(
        kernel,
        (tokens // NORM_ROWS,),
        [rows, rows, row_spec(masked), whole(embed), whole(gain)],
        [rows] * 3,
        [shape((tokens, width), F32), shape((tokens, width)), shape((tokens, width))],
        [hidden, cotangent, masked, embed, gain],
        "start",
    )


def layer_output(upper, terms, unit, order):
    arrays, specs = terms_of(terms)
    tokens, width = upper.shape

    def kernel(*refs):
        values = refs[-2][...] + total_of(refs[:-2])
        refs[-1][...] = reorder(values.astype(BF), unit, order)

    return call(
        kernel,
        (tokens // NORM_ROWS,),
        specs + [row_spec(upper)],
        row_spec(upper),
        shape((tokens, width)),
        [*arrays, upper],
        "layer_output",
    )


def feed_up(pieces, weight):
    rows, width = pieces[0].shape
    hidden = weight.shape[1]
    step = 256

    def kernel(*refs):
        up, tokens, act, slope, sems = refs[5:]

        @pl.when(pl.program_id(0) == 0)
        def _():
            assemble(tokens, refs[:5], sems)

        u = mm(tokens[...], up[...])
        square = u * u
        bend = jnp.tanh(SLOPE * u * (1.0 + CUBIC * square))
        half = 0.5 * (1.0 + bend)
        act[...] = (u * half).astype(BF)
        slope[...] = half + 0.5 * u * (1.0 - bend * bend) * SLOPE * (1.0 + 3.0 * CUBIC * square)

    part = pl.BlockSpec((4 * rows, step), lambda j: (0, j))
    return call(
        kernel,
        (hidden // step,),
        [ANY] * 5 + [pl.BlockSpec((width, step), lambda j: (0, j))],
        [pl.BlockSpec((4 * rows, width), lambda j: (0, 0)), part, part],
        [shape((4 * rows, width)), shape((4 * rows, hidden)), shape((4 * rows, hidden), F32)],
        [*pieces, weight],
        "feed_up",
        scratch=[pltpu.SemaphoreType.DMA((5,))],
        flops=8 * rows * width * hidden,
        size=2 * width * (hidden + 8 * rows),
    )


def feed_down(grad_y, slope, weight):
    tokens, width = grad_y.shape
    hidden = weight.shape[1]
    step = 256

    def kernel(dy, slope_ref, down, out):
        out[...] = (mm(dy[...], down[...]) * slope_ref[...]).astype(BF)

    part = pl.BlockSpec((tokens, step), lambda j: (0, j))
    return call(
        kernel,
        (hidden // step,),
        [whole(grad_y), part, pl.BlockSpec((width, step), lambda j: (0, j))],
        part,
        shape((tokens, hidden)),
        [grad_y, slope, weight],
        "feed_down",
        flops=2 * tokens * width * hidden,
        size=2 * width * (hidden + 8 * tokens),
    )


def softmax(scores):
    exp_terms = jnp.exp(scores - jnp.max(scores, axis=-1, keepdims=True))
    return exp_terms / jnp.sum(exp_terms, axis=-1, keepdims=True)


def score_grad(probs, grad_probs):
    return (
        probs * (grad_probs - jnp.sum(probs * grad_probs, axis=-1, keepdims=True))
    ).astype(BF)


def head(ref, k):
    return ref[:, k * HD : (k + 1) * HD]


def self_forward(projected, images):
    tokens, width = projected.shape
    rows, group = tokens // images, width // 3
    heads = group // HD

    def kernel(proj, mixed):
        for k in range(heads):
            query, key, value = (head(proj, j * heads + k) for j in range(3))
            probs = softmax(mm_t(query, key) * SCALE).astype(BF)
            mixed[:, k * HD : (k + 1) * HD] = mm(probs, value).astype(BF)

    return call(
        kernel,
        (images,),
        [pl.BlockSpec((rows, width), lambda i: (i, 0))],
        pl.BlockSpec((rows, group), lambda i: (i, 0)),
        shape((tokens, group)),
        [projected],
        "self_forward",
        flops=4 * tokens * rows * group,
    )


def self_back(projected, grad_mixed, images):
    tokens, width = projected.shape
    rows, group = tokens // images, width // 3
    heads = group // HD

    def kernel(proj, grad, out):
        for k in range(heads):
            query, key, value = (head(proj, j * heads + k) for j in range(3))
            grad_head = head(grad, k)
            probs = softmax(mm_t(query, key) * SCALE)
            grad_scores = score_grad(probs, mm_t(grad_head, value))
            parts = (
                mm(grad_scores, key) * SCALE,
                t_mm(grad_scores, query) * SCALE,
                t_mm(probs.astype(BF), grad_head),
            )
            for j, part in enumerate(parts):
                at = (j * heads + k) * HD
                out[:, at : at + HD] = part.astype(BF)

    return call(
        kernel,
        (images,),
        [
            pl.BlockSpec((rows, width), lambda i: (i, 0)),
            pl.BlockSpec((rows, group), lambda i: (i, 0)),
        ],
        pl.BlockSpec((rows, width), lambda i: (i, 0)),
        shape((tokens, width)),
        [projected, grad_mixed],
        "self_back",
        flops=10 * tokens * rows * group,
    )


def cross_forward(queries, text_kv):
    tokens, group = queries.shape
    heads = group // HD

    def kernel(query, text, mixed):
        for k in range(heads):
            probs = softmax(mm_t(head(query, k), head(text, k)) * SCALE).astype(BF)
            mixed[:, k * HD : (k + 1) * HD] = mm(probs, head(text, heads + k)).astype(BF)

    return call(
        kernel,
        (1,),
        [whole(queries), whole(text_kv)],
        whole(queries),
        shape((tokens, group)),
        [queries, text_kv],
        "cross_forward",
        flops=4 * tokens * text_kv.shape[0] * group,
    )


def cross_back(queries, text_kv, grad_mixed):
    tokens, group = queries.shape
    context = text_kv.shape[0]
    heads = group // HD

    def kernel(query, text, grad, grad_query, grad_text):
        for k in range(heads):
            query_head, key, value = head(query, k), head(text, k), head(text, heads + k)
            grad_head = head(grad, k)
            probs = softmax(mm_t(query_head, key) * SCALE)
            grad_scores = score_grad(probs, mm_t(grad_head, value))
            grad_query[:, k * HD : (k + 1) * HD] = (mm(grad_scores, key) * SCALE).astype(BF)
            at = (heads + k) * HD
            grad_text[:, k * HD : (k + 1) * HD] = t_mm(grad_scores, query_head) * SCALE
            grad_text[:, at : at + HD] = t_mm(probs.astype(BF), grad_head)

    return call(
        kernel,
        (1,),
        [whole(queries), whole(text_kv), whole(grad_mixed)],
        [whole(queries), whole(text_kv)],
        [shape((tokens, group)), shape((context, 2 * group), F32)],
        [queries, text_kv, grad_mixed],
        "cross_back",
        flops=10 * tokens * context * group,
    )


def grad_products(pairs, name, core=None, blocks=0):
    count_in = len(pairs[0][0])
    tokens, width = pairs[0][0][0].shape
    widths = [y[0].shape[1] for _, y in pairs]
    total = sum(widths)
    rows = 256 if core is None else width // (2 * blocks)
    steps = width // rows if core is None else blocks
    step = 512
    count = len(pairs) * count_in

    def kernel(r, *refs):
        out = refs[2 * count]
        offset = 0
        for k, wide in enumerate(widths):
            left = [refs[k * count_in + b][...].T for b in range(count_in)]
            for at in range(0, wide, step):
                out[:, offset + at : offset + at + step] = sum(
                    mm(left[b], refs[count + k * count_in + b][:, at : at + step])
                    for b in range(count_in)
                ).astype(BF)
            offset += wide

    pick = (lambda i, r: (0, i)) if core is None else (lambda i, r: (0, 2 * i + r[0]))
    return call(
        kernel,
        (steps,),
        [pl.BlockSpec((tokens, rows), pick)] * count
        + [pl.BlockSpec((tokens, w), lambda i, r: (0, 0)) for w in widths for _ in range(count_in)],
        pl.BlockSpec((rows, total), lambda i, r: (i, 0)),
        shape((steps * rows, total)),
        [b for x, _ in pairs for b in x] + [b for _, y in pairs for b in y],
        name,
        flops=2 * tokens * count_in * steps * rows * total,
        size=4 * width * total,
        rank=jnp.zeros((), jnp.int32) if core is None else core,
    )


def pick_weights(three, rank):
    rows, width = three.shape[1], three.shape[2] // 4

    def kernel(r, three_ref, *outs):
        for k in range(4):

            @pl.when(pl.program_id(0) == k)
            def _():
                for j in range(3):
                    outs[k][:, j * width : (j + 1) * width] = three_ref[j]

    outs = [shape((rows, 3 * width))] * 4
    return call(
        kernel,
        (4,),
        [pl.BlockSpec((3, rows, width), lambda k, r: (0, 0, k ^ r[0]))],
        [whole(a) for a in outs],
        outs,
        [three],
        "pick_weights",
        rank=rank,
    )


def pick_rows(arrays, rank):
    rows = arrays[0].shape[1]
    widths = [a.shape[2] for a in arrays]
    count = len(arrays)

    def kernel(r, *refs):
        for k in range(4):

            @pl.when(pl.program_id(0) == k)
            def _():
                at = 0
                for ref, width in zip(refs, widths):
                    refs[count + k][:, at : at + width] = ref[0]
                    at += width

    outs = [shape((rows, sum(widths)))] * 4
    return call(
        kernel,
        (4,),
        [pl.BlockSpec((1, rows, w), lambda k, r: (k ^ r[0], 0, 0)) for w in widths],
        [whole(a) for a in outs],
        outs,
        arrays,
        "pick_rows",
        rank=rank,
    )


def place(parts, rank):
    def kernel(r, *refs):
        for k in range(4):

            @pl.when(pl.program_id(0) == k)
            def _():
                refs[4][0] = refs[k][...]

    rows, columns = parts[0].shape
    return call(
        kernel,
        (4,),
        [whole(p) for p in parts],
        pl.BlockSpec((1, rows, columns), lambda k, r: (k ^ r[0], 0, 0)),
        shape((4, rows, columns)),
        parts,
        "place",
        rank=rank,
    )


def finish_wide(parts, rank):
    rows, width = parts[0].shape

    def kernel(r, *refs):
        for k in range(4):

            @pl.when(pl.program_id(0) == k)
            def _():
                refs[4][...] = refs[k][...].astype(F32)

    return call(
        kernel,
        (4,),
        [whole(p) for p in parts],
        pl.BlockSpec((rows, width), lambda k, r: (0, k ^ r[0])),
        shape((rows, 4 * width), F32),
        parts,
        "finish_wide",
        rank=rank,
    )


def finish_all(parts, text_grad, rank):
    rows, total = parts[0].shape
    width = total // 6

    def kernel(r, *refs):
        key, value, three, out, cross, cross_out = refs[4:]
        for k in range(4):

            @pl.when(pl.program_id(0) == k)
            def _():
                def part(j):
                    return refs[k][:, j * width : (j + 1) * width].astype(F32)

                for j in range(3):
                    three[j] = part(j)
                out[...] = part(3)
                cross[0] = part(4)
                cross_out[...] = part(5)

        cross[1] = key[...]
        cross[2] = value[...]

    wide = pl.BlockSpec((3, rows, width), lambda k, r: (0, 0, k ^ r[0]))
    flat = pl.BlockSpec((rows, width), lambda k, r: (0, k ^ r[0]))
    return call(
        kernel,
        (4,),
        [whole(p) for p in parts]
        + [flat, pl.BlockSpec((rows, width), lambda k, r: (0, 4 + (k ^ r[0])))],
        [wide, flat, wide, flat],
        [shape((3, rows, 4 * width), F32), shape((rows, 4 * width), F32)] * 2,
        [*parts, text_grad, text_grad],
        "finish_all",
        rank=rank,
    )


def plane_block(k):
    return (k >> 1) & 1, (k >> 2) * 2 + (k & 1)


def text_forward(caption, w_text, w_cross):
    context, rows = caption.shape[0], w_text.shape[0]
    half, width = context // 2, w_cross.shape[2] // 4

    def kernel(cap, weight, cross, own, blocks):
        own[...] = mm_t(cap[...], weight[...]).astype(BF)
        for j in range(2):
            part = mm(own[...], cross[1 + j]).astype(BF)
            for k in range(8):
                core, group = plane_block(k)
                blocks[k, :, j * width : (j + 1) * width] = part[
                    core * half : (core + 1) * half, group * width : (group + 1) * width
                ]

    return call(
        kernel,
        (1,),
        [whole(caption), whole(w_text), whole(w_cross)],
        [
            pl.BlockSpec((context, rows), lambda i: (0, 0)),
            pl.BlockSpec((8, half, 2 * width), lambda i: (0, 0, 0)),
        ],
        [shape((context, rows)), shape((8, half, 2 * width))],
        [caption, w_text, w_cross],
        "text_forward",
    )


def text_back(blocks, own_text, w_cross, caption, w_text, extra):
    context, rows = own_text.shape
    half, width = context // 2, w_cross.shape[2] // 4
    wide = caption.shape[1] // 4
    tail = extra.shape[0]

    def kernel(block, own, cross, cap, weight, more, kv_grad, text_grad, out, grads):
        for k in range(8):
            core, group = plane_block(k)
            for j in range(2):
                at = (4 * j + group) * width
                grads[core * half : (core + 1) * half, at : at + width] = block[
                    k, :, j * width : (j + 1) * width
                ]
        kv_grad[...] = t_mm(own[...], grads[...])
        grad_text = sum(
            mm_t(grads[:, 4 * j * width : 4 * (j + 1) * width], cross[1 + j]) for j in range(2)
        ).astype(BF)
        text_grad[...] = t_mm(grad_text, cap[...])
        part = mm(grad_text, weight[...]).astype(BF)
        for k in range(8):
            core, group = plane_block(k)
            out[k, :half, :] = part[core * half : (core + 1) * half, group * wide : (group + 1) * wide]
            out[k, half:, :] = more[...]

    operands = [blocks, own_text, w_cross, caption, w_text, extra]
    outs = [
        shape((rows, 8 * width), F32),
        shape((rows, 4 * wide), F32),
        shape((8, half + tail, wide)),
    ]
    return call(
        kernel,
        (1,),
        [whole(a) for a in operands],
        [whole(a) for a in outs],
        outs,
        operands,
        "text_back",
        scratch=[pltpu.VMEM((context, 8 * width), BF)],
    )


def caption_output(own, other, core):
    count, half, wide = own.shape

    def kernel(r, own_ref, other_ref, out):
        block = jnp.where(pl.program_id(0) == r[0], own_ref[0], other_ref[0])
        out[...] = block.astype(F32)

    block = pl.BlockSpec((1, half, wide), lambda i, k, r: (k, 0, 0))
    return call(
        kernel,
        (2, count),
        [block, block],
        pl.BlockSpec((half, wide), lambda i, k, r: (i, k)),
        shape((2 * half, 4 * wide), F32),
        [own, other],
        "caption_output",
        rank=core,
    )


def column_blocks(weight, count):
    rows = weight.shape[0]
    return weight.reshape(rows, count, -1).transpose(1, 0, 2)


def halves_of(values, width):
    high = values.astype(BF)
    low = (values - high.astype(F32)).astype(BF)
    return jnp.concatenate([high.reshape(-1, width), low.reshape(-1, width)], axis=0)


def whole_of(halves, width):
    rows = halves.shape[0] // 2
    return (halves[:rows] + halves[rows:]).reshape(-1, width)


def make_local(z_size):
    def sum_z(values):
        parts = values.reshape(z_size, -1, values.shape[-1])
        mine = trade(parts, "z").astype(F32).sum(axis=0).astype(BF)
        return spread(mine, "z", z_size).reshape(values.shape)

    def add_z(values):
        step = 1
        while step < z_size:
            values = values + lax.ppermute(
                values, "z", tuple((k, k ^ step) for k in range(z_size))
            )
            step *= 2
        return values

    def layer_order(values):
        shaped = values.reshape(values.shape[:-1] + (z_size, 2, 2, -1))
        return jnp.swapaxes(shaped, -3, -2).reshape(values.shape)

    def local(
        hidden,
        mask_index,
        mask_count,
        mask_embed,
        norm_gains,
        caption,
        w_qkv,
        w_out,
        w_cross,
        w_cross_out,
        w_text,
        w_up,
        w_down,
        cotangent,
    ):
        images, local_rows, width = hidden.shape
        full_length = mask_index.shape[1]
        rank = lax.axis_index("x") * 2 + lax.axis_index("y")
        core = lax.axis_index("c")
        tokens = images * local_rows
        group = width // 4
        text_width = caption.shape[1]

        unit = width // (4 * z_size)
        inside = unit % 128 == 0
        order = [4 * k + j for k in range(z_size) for j in (0, 2, 1, 3)] if inside else None

        def outer(values):
            return values if inside else layer_order(values)

        w_qkv, w_cross = w_qkv.transpose(1, 0, 2), w_cross.transpose(1, 0, 2)
        first = swap_parts(pick_weights(w_qkv, rank))
        first = gather_rows(place(first, rank))

        positions = lax.axis_index("y") * local_rows + jnp.arange(local_rows, dtype=jnp.int32)
        ranks = jnp.arange(full_length, dtype=jnp.int32)
        matches = (mask_index[:, :, None] == positions[None, None, :]) & (
            ranks[None, :, None] < mask_count[:, None, None]
        )
        masked = jnp.any(matches, axis=1).reshape(tokens, 1).astype(F32)
        gains = layer_order(norm_gains)
        gain_a, gain_b, gain_c = gains[:1], gains[1:2], gains[2:]
        start_x, attn_in, grad_top = start(
            outer(hidden.reshape(tokens, width)),
            outer(cotangent.reshape(tokens, width)),
            masked,
            layer_order(mask_embed)[None],
            gain_a,
            unit,
            order,
        )
        attn_in = gather_tokens(attn_in)
        mid = [column_blocks(weight, 4) for weight in (w_out, w_cross[0], w_cross_out)]
        mid = jnp.concatenate(mid, axis=2)
        up = column_blocks(w_up, 4)
        attn_in, mid, up = lax.optimization_barrier((attn_in, mid, up))
        mid, up = gather_rows(trade(mid)), gather_rows(trade(up))

        own_text, kv_part = text_forward(caption, w_text, w_cross)
        text_kv = trade(kv_part, PLANE).astype(F32).sum(axis=0).astype(BF)
        text_kv = sum_z(text_kv)
        other = swap(text_kv, "c")
        text_kv = jnp.concatenate(
            [jnp.where(core == 0, text_kv, other), jnp.where(core == 0, other, text_kv)], axis=0
        )
        attn_in, text_kv = lax.optimization_barrier((attn_in, text_kv))

        attn_in, projected = gather_mm(attn_in, first, 0, 3 * group, "qkv_mm")
        self_mixed = self_forward(projected, 2 * images)
        down = column_blocks(w_down, 4)
        self_mixed, down = lax.optimization_barrier((self_mixed, down))
        down = gather_rows(trade(down))
        parts = mm_scatter(self_mixed, mid[:, :group])
        after_attn, cross_in = add_norm([start_x] + parts, gain_b)

        cross_in, cross_queries = gather_mm(
            gather_tokens(cross_in), mid, group, group, "query_mm"
        )
        cross_mixed = cross_forward(cross_queries, text_kv)
        parts = mm_scatter(cross_mixed, mid[:, 2 * group :])
        after_cross, mlp_in = add_norm([after_attn] + parts, gain_c)

        mlp_in = gather_tokens(mlp_in)
        mlp_in, grad_top = lax.optimization_barrier((mlp_in, grad_top))
        grad_y = jnp.concatenate(gather_tokens(grad_top), axis=0)
        mlp_in, activated, slope = feed_up(mlp_in, up)
        early = [attn_in, self_mixed, cross_in, cross_mixed]
        if inside:
            grad_axes, halves = "z", (core, z_size)

            def both(values):
                return [values, swap(values, "c")]

        else:
            grad_axes, halves = DATA, ()

            def both(values):
                return [values]

        early = [both(values) for values in early]
        down_part = grad_products([(both(grad_y), both(activated))], "down_grads", *halves)
        mlp_in = both(mlp_in)
        slope, down_part, early, mlp_in = lax.optimization_barrier((slope, down_part, early, mlp_in))
        down_rows = scatter_grad(down_part, grad_axes)
        grad_pre = feed_down(grad_y, slope, down)
        parts = mm_scatter(grad_pre, up)
        up_part = grad_products([(mlp_in, both(grad_pre))], "up_grads", *halves)
        grad_after_cross, cross_branch, gain_grad_c = norm_back(
            parts, grad_top, after_cross, gain_c
        )

        cross_branch, up_part = gather_beside(cross_branch, up_part)
        cross_branch, grad_cross_mixed = gather_mm(
            cross_branch, mid, 2 * group, group, "cross_out_back"
        )
        grad_cq, kv_grad = cross_back(cross_queries, text_kv, grad_cross_mixed)
        up_part, down_rows, kv_grad = lax.optimization_barrier((up_part, down_rows, kv_grad))
        up_rows = scatter_grad(up_part, grad_axes)
        cross_branch, grad_cq_both = both(cross_branch), both(grad_cq)
        parts = mm_scatter(grad_cq, mid[:, group : 2 * group])
        grad_after_attn, attn_branch, gain_grad_b = norm_back(
            parts, grad_after_cross, after_attn, gain_b
        )

        activated, attn_branch = lax.optimization_barrier((activated, attn_branch))
        result = mm_t(activated, down).astype(BF)
        attn_branch, result = gather_beside(attn_branch, result)
        attn_branch, result = lax.optimization_barrier((attn_branch, result))
        result = scatter_first(token_blocks(result))
        attn_branch, grad_self_mixed = gather_mm(attn_branch, mid, 0, group, "out_back")
        grad_projected = self_back(projected, grad_self_mixed, 2 * images)
        kv_part = kv_grad.astype(BF).reshape(2, z_size, -1, 2 * group)
        kv_part = kv_part.transpose(1, 0, 2, 3).reshape(2 * z_size, -1, 2 * group)
        grad_projected, result, kv_part = lax.optimization_barrier(
            (grad_projected, result, kv_part)
        )
        kv_part = trade(kv_part, DATA)
        result = scatter_second(result)
        rest_part = grad_products(
            [
                (early[0], both(grad_projected)),
                (both(attn_branch), early[1]),
                (early[2], grad_cq_both),
                (cross_branch, early[3]),
            ],
            "attention_grads",
            *halves,
        )
        grad_projected, result, kv_part, rest_part = lax.optimization_barrier(
            (grad_projected, result, kv_part, rest_part)
        )
        rest_part, up_rows = lax.optimization_barrier((rest_part, up_rows))
        rest_rows = scatter_grad(rest_part, grad_axes)
        kv_part = kv_part.astype(F32).sum(axis=0).astype(BF)
        kv_part, grad_projected = lax.optimization_barrier((kv_part, grad_projected))
        parts = mm_scatter(grad_projected, first)
        grad_hidden, gain_grad_a, mask_grad = last_back(
            parts,
            grad_after_attn,
            start_x,
            gain_a,
            masked,
            unit,
            order,
        )
        sums = jnp.concatenate([gain_grad_a, gain_grad_b, gain_grad_c, mask_grad], axis=0)


        kv_sum = spread(kv_part, "z", z_size).reshape(-1, 2 * group)
        kv_grads = spread(kv_sum, PLANE, 8)
        kv_weight_grad, grad_text_w, caption_part = text_back(
            kv_grads, own_text, w_cross, caption, w_text, halves_of(sums, text_width // 4)
        )
        half_context = caption.shape[0] // 2
        caption_part = trade(caption_part, PLANE)
        output = layer_output(after_cross, result, unit, order)
        caption_part, output, down_rows, up_rows = lax.optimization_barrier(
            (caption_part, output, down_rows, up_rows)
        )

        caption_part = caption_part.astype(F32).sum(axis=0)
        sums = layer_order(add_z(whole_of(caption_part[half_context:], width)))
        caption_part = caption_part[:half_context].astype(BF).reshape(z_size, -1, text_width // 4)
        caption_part = trade(caption_part, "z")
        down_parts = swap_parts(pick_rows([down_rows], rank))
        caption_part, down_parts, up_rows = lax.optimization_barrier(
            (caption_part, down_parts, up_rows)
        )

        caption_part = caption_part.astype(F32).sum(axis=0).astype(BF)
        caption_part = spread(caption_part, "z", z_size).reshape(half_context, -1)
        up_parts = swap_parts(pick_rows([up_rows], rank))
        down_grad = finish_wide(down_parts, rank)
        caption_part, up_parts, down_grad = lax.optimization_barrier(
            (caption_part, up_parts, down_grad)
        )

        caption_part = spread(caption_part)
        up_grad = finish_wide(up_parts, rank)
        caption_part, rest_rows, up_grad = lax.optimization_barrier(
            (caption_part, rest_rows, up_grad)
        )
        grad_caption = caption_output(caption_part, swap(caption_part, "c"), core)
        rest_rows = swap_parts(pick_rows([rest_rows], rank))
        grad_caption, rest_rows = lax.optimization_barrier((grad_caption, rest_rows))
        qkv_grad, out_grad, grad_cross, cross_out_grad = finish_all(
            rest_rows, kv_weight_grad, rank
        )
        return (
            outer(output).reshape(hidden.shape),
            outer(grad_hidden).reshape(hidden.shape),
            grad_caption,
            sums[:3],
            sums[3],
            qkv_grad.transpose(1, 0, 2),
            out_grad,
            grad_cross.transpose(1, 0, 2),
            cross_out_grad,
            grad_text_w,
            up_grad,
            down_grad,
        )

    return local


def solution(mesh):
    z_size = mesh.shape["img"] // 4
    inner = Mesh(mesh.devices.reshape(z_size, 2, 2, 2), ("z", "x", "c", "y"))
    image = ("z", "x", "c")
    tokens = P(image, "y", None)
    rows = P(image + ("y",))
    in_specs = (tokens, P(image, None), P(image), P(), P(), P()) + (rows,) * 7 + (tokens,)
    out_specs = (tokens, tokens, P(), P(), P()) + (rows,) * 7
    return jax.shard_map(
        make_local(z_size), mesh=inner, in_specs=in_specs, out_specs=out_specs, check_vma=False
    )
```

```python
import math

import jax
import jax.numpy as jnp
from jax import lax
from jax.experimental import pallas as pl
from jax.experimental.pallas import tpu as pltpu
from jax.sharding import Mesh
from jax.sharding import PartitionSpec as P

HD = 128
EPS = 1e-05
BF = jnp.bfloat16
F32 = jnp.float32
PAIR = ((0, 1), (1, 0))
GROUP = ("x", "y")
DATA = ("z", "c")
PLANE = ("x", "c", "y")
VMEM = 48 * 1024 * 1024
SCALE = 1.0 / math.sqrt(HD)
SLOPE = math.sqrt(2.0 / math.pi)
CUBIC = 0.044715


def dot(a, b, dims):
    return lax.dot_general(a, b, (dims, ((), ())), preferred_element_type=F32)


def mm(a, b):
    return dot(a, b, ((1,), (0,)))


def mm_t(a, b):
    return dot(a, b, ((1,), (1,)))


def t_mm(a, b):
    return dot(a, b, ((0,), (0,)))


def shape(dims, dtype=BF):
    return jax.ShapeDtypeStruct(dims, dtype)


def swap(values, axis):
    return lax.ppermute(values, axis, PAIR)


def trade(blocks, axes=GROUP):
    return lax.all_to_all(blocks, axes, 0, 0, tiled=True)


def spread(values, axes=GROUP, count=4):
    return trade(jnp.broadcast_to(values[None], (count,) + values.shape), axes)


def gather_tokens(own):
    half = own.shape[0] // 2
    from_x = swap(own, "x")
    from_y = swap(own, "y")
    return own, from_y, from_x, swap(from_x[:half], "y"), swap(from_y[half:], "x")


def gather_beside(own, work):
    half = own.shape[0] // 2
    from_x, from_y, work = lax.optimization_barrier((swap(own, "x"), swap(own, "y"), work))
    return (own, from_y, from_x, swap(from_x[:half], "y"), swap(from_y[half:], "x")), work


def scatter_first(parts):
    own, for_y, for_x, for_low, for_high = parts
    half = for_low.shape[0]
    low = swap(for_low, "y").astype(F32) + for_x[:half].astype(F32)
    high = swap(for_high, "x").astype(F32) + for_y[half:].astype(F32)
    return (
        own,
        jnp.concatenate([low.astype(BF), for_x[half:]], axis=0),
        jnp.concatenate([for_y[:half], high.astype(BF)], axis=0),
    )


def scatter_second(parts):
    own, for_x, for_y = parts
    return [own, swap(for_x, "x"), swap(for_y, "y")]


def scatter_tokens(parts):
    return scatter_second(scatter_first(parts))


def swap_parts(parts):
    return [
        parts[0],
        swap(parts[1], "y"),
        swap(parts[2], "x"),
        lax.ppermute(parts[3], GROUP, ((0, 3), (1, 2), (2, 1), (3, 0))),
    ]


def gather_rows(rows):
    return lax.all_gather(rows.reshape(-1, rows.shape[-1]), DATA, axis=0, tiled=True)


def scatter_grad(partial, axes):
    summed = lax.psum_scatter(partial, axes, scatter_dimension=0, tiled=True)
    return summed.reshape(4, -1, summed.shape[-1])


def call(kernel, grid, in_specs, out_specs, out_shape, operands, name, flops=0, size=1 << 22,
         rank=None, scratch=()):
    options = dict(
        out_shape=out_shape,
        compiler_params=pltpu.CompilerParams(vmem_limit_bytes=VMEM),
        cost_estimate=pl.CostEstimate(flops=flops, bytes_accessed=size, transcendentals=0),
        name=name,
    )
    if rank is None:
        return pl.pallas_call(
            kernel, grid=grid, in_specs=in_specs, out_specs=out_specs, scratch_shapes=scratch,
            **options,
        )(*operands)
    spec = pltpu.PrefetchScalarGridSpec(
        num_scalar_prefetch=1,
        grid=grid,
        in_specs=in_specs,
        out_specs=out_specs,
        scratch_shapes=scratch,
    )
    return pl.pallas_call(kernel, grid_spec=spec, **options)(rank.reshape(1), *operands)


def whole(array):
    return pl.BlockSpec(array.shape, lambda *_: (0,) * len(array.shape))


def reorder(values, unit, order):
    if order is None:
        return values
    return jnp.concatenate([values[:, k * unit : (k + 1) * unit] for k in order], axis=1)


def assemble(target, pieces, sems):
    copies, at = [], 0
    for k, piece in enumerate(pieces):
        rows = piece.shape[0]
        copies.append(pltpu.make_async_copy(piece, target.at[at : at + rows], sems.at[k]))
        at += rows
    for copy in copies:
        copy.start()
    for copy in copies:
        copy.wait()


ANY = pl.BlockSpec(memory_space=pl.ANY)


def gather_mm(pieces, weight, first, columns, name):
    rows, width = pieces[0].shape
    step = 256

    def kernel(*refs):
        tokens, out, sems = refs[6:]

        @pl.when(pl.program_id(0) == 0)
        def _():
            assemble(tokens, refs[:5], sems)

        out[...] = mm(tokens[...], refs[5][...]).astype(BF)

    return call(
        kernel,
        (columns // step,),
        [ANY] * 5 + [pl.BlockSpec((width, step), lambda j: (0, first // step + j))],
        [
            pl.BlockSpec((4 * rows, width), lambda j: (0, 0)),
            pl.BlockSpec((4 * rows, step), lambda j: (0, j)),
        ],
        [shape((4 * rows, width)), shape((4 * rows, columns))],
        [*pieces, weight],
        name,
        flops=8 * rows * width * columns,
        size=2 * width * (columns + 8 * rows),
        scratch=[pltpu.SemaphoreType.DMA((5,))],
    )


def mm_scatter(values, weight):
    return scatter_tokens(token_blocks(mm_t(values, weight).astype(BF)))


def token_blocks(partial):
    rows = partial.shape[0] // 4
    cuts = [0, rows, 2 * rows, 3 * rows, 3 * rows + rows // 2, 4 * rows]
    return [partial[a:b] for a, b in zip(cuts, cuts[1:])]


def normalize(values):
    centred = values - jnp.mean(values, axis=-1, keepdims=True)
    inv_std = lax.rsqrt(jnp.mean(centred * centred, axis=-1, keepdims=True) + EPS)
    return centred * inv_std, inv_std


NORM_ROWS = 32


def row_spec(array, at=None):
    width = array.shape[-1]
    if at is None:
        return pl.BlockSpec((NORM_ROWS, width), lambda i: (i, 0))
    return pl.BlockSpec((1, NORM_ROWS, width), lambda i, at=at: (at, i, 0))


def terms_of(terms):
    arrays, specs = [], []
    for term in terms:
        array, at = term if isinstance(term, tuple) else (term, None)
        arrays.append(array)
        specs.append(row_spec(array, at))
    return arrays, specs


def total_of(refs):
    values = [ref[0] if len(ref.shape) == 3 else ref[...] for ref in refs]
    return sum(value.astype(F32) for value in values)


def add_norm(terms, gain):
    arrays, specs = terms_of(terms)
    tokens, width = arrays[0].shape[-2], arrays[0].shape[-1]
    tokens = min(a.shape[-2] for a in arrays)

    def kernel(*refs):
        gain_ref, x, out = refs[-3:]
        values = total_of(refs[:-3])
        x[...] = values
        out[...] = (normalize(values)[0] * gain_ref[...]).astype(BF)

    return call(
        kernel,
        (tokens // NORM_ROWS,),
        specs + [whole(gain)],
        [row_spec(shape((tokens, width)))] * 2,
        [shape((tokens, width), F32), shape((tokens, width))],
        [*arrays, gain],
        "add_norm",
    )


def norm_grad(grad, values, gain):
    normed, inv_std = normalize(values)
    scaled = grad * gain
    first_mean = jnp.mean(scaled, axis=-1, keepdims=True)
    second_mean = jnp.mean(scaled * normed, axis=-1, keepdims=True)
    return (
        inv_std * (scaled - first_mean - normed * second_mean),
        jnp.sum(grad * normed, axis=0, keepdims=True),
    )


def accumulate(ref, value):
    @pl.when(pl.program_id(0) == 0)
    def _():
        ref[...] = jnp.zeros_like(ref)

    ref[...] += value


def norm_back(terms, upper, values, gain):
    arrays, specs = terms_of(terms)
    tokens, width = values.shape

    def kernel(*refs):
        upper_ref, x, gain_ref, out, out_low, gain_grad = refs[-6:]
        back, part = norm_grad(total_of(refs[:-6]), x[...], gain_ref[...])
        result = upper_ref[...].astype(F32) + back
        out[...] = result
        out_low[...] = result.astype(BF)
        accumulate(gain_grad, part)

    return call(
        kernel,
        (tokens // NORM_ROWS,),
        specs + [row_spec(upper), row_spec(values), whole(gain)],
        [row_spec(values)] * 2 + [pl.BlockSpec((1, width), lambda i: (0, 0))],
        [shape((tokens, width), F32), shape((tokens, width)), shape((1, width), F32)],
        [*arrays, upper, values, gain],
        "norm_back",
    )


def last_back(terms, upper, values, gain, masked, unit, order):
    arrays, specs = terms_of(terms)
    tokens, width = values.shape

    def kernel(*refs):
        upper_ref, x, gain_ref, mask, out, gain_grad, mask_grad = refs[-7:]
        back, part = norm_grad(total_of(refs[:-7]), x[...], gain_ref[...])
        result = upper_ref[...].astype(F32) + back
        hit = mask[...] > 0.5
        out[...] = reorder(jnp.where(hit, 0.0, result).astype(BF), unit, order)
        accumulate(gain_grad, part)
        accumulate(mask_grad, jnp.sum(jnp.where(hit, result, 0.0), axis=0, keepdims=True))

    line = pl.BlockSpec((1, width), lambda i: (0, 0))
    return call(
        kernel,
        (tokens // NORM_ROWS,),
        specs + [row_spec(upper), row_spec(values), whole(gain), row_spec(masked)],
        [row_spec(values), line, line],
        [shape((tokens, width)), shape((1, width), F32), shape((1, width), F32)],
        [*arrays, upper, values, gain, masked],
        "last_back",
    )


def start(hidden, cotangent, masked, embed, gain, unit, order):
    tokens, width = hidden.shape

    def kernel(hid, cot, mask, embed_ref, gain_ref, x, out, grad):
        hit = mask[...] > 0.5
        values = jnp.where(
            hit, embed_ref[...], reorder(hid[...], unit, order).astype(F32)
        )
        x[...] = values
        out[...] = (normalize(values)[0] * gain_ref[...]).astype(BF)
        grad[...] = jnp.where(hit, reorder(cot[...], unit, order).astype(F32), 0.0).astype(BF)

    rows = row_spec(hidden)
    return call(
        kernel,
        (tokens // NORM_ROWS,),
        [rows, rows, row_spec(masked), whole(embed), whole(gain)],
        [rows] * 3,
        [shape((tokens, width), F32), shape((tokens, width)), shape((tokens, width))],
        [hidden, cotangent, masked, embed, gain],
        "start",
    )


def layer_output(upper, terms, unit, order):
    arrays, specs = terms_of(terms)
    tokens, width = upper.shape

    def kernel(*refs):
        values = refs[-2][...] + total_of(refs[:-2])
        refs[-1][...] = reorder(values.astype(BF), unit, order)

    return call(
        kernel,
        (tokens // NORM_ROWS,),
        specs + [row_spec(upper)],
        row_spec(upper),
        shape((tokens, width)),
        [*arrays, upper],
        "layer_output",
    )


def feed_up(pieces, weight):
    rows, width = pieces[0].shape
    hidden = weight.shape[1]
    step = 256

    def kernel(*refs):
        up, tokens, act, slope, sems = refs[5:]

        @pl.when(pl.program_id(0) == 0)
        def _():
            assemble(tokens, refs[:5], sems)

        u = mm(tokens[...], up[...])
        square = u * u
        bend = jnp.tanh(SLOPE * u * (1.0 + CUBIC * square))
        half = 0.5 * (1.0 + bend)
        act[...] = (u * half).astype(BF)
        slope[...] = half + 0.5 * u * (1.0 - bend * bend) * SLOPE * (1.0 + 3.0 * CUBIC * square)

    part = pl.BlockSpec((4 * rows, step), lambda j: (0, j))
    return call(
        kernel,
        (hidden // step,),
        [ANY] * 5 + [pl.BlockSpec((width, step), lambda j: (0, j))],
        [pl.BlockSpec((4 * rows, width), lambda j: (0, 0)), part, part],
        [shape((4 * rows, width)), shape((4 * rows, hidden)), shape((4 * rows, hidden), F32)],
        [*pieces, weight],
        "feed_up",
        scratch=[pltpu.SemaphoreType.DMA((5,))],
        flops=8 * rows * width * hidden,
        size=2 * width * (hidden + 8 * rows),
    )


def feed_down(grad_y, slope, weight):
    tokens, width = grad_y.shape
    hidden = weight.shape[1]
    step = 256

    def kernel(dy, slope_ref, down, out):
        out[...] = (mm(dy[...], down[...]) * slope_ref[...]).astype(BF)

    part = pl.BlockSpec((tokens, step), lambda j: (0, j))
    return call(
        kernel,
        (hidden // step,),
        [whole(grad_y), part, pl.BlockSpec((width, step), lambda j: (0, j))],
        part,
        shape((tokens, hidden)),
        [grad_y, slope, weight],
        "feed_down",
        flops=2 * tokens * width * hidden,
        size=2 * width * (hidden + 8 * tokens),
    )


def softmax(scores):
    exp_terms = jnp.exp(scores - jnp.max(scores, axis=-1, keepdims=True))
    return exp_terms / jnp.sum(exp_terms, axis=-1, keepdims=True)


def score_grad(probs, grad_probs):
    return (
        probs * (grad_probs - jnp.sum(probs * grad_probs, axis=-1, keepdims=True))
    ).astype(BF)


def head(ref, k):
    return ref[:, k * HD : (k + 1) * HD]


def self_forward(projected, images):
    tokens, width = projected.shape
    rows, group = tokens // images, width // 3
    heads = group // HD

    def kernel(proj, mixed):
        for k in range(heads):
            query, key, value = (head(proj, j * heads + k) for j in range(3))
            probs = softmax(mm_t(query, key) * SCALE).astype(BF)
            mixed[:, k * HD : (k + 1) * HD] = mm(probs, value).astype(BF)

    return call(
        kernel,
        (images,),
        [pl.BlockSpec((rows, width), lambda i: (i, 0))],
        pl.BlockSpec((rows, group), lambda i: (i, 0)),
        shape((tokens, group)),
        [projected],
        "self_forward",
        flops=4 * tokens * rows * group,
    )


def self_back(projected, grad_mixed, images):
    tokens, width = projected.shape
    rows, group = tokens // images, width // 3
    heads = group // HD

    def kernel(proj, grad, out):
        for k in range(heads):
            query, key, value = (head(proj, j * heads + k) for j in range(3))
            grad_head = head(grad, k)
            probs = softmax(mm_t(query, key) * SCALE)
            grad_scores = score_grad(probs, mm_t(grad_head, value))
            parts = (
                mm(grad_scores, key) * SCALE,
                t_mm(grad_scores, query) * SCALE,
                t_mm(probs.astype(BF), grad_head),
            )
            for j, part in enumerate(parts):
                at = (j * heads + k) * HD
                out[:, at : at + HD] = part.astype(BF)

    return call(
        kernel,
        (images,),
        [
            pl.BlockSpec((rows, width), lambda i: (i, 0)),
            pl.BlockSpec((rows, group), lambda i: (i, 0)),
        ],
        pl.BlockSpec((rows, width), lambda i: (i, 0)),
        shape((tokens, width)),
        [projected, grad_mixed],
        "self_back",
        flops=10 * tokens * rows * group,
    )


def cross_forward(queries, text_kv):
    tokens, group = queries.shape
    heads = group // HD

    def kernel(query, text, mixed):
        for k in range(heads):
            probs = softmax(mm_t(head(query, k), head(text, k)) * SCALE).astype(BF)
            mixed[:, k * HD : (k + 1) * HD] = mm(probs, head(text, heads + k)).astype(BF)

    return call(
        kernel,
        (1,),
        [whole(queries), whole(text_kv)],
        whole(queries),
        shape((tokens, group)),
        [queries, text_kv],
        "cross_forward",
        flops=4 * tokens * text_kv.shape[0] * group,
    )


def cross_back(queries, text_kv, grad_mixed):
    tokens, group = queries.shape
    context = text_kv.shape[0]
    heads = group // HD

    def kernel(query, text, grad, grad_query, grad_text):
        for k in range(heads):
            query_head, key, value = head(query, k), head(text, k), head(text, heads + k)
            grad_head = head(grad, k)
            probs = softmax(mm_t(query_head, key) * SCALE)
            grad_scores = score_grad(probs, mm_t(grad_head, value))
            grad_query[:, k * HD : (k + 1) * HD] = (mm(grad_scores, key) * SCALE).astype(BF)
            at = (heads + k) * HD
            grad_text[:, k * HD : (k + 1) * HD] = t_mm(grad_scores, query_head) * SCALE
            grad_text[:, at : at + HD] = t_mm(probs.astype(BF), grad_head)

    return call(
        kernel,
        (1,),
        [whole(queries), whole(text_kv), whole(grad_mixed)],
        [whole(queries), whole(text_kv)],
        [shape((tokens, group)), shape((context, 2 * group), F32)],
        [queries, text_kv, grad_mixed],
        "cross_back",
        flops=10 * tokens * context * group,
    )


def grad_products(pairs, name, core=None, blocks=0):
    count_in = len(pairs[0][0])
    tokens, width = pairs[0][0][0].shape
    widths = [y[0].shape[1] for _, y in pairs]
    total = sum(widths)
    rows = 256 if core is None else width // (2 * blocks)
    steps = width // rows if core is None else blocks
    step = 512
    count = len(pairs) * count_in

    def kernel(r, *refs):
        out = refs[2 * count]
        offset = 0
        for k, wide in enumerate(widths):
            left = [refs[k * count_in + b][...].T for b in range(count_in)]
            for at in range(0, wide, step):
                out[:, offset + at : offset + at + step] = sum(
                    mm(left[b], refs[count + k * count_in + b][:, at : at + step])
                    for b in range(count_in)
                ).astype(BF)
            offset += wide

    pick = (lambda i, r: (0, i)) if core is None else (lambda i, r: (0, 2 * i + r[0]))
    return call(
        kernel,
        (steps,),
        [pl.BlockSpec((tokens, rows), pick)] * count
        + [pl.BlockSpec((tokens, w), lambda i, r: (0, 0)) for w in widths for _ in range(count_in)],
        pl.BlockSpec((rows, total), lambda i, r: (i, 0)),
        shape((steps * rows, total)),
        [b for x, _ in pairs for b in x] + [b for _, y in pairs for b in y],
        name,
        flops=2 * tokens * count_in * steps * rows * total,
        size=4 * width * total,
        rank=jnp.zeros((), jnp.int32) if core is None else core,
    )


def pick_weights(three, rank):
    rows, width = three.shape[1], three.shape[2] // 4

    def kernel(r, three_ref, *outs):
        for k in range(4):

            @pl.when(pl.program_id(0) == k)
            def _():
                for j in range(3):
                    outs[k][:, j * width : (j + 1) * width] = three_ref[j]

    outs = [shape((rows, 3 * width))] * 4
    return call(
        kernel,
        (4,),
        [pl.BlockSpec((3, rows, width), lambda k, r: (0, 0, k ^ r[0]))],
        [whole(a) for a in outs],
        outs,
        [three],
        "pick_weights",
        rank=rank,
    )


def pick_rows(arrays, rank):
    rows = arrays[0].shape[1]
    widths = [a.shape[2] for a in arrays]
    count = len(arrays)

    def kernel(r, *refs):
        for k in range(4):

            @pl.when(pl.program_id(0) == k)
            def _():
                at = 0
                for ref, width in zip(refs, widths):
                    refs[count + k][:, at : at + width] = ref[0]
                    at += width

    outs = [shape((rows, sum(widths)))] * 4
    return call(
        kernel,
        (4,),
        [pl.BlockSpec((1, rows, w), lambda k, r: (k ^ r[0], 0, 0)) for w in widths],
        [whole(a) for a in outs],
        outs,
        arrays,
        "pick_rows",
        rank=rank,
    )


def place(parts, rank):
    def kernel(r, *refs):
        for k in range(4):

            @pl.when(pl.program_id(0) == k)
            def _():
                refs[4][0] = refs[k][...]

    rows, columns = parts[0].shape
    return call(
        kernel,
        (4,),
        [whole(p) for p in parts],
        pl.BlockSpec((1, rows, columns), lambda k, r: (k ^ r[0], 0, 0)),
        shape((4, rows, columns)),
        parts,
        "place",
        rank=rank,
    )


def finish_wide(parts, rank):
    rows, width = parts[0].shape

    def kernel(r, *refs):
        for k in range(4):

            @pl.when(pl.program_id(0) == k)
            def _():
                refs[4][...] = refs[k][...].astype(F32)

    return call(
        kernel,
        (4,),
        [whole(p) for p in parts],
        pl.BlockSpec((rows, width), lambda k, r: (0, k ^ r[0])),
        shape((rows, 4 * width), F32),
        parts,
        "finish_wide",
        rank=rank,
    )


def finish_all(parts, text_grad, rank):
    rows, total = parts[0].shape
    width = total // 6

    def kernel(r, *refs):
        key, value, three, out, cross, cross_out = refs[4:]
        for k in range(4):

            @pl.when(pl.program_id(0) == k)
            def _():
                def part(j):
                    return refs[k][:, j * width : (j + 1) * width].astype(F32)

                for j in range(3):
                    three[j] = part(j)
                out[...] = part(3)
                cross[0] = part(4)
                cross_out[...] = part(5)

        cross[1] = key[...]
        cross[2] = value[...]

    wide = pl.BlockSpec((3, rows, width), lambda k, r: (0, 0, k ^ r[0]))
    flat = pl.BlockSpec((rows, width), lambda k, r: (0, k ^ r[0]))
    return call(
        kernel,
        (4,),
        [whole(p) for p in parts]
        + [flat, pl.BlockSpec((rows, width), lambda k, r: (0, 4 + (k ^ r[0])))],
        [wide, flat, wide, flat],
        [shape((3, rows, 4 * width), F32), shape((rows, 4 * width), F32)] * 2,
        [*parts, text_grad, text_grad],
        "finish_all",
        rank=rank,
    )


def plane_block(k):
    return (k >> 1) & 1, (k >> 2) * 2 + (k & 1)


def text_forward(caption, w_text, w_cross):
    context, rows = caption.shape[0], w_text.shape[0]
    half, width = context // 2, w_cross.shape[2] // 4

    def kernel(cap, weight, cross, own, blocks):
        own[...] = mm_t(cap[...], weight[...]).astype(BF)
        for j in range(2):
            part = mm(own[...], cross[1 + j]).astype(BF)
            for k in range(8):
                core, group = plane_block(k)
                blocks[k, :, j * width : (j + 1) * width] = part[
                    core * half : (core + 1) * half, group * width : (group + 1) * width
                ]

    return call(
        kernel,
        (1,),
        [whole(caption), whole(w_text), whole(w_cross)],
        [
            pl.BlockSpec((context, rows), lambda i: (0, 0)),
            pl.BlockSpec((8, half, 2 * width), lambda i: (0, 0, 0)),
        ],
        [shape((context, rows)), shape((8, half, 2 * width))],
        [caption, w_text, w_cross],
        "text_forward",
    )


def text_back(blocks, own_text, w_cross, caption, w_text):
    context, rows = own_text.shape
    half, width = context // 2, w_cross.shape[2] // 4
    wide = caption.shape[1] // 4

    def kernel(block, own, cross, cap, weight, kv_grad, text_grad, out, grads):
        for k in range(8):
            core, group = plane_block(k)
            for j in range(2):
                at = (4 * j + group) * width
                grads[core * half : (core + 1) * half, at : at + width] = block[
                    k, :, j * width : (j + 1) * width
                ]
        kv_grad[...] = t_mm(own[...], grads[...])
        grad_text = sum(
            mm_t(grads[:, 4 * j * width : 4 * (j + 1) * width], cross[1 + j]) for j in range(2)
        ).astype(BF)
        text_grad[...] = t_mm(grad_text, cap[...])
        part = mm(grad_text, weight[...]).astype(BF)
        for k in range(8):
            core, group = plane_block(k)
            out[k] = part[core * half : (core + 1) * half, group * wide : (group + 1) * wide]

    operands = [blocks, own_text, w_cross, caption, w_text]
    outs = [
        shape((rows, 8 * width), F32),
        shape((rows, 4 * wide), F32),
        shape((8, half, wide)),
    ]
    return call(
        kernel,
        (1,),
        [whole(a) for a in operands],
        [whole(a) for a in outs],
        outs,
        operands,
        "text_back",
        scratch=[pltpu.VMEM((context, 8 * width), BF)],
    )


def caption_output(own, other, core, half):
    count, _, wide = own.shape

    def kernel(r, own_ref, other_ref, out):
        block = jnp.where(pl.program_id(0) == r[0], own_ref[0], other_ref[0])
        out[...] = block.astype(F32)

    block = pl.BlockSpec((1, half, wide), lambda i, k, r: (k, 0, 0))
    return call(
        kernel,
        (2, count),
        [block, block],
        pl.BlockSpec((half, wide), lambda i, k, r: (i, k)),
        shape((2 * half, 4 * wide), F32),
        [own, other],
        "caption_output",
        rank=core,
    )


def column_blocks(weight, count):
    rows = weight.shape[0]
    return weight.reshape(rows, count, -1).transpose(1, 0, 2)


def halves_of(values, width):
    high = values.astype(BF)
    low = (values - high.astype(F32)).astype(BF)
    return jnp.concatenate([high.reshape(-1, width), low.reshape(-1, width)], axis=0)


def whole_of(halves, width):
    rows = halves.shape[0] // 2
    return (halves[:rows] + halves[rows:]).reshape(-1, width)


def make_local(z_size):
    def sum_z(values):
        parts = values.reshape(z_size, -1, values.shape[-1])
        mine = trade(parts, "z").astype(F32).sum(axis=0).astype(BF)
        return spread(mine, "z", z_size).reshape(values.shape)

    def add_z(values):
        step = 1
        while step < z_size:
            values = values + lax.ppermute(
                values, "z", tuple((k, k ^ step) for k in range(z_size))
            )
            step *= 2
        return values

    def layer_order(values):
        shaped = values.reshape(values.shape[:-1] + (z_size, 2, 2, -1))
        return jnp.swapaxes(shaped, -3, -2).reshape(values.shape)

    def local(
        hidden,
        mask_index,
        mask_count,
        mask_embed,
        norm_gains,
        caption,
        w_qkv,
        w_out,
        w_cross,
        w_cross_out,
        w_text,
        w_up,
        w_down,
        cotangent,
    ):
        images, local_rows, width = hidden.shape
        full_length = mask_index.shape[1]
        rank = lax.axis_index("x") * 2 + lax.axis_index("y")
        core = lax.axis_index("c")
        tokens = images * local_rows
        group = width // 4
        text_width = caption.shape[1]

        unit = width // (4 * z_size)
        inside = unit % 128 == 0
        order = [4 * k + j for k in range(z_size) for j in (0, 2, 1, 3)] if inside else None

        def outer(values):
            return values if inside else layer_order(values)

        w_qkv, w_cross = w_qkv.transpose(1, 0, 2), w_cross.transpose(1, 0, 2)
        first = swap_parts(pick_weights(w_qkv, rank))
        first = gather_rows(place(first, rank))

        positions = lax.axis_index("y") * local_rows + jnp.arange(local_rows, dtype=jnp.int32)
        ranks = jnp.arange(full_length, dtype=jnp.int32)
        matches = (mask_index[:, :, None] == positions[None, None, :]) & (
            ranks[None, :, None] < mask_count[:, None, None]
        )
        masked = jnp.any(matches, axis=1).reshape(tokens, 1).astype(F32)
        gains = layer_order(norm_gains)
        gain_a, gain_b, gain_c = gains[:1], gains[1:2], gains[2:]
        start_x, attn_in, grad_top = start(
            outer(hidden.reshape(tokens, width)),
            outer(cotangent.reshape(tokens, width)),
            masked,
            layer_order(mask_embed)[None],
            gain_a,
            unit,
            order,
        )
        attn_in = gather_tokens(attn_in)
        mid = [column_blocks(weight, 4) for weight in (w_out, w_cross[0], w_cross_out)]
        mid = jnp.concatenate(mid, axis=2)
        up = column_blocks(w_up, 4)
        attn_in, mid, up = lax.optimization_barrier((attn_in, mid, up))
        mid, up = gather_rows(trade(mid)), gather_rows(trade(up))

        own_text, kv_part = text_forward(caption, w_text, w_cross)
        text_kv = trade(kv_part, PLANE).astype(F32).sum(axis=0).astype(BF)
        text_kv = sum_z(text_kv)
        other = swap(text_kv, "c")
        text_kv = jnp.concatenate(
            [jnp.where(core == 0, text_kv, other), jnp.where(core == 0, other, text_kv)], axis=0
        )
        attn_in, text_kv = lax.optimization_barrier((attn_in, text_kv))

        attn_in, projected = gather_mm(attn_in, first, 0, 3 * group, "qkv_mm")
        self_mixed = self_forward(projected, 2 * images)
        down = column_blocks(w_down, 4)
        self_mixed, down = lax.optimization_barrier((self_mixed, down))
        down = gather_rows(trade(down))
        parts = mm_scatter(self_mixed, mid[:, :group])
        after_attn, cross_in = add_norm([start_x] + parts, gain_b)

        cross_in, cross_queries = gather_mm(
            gather_tokens(cross_in), mid, group, group, "query_mm"
        )
        cross_mixed = cross_forward(cross_queries, text_kv)
        parts = mm_scatter(cross_mixed, mid[:, 2 * group :])
        after_cross, mlp_in = add_norm([after_attn] + parts, gain_c)

        mlp_in = gather_tokens(mlp_in)
        mlp_in, grad_top = lax.optimization_barrier((mlp_in, grad_top))
        grad_y = jnp.concatenate(gather_tokens(grad_top), axis=0)
        mlp_in, activated, slope = feed_up(mlp_in, up)
        early = [attn_in, self_mixed, cross_in, cross_mixed]
        if inside:
            grad_axes, halves = "z", (core, z_size)

            def both(values):
                return [values, swap(values, "c")]

        else:
            grad_axes, halves = DATA, ()

            def both(values):
                return [values]

        early = [both(values) for values in early]
        down_part = grad_products([(both(grad_y), both(activated))], "down_grads", *halves)
        mlp_in = both(mlp_in)
        slope, down_part, early, mlp_in = lax.optimization_barrier((slope, down_part, early, mlp_in))
        down_rows = scatter_grad(down_part, grad_axes)
        grad_pre = feed_down(grad_y, slope, down)
        parts = mm_scatter(grad_pre, up)
        up_part = grad_products([(mlp_in, both(grad_pre))], "up_grads", *halves)
        grad_after_cross, cross_branch, gain_grad_c = norm_back(
            parts, grad_top, after_cross, gain_c
        )

        cross_branch, up_part = gather_beside(cross_branch, up_part)
        cross_branch, grad_cross_mixed = gather_mm(
            cross_branch, mid, 2 * group, group, "cross_out_back"
        )
        grad_cq, kv_grad = cross_back(cross_queries, text_kv, grad_cross_mixed)
        up_part, down_rows, kv_grad = lax.optimization_barrier((up_part, down_rows, kv_grad))
        up_rows = scatter_grad(up_part, grad_axes)
        cross_branch, grad_cq_both = both(cross_branch), both(grad_cq)
        parts = mm_scatter(grad_cq, mid[:, group : 2 * group])
        grad_after_attn, attn_branch, gain_grad_b = norm_back(
            parts, grad_after_cross, after_attn, gain_b
        )

        activated, attn_branch = lax.optimization_barrier((activated, attn_branch))
        result = mm_t(activated, down).astype(BF)
        attn_branch, result = gather_beside(attn_branch, result)
        attn_branch, result = lax.optimization_barrier((attn_branch, result))
        result = scatter_first(token_blocks(result))
        attn_branch, grad_self_mixed = gather_mm(attn_branch, mid, 0, group, "out_back")
        grad_projected = self_back(projected, grad_self_mixed, 2 * images)
        kv_part = kv_grad.astype(BF).reshape(2, z_size, -1, 2 * group)
        kv_part = kv_part.transpose(1, 0, 2, 3).reshape(2 * z_size, -1, 2 * group)
        grad_projected, result, kv_part = lax.optimization_barrier(
            (grad_projected, result, kv_part)
        )
        kv_part = trade(kv_part, DATA)
        result = scatter_second(result)
        rest_part = grad_products(
            [
                (early[0], both(grad_projected)),
                (both(attn_branch), early[1]),
                (early[2], grad_cq_both),
                (cross_branch, early[3]),
            ],
            "attention_grads",
            *halves,
        )
        grad_projected, result, kv_part, rest_part = lax.optimization_barrier(
            (grad_projected, result, kv_part, rest_part)
        )
        rest_part, up_rows = lax.optimization_barrier((rest_part, up_rows))
        rest_rows = scatter_grad(rest_part, grad_axes)

        kv_part = kv_part.astype(F32).sum(axis=0).astype(BF)
        kv_sum = spread(kv_part, "z", z_size).reshape(-1, 2 * group)
        kv_sum, grad_projected = lax.optimization_barrier((kv_sum, grad_projected))
        kv_grads = spread(kv_sum, PLANE, 8)
        parts = mm_scatter(grad_projected, first)
        kv_weight_grad, grad_text_w, caption_part = text_back(
            kv_grads, own_text, w_cross, caption, w_text
        )
        half_context = caption.shape[0] // 2
        caption_part = trade(caption_part, PLANE)
        output = layer_output(after_cross, result, unit, order)
        caption_part, output, parts, down_rows, up_rows = lax.optimization_barrier(
            (caption_part, output, parts, down_rows, up_rows)
        )

        caption_part = caption_part.astype(F32).sum(axis=0).astype(BF)
        caption_part = trade(caption_part.reshape(z_size, -1, text_width // 4), "z")
        down_parts = swap_parts(pick_rows([down_rows], rank))
        caption_part, down_parts, up_rows = lax.optimization_barrier(
            (caption_part, down_parts, up_rows)
        )

        caption_part = caption_part.astype(F32).sum(axis=0).astype(BF)
        caption_part = spread(caption_part, "z", z_size).reshape(half_context, -1)
        grad_hidden, gain_grad_a, mask_grad = last_back(
            parts, grad_after_attn, start_x, gain_a, masked, unit, order
        )
        sums = jnp.concatenate([gain_grad_a, gain_grad_b, gain_grad_c, mask_grad], axis=0)
        up_parts = swap_parts(pick_rows([up_rows], rank))
        down_grad = finish_wide(down_parts, rank)
        caption_part, sums, up_parts, down_grad = lax.optimization_barrier(
            (caption_part, sums, up_parts, down_grad)
        )

        caption_part = jnp.concatenate([caption_part, halves_of(sums, text_width // 4)], axis=0)
        caption_part = spread(caption_part)
        up_grad = finish_wide(up_parts, rank)
        caption_part, rest_rows, up_grad = lax.optimization_barrier(
            (caption_part, rest_rows, up_grad)
        )
        caption_far = swap(caption_part, "c")
        grad_caption = caption_output(caption_part, caption_far, core, half_context)
        sums = sum(
            part[:, half_context:].astype(F32).sum(axis=0) for part in (caption_part, caption_far)
        )
        sums = layer_order(add_z(whole_of(sums, width)))
        rest_rows = swap_parts(pick_rows([rest_rows], rank))
        grad_caption, rest_rows = lax.optimization_barrier((grad_caption, rest_rows))
        qkv_grad, out_grad, grad_cross, cross_out_grad = finish_all(
            rest_rows, kv_weight_grad, rank
        )
        return (
            outer(output).reshape(hidden.shape),
            outer(grad_hidden).reshape(hidden.shape),
            grad_caption,
            sums[:3],
            sums[3],
            qkv_grad.transpose(1, 0, 2),
            out_grad,
            grad_cross.transpose(1, 0, 2),
            cross_out_grad,
            grad_text_w,
            up_grad,
            down_grad,
        )

    return local


def solution(mesh):
    z_size = mesh.shape["img"] // 4
    inner = Mesh(mesh.devices.reshape(z_size, 2, 2, 2), ("z", "x", "c", "y"))
    image = ("z", "x", "c")
    tokens = P(image, "y", None)
    rows = P(image + ("y",))
    in_specs = (tokens, P(image, None), P(image), P(), P(), P()) + (rows,) * 7 + (tokens,)
    out_specs = (tokens, tokens, P(), P(), P()) + (rows,) * 7
    return jax.shard_map(
        make_local(z_size), mesh=inner, in_specs=in_specs, out_specs=out_specs, check_vma=False
    )
```

```python
import math

import jax
import jax.numpy as jnp
from jax import lax
from jax.experimental import pallas as pl
from jax.experimental.pallas import tpu as pltpu
from jax.sharding import Mesh
from jax.sharding import PartitionSpec as P

HD = 128
EPS = 1e-05
BF = jnp.bfloat16
F32 = jnp.float32
PAIR = ((0, 1), (1, 0))
GROUP = ("x", "y")
DATA = ("z", "c")
PLANE = ("x", "c", "y")
VMEM = 48 * 1024 * 1024
SCALE = 1.0 / math.sqrt(HD)
SLOPE = math.sqrt(2.0 / math.pi)
CUBIC = 0.044715


def dot(a, b, dims):
    return lax.dot_general(a, b, (dims, ((), ())), preferred_element_type=F32)


def mm(a, b):
    return dot(a, b, ((1,), (0,)))


def mm_t(a, b):
    return dot(a, b, ((1,), (1,)))


def t_mm(a, b):
    return dot(a, b, ((0,), (0,)))


def shape(dims, dtype=BF):
    return jax.ShapeDtypeStruct(dims, dtype)


def swap(values, axis):
    return lax.ppermute(values, axis, PAIR)


def trade(blocks, axes=GROUP):
    return lax.all_to_all(blocks, axes, 0, 0, tiled=True)


def spread(values, axes=GROUP, count=4):
    return trade(jnp.broadcast_to(values[None], (count,) + values.shape), axes)


def gather_tokens(own):
    half = own.shape[0] // 2
    from_x = swap(own, "x")
    from_y = swap(own, "y")
    return own, from_y, from_x, swap(from_x[:half], "y"), swap(from_y[half:], "x")


def gather_beside(own, work):
    half = own.shape[0] // 2
    from_x, from_y, work = lax.optimization_barrier((swap(own, "x"), swap(own, "y"), work))
    return (own, from_y, from_x, swap(from_x[:half], "y"), swap(from_y[half:], "x")), work


def scatter_first(parts):
    own, for_y, for_x, for_low, for_high = parts
    half = for_low.shape[0]
    low = swap(for_low, "y").astype(F32) + for_x[:half].astype(F32)
    high = swap(for_high, "x").astype(F32) + for_y[half:].astype(F32)
    return (
        own,
        jnp.concatenate([low.astype(BF), for_x[half:]], axis=0),
        jnp.concatenate([for_y[:half], high.astype(BF)], axis=0),
    )


def scatter_second(parts):
    own, for_x, for_y = parts
    return [own, swap(for_x, "x"), swap(for_y, "y")]


def scatter_tokens(parts):
    return scatter_second(scatter_first(parts))


def swap_parts(parts):
    return [
        parts[0],
        swap(parts[1], "y"),
        swap(parts[2], "x"),
        lax.ppermute(parts[3], GROUP, ((0, 3), (1, 2), (2, 1), (3, 0))),
    ]


def gather_rows(rows):
    return lax.all_gather(rows.reshape(-1, rows.shape[-1]), DATA, axis=0, tiled=True)


def scatter_grad(partial, axes):
    summed = lax.psum_scatter(partial, axes, scatter_dimension=0, tiled=True)
    return summed.reshape(4, -1, summed.shape[-1])


def call(kernel, grid, in_specs, out_specs, out_shape, operands, name, flops=0, size=1 << 22,
         rank=None, scratch=()):
    options = dict(
        out_shape=out_shape,
        compiler_params=pltpu.CompilerParams(vmem_limit_bytes=VMEM),
        cost_estimate=pl.CostEstimate(flops=flops, bytes_accessed=size, transcendentals=0),
        name=name,
    )
    if rank is None:
        return pl.pallas_call(
            kernel, grid=grid, in_specs=in_specs, out_specs=out_specs, scratch_shapes=scratch,
            **options,
        )(*operands)
    spec = pltpu.PrefetchScalarGridSpec(
        num_scalar_prefetch=1,
        grid=grid,
        in_specs=in_specs,
        out_specs=out_specs,
        scratch_shapes=scratch,
    )
    return pl.pallas_call(kernel, grid_spec=spec, **options)(rank.reshape(1), *operands)


def whole(array):
    return pl.BlockSpec(array.shape, lambda *_: (0,) * len(array.shape))


def reorder(values, unit, order):
    if order is None:
        return values
    return jnp.concatenate([values[:, k * unit : (k + 1) * unit] for k in order], axis=1)


def assemble(target, pieces, sems):
    copies, at = [], 0
    for k, piece in enumerate(pieces):
        rows = piece.shape[0]
        copies.append(pltpu.make_async_copy(piece, target.at[at : at + rows], sems.at[k]))
        at += rows
    for copy in copies:
        copy.start()
    for copy in copies:
        copy.wait()


ANY = pl.BlockSpec(memory_space=pl.ANY)


def gather_mm(pieces, weight, first, columns, name):
    rows, width = pieces[0].shape
    step = 256

    def kernel(*refs):
        tokens, out, sems = refs[6:]

        @pl.when(pl.program_id(0) == 0)
        def _():
            assemble(tokens, refs[:5], sems)

        out[...] = mm(tokens[...], refs[5][...]).astype(BF)

    return call(
        kernel,
        (columns // step,),
        [ANY] * 5 + [pl.BlockSpec((width, step), lambda j: (0, first // step + j))],
        [
            pl.BlockSpec((4 * rows, width), lambda j: (0, 0)),
            pl.BlockSpec((4 * rows, step), lambda j: (0, j)),
        ],
        [shape((4 * rows, width)), shape((4 * rows, columns))],
        [*pieces, weight],
        name,
        flops=8 * rows * width * columns,
        size=2 * width * (columns + 8 * rows),
        scratch=[pltpu.SemaphoreType.DMA((5,))],
    )


def mm_scatter(values, weight):
    return scatter_tokens(token_blocks(mm_t(values, weight).astype(BF)))


def token_blocks(partial):
    rows = partial.shape[0] // 4
    cuts = [0, rows, 2 * rows, 3 * rows, 3 * rows + rows // 2, 4 * rows]
    return [partial[a:b] for a, b in zip(cuts, cuts[1:])]


def normalize(values):
    centred = values - jnp.mean(values, axis=-1, keepdims=True)
    inv_std = lax.rsqrt(jnp.mean(centred * centred, axis=-1, keepdims=True) + EPS)
    return centred * inv_std, inv_std


NORM_ROWS = 32


def row_spec(array, at=None):
    width = array.shape[-1]
    if at is None:
        return pl.BlockSpec((NORM_ROWS, width), lambda i: (i, 0))
    return pl.BlockSpec((1, NORM_ROWS, width), lambda i, at=at: (at, i, 0))


def terms_of(terms):
    arrays, specs = [], []
    for term in terms:
        array, at = term if isinstance(term, tuple) else (term, None)
        arrays.append(array)
        specs.append(row_spec(array, at))
    return arrays, specs


def total_of(refs):
    values = [ref[0] if len(ref.shape) == 3 else ref[...] for ref in refs]
    return sum(value.astype(F32) for value in values)


def add_norm(terms, gain):
    arrays, specs = terms_of(terms)
    tokens, width = arrays[0].shape[-2], arrays[0].shape[-1]
    tokens = min(a.shape[-2] for a in arrays)

    def kernel(*refs):
        gain_ref, x, out = refs[-3:]
        values = total_of(refs[:-3])
        x[...] = values
        out[...] = (normalize(values)[0] * gain_ref[...]).astype(BF)

    return call(
        kernel,
        (tokens // NORM_ROWS,),
        specs + [whole(gain)],
        [row_spec(shape((tokens, width)))] * 2,
        [shape((tokens, width), F32), shape((tokens, width))],
        [*arrays, gain],
        "add_norm",
    )


def norm_grad(grad, values, gain):
    normed, inv_std = normalize(values)
    scaled = grad * gain
    first_mean = jnp.mean(scaled, axis=-1, keepdims=True)
    second_mean = jnp.mean(scaled * normed, axis=-1, keepdims=True)
    return (
        inv_std * (scaled - first_mean - normed * second_mean),
        jnp.sum(grad * normed, axis=0, keepdims=True),
    )


def accumulate(ref, value):
    @pl.when(pl.program_id(0) == 0)
    def _():
        ref[...] = jnp.zeros_like(ref)

    ref[...] += value


def norm_back(terms, upper, values, gain):
    arrays, specs = terms_of(terms)
    tokens, width = values.shape

    def kernel(*refs):
        upper_ref, x, gain_ref, out, out_low, gain_grad = refs[-6:]
        back, part = norm_grad(total_of(refs[:-6]), x[...], gain_ref[...])
        result = upper_ref[...].astype(F32) + back
        out[...] = result
        out_low[...] = result.astype(BF)
        accumulate(gain_grad, part)

    return call(
        kernel,
        (tokens // NORM_ROWS,),
        specs + [row_spec(upper), row_spec(values), whole(gain)],
        [row_spec(values)] * 2 + [pl.BlockSpec((1, width), lambda i: (0, 0))],
        [shape((tokens, width), F32), shape((tokens, width)), shape((1, width), F32)],
        [*arrays, upper, values, gain],
        "norm_back",
    )


def last_back(terms, upper, values, gain, masked, unit, order):
    arrays, specs = terms_of(terms)
    tokens, width = values.shape

    def kernel(*refs):
        upper_ref, x, gain_ref, mask, out, gain_grad, mask_grad = refs[-7:]
        back, part = norm_grad(total_of(refs[:-7]), x[...], gain_ref[...])
        result = upper_ref[...].astype(F32) + back
        hit = mask[...] > 0.5
        out[...] = reorder(jnp.where(hit, 0.0, result).astype(BF), unit, order)
        accumulate(gain_grad, part)
        accumulate(mask_grad, jnp.sum(jnp.where(hit, result, 0.0), axis=0, keepdims=True))

    line = pl.BlockSpec((1, width), lambda i: (0, 0))
    return call(
        kernel,
        (tokens // NORM_ROWS,),
        specs + [row_spec(upper), row_spec(values), whole(gain), row_spec(masked)],
        [row_spec(values), line, line],
        [shape((tokens, width)), shape((1, width), F32), shape((1, width), F32)],
        [*arrays, upper, values, gain, masked],
        "last_back",
    )


def start(hidden, cotangent, masked, embed, gain, unit, order):
    tokens, width = hidden.shape

    def kernel(hid, cot, mask, embed_ref, gain_ref, x, out, grad):
        hit = mask[...] > 0.5
        values = jnp.where(
            hit, embed_ref[...], reorder(hid[...], unit, order).astype(F32)
        )
        x[...] = values
        out[...] = (normalize(values)[0] * gain_ref[...]).astype(BF)
        grad[...] = jnp.where(hit, reorder(cot[...], unit, order).astype(F32), 0.0).astype(BF)

    rows = row_spec(hidden)
    return call(
        kernel,
        (tokens // NORM_ROWS,),
        [rows, rows, row_spec(masked), whole(embed), whole(gain)],
        [rows] * 3,
        [shape((tokens, width), F32), shape((tokens, width)), shape((tokens, width))],
        [hidden, cotangent, masked, embed, gain],
        "start",
    )


def layer_output(upper, terms, unit, order):
    arrays, specs = terms_of(terms)
    tokens, width = upper.shape

    def kernel(*refs):
        values = refs[-2][...] + total_of(refs[:-2])
        refs[-1][...] = reorder(values.astype(BF), unit, order)

    return call(
        kernel,
        (tokens // NORM_ROWS,),
        specs + [row_spec(upper)],
        row_spec(upper),
        shape((tokens, width)),
        [*arrays, upper],
        "layer_output",
    )


def feed_up(pieces, weight):
    rows, width = pieces[0].shape
    hidden = weight.shape[1]
    step = 256

    def kernel(*refs):
        up, tokens, act, slope, sems = refs[5:]

        @pl.when(pl.program_id(0) == 0)
        def _():
            assemble(tokens, refs[:5], sems)

        u = mm(tokens[...], up[...])
        square = u * u
        bend = jnp.tanh(SLOPE * u * (1.0 + CUBIC * square))
        half = 0.5 * (1.0 + bend)
        act[...] = (u * half).astype(BF)
        slope[...] = half + 0.5 * u * (1.0 - bend * bend) * SLOPE * (1.0 + 3.0 * CUBIC * square)

    part = pl.BlockSpec((4 * rows, step), lambda j: (0, j))
    return call(
        kernel,
        (hidden // step,),
        [ANY] * 5 + [pl.BlockSpec((width, step), lambda j: (0, j))],
        [pl.BlockSpec((4 * rows, width), lambda j: (0, 0)), part, part],
        [shape((4 * rows, width)), shape((4 * rows, hidden)), shape((4 * rows, hidden), F32)],
        [*pieces, weight],
        "feed_up",
        scratch=[pltpu.SemaphoreType.DMA((5,))],
        flops=8 * rows * width * hidden,
        size=2 * width * (hidden + 8 * rows),
    )


def feed_down(grad_y, slope, weight):
    tokens, width = grad_y.shape
    hidden = weight.shape[1]
    step = 256

    def kernel(dy, slope_ref, down, out):
        out[...] = (mm(dy[...], down[...]) * slope_ref[...]).astype(BF)

    part = pl.BlockSpec((tokens, step), lambda j: (0, j))
    return call(
        kernel,
        (hidden // step,),
        [whole(grad_y), part, pl.BlockSpec((width, step), lambda j: (0, j))],
        part,
        shape((tokens, hidden)),
        [grad_y, slope, weight],
        "feed_down",
        flops=2 * tokens * width * hidden,
        size=2 * width * (hidden + 8 * tokens),
    )


def softmax(scores):
    exp_terms = jnp.exp(scores - jnp.max(scores, axis=-1, keepdims=True))
    return exp_terms / jnp.sum(exp_terms, axis=-1, keepdims=True)


def score_grad(probs, grad_probs):
    return (
        probs * (grad_probs - jnp.sum(probs * grad_probs, axis=-1, keepdims=True))
    ).astype(BF)


def head(ref, k):
    return ref[:, k * HD : (k + 1) * HD]


def self_forward(projected, images):
    tokens, width = projected.shape
    rows, group = tokens // images, width // 3
    heads = group // HD

    def kernel(proj, mixed):
        for k in range(heads):
            query, key, value = (head(proj, j * heads + k) for j in range(3))
            probs = softmax(mm_t(query, key) * SCALE).astype(BF)
            mixed[:, k * HD : (k + 1) * HD] = mm(probs, value).astype(BF)

    return call(
        kernel,
        (images,),
        [pl.BlockSpec((rows, width), lambda i: (i, 0))],
        pl.BlockSpec((rows, group), lambda i: (i, 0)),
        shape((tokens, group)),
        [projected],
        "self_forward",
        flops=4 * tokens * rows * group,
    )


def self_back(projected, grad_mixed, images):
    tokens, width = projected.shape
    rows, group = tokens // images, width // 3
    heads = group // HD

    def kernel(proj, grad, out):
        for k in range(heads):
            query, key, value = (head(proj, j * heads + k) for j in range(3))
            grad_head = head(grad, k)
            probs = softmax(mm_t(query, key) * SCALE)
            grad_scores = score_grad(probs, mm_t(grad_head, value))
            parts = (
                mm(grad_scores, key) * SCALE,
                t_mm(grad_scores, query) * SCALE,
                t_mm(probs.astype(BF), grad_head),
            )
            for j, part in enumerate(parts):
                at = (j * heads + k) * HD
                out[:, at : at + HD] = part.astype(BF)

    return call(
        kernel,
        (images,),
        [
            pl.BlockSpec((rows, width), lambda i: (i, 0)),
            pl.BlockSpec((rows, group), lambda i: (i, 0)),
        ],
        pl.BlockSpec((rows, width), lambda i: (i, 0)),
        shape((tokens, width)),
        [projected, grad_mixed],
        "self_back",
        flops=10 * tokens * rows * group,
    )


def cross_forward(queries, text_kv):
    tokens, group = queries.shape
    heads = group // HD

    def kernel(query, text, mixed):
        for k in range(heads):
            probs = softmax(mm_t(head(query, k), head(text, k)) * SCALE).astype(BF)
            mixed[:, k * HD : (k + 1) * HD] = mm(probs, head(text, heads + k)).astype(BF)

    return call(
        kernel,
        (1,),
        [whole(queries), whole(text_kv)],
        whole(queries),
        shape((tokens, group)),
        [queries, text_kv],
        "cross_forward",
        flops=4 * tokens * text_kv.shape[0] * group,
    )


def cross_back(queries, text_kv, grad_mixed):
    tokens, group = queries.shape
    context = text_kv.shape[0]
    heads = group // HD

    def kernel(query, text, grad, grad_query, grad_text):
        for k in range(heads):
            query_head, key, value = head(query, k), head(text, k), head(text, heads + k)
            grad_head = head(grad, k)
            probs = softmax(mm_t(query_head, key) * SCALE)
            grad_scores = score_grad(probs, mm_t(grad_head, value))
            grad_query[:, k * HD : (k + 1) * HD] = (mm(grad_scores, key) * SCALE).astype(BF)
            at = (heads + k) * HD
            grad_text[:, k * HD : (k + 1) * HD] = t_mm(grad_scores, query_head) * SCALE
            grad_text[:, at : at + HD] = t_mm(probs.astype(BF), grad_head)

    return call(
        kernel,
        (1,),
        [whole(queries), whole(text_kv), whole(grad_mixed)],
        [whole(queries), whole(text_kv)],
        [shape((tokens, group)), shape((context, 2 * group), F32)],
        [queries, text_kv, grad_mixed],
        "cross_back",
        flops=10 * tokens * context * group,
    )


def grad_products(pairs, name, core=None, blocks=0):
    count_in = len(pairs[0][0])
    tokens, width = pairs[0][0][0].shape
    widths = [y[0].shape[1] for _, y in pairs]
    total = sum(widths)
    rows = 256 if core is None else width // (2 * blocks)
    steps = width // rows if core is None else blocks
    step = 512
    count = len(pairs) * count_in

    def kernel(r, *refs):
        out = refs[2 * count]
        offset = 0
        for k, wide in enumerate(widths):
            left = [refs[k * count_in + b][...].T for b in range(count_in)]
            for at in range(0, wide, step):
                out[:, offset + at : offset + at + step] = sum(
                    mm(left[b], refs[count + k * count_in + b][:, at : at + step])
                    for b in range(count_in)
                ).astype(BF)
            offset += wide

    pick = (lambda i, r: (0, i)) if core is None else (lambda i, r: (0, 2 * i + r[0]))
    return call(
        kernel,
        (steps,),
        [pl.BlockSpec((tokens, rows), pick)] * count
        + [pl.BlockSpec((tokens, w), lambda i, r: (0, 0)) for w in widths for _ in range(count_in)],
        pl.BlockSpec((rows, total), lambda i, r: (i, 0)),
        shape((steps * rows, total)),
        [b for x, _ in pairs for b in x] + [b for _, y in pairs for b in y],
        name,
        flops=2 * tokens * count_in * steps * rows * total,
        size=4 * width * total,
        rank=jnp.zeros((), jnp.int32) if core is None else core,
    )


def pick_weights(three, rank):
    rows, width = three.shape[1], three.shape[2] // 4

    def kernel(r, three_ref, *outs):
        for k in range(4):

            @pl.when(pl.program_id(0) == k)
            def _():
                for j in range(3):
                    outs[k][:, j * width : (j + 1) * width] = three_ref[j]

    outs = [shape((rows, 3 * width))] * 4
    return call(
        kernel,
        (4,),
        [pl.BlockSpec((3, rows, width), lambda k, r: (0, 0, k ^ r[0]))],
        [whole(a) for a in outs],
        outs,
        [three],
        "pick_weights",
        rank=rank,
    )


def pick_rows(arrays, rank):
    rows = arrays[0].shape[1]
    widths = [a.shape[2] for a in arrays]
    count = len(arrays)

    def kernel(r, *refs):
        for k in range(4):

            @pl.when(pl.program_id(0) == k)
            def _():
                at = 0
                for ref, width in zip(refs, widths):
                    refs[count + k][:, at : at + width] = ref[0]
                    at += width

    outs = [shape((rows, sum(widths)))] * 4
    return call(
        kernel,
        (4,),
        [pl.BlockSpec((1, rows, w), lambda k, r: (k ^ r[0], 0, 0)) for w in widths],
        [whole(a) for a in outs],
        outs,
        arrays,
        "pick_rows",
        rank=rank,
    )


def place(parts, rank):
    def kernel(r, *refs):
        for k in range(4):

            @pl.when(pl.program_id(0) == k)
            def _():
                refs[4][0] = refs[k][...]

    rows, columns = parts[0].shape
    return call(
        kernel,
        (4,),
        [whole(p) for p in parts],
        pl.BlockSpec((1, rows, columns), lambda k, r: (k ^ r[0], 0, 0)),
        shape((4, rows, columns)),
        parts,
        "place",
        rank=rank,
    )


def finish_wide(parts, rank):
    rows, width = parts[0].shape

    def kernel(r, *refs):
        for k in range(4):

            @pl.when(pl.program_id(0) == k)
            def _():
                refs[4][...] = refs[k][...].astype(F32)

    return call(
        kernel,
        (4,),
        [whole(p) for p in parts],
        pl.BlockSpec((rows, width), lambda k, r: (0, k ^ r[0])),
        shape((rows, 4 * width), F32),
        parts,
        "finish_wide",
        rank=rank,
    )


def finish_attention(parts, rank):
    rows, total = parts[0].shape
    width = total // 4

    def kernel(r, *refs):
        three, out = refs[4:]
        for k in range(4):

            @pl.when(pl.program_id(0) == k)
            def _():
                for j in range(3):
                    three[j] = refs[k][:, j * width : (j + 1) * width].astype(F32)
                out[...] = refs[k][:, 3 * width :].astype(F32)

    return call(
        kernel,
        (4,),
        [whole(p) for p in parts],
        [
            pl.BlockSpec((3, rows, width), lambda k, r: (0, 0, k ^ r[0])),
            pl.BlockSpec((rows, width), lambda k, r: (0, k ^ r[0])),
        ],
        [shape((3, rows, 4 * width), F32), shape((rows, 4 * width), F32)],
        parts,
        "finish_attention",
        rank=rank,
    )


def finish_cross(parts, text_grad, rank):
    rows, total = parts[0].shape
    width = total // 2

    def kernel(r, *refs):
        key, value, three, out = refs[4:]
        for k in range(4):

            @pl.when(pl.program_id(0) == k)
            def _():
                three[0] = refs[k][:, :width].astype(F32)
                out[...] = refs[k][:, width:].astype(F32)

        three[1] = key[...]
        three[2] = value[...]

    flat = pl.BlockSpec((rows, width), lambda k, r: (0, k ^ r[0]))
    return call(
        kernel,
        (4,),
        [whole(p) for p in parts]
        + [flat, pl.BlockSpec((rows, width), lambda k, r: (0, 4 + (k ^ r[0])))],
        [pl.BlockSpec((3, rows, width), lambda k, r: (0, 0, k ^ r[0])), flat],
        [shape((3, rows, 4 * width), F32), shape((rows, 4 * width), F32)],
        [*parts, text_grad, text_grad],
        "finish_cross",
        rank=rank,
    )


def plane_block(k):
    return (k >> 1) & 1, (k >> 2) * 2 + (k & 1)


def text_forward(caption, w_text, w_cross):
    context, rows = caption.shape[0], w_text.shape[0]
    half, width = context // 2, w_cross.shape[2] // 4

    def kernel(cap, weight, cross, own, blocks):
        own[...] = mm_t(cap[...], weight[...]).astype(BF)
        for j in range(2):
            part = mm(own[...], cross[1 + j]).astype(BF)
            for k in range(8):
                core, group = plane_block(k)
                blocks[k, :, j * width : (j + 1) * width] = part[
                    core * half : (core + 1) * half, group * width : (group + 1) * width
                ]

    return call(
        kernel,
        (1,),
        [whole(caption), whole(w_text), whole(w_cross)],
        [
            pl.BlockSpec((context, rows), lambda i: (0, 0)),
            pl.BlockSpec((8, half, 2 * width), lambda i: (0, 0, 0)),
        ],
        [shape((context, rows)), shape((8, half, 2 * width))],
        [caption, w_text, w_cross],
        "text_forward",
    )


def text_back(blocks, own_text, w_cross, caption, w_text, extra):
    context, rows = own_text.shape
    half, width = context // 2, w_cross.shape[2] // 4
    wide = caption.shape[1] // 4
    tail = extra.shape[0]

    def kernel(block, own, cross, cap, weight, more, kv_grad, text_grad, out, grads):
        for k in range(8):
            core, group = plane_block(k)
            for j in range(2):
                at = (4 * j + group) * width
                grads[core * half : (core + 1) * half, at : at + width] = block[
                    k, :, j * width : (j + 1) * width
                ]
        kv_grad[...] = t_mm(own[...], grads[...])
        grad_text = sum(
            mm_t(grads[:, 4 * j * width : 4 * (j + 1) * width], cross[1 + j]) for j in range(2)
        ).astype(BF)
        text_grad[...] = t_mm(grad_text, cap[...])
        part = mm(grad_text, weight[...]).astype(BF)
        for k in range(8):
            core, group = plane_block(k)
            out[k, :half, :] = part[core * half : (core + 1) * half, group * wide : (group + 1) * wide]
            out[k, half:, :] = more[...]

    operands = [blocks, own_text, w_cross, caption, w_text, extra]
    outs = [
        shape((rows, 8 * width), F32),
        shape((rows, 4 * wide), F32),
        shape((8, half + tail, wide)),
    ]
    return call(
        kernel,
        (1,),
        [whole(a) for a in operands],
        [whole(a) for a in outs],
        outs,
        operands,
        "text_back",
        scratch=[pltpu.VMEM((context, 8 * width), BF)],
    )


def caption_output(own, other, core):
    count, half, wide = own.shape

    def kernel(r, own_ref, other_ref, out):
        block = jnp.where(pl.program_id(0) == r[0], own_ref[0], other_ref[0])
        out[...] = block.astype(F32)

    block = pl.BlockSpec((1, half, wide), lambda i, k, r: (k, 0, 0))
    return call(
        kernel,
        (2, count),
        [block, block],
        pl.BlockSpec((half, wide), lambda i, k, r: (i, k)),
        shape((2 * half, 4 * wide), F32),
        [own, other],
        "caption_output",
        rank=core,
    )


def column_blocks(weight, count):
    rows = weight.shape[0]
    return weight.reshape(rows, count, -1).transpose(1, 0, 2)


def halves_of(values, width):
    high = values.astype(BF)
    low = (values - high.astype(F32)).astype(BF)
    return jnp.concatenate([high.reshape(-1, width), low.reshape(-1, width)], axis=0)


def whole_of(halves, width):
    rows = halves.shape[0] // 2
    return (halves[:rows] + halves[rows:]).reshape(-1, width)


def make_local(z_size):
    def sum_z(values):
        parts = values.reshape(z_size, -1, values.shape[-1])
        mine = trade(parts, "z").astype(F32).sum(axis=0).astype(BF)
        return spread(mine, "z", z_size).reshape(values.shape)

    def add_z(values):
        step = 1
        while step < z_size:
            values = values + lax.ppermute(
                values, "z", tuple((k, k ^ step) for k in range(z_size))
            )
            step *= 2
        return values

    def layer_order(values):
        shaped = values.reshape(values.shape[:-1] + (z_size, 2, 2, -1))
        return jnp.swapaxes(shaped, -3, -2).reshape(values.shape)

    def local(
        hidden,
        mask_index,
        mask_count,
        mask_embed,
        norm_gains,
        caption,
        w_qkv,
        w_out,
        w_cross,
        w_cross_out,
        w_text,
        w_up,
        w_down,
        cotangent,
    ):
        images, local_rows, width = hidden.shape
        full_length = mask_index.shape[1]
        rank = lax.axis_index("x") * 2 + lax.axis_index("y")
        core = lax.axis_index("c")
        tokens = images * local_rows
        group = width // 4
        text_width = caption.shape[1]

        unit = width // (4 * z_size)
        inside = unit % 128 == 0
        order = [4 * k + j for k in range(z_size) for j in (0, 2, 1, 3)] if inside else None

        def outer(values):
            return values if inside else layer_order(values)

        w_qkv, w_cross = w_qkv.transpose(1, 0, 2), w_cross.transpose(1, 0, 2)
        first = swap_parts(pick_weights(w_qkv, rank))
        first = gather_rows(place(first, rank))

        positions = lax.axis_index("y") * local_rows + jnp.arange(local_rows, dtype=jnp.int32)
        ranks = jnp.arange(full_length, dtype=jnp.int32)
        matches = (mask_index[:, :, None] == positions[None, None, :]) & (
            ranks[None, :, None] < mask_count[:, None, None]
        )
        masked = jnp.any(matches, axis=1).reshape(tokens, 1).astype(F32)
        gains = layer_order(norm_gains)
        gain_a, gain_b, gain_c = gains[:1], gains[1:2], gains[2:]
        start_x, attn_in, grad_top = start(
            outer(hidden.reshape(tokens, width)),
            outer(cotangent.reshape(tokens, width)),
            masked,
            layer_order(mask_embed)[None],
            gain_a,
            unit,
            order,
        )
        attn_in = gather_tokens(attn_in)
        mid = [column_blocks(weight, 4) for weight in (w_out, w_cross[0], w_cross_out)]
        mid = jnp.concatenate(mid, axis=2)
        up = column_blocks(w_up, 4)
        attn_in, mid, up = lax.optimization_barrier((attn_in, mid, up))
        mid, up = gather_rows(trade(mid)), gather_rows(trade(up))

        own_text, kv_part = text_forward(caption, w_text, w_cross)
        text_kv = trade(kv_part, PLANE).astype(F32).sum(axis=0).astype(BF)
        text_kv = sum_z(text_kv)
        other = swap(text_kv, "c")
        text_kv = jnp.concatenate(
            [jnp.where(core == 0, text_kv, other), jnp.where(core == 0, other, text_kv)], axis=0
        )
        attn_in, text_kv = lax.optimization_barrier((attn_in, text_kv))

        attn_in, projected = gather_mm(attn_in, first, 0, 3 * group, "qkv_mm")
        self_mixed = self_forward(projected, 2 * images)
        down = column_blocks(w_down, 4)
        self_mixed, down = lax.optimization_barrier((self_mixed, down))
        down = gather_rows(trade(down))
        parts = mm_scatter(self_mixed, mid[:, :group])
        after_attn, cross_in = add_norm([start_x] + parts, gain_b)

        cross_in, cross_queries = gather_mm(
            gather_tokens(cross_in), mid, group, group, "query_mm"
        )
        cross_mixed = cross_forward(cross_queries, text_kv)
        parts = mm_scatter(cross_mixed, mid[:, 2 * group :])
        after_cross, mlp_in = add_norm([after_attn] + parts, gain_c)

        mlp_in = gather_tokens(mlp_in)
        mlp_in, grad_top = lax.optimization_barrier((mlp_in, grad_top))
        grad_y = jnp.concatenate(gather_tokens(grad_top), axis=0)
        mlp_in, activated, slope = feed_up(mlp_in, up)
        early = [attn_in, self_mixed, cross_in, cross_mixed]
        if inside:
            grad_axes, halves = "z", (core, z_size)

            def both(values):
                return [values, swap(values, "c")]

        else:
            grad_axes, halves = DATA, ()

            def both(values):
                return [values]

        early = [both(values) for values in early]
        down_part = grad_products([(both(grad_y), both(activated))], "down_grads", *halves)
        mlp_in = both(mlp_in)
        slope, down_part, early, mlp_in = lax.optimization_barrier((slope, down_part, early, mlp_in))
        down_rows = scatter_grad(down_part, grad_axes)
        grad_pre = feed_down(grad_y, slope, down)
        parts = mm_scatter(grad_pre, up)
        up_part = grad_products([(mlp_in, both(grad_pre))], "up_grads", *halves)
        grad_after_cross, cross_branch, gain_grad_c = norm_back(
            parts, grad_top, after_cross, gain_c
        )

        cross_branch, up_part = gather_beside(cross_branch, up_part)
        cross_branch, grad_cross_mixed = gather_mm(
            cross_branch, mid, 2 * group, group, "cross_out_back"
        )
        grad_cq, kv_grad = cross_back(cross_queries, text_kv, grad_cross_mixed)
        up_part, down_rows, kv_grad = lax.optimization_barrier((up_part, down_rows, kv_grad))
        up_rows = scatter_grad(up_part, grad_axes)
        cross_branch, grad_cq_both = both(cross_branch), both(grad_cq)
        parts = mm_scatter(grad_cq, mid[:, group : 2 * group])
        grad_after_attn, attn_branch, gain_grad_b = norm_back(
            parts, grad_after_cross, after_attn, gain_b
        )

        activated, attn_branch = lax.optimization_barrier((activated, attn_branch))
        result = mm_t(activated, down).astype(BF)
        attn_branch, result = gather_beside(attn_branch, result)
        attn_branch, result = lax.optimization_barrier((attn_branch, result))
        result = scatter_first(token_blocks(result))
        attn_branch, grad_self_mixed = gather_mm(attn_branch, mid, 0, group, "out_back")
        grad_projected = self_back(projected, grad_self_mixed, 2 * images)
        kv_part = kv_grad.astype(BF).reshape(2, z_size, -1, 2 * group)
        kv_part = kv_part.transpose(1, 0, 2, 3).reshape(2 * z_size, -1, 2 * group)
        grad_projected, result, kv_part = lax.optimization_barrier(
            (grad_projected, result, kv_part)
        )
        kv_part = trade(kv_part, DATA)
        result = scatter_second(result)
        attn_part = grad_products(
            [(early[0], both(grad_projected)), (both(attn_branch), early[1])],
            "attention_grads",
            *halves,
        )
        grad_projected, result, kv_part, attn_part, cross_branch = lax.optimization_barrier(
            (grad_projected, result, kv_part, attn_part, cross_branch)
        )
        attn_part, up_rows = lax.optimization_barrier((attn_part, up_rows))
        attn_rows = scatter_grad(attn_part, grad_axes)
        cross_part = grad_products(
            [(early[2], grad_cq_both), (cross_branch, early[3])], "cross_grads", *halves
        )
        parts = mm_scatter(grad_projected, first)
        grad_hidden, gain_grad_a, mask_grad = last_back(
            parts,
            grad_after_attn,
            start_x,
            gain_a,
            masked,
            unit,
            order,
        )
        sums = jnp.concatenate([gain_grad_a, gain_grad_b, gain_grad_c, mask_grad], axis=0)


        kv_part = kv_part.astype(F32).sum(axis=0).astype(BF)
        kv_sum = spread(kv_part, "z", z_size).reshape(-1, 2 * group)
        kv_grads = spread(kv_sum, PLANE, 8)
        kv_weight_grad, grad_text_w, caption_part = text_back(
            kv_grads, own_text, w_cross, caption, w_text, halves_of(sums, text_width // 4)
        )
        half_context = caption.shape[0] // 2
        caption_part = trade(caption_part, PLANE)
        output = layer_output(after_cross, result, unit, order)
        caption_part, output, down_rows, up_rows, attn_rows, cross_part = lax.optimization_barrier(
            (caption_part, output, down_rows, up_rows, attn_rows, cross_part)
        )
        cross_rows = scatter_grad(cross_part, grad_axes)

        caption_part = caption_part.astype(F32).sum(axis=0)
        sums = layer_order(add_z(whole_of(caption_part[half_context:], width)))
        caption_part = caption_part[:half_context].astype(BF).reshape(z_size, -1, text_width // 4)
        caption_part = trade(caption_part, "z")
        down_parts = swap_parts(pick_rows([down_rows], rank))
        caption_part, down_parts, up_rows = lax.optimization_barrier(
            (caption_part, down_parts, up_rows)
        )

        caption_part = caption_part.astype(F32).sum(axis=0).astype(BF)
        caption_part = spread(caption_part, "z", z_size).reshape(half_context, -1)
        up_parts = swap_parts(pick_rows([up_rows], rank))
        down_grad = finish_wide(down_parts, rank)
        caption_part, up_parts, down_grad = lax.optimization_barrier(
            (caption_part, up_parts, down_grad)
        )

        caption_part = spread(caption_part)
        up_grad = finish_wide(up_parts, rank)
        attn_parts = swap_parts(pick_rows([attn_rows], rank))
        caption_part, cross_rows, up_grad, attn_parts = lax.optimization_barrier(
            (caption_part, cross_rows, up_grad, attn_parts)
        )
        grad_caption = caption_output(caption_part, swap(caption_part, "c"), core)
        qkv_grad, out_grad = finish_attention(attn_parts, rank)
        cross_rows = swap_parts(pick_rows([cross_rows], rank))
        grad_caption, qkv_grad, out_grad, cross_rows = lax.optimization_barrier(
            (grad_caption, qkv_grad, out_grad, cross_rows)
        )
        grad_cross, cross_out_grad = finish_cross(cross_rows, kv_weight_grad, rank)
        return (
            outer(output).reshape(hidden.shape),
            outer(grad_hidden).reshape(hidden.shape),
            grad_caption,
            sums[:3],
            sums[3],
            qkv_grad.transpose(1, 0, 2),
            out_grad,
            grad_cross.transpose(1, 0, 2),
            cross_out_grad,
            grad_text_w,
            up_grad,
            down_grad,
        )

    return local


def solution(mesh):
    z_size = mesh.shape["img"] // 4
    inner = Mesh(mesh.devices.reshape(z_size, 2, 2, 2), ("z", "x", "c", "y"))
    image = ("z", "x", "c")
    tokens = P(image, "y", None)
    rows = P(image + ("y",))
    in_specs = (tokens, P(image, None), P(image), P(), P(), P()) + (rows,) * 7 + (tokens,)
    out_specs = (tokens, tokens, P(), P(), P()) + (rows,) * 7
    return jax.shard_map(
        make_local(z_size), mesh=inner, in_specs=in_specs, out_specs=out_specs, check_vma=False
    )
```

```python
import math

import jax
import jax.numpy as jnp
from jax import lax
from jax.experimental import pallas as pl
from jax.experimental.pallas import tpu as pltpu
from jax.sharding import Mesh
from jax.sharding import PartitionSpec as P

HD = 128
EPS = 1e-05
BF = jnp.bfloat16
F32 = jnp.float32
PAIR = ((0, 1), (1, 0))
GROUP = ("x", "y")
DATA = ("z", "c")
PLANE = ("x", "c", "y")
VMEM = 48 * 1024 * 1024
SCALE = 1.0 / math.sqrt(HD)
SLOPE = math.sqrt(2.0 / math.pi)
CUBIC = 0.044715


def dot(a, b, dims):
    return lax.dot_general(a, b, (dims, ((), ())), preferred_element_type=F32)


def mm(a, b):
    return dot(a, b, ((1,), (0,)))


def mm_t(a, b):
    return dot(a, b, ((1,), (1,)))


def t_mm(a, b):
    return dot(a, b, ((0,), (0,)))


def shape(dims, dtype=BF):
    return jax.ShapeDtypeStruct(dims, dtype)


def swap(values, axis):
    return lax.ppermute(values, axis, PAIR)


def trade(blocks, axes=GROUP):
    return lax.all_to_all(blocks, axes, 0, 0, tiled=True)


def spread(values, axes=GROUP, count=4):
    return trade(jnp.broadcast_to(values[None], (count,) + values.shape), axes)


def gather_tokens(own):
    half = own.shape[0] // 2
    from_x = swap(own, "x")
    from_y = swap(own, "y")
    return own, from_y, from_x, swap(from_x[:half], "y"), swap(from_y[half:], "x")


def gather_beside(own, work):
    half = own.shape[0] // 2
    from_x, from_y, work = lax.optimization_barrier((swap(own, "x"), swap(own, "y"), work))
    return (own, from_y, from_x, swap(from_x[:half], "y"), swap(from_y[half:], "x")), work


def scatter_first(parts):
    own, for_y, for_x, for_low, for_high = parts
    half = for_low.shape[0]
    low = swap(for_low, "y").astype(F32) + for_x[:half].astype(F32)
    high = swap(for_high, "x").astype(F32) + for_y[half:].astype(F32)
    return (
        own,
        jnp.concatenate([low.astype(BF), for_x[half:]], axis=0),
        jnp.concatenate([for_y[:half], high.astype(BF)], axis=0),
    )


def scatter_second(parts):
    own, for_x, for_y = parts
    return [own, swap(for_x, "x"), swap(for_y, "y")]


def scatter_tokens(parts):
    return scatter_second(scatter_first(parts))


def swap_parts(parts):
    return [
        parts[0],
        swap(parts[1], "y"),
        swap(parts[2], "x"),
        lax.ppermute(parts[3], GROUP, ((0, 3), (1, 2), (2, 1), (3, 0))),
    ]


def gather_rows(rows):
    return lax.all_gather(rows.reshape(-1, rows.shape[-1]), DATA, axis=0, tiled=True)


def scatter_grad(partial, axes):
    summed = lax.psum_scatter(partial, axes, scatter_dimension=0, tiled=True)
    return summed.reshape(4, -1, summed.shape[-1])


def call(kernel, grid, in_specs, out_specs, out_shape, operands, name, flops=0, size=1 << 22,
         rank=None, scratch=()):
    options = dict(
        out_shape=out_shape,
        compiler_params=pltpu.CompilerParams(vmem_limit_bytes=VMEM),
        cost_estimate=pl.CostEstimate(flops=flops, bytes_accessed=size, transcendentals=0),
        name=name,
    )
    if rank is None:
        return pl.pallas_call(
            kernel, grid=grid, in_specs=in_specs, out_specs=out_specs, scratch_shapes=scratch,
            **options,
        )(*operands)
    spec = pltpu.PrefetchScalarGridSpec(
        num_scalar_prefetch=1,
        grid=grid,
        in_specs=in_specs,
        out_specs=out_specs,
        scratch_shapes=scratch,
    )
    return pl.pallas_call(kernel, grid_spec=spec, **options)(rank.reshape(1), *operands)


def whole(array):
    return pl.BlockSpec(array.shape, lambda *_: (0,) * len(array.shape))


def reorder(values, unit, order):
    if order is None:
        return values
    return jnp.concatenate([values[:, k * unit : (k + 1) * unit] for k in order], axis=1)


def assemble(target, pieces, sems):
    copies, at = [], 0
    for k, piece in enumerate(pieces):
        rows = piece.shape[0]
        copies.append(pltpu.make_async_copy(piece, target.at[at : at + rows], sems.at[k]))
        at += rows
    for copy in copies:
        copy.start()
    for copy in copies:
        copy.wait()


ANY = pl.BlockSpec(memory_space=pl.ANY)


def gather_mm(pieces, weight, first, columns, name):
    rows, width = pieces[0].shape
    step = 256

    def kernel(*refs):
        tokens, out, sems = refs[6:]

        @pl.when(pl.program_id(0) == 0)
        def _():
            assemble(tokens, refs[:5], sems)

        out[...] = mm(tokens[...], refs[5][...]).astype(BF)

    return call(
        kernel,
        (columns // step,),
        [ANY] * 5 + [pl.BlockSpec((width, step), lambda j: (0, first // step + j))],
        [
            pl.BlockSpec((4 * rows, width), lambda j: (0, 0)),
            pl.BlockSpec((4 * rows, step), lambda j: (0, j)),
        ],
        [shape((4 * rows, width)), shape((4 * rows, columns))],
        [*pieces, weight],
        name,
        flops=8 * rows * width * columns,
        size=2 * width * (columns + 8 * rows),
        scratch=[pltpu.SemaphoreType.DMA((5,))],
    )


def mm_scatter(values, weight):
    return scatter_tokens(token_blocks(mm_t(values, weight).astype(BF)))


def token_blocks(partial):
    rows = partial.shape[0] // 4
    cuts = [0, rows, 2 * rows, 3 * rows, 3 * rows + rows // 2, 4 * rows]
    return [partial[a:b] for a, b in zip(cuts, cuts[1:])]


def normalize(values):
    centred = values - jnp.mean(values, axis=-1, keepdims=True)
    inv_std = lax.rsqrt(jnp.mean(centred * centred, axis=-1, keepdims=True) + EPS)
    return centred * inv_std, inv_std


NORM_ROWS = 32


def row_spec(array, at=None):
    width = array.shape[-1]
    if at is None:
        return pl.BlockSpec((NORM_ROWS, width), lambda i: (i, 0))
    return pl.BlockSpec((1, NORM_ROWS, width), lambda i, at=at: (at, i, 0))


def terms_of(terms):
    arrays, specs = [], []
    for term in terms:
        array, at = term if isinstance(term, tuple) else (term, None)
        arrays.append(array)
        specs.append(row_spec(array, at))
    return arrays, specs


def total_of(refs):
    values = [ref[0] if len(ref.shape) == 3 else ref[...] for ref in refs]
    return sum(value.astype(F32) for value in values)


def add_norm(terms, gain):
    arrays, specs = terms_of(terms)
    tokens, width = arrays[0].shape[-2], arrays[0].shape[-1]
    tokens = min(a.shape[-2] for a in arrays)

    def kernel(*refs):
        gain_ref, x, out = refs[-3:]
        values = total_of(refs[:-3])
        x[...] = values
        out[...] = (normalize(values)[0] * gain_ref[...]).astype(BF)

    return call(
        kernel,
        (tokens // NORM_ROWS,),
        specs + [whole(gain)],
        [row_spec(shape((tokens, width)))] * 2,
        [shape((tokens, width), F32), shape((tokens, width))],
        [*arrays, gain],
        "add_norm",
    )


def norm_grad(grad, values, gain):
    normed, inv_std = normalize(values)
    scaled = grad * gain
    first_mean = jnp.mean(scaled, axis=-1, keepdims=True)
    second_mean = jnp.mean(scaled * normed, axis=-1, keepdims=True)
    return (
        inv_std * (scaled - first_mean - normed * second_mean),
        jnp.sum(grad * normed, axis=0, keepdims=True),
    )


def accumulate(ref, value):
    @pl.when(pl.program_id(0) == 0)
    def _():
        ref[...] = jnp.zeros_like(ref)

    ref[...] += value


def norm_back(terms, upper, values, gain):
    arrays, specs = terms_of(terms)
    tokens, width = values.shape

    def kernel(*refs):
        upper_ref, x, gain_ref, out, out_low, gain_grad = refs[-6:]
        back, part = norm_grad(total_of(refs[:-6]), x[...], gain_ref[...])
        result = upper_ref[...].astype(F32) + back
        out[...] = result
        out_low[...] = result.astype(BF)
        accumulate(gain_grad, part)

    return call(
        kernel,
        (tokens // NORM_ROWS,),
        specs + [row_spec(upper), row_spec(values), whole(gain)],
        [row_spec(values)] * 2 + [pl.BlockSpec((1, width), lambda i: (0, 0))],
        [shape((tokens, width), F32), shape((tokens, width)), shape((1, width), F32)],
        [*arrays, upper, values, gain],
        "norm_back",
    )


def last_back(terms, upper, values, gain, masked, unit, order):
    arrays, specs = terms_of(terms)
    tokens, width = values.shape

    def kernel(*refs):
        upper_ref, x, gain_ref, mask, out, gain_grad, mask_grad = refs[-7:]
        back, part = norm_grad(total_of(refs[:-7]), x[...], gain_ref[...])
        result = upper_ref[...].astype(F32) + back
        hit = mask[...] > 0.5
        out[...] = reorder(jnp.where(hit, 0.0, result).astype(BF), unit, order)
        accumulate(gain_grad, part)
        accumulate(mask_grad, jnp.sum(jnp.where(hit, result, 0.0), axis=0, keepdims=True))

    line = pl.BlockSpec((1, width), lambda i: (0, 0))
    return call(
        kernel,
        (tokens // NORM_ROWS,),
        specs + [row_spec(upper), row_spec(values), whole(gain), row_spec(masked)],
        [row_spec(values), line, line],
        [shape((tokens, width)), shape((1, width), F32), shape((1, width), F32)],
        [*arrays, upper, values, gain, masked],
        "last_back",
    )


def start(hidden, cotangent, masked, embed, gain, unit, order):
    tokens, width = hidden.shape

    def kernel(hid, cot, mask, embed_ref, gain_ref, x, out, grad):
        hit = mask[...] > 0.5
        values = jnp.where(
            hit, embed_ref[...], reorder(hid[...], unit, order).astype(F32)
        )
        x[...] = values
        out[...] = (normalize(values)[0] * gain_ref[...]).astype(BF)
        grad[...] = jnp.where(hit, reorder(cot[...], unit, order).astype(F32), 0.0).astype(BF)

    rows = row_spec(hidden)
    return call(
        kernel,
        (tokens // NORM_ROWS,),
        [rows, rows, row_spec(masked), whole(embed), whole(gain)],
        [rows] * 3,
        [shape((tokens, width), F32), shape((tokens, width)), shape((tokens, width))],
        [hidden, cotangent, masked, embed, gain],
        "start",
    )


def layer_output(upper, terms, unit, order):
    arrays, specs = terms_of(terms)
    tokens, width = upper.shape

    def kernel(*refs):
        values = refs[-2][...] + total_of(refs[:-2])
        refs[-1][...] = reorder(values.astype(BF), unit, order)

    return call(
        kernel,
        (tokens // NORM_ROWS,),
        specs + [row_spec(upper)],
        row_spec(upper),
        shape((tokens, width)),
        [*arrays, upper],
        "layer_output",
    )


def feed_up(pieces, weight):
    rows, width = pieces[0].shape
    hidden = weight.shape[1]
    step = 256

    def kernel(*refs):
        up, tokens, act, slope, sems = refs[5:]

        @pl.when(pl.program_id(0) == 0)
        def _():
            assemble(tokens, refs[:5], sems)

        u = mm(tokens[...], up[...])
        square = u * u
        bend = jnp.tanh(SLOPE * u * (1.0 + CUBIC * square))
        half = 0.5 * (1.0 + bend)
        act[...] = (u * half).astype(BF)
        slope[...] = half + 0.5 * u * (1.0 - bend * bend) * SLOPE * (1.0 + 3.0 * CUBIC * square)

    part = pl.BlockSpec((4 * rows, step), lambda j: (0, j))
    return call(
        kernel,
        (hidden // step,),
        [ANY] * 5 + [pl.BlockSpec((width, step), lambda j: (0, j))],
        [pl.BlockSpec((4 * rows, width), lambda j: (0, 0)), part, part],
        [shape((4 * rows, width)), shape((4 * rows, hidden)), shape((4 * rows, hidden), F32)],
        [*pieces, weight],
        "feed_up",
        scratch=[pltpu.SemaphoreType.DMA((5,))],
        flops=8 * rows * width * hidden,
        size=2 * width * (hidden + 8 * rows),
    )


def feed_down(grad_y, slope, weight):
    tokens, width = grad_y.shape
    hidden = weight.shape[1]
    step = 256

    def kernel(dy, slope_ref, down, out):
        out[...] = (mm(dy[...], down[...]) * slope_ref[...]).astype(BF)

    part = pl.BlockSpec((tokens, step), lambda j: (0, j))
    return call(
        kernel,
        (hidden // step,),
        [whole(grad_y), part, pl.BlockSpec((width, step), lambda j: (0, j))],
        part,
        shape((tokens, hidden)),
        [grad_y, slope, weight],
        "feed_down",
        flops=2 * tokens * width * hidden,
        size=2 * width * (hidden + 8 * tokens),
    )


def softmax(scores):
    exp_terms = jnp.exp(scores - jnp.max(scores, axis=-1, keepdims=True))
    return exp_terms / jnp.sum(exp_terms, axis=-1, keepdims=True)


def score_grad(probs, grad_probs):
    return (
        probs * (grad_probs - jnp.sum(probs * grad_probs, axis=-1, keepdims=True))
    ).astype(BF)


def head(ref, k):
    return ref[:, k * HD : (k + 1) * HD]


def self_forward(projected, images):
    tokens, width = projected.shape
    rows, group = tokens // images, width // 3
    heads = group // HD

    def kernel(proj, mixed):
        for k in range(heads):
            query, key, value = (head(proj, j * heads + k) for j in range(3))
            probs = softmax(mm_t(query, key) * SCALE).astype(BF)
            mixed[:, k * HD : (k + 1) * HD] = mm(probs, value).astype(BF)

    return call(
        kernel,
        (images,),
        [pl.BlockSpec((rows, width), lambda i: (i, 0))],
        pl.BlockSpec((rows, group), lambda i: (i, 0)),
        shape((tokens, group)),
        [projected],
        "self_forward",
        flops=4 * tokens * rows * group,
    )


def self_back(projected, grad_mixed, images):
    tokens, width = projected.shape
    rows, group = tokens // images, width // 3
    heads = group // HD

    def kernel(proj, grad, out):
        for k in range(heads):
            query, key, value = (head(proj, j * heads + k) for j in range(3))
            grad_head = head(grad, k)
            probs = softmax(mm_t(query, key) * SCALE)
            grad_scores = score_grad(probs, mm_t(grad_head, value))
            parts = (
                mm(grad_scores, key) * SCALE,
                t_mm(grad_scores, query) * SCALE,
                t_mm(probs.astype(BF), grad_head),
            )
            for j, part in enumerate(parts):
                at = (j * heads + k) * HD
                out[:, at : at + HD] = part.astype(BF)

    return call(
        kernel,
        (images,),
        [
            pl.BlockSpec((rows, width), lambda i: (i, 0)),
            pl.BlockSpec((rows, group), lambda i: (i, 0)),
        ],
        pl.BlockSpec((rows, width), lambda i: (i, 0)),
        shape((tokens, width)),
        [projected, grad_mixed],
        "self_back",
        flops=10 * tokens * rows * group,
    )


def cross_forward(queries, text_kv):
    tokens, group = queries.shape
    heads = group // HD

    def kernel(query, text, mixed):
        for k in range(heads):
            probs = softmax(mm_t(head(query, k), head(text, k)) * SCALE).astype(BF)
            mixed[:, k * HD : (k + 1) * HD] = mm(probs, head(text, heads + k)).astype(BF)

    return call(
        kernel,
        (1,),
        [whole(queries), whole(text_kv)],
        whole(queries),
        shape((tokens, group)),
        [queries, text_kv],
        "cross_forward",
        flops=4 * tokens * text_kv.shape[0] * group,
    )


def cross_back(queries, text_kv, grad_mixed):
    tokens, group = queries.shape
    context = text_kv.shape[0]
    heads = group // HD

    def kernel(query, text, grad, grad_query, grad_text):
        for k in range(heads):
            query_head, key, value = head(query, k), head(text, k), head(text, heads + k)
            grad_head = head(grad, k)
            probs = softmax(mm_t(query_head, key) * SCALE)
            grad_scores = score_grad(probs, mm_t(grad_head, value))
            grad_query[:, k * HD : (k + 1) * HD] = (mm(grad_scores, key) * SCALE).astype(BF)
            at = (heads + k) * HD
            grad_text[:, k * HD : (k + 1) * HD] = t_mm(grad_scores, query_head) * SCALE
            grad_text[:, at : at + HD] = t_mm(probs.astype(BF), grad_head)

    return call(
        kernel,
        (1,),
        [whole(queries), whole(text_kv), whole(grad_mixed)],
        [whole(queries), whole(text_kv)],
        [shape((tokens, group)), shape((context, 2 * group), F32)],
        [queries, text_kv, grad_mixed],
        "cross_back",
        flops=10 * tokens * context * group,
    )


def grad_products(pairs, name, core=None, blocks=0):
    count_in = len(pairs[0][0])
    tokens, width = pairs[0][0][0].shape
    widths = [y[0].shape[1] for _, y in pairs]
    total = sum(widths)
    rows = 256 if core is None else width // (2 * blocks)
    steps = width // rows if core is None else blocks
    step = 512
    count = len(pairs) * count_in

    def kernel(r, *refs):
        out = refs[2 * count]
        offset = 0
        for k, wide in enumerate(widths):
            left = [refs[k * count_in + b][...].T for b in range(count_in)]
            for at in range(0, wide, step):
                out[:, offset + at : offset + at + step] = sum(
                    mm(left[b], refs[count + k * count_in + b][:, at : at + step])
                    for b in range(count_in)
                ).astype(BF)
            offset += wide

    pick = (lambda i, r: (0, i)) if core is None else (lambda i, r: (0, 2 * i + r[0]))
    return call(
        kernel,
        (steps,),
        [pl.BlockSpec((tokens, rows), pick)] * count
        + [pl.BlockSpec((tokens, w), lambda i, r: (0, 0)) for w in widths for _ in range(count_in)],
        pl.BlockSpec((rows, total), lambda i, r: (i, 0)),
        shape((steps * rows, total)),
        [b for x, _ in pairs for b in x] + [b for _, y in pairs for b in y],
        name,
        flops=2 * tokens * count_in * steps * rows * total,
        size=4 * width * total,
        rank=jnp.zeros((), jnp.int32) if core is None else core,
    )


def pick_weights(three, rank):
    rows, width = three.shape[1], three.shape[2] // 4

    def kernel(r, three_ref, *outs):
        for k in range(4):

            @pl.when(pl.program_id(0) == k)
            def _():
                for j in range(3):
                    outs[k][:, j * width : (j + 1) * width] = three_ref[j]

    outs = [shape((rows, 3 * width))] * 4
    return call(
        kernel,
        (4,),
        [pl.BlockSpec((3, rows, width), lambda k, r: (0, 0, k ^ r[0]))],
        [whole(a) for a in outs],
        outs,
        [three],
        "pick_weights",
        rank=rank,
    )


def pick_rows(arrays, rank):
    rows = arrays[0].shape[1]
    widths = [a.shape[2] for a in arrays]
    count = len(arrays)

    def kernel(r, *refs):
        for k in range(4):

            @pl.when(pl.program_id(0) == k)
            def _():
                at = 0
                for ref, width in zip(refs, widths):
                    refs[count + k][:, at : at + width] = ref[0]
                    at += width

    outs = [shape((rows, sum(widths)))] * 4
    return call(
        kernel,
        (4,),
        [pl.BlockSpec((1, rows, w), lambda k, r: (k ^ r[0], 0, 0)) for w in widths],
        [whole(a) for a in outs],
        outs,
        arrays,
        "pick_rows",
        rank=rank,
    )


def place(parts, rank):
    def kernel(r, *refs):
        for k in range(4):

            @pl.when(pl.program_id(0) == k)
            def _():
                refs[4][0] = refs[k][...]

    rows, columns = parts[0].shape
    return call(
        kernel,
        (4,),
        [whole(p) for p in parts],
        pl.BlockSpec((1, rows, columns), lambda k, r: (k ^ r[0], 0, 0)),
        shape((4, rows, columns)),
        parts,
        "place",
        rank=rank,
    )


def finish_wide(parts, rank):
    rows, width = parts[0].shape

    def kernel(r, *refs):
        for k in range(4):

            @pl.when(pl.program_id(0) == k)
            def _():
                refs[4][...] = refs[k][...].astype(F32)

    return call(
        kernel,
        (4,),
        [whole(p) for p in parts],
        pl.BlockSpec((rows, width), lambda k, r: (0, k ^ r[0])),
        shape((rows, 4 * width), F32),
        parts,
        "finish_wide",
        rank=rank,
    )


def finish_all(parts, text_grad, rank):
    rows, total = parts[0].shape
    width = total // 6

    def kernel(r, *refs):
        key, value, three, out, cross, cross_out = refs[4:]
        for k in range(4):

            @pl.when(pl.program_id(0) == k)
            def _():
                def part(j):
                    return refs[k][:, j * width : (j + 1) * width].astype(F32)

                for j in range(3):
                    three[j] = part(j)
                out[...] = part(3)
                cross[0] = part(4)
                cross_out[...] = part(5)

        cross[1] = key[...]
        cross[2] = value[...]

    wide = pl.BlockSpec((3, rows, width), lambda k, r: (0, 0, k ^ r[0]))
    flat = pl.BlockSpec((rows, width), lambda k, r: (0, k ^ r[0]))
    return call(
        kernel,
        (4,),
        [whole(p) for p in parts]
        + [flat, pl.BlockSpec((rows, width), lambda k, r: (0, 4 + (k ^ r[0])))],
        [wide, flat, wide, flat],
        [shape((3, rows, 4 * width), F32), shape((rows, 4 * width), F32)] * 2,
        [*parts, text_grad, text_grad],
        "finish_all",
        rank=rank,
    )


def plane_block(k):
    return (k >> 1) & 1, (k >> 2) * 2 + (k & 1)


def text_forward(caption, w_text, w_cross):
    context, rows = caption.shape[0], w_text.shape[0]
    half, width = context // 2, w_cross.shape[2] // 4

    def kernel(cap, weight, cross, own, blocks):
        own[...] = mm_t(cap[...], weight[...]).astype(BF)
        for j in range(2):
            part = mm(own[...], cross[1 + j]).astype(BF)
            for k in range(8):
                core, group = plane_block(k)
                blocks[k, :, j * width : (j + 1) * width] = part[
                    core * half : (core + 1) * half, group * width : (group + 1) * width
                ]

    return call(
        kernel,
        (1,),
        [whole(caption), whole(w_text), whole(w_cross)],
        [
            pl.BlockSpec((context, rows), lambda i: (0, 0)),
            pl.BlockSpec((8, half, 2 * width), lambda i: (0, 0, 0)),
        ],
        [shape((context, rows)), shape((8, half, 2 * width))],
        [caption, w_text, w_cross],
        "text_forward",
    )


def text_back(blocks, own_text, w_cross, caption, w_text, extra):
    context, rows = own_text.shape
    half, width = context // 2, w_cross.shape[2] // 4
    wide = caption.shape[1] // 4
    tail = extra.shape[0]

    def kernel(block, own, cross, cap, weight, more, kv_grad, text_grad, out, grads):
        for k in range(8):
            core, group = plane_block(k)
            for j in range(2):
                at = (4 * j + group) * width
                grads[core * half : (core + 1) * half, at : at + width] = block[
                    k, :, j * width : (j + 1) * width
                ]
        kv_grad[...] = t_mm(own[...], grads[...])
        grad_text = sum(
            mm_t(grads[:, 4 * j * width : 4 * (j + 1) * width], cross[1 + j]) for j in range(2)
        ).astype(BF)
        text_grad[...] = t_mm(grad_text, cap[...])
        part = mm(grad_text, weight[...]).astype(BF)
        for k in range(8):
            core, group = plane_block(k)
            out[k, :half, :] = part[core * half : (core + 1) * half, group * wide : (group + 1) * wide]
            out[k, half:, :] = more[...]

    operands = [blocks, own_text, w_cross, caption, w_text, extra]
    outs = [
        shape((rows, 8 * width), F32),
        shape((rows, 4 * wide), F32),
        shape((8, half + tail, wide)),
    ]
    return call(
        kernel,
        (1,),
        [whole(a) for a in operands],
        [whole(a) for a in outs],
        outs,
        operands,
        "text_back",
        scratch=[pltpu.VMEM((context, 8 * width), BF)],
    )


def caption_output(own, other, core):
    count, half, wide = own.shape

    def kernel(r, own_ref, other_ref, out):
        block = jnp.where(pl.program_id(0) == r[0], own_ref[0], other_ref[0])
        out[...] = block.astype(F32)

    block = pl.BlockSpec((1, half, wide), lambda i, k, r: (k, 0, 0))
    return call(
        kernel,
        (2, count),
        [block, block],
        pl.BlockSpec((half, wide), lambda i, k, r: (i, k)),
        shape((2 * half, 4 * wide), F32),
        [own, other],
        "caption_output",
        rank=core,
    )


def column_blocks(weight, count):
    rows = weight.shape[0]
    return weight.reshape(rows, count, -1).transpose(1, 0, 2)


def halves_of(values, width):
    high = values.astype(BF)
    low = (values - high.astype(F32)).astype(BF)
    return jnp.concatenate([high.reshape(-1, width), low.reshape(-1, width)], axis=0)


def whole_of(halves, width):
    rows = halves.shape[0] // 2
    return (halves[:rows] + halves[rows:]).reshape(-1, width)


def make_local(z_size):
    def sum_z(values):
        parts = values.reshape(z_size, -1, values.shape[-1])
        mine = trade(parts, "z").astype(F32).sum(axis=0).astype(BF)
        return spread(mine, "z", z_size).reshape(values.shape)

    def add_z(values):
        step = 1
        while step < z_size:
            values = values + lax.ppermute(
                values, "z", tuple((k, k ^ step) for k in range(z_size))
            )
            step *= 2
        return values

    def layer_order(values):
        shaped = values.reshape(values.shape[:-1] + (z_size, 2, 2, -1))
        return jnp.swapaxes(shaped, -3, -2).reshape(values.shape)

    def local(
        hidden,
        mask_index,
        mask_count,
        mask_embed,
        norm_gains,
        caption,
        w_qkv,
        w_out,
        w_cross,
        w_cross_out,
        w_text,
        w_up,
        w_down,
        cotangent,
    ):
        images, local_rows, width = hidden.shape
        full_length = mask_index.shape[1]
        rank = lax.axis_index("x") * 2 + lax.axis_index("y")
        core = lax.axis_index("c")
        tokens = images * local_rows
        group = width // 4
        text_width = caption.shape[1]

        unit = width // (4 * z_size)
        inside = unit % 128 == 0
        order = [4 * k + j for k in range(z_size) for j in (0, 2, 1, 3)] if inside else None

        def outer(values):
            return values if inside else layer_order(values)

        w_qkv, w_cross = w_qkv.transpose(1, 0, 2), w_cross.transpose(1, 0, 2)
        first = swap_parts(pick_weights(w_qkv, rank))
        first = gather_rows(place(first, rank))

        positions = lax.axis_index("y") * local_rows + jnp.arange(local_rows, dtype=jnp.int32)
        ranks = jnp.arange(full_length, dtype=jnp.int32)
        matches = (mask_index[:, :, None] == positions[None, None, :]) & (
            ranks[None, :, None] < mask_count[:, None, None]
        )
        masked = jnp.any(matches, axis=1).reshape(tokens, 1).astype(F32)
        gains = layer_order(norm_gains)
        gain_a, gain_b, gain_c = gains[:1], gains[1:2], gains[2:]
        start_x, attn_in, grad_top = start(
            outer(hidden.reshape(tokens, width)),
            outer(cotangent.reshape(tokens, width)),
            masked,
            layer_order(mask_embed)[None],
            gain_a,
            unit,
            order,
        )
        attn_in = gather_tokens(attn_in)
        mid = [column_blocks(weight, 4) for weight in (w_out, w_cross[0], w_cross_out)]
        mid = jnp.concatenate(mid, axis=2)
        up = column_blocks(w_up, 4)
        attn_in, mid, up = lax.optimization_barrier((attn_in, mid, up))
        mid, up = gather_rows(trade(mid)), gather_rows(trade(up))

        own_text, kv_part = text_forward(caption, w_text, w_cross)
        text_kv = trade(kv_part, PLANE).astype(F32).sum(axis=0).astype(BF)
        text_kv = sum_z(text_kv)
        other = swap(text_kv, "c")
        text_kv = jnp.concatenate(
            [jnp.where(core == 0, text_kv, other), jnp.where(core == 0, other, text_kv)], axis=0
        )
        attn_in, text_kv = lax.optimization_barrier((attn_in, text_kv))

        attn_in, projected = gather_mm(attn_in, first, 0, 3 * group, "qkv_mm")
        self_mixed = self_forward(projected, 2 * images)
        down = column_blocks(w_down, 4)
        self_mixed, down = lax.optimization_barrier((self_mixed, down))
        down = gather_rows(trade(down))
        parts = mm_scatter(self_mixed, mid[:, :group])
        after_attn, cross_in = add_norm([start_x] + parts, gain_b)

        cross_in, cross_queries = gather_mm(
            gather_tokens(cross_in), mid, group, group, "query_mm"
        )
        cross_mixed = cross_forward(cross_queries, text_kv)
        parts = mm_scatter(cross_mixed, mid[:, 2 * group :])
        after_cross, mlp_in = add_norm([after_attn] + parts, gain_c)

        mlp_in = gather_tokens(mlp_in)
        mlp_in, grad_top = lax.optimization_barrier((mlp_in, grad_top))
        grad_y = jnp.concatenate(gather_tokens(grad_top), axis=0)
        mlp_in, activated, slope = feed_up(mlp_in, up)
        early = [attn_in, self_mixed, cross_in, cross_mixed]
        if inside:
            grad_axes, halves = "z", (core, z_size)

            def both(values):
                return [values, swap(values, "c")]

        else:
            grad_axes, halves = DATA, ()

            def both(values):
                return [values]

        early = [both(values) for values in early]
        down_part = grad_products([(both(grad_y), both(activated))], "down_grads", *halves)
        mlp_in = both(mlp_in)
        slope, down_part, early, mlp_in = lax.optimization_barrier((slope, down_part, early, mlp_in))
        down_rows = scatter_grad(down_part, grad_axes)
        grad_pre = feed_down(grad_y, slope, down)
        parts = mm_scatter(grad_pre, up)
        up_part = grad_products([(mlp_in, both(grad_pre))], "up_grads", *halves)
        grad_after_cross, cross_branch, gain_grad_c = norm_back(
            parts, grad_top, after_cross, gain_c
        )

        cross_branch, up_part = gather_beside(cross_branch, up_part)
        cross_branch, grad_cross_mixed = gather_mm(
            cross_branch, mid, 2 * group, group, "cross_out_back"
        )
        grad_cq, kv_grad = cross_back(cross_queries, text_kv, grad_cross_mixed)
        up_part, down_rows, kv_grad = lax.optimization_barrier((up_part, down_rows, kv_grad))
        up_rows = scatter_grad(up_part, grad_axes)
        cross_branch, grad_cq_both = both(cross_branch), both(grad_cq)
        parts = mm_scatter(grad_cq, mid[:, group : 2 * group])
        grad_after_attn, attn_branch, gain_grad_b = norm_back(
            parts, grad_after_cross, after_attn, gain_b
        )

        activated, attn_branch = lax.optimization_barrier((activated, attn_branch))
        result = mm_t(activated, down).astype(BF)
        attn_branch, result = gather_beside(attn_branch, result)
        attn_branch, result = lax.optimization_barrier((attn_branch, result))
        result = scatter_first(token_blocks(result))
        attn_branch, grad_self_mixed = gather_mm(attn_branch, mid, 0, group, "out_back")
        grad_projected = self_back(projected, grad_self_mixed, 2 * images)
        kv_part = kv_grad.astype(BF).reshape(2, z_size, -1, 2 * group)
        kv_part = kv_part.transpose(1, 0, 2, 3).reshape(2 * z_size, -1, 2 * group)
        grad_projected, result, kv_part = lax.optimization_barrier(
            (grad_projected, result, kv_part)
        )
        kv_part = trade(kv_part, DATA)
        result = scatter_second(result)
        rest_part = grad_products(
            [
                (early[0], both(grad_projected)),
                (both(attn_branch), early[1]),
                (early[2], grad_cq_both),
                (cross_branch, early[3]),
            ],
            "attention_grads",
            *halves,
        )
        grad_projected, result, kv_part, rest_part = lax.optimization_barrier(
            (grad_projected, result, kv_part, rest_part)
        )
        rest_part, up_rows = lax.optimization_barrier((rest_part, up_rows))
        rest_rows = scatter_grad(rest_part, grad_axes)
        parts = mm_scatter(grad_projected, first)
        grad_hidden, gain_grad_a, mask_grad = last_back(
            parts,
            grad_after_attn,
            start_x,
            gain_a,
            masked,
            unit,
            order,
        )
        sums = jnp.concatenate([gain_grad_a, gain_grad_b, gain_grad_c, mask_grad], axis=0)


        kv_part = kv_part.astype(F32).sum(axis=0).astype(BF)
        kv_sum = spread(kv_part, "z", z_size).reshape(-1, 2 * group)
        kv_grads = spread(kv_sum, PLANE, 8)
        kv_weight_grad, grad_text_w, caption_part = text_back(
            kv_grads, own_text, w_cross, caption, w_text, halves_of(sums, text_width // 4)
        )
        half_context = caption.shape[0] // 2
        caption_part = trade(caption_part, PLANE)
        output = layer_output(after_cross, result, unit, order)
        caption_part, output, down_rows, up_rows = lax.optimization_barrier(
            (caption_part, output, down_rows, up_rows)
        )

        caption_part = caption_part.astype(F32).sum(axis=0)
        sums = layer_order(add_z(whole_of(caption_part[half_context:], width)))
        caption_part = caption_part[:half_context].astype(BF).reshape(z_size, -1, text_width // 4)
        caption_part = trade(caption_part, "z")
        down_parts = swap_parts(pick_rows([down_rows], rank))
        caption_part, down_parts, up_rows = lax.optimization_barrier(
            (caption_part, down_parts, up_rows)
        )

        caption_part = caption_part.astype(F32).sum(axis=0).astype(BF)
        caption_part = spread(caption_part, "z", z_size).reshape(half_context, -1)
        up_parts = swap_parts(pick_rows([up_rows], rank))
        down_grad = finish_wide(down_parts, rank)
        caption_part, up_parts, down_grad = lax.optimization_barrier(
            (caption_part, up_parts, down_grad)
        )

        caption_part = spread(caption_part)
        up_grad = finish_wide(up_parts, rank)
        rest_rows, up_grad = lax.optimization_barrier((rest_rows, up_grad))
        grad_caption = caption_output(caption_part, swap(caption_part, "c"), core)
        rest_rows = swap_parts(pick_rows([rest_rows], rank))
        grad_caption, rest_rows = lax.optimization_barrier((grad_caption, rest_rows))
        qkv_grad, out_grad, grad_cross, cross_out_grad = finish_all(
            rest_rows, kv_weight_grad, rank
        )
        return (
            outer(output).reshape(hidden.shape),
            outer(grad_hidden).reshape(hidden.shape),
            grad_caption,
            sums[:3],
            sums[3],
            qkv_grad.transpose(1, 0, 2),
            out_grad,
            grad_cross.transpose(1, 0, 2),
            cross_out_grad,
            grad_text_w,
            up_grad,
            down_grad,
        )

    return local


def solution(mesh):
    z_size = mesh.shape["img"] // 4
    inner = Mesh(mesh.devices.reshape(z_size, 2, 2, 2), ("z", "x", "c", "y"))
    image = ("z", "x", "c")
    tokens = P(image, "y", None)
    rows = P(image + ("y",))
    in_specs = (tokens, P(image, None), P(image), P(), P(), P()) + (rows,) * 7 + (tokens,)
    out_specs = (tokens, tokens, P(), P(), P()) + (rows,) * 7
    return jax.shard_map(
        make_local(z_size), mesh=inner, in_specs=in_specs, out_specs=out_specs, check_vma=False
    )
```

```python
import math

import jax
import jax.numpy as jnp
from jax import lax
from jax.experimental import pallas as pl
from jax.experimental.pallas import tpu as pltpu
from jax.sharding import Mesh
from jax.sharding import PartitionSpec as P

HD = 128
EPS = 1e-05
BF = jnp.bfloat16
F32 = jnp.float32
PAIR = ((0, 1), (1, 0))
GROUP = ("x", "y")
DATA = ("z", "c")
PLANE = ("x", "c", "y")
VMEM = 48 * 1024 * 1024
SCALE = 1.0 / math.sqrt(HD)
SLOPE = math.sqrt(2.0 / math.pi)
CUBIC = 0.044715


def dot(a, b, dims):
    return lax.dot_general(a, b, (dims, ((), ())), preferred_element_type=F32)


def mm(a, b):
    return dot(a, b, ((1,), (0,)))


def mm_t(a, b):
    return dot(a, b, ((1,), (1,)))


def t_mm(a, b):
    return dot(a, b, ((0,), (0,)))


def shape(dims, dtype=BF):
    return jax.ShapeDtypeStruct(dims, dtype)


def swap(values, axis):
    return lax.ppermute(values, axis, PAIR)


def trade(blocks, axes=GROUP):
    return lax.all_to_all(blocks, axes, 0, 0, tiled=True)


def spread(values, axes=GROUP, count=4):
    return trade(jnp.broadcast_to(values[None], (count,) + values.shape), axes)


def gather_tokens(own):
    half = own.shape[0] // 2
    from_x = swap(own, "x")
    from_y = swap(own, "y")
    return own, from_y, from_x, swap(from_x[:half], "y"), swap(from_y[half:], "x")


def gather_beside(own, work):
    half = own.shape[0] // 2
    from_x, from_y, work = lax.optimization_barrier((swap(own, "x"), swap(own, "y"), work))
    return (own, from_y, from_x, swap(from_x[:half], "y"), swap(from_y[half:], "x")), work


def scatter_first(parts):
    own, for_y, for_x, for_low, for_high = parts
    half = for_low.shape[0]
    low = swap(for_low, "y").astype(F32) + for_x[:half].astype(F32)
    high = swap(for_high, "x").astype(F32) + for_y[half:].astype(F32)
    return (
        own,
        jnp.concatenate([low.astype(BF), for_x[half:]], axis=0),
        jnp.concatenate([for_y[:half], high.astype(BF)], axis=0),
    )


def scatter_second(parts):
    own, for_x, for_y = parts
    return [own, swap(for_x, "x"), swap(for_y, "y")]


def scatter_tokens(parts):
    return scatter_second(scatter_first(parts))


def swap_parts(parts):
    return [
        parts[0],
        swap(parts[1], "y"),
        swap(parts[2], "x"),
        lax.ppermute(parts[3], GROUP, ((0, 3), (1, 2), (2, 1), (3, 0))),
    ]


def gather_rows(rows):
    return lax.all_gather(rows.reshape(-1, rows.shape[-1]), DATA, axis=0, tiled=True)


def scatter_grad(partial, axes):
    summed = lax.psum_scatter(partial, axes, scatter_dimension=0, tiled=True)
    return summed.reshape(4, -1, summed.shape[-1])


def call(kernel, grid, in_specs, out_specs, out_shape, operands, name, flops=0, size=1 << 22,
         rank=None, scratch=()):
    options = dict(
        out_shape=out_shape,
        compiler_params=pltpu.CompilerParams(vmem_limit_bytes=VMEM),
        cost_estimate=pl.CostEstimate(flops=flops, bytes_accessed=size, transcendentals=0),
        name=name,
    )
    if rank is None:
        return pl.pallas_call(
            kernel, grid=grid, in_specs=in_specs, out_specs=out_specs, scratch_shapes=scratch,
            **options,
        )(*operands)
    spec = pltpu.PrefetchScalarGridSpec(
        num_scalar_prefetch=1,
        grid=grid,
        in_specs=in_specs,
        out_specs=out_specs,
        scratch_shapes=scratch,
    )
    return pl.pallas_call(kernel, grid_spec=spec, **options)(rank.reshape(1), *operands)


def whole(array):
    return pl.BlockSpec(array.shape, lambda *_: (0,) * len(array.shape))


def reorder(values, unit, order):
    if order is None:
        return values
    return jnp.concatenate([values[:, k * unit : (k + 1) * unit] for k in order], axis=1)


def assemble(target, pieces, sems):
    copies, at = [], 0
    for k, piece in enumerate(pieces):
        rows = piece.shape[0]
        copies.append(pltpu.make_async_copy(piece, target.at[at : at + rows], sems.at[k]))
        at += rows
    for copy in copies:
        copy.start()
    for copy in copies:
        copy.wait()


ANY = pl.BlockSpec(memory_space=pl.ANY)


def gather_mm(pieces, weight, first, columns, name):
    rows, width = pieces[0].shape
    step = 256

    def kernel(*refs):
        tokens, out, sems = refs[6:]

        @pl.when(pl.program_id(0) == 0)
        def _():
            assemble(tokens, refs[:5], sems)

        out[...] = mm(tokens[...], refs[5][...]).astype(BF)

    return call(
        kernel,
        (columns // step,),
        [ANY] * 5 + [pl.BlockSpec((width, step), lambda j: (0, first // step + j))],
        [
            pl.BlockSpec((4 * rows, width), lambda j: (0, 0)),
            pl.BlockSpec((4 * rows, step), lambda j: (0, j)),
        ],
        [shape((4 * rows, width)), shape((4 * rows, columns))],
        [*pieces, weight],
        name,
        flops=8 * rows * width * columns,
        size=2 * width * (columns + 8 * rows),
        scratch=[pltpu.SemaphoreType.DMA((5,))],
    )


def mm_scatter(values, weight):
    return scatter_tokens(token_blocks(mm_t(values, weight).astype(BF)))


def token_blocks(partial):
    rows = partial.shape[0] // 4
    cuts = [0, rows, 2 * rows, 3 * rows, 3 * rows + rows // 2, 4 * rows]
    return [partial[a:b] for a, b in zip(cuts, cuts[1:])]


def normalize(values):
    centred = values - jnp.mean(values, axis=-1, keepdims=True)
    inv_std = lax.rsqrt(jnp.mean(centred * centred, axis=-1, keepdims=True) + EPS)
    return centred * inv_std, inv_std


NORM_ROWS = 32


def row_spec(array, at=None):
    width = array.shape[-1]
    if at is None:
        return pl.BlockSpec((NORM_ROWS, width), lambda i: (i, 0))
    return pl.BlockSpec((1, NORM_ROWS, width), lambda i, at=at: (at, i, 0))


def terms_of(terms):
    arrays, specs = [], []
    for term in terms:
        array, at = term if isinstance(term, tuple) else (term, None)
        arrays.append(array)
        specs.append(row_spec(array, at))
    return arrays, specs


def total_of(refs):
    values = [ref[0] if len(ref.shape) == 3 else ref[...] for ref in refs]
    return sum(value.astype(F32) for value in values)


def add_norm(terms, gain):
    arrays, specs = terms_of(terms)
    tokens, width = arrays[0].shape[-2], arrays[0].shape[-1]
    tokens = min(a.shape[-2] for a in arrays)

    def kernel(*refs):
        gain_ref, x, out = refs[-3:]
        values = total_of(refs[:-3])
        x[...] = values
        out[...] = (normalize(values)[0] * gain_ref[...]).astype(BF)

    return call(
        kernel,
        (tokens // NORM_ROWS,),
        specs + [whole(gain)],
        [row_spec(shape((tokens, width)))] * 2,
        [shape((tokens, width), F32), shape((tokens, width))],
        [*arrays, gain],
        "add_norm",
    )


def norm_grad(grad, values, gain):
    normed, inv_std = normalize(values)
    scaled = grad * gain
    first_mean = jnp.mean(scaled, axis=-1, keepdims=True)
    second_mean = jnp.mean(scaled * normed, axis=-1, keepdims=True)
    return (
        inv_std * (scaled - first_mean - normed * second_mean),
        jnp.sum(grad * normed, axis=0, keepdims=True),
    )


def accumulate(ref, value):
    @pl.when(pl.program_id(0) == 0)
    def _():
        ref[...] = jnp.zeros_like(ref)

    ref[...] += value


def norm_back(terms, upper, values, gain):
    arrays, specs = terms_of(terms)
    tokens, width = values.shape

    def kernel(*refs):
        upper_ref, x, gain_ref, out, out_low, gain_grad = refs[-6:]
        back, part = norm_grad(total_of(refs[:-6]), x[...], gain_ref[...])
        result = upper_ref[...].astype(F32) + back
        out[...] = result
        out_low[...] = result.astype(BF)
        accumulate(gain_grad, part)

    return call(
        kernel,
        (tokens // NORM_ROWS,),
        specs + [row_spec(upper), row_spec(values), whole(gain)],
        [row_spec(values)] * 2 + [pl.BlockSpec((1, width), lambda i: (0, 0))],
        [shape((tokens, width), F32), shape((tokens, width)), shape((1, width), F32)],
        [*arrays, upper, values, gain],
        "norm_back",
    )


def last_back(terms, upper, values, gain, masked, unit, order):
    arrays, specs = terms_of(terms)
    tokens, width = values.shape

    def kernel(*refs):
        upper_ref, x, gain_ref, mask, out, gain_grad, mask_grad = refs[-7:]
        back, part = norm_grad(total_of(refs[:-7]), x[...], gain_ref[...])
        result = upper_ref[...].astype(F32) + back
        hit = mask[...] > 0.5
        out[...] = reorder(jnp.where(hit, 0.0, result).astype(BF), unit, order)
        accumulate(gain_grad, part)
        accumulate(mask_grad, jnp.sum(jnp.where(hit, result, 0.0), axis=0, keepdims=True))

    line = pl.BlockSpec((1, width), lambda i: (0, 0))
    return call(
        kernel,
        (tokens // NORM_ROWS,),
        specs + [row_spec(upper), row_spec(values), whole(gain), row_spec(masked)],
        [row_spec(values), line, line],
        [shape((tokens, width)), shape((1, width), F32), shape((1, width), F32)],
        [*arrays, upper, values, gain, masked],
        "last_back",
    )


def start(hidden, cotangent, masked, embed, gain, unit, order):
    tokens, width = hidden.shape

    def kernel(hid, cot, mask, embed_ref, gain_ref, x, out, grad):
        hit = mask[...] > 0.5
        values = jnp.where(
            hit, embed_ref[...], reorder(hid[...], unit, order).astype(F32)
        )
        x[...] = values
        out[...] = (normalize(values)[0] * gain_ref[...]).astype(BF)
        grad[...] = jnp.where(hit, reorder(cot[...], unit, order).astype(F32), 0.0).astype(BF)

    rows = row_spec(hidden)
    return call(
        kernel,
        (tokens // NORM_ROWS,),
        [rows, rows, row_spec(masked), whole(embed), whole(gain)],
        [rows] * 3,
        [shape((tokens, width), F32), shape((tokens, width)), shape((tokens, width))],
        [hidden, cotangent, masked, embed, gain],
        "start",
    )


def layer_output(upper, terms, unit, order):
    arrays, specs = terms_of(terms)
    tokens, width = upper.shape

    def kernel(*refs):
        values = refs[-2][...] + total_of(refs[:-2])
        refs[-1][...] = reorder(values.astype(BF), unit, order)

    return call(
        kernel,
        (tokens // NORM_ROWS,),
        specs + [row_spec(upper)],
        row_spec(upper),
        shape((tokens, width)),
        [*arrays, upper],
        "layer_output",
    )


def feed_up(pieces, weight):
    rows, width = pieces[0].shape
    hidden = weight.shape[1]
    step = 256

    def kernel(*refs):
        up, tokens, act, slope, sems = refs[5:]

        @pl.when(pl.program_id(0) == 0)
        def _():
            assemble(tokens, refs[:5], sems)

        u = mm(tokens[...], up[...])
        square = u * u
        bend = jnp.tanh(SLOPE * u * (1.0 + CUBIC * square))
        half = 0.5 * (1.0 + bend)
        act[...] = (u * half).astype(BF)
        slope[...] = half + 0.5 * u * (1.0 - bend * bend) * SLOPE * (1.0 + 3.0 * CUBIC * square)

    part = pl.BlockSpec((4 * rows, step), lambda j: (0, j))
    return call(
        kernel,
        (hidden // step,),
        [ANY] * 5 + [pl.BlockSpec((width, step), lambda j: (0, j))],
        [pl.BlockSpec((4 * rows, width), lambda j: (0, 0)), part, part],
        [shape((4 * rows, width)), shape((4 * rows, hidden)), shape((4 * rows, hidden), F32)],
        [*pieces, weight],
        "feed_up",
        scratch=[pltpu.SemaphoreType.DMA((5,))],
        flops=8 * rows * width * hidden,
        size=2 * width * (hidden + 8 * rows),
    )


def feed_down(grad_y, slope, weight):
    tokens, width = grad_y.shape
    hidden = weight.shape[1]
    step = 256

    def kernel(dy, slope_ref, down, out):
        out[...] = (mm(dy[...], down[...]) * slope_ref[...]).astype(BF)

    part = pl.BlockSpec((tokens, step), lambda j: (0, j))
    return call(
        kernel,
        (hidden // step,),
        [whole(grad_y), part, pl.BlockSpec((width, step), lambda j: (0, j))],
        part,
        shape((tokens, hidden)),
        [grad_y, slope, weight],
        "feed_down",
        flops=2 * tokens * width * hidden,
        size=2 * width * (hidden + 8 * tokens),
    )


def softmax(scores):
    exp_terms = jnp.exp(scores - jnp.max(scores, axis=-1, keepdims=True))
    return exp_terms / jnp.sum(exp_terms, axis=-1, keepdims=True)


def score_grad(probs, grad_probs):
    return (
        probs * (grad_probs - jnp.sum(probs * grad_probs, axis=-1, keepdims=True))
    ).astype(BF)


def head(ref, k):
    return ref[:, k * HD : (k + 1) * HD]


def self_forward(projected, images):
    tokens, width = projected.shape
    rows, group = tokens // images, width // 3
    heads = group // HD

    def kernel(proj, mixed):
        for k in range(heads):
            query, key, value = (head(proj, j * heads + k) for j in range(3))
            probs = softmax(mm_t(query, key) * SCALE).astype(BF)
            mixed[:, k * HD : (k + 1) * HD] = mm(probs, value).astype(BF)

    return call(
        kernel,
        (images,),
        [pl.BlockSpec((rows, width), lambda i: (i, 0))],
        pl.BlockSpec((rows, group), lambda i: (i, 0)),
        shape((tokens, group)),
        [projected],
        "self_forward",
        flops=4 * tokens * rows * group,
    )


def self_back(projected, grad_mixed, images):
    tokens, width = projected.shape
    rows, group = tokens // images, width // 3
    heads = group // HD

    def kernel(proj, grad, out):
        for k in range(heads):
            query, key, value = (head(proj, j * heads + k) for j in range(3))
            grad_head = head(grad, k)
            probs = softmax(mm_t(query, key) * SCALE)
            grad_scores = score_grad(probs, mm_t(grad_head, value))
            parts = (
                mm(grad_scores, key) * SCALE,
                t_mm(grad_scores, query) * SCALE,
                t_mm(probs.astype(BF), grad_head),
            )
            for j, part in enumerate(parts):
                at = (j * heads + k) * HD
                out[:, at : at + HD] = part.astype(BF)

    return call(
        kernel,
        (images,),
        [
            pl.BlockSpec((rows, width), lambda i: (i, 0)),
            pl.BlockSpec((rows, group), lambda i: (i, 0)),
        ],
        pl.BlockSpec((rows, width), lambda i: (i, 0)),
        shape((tokens, width)),
        [projected, grad_mixed],
        "self_back",
        flops=10 * tokens * rows * group,
    )


def cross_forward(queries, text_kv):
    tokens, group = queries.shape
    heads = group // HD

    def kernel(query, text, mixed):
        for k in range(heads):
            probs = softmax(mm_t(head(query, k), head(text, k)) * SCALE).astype(BF)
            mixed[:, k * HD : (k + 1) * HD] = mm(probs, head(text, heads + k)).astype(BF)

    return call(
        kernel,
        (1,),
        [whole(queries), whole(text_kv)],
        whole(queries),
        shape((tokens, group)),
        [queries, text_kv],
        "cross_forward",
        flops=4 * tokens * text_kv.shape[0] * group,
    )


def cross_back(queries, text_kv, grad_mixed):
    tokens, group = queries.shape
    context = text_kv.shape[0]
    heads = group // HD

    def kernel(query, text, grad, grad_query, grad_text):
        for k in range(heads):
            query_head, key, value = head(query, k), head(text, k), head(text, heads + k)
            grad_head = head(grad, k)
            probs = softmax(mm_t(query_head, key) * SCALE)
            grad_scores = score_grad(probs, mm_t(grad_head, value))
            grad_query[:, k * HD : (k + 1) * HD] = (mm(grad_scores, key) * SCALE).astype(BF)
            at = (heads + k) * HD
            grad_text[:, k * HD : (k + 1) * HD] = t_mm(grad_scores, query_head) * SCALE
            grad_text[:, at : at + HD] = t_mm(probs.astype(BF), grad_head)

    return call(
        kernel,
        (1,),
        [whole(queries), whole(text_kv), whole(grad_mixed)],
        [whole(queries), whole(text_kv)],
        [shape((tokens, group)), shape((context, 2 * group), F32)],
        [queries, text_kv, grad_mixed],
        "cross_back",
        flops=10 * tokens * context * group,
    )


def grad_products(pairs, name, core=None, blocks=0):
    count_in = len(pairs[0][0])
    tokens, width = pairs[0][0][0].shape
    widths = [y[0].shape[1] for _, y in pairs]
    total = sum(widths)
    rows = 256 if core is None else width // (2 * blocks)
    steps = width // rows if core is None else blocks
    step = 512
    count = len(pairs) * count_in

    def kernel(r, *refs):
        out = refs[2 * count]
        offset = 0
        for k, wide in enumerate(widths):
            left = [refs[k * count_in + b][...].T for b in range(count_in)]
            for at in range(0, wide, step):
                out[:, offset + at : offset + at + step] = sum(
                    mm(left[b], refs[count + k * count_in + b][:, at : at + step])
                    for b in range(count_in)
                ).astype(BF)
            offset += wide

    pick = (lambda i, r: (0, i)) if core is None else (lambda i, r: (0, 2 * i + r[0]))
    return call(
        kernel,
        (steps,),
        [pl.BlockSpec((tokens, rows), pick)] * count
        + [pl.BlockSpec((tokens, w), lambda i, r: (0, 0)) for w in widths for _ in range(count_in)],
        pl.BlockSpec((rows, total), lambda i, r: (i, 0)),
        shape((steps * rows, total)),
        [b for x, _ in pairs for b in x] + [b for _, y in pairs for b in y],
        name,
        flops=2 * tokens * count_in * steps * rows * total,
        size=4 * width * total,
        rank=jnp.zeros((), jnp.int32) if core is None else core,
    )


def pick_weights(three, rank):
    rows, width = three.shape[1], three.shape[2] // 4

    def kernel(r, three_ref, *outs):
        for k in range(4):

            @pl.when(pl.program_id(0) == k)
            def _():
                for j in range(3):
                    outs[k][:, j * width : (j + 1) * width] = three_ref[j]

    outs = [shape((rows, 3 * width))] * 4
    return call(
        kernel,
        (4,),
        [pl.BlockSpec((3, rows, width), lambda k, r: (0, 0, k ^ r[0]))],
        [whole(a) for a in outs],
        outs,
        [three],
        "pick_weights",
        rank=rank,
    )


def pick_rows(arrays, rank):
    rows = arrays[0].shape[1]
    widths = [a.shape[2] for a in arrays]
    count = len(arrays)

    def kernel(r, *refs):
        for k in range(4):

            @pl.when(pl.program_id(0) == k)
            def _():
                at = 0
                for ref, width in zip(refs, widths):
                    refs[count + k][:, at : at + width] = ref[0]
                    at += width

    outs = [shape((rows, sum(widths)))] * 4
    return call(
        kernel,
        (4,),
        [pl.BlockSpec((1, rows, w), lambda k, r: (k ^ r[0], 0, 0)) for w in widths],
        [whole(a) for a in outs],
        outs,
        arrays,
        "pick_rows",
        rank=rank,
    )


def place(parts, rank):
    def kernel(r, *refs):
        for k in range(4):

            @pl.when(pl.program_id(0) == k)
            def _():
                refs[4][0] = refs[k][...]

    rows, columns = parts[0].shape
    return call(
        kernel,
        (4,),
        [whole(p) for p in parts],
        pl.BlockSpec((1, rows, columns), lambda k, r: (k ^ r[0], 0, 0)),
        shape((4, rows, columns)),
        parts,
        "place",
        rank=rank,
    )


def finish_wide(parts, rank):
    rows, width = parts[0].shape

    def kernel(r, *refs):
        for k in range(4):

            @pl.when(pl.program_id(0) == k)
            def _():
                refs[4][...] = refs[k][...].astype(F32)

    return call(
        kernel,
        (4,),
        [whole(p) for p in parts],
        pl.BlockSpec((rows, width), lambda k, r: (0, k ^ r[0])),
        shape((rows, 4 * width), F32),
        parts,
        "finish_wide",
        rank=rank,
    )


def finish_all(parts, text_grad, rank):
    rows, total = parts[0].shape
    width = total // 6

    def kernel(r, *refs):
        key, value, three, out, cross, cross_out = refs[4:]
        for k in range(4):

            @pl.when(pl.program_id(0) == k)
            def _():
                def part(j):
                    return refs[k][:, j * width : (j + 1) * width].astype(F32)

                for j in range(3):
                    three[j] = part(j)
                out[...] = part(3)
                cross[0] = part(4)
                cross_out[...] = part(5)

        cross[1] = key[...]
        cross[2] = value[...]

    wide = pl.BlockSpec((3, rows, width), lambda k, r: (0, 0, k ^ r[0]))
    flat = pl.BlockSpec((rows, width), lambda k, r: (0, k ^ r[0]))
    return call(
        kernel,
        (4,),
        [whole(p) for p in parts]
        + [flat, pl.BlockSpec((rows, width), lambda k, r: (0, 4 + (k ^ r[0])))],
        [wide, flat, wide, flat],
        [shape((3, rows, 4 * width), F32), shape((rows, 4 * width), F32)] * 2,
        [*parts, text_grad, text_grad],
        "finish_all",
        rank=rank,
    )


def plane_block(k):
    return (k >> 1) & 1, (k >> 2) * 2 + (k & 1)


def text_forward(caption, w_text, w_cross):
    context, rows = caption.shape[0], w_text.shape[0]
    half, width = context // 2, w_cross.shape[2] // 4

    def kernel(cap, weight, cross, own, blocks):
        own[...] = mm_t(cap[...], weight[...]).astype(BF)
        for j in range(2):
            part = mm(own[...], cross[1 + j]).astype(BF)
            for k in range(8):
                core, group = plane_block(k)
                blocks[k, :, j * width : (j + 1) * width] = part[
                    core * half : (core + 1) * half, group * width : (group + 1) * width
                ]

    return call(
        kernel,
        (1,),
        [whole(caption), whole(w_text), whole(w_cross)],
        [
            pl.BlockSpec((context, rows), lambda i: (0, 0)),
            pl.BlockSpec((8, half, 2 * width), lambda i: (0, 0, 0)),
        ],
        [shape((context, rows)), shape((8, half, 2 * width))],
        [caption, w_text, w_cross],
        "text_forward",
    )


def text_back(blocks, own_text, w_cross, caption, w_text, extra):
    context, rows = own_text.shape
    half, width = context // 2, w_cross.shape[2] // 4
    wide = caption.shape[1] // 4
    tail = extra.shape[0]

    def kernel(block, own, cross, cap, weight, more, kv_grad, text_grad, out, grads):
        for k in range(8):
            core, group = plane_block(k)
            for j in range(2):
                at = (4 * j + group) * width
                grads[core * half : (core + 1) * half, at : at + width] = block[
                    k, :, j * width : (j + 1) * width
                ]
        kv_grad[...] = t_mm(own[...], grads[...])
        grad_text = sum(
            mm_t(grads[:, 4 * j * width : 4 * (j + 1) * width], cross[1 + j]) for j in range(2)
        ).astype(BF)
        text_grad[...] = t_mm(grad_text, cap[...])
        part = mm(grad_text, weight[...]).astype(BF)
        for k in range(8):
            core, group = plane_block(k)
            out[k, :half, :] = part[core * half : (core + 1) * half, group * wide : (group + 1) * wide]
            out[k, half:, :] = more[...]

    operands = [blocks, own_text, w_cross, caption, w_text, extra]
    outs = [
        shape((rows, 8 * width), F32),
        shape((rows, 4 * wide), F32),
        shape((8, half + tail, wide)),
    ]
    return call(
        kernel,
        (1,),
        [whole(a) for a in operands],
        [whole(a) for a in outs],
        outs,
        operands,
        "text_back",
        scratch=[pltpu.VMEM((context, 8 * width), BF)],
    )


def caption_output(own, other, core):
    count, half, wide = own.shape

    def kernel(r, own_ref, other_ref, out):
        block = jnp.where(pl.program_id(0) == r[0], own_ref[0], other_ref[0])
        out[...] = block.astype(F32)

    block = pl.BlockSpec((1, half, wide), lambda i, k, r: (k, 0, 0))
    return call(
        kernel,
        (2, count),
        [block, block],
        pl.BlockSpec((half, wide), lambda i, k, r: (i, k)),
        shape((2 * half, 4 * wide), F32),
        [own, other],
        "caption_output",
        rank=core,
    )


def column_blocks(weight, count):
    rows = weight.shape[0]
    return weight.reshape(rows, count, -1).transpose(1, 0, 2)


def halves_of(values, width):
    high = values.astype(BF)
    low = (values - high.astype(F32)).astype(BF)
    return jnp.concatenate([high.reshape(-1, width), low.reshape(-1, width)], axis=0)


def whole_of(halves, width):
    rows = halves.shape[0] // 2
    return (halves[:rows] + halves[rows:]).reshape(-1, width)


def make_local(z_size):
    def sum_z(values):
        parts = values.reshape(z_size, -1, values.shape[-1])
        mine = trade(parts, "z").astype(F32).sum(axis=0).astype(BF)
        return spread(mine, "z", z_size).reshape(values.shape)

    def add_z(values):
        step = 1
        while step < z_size:
            values = values + lax.ppermute(
                values, "z", tuple((k, k ^ step) for k in range(z_size))
            )
            step *= 2
        return values

    def layer_order(values):
        shaped = values.reshape(values.shape[:-1] + (z_size, 2, 2, -1))
        return jnp.swapaxes(shaped, -3, -2).reshape(values.shape)

    def local(
        hidden,
        mask_index,
        mask_count,
        mask_embed,
        norm_gains,
        caption,
        w_qkv,
        w_out,
        w_cross,
        w_cross_out,
        w_text,
        w_up,
        w_down,
        cotangent,
    ):
        images, local_rows, width = hidden.shape
        full_length = mask_index.shape[1]
        rank = lax.axis_index("x") * 2 + lax.axis_index("y")
        core = lax.axis_index("c")
        tokens = images * local_rows
        group = width // 4
        text_width = caption.shape[1]

        unit = width // (4 * z_size)
        inside = unit % 128 == 0
        order = [4 * k + j for k in range(z_size) for j in (0, 2, 1, 3)] if inside else None

        def outer(values):
            return values if inside else layer_order(values)

        w_qkv, w_cross = w_qkv.transpose(1, 0, 2), w_cross.transpose(1, 0, 2)
        first = swap_parts(pick_weights(w_qkv, rank))
        first = gather_rows(place(first, rank))

        positions = lax.axis_index("y") * local_rows + jnp.arange(local_rows, dtype=jnp.int32)
        ranks = jnp.arange(full_length, dtype=jnp.int32)
        matches = (mask_index[:, :, None] == positions[None, None, :]) & (
            ranks[None, :, None] < mask_count[:, None, None]
        )
        masked = jnp.any(matches, axis=1).reshape(tokens, 1).astype(F32)
        gains = layer_order(norm_gains)
        gain_a, gain_b, gain_c = gains[:1], gains[1:2], gains[2:]
        start_x, attn_in, grad_top = start(
            outer(hidden.reshape(tokens, width)),
            outer(cotangent.reshape(tokens, width)),
            masked,
            layer_order(mask_embed)[None],
            gain_a,
            unit,
            order,
        )
        attn_in = gather_tokens(attn_in)
        mid = [column_blocks(weight, 4) for weight in (w_out, w_cross[0], w_cross_out)]
        mid = jnp.concatenate(mid, axis=2)
        up = column_blocks(w_up, 4)
        attn_in, mid, up = lax.optimization_barrier((attn_in, mid, up))
        mid, up = gather_rows(trade(mid)), gather_rows(trade(up))

        own_text, kv_part = text_forward(caption, w_text, w_cross)
        text_kv = trade(kv_part, PLANE).astype(F32).sum(axis=0).astype(BF)
        text_kv = sum_z(text_kv)
        other = swap(text_kv, "c")
        text_kv = jnp.concatenate(
            [jnp.where(core == 0, text_kv, other), jnp.where(core == 0, other, text_kv)], axis=0
        )
        attn_in, text_kv = lax.optimization_barrier((attn_in, text_kv))

        attn_in, projected = gather_mm(attn_in, first, 0, 3 * group, "qkv_mm")
        self_mixed = self_forward(projected, 2 * images)
        down = column_blocks(w_down, 4)
        self_mixed, down = lax.optimization_barrier((self_mixed, down))
        down = gather_rows(trade(down))
        parts = mm_scatter(self_mixed, mid[:, :group])
        after_attn, cross_in = add_norm([start_x] + parts, gain_b)

        cross_in, cross_queries = gather_mm(
            gather_tokens(cross_in), mid, group, group, "query_mm"
        )
        cross_mixed = cross_forward(cross_queries, text_kv)
        parts = mm_scatter(cross_mixed, mid[:, 2 * group :])
        after_cross, mlp_in = add_norm([after_attn] + parts, gain_c)

        mlp_in = gather_tokens(mlp_in)
        mlp_in, grad_top = lax.optimization_barrier((mlp_in, grad_top))
        grad_y = jnp.concatenate(gather_tokens(grad_top), axis=0)
        mlp_in, activated, slope = feed_up(mlp_in, up)
        early = [attn_in, self_mixed, cross_in, cross_mixed]
        if inside:
            grad_axes, halves = "z", (core, z_size)

            def both(values):
                return [values, swap(values, "c")]

        else:
            grad_axes, halves = DATA, ()

            def both(values):
                return [values]

        early = [both(values) for values in early]
        down_part = grad_products([(both(grad_y), both(activated))], "down_grads", *halves)
        mlp_in = both(mlp_in)
        slope, down_part, early, mlp_in = lax.optimization_barrier((slope, down_part, early, mlp_in))
        down_rows = scatter_grad(down_part, grad_axes)
        grad_pre = feed_down(grad_y, slope, down)
        parts = mm_scatter(grad_pre, up)
        up_part = grad_products([(mlp_in, both(grad_pre))], "up_grads", *halves)
        grad_after_cross, cross_branch, gain_grad_c = norm_back(
            parts, grad_top, after_cross, gain_c
        )

        cross_branch, up_part = gather_beside(cross_branch, up_part)
        cross_branch, grad_cross_mixed = gather_mm(
            cross_branch, mid, 2 * group, group, "cross_out_back"
        )
        grad_cq, kv_grad = cross_back(cross_queries, text_kv, grad_cross_mixed)
        up_part, down_rows, kv_grad = lax.optimization_barrier((up_part, down_rows, kv_grad))
        up_rows = scatter_grad(up_part, grad_axes)
        cross_branch, grad_cq_both = both(cross_branch), both(grad_cq)
        parts = mm_scatter(grad_cq, mid[:, group : 2 * group])
        grad_after_attn, attn_branch, gain_grad_b = norm_back(
            parts, grad_after_cross, after_attn, gain_b
        )

        activated, attn_branch = lax.optimization_barrier((activated, attn_branch))
        result = mm_t(activated, down).astype(BF)
        attn_branch, result = gather_beside(attn_branch, result)
        attn_branch, result = lax.optimization_barrier((attn_branch, result))
        result = scatter_first(token_blocks(result))
        attn_branch, grad_self_mixed = gather_mm(attn_branch, mid, 0, group, "out_back")
        grad_projected = self_back(projected, grad_self_mixed, 2 * images)
        kv_part = kv_grad.astype(BF).reshape(2, z_size, -1, 2 * group)
        kv_part = kv_part.transpose(1, 0, 2, 3).reshape(2 * z_size, -1, 2 * group)
        grad_projected, result, kv_part = lax.optimization_barrier(
            (grad_projected, result, kv_part)
        )
        kv_part = trade(kv_part, DATA)
        result = scatter_second(result)
        rest_part = grad_products(
            [
                (early[0], both(grad_projected)),
                (both(attn_branch), early[1]),
                (early[2], grad_cq_both),
                (cross_branch, early[3]),
            ],
            "attention_grads",
            *halves,
        )
        grad_projected, result, kv_part, rest_part = lax.optimization_barrier(
            (grad_projected, result, kv_part, rest_part)
        )
        rest_part, up_rows = lax.optimization_barrier((rest_part, up_rows))
        rest_rows = scatter_grad(rest_part, grad_axes)
        parts = mm_scatter(grad_projected, first)
        grad_hidden, gain_grad_a, mask_grad = last_back(
            parts,
            grad_after_attn,
            start_x,
            gain_a,
            masked,
            unit,
            order,
        )
        sums = jnp.concatenate([gain_grad_a, gain_grad_b, gain_grad_c, mask_grad], axis=0)


        kv_part = kv_part.astype(F32).sum(axis=0).astype(BF)
        kv_sum = spread(kv_part, "z", z_size).reshape(-1, 2 * group)
        kv_grads = spread(kv_sum, PLANE, 8)
        kv_weight_grad, grad_text_w, caption_part = text_back(
            kv_grads, own_text, w_cross, caption, w_text, halves_of(sums, text_width // 4)
        )
        half_context = caption.shape[0] // 2
        caption_part = trade(caption_part, PLANE)
        output = layer_output(after_cross, result, unit, order)
        caption_part, output, down_rows, up_rows = lax.optimization_barrier(
            (caption_part, output, down_rows, up_rows)
        )

        caption_part = caption_part.astype(F32).sum(axis=0)
        sums = layer_order(add_z(whole_of(caption_part[half_context:], width)))
        caption_part = caption_part[:half_context].astype(BF).reshape(z_size, -1, text_width // 4)
        caption_part = trade(caption_part, "z")
        down_parts = swap_parts(pick_rows([down_rows], rank))
        caption_part, down_parts, up_rows = lax.optimization_barrier(
            (caption_part, down_parts, up_rows)
        )

        caption_part = caption_part.astype(F32).sum(axis=0).astype(BF)
        caption_part = spread(caption_part, "z", z_size).reshape(half_context, -1)
        up_parts = swap_parts(pick_rows([up_rows], rank))
        down_grad = finish_wide(down_parts, rank)
        caption_part, up_parts, down_grad = lax.optimization_barrier(
            (caption_part, up_parts, down_grad)
        )

        caption_part = spread(caption_part)
        up_grad = finish_wide(up_parts, rank)
        grad_caption = caption_output(caption_part, swap(caption_part, "c"), core)
        rest_rows = swap_parts(pick_rows([rest_rows], rank))
        grad_caption, up_grad, rest_rows = lax.optimization_barrier(
            (grad_caption, up_grad, rest_rows)
        )
        qkv_grad, out_grad, grad_cross, cross_out_grad = finish_all(
            rest_rows, kv_weight_grad, rank
        )
        return (
            outer(output).reshape(hidden.shape),
            outer(grad_hidden).reshape(hidden.shape),
            grad_caption,
            sums[:3],
            sums[3],
            qkv_grad.transpose(1, 0, 2),
            out_grad,
            grad_cross.transpose(1, 0, 2),
            cross_out_grad,
            grad_text_w,
            up_grad,
            down_grad,
        )

    return local


def solution(mesh):
    z_size = mesh.shape["img"] // 4
    inner = Mesh(mesh.devices.reshape(z_size, 2, 2, 2), ("z", "x", "c", "y"))
    image = ("z", "x", "c")
    tokens = P(image, "y", None)
    rows = P(image + ("y",))
    in_specs = (tokens, P(image, None), P(image), P(), P(), P()) + (rows,) * 7 + (tokens,)
    out_specs = (tokens, tokens, P(), P(), P()) + (rows,) * 7
    return jax.shard_map(
        make_local(z_size), mesh=inner, in_specs=in_specs, out_specs=out_specs, check_vma=False
    )
```
